32 devices in a mesh: dp: 8 (over z, x), mp: 4 (over y, core).
Axes of the slice: x: 2, y: 2, z: 4, core: 2. Of those that a mesh axis runs over, the one named last changes fastest.
Arguments:
- token_ids: int32 [64, 128], P(('dp', 'mp')), may hold values from 0 to 31999, as said below
- levels: int32 [64], P(('dp', 'mp')), may hold values from 0 to 63
- noise: bfloat16 [64, 128, 256], P(('dp', 'mp')), may hold values from -6 to 6
- cotangent: bfloat16 [64, 128, 1024], P(('dp', 'mp'))
- table: float32 [32000, 256], P('dp'), may hold values from -6 to 6
- table_m: float32 [32000, 256], P('dp'), may hold values from -0.625 to 0.625
- table_v: float32 [32000, 256], P('dp'), may hold values from 0.0001024 to 0.001536
- w_in: float32 [256, 1024], P('dp'), may hold values from -0.375 to 0.375
- w_in_m: float32 [256, 1024], P('dp'), may hold values from -80 to 80
- w_in_v: float32 [256, 1024], P('dp'), may hold values from 7.3728 to 114.688
- ln_params: float32 [4, 1024], P(None, 'dp'), as said below
- ln_m: float32 [4, 1024], P(None, 'dp'), may hold values from -64 to 64
- ln_v: float32 [4, 1024], P(None, 'dp'), may hold values from 4.096 to 65.536
- w_qkv: float32 [3, 1024, 1024], P(None, 'dp', 'mp'), may hold values from -0.1875 to 0.1875
- qkv_m: float32 [3, 1024, 1024], P(None, 'dp', 'mp'), may hold values from -64 to 64
- qkv_v: float32 [3, 1024, 1024], P(None, 'dp', 'mp'), may hold values from 4.096 to 65.536
- w_out: float32 [1024, 1024], P('mp', 'dp'), may hold values from -0.75 to 0.75
- out_m: float32 [1024, 1024], P('mp', 'dp'), may hold values from -16 to 16
- out_v: float32 [1024, 1024], P('mp', 'dp'), may hold values from 0.4096 to 5.7344
- w_up: float32 [1024, 4096], P('dp', 'mp'), may hold values from -0.1875 to 0.1875
- up_m: float32 [1024, 4096], P('dp', 'mp'), may hold values from -16 to 16
- up_v: float32 [1024, 4096], P('dp', 'mp'), may hold values from 0.24576 to 4.096
- w_down: float32 [4096, 1024], P('mp', 'dp'), may hold values from -0.09375 to 0.09375
- down_m: float32 [4096, 1024], P('mp', 'dp'), may hold values from -32 to 32
- down_v: float32 [4096, 1024], P('mp', 'dp'), may hold values from 0.98304 to 16.384
Outputs:
- output: float32 [64, 128, 1024], P(('dp', 'mp'))
- table_new: float32 [32000, 256], P('dp')
- table_m_new: float32 [32000, 256], P('dp')
- table_v_new: float32 [32000, 256], P('dp')
- w_in_new: float32 [256, 1024], P('dp')
- w_in_m_new: float32 [256, 1024], P('dp')
- w_in_v_new: float32 [256, 1024], P('dp')
- ln_new: float32 [4, 1024], P(None, 'dp')
- ln_m_new: float32 [4, 1024], P(None, 'dp')
- ln_v_new: float32 [4, 1024], P(None, 'dp')
- qkv_new: float32 [3, 1024, 1024], P(None, 'dp', 'mp')
- qkv_m_new: float32 [3, 1024, 1024], P(None, 'dp', 'mp')
- qkv_v_new: float32 [3, 1024, 1024], P(None, 'dp', 'mp')
- out_new: float32 [1024, 1024], P('mp', 'dp')
- out_m_new: float32 [1024, 1024], P('mp', 'dp')
- out_v_new: float32 [1024, 1024], P('mp', 'dp')
- up_new: float32 [1024, 4096], P('dp', 'mp')
- up_m_new: float32 [1024, 4096], P('dp', 'mp')
- up_v_new: float32 [1024, 4096], P('dp', 'mp')
- down_new: float32 [4096, 1024], P('mp', 'dp')
- down_m_new: float32 [4096, 1024], P('mp', 'dp')
- down_v_new: float32 [4096, 1024], P('mp', 'dp')
- norms: float32 [2, 12], replicated
The draws below stay inside these ranges and needn't reach their ends.
Inputs may be any that keep to these rules, and one draw needn't show every extreme that they name: `token_ids`: of the 256 tokens of one device, at most 48 name rows among the 4000 rows held by one index of dp, and in every draw some index of dp is named by exactly 48 tokens of every device. `ln_params`: rows 0 and 2 are positive gains.
All inputs are finite; a program needn't handle non-finite values.
Results may differ from the reference program's by a relative error of at most 0.025.
Values may be sent and summed in bfloat16 or wider, within the bound.
A program may use at most 192 MiB of HBM per device.

```python
import math
import jax
import jax.numpy as jnp
from jax import lax

V = 32000
E = 256
D = 1024
HEADS = 16
HD = 64
FF = 4096
SEQ = 128
SEQ_DEV = 2
LEVELS = 64
STEP = 10
SEQS = 64
TOK_DEV = 256
TOKENS = 8192
ROWS_DEV = 4000
CAP = 48
N_DP = 8


def draw_token_ids(key, part):
    key = jax.random.fold_in(key, 7)
    chosen = jax.random.randint(jax.random.fold_in(key, 1), (), 0, N_DP)
    blocks = SEQS // SEQ_DEV
    slot_total = CAP * N_DP

    def one_block(block_key):
        key_perm, key_place, key_row = jax.random.split(block_key, 3)
        shuffled = jax.random.permutation(key_perm, slot_total)
        ordering = jnp.where(shuffled // CAP == chosen, 0, slot_total) + jnp.arange(slot_total)
        picked = shuffled[jnp.argsort(ordering)][:TOK_DEV]
        picked = jax.random.permutation(key_place, picked)
        owners = picked // CAP
        return owners * ROWS_DEV + jax.random.randint(key_row, (TOK_DEV,), 0, ROWS_DEV)
    block_keys = jax.random.split(jax.random.fold_in(key, 2), blocks)
    return jax.vmap(one_block)(block_keys).reshape(SEQS, SEQ).astype(jnp.int32)


def draw_ln_params(key, part):
    key = jax.random.fold_in(key, 5)
    key_gain, key_shift = jax.random.split(key)
    column = jnp.arange(D, dtype=jnp.float32) / max(D - 1, 1)
    rising = 0.5 * 3.0 ** column
    spread = jnp.exp(0.2 * jax.random.normal(key_gain, (2, D), jnp.float32))
    shifts = 0.3 * jax.random.normal(key_shift, (2, D), jnp.float32)
    gains = rising * spread
    return jnp.stack([gains[0], shifts[0], gains[1], shifts[1]]).astype(jnp.float32)


def draw_cotangent(key, part):
    key = jax.random.fold_in(key, 13)
    column = jnp.arange(D, dtype=jnp.float32) / max(D - 1, 1)
    scales = 0.25 * 10.0 ** column
    base = jax.random.normal(key, (SEQS, SEQ, D), jnp.float32)
    return (base * scales).astype(jnp.bfloat16)


def set_ends(values, rng, smallest, top_value):
    index_at = [jax.random.randint(jax.random.fold_in(rng, axis), (), 0, length) for axis, length in enumerate(values.shape)]
    main_axis = values.shape.index(max(values.shape))
    neighbour = index_at[:main_axis] + [(index_at[main_axis] + 1) % values.shape[main_axis]] + index_at[main_axis + 1:]
    return values.at[tuple(index_at)].set(smallest).at[tuple(neighbour)].set(top_value)


def steps_of(own_key, dims, pieces, low, high):
    def one(axis_at, shards_of):
        draws = jax.random.uniform(jax.random.fold_in(jax.random.fold_in(own_key, 6), axis_at), (shards_of,), jnp.float32, low / len(pieces), high / len(pieces))
        return jnp.repeat(jnp.exp(draws), dims[axis_at] // shards_of).reshape((-1,) + (1,) * (len(dims) - axis_at - 1))

    factor_of = one(*pieces[0])
    for cut in pieces[1:]:
        factor_of = factor_of * one(*cut)
    return factor_of


def bell_draw(own_key, shape, width, reach, shards=(), held_as=jnp.bfloat16):
    loudness = steps_of(own_key, shape, shards, -0.22, 0.18) if shards else 1.0
    entries = jax.random.normal(own_key, shape, jnp.float32) * width * loudness
    return jnp.minimum(jnp.maximum(entries, -reach), reach).astype(held_as)


def setup_inputs(seed: int = 0) -> dict:
    seeds = jax.random.split(jax.random.key(seed), 26)
    token_ids = draw_token_ids(jax.random.fold_in(seeds[25], 71), 0)
    levels = set_ends(jax.random.randint(seeds[1], (SEQS,), 0, LEVELS), jax.random.fold_in(seeds[1], 1), 0, LEVELS - 1).astype(jnp.int32)
    noise = bell_draw(seeds[2], (SEQS, SEQ, E), 1.0, 6.0, ((0, 32),))
    cotangent = draw_cotangent(jax.random.fold_in(seeds[25], 71), 0)
    table = bell_draw(seeds[4], (V, E), 1.0, 6.0, ((0, 8),), jnp.float32)
    table_m = bell_draw(seeds[5], (V, E), (0.09 * TOKENS ** 0.5 * V ** -0.5), 0.625, ((0, 8),), jnp.float32)
    table_v = jnp.clip(jnp.exp(math.log(0.001536) - 2.7080502 * jax.random.uniform(seeds[6], (V, E), jnp.float32) ** steps_of(seeds[6], (V, E), ((0, 8),), -0.2, 0.2)), 0.0001024, 0.001536)
    w_in = bell_draw(seeds[7], (E, D), E ** -0.5, 0.375, ((0, 8),), jnp.float32)
    w_in_m = bell_draw(seeds[8], (E, D), (0.14 * TOKENS ** 0.5), 80.0, ((0, 8),), jnp.float32)
    w_in_v = jnp.clip(jnp.exp(math.log(114.688) - 2.744418 * jax.random.uniform(seeds[9], (E, D), jnp.float32) ** steps_of(seeds[9], (E, D), ((0, 8),), -0.2, 0.2)), 7.3728, 114.688)
    ln_params = draw_ln_params(jax.random.fold_in(seeds[25], 71), 0)
    ln_m = bell_draw(seeds[11], (4, D), (0.11 * TOKENS ** 0.5), 64.0, ((1, 8),), jnp.float32)
    ln_v = jnp.clip(jnp.exp(math.log(65.536) - 2.7725887 * jax.random.uniform(seeds[12], (4, D), jnp.float32) ** steps_of(seeds[12], (4, D), ((1, 8),), -0.2, 0.2)), 4.096, 65.536)
    w_qkv = bell_draw(seeds[13], (3, D, D), D ** -0.5, 0.1875, ((1, 8), (2, 4)), jnp.float32)
    qkv_m = bell_draw(seeds[14], (3, D, D), (0.11 * TOKENS ** 0.5), 64.0, ((1, 8), (2, 4)), jnp.float32)
    qkv_v = jnp.clip(jnp.exp(math.log(65.536) - 2.7725887 * jax.random.uniform(seeds[15], (3, D, D), jnp.float32) ** steps_of(seeds[15], (3, D, D), ((1, 8), (2, 4)), -0.2, 0.2)), 4.096, 65.536)
    w_out = bell_draw(seeds[16], (D, D), (D // 16) ** -0.5, 0.75, ((0, 4), (1, 8)), jnp.float32)
    out_m = bell_draw(seeds[17], (D, D), (0.033 * TOKENS ** 0.5), 16.0, ((0, 4), (1, 8)), jnp.float32)
    out_v = jnp.clip(jnp.exp(math.log(5.7344) - 2.6390573 * jax.random.uniform(seeds[18], (D, D), jnp.float32) ** steps_of(seeds[18], (D, D), ((0, 4), (1, 8)), -0.2, 0.2)), 0.4096, 5.7344)
    w_up = bell_draw(seeds[19], (D, FF), D ** -0.5, 0.1875, ((0, 8), (1, 4)), jnp.float32)
    up_m = bell_draw(seeds[20], (D, FF), (0.028 * TOKENS ** 0.5), 16.0, ((0, 8), (1, 4)), jnp.float32)
    up_v = jnp.clip(jnp.exp(math.log(4.096) - 2.8134108 * jax.random.uniform(seeds[21], (D, FF), jnp.float32) ** steps_of(seeds[21], (D, FF), ((0, 8), (1, 4)), -0.2, 0.2)), 0.24576, 4.096)
    w_down = bell_draw(seeds[22], (FF, D), FF ** -0.5, 0.09375, ((0, 4), (1, 8)), jnp.float32)
    down_m = bell_draw(seeds[23], (FF, D), (0.055 * TOKENS ** 0.5), 32.0, ((0, 4), (1, 8)), jnp.float32)
    down_v = jnp.clip(jnp.exp(math.log(16.384) - 2.8134108 * jax.random.uniform(seeds[24], (FF, D), jnp.float32) ** steps_of(seeds[24], (FF, D), ((0, 4), (1, 8)), -0.2, 0.2)), 0.98304, 16.384)
    return {"token_ids": token_ids, "levels": levels, "noise": noise, "cotangent": cotangent, "table": table, "table_m": table_m, "table_v": table_v, "w_in": w_in, "w_in_m": w_in_m, "w_in_v": w_in_v, "ln_params": ln_params, "ln_m": ln_m, "ln_v": ln_v, "w_qkv": w_qkv, "qkv_m": qkv_m, "qkv_v": qkv_v, "w_out": w_out, "out_m": out_m, "out_v": out_v, "w_up": w_up, "up_m": up_m, "up_v": up_v, "w_down": w_down, "down_m": down_m, "down_v": down_v}


EPS_NORM = 1e-06
EPS_LAYER = 1e-05
EPS_ADAM = 1e-06
BETA_ONE = 0.9
BETA_TWO = 0.999
DECAY = 0.01
RATE = 0.5
SIGMA_TOP = 10.0
HIGH = lax.Precision.HIGHEST

@jax.custom_vjp
def low(v):
    return lax.optimization_barrier(v.astype(jnp.bfloat16)).astype(jnp.float32)

@jax.custom_vjp
def low_back(v):
    return v

def low_keep(v):
    return (low(v), None)

def low_pass(kept, grad):
    return (grad,)

def back_keep(v):
    return (v, None)

def back_low(kept, grad):
    return (low(grad),)
low.defvjp(low_keep, low_pass)
low_back.defvjp(back_keep, back_low)

def sigma_of(levels):
    frac = levels.astype(jnp.float32) / (LEVELS - 1)
    return jnp.exp(frac * jnp.log(SIGMA_TOP))

def layer_norm(inputs, gain, shift):
    center = inputs - lax.optimization_barrier(jnp.mean(inputs, -1, keepdims=True))
    spread = lax.optimization_barrier(jnp.mean(center * center, -1, keepdims=True))
    return center * lax.rsqrt(spread + EPS_LAYER) * gain + shift

def embed_rows(rows, noise, sigmas):
    unit = rows * lax.rsqrt(lax.optimization_barrier(jnp.mean(rows * rows, -1, keepdims=True)) + EPS_NORM)
    return (unit + sigmas * noise) * lax.rsqrt(1.0 + sigmas * sigmas)

def lamb_moments(weight, gradient, first, second):
    first_new = BETA_ONE * first + (1.0 - BETA_ONE) * gradient
    second_new = BETA_TWO * second + (1.0 - BETA_TWO) * gradient * gradient
    first_hat = first_new / (1.0 - BETA_ONE ** STEP)
    second_hat = second_new / (1.0 - BETA_TWO ** STEP)
    direction = first_hat / (jnp.sqrt(second_hat) + EPS_ADAM) + DECAY * weight
    return (first_new, second_new, direction)

def group_squares(arrays, shared_mask):
    table, w_in, ln_params, w_qkv, w_out, w_up, w_down = arrays
    shared = jnp.concatenate([jnp.sum(table * table)[None], jnp.sum(w_in * w_in)[None], lax.optimization_barrier(jnp.sum(ln_params * ln_params, 1))])
    own = jnp.concatenate([lax.optimization_barrier(jnp.sum(w_qkv * w_qkv, (1, 2))), jnp.sum(w_out * w_out)[None], jnp.sum(w_up * w_up)[None], jnp.sum(w_down * w_down)[None]])
    return jnp.concatenate([shared * shared_mask, own])

def trust_factors(ratio):
    return (ratio[0], ratio[1], ratio[2:6][:, None], ratio[6:9][:, None, None], ratio[9], ratio[10], ratio[11])

def forward(params, token_rows, level_rows, noise_rows):
    table, w_in, ln_params, w_qkv, w_out, w_up, w_down = params
    count = token_rows.shape[0]
    rows = table[token_rows]
    sigmas = sigma_of(level_rows)[:, None, None]
    mixed_in = low(embed_rows(rows, noise_rows, sigmas))
    resid_in = low_back(jnp.einsum('bse,ed->bsd', mixed_in, low(w_in), precision=HIGH))
    ln_low = low(ln_params)
    normed_one = low(layer_norm(resid_in, ln_low[0], ln_low[1]))
    qkv_low = low(w_qkv)

    def project(index):
        made = jnp.einsum('bsd,dk->bsk', normed_one, qkv_low[index], precision=HIGH)
        return low_back(low(made)).reshape(count, SEQ, HEADS, HD)
    queries, key_rows, value_rows = (project(0), project(1), project(2))
    scores = low_back(jnp.einsum('bqhd,bkhd->bhqk', queries, key_rows, precision=HIGH) * HD ** (-0.5))
    attn_probs = low(jax.nn.softmax(scores, -1))
    attended = low_back(low(jnp.einsum('bhqk,bkhd->bqhd', attn_probs, value_rows, precision=HIGH))).reshape(count, SEQ, D)
    resid_mid = resid_in + low_back(jnp.einsum('bsd,de->bse', attended, low(w_out), precision=HIGH))
    normed_two = low(layer_norm(resid_mid, ln_low[2], ln_low[3]))
    pre_act = low_back(jnp.einsum('bsd,df->bsf', normed_two, low(w_up), precision=HIGH))
    hidden = low(jax.nn.gelu(pre_act, approximate=False))
    resid_out = resid_mid + low_back(jnp.einsum('bsf,fd->bsd', hidden, low(w_down), precision=HIGH))
    return resid_out * sigmas * lax.rsqrt(1.0 + sigmas * sigmas)

def reference(token_ids, levels, noise, cotangent, table, table_m, table_v, w_in, w_in_m, w_in_v, ln_params, ln_m, ln_v, w_qkv, qkv_m, qkv_v, w_out, out_m, out_v, w_up, up_m, up_v, w_down, down_m, down_v):
    params = (table, w_in, ln_params, w_qkv, w_out, w_up, w_down)
    block_seqs = math.gcd(SEQS, max(1, 4096 // SEQ))
    block_count = SEQS // block_seqs
    ids_blocks = token_ids.reshape(block_count, block_seqs, SEQ)
    level_blocks = levels.reshape(block_count, block_seqs)
    noise_blocks = noise.astype(jnp.float32).reshape(block_count, block_seqs, SEQ, E)
    cot_blocks = cotangent.astype(jnp.float32).reshape(block_count, block_seqs, SEQ, D)

    def block_step(carry, block_data):
        ids_part, level_part, noise_part, cot_part = block_data
        result, pullback = jax.vjp(lambda *weights: forward(weights, ids_part, level_part, noise_part), *params)
        gradients = pullback(cot_part)
        return (jax.tree.map(jnp.add, carry, tuple(gradients)), result)
    zero_grads = tuple((jnp.zeros_like(weight) for weight in params))
    gradients, outputs = lax.scan(block_step, zero_grads, (ids_blocks, level_blocks, noise_blocks, cot_blocks))
    output = outputs.reshape(SEQS, SEQ, D)
    moments = ((table_m, table_v), (w_in_m, w_in_v), (ln_m, ln_v), (qkv_m, qkv_v), (out_m, out_v), (up_m, up_v), (down_m, down_v))
    updated = [lamb_moments(weight, gradient, pair[0], pair[1]) for weight, gradient, pair in zip(params, gradients, moments)]
    directions = tuple((entry[2] for entry in updated))
    weight_norm = jnp.sqrt(group_squares(params, 1.0))
    update_norm = jnp.sqrt(group_squares(directions, 1.0))
    factors = trust_factors(weight_norm / (update_norm + EPS_ADAM))
    results = [output]
    for weight, entry, factor in zip(params, updated, factors):
        results.append(weight - RATE * factor * entry[2])
        results.append(entry[0])
        results.append(entry[1])
    results.append(jnp.stack([weight_norm, update_norm]))
    return tuple(results)
```

```python
import functools

import jax
import jax.numpy as jnp
from jax import lax
from jax.experimental import pallas as pl
from jax.experimental.pallas import tpu as pltpu
from jax.sharding import PartitionSpec as P

HD = 64
LEVELS = 64
STEP = 10


EPS_NORM = 1e-06
EPS_LAYER = 1e-05
EPS_ADAM = 1e-06
BETA_ONE = 0.9
BETA_TWO = 0.999
DECAY = 0.01
RATE = 0.5
SIGMA_TOP = 10.0

F32 = jnp.float32
LOW = jnp.bfloat16
VMEM_BYTES = 60 * 1024 * 1024


def sigma_of(levels):
    frac = levels.astype(jnp.float32) / (LEVELS - 1)
    return jnp.exp(frac * jnp.log(SIGMA_TOP))


def lamb_moments(weight, gradient, first, second):
    first_new = BETA_ONE * first + (1.0 - BETA_ONE) * gradient
    second_new = BETA_TWO * second + (1.0 - BETA_TWO) * gradient * gradient
    first_hat = first_new / (1.0 - BETA_ONE**STEP)
    second_hat = second_new / (1.0 - BETA_TWO**STEP)
    direction = first_hat / (jnp.sqrt(second_hat) + EPS_ADAM) + DECAY * weight
    return (first_new, second_new, direction)


def trust_factors(ratio):
    return (
        ratio[0],
        ratio[1],
        ratio[2:6][:, None],
        ratio[6:9][:, None, None],
        ratio[9],
        ratio[10],
        ratio[11],
    )


def round_up(value, step):
    return -(-value // step) * step


def dot(left, right):
    return jnp.dot(left, right, preferred_element_type=F32)


def dot_nt(left, right):
    return lax.dot_general(left, right, (((1,), (1,)), ((), ())), preferred_element_type=F32)


def dot_tn(left, right):
    return lax.dot_general(left, right, (((0,), (0,)), ((), ())), preferred_element_type=F32)


def strips(total, step, body):
    step = min(step, total)

    def one(turn, carry):
        body(pl.multiple_of(turn * step, step))
        return carry

    lax.fori_loop(0, total // step, one, 0)


class Line:
    def __init__(self, axis):
        self.axis = axis
        self.size = lax.axis_size(axis)
        self.far = self.size // 2
        self.me = lax.axis_index(axis)
        self.hi = lax.div(self.me, 2)
        self.lo = lax.rem(self.me, 2)
        self.partner = self.hi * 2 + (1 - self.lo)

    def at(self, step):
        return lax.rem(self.hi + step + self.far, self.far)

    def push(self, index, src, dst, send, recv):
        return pltpu.make_async_remote_copy(
            src_ref=src,
            dst_ref=dst,
            send_sem=send,
            recv_sem=recv,
            device_id={self.axis: index},
            device_id_type=pl.DeviceIdType.MESH,
        )

    def signal(self, sem, index):
        pl.semaphore_signal(
            sem, inc=1, device_id={self.axis: index}, device_id_type=pl.DeviceIdType.MESH
        )


def meet(pair_lines, all_lines=()):
    sem = pltpu.get_barrier_semaphore()
    count = 0
    for line in pair_lines:
        for step in range(1, line.far):
            line.signal(sem, line.at(step) * 2 + line.lo)
            count += 1
        line.signal(sem, line.partner)
        count += 1
    for line in all_lines:
        for step in range(1, line.size):
            line.signal(sem, lax.rem(line.me + step, line.size))
            count += 1
    pl.semaphore_wait(sem, count)


class Gather:
    def __init__(self, line, at, send, recv):
        self.line, self.at, self.send, self.recv = line, at, send, recv

    @staticmethod
    def sems(size):
        return [pltpu.SemaphoreType.DMA((size,)), pltpu.SemaphoreType.DMA((size,))]

    def copy(self, index, slot, dest):
        block = self.at(index)
        return self.line.push(dest, block, block, self.send.at[slot], self.recv.at[index])

    def start(self):
        line = self.line
        for step in range(1, line.far):
            self.copy(line.me, step - 1, line.at(step) * 2 + line.lo).start()
        self.copy(line.me, line.far - 1, line.partner).start()

    def relay(self, step):
        line = self.line
        handed = self.copy(line.at(-step) * 2 + line.lo, line.far - 1 + step, line.partner)
        handed.wait_recv()
        handed.start()

    def relays(self):
        for step in range(1, self.line.far):
            self.relay(step)

    def close(self):
        line = self.line
        for step in range(line.far):
            self.copy(line.at(-step) * 2 + (1 - line.lo), 0, line.partner).wait_recv()

    def drain(self):
        for slot in range(2 * self.line.far - 1):
            self.copy(self.line.me, slot, self.line.partner).wait_send()


class Scatter:
    def __init__(self, line, part, first, second, send, recv, rows):
        self.line, self.part, self.first, self.second = line, part, first, second
        self.send, self.recv, self.rows = send, recv, rows

    @staticmethod
    def sems(size):
        return [pltpu.SemaphoreType.DMA((size,)), pltpu.SemaphoreType.DMA((size,))]

    def traded(self, hi):
        line = self.line
        return line.push(
            line.partner,
            self.part(hi * 2 + (1 - line.lo)),
            self.first(hi),
            self.send.at[hi],
            self.recv.at[hi],
        )

    def passed(self, step):
        line = self.line
        hi = line.at(step)
        return line.push(
            hi * 2 + line.lo,
            self.part(hi * 2 + line.lo),
            self.second(line.hi),
            self.send.at[line.far + step - 1],
            self.recv.at[line.far + line.hi],
        )

    def trade(self, hi):
        self.traded(hi).start()

    def trade_all(self):
        for step in range(1, self.line.far + 1):
            self.trade(self.line.at(step))

    def pass_on(self, step):
        line = self.line
        hi = line.at(step)
        self.traded(hi).wait_recv()
        mine, other = self.part(hi * 2 + line.lo), self.first(hi)

        def add(row):
            here = pl.ds(row, 16)
            mine[here, :] = (mine[here, :].astype(F32) + other[here, :].astype(F32)).astype(LOW)

        strips(self.rows, 16, add)
        self.passed(step).start()

    def arrive(self):
        line = self.line
        self.traded(line.hi).wait_recv()
        for step in range(1, line.far):
            hi = line.at(-step)
            line.push(
                line.partner,
                self.second(hi),
                self.second(hi),
                self.send.at[0],
                self.recv.at[line.far + hi],
            ).wait_recv()

    def total(self, here):
        line = self.line
        value = self.part(line.me)[here, :].astype(F32) + self.first(line.hi)[here, :].astype(F32)
        for step in range(1, line.far):
            value = value + self.second(line.at(-step))[here, :].astype(F32)
        return value

    def drain(self):
        line = self.line
        for step in range(line.far):
            self.traded(line.at(step)).wait_send()
        for step in range(1, line.far):
            self.passed(step).wait_send()


def block_rows(ref, rows):
    return lambda index: ref.at[pl.ds(pl.multiple_of(index * rows, rows), rows)]


def block_of(ref, rows, first, count):
    return lambda index: ref.at[pl.ds(pl.multiple_of(index * rows + first, count), count)]


def kernel_call(kernel, name, outs, scratch, collective=None, far_inputs=(), count=0, flops=0):
    vmem = pl.BlockSpec(memory_space=pltpu.VMEM)
    params = dict(vmem_limit_bytes=VMEM_BYTES)
    if collective is not None:
        params.update(collective_id=collective, has_side_effects=True)
    return pl.pallas_call(
        kernel,
        out_shape=[jax.ShapeDtypeStruct(shape, kind) for shape, kind in outs],
        in_specs=[
            pl.BlockSpec(memory_space=pl.ANY) if place in far_inputs else vmem
            for place in range(count)
        ],
        out_specs=[vmem] * len(outs),
        scratch_shapes=scratch,
        compiler_params=pltpu.CompilerParams(**params),
        name=name,
    )


def norm_rows(values):
    center = values - jnp.mean(values, -1, keepdims=True)
    spread = jnp.mean(center * center, -1, keepdims=True)
    inverse = lax.rsqrt(spread + EPS_LAYER)
    return center * inverse, inverse


def norm_back(values, gain, grad):
    unit, inverse = norm_rows(values)
    inner = grad * gain
    shared = jnp.mean(inner, -1, keepdims=True)
    along = jnp.mean(inner * unit, -1, keepdims=True)
    return inverse * (inner - shared - unit * along), unit


def embed_kernel(
    cap,
    ids_ref,
    sig_ref,
    noise_ref,
    cot_ref,
    table_ref,
    win_ref,
    ln_ref,
    wa_ref,
    x0_ref,
    mixed_ref,
    rows_ref,
    pick_ref,
    want_ref,
    a_ref,
    dx_ref,
    winf_ref,
    ln_full_ref,
    waf_ref,
    tab_ref,
    tabl_ref,
    hot_ref,
    ask_ref,
    give_ref,
    got_ref,
    lnf_ref,
    tab_sem,
    win_send,
    win_recv,
    ln_send,
    ln_recv,
    wa_send,
    wa_recv,
    dx_send,
    dx_recv,
    a_send,
    a_recv,
    b_send,
    b_recv,
    ask_send,
    ask_recv,
    give_send,
    give_recv,
):
    dp, mp = Line("dp"), Line("mp")
    size = dp.size
    tokens, width = noise_ref.shape
    model = cot_ref.shape[1]
    table_rows = table_ref.shape[0]
    padded = tab_ref.shape[0]
    rin = win_ref.shape[0]
    wide = ln_ref.shape[1]
    half = tokens // 2

    fetch = pltpu.make_async_copy(table_ref, tab_ref.at[pl.ds(0, table_rows)], tab_sem)
    fetch.start()
    meet([mp], [dp])

    win = Gather(dp, block_rows(winf_ref, rin), win_send, win_recv)
    ln = Gather(dp, lambda index: lnf_ref.at[index], ln_send, ln_recv)
    wa = Gather(dp, block_rows(waf_ref, wa_ref.shape[0]), wa_send, wa_recv)
    dxg = Gather(mp, block_rows(dx_ref, tokens), dx_send, dx_recv)
    ag = [
        Gather(mp, block_of(a_ref, tokens, piece * half, half), send, recv)
        for piece, send, recv in ((0, a_send, a_recv), (1, b_send, b_recv))
    ]

    ids = ids_ref[...]
    lane = lax.broadcasted_iota(jnp.int32, (tokens, 128), 1)
    low_end = lane * table_rows
    owned = jnp.where((ids >= low_end) & (ids < low_end + table_rows), 1.0, 0.0)
    before = jnp.where(
        lax.broadcasted_iota(jnp.int32, (tokens, tokens), 0)
        >= lax.broadcasted_iota(jnp.int32, (tokens, tokens), 1),
        1.0,
        0.0,
    )
    ranks = dot(before.astype(LOW), owned.astype(LOW))
    rank = jnp.sum(owned * ranks, 1, keepdims=True) - 1.0
    lane_f = lane.astype(F32)
    owner = jnp.sum(owned * lane_f, 1, keepdims=True)
    slot = owner * cap + rank
    spots = size * cap
    pick_ref[...] = jnp.where(
        lax.broadcasted_iota(jnp.int32, (tokens, spots), 1).astype(F32) == slot, 1.0, 0.0
    ).astype(LOW)
    placed = jnp.where(lane_f == rank, 1.0, 0.0)
    ids_f = ids.astype(F32)
    upper = jnp.floor(ids_f * (1.0 / 256.0))
    lower = ids_f - upper * 256.0
    parts = jnp.concatenate([placed * upper, placed * lower, placed], 1).astype(LOW)
    asked = dot_tn(owned.astype(LOW), parts)
    asked = asked[:, :128] * 256.0 + asked[:, 128:256] + asked[:, 256:] - 1.0
    for index in range(size):
        ask_ref[index] = jnp.broadcast_to(asked[index : index + 1, :], (8, 128))

    def ask(step):
        dest = lax.rem(dp.me + step, size)
        return dp.push(
            dest, ask_ref.at[dest], want_ref.at[dp.me], ask_send.at[step], ask_recv.at[dp.me]
        )

    for step in range(1, size):
        ask(step).start()
    want_ref[dp.me] = ask_ref[dp.me]

    winf_ref[pl.ds(pl.multiple_of(dp.me * rin, rin), rin), :] = win_ref[...]
    win.start()
    lnf_ref[dp.me] = ln_ref[...]
    ln.start()
    waf_ref[pl.ds(pl.multiple_of(dp.me * wa_ref.shape[0], wa_ref.shape[0]), wa_ref.shape[0]), :] = (
        wa_ref[...]
    )
    wa.start()

    def scale_cot(row):
        here = pl.ds(row, 32)
        sig = sig_ref[here, :]
        scale = sig * lax.rsqrt(1.0 + sig * sig)
        dx_ref[pl.ds(pl.multiple_of(mp.me * tokens + row, 32), 32), :] = (
            cot_ref[here, :].astype(F32) * scale
        ).astype(LOW)

    strips(tokens, 32, scale_cot)
    dxg.start()

    if padded > table_rows:
        tab_ref[pl.ds(table_rows, padded - table_rows), :] = jnp.zeros(
            (padded - table_rows, width), F32
        )
    fetch.wait()

    def cast(row):
        here = pl.ds(row, 128)
        tabl_ref[here, :] = tab_ref[here, :].astype(LOW)

    strips(padded, 128, cast)

    for step in range(1, size):
        source = lax.rem(dp.me + size - step, size)
        dp.push(
            dp.partner,
            want_ref.at[source],
            want_ref.at[source],
            ask_send.at[0],
            ask_recv.at[source],
        ).wait_recv()

    def find(index, carry):
        row = want_ref[index][0:1, :]
        eye = lax.broadcasted_iota(jnp.int32, (cap, 128), 0) == lax.broadcasted_iota(
            jnp.int32, (cap, 128), 1
        )
        column = jnp.sum(jnp.where(eye, row, 0.0), 1, keepdims=True)
        local = column.astype(jnp.int32) - dp.me * table_rows
        hot_ref[pl.ds(pl.multiple_of(index * cap, cap), cap), :] = jnp.where(
            lax.broadcasted_iota(jnp.int32, (cap, padded), 1) == local, 1.0, 0.0
        ).astype(LOW)
        return carry

    lax.fori_loop(0, size, find, 0)
    give_ref[...] = dot(hot_ref[...], tabl_ref[...]).astype(LOW)

    def give(step):
        dest = lax.rem(dp.me + step, size)
        return dp.push(
            dest,
            block_rows(give_ref, cap)(dest),
            block_rows(got_ref, cap)(dp.me),
            give_send.at[step],
            give_recv.at[dp.me],
        )

    for step in range(1, size):
        give(step).start()
    mine = pl.ds(pl.multiple_of(dp.me * cap, cap), cap)
    got_ref[mine, :] = give_ref[mine, :]

    ln.relays()
    win.relays()
    dxg.relays()

    for step in range(1, size):
        source = lax.rem(dp.me + size - step, size)
        spot = block_rows(got_ref, cap)(source)
        dp.push(dp.partner, spot, spot, give_send.at[0], give_recv.at[source]).wait_recv()
    rows = dot(pick_ref[...], got_ref[...])
    rows_ref[...] = rows.astype(LOW)
    sig = sig_ref[...]
    unit = rows * lax.rsqrt(jnp.mean(rows * rows, -1, keepdims=True) + EPS_NORM)
    mixed_ref[...] = (
        (unit + sig * noise_ref[...].astype(F32)) * lax.rsqrt(1.0 + sig * sig)
    ).astype(LOW)

    ln.close()
    if wide % 128 == 0:
        ln_full_ref[...] = jnp.concatenate([lnf_ref[index] for index in range(size)], 1)
    else:
        total = jnp.zeros((8, model), F32)
        for index in range(size):
            place = lax.broadcasted_iota(
                jnp.int32, (wide, model), 1
            ) == index * wide + lax.broadcasted_iota(jnp.int32, (wide, model), 0)
            total = total + dot(lnf_ref[index].astype(LOW), jnp.where(place, 1.0, 0.0).astype(LOW))
        ln_full_ref[...] = total
    win.close()
    x0_ref[...] = dot(mixed_ref[...], winf_ref[...].astype(LOW))

    for piece in range(2):

        def first_norm(row):
            here = pl.ds(pl.multiple_of(row + piece * half, 32), 32)
            unit, _ = norm_rows(x0_ref[here, :])
            a_ref[pl.ds(pl.multiple_of(mp.me * tokens + row + piece * half, 32), 32), :] = (
                unit * ln_full_ref[0:1, :] + ln_full_ref[1:2, :]
            ).astype(LOW)

        strips(half, 32, first_norm)
        ag[piece].start()

    wa.relays()
    for gather in ag:
        gather.relays()
    dxg.close()
    for gather in ag:
        gather.close()
    wa.close()
    for gather in (win, ln, wa, dxg, *ag):
        gather.drain()
    for step in range(1, size):
        ask(step).wait_send()
        give(step).wait_send()


def run_embed(cap, ids, sig, noise, cot, table, win, ln, wa):
    dp, mp = lax.axis_size("dp"), lax.axis_size("mp")
    tokens, width = noise.shape
    model = cot.shape[1]
    rin = win.shape[0]
    table_rows = table.shape[0]
    padded = round_up(table_rows, 128)
    spots = dp * cap
    outs = [
        ((tokens, model), F32),
        ((tokens, width), LOW),
        ((tokens, width), LOW),
        ((tokens, spots), LOW),
        ((dp, 8, 128), F32),
        ((tokens * mp, model), LOW),
        ((tokens * mp, model), LOW),
        ((rin * dp, model), win.dtype),
        ((8, model), F32),
        ((model, wa.shape[1]), LOW),
    ]
    scratch = [
        pltpu.VMEM((padded, width), F32),
        pltpu.VMEM((padded, width), LOW),
        pltpu.VMEM((spots, padded), LOW),
        pltpu.VMEM((dp, 8, 128), F32),
        pltpu.VMEM((spots, width), LOW),
        pltpu.VMEM((spots, width), LOW),
        pltpu.VMEM((dp, 8, ln.shape[1]), F32),
        pltpu.SemaphoreType.DMA,
        *Gather.sems(dp),
        *Gather.sems(dp),
        *Gather.sems(dp),
        *Gather.sems(mp),
        *Gather.sems(mp),
        *Gather.sems(mp),
        *Gather.sems(dp),
        *Gather.sems(dp),
    ]
    return kernel_call(
        functools.partial(embed_kernel, cap), "embed", outs, scratch, 1, (4,), 8
    )(ids, sig, noise, cot, table, win, ln, wa)


def head_masks(width):
    lane = lax.broadcasted_iota(jnp.int32, (1, width), 1)
    return [
        jnp.where((lane >= head * HD) & (lane < (head + 1) * HD), 1.0, 0.0)
        for head in range(width // HD)
    ]


def spread_heads(values, masks):
    return jnp.concatenate([values * mask.astype(LOW) for mask in masks], 0)


def join_heads(values, masks, rows):
    total = values[0:rows] * masks[0]
    for head in range(1, len(masks)):
        total = total + values[head * rows : (head + 1) * rows] * masks[head]
    return total


def softmax_rows(queries, keys):
    scores = dot_nt(queries, keys) * (HD ** (-0.5))
    raised = jnp.exp(scores - jnp.max(scores, -1, keepdims=True))
    return raised * (1.0 / jnp.sum(raised, -1, keepdims=True))


def owner_order(line, turn):
    step = lax.div(turn, 2) + 1
    mine = lax.rem(turn, 2)
    hi = lax.rem(line.hi + step, line.far)
    lo = jnp.where(mine == 1, line.lo, 1 - line.lo)
    return hi, hi * 2 + lo, mine


def send_partial(line, scatter, turn):
    hi, _, mine = owner_order(line, turn)

    @pl.when(mine == 0)
    def _():
        scatter.trade(hi)

    for step in range(1, line.far):

        @pl.when(turn == 2 * step - 1)
        def _():
            scatter.pass_on(step)


def attend_kernel(
    seq_len,
    a_ref,
    wa_ref,
    x0_ref,
    ln_ref,
    wb_ref,
    wc_ref,
    qkv_ref,
    o_ref,
    x1_ref,
    c_ref,
    wbf_ref,
    wcf_ref,
    part_ref,
    first_ref,
    second_ref,
    wb_send,
    wb_recv,
    wc_send,
    wc_recv,
    rs_send,
    rs_recv,
    c_send,
    c_recv,
    d_send,
    d_recv,
):
    dp, mp = Line("dp"), Line("mp")
    tokens = x0_ref.shape[0]
    heads_w = o_ref.shape[1]
    half = tokens // 2
    strip = wb_ref.shape[0]
    meet([mp, dp])
    wb = Gather(dp, block_rows(wbf_ref, strip), wb_send, wb_recv)
    wc = Gather(dp, block_rows(wcf_ref, strip), wc_send, wc_recv)
    mine = pl.ds(pl.multiple_of(dp.me * strip, strip), strip)
    wbf_ref[mine, :] = wb_ref[...]
    wb.start()
    wcf_ref[mine, :] = wc_ref[...]
    wc.start()
    scatter = Scatter(
        mp,
        block_rows(part_ref, tokens),
        block_rows(first_ref, tokens),
        block_rows(second_ref, tokens),
        rs_send,
        rs_recv,
        tokens,
    )
    masks = head_masks(heads_w)

    def one(turn, carry):
        _, index, _ = owner_order(mp, turn)
        base = pl.multiple_of(index * tokens, tokens)
        here = pl.ds(base, tokens)
        qkv_ref[here, :] = dot(a_ref[here, :], wa_ref[:, : 3 * heads_w]).astype(LOW)
        for seq in range(tokens // seq_len):
            rows = pl.ds(pl.multiple_of(base + seq * seq_len, seq_len), seq_len)
            queries = spread_heads(qkv_ref[rows, :heads_w], masks)
            probs = softmax_rows(queries, qkv_ref[rows, heads_w : 2 * heads_w]).astype(LOW)
            seen = dot(probs, qkv_ref[rows, 2 * heads_w : 3 * heads_w])
            o_ref[rows, :] = join_heads(seen, masks, seq_len).astype(LOW)
        part_ref[here, :] = dot_nt(o_ref[here, :], wa_ref[:, 3 * heads_w :]).astype(LOW)
        send_partial(mp, scatter, turn)
        return carry

    lax.fori_loop(0, mp.size, one, 0)
    wb.relays()
    scatter.arrive()
    gathers = [
        Gather(mp, block_of(c_ref, tokens, piece * half, half), send, recv)
        for piece, send, recv in ((0, c_send, c_recv), (1, d_send, d_recv))
    ]
    for piece in range(2):

        def second_norm(row):
            here = pl.ds(pl.multiple_of(row + piece * half, 32), 32)
            x1 = x0_ref[here, :] + scatter.total(here)
            x1_ref[here, :] = x1
            unit, _ = norm_rows(x1)
            c_ref[pl.ds(pl.multiple_of(mp.me * tokens + row + piece * half, 32), 32), :] = (
                unit * ln_ref[2:3, :] + ln_ref[3:4, :]
            ).astype(LOW)

        strips(half, 32, second_norm)
        gathers[piece].start()
    wc.relays()
    for gather in gathers:
        gather.relays()
    for gather in (wb, wc, *gathers):
        gather.close()
    for gather in (wb, wc, *gathers):
        gather.drain()
    scatter.drain()


def run_attend(seq_len, a, wa, x0, ln, wb, wc):
    dp, mp = lax.axis_size("dp"), lax.axis_size("mp")
    tokens, model = x0.shape
    group = a.shape[0]
    heads_w = wa.shape[1] // 4
    hidden = wb.shape[1]
    far = mp // 2
    outs = [
        ((group, 3 * heads_w), LOW),
        ((group, heads_w), LOW),
        ((tokens, model), F32),
        ((group, model), LOW),
        ((model, hidden), LOW),
        ((model, hidden), LOW),
    ]
    scratch = [
        pltpu.VMEM((group, model), LOW),
        pltpu.VMEM((far * tokens, model), LOW),
        pltpu.VMEM((far * tokens, model), LOW),
        *Gather.sems(dp),
        *Gather.sems(dp),
        *Scatter.sems(mp),
        *Gather.sems(mp),
        *Gather.sems(mp),
    ]
    return kernel_call(
        functools.partial(attend_kernel, seq_len), "attend", outs, scratch, 2, (), 6
    )(a, wa, x0, ln, wb, wc)


def feed_kernel(
    c_ref,
    dx_ref,
    wb_ref,
    wc_ref,
    x1_ref,
    ln_ref,
    sig_ref,
    cot_ref,
    out_ref,
    dmid_ref,
    dmid_all_ref,
    gup_ref,
    gdn_ref,
    gln_ref,
    h_ref,
    dh_ref,
    hb_ref,
    dhb_ref,
    part_ref,
    first_ref,
    second_ref,
    opart_ref,
    ofirst_ref,
    osecond_ref,
    dc_ref,
    rs_send,
    rs_recv,
    os_send,
    os_recv,
    d_send,
    d_recv,
    e_send,
    e_recv,
):
    mp = Line("mp")
    tokens, model = x1_ref.shape
    half = tokens // 2
    hidden = wb_ref.shape[1]
    meet([mp])
    scatter = Scatter(
        mp,
        block_rows(part_ref, tokens),
        block_rows(first_ref, tokens),
        block_rows(second_ref, tokens),
        rs_send,
        rs_recv,
        tokens,
    )
    out_scatter = Scatter(
        mp,
        block_rows(opart_ref, tokens),
        block_rows(ofirst_ref, tokens),
        block_rows(osecond_ref, tokens),
        os_send,
        os_recv,
        tokens,
    )

    def one(turn, carry):
        _, index, _ = owner_order(mp, turn)
        base = pl.multiple_of(index * tokens, tokens)
        here = pl.ds(base, tokens)
        h_ref[...] = dot(c_ref[here, :], wb_ref[...])
        dh_ref[...] = dot(dx_ref[here, :], wc_ref[...])

        def activate(row):
            rows = pl.ds(row, 16)
            h = h_ref[rows, :]
            gate = 0.5 + 0.5 * lax.erf(h * (0.5**0.5))
            slope = gate + h * (jnp.exp(-0.5 * h * h) * 0.3989422804014327)
            there = pl.ds(pl.multiple_of(base + row, 16), 16)
            hb_ref[there, :] = (h * gate).astype(LOW)
            dhb_ref[there, :] = (dh_ref[rows, :] * slope).astype(LOW)

        strips(tokens, 16, activate)
        part_ref[here, :] = dot_nt(dhb_ref[here, :], wb_ref[...]).astype(LOW)
        send_partial(mp, scatter, turn)
        return carry

    lax.fori_loop(0, mp.size, one, 0)

    def two(turn, carry):
        _, index, _ = owner_order(mp, turn)
        here = pl.ds(pl.multiple_of(index * tokens, tokens), tokens)
        opart_ref[here, :] = dot_nt(hb_ref[here, :], wc_ref[...]).astype(LOW)
        send_partial(mp, out_scatter, turn)
        return carry

    lax.fori_loop(0, mp.size, two, 0)

    scatter.arrive()
    gathers = [
        Gather(mp, block_of(dmid_all_ref, tokens, piece * half, half), send, recv)
        for piece, send, recv in ((0, d_send, d_recv), (1, e_send, e_recv))
    ]
    gln_ref[...] = jnp.zeros_like(gln_ref)
    for piece in range(2):

        def back(row):
            here = pl.ds(pl.multiple_of(row + piece * half, 32), 32)
            dc = scatter.total(here)
            grad, unit = norm_back(x1_ref[here, :], ln_ref[2:3, :], dc)
            sig = sig_ref[here, :]
            scale = sig * lax.rsqrt(1.0 + sig * sig)
            grad = grad + cot_ref[here, :].astype(F32) * scale
            dmid_ref[here, :] = grad
            dmid_all_ref[pl.ds(pl.multiple_of(mp.me * tokens + row + piece * half, 32), 32), :] = (
                grad.astype(LOW)
            )
            gln_ref[0:1, :] += jnp.sum(dc * unit, 0, keepdims=True)
            gln_ref[1:2, :] += jnp.sum(dc, 0, keepdims=True)

        strips(half, 32, back)
        gathers[piece].start()

    block = min(256, model)

    def grads(col):
        cols = pl.ds(col, block)
        gdn_ref[cols, :] = dot_tn(dx_ref[:, cols], hb_ref[...]).astype(LOW)
        gup_ref[cols, :] = dot_tn(c_ref[:, cols], dhb_ref[...]).astype(LOW)

    strips(model, block, grads)
    for gather in gathers:
        gather.relays()
    out_scatter.arrive()

    def finish(row):
        here = pl.ds(row, 32)
        sig = sig_ref[here, :]
        scale = sig * lax.rsqrt(1.0 + sig * sig)
        out_ref[here, :] = (x1_ref[here, :] + out_scatter.total(here)) * scale

    strips(tokens, 32, finish)
    for gather in gathers:
        gather.close()
    for thing in (scatter, out_scatter, *gathers):
        thing.drain()


def run_feed(c, dx, wb, wc, x1, ln, sig, cot):
    mp = lax.axis_size("mp")
    tokens, model = x1.shape
    group = c.shape[0]
    hidden = wb.shape[1]
    far = mp // 2
    outs = [
        ((tokens, model), F32),
        ((tokens, model), F32),
        ((group, model), LOW),
        ((model, hidden), LOW),
        ((model, hidden), LOW),
        ((8, model), F32),
    ]
    scratch = [
        pltpu.VMEM((tokens, hidden), F32),
        pltpu.VMEM((tokens, hidden), F32),
        pltpu.VMEM((group, hidden), LOW),
        pltpu.VMEM((group, hidden), LOW),
        pltpu.VMEM((group, model), LOW),
        pltpu.VMEM((far * tokens, model), LOW),
        pltpu.VMEM((far * tokens, model), LOW),
        pltpu.VMEM((group, model), LOW),
        pltpu.VMEM((far * tokens, model), LOW),
        pltpu.VMEM((far * tokens, model), LOW),
        pltpu.VMEM((8, model), F32),
        *Scatter.sems(mp),
        *Scatter.sems(mp),
        *Gather.sems(mp),
        *Gather.sems(mp),
    ]
    return kernel_call(feed_kernel, "feed", outs, scratch, 3, (), 8)(
        c, dx, wb, wc, x1, ln, sig, cot
    )


def back_kernel(
    seq_len,
    cap,
    dmid_all_ref,
    dmid_ref,
    a_ref,
    qkv_ref,
    o_ref,
    wa_ref,
    x0_ref,
    ln_ref,
    gln_ref,
    mixed_ref,
    rows_ref,
    sig_ref,
    pick_ref,
    want_ref,
    win_ref,
    gup_ref,
    gdn_ref,
    red_up_ref,
    red_dn_ref,
    red_a_ref,
    red_w_ref,
    inc_ref,
    idx_ref,
    dqkv_ref,
    part_ref,
    first_ref,
    second_ref,
    ga_ref,
    gw_ref,
    low_ref,
    dx0_ref,
    gwin_ref,
    up_first,
    up_second,
    dn_first,
    dn_second,
    a_first,
    a_second,
    w_first,
    w_second,
    wsum_ref,
    give_ref,
    norm_ref,
    rs_send,
    rs_recv,
    up_send,
    up_recv,
    dn_send,
    dn_recv,
    a_send,
    a_recv,
    w_send,
    w_recv,
    id_send,
    id_recv,
    inc_send,
    inc_recv,
    ws_send,
    ws_recv,
    give_send,
    give_recv,
):
    dp, mp = Line("dp"), Line("mp")
    size = dp.size
    tokens, model = x0_ref.shape
    group = a_ref.shape[0]
    heads_w = o_ref.shape[1]
    strip = model // size
    rin = win_ref.shape[0] // size
    rin_up = round_up(rin, 16)
    wide = gw_ref.shape[1]
    meet([mp], [dp])

    def spread(part, first, second, send, recv, rows):
        return Scatter(
            dp,
            block_rows(part, rows),
            block_rows(first, rows),
            block_rows(second, rows),
            send,
            recv,
            rows,
        )

    up = spread(gup_ref, up_first, up_second, up_send, up_recv, strip)
    down = spread(gdn_ref, dn_first, dn_second, dn_send, dn_recv, strip)
    first_w = spread(ga_ref, a_first, a_second, a_send, a_recv, strip)
    small = Scatter(
        dp,
        lambda index: gw_ref.at[index],
        lambda index: w_first.at[index],
        lambda index: w_second.at[index],
        w_send,
        w_recv,
        wide,
    )
    for step in range(1, dp.far + 1):
        up.trade(dp.at(step))
        down.trade(dp.at(step))
    idx_ref[mp.me] = want_ref[...]
    ids = Gather(mp, lambda index: idx_ref.at[index], id_send, id_recv)
    ids.start()
    scatter = Scatter(
        mp,
        block_rows(part_ref, tokens),
        block_rows(first_ref, tokens),
        block_rows(second_ref, tokens),
        rs_send,
        rs_recv,
        tokens,
    )
    masks = head_masks(heads_w)
    scale = HD ** (-0.5)

    def one(turn, carry):
        _, index, _ = owner_order(mp, turn)
        base = pl.multiple_of(index * tokens, tokens)
        here = pl.ds(base, tokens)
        low_ref[...] = dot(dmid_all_ref[here, :], wa_ref[:, 3 * heads_w :]).astype(LOW)
        for seq in range(tokens // seq_len):
            rows = pl.ds(pl.multiple_of(base + seq * seq_len, seq_len), seq_len)
            keys = qkv_ref[rows, heads_w : 2 * heads_w]
            values = qkv_ref[rows, 2 * heads_w : 3 * heads_w]
            queries = spread_heads(qkv_ref[rows, :heads_w], masks)
            grads = spread_heads(low_ref[seq * seq_len : (seq + 1) * seq_len, :], masks)
            probs = softmax_rows(queries, keys)
            grad_probs = dot_nt(grads, values)
            inner = jnp.sum(probs * grad_probs, -1, keepdims=True)
            grad_scores = (probs * (grad_probs - inner)).astype(LOW)
            dqkv_ref[rows, 2 * heads_w : 3 * heads_w] = dot_tn(probs.astype(LOW), grads).astype(LOW)
            dqkv_ref[rows, heads_w : 2 * heads_w] = (dot_tn(grad_scores, queries) * scale).astype(LOW)
            dqkv_ref[rows, :heads_w] = (
                join_heads(dot(grad_scores, keys), masks, seq_len) * scale
            ).astype(LOW)
        part_ref[here, :] = dot_nt(dqkv_ref[here, :], wa_ref[:, : 3 * heads_w]).astype(LOW)
        send_partial(mp, scatter, turn)
        return carry

    lax.fori_loop(0, mp.size, one, 0)
    up.pass_on(1)
    down.pass_on(1)

    block = min(256, model)

    def grads_a(col):
        cols = pl.ds(col, block)
        ga_ref[cols, : 3 * heads_w] = dot_tn(a_ref[:, cols], dqkv_ref[...]).astype(LOW)
        ga_ref[cols, 3 * heads_w :] = dot_tn(dmid_all_ref[:, cols], o_ref[...]).astype(LOW)

    strips(model, block, grads_a)
    first_w.trade_all()
    ids.relays()

    scatter.arrive()
    norm_ref[...] = jnp.zeros_like(norm_ref)

    def back(row):
        here = pl.ds(row, 32)
        da = scatter.total(here)
        grad, unit = norm_back(x0_ref[here, :], ln_ref[0:1, :], da)
        dx0_ref[here, :] = (dmid_ref[here, :] + grad).astype(LOW)
        norm_ref[0:1, :] += jnp.sum(da * unit, 0, keepdims=True)
        norm_ref[1:2, :] += jnp.sum(da, 0, keepdims=True)

    strips(tokens, 32, back)

    dx0 = dx0_ref[...]
    grad_mixed = dot_nt(dx0, win_ref[...].astype(LOW))
    sig = sig_ref[...]
    grad_unit = grad_mixed * lax.rsqrt(1.0 + sig * sig)
    rows = rows_ref[...].astype(F32)
    inverse = lax.rsqrt(jnp.mean(rows * rows, -1, keepdims=True) + EPS_NORM)
    unit = rows * inverse
    grad_rows = inverse * (grad_unit - unit * jnp.mean(grad_unit * unit, -1, keepdims=True))
    give_ref[...] = dot_tn(pick_ref[...], grad_rows.astype(LOW)).astype(LOW)

    def spot(index):
        return inc_ref.at[mp.me, pl.ds(pl.multiple_of(index * cap, cap), cap)]

    def give(step):
        dest = lax.rem(dp.me + step, size)
        return dp.push(
            dest, block_rows(give_ref, cap)(dest), spot(dp.me), give_send.at[step], give_recv.at[dp.me]
        )

    for step in range(1, size):
        give(step).start()
    inc_ref[mp.me, pl.ds(pl.multiple_of(dp.me * cap, cap), cap), :] = give_ref[
        pl.ds(pl.multiple_of(dp.me * cap, cap), cap), :
    ]

    gwin_ref[...] = dot_tn(mixed_ref[...], dx0)
    norms = jnp.concatenate(
        [norm_ref[0:2, :], gln_ref[0:2, :], jnp.zeros((12, model), F32)], 0
    ).astype(LOW)
    for index in range(size):
        piece = gwin_ref[index * rin : (index + 1) * rin, :]
        if rin_up > rin:
            piece = jnp.concatenate([piece, jnp.zeros((rin_up - rin, model), F32)], 0)
        gw_ref[index, :rin_up, :] = piece.astype(LOW)
        gw_ref[index, rin_up:, :] = norms
    small.trade_all()

    for step in range(2, dp.far):
        up.pass_on(step)
        down.pass_on(step)

    for step in range(1, size):
        source = lax.rem(dp.me + size - step, size)
        dp.push(
            dp.partner, spot(source), spot(source), give_send.at[0], give_recv.at[source]
        ).wait_recv()
    rows_in = Gather(mp, lambda index: inc_ref.at[index], inc_send, inc_recv)
    rows_in.start()

    for step in range(1, dp.far):
        first_w.pass_on(step)
        small.pass_on(step)
    rows_in.relays()
    small.arrive()

    def sum_small(row):
        here = pl.ds(row, 16)
        wsum_ref[mp.me, here, :] = small.total(here).astype(LOW)

    strips(wide, 16, sum_small)
    weights_in = Gather(mp, lambda index: wsum_ref.at[index], ws_send, ws_recv)
    weights_in.start()
    for scatter_of, out in ((up, red_up_ref), (down, red_dn_ref), (first_w, red_a_ref)):
        scatter_of.arrive()

        def finish(row, scatter_of=scatter_of, out=out):
            here = pl.ds(row, 16)
            out[here, :] = scatter_of.total(here)

        strips(strip, 16, finish)
    weights_in.relays()
    weights_in.close()
    red = wsum_ref[0].astype(F32)
    for index in range(1, mp.size):
        red = red + wsum_ref[index].astype(F32)
    red_w_ref[...] = red
    rows_in.close()
    ids.close()
    for thing in (scatter, up, down, first_w, small, ids, rows_in, weights_in):
        thing.drain()
    for step in range(1, size):
        give(step).wait_send()


def run_back(
    seq_len, cap, dmid_all, dmid, a, qkv, o, wa, x0, ln, gln, mixed, rows, sig, pick, want, win, gup, gdn
):
    dp, mp = lax.axis_size("dp"), lax.axis_size("mp")
    tokens, model = x0.shape
    group = a.shape[0]
    heads_w = o.shape[1]
    hidden = gup.shape[1]
    strip = model // dp
    rin = win.shape[0] // dp
    width = rows.shape[1]
    wide = round_up(rin, 16) + 16
    spots = dp * cap
    far, far_dp = mp // 2, dp // 2
    outs = [
        ((strip, hidden), F32),
        ((strip, hidden), F32),
        ((strip, 4 * heads_w), F32),
        ((wide, model), F32),
        ((mp, spots, width), LOW),
        ((mp, dp, 8, 128), F32),
    ]
    scratch = [
        pltpu.VMEM((group, 3 * heads_w), LOW),
        pltpu.VMEM((group, model), LOW),
        pltpu.VMEM((far * tokens, model), LOW),
        pltpu.VMEM((far * tokens, model), LOW),
        pltpu.VMEM((model, 4 * heads_w), LOW),
        pltpu.VMEM((dp, wide, model), LOW),
        pltpu.VMEM((tokens, heads_w), LOW),
        pltpu.VMEM((tokens, model), LOW),
        pltpu.VMEM((width, model), F32),
        *[pltpu.VMEM((far_dp * strip, hidden), LOW)] * 4,
        *[pltpu.VMEM((far_dp * strip, 4 * heads_w), LOW)] * 2,
        *[pltpu.VMEM((far_dp, wide, model), LOW)] * 2,
        pltpu.VMEM((mp, wide, model), LOW),
        pltpu.VMEM((spots, width), LOW),
        pltpu.VMEM((8, model), F32),
        *Scatter.sems(mp),
        *Scatter.sems(dp),
        *Scatter.sems(dp),
        *Scatter.sems(dp),
        *Scatter.sems(dp),
        *Gather.sems(mp),
        *Gather.sems(mp),
        *Gather.sems(mp),
        *Gather.sems(dp),
    ]
    return kernel_call(
        functools.partial(back_kernel, seq_len, cap), "back", outs, scratch, 4, (), 17
    )(dmid_all, dmid, a, qkv, o, wa, x0, ln, gln, mixed, rows, sig, pick, want, win, gup, gdn)


def table_kernel(tile, w_ref, m_ref, v_ref, idx_ref, inc_ref, m_new_ref, v_new_ref, u_ref, sq_ref):
    turn = pl.program_id(0)

    @pl.when(turn == 0)
    def _():
        sq_ref[...] = jnp.zeros_like(sq_ref)

    spots = idx_ref.shape[1]
    hit = lax.broadcasted_iota(jnp.int32, (tile, spots), 0) + turn * tile == idx_ref[...]
    gradient = dot(jnp.where(hit, 1.0, 0.0).astype(LOW), inc_ref[...])
    weight = w_ref[...]
    first_new, second_new, direction = lamb_moments(weight, gradient, m_ref[...], v_ref[...])
    m_new_ref[...] = first_new
    v_new_ref[...] = second_new
    u_ref[...] = direction
    width = weight.shape[1]
    sq_ref[0:1, :] += jnp.sum((weight * weight).reshape(tile, width), 0, keepdims=True)
    sq_ref[1:2, :] += jnp.sum((direction * direction).reshape(tile, width), 0, keepdims=True)


def run_table(table, table_m, table_v, idx, inc):
    rows, width = table.shape
    tile = max(size for size in range(8, 513, 8) if rows % size == 0)
    spec = pl.BlockSpec((tile, width), lambda turn: (turn, 0))
    whole = pl.BlockSpec(memory_space=pltpu.VMEM)
    return pl.pallas_call(
        functools.partial(table_kernel, tile),
        grid=(rows // tile,),
        in_specs=[spec, spec, spec, whole, whole],
        out_specs=[spec, spec, spec, pl.BlockSpec((8, width), lambda turn: (0, 0))],
        out_shape=[jax.ShapeDtypeStruct((rows, width), F32)] * 3
        + [jax.ShapeDtypeStruct((8, width), F32)],
        compiler_params=pltpu.CompilerParams(vmem_limit_bytes=VMEM_BYTES),
        name="table_update",
    )(table, table_m, table_v, idx, inc)


def totals_kernel(values_ref, out_ref, near_ref, wide_ref, dp_send, dp_recv, mp_send, mp_recv):
    dp, mp = Line("dp"), Line("mp")
    meet([], [dp, mp])
    near_ref[dp.me] = values_ref[...]

    def to_dp(step):
        block = near_ref.at[dp.me]
        return dp.push(
            lax.rem(dp.me + step, dp.size), block, block, dp_send.at[step], dp_recv.at[dp.me]
        )

    def to_mp(step):
        block = wide_ref.at[mp.me]
        return mp.push(
            lax.rem(mp.me + step, mp.size), block, block, mp_send.at[step], mp_recv.at[mp.me]
        )

    for step in range(1, dp.size):
        to_dp(step).start()
    for step in range(1, dp.size):
        source = lax.rem(dp.me + step, dp.size)
        block = near_ref.at[source]
        dp.push(dp.partner, block, block, dp_send.at[0], dp_recv.at[source]).wait_recv()
    wide_ref[mp.me] = jnp.sum(near_ref[...], 0)
    for step in range(1, mp.size):
        to_mp(step).start()
    for step in range(1, mp.size):
        source = lax.rem(mp.me + step, mp.size)
        block = wide_ref.at[source]
        mp.push(mp.partner, block, block, mp_send.at[0], mp_recv.at[source]).wait_recv()
    out_ref[...] = jnp.sum(wide_ref[...], 0)
    for step in range(1, dp.size):
        to_dp(step).wait_send()
    for step in range(1, mp.size):
        to_mp(step).wait_send()


def run_totals(values):
    dp, mp = lax.axis_size("dp"), lax.axis_size("mp")
    scratch = [
        pltpu.VMEM((dp, 8, 128), F32),
        pltpu.VMEM((mp, 8, 128), F32),
        *Gather.sems(dp),
        *Gather.sems(mp),
    ]
    return kernel_call(totals_kernel, "totals", [((8, 128), F32)], scratch, 5, (), 1)(values)[0]


def per_device(
    token_ids,
    levels,
    noise,
    cotangent,
    table,
    table_m,
    table_v,
    w_in,
    w_in_m,
    w_in_v,
    ln_params,
    ln_m,
    ln_v,
    w_qkv,
    qkv_m,
    qkv_v,
    w_out,
    out_m,
    out_v,
    w_up,
    up_m,
    up_v,
    w_down,
    down_m,
    down_v,
):
    dp_count = lax.axis_size("dp")
    dp_index, mp_index = lax.axis_index("dp"), lax.axis_index("mp")
    seq_count, seq_len = token_ids.shape
    tokens = seq_count * seq_len
    model = cotangent.shape[2]
    table_rows = table.shape[0]
    rin = w_in.shape[0]
    strip = ln_params.shape[1]
    heads_w = w_qkv.shape[2]
    cap = round_up(max(2, (3 * tokens + 2 * dp_count - 1) // (2 * dp_count)), 16)

    low_in = w_in.astype(LOW)
    if rin % 16:
        low_in = low_in.astype(F32)
    low_ln = jnp.pad(ln_params.astype(LOW).astype(F32), ((0, 4), (0, 0)))
    low_a = jnp.concatenate(
        [
            jnp.transpose(w_qkv.astype(LOW), (1, 0, 2)).reshape(strip, 3 * heads_w),
            w_out.astype(LOW).T,
        ],
        1,
    )
    low_up = w_up.astype(LOW)
    low_down = w_down.astype(LOW).T

    ids = token_ids.reshape(tokens, 1)
    sig = jnp.repeat(sigma_of(levels), seq_len)[:, None]
    cot = cotangent.reshape(tokens, model)
    x0, mixed, rows, pick, want, a, dx, win, ln, wa = run_embed(
        cap, ids, sig, noise.reshape(tokens, -1), cot, table, low_in, low_ln, low_a
    )
    qkv, o, x1, c, wb, wc = run_attend(seq_len, a, wa, x0, ln, low_up, low_down)
    out, dmid, dmid_all, gup, gdn, gln = run_feed(c, dx, wb, wc, x1, ln, sig, cot)
    red_up, red_down, red_a, red_w, inc, idx = run_back(
        seq_len, cap, dmid_all, dmid, a, qkv, o, wa, x0, ln, gln, mixed, rows, sig, pick, want, win,
        gup, gdn,
    )
    output = out.reshape(seq_count, seq_len, model)

    spots = inc.shape[0] * inc.shape[1]
    named = idx[:, :, 0, :cap].reshape(1, spots).astype(jnp.int32) - dp_index * table_rows
    table_m_new, table_v_new, table_u, table_sq = run_table(
        table, table_m, table_v, named, inc.reshape(spots, -1)
    )
    red_in = red_w[:rin]
    red_ln = lax.dynamic_slice(red_w, (round_up(rin, 16), dp_index * strip), (4, strip))
    red_qkv = jnp.transpose(red_a[:, : 3 * heads_w].reshape(strip, 3, heads_w), (1, 0, 2))
    red_out = red_a[:, 3 * heads_w :].T
    params = (w_in, ln_params, w_qkv, w_out, w_up, w_down)
    gradients = (red_in, red_ln, red_qkv, red_out, red_up, red_down.T)
    moments = (
        (w_in_m, w_in_v),
        (ln_m, ln_v),
        (qkv_m, qkv_v),
        (out_m, out_v),
        (up_m, up_v),
        (down_m, down_v),
    )
    updated = [
        lamb_moments(weight, gradient, pair[0], pair[1])
        for weight, gradient, pair in zip(params, gradients, moments)
    ]
    once = (mp_index == 0).astype(F32)

    def squares(table_part, arrays):
        win_, ln_, qkv_, out_, up_, down_ = arrays
        shared = jnp.concatenate(
            [jnp.sum(table_part)[None], jnp.sum(win_ * win_)[None], jnp.sum(ln_ * ln_, 1)]
        )
        own = jnp.concatenate(
            [
                jnp.sum(qkv_ * qkv_, (1, 2)),
                jnp.sum(out_ * out_)[None],
                jnp.sum(up_ * up_)[None],
                jnp.sum(down_ * down_)[None],
            ]
        )
        return jnp.concatenate([shared * once, own])

    local = jnp.stack(
        [squares(table_sq[0], params), squares(table_sq[1], [entry[2] for entry in updated])]
    )
    totals = run_totals(jnp.pad(local, ((0, 6), (0, 116))))[:2, :12]
    norms = jnp.sqrt(totals)
    factors = trust_factors(norms[0] / (norms[1] + EPS_ADAM))
    results = [output, table - RATE * factors[0] * table_u, table_m_new, table_v_new]
    for weight, entry, factor in zip(params, updated, factors[1:]):
        results.append(weight - RATE * factor * entry[2])
        results.append(entry[0])
        results.append(entry[1])
    results.append(norms)
    return tuple(results)


def solution(mesh):
    return jax.shard_map(
        per_device,
        mesh=mesh,
        in_specs=(
            P(("dp", "mp"), None),
            P(("dp", "mp")),
            P(("dp", "mp"), None, None),
            P(("dp", "mp"), None, None),
            P("dp", None),
            P("dp", None),
            P("dp", None),
            P("dp", None),
            P("dp", None),
            P("dp", None),
            P(None, "dp"),
            P(None, "dp"),
            P(None, "dp"),
            P(None, "dp", "mp"),
            P(None, "dp", "mp"),
            P(None, "dp", "mp"),
            P("mp", "dp"),
            P("mp", "dp"),
            P("mp", "dp"),
            P("dp", "mp"),
            P("dp", "mp"),
            P("dp", "mp"),
            P("mp", "dp"),
            P("mp", "dp"),
            P("mp", "dp"),
        ),
        out_specs=(
            P(("dp", "mp"), None, None),
            P("dp", None),
            P("dp", None),
            P("dp", None),
            P("dp", None),
            P("dp", None),
            P("dp", None),
            P(None, "dp"),
            P(None, "dp"),
            P(None, "dp"),
            P(None, "dp", "mp"),
            P(None, "dp", "mp"),
            P(None, "dp", "mp"),
            P("mp", "dp"),
            P("mp", "dp"),
            P("mp", "dp"),
            P("dp", "mp"),
            P("dp", "mp"),
            P("dp", "mp"),
            P("mp", "dp"),
            P("mp", "dp"),
            P("mp", "dp"),
            P(),
        ),
        check_vma=False,
    )
```

```python
import functools
import types

import jax
import jax.numpy as jnp
from jax import lax
from jax.experimental import pallas as pl
from jax.experimental.pallas import tpu as pltpu
from jax.sharding import PartitionSpec as P

HD = 64
LEVELS = 64
STEP = 10


EPS_NORM = 1e-06
EPS_LAYER = 1e-05
EPS_ADAM = 1e-06
BETA_ONE = 0.9
BETA_TWO = 0.999
DECAY = 0.01
RATE = 0.5
SIGMA_TOP = 10.0

F32 = jnp.float32
LOW = jnp.bfloat16
VMEM_BYTES = 60 * 1024 * 1024


def sigma_of(levels):
    frac = levels.astype(jnp.float32) / (LEVELS - 1)
    return jnp.exp(frac * jnp.log(SIGMA_TOP))


def lamb_moments(weight, gradient, first, second):
    first_new = BETA_ONE * first + (1.0 - BETA_ONE) * gradient
    second_new = BETA_TWO * second + (1.0 - BETA_TWO) * gradient * gradient
    first_hat = first_new / (1.0 - BETA_ONE**STEP)
    second_hat = second_new / (1.0 - BETA_TWO**STEP)
    direction = first_hat / (jnp.sqrt(second_hat) + EPS_ADAM) + DECAY * weight
    return (first_new, second_new, direction)


def trust_factors(ratio):
    return (
        ratio[0],
        ratio[1],
        ratio[2:6][:, None],
        ratio[6:9][:, None, None],
        ratio[9],
        ratio[10],
        ratio[11],
    )


def round_up(value, step):
    return -(-value // step) * step


def dot(left, right):
    return jnp.dot(left, right, preferred_element_type=F32)


def dot_nt(left, right):
    return lax.dot_general(left, right, (((1,), (1,)), ((), ())), preferred_element_type=F32)


def dot_tn(left, right):
    return lax.dot_general(left, right, (((0,), (0,)), ((), ())), preferred_element_type=F32)


def strips(total, step, body):
    step = min(step, total)

    def one(turn, carry):
        body(pl.multiple_of(turn * step, step))
        return carry

    lax.fori_loop(0, total // step, one, 0)


class Line:
    def __init__(self, axis):
        self.axis = axis
        self.size = lax.axis_size(axis)
        self.far = self.size // 2
        self.me = lax.axis_index(axis)
        self.hi = lax.div(self.me, 2)
        self.lo = lax.rem(self.me, 2)
        self.partner = self.hi * 2 + (1 - self.lo)

    def at(self, step):
        return lax.rem(self.hi + step + self.far, self.far)

    def push(self, index, src, dst, send, recv):
        return pltpu.make_async_remote_copy(
            src_ref=src,
            dst_ref=dst,
            send_sem=send,
            recv_sem=recv,
            device_id={self.axis: index},
            device_id_type=pl.DeviceIdType.MESH,
        )

    def signal(self, sem, index):
        pl.semaphore_signal(
            sem, inc=1, device_id={self.axis: index}, device_id_type=pl.DeviceIdType.MESH
        )


def meet(pair_lines, all_lines=()):
    sem = pltpu.get_barrier_semaphore()
    count = 0
    for line in pair_lines:
        for step in range(1, line.far):
            line.signal(sem, line.at(step) * 2 + line.lo)
            count += 1
        line.signal(sem, line.partner)
        count += 1
    for line in all_lines:
        for step in range(1, line.size):
            line.signal(sem, lax.rem(line.me + step, line.size))
            count += 1
    pl.semaphore_wait(sem, count)


class Gather:
    def __init__(self, line, at, send, recv):
        self.line, self.at, self.send, self.recv = line, at, send, recv

    @staticmethod
    def sems(size):
        return [pltpu.SemaphoreType.DMA((size,)), pltpu.SemaphoreType.DMA((size,))]

    def copy(self, index, slot, dest):
        block = self.at(index)
        return self.line.push(dest, block, block, self.send.at[slot], self.recv.at[index])

    def start_far(self):
        line = self.line
        for step in range(1, line.far):
            self.copy(line.me, step - 1, line.at(step) * 2 + line.lo).start()

    def start_near(self):
        self.copy(self.line.me, self.line.far - 1, self.line.partner).start()

    def start(self):
        self.start_far()
        self.start_near()

    def relay(self, step):
        line = self.line
        handed = self.copy(line.at(-step) * 2 + line.lo, line.far - 1 + step, line.partner)
        handed.wait_recv()
        handed.start()

    def relays(self):
        for step in range(1, self.line.far):
            self.relay(step)

    def close(self):
        line = self.line
        for step in range(line.far):
            self.copy(line.at(-step) * 2 + (1 - line.lo), 0, line.partner).wait_recv()

    def drain(self):
        for slot in range(2 * self.line.far - 1):
            self.copy(self.line.me, slot, self.line.partner).wait_send()


class Scatter:
    def __init__(self, line, part, first, second, send, recv, rows):
        self.line, self.part, self.first, self.second = line, part, first, second
        self.send, self.recv, self.rows = send, recv, rows

    @staticmethod
    def sems(size):
        return [pltpu.SemaphoreType.DMA((size,)), pltpu.SemaphoreType.DMA((size,))]

    def traded(self, hi):
        line = self.line
        return line.push(
            line.partner,
            self.part(hi * 2 + (1 - line.lo)),
            self.first(hi),
            self.send.at[hi],
            self.recv.at[hi],
        )

    def passed(self, step):
        line = self.line
        hi = line.at(step)
        return line.push(
            hi * 2 + line.lo,
            self.part(hi * 2 + line.lo),
            self.second(line.hi),
            self.send.at[line.far + step - 1],
            self.recv.at[line.far + line.hi],
        )

    def trade(self, hi):
        self.traded(hi).start()

    def trade_all(self):
        for step in range(1, self.line.far + 1):
            self.trade(self.line.at(step))

    def pass_on(self, step):
        line = self.line
        hi = line.at(step)
        self.traded(hi).wait_recv()
        mine, other = self.part(hi * 2 + line.lo), self.first(hi)

        def add(row):
            here = pl.ds(row, 16)
            mine[here, :] = (mine[here, :].astype(F32) + other[here, :].astype(F32)).astype(LOW)

        strips(self.rows, 16, add)
        self.passed(step).start()

    def arrive(self):
        line = self.line
        self.traded(line.hi).wait_recv()
        for step in range(1, line.far):
            hi = line.at(-step)
            line.push(
                line.partner,
                self.second(hi),
                self.second(hi),
                self.send.at[0],
                self.recv.at[line.far + hi],
            ).wait_recv()

    def total(self, here):
        line = self.line
        value = self.part(line.me)[here, :].astype(F32) + self.first(line.hi)[here, :].astype(F32)
        for step in range(1, line.far):
            value = value + self.second(line.at(-step))[here, :].astype(F32)
        return value

    def drain(self):
        line = self.line
        for step in range(line.far):
            self.traded(line.at(step)).wait_send()
        for step in range(1, line.far):
            self.passed(step).wait_send()


def block_rows(ref, rows):
    return lambda index: ref.at[pl.ds(pl.multiple_of(index * rows, rows), rows)]


def block_of(ref, rows, first, count):
    return lambda index: ref.at[pl.ds(pl.multiple_of(index * rows + first, count), count)]


def norm_rows(values):
    center = values - jnp.mean(values, -1, keepdims=True)
    spread = jnp.mean(center * center, -1, keepdims=True)
    inverse = lax.rsqrt(spread + EPS_LAYER)
    return center * inverse, inverse


def norm_back(values, gain, grad):
    unit, inverse = norm_rows(values)
    inner = grad * gain
    shared = jnp.mean(inner, -1, keepdims=True)
    along = jnp.mean(inner * unit, -1, keepdims=True)
    return inverse * (inner - shared - unit * along), unit


def head_masks(width):
    lane = lax.broadcasted_iota(jnp.int32, (1, width), 1)
    return [
        jnp.where((lane >= head * HD) & (lane < (head + 1) * HD), 1.0, 0.0)
        for head in range(width // HD)
    ]


def spread_heads(values, masks):
    return jnp.concatenate([values * mask.astype(LOW) for mask in masks], 0)


def join_heads(values, masks, rows):
    total = values[0:rows] * masks[0]
    for head in range(1, len(masks)):
        total = total + values[head * rows : (head + 1) * rows] * masks[head]
    return total


def softmax_rows(queries, keys):
    scores = dot_nt(queries, keys) * (HD ** (-0.5))
    raised = jnp.exp(scores - jnp.max(scores, -1, keepdims=True))
    return raised * (1.0 / jnp.sum(raised, -1, keepdims=True))


def owner_order(line, turn):
    step = lax.div(turn, 2) + 1
    mine = lax.rem(turn, 2)
    hi = lax.rem(line.hi + step, line.far)
    lo = jnp.where(mine == 1, line.lo, 1 - line.lo)
    return hi, hi * 2 + lo, mine


def send_partial(line, scatter, turn):
    hi, _, mine = owner_order(line, turn)

    @pl.when(mine == 0)
    def _():
        scatter.trade(hi)

    for step in range(1, line.far):

        @pl.when(turn == 2 * step - 1)
        def _():
            scatter.pass_on(step)


def far_copies(line, make, sends, recvs):
    def copy(step):
        dest = lax.rem(line.me + step, line.size)
        src, dst = make(dest, line.me)
        return line.push(dest, src, dst, sends.at[step], recvs.at[line.me])

    def wait():
        for step in range(1, line.size):
            source = lax.rem(line.me + line.size - step, line.size)
            _, dst = make(source, source)
            line.push(line.partner, dst, dst, sends.at[0], recvs.at[source]).wait_recv()

    return copy, wait


def layer_kernel(seq_len, cap, names, *refs):
    R = types.SimpleNamespace(**dict(zip(names, refs)))
    dp, mp = Line("dp"), Line("mp")
    size = dp.size
    tokens, width = R.noise.shape
    model = R.cot.shape[1]
    group = R.a.shape[0]
    heads_w = R.o.shape[1]
    hidden = R.wbf.shape[1]
    table_rows = R.table.shape[0]
    rin = R.w_in.shape[0]
    rin_up = round_up(rin, 16)
    strip = R.w_up.shape[0]
    half = tokens // 2
    seqs = tokens // seq_len
    wide = R.gw.shape[1]
    spots = size * cap
    own = pl.multiple_of(mp.me * tokens, tokens)
    own_strip = pl.ds(pl.multiple_of(dp.me * strip, strip), strip)

    chunk = R.tab.shape[1]
    pieces = -(-table_rows // chunk)

    def fetch(piece):
        rows = min(chunk, table_rows - piece * chunk)
        return pltpu.make_async_copy(
            R.table.at[pl.ds(piece * chunk, rows)],
            R.tab.at[piece % 2, pl.ds(0, rows)],
            R.tab_sem.at[piece % 2],
        )

    for piece in range(min(2, pieces)):
        fetch(piece).start()

    eye = lax.broadcasted_iota(jnp.int32, (seq_len, seq_len), 0) == lax.broadcasted_iota(
        jnp.int32, (seq_len, seq_len), 1
    )
    id_rows = R.ids[...].astype(F32)
    ids = jnp.concatenate(
        [
            jnp.sum(jnp.where(eye, id_rows[seq : seq + 1, :], 0.0), 1, keepdims=True)
            for seq in range(seqs)
        ],
        0,
    )
    lane = lax.broadcasted_iota(jnp.int32, (tokens, 128), 1).astype(F32)
    low_end = lane * float(table_rows)
    owned = jnp.where((ids >= low_end) & (ids < low_end + float(table_rows)), 1.0, 0.0)
    before = jnp.where(
        lax.broadcasted_iota(jnp.int32, (tokens, tokens), 0)
        >= lax.broadcasted_iota(jnp.int32, (tokens, tokens), 1),
        1.0,
        0.0,
    )
    ranks = dot(before.astype(LOW), owned.astype(LOW))
    rank = jnp.sum(owned * ranks, 1, keepdims=True) - 1.0
    slot = jnp.sum(owned * lane, 1, keepdims=True) * cap + rank
    placed = jnp.where(lane == rank, 1.0, 0.0)
    upper = jnp.floor(ids * (1.0 / 256.0))
    lower = ids - upper * 256.0
    parts = jnp.concatenate([placed * upper, placed * lower, placed], 1).astype(LOW)
    asked = dot_tn(owned.astype(LOW), parts)
    asked = asked[:, :128] * 256.0 + asked[:, 128:256] + asked[:, 256:] - 1.0
    for index in range(size):
        R.ask[index] = jnp.broadcast_to(asked[index : index + 1, :], (8, 128))
    R.idx[mp.me, dp.me] = R.ask[dp.me]

    meet([mp], [dp])
    ask, ask_wait = far_copies(
        dp,
        lambda dest, source: (R.ask.at[dest], R.idx.at[mp.me, source]),
        R.ask_send,
        R.ask_recv,
    )
    for step in range(1, size):
        ask(step).start()

    win = Gather(dp, block_rows(R.winf, rin), R.win_send, R.win_recv)
    ln = Gather(dp, lambda index: R.lnf.at[index], R.ln_send, R.ln_recv)
    half_strip = strip // 2
    wa = [
        Gather(dp, block_of(R.waf, strip, piece * half_strip, half_strip), send, recv)
        for piece, send, recv in ((0, R.wa_send, R.wa_recv), (1, R.wx_send, R.wx_recv))
    ]
    wb = Gather(dp, block_rows(R.wbf, strip), R.wb_send, R.wb_recv)
    wc = Gather(dp, block_rows(R.wcf, strip), R.wc_send, R.wc_recv)
    dxg = Gather(mp, block_rows(R.dx, tokens), R.dx_send, R.dx_recv)

    def halves(ref, names_of):
        return [
            Gather(mp, block_of(ref, tokens, piece * half, half), send, recv)
            for piece, (send, recv) in enumerate(names_of)
        ]

    ag = halves(R.a, ((R.a_send, R.a_recv), (R.b_send, R.b_recv)))
    cg = halves(R.c, ((R.c_send, R.c_recv), (R.d_send, R.d_recv)))
    mg = halves(R.dmid_all, ((R.e_send, R.e_recv), (R.f_send, R.f_recv)))

    R.winf[pl.ds(pl.multiple_of(dp.me * rin, rin), rin), :] = (
        R.w_in[...].astype(LOW).astype(R.winf.dtype)
    )
    win.start()
    shares = R.ln_params[...].astype(LOW).astype(F32)
    R.lnf[dp.me] = jnp.concatenate([shares, jnp.zeros_like(shares)], 0)
    ln.start()
    for part in range(3):
        R.waf[own_strip, part * heads_w : (part + 1) * heads_w] = R.w_qkv[part].astype(LOW)
    R.waf[own_strip, 3 * heads_w :] = R.w_out[...].T.astype(LOW)
    wa[0].start()
    wa[1].start_near()

    for seq in range(seqs):
        level = jnp.full((seq_len, 1), R.levels[seq], jnp.int32).astype(F32) / (LEVELS - 1)
        R.sig[seq * seq_len : (seq + 1) * seq_len, :] = jnp.exp(level * jnp.log(SIGMA_TOP))

    def scale_at(here):
        sig = R.sig[here, :]
        return sig * lax.rsqrt(1.0 + sig * sig)

    def scale_cot(row):
        here = pl.ds(row, 32)
        R.dx[pl.ds(pl.multiple_of(own + row, 32), 32), :] = (
            R.cot[here, :].astype(F32) * scale_at(here)
        ).astype(LOW)

    strips(tokens, 32, scale_cot)
    dxg.start()
    R.wbf[own_strip, :] = R.w_up[...].astype(LOW)
    R.wcf[own_strip, :] = R.w_down[...].T.astype(LOW)
    R.pick[...] = jnp.where(
        lax.broadcasted_iota(jnp.int32, (tokens, spots), 1).astype(F32) == slot, 1.0, 0.0
    ).astype(LOW)

    ask_wait()
    small_eye = lax.broadcasted_iota(jnp.int32, (cap, 128), 0) == lax.broadcasted_iota(
        jnp.int32, (cap, 128), 1
    )

    def locate(index, carry):
        row = R.idx[mp.me, index][0:1, :]
        column = jnp.sum(jnp.where(small_eye, row, 0.0), 1, keepdims=True)
        local = column.astype(jnp.int32) - dp.me * table_rows
        R.loc[pl.ds(pl.multiple_of(index * cap, cap), cap), :] = jnp.broadcast_to(local, (cap, 128))
        return carry

    lax.fori_loop(0, size, locate, 0)
    found = None
    for piece in range(pieces):
        fetch(piece).wait()
        rows = min(chunk, table_rows - piece * chunk)
        if rows < chunk:
            R.tab[piece % 2, rows:, :] = jnp.zeros((chunk - rows, width), F32)
        hit = (
            lax.broadcasted_iota(jnp.int32, (spots, chunk), 1) + piece * chunk == R.loc[:, 0:1]
        )
        more = dot(jnp.where(hit, 1.0, 0.0).astype(LOW), R.tab[piece % 2].astype(LOW))
        found = more if found is None else found + more
        if piece + 2 < pieces:
            fetch(piece + 2).start()
    R.give[...] = found.astype(LOW)

    give, give_wait = far_copies(
        dp,
        lambda dest, source: (block_rows(R.give, cap)(dest), block_rows(R.got, cap)(source)),
        R.give_send,
        R.give_recv,
    )
    for step in range(1, size):
        give(step).start()
    mine = pl.ds(pl.multiple_of(dp.me * cap, cap), cap)
    R.got[mine, :] = R.give[mine, :]
    wa[1].start_far()

    ln.relays()
    win.relays()
    ln.close()
    wide_ln = R.ln_params.shape[1]
    if wide_ln % 128 == 0:
        R.gains[...] = jnp.concatenate([R.lnf[index] for index in range(size)], 1)
    else:
        total = jnp.zeros((8, model), F32)
        for index in range(size):
            place = lax.broadcasted_iota(
                jnp.int32, (wide_ln, model), 1
            ) == index * wide_ln + lax.broadcasted_iota(jnp.int32, (wide_ln, model), 0)
            total = total + dot(R.lnf[index].astype(LOW), jnp.where(place, 1.0, 0.0).astype(LOW))
        R.gains[...] = total

    give_wait()
    rows = dot(R.pick[...], R.got[...])
    R.rows[...] = rows.astype(LOW)
    sig = R.sig[...]
    unit = rows * lax.rsqrt(jnp.mean(rows * rows, -1, keepdims=True) + EPS_NORM)
    R.mixed[...] = ((unit + sig * R.noise[...].astype(F32)) * lax.rsqrt(1.0 + sig * sig)).astype(LOW)
    win.close()
    R.x0[...] = dot(R.mixed[...], R.winf[...].astype(LOW))

    for piece in range(2):

        def first_norm(row):
            here = pl.ds(pl.multiple_of(row + piece * half, 32), 32)
            normed, _ = norm_rows(R.x0[here, :])
            R.a[pl.ds(pl.multiple_of(own + row + piece * half, 32), 32), :] = (
                normed * R.gains[0:1, :] + R.gains[1:2, :]
            ).astype(LOW)

        strips(half, 32, first_norm)
        ag[piece].start()

    wa[0].relays()
    wa[1].relays()
    wb.start()
    wc.start()
    dxg.relays()
    for gather in ag:
        gather.relays()
    for gather in (*wa, *ag):
        gather.close()

    def pair(part, first, second, send, recv):
        return Scatter(
            mp,
            block_rows(part, tokens),
            block_rows(first, tokens),
            block_rows(second, tokens),
            send,
            recv,
            tokens,
        )

    att = pair(R.part, R.fold, R.fold_far, R.as_send, R.as_recv)
    out = pair(R.c, R.first, R.second, R.os_send, R.os_recv)
    dcs = pair(R.part, R.fold, R.fold_far, R.cs_send, R.cs_recv)
    das = pair(R.part, R.fold, R.fold_far, R.ds_send, R.ds_recv)
    masks = head_masks(heads_w)

    def attend(turn, carry):
        _, index, _ = owner_order(mp, turn)
        base = pl.multiple_of(index * tokens, tokens)
        here = pl.ds(base, tokens)
        R.qkv[here, :] = dot(R.a[here, :], R.waf[:, : 3 * heads_w]).astype(LOW)
        for seq in range(seqs):
            rows = pl.ds(pl.multiple_of(base + seq * seq_len, seq_len), seq_len)
            queries = spread_heads(R.qkv[rows, :heads_w], masks)
            probs = softmax_rows(queries, R.qkv[rows, heads_w : 2 * heads_w]).astype(LOW)
            seen = dot(probs, R.qkv[rows, 2 * heads_w : 3 * heads_w])
            R.o[rows, :] = join_heads(seen, masks, seq_len).astype(LOW)
        R.part[here, :] = dot_nt(R.o[here, :], R.waf[:, 3 * heads_w :]).astype(LOW)
        send_partial(mp, att, turn)
        return carry

    lax.fori_loop(0, mp.size, attend, 0)
    wb.relays()
    att.arrive()
    for piece in range(2):

        def second_norm(row):
            here = pl.ds(pl.multiple_of(row + piece * half, 32), 32)
            x1 = R.x0[here, :] + att.total(here)
            R.out[here, :] = x1
            normed, _ = norm_rows(x1)
            R.c[pl.ds(pl.multiple_of(own + row + piece * half, 32), 32), :] = (
                normed * R.gains[2:3, :] + R.gains[3:4, :]
            ).astype(LOW)

        strips(half, 32, second_norm)
        cg[piece].start()
    for gather in cg:
        gather.relays()
    wc.relays()
    for gather in (wb, *cg, dxg, wc):
        gather.close()
    att.drain()

    def feed(turn, carry):
        _, index, _ = owner_order(mp, turn)
        base = pl.multiple_of(index * tokens, tokens)
        here = pl.ds(base, tokens)
        R.h[...] = dot(R.c[here, :], R.wbf[...])
        R.dh[...] = dot(R.dx[here, :], R.wcf[...])

        def activate(row):
            rows = pl.ds(row, 16)
            h = R.h[rows, :]
            gate = 0.5 + 0.5 * lax.erf(h * (0.5**0.5))
            slope = gate + h * (jnp.exp(-0.5 * h * h) * 0.3989422804014327)
            there = pl.ds(pl.multiple_of(base + row, 16), 16)
            R.hb[there, :] = (h * gate).astype(LOW)
            R.dhb[there, :] = (R.dh[rows, :] * slope).astype(LOW)

        strips(tokens, 16, activate)
        R.part[here, :] = dot_nt(R.dhb[here, :], R.wbf[...]).astype(LOW)
        send_partial(mp, dcs, turn)
        return carry

    lax.fori_loop(0, mp.size, feed, 0)

    def spread(part, first, second, send, recv):
        return Scatter(
            dp,
            block_rows(part, strip),
            block_rows(first, strip),
            block_rows(second, strip),
            send,
            recv,
            strip,
        )

    for gather in (wb, *wa):
        gather.drain()
    up = spread(R.wbf, R.up_first, R.up_second, R.up_send, R.up_recv)
    down = spread(R.gdn, R.dn_first, R.dn_second, R.dn_send, R.dn_recv)
    first_w = spread(R.waf, R.wa_first, R.wa_second, R.ga_send, R.ga_recv)
    small = Scatter(
        dp,
        lambda index: R.gw.at[index],
        lambda index: R.w_first.at[index],
        lambda index: R.w_second.at[index],
        R.gw_send,
        R.gw_recv,
        wide,
    )
    block = 2 * strip if (2 * strip) % 128 == 0 else min(256, model)

    def grads(make, scatters):
        if block == 2 * strip:

            def turn_of(turn, carry):
                hi = lax.rem(dp.hi + turn + 1, dp.far)
                make(pl.ds(pl.multiple_of(hi * block, block), block))
                for scatter in scatters:
                    scatter.trade(hi)
                return carry

            lax.fori_loop(0, dp.far, turn_of, 0)
        else:
            strips(model, block, lambda col: make(pl.ds(col, block)))
            for scatter in scatters:
                scatter.trade_all()

    def feed_grads(cols):
        R.gdn[cols, :] = dot_tn(R.dx[:, cols], R.hb[...]).astype(LOW)
        R.wbf[cols, :] = dot_tn(R.c[:, cols], R.dhb[...]).astype(LOW)

    grads(feed_grads, (down, up))

    dcs.arrive()
    R.norms[...] = jnp.zeros_like(R.norms)
    for piece in range(2):

        def second_back(row):
            here = pl.ds(pl.multiple_of(row + piece * half, 32), 32)
            dc = dcs.total(here)
            grad, unit = norm_back(R.out[here, :], R.gains[2:3, :], dc)
            grad = grad + R.cot[here, :].astype(F32) * scale_at(here)
            R.dmid[here, :] = grad
            R.dmid_all[pl.ds(pl.multiple_of(own + row + piece * half, 32), 32), :] = grad.astype(LOW)
            R.norms[2:3, :] += jnp.sum(dc * unit, 0, keepdims=True)
            R.norms[3:4, :] += jnp.sum(dc, 0, keepdims=True)

        strips(half, 32, second_back)
        mg[piece].start()

    for gather in cg:
        gather.drain()

    def feed_out(turn, carry):
        _, index, _ = owner_order(mp, turn)
        here = pl.ds(pl.multiple_of(index * tokens, tokens), tokens)
        R.c[here, :] = dot_nt(R.hb[here, :], R.wcf[...]).astype(LOW)
        send_partial(mp, out, turn)
        return carry

    lax.fori_loop(0, mp.size, feed_out, 0)
    for gather in mg:
        gather.relays()
    up.pass_on(1)
    down.pass_on(1)
    for gather in mg:
        gather.close()
    dcs.drain()

    scale = HD ** (-0.5)

    def attend_back(turn, carry):
        _, index, _ = owner_order(mp, turn)
        base = pl.multiple_of(index * tokens, tokens)
        here = pl.ds(base, tokens)
        R.low[...] = dot(R.dmid_all[here, :], R.waf[:, 3 * heads_w :]).astype(LOW)
        for seq in range(seqs):
            rows = pl.ds(pl.multiple_of(base + seq * seq_len, seq_len), seq_len)
            keys = R.qkv[rows, heads_w : 2 * heads_w]
            values = R.qkv[rows, 2 * heads_w : 3 * heads_w]
            queries = spread_heads(R.qkv[rows, :heads_w], masks)
            upper_grads = spread_heads(R.low[seq * seq_len : (seq + 1) * seq_len, :], masks)
            probs = softmax_rows(queries, keys)
            grad_probs = dot_nt(upper_grads, values)
            inner = jnp.sum(probs * grad_probs, -1, keepdims=True)
            grad_scores = (probs * (grad_probs - inner)).astype(LOW)
            R.qkv[rows, 2 * heads_w : 3 * heads_w] = dot_tn(
                probs.astype(LOW), upper_grads
            ).astype(LOW)
            R.qkv[rows, heads_w : 2 * heads_w] = (dot_tn(grad_scores, queries) * scale).astype(LOW)
            R.qkv[rows, :heads_w] = (
                join_heads(dot(grad_scores, keys), masks, seq_len) * scale
            ).astype(LOW)
        R.part[here, :] = dot_nt(R.qkv[here, :], R.waf[:, : 3 * heads_w]).astype(LOW)
        send_partial(mp, das, turn)
        return carry

    lax.fori_loop(0, mp.size, attend_back, 0)

    def attend_grads(cols):
        R.waf[cols, : 3 * heads_w] = dot_tn(R.a[:, cols], R.qkv[...]).astype(LOW)
        R.waf[cols, 3 * heads_w :] = dot_tn(R.dmid_all[:, cols], R.o[...]).astype(LOW)

    grads(attend_grads, (first_w,))
    for step in range(2, max(2, dp.far - 1)):
        up.pass_on(step)
        down.pass_on(step)

    das.arrive()

    def first_back(row):
        here = pl.ds(row, 32)
        da = das.total(here)
        grad, unit = norm_back(R.x0[here, :], R.gains[0:1, :], da)
        R.dx0[here, :] = (R.dmid[here, :] + grad).astype(LOW)
        R.norms[0:1, :] += jnp.sum(da * unit, 0, keepdims=True)
        R.norms[1:2, :] += jnp.sum(da, 0, keepdims=True)

    strips(tokens, 32, first_back)

    dx0 = R.dx0[...]
    grad_mixed = dot_nt(dx0, R.winf[...].astype(LOW))
    sig = R.sig[...]
    grad_unit = grad_mixed * lax.rsqrt(1.0 + sig * sig)
    rows = R.rows[...].astype(F32)
    inverse = lax.rsqrt(jnp.mean(rows * rows, -1, keepdims=True) + EPS_NORM)
    unit = rows * inverse
    grad_rows = inverse * (grad_unit - unit * jnp.mean(grad_unit * unit, -1, keepdims=True))
    for step in range(1, size):
        give(step).wait_send()
    R.give[...] = dot_tn(R.pick[...], grad_rows.astype(LOW)).astype(LOW)

    def spot(index):
        return R.inc.at[mp.me, pl.ds(pl.multiple_of(index * cap, cap), cap)]

    back, back_wait = far_copies(
        dp,
        lambda dest, source: (block_rows(R.give, cap)(dest), spot(source)),
        R.back_send,
        R.back_recv,
    )
    for step in range(1, size):
        back(step).start()
    R.inc[mp.me, mine, :] = R.give[mine, :]

    grad_win = dot_tn(R.mixed[...], dx0)
    norms = jnp.concatenate([R.norms[0:4, :], jnp.zeros((12, model), F32)], 0).astype(LOW)
    for index in range(size):
        piece = grad_win[index * rin : (index + 1) * rin, :]
        if rin_up > rin:
            piece = jnp.concatenate([piece, jnp.zeros((rin_up - rin, model), F32)], 0)
        R.gw[index, :rin_up, :] = piece.astype(LOW)
        R.gw[index, rin_up:, :] = norms
    small.trade_all()
    named = Gather(mp, lambda index: R.idx.at[index], R.id_send, R.id_recv)
    named.start()

    for step in range(max(2, dp.far - 1), dp.far):
        up.pass_on(step)
        down.pass_on(step)

    back_wait()
    rows_in = Gather(mp, lambda index: R.inc.at[index], R.in_send, R.in_recv)
    rows_in.start()

    out.arrive()

    def finish(row):
        here = pl.ds(row, 32)
        R.out[here, :] = (R.out[here, :] + out.total(here)) * scale_at(here)

    strips(tokens, 32, finish)

    for step in range(1, dp.far):
        first_w.pass_on(step)
    for step in range(1, dp.far):
        small.pass_on(step)
    named.relays()
    rows_in.relays()

    def sum_to(scatter, ref):
        scatter.arrive()

        def add(row):
            here = pl.ds(row, 16)
            ref[here, :] = scatter.total(here).astype(ref.dtype)

        strips(scatter.rows, 16, add)

    sum_to(up, R.red_up)
    sum_to(down, R.red_dn)
    sum_to(small, R.wsum.at[mp.me])
    weights_in = Gather(mp, lambda index: R.wsum.at[index], R.ws_send, R.ws_recv)
    weights_in.start()
    sum_to(first_w, R.red_a)
    weights_in.relays()
    weights_in.close()
    red = R.wsum[0].astype(F32)
    for index in range(1, mp.size):
        red = red + R.wsum[index].astype(F32)
    R.red_w[...] = red
    rows_in.close()
    named.close()
    for thing in (win, ln, wc, dxg, *ag, *mg, out, das, up, down, first_w, small):
        thing.drain()
    for thing in (named, rows_in, weights_in):
        thing.drain()
    for step in range(1, size):
        ask(step).wait_send()
        back(step).wait_send()


def run_layer(seq_len, cap, ids, levels, noise, cot, table, w_in, ln_params, w_qkv, w_out, w_up, w_down):
    dp, mp = lax.axis_size("dp"), lax.axis_size("mp")
    tokens, width = noise.shape
    model = cot.shape[1]
    rin = w_in.shape[0]
    heads_w = w_qkv.shape[2]
    strip, hidden = w_up.shape
    group = tokens * mp
    spots = dp * cap
    wide = round_up(rin, 16) + 16
    far, far_dp = mp // 2, dp // 2
    in_kind = LOW if rin % 16 == 0 else F32
    vmem = pl.BlockSpec(memory_space=pltpu.VMEM)
    inputs = dict(
        ids=(ids, vmem),
        levels=(levels, pl.BlockSpec(memory_space=pltpu.SMEM)),
        noise=(noise, vmem),
        cot=(cot, vmem),
        table=(table, pl.BlockSpec(memory_space=pl.ANY)),
        w_in=(w_in, vmem),
        ln_params=(ln_params, vmem),
        w_qkv=(w_qkv, vmem),
        w_out=(w_out, vmem),
        w_up=(w_up, vmem),
        w_down=(w_down, vmem),
    )
    outputs = dict(
        out=((tokens, model), F32),
        red_up=((strip, hidden), F32),
        red_dn=((strip, hidden), F32),
        red_a=((strip, 4 * heads_w), F32),
        red_w=((wide, model), F32),
        inc=((mp, spots, width), LOW),
        idx=((mp, dp, 8, 128), F32),
    )
    buffers = dict(
        tab=((2, 512, width), F32),
        ask=((dp, 8, 128), F32),
        loc=((spots, 128), jnp.int32),
        give=((spots, width), LOW),
        got=((spots, width), LOW),
        lnf=((dp, 8, ln_params.shape[1]), F32),
        gains=((8, model), F32),
        sig=((tokens, 1), F32),
        pick=((tokens, spots), LOW),
        rows=((tokens, width), LOW),
        mixed=((tokens, width), LOW),
        x0=((tokens, model), F32),
        a=((group, model), LOW),
        c=((group, model), LOW),
        dx=((group, model), LOW),
        dmid=((tokens, model), F32),
        dmid_all=((group, model), LOW),
        winf=((rin * dp, model), in_kind),
        waf=((model, 4 * heads_w), LOW),
        wbf=((model, hidden), LOW),
        wcf=((model, hidden), LOW),
        qkv=((group, 3 * heads_w), LOW),
        o=((group, heads_w), LOW),
        low=((tokens, heads_w), LOW),
        part=((group, model), LOW),
        first=((far * tokens, model), LOW),
        fold=((far * tokens, model), LOW),
        second=((far * tokens, model), LOW),
        fold_far=((far * tokens, model), LOW),
        h=((tokens, hidden), F32),
        dh=((tokens, hidden), F32),
        hb=((group, hidden), LOW),
        dhb=((group, hidden), LOW),
        gdn=((model, hidden), LOW),
        dx0=((tokens, model), LOW),
        norms=((8, model), F32),
        gw=((dp, wide, model), LOW),
        up_first=((far_dp * strip, hidden), LOW),
        up_second=((far_dp * strip, hidden), LOW),
        dn_first=((far_dp * strip, hidden), LOW),
        dn_second=((far_dp * strip, hidden), LOW),
        wa_first=((far_dp * strip, 4 * heads_w), LOW),
        wa_second=((far_dp * strip, 4 * heads_w), LOW),
        w_first=((far_dp, wide, model), LOW),
        w_second=((far_dp, wide, model), LOW),
        wsum=((mp, wide, model), LOW),
    )
    sems = dict(tab=2)
    for name in ("win", "ln", "wa", "wx", "wb", "wc", "ask", "give", "back", "up", "dn", "ga", "gw"):
        sems[name + "_send"] = sems[name + "_recv"] = dp
    for name in ("dx", "a", "b", "c", "d", "e", "f", "as", "os", "cs", "ds", "id", "in", "ws"):
        sems[name + "_send"] = sems[name + "_recv"] = mp
    sems = {("tab_sem" if name == "tab" else name): count for name, count in sems.items()}
    names = [*inputs, *outputs, *buffers, *sems]
    return pl.pallas_call(
        functools.partial(layer_kernel, seq_len, cap, names),
        out_shape=[jax.ShapeDtypeStruct(shape, kind) for shape, kind in outputs.values()],
        in_specs=[spec for _, spec in inputs.values()],
        out_specs=[vmem] * len(outputs),
        scratch_shapes=[
            *[pltpu.VMEM(shape, kind) for shape, kind in buffers.values()],
            *[pltpu.SemaphoreType.DMA((count,)) for count in sems.values()],
        ],
        compiler_params=pltpu.CompilerParams(
            vmem_limit_bytes=VMEM_BYTES, collective_id=1, has_side_effects=True
        ),
        name="layer",
    )(*[value for value, _ in inputs.values()])


def direction_of(weight, gradient, first, second):
    first_new = BETA_ONE * first + (1.0 - BETA_ONE) * gradient
    second_new = BETA_TWO * second + (1.0 - BETA_TWO) * gradient * gradient
    second_hat = second_new * (1.0 / (1.0 - BETA_TWO**STEP))
    inverse = lax.rsqrt(second_hat)
    root = second_hat * inverse + EPS_ADAM
    inverse = inverse * (2.0 - root * inverse)
    inverse = inverse * (2.0 - root * inverse)
    direction = first_new * (1.0 / (1.0 - BETA_ONE**STEP)) * inverse + DECAY * weight
    return first_new, second_new, direction


def total_of(values):
    return jnp.sum(jnp.sum(values, 0, keepdims=True), 1, keepdims=True)


def moments_kernel(tile, turns, names, *refs):
    R = types.SimpleNamespace(**dict(zip(names, refs)))
    turn = pl.program_id(0)

    @pl.when(turn == 0)
    def _():
        R.sums[...] = jnp.zeros_like(R.sums)

    once = jnp.where(lax.axis_index("mp") == 0, 1.0, 0.0)
    lane = lax.broadcasted_iota(jnp.int32, (1, 128), 1)

    def put(place, weight, direction, factor=None):
        for row, values in ((0, weight), (1, direction)):
            total = total_of(values * values)
            if factor is not None:
                total = total * factor
            R.sums[row : row + 1, :] += jnp.where(lane == place, total, 0.0)

    def update(name, here, gradient, place, factor=None):
        weight = getattr(R, name)[here]
        first_new, second_new, direction = direction_of(
            weight, gradient, getattr(R, name + "_m")[here], getattr(R, name + "_v")[here]
        )
        getattr(R, name + "_m_new")[here] = first_new
        getattr(R, name + "_v_new")[here] = second_new
        getattr(R, name + "_u")[here] = direction
        if place is not None:
            put(place, weight, direction, factor)
        return weight, direction

    spots = R.named.shape[1]
    part = tile // 5 if tile % 40 == 0 else tile

    def table_part(row):
        here = pl.ds(row, part)
        base = turn * tile + row
        hit = lax.broadcasted_iota(jnp.int32, (part, spots), 0) + base == R.named[...]
        gradient = dot(jnp.where(hit, 1.0, 0.0).astype(LOW), R.inc[...])
        update("table", (here, slice(None)), gradient, 0, once)

    strips(tile, part, table_part)

    strip, heads_w = R.qkv.shape[1:]
    share = R.qkv.shape[1]
    for group in range(3):
        update(
            "qkv",
            (group, slice(None), slice(None)),
            R.red_a[:, group * heads_w : (group + 1) * heads_w],
            6 + group,
        )
    update("up", (slice(None), slice(None)), R.red_up[...], 10)
    update("down", (slice(None), slice(None)), R.red_dn[...].T, 11)

    @pl.when(turn == 0)
    def _():
        everything = (slice(None), slice(None))
        update("out", everything, R.red_out[...].T, 9)
        update("w_in", everything, R.red_in[...], 1, once)
        weight, direction = update("ln", everything, R.red_ln[...], None)
        for row in range(4):
            put(2 + row, weight[row : row + 1, :], direction[row : row + 1, :], once)


def tiles_of(rows, parts):
    return [
        turns
        for turns in (5, 4, 2, 1)
        if rows % turns == 0
        and (rows // turns) % 8 == 0
        and all(size % turns == 0 and (size // turns) % step == 0 for size, step in parts)
    ][0]


def run_moments(weights, moments, named, inc, red_up, red_dn, red_a, red_w, strip, first_row):
    names = ("table", "w_in", "ln", "qkv", "out", "up", "down")
    by_name = dict(zip(names, weights))
    rows, width = by_name["table"].shape
    hidden = by_name["down"].shape[0]
    heads_w = by_name["qkv"].shape[2]
    rin = by_name["w_in"].shape[0]
    turns = tiles_of(rows, ((strip, 8), (hidden, 128)))
    tile = rows // turns
    specs = dict(
        table=pl.BlockSpec((tile, width), lambda turn: (turn, 0)),
        w_in=pl.BlockSpec(by_name["w_in"].shape, lambda turn: (0, 0)),
        ln=pl.BlockSpec(by_name["ln"].shape, lambda turn: (0, 0)),
        qkv=pl.BlockSpec((3, strip // turns, heads_w), lambda turn: (0, turn, 0)),
        out=pl.BlockSpec(by_name["out"].shape, lambda turn: (0, 0)),
        up=pl.BlockSpec((strip // turns, hidden), lambda turn: (turn, 0)),
        down=pl.BlockSpec((hidden // turns, strip), lambda turn: (turn, 0)),
    )
    inputs = {}
    for name, weight, (first, second) in zip(names, weights, moments):
        inputs[name] = (weight, specs[name])
        inputs[name + "_m"] = (first, specs[name])
        inputs[name + "_v"] = (second, specs[name])
    whole = lambda array: pl.BlockSpec(array.shape, lambda turn: (0,) * array.ndim)
    red_out = red_a[:, 3 * heads_w :]
    red_in = red_w[:rin]
    red_ln = lax.dynamic_slice(
        red_w, (round_up(rin, 16), lax.axis_index("dp") * strip), (4, strip)
    )
    inputs["named"] = (named, whole(named))
    inputs["inc"] = (inc, whole(inc))
    inputs["red_up"] = (red_up, specs["up"])
    inputs["red_dn"] = (red_dn, pl.BlockSpec((strip, hidden // turns), lambda turn: (0, turn)))
    inputs["red_a"] = (red_a, pl.BlockSpec((strip // turns, 4 * heads_w), lambda turn: (turn, 0)))
    inputs["red_out"] = (red_out, whole(red_out))
    inputs["red_in"] = (red_in, whole(red_in))
    inputs["red_ln"] = (red_ln, whole(red_ln))
    outputs = {}
    for name, weight in by_name.items():
        for kind in ("_m_new", "_v_new", "_u"):
            outputs[name + kind] = (weight.shape, specs[name])
    outputs["sums"] = ((8, 128), pl.BlockSpec((8, 128), lambda turn: (0, 0)))
    results = pl.pallas_call(
        functools.partial(moments_kernel, tile, turns, [*inputs, *outputs]),
        grid=(turns,),
        out_shape=[jax.ShapeDtypeStruct(shape, F32) for shape, _ in outputs.values()],
        in_specs=[spec for _, spec in inputs.values()],
        out_specs=[spec for _, spec in outputs.values()],
        compiler_params=pltpu.CompilerParams(vmem_limit_bytes=VMEM_BYTES),
        name="moments",
    )(*[value for value, _ in inputs.values()])
    return dict(zip(outputs, results)), turns, specs


def weights_kernel(names, *refs):
    R = types.SimpleNamespace(**dict(zip(names, refs)))
    norms = jnp.sqrt(R.totals[...])
    factors = norms[0:1, :] / (norms[1:2, :] + EPS_ADAM)
    R.norms[...] = norms[0:2, 0:12]

    def factor(place):
        return RATE * factors[0:1, place : place + 1]

    for name, place in (("table", 0), ("w_in", 1), ("out", 9), ("up", 10), ("down", 11)):
        new, old, direction = (getattr(R, name + kind) for kind in ("_new", "", "_u"))
        new[...] = old[...] - factor(place) * direction[...]
    for row in range(4):
        here = slice(row, row + 1)
        R.ln_new[here, :] = R.ln[here, :] - factor(2 + row) * R.ln_u[here, :]
    for part in range(3):
        R.qkv_new[part] = R.qkv[part] - factor(6 + part) * R.qkv_u[part]


def run_weights(totals, weights, results, turns, specs):
    names = ("table", "w_in", "ln", "qkv", "out", "up", "down")
    inputs = {"totals": (totals, pl.BlockSpec((8, 128), lambda turn: (0, 0)))}
    outputs = {}
    for name, weight in zip(names, weights):
        inputs[name] = (weight, specs[name])
        inputs[name + "_u"] = (results[name + "_u"], specs[name])
        outputs[name + "_new"] = (weight.shape, specs[name])
    outputs["norms"] = ((2, 12), pl.BlockSpec((2, 12), lambda turn: (0, 0)))
    made = pl.pallas_call(
        functools.partial(weights_kernel, [*inputs, *outputs]),
        grid=(turns,),
        out_shape=[jax.ShapeDtypeStruct(shape, F32) for shape, _ in outputs.values()],
        in_specs=[spec for _, spec in inputs.values()],
        out_specs=[spec for _, spec in outputs.values()],
        compiler_params=pltpu.CompilerParams(vmem_limit_bytes=VMEM_BYTES),
        name="new_weights",
    )(*[value for value, _ in inputs.values()])
    return dict(zip(outputs, made))


def totals_kernel(values_ref, out_ref, near_ref, wide_ref, dp_send, dp_recv, mp_send, mp_recv):
    dp, mp = Line("dp"), Line("mp")
    meet([], [dp, mp])
    near_ref[dp.me] = values_ref[...]

    def to_dp(step):
        block = near_ref.at[dp.me]
        return dp.push(
            lax.rem(dp.me + step, dp.size), block, block, dp_send.at[step], dp_recv.at[dp.me]
        )

    def to_mp(step):
        block = wide_ref.at[mp.me]
        return mp.push(
            lax.rem(mp.me + step, mp.size), block, block, mp_send.at[step], mp_recv.at[mp.me]
        )

    for step in range(1, dp.size):
        to_dp(step).start()
    for step in range(1, dp.size):
        source = lax.rem(dp.me + step, dp.size)
        block = near_ref.at[source]
        dp.push(dp.partner, block, block, dp_send.at[0], dp_recv.at[source]).wait_recv()
    wide_ref[mp.me] = jnp.sum(near_ref[...], 0)
    for step in range(1, mp.size):
        to_mp(step).start()
    for step in range(1, mp.size):
        source = lax.rem(mp.me + step, mp.size)
        block = wide_ref.at[source]
        mp.push(mp.partner, block, block, mp_send.at[0], mp_recv.at[source]).wait_recv()
    out_ref[...] = jnp.sum(wide_ref[...], 0)
    for step in range(1, dp.size):
        to_dp(step).wait_send()
    for step in range(1, mp.size):
        to_mp(step).wait_send()


def run_totals(values):
    dp, mp = lax.axis_size("dp"), lax.axis_size("mp")
    vmem = pl.BlockSpec(memory_space=pltpu.VMEM)
    return pl.pallas_call(
        totals_kernel,
        out_shape=jax.ShapeDtypeStruct((8, 128), F32),
        in_specs=[vmem],
        out_specs=vmem,
        scratch_shapes=[
            pltpu.VMEM((dp, 8, 128), F32),
            pltpu.VMEM((mp, 8, 128), F32),
            *Gather.sems(dp),
            *Gather.sems(mp),
        ],
        compiler_params=pltpu.CompilerParams(collective_id=2, has_side_effects=True),
        name="totals",
    )(values)


def per_device(
    token_ids,
    levels,
    noise,
    cotangent,
    table,
    table_m,
    table_v,
    w_in,
    w_in_m,
    w_in_v,
    ln_params,
    ln_m,
    ln_v,
    w_qkv,
    qkv_m,
    qkv_v,
    w_out,
    out_m,
    out_v,
    w_up,
    up_m,
    up_v,
    w_down,
    down_m,
    down_v,
):
    dp_count = lax.axis_size("dp")
    seq_count, seq_len = token_ids.shape
    tokens = seq_count * seq_len
    model = cotangent.shape[2]
    table_rows = table.shape[0]
    strip = ln_params.shape[1]
    cap = round_up(max(2, (3 * tokens + 2 * dp_count - 1) // (2 * dp_count)), 16)
    out, red_up, red_dn, red_a, red_w, inc, idx = run_layer(
        seq_len,
        cap,
        token_ids,
        levels,
        noise.reshape(tokens, -1),
        cotangent.reshape(tokens, model),
        table,
        w_in,
        ln_params,
        w_qkv,
        w_out,
        w_up,
        w_down,
    )
    spots = inc.shape[0] * inc.shape[1]
    first_row = lax.axis_index("dp") * table_rows
    named = idx[:, :, 0, :cap].reshape(1, spots).astype(jnp.int32) - first_row
    weights = (table, w_in, ln_params, w_qkv, w_out, w_up, w_down)
    moments = (
        (table_m, table_v),
        (w_in_m, w_in_v),
        (ln_m, ln_v),
        (qkv_m, qkv_v),
        (out_m, out_v),
        (up_m, up_v),
        (down_m, down_v),
    )
    made, turns, specs = run_moments(
        weights, moments, named, inc.reshape(spots, -1), red_up, red_dn, red_a, red_w, strip, first_row
    )
    totals = run_totals(made["sums"])
    fresh = run_weights(totals, weights, made, turns, specs)
    results = [out.reshape(seq_count, seq_len, model)]
    for name in ("table", "w_in", "ln", "qkv", "out", "up", "down"):
        results += [fresh[name + "_new"], made[name + "_m_new"], made[name + "_v_new"]]
    results.append(fresh["norms"])
    return tuple(results)


def solution(mesh):
    return jax.shard_map(
        per_device,
        mesh=mesh,
        in_specs=(
            P(("dp", "mp"), None),
            P(("dp", "mp")),
            P(("dp", "mp"), None, None),
            P(("dp", "mp"), None, None),
            P("dp", None),
            P("dp", None),
            P("dp", None),
            P("dp", None),
            P("dp", None),
            P("dp", None),
            P(None, "dp"),
            P(None, "dp"),
            P(None, "dp"),
            P(None, "dp", "mp"),
            P(None, "dp", "mp"),
            P(None, "dp", "mp"),
            P("mp", "dp"),
            P("mp", "dp"),
            P("mp", "dp"),
            P("dp", "mp"),
            P("dp", "mp"),
            P("dp", "mp"),
            P("mp", "dp"),
            P("mp", "dp"),
            P("mp", "dp"),
        ),
        out_specs=(
            P(("dp", "mp"), None, None),
            P("dp", None),
            P("dp", None),
            P("dp", None),
            P("dp", None),
            P("dp", None),
            P("dp", None),
            P(None, "dp"),
            P(None, "dp"),
            P(None, "dp"),
            P(None, "dp", "mp"),
            P(None, "dp", "mp"),
            P(None, "dp", "mp"),
            P("mp", "dp"),
            P("mp", "dp"),
            P("mp", "dp"),
            P("dp", "mp"),
            P("dp", "mp"),
            P("dp", "mp"),
            P("mp", "dp"),
            P("mp", "dp"),
            P("mp", "dp"),
            P(),
        ),
        check_vma=False,
    )
```

```python
import functools
import types

import jax
import jax.numpy as jnp
from jax import lax
from jax.experimental import pallas as pl
from jax.experimental.pallas import tpu as pltpu
from jax.sharding import PartitionSpec as P

HD = 64
LEVELS = 64
STEP = 10


EPS_NORM = 1e-06
EPS_LAYER = 1e-05
EPS_ADAM = 1e-06
BETA_ONE = 0.9
BETA_TWO = 0.999
DECAY = 0.01
RATE = 0.5
SIGMA_TOP = 10.0

F32 = jnp.float32
LOW = jnp.bfloat16
VMEM_BYTES = 60 * 1024 * 1024


def sigma_of(levels):
    frac = levels.astype(jnp.float32) / (LEVELS - 1)
    return jnp.exp(frac * jnp.log(SIGMA_TOP))


def lamb_moments(weight, gradient, first, second):
    first_new = BETA_ONE * first + (1.0 - BETA_ONE) * gradient
    second_new = BETA_TWO * second + (1.0 - BETA_TWO) * gradient * gradient
    first_hat = first_new / (1.0 - BETA_ONE**STEP)
    second_hat = second_new / (1.0 - BETA_TWO**STEP)
    direction = first_hat / (jnp.sqrt(second_hat) + EPS_ADAM) + DECAY * weight
    return (first_new, second_new, direction)


def trust_factors(ratio):
    return (
        ratio[0],
        ratio[1],
        ratio[2:6][:, None],
        ratio[6:9][:, None, None],
        ratio[9],
        ratio[10],
        ratio[11],
    )


def round_up(value, step):
    return -(-value // step) * step


def dot(left, right):
    return jnp.dot(left, right, preferred_element_type=F32)


def dot_nt(left, right):
    return lax.dot_general(left, right, (((1,), (1,)), ((), ())), preferred_element_type=F32)


def dot_tn(left, right):
    return lax.dot_general(left, right, (((0,), (0,)), ((), ())), preferred_element_type=F32)


def strips(total, step, body, unroll=1):
    step = min(step, total)

    def one(turn, carry):
        body(pl.multiple_of(turn * step, step))
        return carry

    lax.fori_loop(0, total // step, one, 0, unroll=unroll)


class Line:
    def __init__(self, axis):
        self.axis = axis
        self.size = lax.axis_size(axis)
        self.far = self.size // 2
        self.me = lax.axis_index(axis)
        self.hi = lax.div(self.me, 2)
        self.lo = lax.rem(self.me, 2)
        self.partner = self.hi * 2 + (1 - self.lo)

    def at(self, step):
        return lax.rem(self.hi + step + self.far, self.far)

    def push(self, index, src, dst, send, recv):
        return pltpu.make_async_remote_copy(
            src_ref=src,
            dst_ref=dst,
            send_sem=send,
            recv_sem=recv,
            device_id={self.axis: index},
            device_id_type=pl.DeviceIdType.MESH,
        )

    def signal(self, sem, index):
        pl.semaphore_signal(
            sem, inc=1, device_id={self.axis: index}, device_id_type=pl.DeviceIdType.MESH
        )


def meet(pair_lines, all_lines=()):
    sem = pltpu.get_barrier_semaphore()
    count = 0
    for line in pair_lines:
        for step in range(1, line.far):
            line.signal(sem, line.at(step) * 2 + line.lo)
            count += 1
        line.signal(sem, line.partner)
        count += 1
    for line in all_lines:
        for step in range(1, line.size):
            line.signal(sem, lax.rem(line.me + step, line.size))
            count += 1
    pl.semaphore_wait(sem, count)


class Gather:
    def __init__(self, line, at, send, recv, base=0):
        self.line, self.at, self.send, self.recv, self.base = line, at, send, recv, base

    def copy(self, index, slot, dest):
        block = self.at(index)
        return self.line.push(
            dest, block, block, self.send.at[self.base + slot], self.recv.at[self.base + index]
        )

    def start_far(self):
        line = self.line
        for step in range(1, line.far):
            self.copy(line.me, step - 1, line.at(step) * 2 + line.lo).start()

    def start_near(self):
        self.copy(self.line.me, self.line.far - 1, self.line.partner).start()

    def start(self):
        self.start_far()
        self.start_near()

    def relay(self, step):
        line = self.line
        handed = self.copy(line.at(-step) * 2 + line.lo, line.far - 1 + step, line.partner)
        handed.wait_recv()
        handed.start()

    def relays(self):
        for step in range(1, self.line.far):
            self.relay(step)

    def close(self):
        line = self.line
        for step in range(line.far):
            self.copy(line.at(-step) * 2 + (1 - line.lo), 0, line.partner).wait_recv()

    def drain(self):
        for slot in range(2 * self.line.far - 1):
            self.copy(self.line.me, slot, self.line.partner).wait_send()


class Scatter:
    def __init__(self, line, part, first, second, send, recv, rows, base=0):
        self.line, self.part, self.first, self.second = line, part, first, second
        self.send, self.recv, self.rows, self.base = send, recv, rows, base

    def traded(self, hi):
        line = self.line
        return line.push(
            line.partner,
            self.part(hi * 2 + (1 - line.lo)),
            self.first(hi),
            self.send.at[self.base + hi],
            self.recv.at[self.base + hi],
        )

    def passed(self, step):
        line = self.line
        hi = line.at(step)
        return line.push(
            hi * 2 + line.lo,
            self.part(hi * 2 + line.lo),
            self.second(line.hi),
            self.send.at[self.base + line.far + step - 1],
            self.recv.at[self.base + line.far + line.hi],
        )

    def trade(self, hi):
        self.traded(hi).start()

    def trade_all(self):
        for step in range(1, self.line.far + 1):
            self.trade(self.line.at(step))

    def pass_on(self, step):
        line = self.line
        hi = line.at(step)
        self.traded(hi).wait_recv()
        mine, other = self.part(hi * 2 + line.lo), self.first(hi)

        def add(row):
            here = pl.ds(row, 16)
            mine[here, :] = (mine[here, :].astype(F32) + other[here, :].astype(F32)).astype(LOW)

        strips(self.rows, 16, add)
        self.passed(step).start()

    def arrive(self):
        line = self.line
        self.traded(line.hi).wait_recv()
        for step in range(1, line.far):
            hi = line.at(-step)
            line.push(
                line.partner,
                self.second(hi),
                self.second(hi),
                self.send.at[self.base],
                self.recv.at[self.base + line.far + hi],
            ).wait_recv()

    def total(self, here):
        line = self.line
        value = self.part(line.me)[here, :].astype(F32) + self.first(line.hi)[here, :].astype(F32)
        for step in range(1, line.far):
            value = value + self.second(line.at(-step))[here, :].astype(F32)
        return value

    def drain(self):
        line = self.line
        for step in range(line.far):
            self.traded(line.at(step)).wait_send()
        for step in range(1, line.far):
            self.passed(step).wait_send()


def block_rows(ref, rows, first=0):
    return lambda index: ref.at[pl.ds(pl.multiple_of((index + first) * rows, rows), rows)]


def part_rows(ref, rows, first, count):
    return lambda index: ref.at[pl.ds(pl.multiple_of(index * rows + first, count), count)]


def of_index(ref):
    return lambda index: ref.at[index]


def norm_rows(values):
    center = values - jnp.mean(values, -1, keepdims=True)
    spread = jnp.mean(center * center, -1, keepdims=True)
    inverse = lax.rsqrt(spread + EPS_LAYER)
    return center * inverse, inverse


def norm_back(values, gain, grad):
    unit, inverse = norm_rows(values)
    inner = grad * gain
    shared = jnp.mean(inner, -1, keepdims=True)
    along = jnp.mean(inner * unit, -1, keepdims=True)
    return inverse * (inner - shared - unit * along), unit


def head_masks(width):
    lane = lax.broadcasted_iota(jnp.int32, (1, width), 1)
    return [
        jnp.where((lane >= head * HD) & (lane < (head + 1) * HD), 1.0, 0.0)
        for head in range(width // HD)
    ]


def spread_heads(values, masks):
    return jnp.concatenate([values * mask.astype(LOW) for mask in masks], 0)


def join_heads(values, masks, rows):
    total = values[0:rows] * masks[0]
    for head in range(1, len(masks)):
        total = total + values[head * rows : (head + 1) * rows] * masks[head]
    return total


def softmax_rows(queries, keys):
    scores = dot_nt(queries, keys) * (HD ** (-0.5))
    raised = jnp.exp(scores - jnp.max(scores, -1, keepdims=True))
    return raised * (1.0 / jnp.sum(raised, -1, keepdims=True))


def far_copies(line, make, sends, recvs):
    def copy(step):
        dest = lax.rem(line.me + step, line.size)
        src, dst = make(dest, line.me)
        return line.push(dest, src, dst, sends.at[step], recvs.at[line.me])

    def wait():
        for step in range(1, line.size):
            source = lax.rem(line.me + line.size - step, line.size)
            _, dst = make(source, source)
            line.push(line.partner, dst, dst, sends.at[0], recvs.at[source]).wait_recv()

    return copy, wait


def layer_kernel(cap, names, *refs):
    R = types.SimpleNamespace(**dict(zip(names, refs)))
    dp, mp = Line("dp"), Line("mp")
    size, ways = dp.size, mp.size
    seqs, seq_len = R.ids.shape
    tokens, width = R.noise.shape
    model = R.cot.shape[1]
    heads_w = R.o.shape[1]
    hidden = R.wbf.shape[1]
    table_rows = R.table.shape[0]
    rin = R.w_in.shape[0]
    rin_up = round_up(rin, 16)
    quarter = model // ways
    strip = R.w_up.shape[0]
    spots = size * cap
    far = mp.far
    count = seqs * far
    own_strip = pl.ds(pl.multiple_of(dp.me * strip, strip), strip)
    mine = pl.ds(pl.multiple_of(dp.me * cap, cap), cap)

    def rows_of(piece):
        return lambda row: pl.ds(pl.multiple_of(piece * seq_len + row, 16), 16)

    def own_rows(piece):
        first = pl.multiple_of((piece * ways + mp.me) * seq_len, seq_len)
        return lambda row: pl.ds(pl.multiple_of(first + row, 16), 16)

    def halves(ref, send, recv):
        return [
            Gather(mp, block_rows(ref, seq_len, piece * ways), send, recv, piece * ways)
            for piece in range(seqs)
        ]

    def sums(part, first, second, send, recv):
        return lambda piece: Scatter(
            mp,
            block_rows(part, seq_len, piece * ways),
            block_rows(first, seq_len, piece * far),
            block_rows(second, seq_len, piece * far),
            send,
            recv,
            seq_len,
            piece * ways,
        )

    def turns(body, hooks):
        def one(turn, carry):
            for place, action in hooks:
                pl.when(turn == place)(action)
            piece = lax.div(turn, far)
            hi = lax.rem(mp.hi + lax.rem(turn, far) + 1, far)
            base = pl.multiple_of((piece * ways + 2 * hi) * seq_len, 2 * seq_len)
            body(turn, piece, hi, base)
            return carry

        lax.fori_loop(0, count, one, 0)

    def hand_on(scatter, turn):
        step = lax.rem(turn, far)

        @pl.when(step != 0)
        def _():
            scatter.pass_on(step)

    def later_pieces(gathers):
        hooks = []
        for piece in range(1, seqs):
            hooks.append((piece * far - 1, gathers[piece].relays))
            hooks.append((piece * far, gathers[piece].close))
        return hooks

    def early_ends(end):
        return [((piece + 2) * far - 1, functools.partial(end, piece)) for piece in range(seqs - 1)]

    chunk = R.tab.shape[1]
    pieces = -(-table_rows // chunk)

    def fetch(piece):
        rows = min(chunk, table_rows - piece * chunk)
        return pltpu.make_async_copy(
            R.table.at[pl.ds(piece * chunk, rows)],
            R.tab.at[piece % 2, pl.ds(0, rows)],
            R.tab_sem.at[piece % 2],
        )

    for piece in range(min(2, pieces)):
        fetch(piece).start()

    eye = lax.broadcasted_iota(jnp.int32, (seq_len, seq_len), 0) == lax.broadcasted_iota(
        jnp.int32, (seq_len, seq_len), 1
    )
    id_rows = R.ids[...].astype(F32)
    ids = jnp.concatenate(
        [
            jnp.sum(jnp.where(eye, id_rows[seq : seq + 1, :], 0.0), 1, keepdims=True)
            for seq in range(seqs)
        ],
        0,
    )
    lane = lax.broadcasted_iota(jnp.int32, (tokens, 128), 1).astype(F32)
    low_end = lane * float(table_rows)
    owned = jnp.where((ids >= low_end) & (ids < low_end + float(table_rows)), 1.0, 0.0)
    before = jnp.where(
        lax.broadcasted_iota(jnp.int32, (tokens, tokens), 0)
        >= lax.broadcasted_iota(jnp.int32, (tokens, tokens), 1),
        1.0,
        0.0,
    )
    ranks = dot(before.astype(LOW), owned.astype(LOW))
    rank = jnp.sum(owned * ranks, 1, keepdims=True) - 1.0
    slot = jnp.sum(owned * lane, 1, keepdims=True) * cap + rank
    placed = jnp.where(lane == rank, 1.0, 0.0)
    upper = jnp.floor(ids * (1.0 / 256.0))
    lower = ids - upper * 256.0
    parts = jnp.concatenate([placed * upper, placed * lower, placed], 1).astype(LOW)
    asked = dot_tn(owned.astype(LOW), parts)
    asked = asked[:, :128] * 256.0 + asked[:, 128:256] + asked[:, 256:] - 1.0
    for index in range(size):
        R.ask[index] = jnp.broadcast_to(asked[index : index + 1, :], (8, 128))
    R.idx[mp.me, dp.me] = R.ask[dp.me]

    meet([mp], [dp])
    ask, ask_wait = far_copies(
        dp,
        lambda dest, source: (R.ask.at[dest], R.idx.at[mp.me, source]),
        R.ask_send,
        R.ask_recv,
    )
    for step in range(1, size):
        ask(step).start()

    mine_in = R.winf.at[mp.me]
    win = Gather(dp, block_rows(mine_in, rin), R.win_send, R.win_recv)
    win_all = Gather(mp, of_index(R.winf), R.wim_send, R.wim_recv)
    ln = Gather(dp, of_index(R.lnf), R.ln_send, R.ln_recv)
    half_strip = strip // 2
    wa = [
        Gather(dp, part_rows(R.waf, strip, piece * half_strip, half_strip), send, recv)
        for piece, send, recv in ((0, R.wa_send, R.wa_recv), (1, R.wx_send, R.wx_recv))
    ]
    wb = Gather(dp, block_rows(R.wbf, strip), R.wb_send, R.wb_recv)
    wc = Gather(dp, block_rows(R.wcf, strip), R.wc_send, R.wc_recv)
    dxg = halves(R.dx, R.dx_send, R.dx_recv)
    ag = halves(R.a, R.a_send, R.a_recv)
    cg = halves(R.c, R.c_send, R.c_recv)
    mg = halves(R.dmid_all, R.e_send, R.e_recv)

    mine_in[pl.ds(pl.multiple_of(dp.me * rin, rin), rin), :] = (
        R.w_in[:, pl.ds(pl.multiple_of(mp.me * quarter, quarter), quarter)]
        .astype(LOW)
        .astype(R.winf.dtype)
    )
    win.start()
    shares = R.ln_params[...].astype(LOW).astype(F32)
    R.lnf[dp.me] = jnp.concatenate([shares, jnp.zeros_like(shares)], 0)
    ln.start()
    for part in range(3):
        R.waf[own_strip, part * heads_w : (part + 1) * heads_w] = R.w_qkv[part].astype(LOW)
    R.waf[own_strip, 3 * heads_w :] = R.w_out[...].T.astype(LOW)
    wa[0].start()
    wa[1].start_near()

    for seq in range(seqs):
        level = jnp.full((seq_len, 1), R.levels[seq], jnp.int32).astype(F32) / (LEVELS - 1)
        R.sig[seq * seq_len : (seq + 1) * seq_len, :] = jnp.exp(level * jnp.log(SIGMA_TOP))

    def scale_at(here):
        sig = R.sig[here, :]
        return sig * lax.rsqrt(1.0 + sig * sig)

    for piece in range(seqs):
        here, there = rows_of(piece), own_rows(piece)

        def scale_cot(row, here=here, there=there):
            R.dx[there(row), :] = (R.cot[here(row), :].astype(F32) * scale_at(here(row))).astype(LOW)

        strips(seq_len, 16, scale_cot, 2)
        dxg[piece].start()
    R.wbf[own_strip, :] = R.w_up[...].astype(LOW)
    R.wcf[own_strip, :] = R.w_down[...].T.astype(LOW)
    R.pick[...] = jnp.where(
        lax.broadcasted_iota(jnp.int32, (tokens, spots), 1).astype(F32) == slot, 1.0, 0.0
    ).astype(LOW)
    ln.relays()
    win.relays()

    ask_wait()
    small_eye = lax.broadcasted_iota(jnp.int32, (cap, 128), 0) == lax.broadcasted_iota(
        jnp.int32, (cap, 128), 1
    )

    def locate(index, carry):
        row = R.idx[mp.me, index][0:1, :]
        column = jnp.sum(jnp.where(small_eye, row, 0.0), 1, keepdims=True)
        local = column.astype(jnp.int32) - dp.me * table_rows
        R.loc[pl.ds(pl.multiple_of(index * cap, cap), cap), :] = jnp.broadcast_to(local, (cap, 128))
        return carry

    lax.fori_loop(0, size, locate, 0)
    win.close()
    win_all.start()
    found = None
    for piece in range(pieces):
        fetch(piece).wait()
        rows = min(chunk, table_rows - piece * chunk)
        if rows < chunk:
            R.tab[piece % 2, rows:, :] = jnp.zeros((chunk - rows, width), F32)
        hit = (
            lax.broadcasted_iota(jnp.int32, (spots, chunk), 1) + piece * chunk == R.loc[:, 0:1]
        )
        more = dot(jnp.where(hit, 1.0, 0.0).astype(LOW), R.tab[piece % 2].astype(LOW))
        found = more if found is None else found + more
        if piece + 2 < pieces:
            fetch(piece + 2).start()
    R.give[...] = found.astype(LOW)

    give, give_wait = far_copies(
        dp,
        lambda dest, source: (block_rows(R.give, cap)(dest), block_rows(R.got, cap)(source)),
        R.give_send,
        R.give_recv,
    )
    for step in range(1, size):
        give(step).start()
    R.got[mine, :] = R.give[mine, :]
    wa[1].start_far()
    win_all.relays()
    wa[0].relays()
    ln.close()
    wide_ln = R.ln_params.shape[1]
    if wide_ln % 128 == 0:
        R.gains[...] = jnp.concatenate([R.lnf[index] for index in range(size)], 1)
    else:
        total = jnp.zeros((8, model), F32)
        for index in range(size):
            place = lax.broadcasted_iota(
                jnp.int32, (wide_ln, model), 1
            ) == index * wide_ln + lax.broadcasted_iota(jnp.int32, (wide_ln, model), 0)
            total = total + dot(R.lnf[index].astype(LOW), jnp.where(place, 1.0, 0.0).astype(LOW))
        R.gains[...] = total
    named = Gather(mp, of_index(R.idx), R.id_send, R.id_recv)

    give_wait()
    rows = dot(R.pick[...], R.got[...])
    R.rows[...] = rows.astype(LOW)
    sig = R.sig[...]
    unit = rows * lax.rsqrt(jnp.mean(rows * rows, -1, keepdims=True) + EPS_NORM)
    R.mixed[...] = ((unit + sig * R.noise[...].astype(F32)) * lax.rsqrt(1.0 + sig * sig)).astype(LOW)
    win_all.close()
    for index in range(ways):
        R.x0[:, index * quarter : (index + 1) * quarter] = dot(
            R.mixed[...], R.winf[index].astype(LOW)
        )

    for piece in range(seqs):
        here, there = rows_of(piece), own_rows(piece)

        def first_norm(row, here=here, there=there):
            normed, _ = norm_rows(R.x0[here(row), :])
            R.a[there(row), :] = (normed * R.gains[0:1, :] + R.gains[1:2, :]).astype(LOW)

        strips(seq_len, 16, first_norm, 2)
        ag[piece].start()
    wb.start()
    for gather in dxg:
        gather.relays()
    wa[1].relays()
    wc.start()
    named.start()
    ag[0].relays()
    for gather in (*wa, ag[0]):
        gather.close()

    att = sums(R.part, R.fold, R.fold_far, R.as_send, R.as_recv)
    dcs = sums(R.part, R.fold, R.fold_far, R.cs_send, R.cs_recv)
    das = sums(R.part, R.fold, R.fold_far, R.ds_send, R.ds_recv)
    out = sums(R.c, R.first, R.second, R.os_send, R.os_recv)
    masks = head_masks(heads_w)

    def attend(turn, piece, hi, base):
        here = pl.ds(base, 2 * seq_len)
        R.qkv[here, :] = dot(R.a[here, :], R.waf[:, : 3 * heads_w]).astype(LOW)
        for seq in range(2):
            rows = pl.ds(pl.multiple_of(base + seq * seq_len, seq_len), seq_len)
            queries = spread_heads(R.qkv[rows, :heads_w], masks)
            probs = softmax_rows(queries, R.qkv[rows, heads_w : 2 * heads_w]).astype(LOW)
            seen = dot(probs, R.qkv[rows, 2 * heads_w : 3 * heads_w])
            R.o[rows, :] = join_heads(seen, masks, seq_len).astype(LOW)
        hand_on(att(piece), turn)
        R.part[here, :] = dot_nt(R.o[here, :], R.waf[:, 3 * heads_w :]).astype(LOW)
        att(piece).trade(hi)

    def second_norm(piece):
        scatter, here, there = att(piece), rows_of(piece), own_rows(piece)
        scatter.arrive()

        def norm(row):
            x1 = R.x0[here(row), :] + scatter.total(pl.ds(row, 16))
            R.out[here(row), :] = x1
            normed, _ = norm_rows(x1)
            R.c[there(row), :] = (normed * R.gains[2:3, :] + R.gains[3:4, :]).astype(LOW)

        strips(seq_len, 16, norm, 2)
        cg[piece].start()

    turns(attend, [*later_pieces(ag), *early_ends(second_norm)])
    wb.relay(1)
    second_norm(seqs - 1)
    cg[0].relays()
    for step in range(2, dp.far):
        wb.relay(step)
    named.relays()
    wb.close()
    cg[0].close()
    for piece in range(seqs):
        att(piece).drain()

    def activate(turn, piece, hi, base):
        R.h[...] = dot(R.c[pl.ds(base, 2 * seq_len), :], R.wbf[...])

        def gelu(row):
            there = pl.ds(pl.multiple_of(base + row, 16), 16)
            step = min(256, hidden)
            for col in range(0, hidden, step):
                h = R.h[pl.ds(row, 16), col : col + step]
                gate = 0.5 + 0.5 * lax.erf(h * (0.5**0.5))
                slope = gate + h * (jnp.exp(-0.5 * h * h) * 0.3989422804014327)
                R.hb[there, col : col + step] = (h * gate).astype(LOW)
                R.slope[there, col : col + step] = slope.astype(LOW)

        strips(2 * seq_len, 16, gelu)

    turns(activate, later_pieces(cg))

    def spread(part, first, second, send, recv):
        return Scatter(
            dp,
            block_rows(part, strip),
            block_rows(first, strip),
            block_rows(second, strip),
            send,
            recv,
            strip,
        )

    up = spread(R.wbf, R.up_first, R.up_second, R.up_send, R.up_recv)
    down = spread(R.gdn, R.dn_first, R.dn_second, R.dn_send, R.dn_recv)
    first_w = spread(R.waf, R.wa_first, R.wa_second, R.ga_send, R.ga_recv)
    due = [(scatter, step) for scatter in (down, up) for step in range(1, dp.far)]

    def pass_due(number):
        for _ in range(min(number, len(due))):
            scatter, step = due.pop(0)
            scatter.pass_on(step)

    block = 2 * strip if (2 * strip) % 128 == 0 else min(256, model)

    def grads(make, trades):
        if block == 2 * strip:

            def turn_of(turn, carry):
                hi = lax.rem(dp.hi + turn + 1, dp.far)
                make(pl.ds(pl.multiple_of(hi * block, block), block))
                for scatter in trades:
                    scatter.trade(hi)
                return carry

            lax.fori_loop(0, dp.far, turn_of, 0)
        else:
            strips(model, block, lambda col: make(pl.ds(col, block)))
            for scatter in trades:
                scatter.trade_all()

    def down_grads(cols):
        R.gdn[cols, :] = dot_tn(R.dx[:, cols], R.hb[...]).astype(LOW)

    def up_grads(cols):
        R.wbf[cols, :] = dot_tn(R.c[:, cols], R.dhb[...]).astype(LOW)

    for gather in dxg:
        gather.close()
    grads(down_grads, ())
    wc.relays()
    down.trade_all()
    wc.close()

    def feed_back(turn, piece, hi, base):
        here = pl.ds(base, 2 * seq_len)
        R.h[...] = dot(R.dx[here, :], R.wcf[...])

        def bend(row):
            there = pl.ds(pl.multiple_of(base + row, 16), 16)
            R.dhb[there, :] = (R.h[pl.ds(row, 16), :] * R.slope[there, :].astype(F32)).astype(LOW)

        strips(2 * seq_len, 16, bend, 2)
        hand_on(dcs(piece), turn)
        R.part[here, :] = dot_nt(R.dhb[here, :], R.wbf[...]).astype(LOW)
        dcs(piece).trade(hi)

    R.norms[...] = jnp.zeros_like(R.norms)

    def second_back(piece):
        scatter, here, there = dcs(piece), rows_of(piece), own_rows(piece)
        scatter.arrive()

        def back(row):
            dc = scatter.total(pl.ds(row, 16))
            grad, unit = norm_back(R.out[here(row), :], R.gains[2:3, :], dc)
            grad = grad + R.cot[here(row), :].astype(F32) * scale_at(here(row))
            R.dmid[here(row), :] = grad
            R.dmid_all[there(row), :] = grad.astype(LOW)
            R.norms[2:3, :] += jnp.sum(dc * unit, 0, keepdims=True)
            R.norms[3:4, :] += jnp.sum(dc, 0, keepdims=True)

        strips(seq_len, 16, back, 2)
        mg[piece].start()

    turns(feed_back, early_ends(second_back))
    pass_due(1)
    for gather in (wb, *wa):
        gather.drain()
    grads(up_grads, (up,))
    second_back(seqs - 1)
    mg[0].relays()
    pass_due(1)
    mg[0].close()
    for piece in range(seqs):
        dcs(piece).drain()

    scale = HD ** (-0.5)

    def attend_back(turn, piece, hi, base):
        here = pl.ds(base, 2 * seq_len)
        R.low[...] = dot(R.dmid_all[here, :], R.waf[:, 3 * heads_w :]).astype(LOW)
        for seq in range(2):
            rows = pl.ds(pl.multiple_of(base + seq * seq_len, seq_len), seq_len)
            keys = R.qkv[rows, heads_w : 2 * heads_w]
            values = R.qkv[rows, 2 * heads_w : 3 * heads_w]
            queries = spread_heads(R.qkv[rows, :heads_w], masks)
            upper_grads = spread_heads(R.low[seq * seq_len : (seq + 1) * seq_len, :], masks)
            probs = softmax_rows(queries, keys)
            grad_probs = dot_nt(upper_grads, values)
            inner = jnp.sum(probs * grad_probs, -1, keepdims=True)
            grad_scores = (probs * (grad_probs - inner)).astype(LOW)
            R.qkv[rows, 2 * heads_w : 3 * heads_w] = dot_tn(probs.astype(LOW), upper_grads).astype(LOW)
            R.qkv[rows, heads_w : 2 * heads_w] = (dot_tn(grad_scores, queries) * scale).astype(LOW)
            R.qkv[rows, :heads_w] = (
                join_heads(dot(grad_scores, keys), masks, seq_len) * scale
            ).astype(LOW)
        hand_on(das(piece), turn)
        R.part[here, :] = dot_nt(R.qkv[here, :], R.waf[:, : 3 * heads_w]).astype(LOW)
        das(piece).trade(hi)

    def first_back(piece):
        scatter, here = das(piece), rows_of(piece)
        scatter.arrive()

        def back(row):
            da = scatter.total(pl.ds(row, 16))
            grad, unit = norm_back(R.x0[here(row), :], R.gains[0:1, :], da)
            R.dx0[here(row), :] = (R.dmid[here(row), :] + grad).astype(LOW)
            R.norms[0:1, :] += jnp.sum(da * unit, 0, keepdims=True)
            R.norms[1:2, :] += jnp.sum(da, 0, keepdims=True)

        strips(seq_len, 16, back, 2)

    turns(
        attend_back,
        [
            *later_pieces(mg),
            (count - 2, lambda: pass_due(1)),
            *early_ends(first_back),
            (count - 1, lambda: pass_due(1)),
        ],
    )

    def attend_grads(cols):
        R.waf[cols, : 3 * heads_w] = dot_tn(R.a[:, cols], R.qkv[...]).astype(LOW)
        R.waf[cols, 3 * heads_w :] = dot_tn(R.dmid_all[:, cols], R.o[...]).astype(LOW)

    grads(attend_grads, (first_w,))
    pass_due(1)
    first_back(seqs - 1)

    grad_mixed = sum(
        dot_nt(R.dx0[:, index * quarter : (index + 1) * quarter], R.winf[index].astype(LOW))
        for index in range(ways)
    )
    sig = R.sig[...]
    grad_unit = grad_mixed * lax.rsqrt(1.0 + sig * sig)
    rows = R.rows[...].astype(F32)
    inverse = lax.rsqrt(jnp.mean(rows * rows, -1, keepdims=True) + EPS_NORM)
    unit = rows * inverse
    grad_rows = inverse * (grad_unit - unit * jnp.mean(grad_unit * unit, -1, keepdims=True))
    for step in range(1, size):
        give(step).wait_send()
    R.give[...] = dot_tn(R.pick[...], grad_rows.astype(LOW)).astype(LOW)
    mine_inc = block_rows(R.inc, spots)(mp.me)
    back, back_wait = far_copies(
        dp,
        lambda dest, source: (block_rows(R.give, cap)(dest), block_rows(mine_inc, cap)(source)),
        R.back_send,
        R.back_recv,
    )
    for step in range(1, size):
        back(step).start()
    mine_inc[mine, :] = R.give[mine, :]

    small_mp = Scatter(
        mp, of_index(R.gm), of_index(R.gm_first), of_index(R.gm_second), R.gm_send, R.gm_recv, width + 16
    )
    for index in range(ways):
        cols = slice(index * quarter, (index + 1) * quarter)
        R.gm[index, :width, :] = dot_tn(R.mixed[...], R.dx0[:, cols]).astype(LOW)
        R.gm[index, width:, :] = jnp.concatenate(
            [R.norms[0:4, cols], jnp.zeros((12, quarter), F32)], 0
        ).astype(LOW)
    small_mp.trade_all()
    pass_due(1)
    for step in range(1, far):
        small_mp.pass_on(step)

    for gather in cg:
        gather.drain()

    def feed_out(turn, piece, hi, base):
        here = pl.ds(base, 2 * seq_len)
        R.c[here, :] = dot_nt(R.hb[here, :], R.wcf[...]).astype(LOW)
        out(piece).trade(hi)
        hand_on(out(piece), turn)

    turns(feed_out, [])

    back_wait()
    rows_in = Gather(mp, block_rows(R.inc, spots), R.in_send, R.in_recv)
    rows_in.start()
    pass_due(len(due))
    first_w.pass_on(1)

    small = Scatter(
        dp, of_index(R.gw), of_index(R.gw_first), of_index(R.gw_second), R.gw_send, R.gw_recv, rin_up + 16
    )
    small_mp.arrive()
    summed = small_mp.total(slice(None))
    for index in range(size):
        piece = summed[index * rin : (index + 1) * rin, :]
        if rin_up > rin:
            piece = jnp.concatenate([piece, jnp.zeros((rin_up - rin, quarter), F32)], 0)
        R.gw[index, :rin_up, :] = piece.astype(LOW)
        R.gw[index, rin_up:, :] = summed[width:, :].astype(LOW)
    small.trade_all()
    rows_in.relays()
    for step in range(2, dp.far):
        first_w.pass_on(step)
    for step in range(1, dp.far):
        small.pass_on(step)

    def finish_out(piece):
        scatter, here = out(piece), rows_of(piece)
        scatter.arrive()

        def finish(row):
            R.out[here(row), :] = (
                R.out[here(row), :] + scatter.total(pl.ds(row, 16))
            ) * scale_at(here(row))

        strips(seq_len, 16, finish, 2)

    for piece in range(seqs):
        finish_out(piece)

    named.close()
    rows_in.close()
    groups = ways * size
    spot = lax.broadcasted_iota(jnp.int32, (128, ways * spots), 1).astype(F32)
    block_no = jnp.floor((spot + 0.5) * (1.0 / cap))
    place = lax.broadcasted_iota(jnp.int32, (128, ways * spots), 0).astype(F32)
    spread_out = jnp.where(spot - block_no * cap == place, 1.0, 0.0).astype(LOW)
    named_row = jnp.zeros((1, ways * spots), F32)
    some = min(groups, 32)
    for first in range(0, groups, some):
        wanted = jnp.concatenate(
            [
                R.idx[index // size, index % size][0:1, :] + 1.0
                for index in range(first, first + some)
            ],
            0,
        )
        high = jnp.floor(wanted * (1.0 / 256.0))
        rest = wanted - 256.0 * high
        laid = dot(high.astype(LOW), spread_out) * 256.0 + dot(rest.astype(LOW), spread_out) - 1.0
        own_block = block_no[0:1, :] == first + lax.broadcasted_iota(
            jnp.int32, (some, ways * spots), 0
        ).astype(F32)
        named_row = named_row + jnp.sum(jnp.where(own_block, laid, 0.0), 0, keepdims=True)
    R.named[...] = jnp.broadcast_to(
        named_row.astype(jnp.int32) - dp.me * table_rows, (8, ways * spots)
    )
    tile = R.gtile.shape[1]
    tiles = R.gt.shape[0] // tile

    def store(index):
        return pltpu.make_async_copy(
            R.gtile.at[lax.rem(index, 2)],
            R.gt.at[pl.ds(pl.multiple_of(index * tile, tile), tile)],
            R.gt_sem.at[lax.rem(index, 2)],
        )

    def table_grad(index, carry):
        @pl.when(index >= 2)
        def _():
            store(index - 2).wait()

        hit = (
            lax.broadcasted_iota(jnp.int32, (tile, ways * spots), 0) + index * tile
            == R.named[0:1, :]
        )
        R.gtile[lax.rem(index, 2)] = dot(jnp.where(hit, 1.0, 0.0).astype(LOW), R.inc[...])
        store(index).start()
        return carry

    lax.fori_loop(0, tiles, table_grad, 0)
    for index in range(max(0, tiles - 2), tiles):
        store(index).wait()

    up.arrive()

    def sum_up(row):
        R.red_up[pl.ds(row, 16), :] = up.total(pl.ds(row, 16))

    strips(strip, 16, sum_up)
    down.arrive()

    def sum_down(row):
        R.h[pl.ds(row, 16), :] = down.total(pl.ds(row, 16))

    strips(strip, 16, sum_down)
    R.red_dn[...] = R.h[:strip, :].T

    small.arrive()
    R.wsum[mp.me] = small.total(slice(None)).astype(LOW)
    weights_in = Gather(mp, of_index(R.wsum), R.ws_send, R.ws_recv)
    weights_in.start()
    first_w.arrive()

    def sum_first(row):
        value = first_w.total(pl.ds(row, 16))
        for part in range(3):
            R.red_qkv[part, pl.ds(row, 16), :] = value[:, part * heads_w : (part + 1) * heads_w]
        R.gout[pl.ds(row, 16), :] = value[:, 3 * heads_w :]

    strips(strip, 16, sum_first)
    R.red_out[...] = R.gout[...].T
    weights_in.relays()
    weights_in.close()
    total = jnp.concatenate([R.wsum[index].astype(F32) for index in range(ways)], 1)
    R.red_in[...] = total[:rin, :]
    if strip % 128 == 0:
        R.lnsum[...] = total[rin_up : rin_up + 8, :]
        R.red_ln[...] = R.lnsum[0:4, pl.ds(pl.multiple_of(dp.me * strip, strip), strip)]
    else:
        chosen = lax.broadcasted_iota(jnp.int32, (model, strip), 0) == dp.me * strip + (
            lax.broadcasted_iota(jnp.int32, (model, strip), 1)
        )
        R.red_ln[...] = dot(
            total[rin_up : rin_up + 8, :].astype(LOW), jnp.where(chosen, 1.0, 0.0).astype(LOW)
        )[0:4]

    for thing in (win, win_all, ln, wc, *dxg, *ag, *mg, up, down, first_w, small_mp, small):
        thing.drain()
    for thing in (named, rows_in, weights_in):
        thing.drain()
    for piece in range(seqs):
        out(piece).drain()
        das(piece).drain()
    for step in range(1, size):
        ask(step).wait_send()
        back(step).wait_send()


def run_layer(cap, ids, levels, noise, cot, table, w_in, ln_params, w_qkv, w_out, w_up, w_down):
    dp, mp = lax.axis_size("dp"), lax.axis_size("mp")
    seqs, seq_len = ids.shape
    tokens, width = noise.shape
    model = cot.shape[1]
    rin = w_in.shape[0]
    heads_w = w_qkv.shape[2]
    strip, hidden = w_up.shape
    group = tokens * mp
    spots = dp * cap
    wide = round_up(rin, 16) + 16
    far, far_dp = mp // 2, dp // 2
    quarter = model // mp
    in_kind = LOW if rin % 16 == 0 else F32
    padded = round_up(table.shape[0], 256)
    vmem = pl.BlockSpec(memory_space=pltpu.VMEM)
    outside = pl.BlockSpec(memory_space=pl.ANY)
    inputs = dict(
        ids=(ids, vmem),
        levels=(levels, pl.BlockSpec(memory_space=pltpu.SMEM)),
        noise=(noise, vmem),
        cot=(cot, vmem),
        table=(table, outside),
        w_in=(w_in, vmem),
        ln_params=(ln_params, vmem),
        w_qkv=(w_qkv, vmem),
        w_out=(w_out, vmem),
        w_up=(w_up, vmem),
        w_down=(w_down, vmem),
    )
    outputs = dict(
        out=((tokens, model), F32),
        red_up=((strip, hidden), F32),
        red_dn=((hidden, strip), F32),
        red_qkv=((3, strip, heads_w), F32),
        red_out=((heads_w, strip), F32),
        red_in=((rin, model), F32),
        red_ln=((4, strip), F32),
        gt=((padded, width), F32),
    )
    buffers = dict(
        tab=((2, 512, width), F32),
        ask=((dp, 8, 128), F32),
        idx=((mp, dp, 8, 128), F32),
        loc=((spots, 128), jnp.int32),
        named=((8, mp * spots), jnp.int32),
        give=((spots, width), LOW),
        got=((spots, width), LOW),
        inc=((mp * spots, width), LOW),
        gtile=((2, 256, width), F32),
        lnf=((dp, 8, ln_params.shape[1]), F32),
        gains=((8, model), F32),
        lnsum=((8, model), F32),
        sig=((tokens, 1), F32),
        pick=((tokens, spots), LOW),
        rows=((tokens, width), LOW),
        mixed=((tokens, width), LOW),
        x0=((tokens, model), F32),
        a=((group, model), LOW),
        c=((group, model), LOW),
        dx=((group, model), LOW),
        dmid=((tokens, model), F32),
        dmid_all=((group, model), LOW),
        winf=((mp, rin * dp, quarter), in_kind),
        waf=((model, 4 * heads_w), LOW),
        wbf=((model, hidden), LOW),
        wcf=((model, hidden), LOW),
        qkv=((group, 3 * heads_w), LOW),
        o=((group, heads_w), LOW),
        low=((2 * seq_len, heads_w), LOW),
        part=((group, model), LOW),
        first=((far * tokens, model), LOW),
        fold=((far * tokens, model), LOW),
        second=((far * tokens, model), LOW),
        fold_far=((far * tokens, model), LOW),
        h=((2 * seq_len, hidden), F32),
        hb=((group, hidden), LOW),
        dhb=((group, hidden), LOW),
        slope=((group, hidden), LOW),
        gdn=((model, hidden), LOW),
        gout=((strip, heads_w), F32),
        dx0=((tokens, model), LOW),
        norms=((8, model), F32),
        gm=((mp, width + 16, quarter), LOW),
        gm_first=((far, width + 16, quarter), LOW),
        gm_second=((far, width + 16, quarter), LOW),
        gw=((dp, wide, quarter), LOW),
        gw_first=((far_dp, wide, quarter), LOW),
        gw_second=((far_dp, wide, quarter), LOW),
        up_first=((far_dp * strip, hidden), LOW),
        up_second=((far_dp * strip, hidden), LOW),
        dn_first=((far_dp * strip, hidden), LOW),
        dn_second=((far_dp * strip, hidden), LOW),
        wa_first=((far_dp * strip, 4 * heads_w), LOW),
        wa_second=((far_dp * strip, 4 * heads_w), LOW),
        wsum=((mp, wide, quarter), LOW),
    )
    sems = dict(tab_sem=2, gt_sem=2)
    for name in ("win", "ln", "wa", "wx", "wb", "wc", "ask", "give", "back", "up", "dn", "ga", "gw"):
        sems[name + "_send"] = sems[name + "_recv"] = dp
    for name in ("wim", "id", "in", "ws", "gm"):
        sems[name + "_send"] = sems[name + "_recv"] = mp
    for name in ("dx", "a", "c", "e", "as", "os", "cs", "ds"):
        sems[name + "_send"] = sems[name + "_recv"] = seqs * mp
    names = [*inputs, *outputs, *buffers, *sems]
    made = pl.pallas_call(
        functools.partial(layer_kernel, cap, names),
        out_shape=[jax.ShapeDtypeStruct(shape, kind) for shape, kind in outputs.values()],
        in_specs=[spec for _, spec in inputs.values()],
        out_specs=[outside if name == "gt" else vmem for name in outputs],
        scratch_shapes=[
            *[pltpu.VMEM(shape, kind) for shape, kind in buffers.values()],
            *[pltpu.SemaphoreType.DMA((number,)) for number in sems.values()],
        ],
        compiler_params=pltpu.CompilerParams(
            vmem_limit_bytes=VMEM_BYTES, collective_id=1, has_side_effects=True
        ),
        name="layer",
    )(*[value for value, _ in inputs.values()])
    return dict(zip(outputs, made))


def direction_of(weight, gradient, first, second):
    first_new = BETA_ONE * first + (1.0 - BETA_ONE) * gradient
    second_new = BETA_TWO * second + (1.0 - BETA_TWO) * gradient * gradient
    second_hat = second_new * (1.0 / (1.0 - BETA_TWO**STEP))
    inverse = lax.rsqrt(second_hat)
    root = second_hat * inverse + EPS_ADAM
    inverse = inverse * (2.0 - root * inverse)
    inverse = inverse * (2.0 - root * inverse)
    direction = first_new * (1.0 / (1.0 - BETA_ONE**STEP)) * inverse + DECAY * weight
    return first_new, second_new, direction


def moments_kernel(names, *refs):
    R = types.SimpleNamespace(**dict(zip(names, refs)))
    turn = pl.program_id(0)

    @pl.when(turn == 0)
    def _():
        R.sums[...] = jnp.zeros_like(R.sums)

    once = jnp.where(lax.axis_index("mp") == 0, 1.0, 0.0)
    lane = lax.broadcasted_iota(jnp.int32, (1, 128), 1)

    def put(place, weight, direction, factor=None):
        for row, values in ((0, weight), (1, direction)):
            total = jnp.sum(jnp.sum(values, 0, keepdims=True), 1, keepdims=True)
            if factor is not None:
                total = total * factor
            R.sums[row : row + 1, :] += jnp.where(lane == place, total, 0.0)

    def piece(name, here, gradient):
        weight = getattr(R, name)[here]
        first_new, second_new, direction = direction_of(
            weight, gradient, getattr(R, name + "_m")[here], getattr(R, name + "_v")[here]
        )
        getattr(R, name + "_m_new")[here] = first_new
        getattr(R, name + "_v_new")[here] = second_new
        getattr(R, name + "_u")[here] = direction
        return weight * weight, direction * direction

    def update(name, gradient, place, factor=None, lead=()):
        shape = gradient.shape
        zero = jnp.zeros((8, shape[1]), F32)

        def one(step, carry):
            here = pl.ds(pl.multiple_of(step * 8, 8), 8)
            squares = piece(name, (*lead, here, slice(None)), gradient[here, :])
            return carry[0] + squares[0], carry[1] + squares[1]

        count = shape[0] // 8
        squares = lax.fori_loop(0, count, one, (zero, zero), unroll=4 if count % 4 == 0 else 1)
        put(place, *squares, factor)

    update("table", R.gt, 0, once)
    for group in range(3):
        update("qkv", R.red_qkv.at[group], 6 + group, lead=(group,))
    update("up", R.red_up, 10)
    update("down", R.red_dn, 11)

    @pl.when(turn == 0)
    def _():
        update("out", R.red_out, 9)
        update("w_in", R.red_in, 1, once)
        squares = piece("ln", (slice(None), slice(None)), R.red_ln[...])
        for row in range(4):
            put(2 + row, squares[0][row : row + 1, :], squares[1][row : row + 1, :], once)


def turns_of(rows, parts):
    return [
        turns
        for turns in (5, 4, 2, 1)
        if rows % (8 * turns) == 0 and all(size % (8 * turns) == 0 for size in parts)
    ][0]


def run_moments(weights, moments, grads):
    names = ("table", "w_in", "ln", "qkv", "out", "up", "down")
    by_name = dict(zip(names, weights))
    rows, width = by_name["table"].shape
    strip, hidden = by_name["up"].shape
    heads_w = by_name["qkv"].shape[2]
    turns = turns_of(rows, (strip, hidden))
    fixed = lambda array: pl.BlockSpec(array.shape, lambda turn: (0,) * array.ndim)
    specs = dict(
        table=pl.BlockSpec((rows // turns, width), lambda turn: (turn, 0)),
        w_in=fixed(by_name["w_in"]),
        ln=fixed(by_name["ln"]),
        qkv=pl.BlockSpec((3, strip // turns, heads_w), lambda turn: (0, turn, 0)),
        out=fixed(by_name["out"]),
        up=pl.BlockSpec((strip // turns, hidden), lambda turn: (turn, 0)),
        down=pl.BlockSpec((hidden // turns, strip), lambda turn: (turn, 0)),
    )
    inputs = {}
    for name, weight, (first, second) in zip(names, weights, moments):
        inputs[name] = (weight, specs[name])
        inputs[name + "_m"] = (first, specs[name])
        inputs[name + "_v"] = (second, specs[name])
    for name, like in (
        ("gt", "table"),
        ("red_up", "up"),
        ("red_dn", "down"),
        ("red_qkv", "qkv"),
        ("red_out", "out"),
        ("red_in", "w_in"),
        ("red_ln", "ln"),
    ):
        inputs[name] = (grads[name], specs[like])
    outputs = {}
    for name, weight in by_name.items():
        for kind in ("_m_new", "_v_new", "_u"):
            outputs[name + kind] = (weight.shape, specs[name])
    outputs["sums"] = ((8, 128), pl.BlockSpec((8, 128), lambda turn: (0, 0)))
    results = pl.pallas_call(
        functools.partial(moments_kernel, [*inputs, *outputs]),
        grid=(turns,),
        out_shape=[jax.ShapeDtypeStruct(shape, F32) for shape, _ in outputs.values()],
        in_specs=[spec for _, spec in inputs.values()],
        out_specs=[spec for _, spec in outputs.values()],
        compiler_params=pltpu.CompilerParams(vmem_limit_bytes=VMEM_BYTES),
        name="moments",
    )(*[value for value, _ in inputs.values()])
    return dict(zip(outputs, results)), turns, specs


def weights_kernel(names, *refs):
    R = types.SimpleNamespace(**dict(zip(names, refs)))
    norms = jnp.sqrt(R.totals[...])
    factors = norms[0:1, :] / (norms[1:2, :] + EPS_ADAM)
    R.norms[...] = norms[0:2, 0:12]

    def factor(place):
        return RATE * factors[0:1, place : place + 1]

    for name, place in (("table", 0), ("w_in", 1), ("out", 9), ("up", 10), ("down", 11)):
        new, old, direction = (getattr(R, name + kind) for kind in ("_new", "", "_u"))
        new[...] = old[...] - factor(place) * direction[...]
    for row in range(4):
        here = slice(row, row + 1)
        R.ln_new[here, :] = R.ln[here, :] - factor(2 + row) * R.ln_u[here, :]
    for part in range(3):
        R.qkv_new[part] = R.qkv[part] - factor(6 + part) * R.qkv_u[part]


def run_weights(totals, weights, results, turns, specs):
    names = ("table", "w_in", "ln", "qkv", "out", "up", "down")
    inputs = {"totals": (totals, pl.BlockSpec((8, 128), lambda turn: (0, 0)))}
    outputs = {}
    for name, weight in zip(names, weights):
        inputs[name] = (weight, specs[name])
        inputs[name + "_u"] = (results[name + "_u"], specs[name])
        outputs[name + "_new"] = (weight.shape, specs[name])
    outputs["norms"] = ((2, 12), pl.BlockSpec((2, 12), lambda turn: (0, 0)))
    made = pl.pallas_call(
        functools.partial(weights_kernel, [*inputs, *outputs]),
        grid=(turns,),
        out_shape=[jax.ShapeDtypeStruct(shape, F32) for shape, _ in outputs.values()],
        in_specs=[spec for _, spec in inputs.values()],
        out_specs=[spec for _, spec in outputs.values()],
        compiler_params=pltpu.CompilerParams(vmem_limit_bytes=VMEM_BYTES),
        name="new_weights",
    )(*[value for value, _ in inputs.values()])
    return dict(zip(outputs, made))


def totals_kernel(values_ref, out_ref, near_ref, wide_ref, dp_send, dp_recv, mp_send, mp_recv):
    dp, mp = Line("dp"), Line("mp")
    meet([], [dp, mp])
    near_ref[dp.me] = values_ref[...]

    def to_dp(step):
        block = near_ref.at[dp.me]
        return dp.push(
            lax.rem(dp.me + step, dp.size), block, block, dp_send.at[step], dp_recv.at[dp.me]
        )

    def to_mp(step):
        block = wide_ref.at[mp.me]
        return mp.push(
            lax.rem(mp.me + step, mp.size), block, block, mp_send.at[step], mp_recv.at[mp.me]
        )

    for step in range(1, dp.size):
        to_dp(step).start()
    for step in range(1, dp.size):
        source = lax.rem(dp.me + step, dp.size)
        block = near_ref.at[source]
        dp.push(dp.partner, block, block, dp_send.at[0], dp_recv.at[source]).wait_recv()
    wide_ref[mp.me] = jnp.sum(near_ref[...], 0)
    for step in range(1, mp.size):
        to_mp(step).start()
    for step in range(1, mp.size):
        source = lax.rem(mp.me + step, mp.size)
        block = wide_ref.at[source]
        mp.push(mp.partner, block, block, mp_send.at[0], mp_recv.at[source]).wait_recv()
    out_ref[...] = jnp.sum(wide_ref[...], 0)
    for step in range(1, dp.size):
        to_dp(step).wait_send()
    for step in range(1, mp.size):
        to_mp(step).wait_send()


def run_totals(values):
    dp, mp = lax.axis_size("dp"), lax.axis_size("mp")
    vmem = pl.BlockSpec(memory_space=pltpu.VMEM)
    return pl.pallas_call(
        totals_kernel,
        out_shape=jax.ShapeDtypeStruct((8, 128), F32),
        in_specs=[vmem],
        out_specs=vmem,
        scratch_shapes=[
            pltpu.VMEM((dp, 8, 128), F32),
            pltpu.VMEM((mp, 8, 128), F32),
            *[pltpu.SemaphoreType.DMA((number,)) for number in (dp, dp, mp, mp)],
        ],
        compiler_params=pltpu.CompilerParams(collective_id=2, has_side_effects=True),
        name="totals",
    )(values)


def per_device(
    token_ids,
    levels,
    noise,
    cotangent,
    table,
    table_m,
    table_v,
    w_in,
    w_in_m,
    w_in_v,
    ln_params,
    ln_m,
    ln_v,
    w_qkv,
    qkv_m,
    qkv_v,
    w_out,
    out_m,
    out_v,
    w_up,
    up_m,
    up_v,
    w_down,
    down_m,
    down_v,
):
    dp_count = lax.axis_size("dp")
    seq_count, seq_len = token_ids.shape
    tokens = seq_count * seq_len
    model = cotangent.shape[2]
    cap = round_up(max(2, (3 * tokens + 2 * dp_count - 1) // (2 * dp_count)), 16)
    grads = run_layer(
        cap,
        token_ids,
        levels,
        noise.reshape(tokens, -1),
        cotangent.reshape(tokens, model),
        table,
        w_in,
        ln_params,
        w_qkv,
        w_out,
        w_up,
        w_down,
    )
    weights = (table, w_in, ln_params, w_qkv, w_out, w_up, w_down)
    moments = (
        (table_m, table_v),
        (w_in_m, w_in_v),
        (ln_m, ln_v),
        (qkv_m, qkv_v),
        (out_m, out_v),
        (up_m, up_v),
        (down_m, down_v),
    )
    made, turns, specs = run_moments(weights, moments, grads)
    totals = run_totals(made["sums"])
    fresh = run_weights(totals, weights, made, turns, specs)
    results = [grads["out"].reshape(seq_count, seq_len, model)]
    for name in ("table", "w_in", "ln", "qkv", "out", "up", "down"):
        results += [fresh[name + "_new"], made[name + "_m_new"], made[name + "_v_new"]]
    results.append(fresh["norms"])
    return tuple(results)


def solution(mesh):
    return jax.shard_map(
        per_device,
        mesh=mesh,
        in_specs=(
            P(("dp", "mp"), None),
            P(("dp", "mp")),
            P(("dp", "mp"), None, None),
            P(("dp", "mp"), None, None),
            P("dp", None),
            P("dp", None),
            P("dp", None),
            P("dp", None),
            P("dp", None),
            P("dp", None),
            P(None, "dp"),
            P(None, "dp"),
            P(None, "dp"),
            P(None, "dp", "mp"),
            P(None, "dp", "mp"),
            P(None, "dp", "mp"),
            P("mp", "dp"),
            P("mp", "dp"),
            P("mp", "dp"),
            P("dp", "mp"),
            P("dp", "mp"),
            P("dp", "mp"),
            P("mp", "dp"),
            P("mp", "dp"),
            P("mp", "dp"),
        ),
        out_specs=(
            P(("dp", "mp"), None, None),
            P("dp", None),
            P("dp", None),
            P("dp", None),
            P("dp", None),
            P("dp", None),
            P("dp", None),
            P(None, "dp"),
            P(None, "dp"),
            P(None, "dp"),
            P(None, "dp", "mp"),
            P(None, "dp", "mp"),
            P(None, "dp", "mp"),
            P("mp", "dp"),
            P("mp", "dp"),
            P("mp", "dp"),
            P("dp", "mp"),
            P("dp", "mp"),
            P("dp", "mp"),
            P("mp", "dp"),
            P("mp", "dp"),
            P("mp", "dp"),
            P(),
        ),
        check_vma=False,
    )
```

```python
import functools
import types

import jax
import jax.numpy as jnp
from jax import lax
from jax.experimental import pallas as pl
from jax.experimental.pallas import tpu as pltpu
from jax.sharding import PartitionSpec as P

HD = 64
LEVELS = 64
STEP = 10


EPS_NORM = 1e-06
EPS_LAYER = 1e-05
EPS_ADAM = 1e-06
BETA_ONE = 0.9
BETA_TWO = 0.999
DECAY = 0.01
RATE = 0.5
SIGMA_TOP = 10.0

F32 = jnp.float32
LOW = jnp.bfloat16
VMEM_BYTES = 63 * 1024 * 1024


def sigma_of(levels):
    frac = levels.astype(jnp.float32) / (LEVELS - 1)
    return jnp.exp(frac * jnp.log(SIGMA_TOP))


def lamb_moments(weight, gradient, first, second):
    first_new = BETA_ONE * first + (1.0 - BETA_ONE) * gradient
    second_new = BETA_TWO * second + (1.0 - BETA_TWO) * gradient * gradient
    first_hat = first_new / (1.0 - BETA_ONE**STEP)
    second_hat = second_new / (1.0 - BETA_TWO**STEP)
    direction = first_hat / (jnp.sqrt(second_hat) + EPS_ADAM) + DECAY * weight
    return (first_new, second_new, direction)


def trust_factors(ratio):
    return (
        ratio[0],
        ratio[1],
        ratio[2:6][:, None],
        ratio[6:9][:, None, None],
        ratio[9],
        ratio[10],
        ratio[11],
    )


def round_up(value, step):
    return -(-value // step) * step


def dot(left, right):
    return jnp.dot(left, right, preferred_element_type=F32)


def dot_nt(left, right):
    return lax.dot_general(left, right, (((1,), (1,)), ((), ())), preferred_element_type=F32)


def dot_tn(left, right):
    return lax.dot_general(left, right, (((0,), (0,)), ((), ())), preferred_element_type=F32)


def strips(total, step, body, unroll=1):
    step = min(step, total)

    def one(turn, carry):
        body(pl.multiple_of(turn * step, step))
        return carry

    lax.fori_loop(0, total // step, one, 0, unroll=unroll)


class Line:
    def __init__(self, axis):
        self.axis = axis
        self.size = lax.axis_size(axis)
        self.far = self.size // 2
        self.me = lax.axis_index(axis)
        self.hi = lax.div(self.me, 2)
        self.lo = lax.rem(self.me, 2)
        self.partner = self.hi * 2 + (1 - self.lo)

    def at(self, step):
        return lax.rem(self.hi + step + self.far, self.far)

    def push(self, index, src, dst, send, recv):
        return pltpu.make_async_remote_copy(
            src_ref=src,
            dst_ref=dst,
            send_sem=send,
            recv_sem=recv,
            device_id={self.axis: index},
            device_id_type=pl.DeviceIdType.MESH,
        )

    def signal(self, sem, index):
        pl.semaphore_signal(
            sem, inc=1, device_id={self.axis: index}, device_id_type=pl.DeviceIdType.MESH
        )


def meet(pair_lines, all_lines=()):
    sem = pltpu.get_barrier_semaphore()
    count = 0
    for line in pair_lines:
        for step in range(1, line.far):
            line.signal(sem, line.at(step) * 2 + line.lo)
            count += 1
        line.signal(sem, line.partner)
        count += 1
    for line in all_lines:
        for step in range(1, line.size):
            line.signal(sem, lax.rem(line.me + step, line.size))
            count += 1
    pl.semaphore_wait(sem, count)


class Gather:
    def __init__(self, line, at, send, recv, base=0, ends=False):
        self.line, self.at, self.send, self.recv, self.base = line, at, send, recv, base
        self.ends = ends and line.far == 4

    def source(self, step):
        line = self.line
        if not self.ends:
            return line.at(-step)
        order = ((1, 2, 3), (0, 3, 2), (3, 0, 1), (2, 1, 0))
        hi = order[3][step - 1]
        for place in (2, 1, 0):
            hi = jnp.where(line.hi == place, order[place][step - 1], hi)
        return hi

    def far_sends(self, act):
        line = self.line
        for step in range(1, line.far):
            one = self.copy(line.me, step - 1, line.at(step) * 2 + line.lo)
            if self.ends and step != 2:
                pl.when(line.hi != (3 if step == 1 else 0))(functools.partial(act, one))
            else:
                act(one)

    def to_end(self, act):
        line = self.line
        dest = jnp.where(line.hi == 1, 0, 3)
        one = self.copy((3 - dest) * 2 + line.lo, 2 * line.far - 1, dest * 2 + line.lo)
        pl.when((line.hi == 1) | (line.hi == 2))(functools.partial(act, one))

    def copy(self, index, slot, dest):
        block = self.at(index)
        return self.line.push(
            dest, block, block, self.send.at[self.base + slot], self.recv.at[self.base + index]
        )

    def start_far(self):
        self.far_sends(lambda one: one.start())

    def start_near(self):
        self.copy(self.line.me, self.line.far - 1, self.line.partner).start()

    def start(self):
        self.start_far()
        self.start_near()

    def relay(self, step):
        line = self.line
        handed = self.copy(self.source(step) * 2 + line.lo, line.far - 1 + step, line.partner)
        handed.wait_recv()
        if self.ends and step == 2:
            self.to_end(lambda one: one.start())
        handed.start()

    def relays(self):
        for step in range(1, self.line.far):
            self.relay(step)

    def close(self):
        line = self.line
        for step in range(line.far):
            self.copy(line.at(-step) * 2 + (1 - line.lo), 0, line.partner).wait_recv()

    def drain(self):
        self.far_sends(lambda one: one.wait_send())
        if self.ends:
            self.to_end(lambda one: one.wait_send())
        for slot in range(self.line.far - 1, 2 * self.line.far - 1):
            self.copy(self.line.me, slot, self.line.partner).wait_send()


class Scatter:
    def __init__(self, line, part, first, second, send, recv, rows, base=0):
        self.line, self.part, self.first, self.second = line, part, first, second
        self.send, self.recv, self.rows, self.base = send, recv, rows, base

    def traded(self, hi):
        line = self.line
        return line.push(
            line.partner,
            self.part(hi * 2 + (1 - line.lo)),
            self.first(hi),
            self.send.at[self.base + hi],
            self.recv.at[self.base + hi],
        )

    def passed(self, step):
        line = self.line
        hi = line.at(step)
        return line.push(
            hi * 2 + line.lo,
            self.part(hi * 2 + line.lo),
            self.second(line.hi),
            self.send.at[self.base + line.far + step - 1],
            self.recv.at[self.base + line.far + line.hi],
        )

    def trade(self, hi):
        self.traded(hi).start()

    def trade_all(self):
        for step in range(1, self.line.far + 1):
            self.trade(self.line.at(step))

    def pass_on(self, step):
        line = self.line
        hi = line.at(step)
        self.traded(hi).wait_recv()
        mine, other = self.part(hi * 2 + line.lo), self.first(hi)

        def add(row):
            here = pl.ds(row, 16)
            mine[here, :] = (mine[here, :].astype(F32) + other[here, :].astype(F32)).astype(LOW)

        strips(self.rows, 16, add)
        self.passed(step).start()

    def arrive(self):
        line = self.line
        self.traded(line.hi).wait_recv()
        for step in range(1, line.far):
            hi = line.at(-step)
            line.push(
                line.partner,
                self.second(hi),
                self.second(hi),
                self.send.at[self.base],
                self.recv.at[self.base + line.far + hi],
            ).wait_recv()

    def total(self, here):
        line = self.line
        value = self.part(line.me)[here, :].astype(F32) + self.first(line.hi)[here, :].astype(F32)
        for step in range(1, line.far):
            value = value + self.second(line.at(-step))[here, :].astype(F32)
        return value

    def drain(self):
        line = self.line
        for step in range(line.far):
            self.traded(line.at(step)).wait_send()
        for step in range(1, line.far):
            self.passed(step).wait_send()


def block_rows(ref, rows, first=0):
    return lambda index: ref.at[pl.ds(pl.multiple_of((index + first) * rows, rows), rows)]


def part_rows(ref, rows, first, count):
    return lambda index: ref.at[pl.ds(pl.multiple_of(index * rows + first, count), count)]


def of_index(ref):
    return lambda index: ref.at[index]


def norm_rows(values):
    center = values - jnp.mean(values, -1, keepdims=True)
    spread = jnp.mean(center * center, -1, keepdims=True)
    inverse = lax.rsqrt(spread + EPS_LAYER)
    return center * inverse, inverse


def norm_back(values, gain, grad):
    unit, inverse = norm_rows(values)
    inner = grad * gain
    shared = jnp.mean(inner, -1, keepdims=True)
    along = jnp.mean(inner * unit, -1, keepdims=True)
    return inverse * (inner - shared - unit * along), unit


def head_masks(width):
    lane = lax.broadcasted_iota(jnp.int32, (1, width), 1)
    return [
        jnp.where((lane >= head * HD) & (lane < (head + 1) * HD), 1.0, 0.0)
        for head in range(width // HD)
    ]


def spread_heads(values, masks):
    return jnp.concatenate([values * mask.astype(LOW) for mask in masks], 0)


def join_heads(values, masks, rows):
    total = values[0:rows] * masks[0]
    for head in range(1, len(masks)):
        total = total + values[head * rows : (head + 1) * rows] * masks[head]
    return total


TAIL = (
    0.2256758632450557,
    0.22566952478278277,
    0.2078438574180613,
    0.16853390514724884,
    0.14146086231844687,
    -0.005667717379728321,
    0.16915486959066833,
    -0.18294364197603524,
    0.05027260226320005,
)


def normal_tail(size, bell):
    base = 1.0 + (0.4 * 0.5**0.5) * size
    t = pl.reciprocal(base, approx=True)
    t = t * (2.0 - base * t)
    t = t * (2.0 - base * t)
    value = jnp.full_like(t, 0.5 * TAIL[-1])
    for factor in TAIL[-2::-1]:
        value = value * t + 0.5 * factor
    return value * t * bell


def far_copies(line, make, sends, recvs):
    def copy(step):
        dest = lax.rem(line.me + step, line.size)
        src, dst = make(dest, line.me)
        return line.push(dest, src, dst, sends.at[step], recvs.at[line.me])

    def wait():
        for step in range(1, line.size):
            source = lax.rem(line.me + line.size - step, line.size)
            _, dst = make(source, source)
            line.push(line.partner, dst, dst, sends.at[0], recvs.at[source]).wait_recv()

    return copy, wait


def layer_kernel(cap, names, *refs):
    R = types.SimpleNamespace(**dict(zip(names, refs)))
    dp, mp = Line("dp"), Line("mp")
    size, ways = dp.size, mp.size
    seqs, seq_len = R.ids.shape
    tokens, width = R.noise.shape
    model = R.cot.shape[1]
    heads_w = R.o.shape[1]
    hidden = R.wbf.shape[1]
    table_rows = R.table.shape[0]
    rin = R.w_in.shape[0]
    rin_up = round_up(rin, 16)
    quarter = model // ways
    strip = R.w_up.shape[0]
    spots = size * cap
    far = mp.far
    count = seqs * far
    own_strip = pl.ds(pl.multiple_of(dp.me * strip, strip), strip)
    mine = pl.ds(pl.multiple_of(dp.me * cap, cap), cap)

    def rows_of(piece):
        return lambda row: pl.ds(pl.multiple_of(piece * seq_len + row, 16), 16)

    def own_rows(piece):
        first = pl.multiple_of((piece * ways + mp.me) * seq_len, seq_len)
        return lambda row: pl.ds(pl.multiple_of(first + row, 16), 16)

    def halves(ref, send, recv):
        return [
            Gather(mp, block_rows(ref, seq_len, piece * ways), send, recv, piece * ways)
            for piece in range(seqs)
        ]

    def sums(part, first, second, send, recv):
        return lambda piece: Scatter(
            mp,
            block_rows(part, seq_len, piece * ways),
            block_rows(first, seq_len, piece * far),
            block_rows(second, seq_len, piece * far),
            send,
            recv,
            seq_len,
            piece * ways,
        )

    def turns(body, hooks):
        def one(turn, carry):
            for place, action in hooks:
                pl.when(turn == place)(action)
            piece = lax.div(turn, far)
            hi = lax.rem(mp.hi + lax.rem(turn, far) + 1, far)
            base = pl.multiple_of((piece * ways + 2 * hi) * seq_len, 2 * seq_len)
            body(turn, piece, hi, base)
            return carry

        lax.fori_loop(0, count, one, 0)

    def hand_on(scatter, turn):
        step = lax.rem(turn, far)

        @pl.when(step != 0)
        def _():
            scatter.pass_on(step)

    def later_pieces(gathers):
        hooks = []
        for piece in range(1, seqs):
            hooks.append((piece * far - 1, gathers[piece].relays))
            hooks.append((piece * far, gathers[piece].close))
        return hooks

    def early_ends(end):
        return [((piece + 2) * far - 1, functools.partial(end, piece)) for piece in range(seqs - 1)]

    chunk = R.tab.shape[1]
    pieces = -(-table_rows // chunk)

    def fetch(piece):
        rows = min(chunk, table_rows - piece * chunk)
        return pltpu.make_async_copy(
            R.table.at[pl.ds(piece * chunk, rows)],
            R.tab.at[piece % 2, pl.ds(0, rows)],
            R.tab_sem.at[piece % 2],
        )

    for piece in range(min(2, pieces)):
        fetch(piece).start()

    names_of_moments = [
        name + kind for name in ("w_in", "ln", "qkv", "out", "up", "down") for kind in ("_m", "_v")
    ]

    def moment(name):
        return pltpu.make_async_copy(
            getattr(R, name), getattr(R, name + "_here"), R.moment_sem.at[names_of_moments.index(name)]
        )

    tile_rows = R.gtile.shape[0]
    tiles = table_rows // tile_rows

    def tile_of(tile):
        side = lax.rem(tile, 2)
        rows = pl.ds(pl.multiple_of(tile * tile_rows, tile_rows), tile_rows)
        return [
            pltpu.make_async_copy(source.at[rows], dest.at[side], R.tile_sem.at[2 * place + side])
            for place, (source, dest) in enumerate(
                ((R.table, R.tw), (R.table_m, R.tm), (R.table_v, R.tv))
            )
        ]

    eye = lax.broadcasted_iota(jnp.int32, (seq_len, seq_len), 0) == lax.broadcasted_iota(
        jnp.int32, (seq_len, seq_len), 1
    )
    id_rows = R.ids[...].astype(F32)
    ids = jnp.concatenate(
        [
            jnp.sum(jnp.where(eye, id_rows[seq : seq + 1, :], 0.0), 1, keepdims=True)
            for seq in range(seqs)
        ],
        0,
    )
    lane = lax.broadcasted_iota(jnp.int32, (tokens, 128), 1).astype(F32)
    low_end = lane * float(table_rows)
    owned = jnp.where((ids >= low_end) & (ids < low_end + float(table_rows)), 1.0, 0.0)
    before = jnp.where(
        lax.broadcasted_iota(jnp.int32, (tokens, tokens), 0)
        >= lax.broadcasted_iota(jnp.int32, (tokens, tokens), 1),
        1.0,
        0.0,
    )
    ranks = dot(before.astype(LOW), owned.astype(LOW))
    rank = jnp.sum(owned * ranks, 1, keepdims=True) - 1.0
    slot = jnp.sum(owned * lane, 1, keepdims=True) * cap + rank
    placed = jnp.where(lane == rank, 1.0, 0.0)
    upper = jnp.floor(ids * (1.0 / 256.0))
    lower = ids - upper * 256.0
    parts = jnp.concatenate([placed * upper, placed * lower, placed], 1).astype(LOW)
    asked = dot_tn(owned.astype(LOW), parts)
    asked = asked[:, :128] * 256.0 + asked[:, 128:256] + asked[:, 256:] - 1.0
    for index in range(size):
        R.ask[index] = jnp.broadcast_to(asked[index : index + 1, :], (8, 128))
    R.idx[mp.me, dp.me] = R.ask[dp.me]

    meet([mp], [dp])
    ask, ask_wait = far_copies(
        dp,
        lambda dest, source: (R.ask.at[dest], R.idx.at[mp.me, source]),
        R.ask_send,
        R.ask_recv,
    )
    for step in range(1, size):
        ask(step).start()

    mine_in = R.winf.at[mp.me]
    win = Gather(dp, block_rows(mine_in, rin), R.win_send, R.win_recv, 0, True)
    win_all = Gather(mp, of_index(R.winf), R.wim_send, R.wim_recv)
    ln = Gather(dp, of_index(R.lnf), R.ln_send, R.ln_recv)
    half_strip = strip // 2

    def in_halves(ref, *names_of):
        return [
            Gather(dp, part_rows(ref, strip, piece * half_strip, half_strip), send, recv, 0, True)
            for piece, (send, recv) in enumerate(names_of)
        ]

    wa = in_halves(R.waf, (R.wa_send, R.wa_recv), (R.wx_send, R.wx_recv))
    wb = in_halves(R.wbf, (R.wb_send, R.wb_recv), (R.wy_send, R.wy_recv))
    wc = in_halves(R.wcf, (R.wc_send, R.wc_recv), (R.wz_send, R.wz_recv))
    dxg = halves(R.dx, R.dx_send, R.dx_recv)
    ag = halves(R.a, R.a_send, R.a_recv)
    cg = halves(R.c, R.c_send, R.c_recv)
    mg = halves(R.dmid_all, R.e_send, R.e_recv)

    mine_in[pl.ds(pl.multiple_of(dp.me * rin, rin), rin), :] = (
        R.w_in[:, pl.ds(pl.multiple_of(mp.me * quarter, quarter), quarter)]
        .astype(LOW)
        .astype(R.winf.dtype)
    )
    win.start()
    shares = R.ln_params[...].astype(LOW).astype(F32)
    R.lnf[dp.me] = jnp.concatenate([shares, jnp.zeros_like(shares)], 0)
    ln.start()
    for part in range(3):
        R.waf[own_strip, part * heads_w : (part + 1) * heads_w] = R.w_qkv[part].astype(LOW)
    R.waf[own_strip, 3 * heads_w :] = R.w_out[...].T.astype(LOW)
    wa[0].start()
    wa[1].start_near()
    for name in names_of_moments:
        moment(name).start()

    for seq in range(seqs):
        level = jnp.full((seq_len, 1), R.levels[seq], jnp.int32).astype(F32) / (LEVELS - 1)
        R.sig[seq * seq_len : (seq + 1) * seq_len, :] = jnp.exp(level * jnp.log(SIGMA_TOP))

    def scale_at(here):
        sig = R.sig[here, :]
        return sig * lax.rsqrt(1.0 + sig * sig)

    for piece in range(seqs):
        here, there = rows_of(piece), own_rows(piece)

        def scale_cot(row, here=here, there=there):
            R.dx[there(row), :] = (R.cot[here(row), :].astype(F32) * scale_at(here(row))).astype(LOW)

        strips(seq_len, 16, scale_cot, 2)
        dxg[piece].start()
    R.wbf[own_strip, :] = R.w_up[...].astype(LOW)
    R.wcf[own_strip, :] = R.w_down[...].T.astype(LOW)
    for gather in wb:
        gather.start_near()
    R.pick[...] = jnp.where(
        lax.broadcasted_iota(jnp.int32, (tokens, spots), 1).astype(F32) == slot, 1.0, 0.0
    ).astype(LOW)
    ln.relays()
    win.relays()

    ask_wait()
    small_eye = lax.broadcasted_iota(jnp.int32, (cap, 128), 0) == lax.broadcasted_iota(
        jnp.int32, (cap, 128), 1
    )

    def locate(index, carry):
        row = R.idx[mp.me, index][0:1, :]
        column = jnp.sum(jnp.where(small_eye, row, 0.0), 1, keepdims=True)
        local = column.astype(jnp.int32) - dp.me * table_rows
        R.loc[pl.ds(pl.multiple_of(index * cap, cap), cap), :] = jnp.broadcast_to(local, (cap, 128))
        return carry

    lax.fori_loop(0, size, locate, 0)
    win.close()
    win_all.start()
    found = None
    for piece in range(pieces):
        fetch(piece).wait()
        rows = min(chunk, table_rows - piece * chunk)
        if rows < chunk:
            R.tab[piece % 2, rows:, :] = jnp.zeros((chunk - rows, width), F32)
        hit = (
            lax.broadcasted_iota(jnp.int32, (spots, chunk), 1) + piece * chunk == R.loc[:, 0:1]
        )
        more = dot(jnp.where(hit, 1.0, 0.0).astype(LOW), R.tab[piece % 2].astype(LOW))
        found = more if found is None else found + more
        if piece + 2 < pieces:
            fetch(piece + 2).start()
    R.give[...] = found.astype(LOW)

    give, give_wait = far_copies(
        dp,
        lambda dest, source: (block_rows(R.give, cap)(dest), block_rows(R.got, cap)(source)),
        R.give_send,
        R.give_recv,
    )
    for step in range(1, size):
        give(step).start()
    R.got[mine, :] = R.give[mine, :]
    win_all.relays()
    wa[0].relays()
    ln.close()
    wide_ln = R.ln_params.shape[1]
    if wide_ln % 128 == 0:
        R.gains[...] = jnp.concatenate([R.lnf[index] for index in range(size)], 1)
    else:
        total = jnp.zeros((8, model), F32)
        for index in range(size):
            place = lax.broadcasted_iota(
                jnp.int32, (wide_ln, model), 1
            ) == index * wide_ln + lax.broadcasted_iota(jnp.int32, (wide_ln, model), 0)
            total = total + dot(R.lnf[index].astype(LOW), jnp.where(place, 1.0, 0.0).astype(LOW))
        R.gains[...] = total
    named = Gather(mp, of_index(R.idx), R.id_send, R.id_recv)

    give_wait()
    wa[1].start_far()
    rows = dot(R.pick[...], R.got[...])
    R.rows[...] = rows.astype(LOW)
    sig = R.sig[...]
    unit = rows * lax.rsqrt(jnp.mean(rows * rows, -1, keepdims=True) + EPS_NORM)
    R.mixed[...] = ((unit + sig * R.noise[...].astype(F32)) * lax.rsqrt(1.0 + sig * sig)).astype(LOW)
    win_all.close()
    for index in range(ways):
        R.x0[:, index * quarter : (index + 1) * quarter] = dot(
            R.mixed[...], R.winf[index].astype(LOW)
        )

    for piece in range(seqs):
        here, there = rows_of(piece), own_rows(piece)

        def first_norm(row, here=here, there=there):
            normed, _ = norm_rows(R.x0[here(row), :])
            R.a[there(row), :] = (normed * R.gains[0:1, :] + R.gains[1:2, :]).astype(LOW)

        strips(seq_len, 16, first_norm, 2)
        ag[piece].start()
    for gather in dxg:
        gather.relays()
    wa[1].relays()
    wb[0].start_far()
    for gather in wc:
        gather.start_near()
    named.start()
    ag[0].relays()
    for gather in (*wa, ag[0]):
        gather.close()

    att = sums(R.part, R.fold, R.fold_far, R.as_send, R.as_recv)
    dcs = sums(R.part, R.fold, R.fold_far, R.cs_send, R.cs_recv)
    das = sums(R.part, R.fold, R.fold_far, R.ds_send, R.ds_recv)
    out = sums(R.c, R.first, R.second, R.os_send, R.os_recv)
    masks = head_masks(heads_w)

    all_rows = (heads_w // HD) * seq_len
    scale = HD ** (-0.5)

    def softmax(seq, row):
        scores = R.scores[seq, row : row + 64, :]
        raised = jnp.exp((scores - jnp.max(scores, -1, keepdims=True)) * scale)
        return raised * (1.0 / jnp.sum(raised, -1, keepdims=True))

    def attend(turn, piece, hi, base):
        here = pl.ds(base, 2 * seq_len)
        R.qkv[here, :] = dot(R.a[here, :], R.waf[:, : 3 * heads_w]).astype(LOW)
        rows_at = [
            pl.ds(pl.multiple_of(base + seq * seq_len, seq_len), seq_len) for seq in range(2)
        ]
        for seq, rows in enumerate(rows_at):
            queries = spread_heads(R.qkv[rows, :heads_w], masks)
            R.scores[seq] = dot_nt(queries, R.qkv[rows, heads_w : 2 * heads_w])
        for seq, rows in enumerate(rows_at):
            for row in range(0, all_rows, 64):
                R.probs[seq, row : row + 64, :] = softmax(seq, row).astype(LOW)
            seen = dot(R.probs[seq], R.qkv[rows, 2 * heads_w : 3 * heads_w])
            R.o[rows, :] = join_heads(seen, masks, seq_len).astype(LOW)
        hand_on(att(piece), turn)
        R.part[here, :] = dot_nt(R.o[here, :], R.waf[:, 3 * heads_w :]).astype(LOW)
        att(piece).trade(hi)

    def second_norm(piece):
        scatter, here, there = att(piece), rows_of(piece), own_rows(piece)
        scatter.arrive()

        def norm(row):
            x1 = R.x0[here(row), :] + scatter.total(pl.ds(row, 16))
            R.out[here(row), :] = x1
            normed, _ = norm_rows(x1)
            R.c[there(row), :] = (normed * R.gains[2:3, :] + R.gains[3:4, :]).astype(LOW)

        strips(seq_len, 16, norm, 2)
        cg[piece].start()

    def second_half():
        wb[0].relay(1)
        wb[1].start_far()

    turns(attend, [*later_pieces(ag), (count - 2, second_half), *early_ends(second_norm)])
    for step in range(2, dp.far):
        wb[0].relay(step)
    second_norm(seqs - 1)
    named.relays()
    cg[0].relays()
    wb[1].relays()
    wc[0].start_far()
    for gather in wb:
        gather.close()
    cg[0].close()
    for piece in range(seqs):
        att(piece).drain()

    def activate(turn, piece, hi, base):
        R.h[...] = dot(R.c[pl.ds(base, 2 * seq_len), :], R.wbf[...])

        def gelu(row):
            there = pl.ds(pl.multiple_of(base + row, 16), 16)
            step = min(256, hidden)
            for col in range(0, hidden, step):
                h = R.h[pl.ds(row, 16), col : col + step]
                bell = jnp.exp(-0.5 * h * h)
                tail = normal_tail(jnp.abs(h), bell)
                gate = jnp.where(h >= 0.0, 1.0 - tail, tail)
                slope = gate + h * (bell * 0.3989422804014327)
                R.hb[there, col : col + step] = (h * gate).astype(LOW)
                R.slope[there, col : col + step] = slope.astype(LOW)

        strips(2 * seq_len, 16, gelu)

    def third_half():
        wc[0].relays()
        wc[1].start_far()

    turns(activate, [*later_pieces(cg), (count - 1, third_half)])

    def spread(part, first, second, send, recv):
        return Scatter(
            dp,
            block_rows(part, strip),
            block_rows(first, strip),
            block_rows(second, strip),
            send,
            recv,
            strip,
        )

    up = spread(R.wbf, R.up_first, R.up_second, R.up_send, R.up_recv)
    down = spread(R.gdn, R.dn_first, R.dn_second, R.dn_send, R.dn_recv)
    first_w = spread(R.waf.at[:, : 3 * heads_w], R.wa_first, R.wa_second, R.ga_send, R.ga_recv)
    wo = spread(R.gwo, R.wo_first, R.wo_second, R.wo_send, R.wo_recv)
    due = [(scatter, step) for scatter in (down, up) for step in range(1, dp.far)]

    def pass_due(number):
        for _ in range(min(number, len(due))):
            scatter, step = due.pop(0)
            scatter.pass_on(step)

    block = 2 * strip if (2 * strip) % 128 == 0 else min(256, model)

    def grads(make, trades):
        if block == 2 * strip:

            def turn_of(turn, carry):
                hi = lax.rem(dp.hi + turn + 1, dp.far)
                make(pl.ds(pl.multiple_of(hi * block, block), block))
                for scatter in trades:
                    scatter.trade(hi)
                return carry

            lax.fori_loop(0, dp.far, turn_of, 0)
        else:
            strips(model, block, lambda col: make(pl.ds(col, block)))
            for scatter in trades:
                scatter.trade_all()

    def down_grads(cols):
        R.gdn[cols, :] = dot_tn(R.dx[:, cols], R.hb[...]).astype(LOW)

    def up_grads(cols):
        R.wbf[cols, :] = dot_tn(R.c[:, cols], R.dhb[...]).astype(LOW)

    for gather in dxg:
        gather.close()
    grads(down_grads, (down,))
    wc[1].relays()
    for gather in wc:
        gather.close()

    def feed_back(turn, piece, hi, base):
        here = pl.ds(base, 2 * seq_len)
        R.h[...] = dot(R.dx[here, :], R.wcf[...])

        def bend(row):
            there = pl.ds(pl.multiple_of(base + row, 16), 16)
            R.dhb[there, :] = (R.h[pl.ds(row, 16), :] * R.slope[there, :].astype(F32)).astype(LOW)

        strips(2 * seq_len, 16, bend, 2)
        hand_on(dcs(piece), turn)
        R.part[here, :] = dot_nt(R.dhb[here, :], R.wbf[...]).astype(LOW)
        dcs(piece).trade(hi)

    R.norms[...] = jnp.zeros_like(R.norms)

    def second_back(piece):
        scatter, here, there = dcs(piece), rows_of(piece), own_rows(piece)
        scatter.arrive()

        def back(row):
            dc = scatter.total(pl.ds(row, 16))
            grad, unit = norm_back(R.out[here(row), :], R.gains[2:3, :], dc)
            grad = grad + R.cot[here(row), :].astype(F32) * scale_at(here(row))
            R.dmid[here(row), :] = grad
            R.dmid_all[there(row), :] = grad.astype(LOW)
            R.norms[2:3, :] += jnp.sum(dc * unit, 0, keepdims=True)
            R.norms[3:4, :] += jnp.sum(dc, 0, keepdims=True)

        strips(seq_len, 16, back, 2)
        mg[piece].start()

    turns(feed_back, early_ends(second_back))
    for gather in (*wb, *wa):
        gather.drain()
    grads(up_grads, (up,))
    second_back(seqs - 1)
    mg[0].relays()
    mg[0].close()
    for piece in range(seqs):
        dcs(piece).drain()

    def attend_back(turn, piece, hi, base):
        here = pl.ds(base, 2 * seq_len)
        R.low[...] = dot(R.dmid_all[here, :], R.waf[:, 3 * heads_w :]).astype(LOW)
        rows_at = [
            pl.ds(pl.multiple_of(base + seq * seq_len, seq_len), seq_len) for seq in range(2)
        ]
        for seq, rows in enumerate(rows_at):
            queries = spread_heads(R.qkv[rows, :heads_w], masks)
            R.scores[seq] = dot_nt(queries, R.qkv[rows, heads_w : 2 * heads_w])
            R.upper[seq] = spread_heads(R.low[seq * seq_len : (seq + 1) * seq_len, :], masks)
            R.dprobs[seq] = dot_nt(R.upper[seq], R.qkv[rows, 2 * heads_w : 3 * heads_w])
        for seq, rows in enumerate(rows_at):
            for row in range(0, all_rows, 64):
                probs = softmax(seq, row)
                grad_probs = R.dprobs[seq, row : row + 64, :]
                inner = jnp.sum(probs * grad_probs, -1, keepdims=True)
                R.probs[seq, row : row + 64, :] = probs.astype(LOW)
                R.dscores[seq, row : row + 64, :] = (probs * (grad_probs - inner)).astype(LOW)
            keys = R.qkv[rows, heads_w : 2 * heads_w]
            queries = spread_heads(R.qkv[rows, :heads_w], masks)
            R.qkv[rows, 2 * heads_w : 3 * heads_w] = dot_tn(R.probs[seq], R.upper[seq]).astype(LOW)
            R.qkv[rows, heads_w : 2 * heads_w] = (dot_tn(R.dscores[seq], queries) * scale).astype(LOW)
            R.qkv[rows, :heads_w] = (
                join_heads(dot(R.dscores[seq], keys), masks, seq_len) * scale
            ).astype(LOW)
        hand_on(das(piece), turn)
        R.part[here, :] = dot_nt(R.qkv[here, :], R.waf[:, : 3 * heads_w]).astype(LOW)
        das(piece).trade(hi)

    def first_back(piece):
        scatter, here = das(piece), rows_of(piece)
        scatter.arrive()

        def back(row):
            da = scatter.total(pl.ds(row, 16))
            grad, unit = norm_back(R.x0[here(row), :], R.gains[0:1, :], da)
            R.dx0[here(row), :] = (R.dmid[here(row), :] + grad).astype(LOW)
            R.norms[0:1, :] += jnp.sum(da * unit, 0, keepdims=True)
            R.norms[1:2, :] += jnp.sum(da, 0, keepdims=True)

        strips(seq_len, 16, back, 2)

    def out_grads():
        def make(cols):
            R.gwo[cols, :] = dot_tn(R.dmid_all[:, cols], R.o[...]).astype(LOW)

        grads(make, (wo,))

    turns(
        attend_back,
        [
            *later_pieces(mg),
            (count - 3, lambda: pass_due(1)),
            (count - 2, lambda: pass_due(1)),
            *early_ends(first_back),
            (count - 1, lambda: pass_due(1)),
            (count - 1, out_grads),
        ],
    )

    def attend_grads(cols):
        R.waf[cols, : 3 * heads_w] = dot_tn(R.a[:, cols], R.qkv[...]).astype(LOW)

    grads(attend_grads, (first_w,))
    pass_due(1)
    first_back(seqs - 1)

    grad_mixed = sum(
        dot_nt(R.dx0[:, index * quarter : (index + 1) * quarter], R.winf[index].astype(LOW))
        for index in range(ways)
    )
    sig = R.sig[...]
    grad_unit = grad_mixed * lax.rsqrt(1.0 + sig * sig)
    rows = R.rows[...].astype(F32)
    inverse = lax.rsqrt(jnp.mean(rows * rows, -1, keepdims=True) + EPS_NORM)
    unit = rows * inverse
    grad_rows = inverse * (grad_unit - unit * jnp.mean(grad_unit * unit, -1, keepdims=True))
    for step in range(1, size):
        give(step).wait_send()
    R.give[...] = dot_tn(R.pick[...], grad_rows.astype(LOW)).astype(LOW)
    mine_inc = block_rows(R.inc, spots)(mp.me)
    back, back_wait = far_copies(
        dp,
        lambda dest, source: (block_rows(R.give, cap)(dest), block_rows(mine_inc, cap)(source)),
        R.back_send,
        R.back_recv,
    )
    for step in range(1, size):
        back(step).start()
    mine_inc[mine, :] = R.give[mine, :]

    small_mp = Scatter(
        mp, of_index(R.gm), of_index(R.gm_first), of_index(R.gm_second), R.gm_send, R.gm_recv, width + 16
    )
    for index in range(ways):
        cols = slice(index * quarter, (index + 1) * quarter)
        R.gm[index, :width, :] = dot_tn(R.mixed[...], R.dx0[:, cols]).astype(LOW)
        R.gm[index, width:, :] = jnp.concatenate(
            [R.norms[0:4, cols], jnp.zeros((12, quarter), F32)], 0
        ).astype(LOW)
    small_mp.trade_all()
    pass_due(1)
    for step in range(1, far):
        small_mp.pass_on(step)

    for gather in cg:
        gather.drain()

    def feed_out(turn, piece, hi, base):
        here = pl.ds(base, 2 * seq_len)
        R.c[here, :] = dot_nt(R.hb[here, :], R.wcf[...]).astype(LOW)
        out(piece).trade(hi)
        hand_on(out(piece), turn)

    turns(feed_out, [])

    back_wait()
    rows_in = Gather(mp, block_rows(R.inc, spots), R.in_send, R.in_recv)
    rows_in.start()
    pass_due(len(due))
    wo.pass_on(1)
    first_w.pass_on(1)

    small = Scatter(
        dp, of_index(R.gw), of_index(R.gw_first), of_index(R.gw_second), R.gw_send, R.gw_recv, rin_up + 16
    )
    small_mp.arrive()
    summed = small_mp.total(slice(None))
    for index in range(size):
        piece = summed[index * rin : (index + 1) * rin, :]
        if rin_up > rin:
            piece = jnp.concatenate([piece, jnp.zeros((rin_up - rin, quarter), F32)], 0)
        R.gw[index, :rin_up, :] = piece.astype(LOW)
        R.gw[index, rin_up:, :] = summed[width:, :].astype(LOW)
    small.trade_all()
    rows_in.relays()
    for step in range(2, dp.far):
        wo.pass_on(step)
        first_w.pass_on(step)
    for step in range(1, dp.far):
        small.pass_on(step)

    def finish_out(piece):
        scatter, here = out(piece), rows_of(piece)
        scatter.arrive()

        def finish(row):
            R.out[here(row), :] = (
                R.out[here(row), :] + scatter.total(pl.ds(row, 16))
            ) * scale_at(here(row))

        strips(seq_len, 16, finish, 2)

    for piece in range(seqs):
        finish_out(piece)

    named.close()
    rows_in.close()
    groups = ways * size
    some, lanes_at = min(groups, 32), min(ways * spots, 512)
    for begin in range(0, ways * spots, lanes_at):
        spot = lax.broadcasted_iota(jnp.int32, (128, lanes_at), 1).astype(F32) + float(begin)
        block_no = jnp.floor((spot + 0.5) * (1.0 / cap))
        place = lax.broadcasted_iota(jnp.int32, (128, lanes_at), 0).astype(F32)
        spread_out = jnp.where(spot - block_no * cap == place, 1.0, 0.0).astype(LOW)
        named_row = jnp.zeros((1, lanes_at), F32)
        for first in range(0, groups, some):
            wanted = jnp.concatenate(
                [
                    R.idx[index // size, index % size][0:1, :] + 1.0
                    for index in range(first, first + some)
                ],
                0,
            )
            high = jnp.floor(wanted * (1.0 / 256.0))
            rest = wanted - 256.0 * high
            laid = dot(high.astype(LOW), spread_out) * 256.0 + dot(rest.astype(LOW), spread_out) - 1.0
            own_block = block_no[0:1, :] == float(first) + lax.broadcasted_iota(
                jnp.int32, (some, lanes_at), 0
            ).astype(F32)
            named_row = named_row + jnp.sum(jnp.where(own_block, laid, 0.0), 0, keepdims=True)
        R.named[:, begin : begin + lanes_at] = jnp.broadcast_to(
            named_row.astype(jnp.int32) - dp.me * table_rows, (8, lanes_at)
        )

    once = jnp.where(mp.me == 0, 1.0, 0.0)
    lanes = lax.broadcasted_iota(jnp.int32, (1, 128), 1)
    R.sums[...] = jnp.zeros_like(R.sums)

    def put(place, squares, factor=None):
        for row, values in enumerate(squares):
            total = jnp.sum(jnp.sum(values, 0, keepdims=True), 1, keepdims=True)
            if factor is not None:
                total = total * factor
            R.sums[row : row + 1, :] += jnp.where(lanes == place, total, 0.0)

    def squares_of(weight, gradient, first, second):
        direction = direction_of(weight, gradient, first, second)[2]
        return weight * weight, direction * direction

    def add_up(weight, gradient, first, second):
        rows, columns = gradient.shape

        def one(step, carry):
            here = pl.ds(pl.multiple_of(step * 8, 8), 8)
            more = squares_of(weight[here, :], gradient[here, :], first[here, :], second[here, :])
            return carry[0] + more[0], carry[1] + more[1]

        zero = jnp.zeros((8, columns), F32)
        number = rows // 8
        unroll = 5 if number % 5 == 0 else 4 if number % 4 == 0 else 1
        return lax.fori_loop(0, number, one, (zero, zero), unroll=unroll)

    for tile in range(min(2, tiles)):
        for one in tile_of(tile):
            one.start()
    zero = jnp.zeros((8, width), F32)

    def add_tile(tile, carry):
        side = lax.rem(tile, 2)
        for one in tile_of(tile):
            one.wait()
        hit = (
            lax.broadcasted_iota(jnp.int32, (tile_rows, ways * spots), 0) + tile * tile_rows
            == R.named[0:1, :]
        )
        R.gtile[...] = dot(jnp.where(hit, 1.0, 0.0).astype(LOW), R.inc[...])
        more = add_up(R.tw.at[side], R.gtile, R.tm.at[side], R.tv.at[side])

        @pl.when(tile + 2 < tiles)
        def _():
            for one in tile_of(tile + 2):
                one.start()

        return carry[0] + more[0], carry[1] + more[1]

    put(0, lax.fori_loop(0, tiles, add_tile, (zero, zero)), once)

    for name in names_of_moments:
        moment(name).wait()
    up.arrive()

    def sum_up(row):
        R.red_up[pl.ds(row, 16), :] = up.total(pl.ds(row, 16))

    strips(strip, 16, sum_up)
    put(10, add_up(R.w_up, R.red_up, R.up_m_here, R.up_v_here))
    down.arrive()

    def sum_down(row):
        R.h[pl.ds(row, 16), :] = down.total(pl.ds(row, 16))

    strips(strip, 16, sum_down)
    R.red_dn[...] = R.h[:strip, :].T
    put(11, add_up(R.w_down, R.red_dn, R.down_m_here, R.down_v_here))
    wo.arrive()
    R.red_out[...] = wo.total(slice(None)).T
    put(9, add_up(R.w_out, R.red_out, R.out_m_here, R.out_v_here))

    small.arrive()
    R.wsum[mp.me] = small.total(slice(None)).astype(LOW)
    weights_in = Gather(mp, of_index(R.wsum), R.ws_send, R.ws_recv)
    weights_in.start()
    first_w.arrive()

    def sum_first(row):
        value = first_w.total(pl.ds(row, 16))
        for part in range(3):
            R.red_qkv[part, pl.ds(row, 16), :] = value[:, part * heads_w : (part + 1) * heads_w]

    strips(strip, 16, sum_first)
    weights_in.relays()
    for part in range(3):
        put(
            6 + part,
            add_up(
                R.w_qkv.at[part], R.red_qkv.at[part], R.qkv_m_here.at[part], R.qkv_v_here.at[part]
            ),
        )
    weights_in.close()
    total = jnp.concatenate([R.wsum[index].astype(F32) for index in range(ways)], 1)
    R.red_in[...] = total[:rin, :]
    put(1, add_up(R.w_in, R.red_in, R.w_in_m_here, R.w_in_v_here), once)
    if strip % 128 == 0:
        R.lnsum[...] = total[rin_up : rin_up + 8, :]
        R.red_ln[...] = R.lnsum[0:4, pl.ds(pl.multiple_of(dp.me * strip, strip), strip)]
    else:
        chosen = lax.broadcasted_iota(jnp.int32, (model, strip), 0) == dp.me * strip + (
            lax.broadcasted_iota(jnp.int32, (model, strip), 1)
        )
        R.red_ln[...] = dot(
            total[rin_up : rin_up + 8, :].astype(LOW), jnp.where(chosen, 1.0, 0.0).astype(LOW)
        )[0:4]
    squares = squares_of(R.ln_params[...], R.red_ln[...], R.ln_m_here[...], R.ln_v_here[...])
    for row in range(4):
        put(2 + row, [values[row : row + 1, :] for values in squares], once)

    R.near[dp.me] = R.sums[...]
    near, near_wait = far_copies(
        dp, lambda dest, source: (R.near.at[dp.me], R.near.at[source]), R.near_send, R.near_recv
    )
    for step in range(1, size):
        near(step).start()
    near_wait()
    R.wide[mp.me] = jnp.sum(R.near[...], 0)
    far_off, far_off_wait = far_copies(
        mp, lambda dest, source: (R.wide.at[mp.me], R.wide.at[source]), R.wide_send, R.wide_recv
    )
    for step in range(1, ways):
        far_off(step).start()
    far_off_wait()
    R.totals[...] = jnp.sum(R.wide[...], 0)

    for thing in (win, win_all, ln, *wc, *dxg, *ag, *mg, up, down, first_w, wo, small_mp, small):
        thing.drain()
    for thing in (named, rows_in, weights_in):
        thing.drain()
    for piece in range(seqs):
        out(piece).drain()
        das(piece).drain()
    for step in range(1, size):
        ask(step).wait_send()
        back(step).wait_send()
        near(step).wait_send()
    for step in range(1, ways):
        far_off(step).wait_send()


def run_layer(cap, ids, levels, noise, cot, weights, moments):
    table, w_in, ln_params, w_qkv, w_out, w_up, w_down = weights
    dp, mp = lax.axis_size("dp"), lax.axis_size("mp")
    seqs, seq_len = ids.shape
    tokens, width = noise.shape
    model = cot.shape[1]
    rin = w_in.shape[0]
    heads_w = w_qkv.shape[2]
    strip, hidden = w_up.shape
    group = tokens * mp
    spots = dp * cap
    wide = round_up(rin, 16) + 16
    far, far_dp = mp // 2, dp // 2
    quarter = model // mp
    in_kind = LOW if rin % 16 == 0 else F32
    tile_rows = max(rows for rows in range(8, 513, 8) if table.shape[0] % rows == 0)
    stacked = (heads_w // HD) * seq_len
    vmem = pl.BlockSpec(memory_space=pltpu.VMEM)
    outside = pl.BlockSpec(memory_space=pl.ANY)
    inputs = dict(
        ids=(ids, vmem),
        levels=(levels, pl.BlockSpec(memory_space=pltpu.SMEM)),
        noise=(noise, vmem),
        cot=(cot, vmem),
        table=(table, outside),
        w_in=(w_in, vmem),
        ln_params=(ln_params, vmem),
        w_qkv=(w_qkv, vmem),
        w_out=(w_out, vmem),
        w_up=(w_up, vmem),
        w_down=(w_down, vmem),
    )
    kept = {}
    for name, (first, second) in zip(("table", "w_in", "ln", "qkv", "out", "up", "down"), moments):
        inputs[name + "_m"] = (first, outside)
        inputs[name + "_v"] = (second, outside)
        if name != "table":
            kept[name + "_m_here"] = kept[name + "_v_here"] = (first.shape, F32)
    outputs = dict(
        out=((tokens, model), F32),
        red_up=((strip, hidden), F32),
        red_dn=((hidden, strip), F32),
        red_qkv=((3, strip, heads_w), F32),
        red_out=((heads_w, strip), F32),
        red_in=((rin, model), F32),
        red_ln=((4, strip), F32),
        inc=((mp * spots, width), LOW),
        named=((8, mp * spots), jnp.int32),
        totals=((8, 128), F32),
    )
    buffers = dict(
        tab=((2, 512, width), F32),
        ask=((dp, 8, 128), F32),
        idx=((mp, dp, 8, 128), F32),
        loc=((spots, 128), jnp.int32),
        give=((spots, width), LOW),
        got=((spots, width), LOW),
        gtile=((tile_rows, width), F32),
        tw=((2, tile_rows, width), F32),
        tm=((2, tile_rows, width), F32),
        tv=((2, tile_rows, width), F32),
        sums=((8, 128), F32),
        near=((dp, 8, 128), F32),
        wide=((mp, 8, 128), F32),
        scores=((2, stacked, seq_len), F32),
        dprobs=((2, stacked, seq_len), F32),
        probs=((2, stacked, seq_len), LOW),
        dscores=((2, stacked, seq_len), LOW),
        upper=((2, stacked, heads_w), LOW),
        gwo=((model, heads_w), LOW),
        wo_first=((far_dp * strip, heads_w), LOW),
        wo_second=((far_dp * strip, heads_w), LOW),
        lnf=((dp, 8, ln_params.shape[1]), F32),
        gains=((8, model), F32),
        lnsum=((8, model), F32),
        sig=((tokens, 1), F32),
        pick=((tokens, spots), LOW),
        rows=((tokens, width), LOW),
        mixed=((tokens, width), LOW),
        x0=((tokens, model), F32),
        a=((group, model), LOW),
        c=((group, model), LOW),
        dx=((group, model), LOW),
        dmid=((tokens, model), F32),
        dmid_all=((group, model), LOW),
        winf=((mp, rin * dp, quarter), in_kind),
        waf=((model, 4 * heads_w), LOW),
        wbf=((model, hidden), LOW),
        wcf=((model, hidden), LOW),
        qkv=((group, 3 * heads_w), LOW),
        o=((group, heads_w), LOW),
        low=((2 * seq_len, heads_w), LOW),
        part=((group, model), LOW),
        first=((far * tokens, model), LOW),
        fold=((far * tokens, model), LOW),
        second=((far * tokens, model), LOW),
        fold_far=((far * tokens, model), LOW),
        h=((2 * seq_len, hidden), F32),
        hb=((group, hidden), LOW),
        dhb=((group, hidden), LOW),
        slope=((group, hidden), LOW),
        gdn=((model, hidden), LOW),
        dx0=((tokens, model), LOW),
        norms=((8, model), F32),
        gm=((mp, width + 16, quarter), LOW),
        gm_first=((far, width + 16, quarter), LOW),
        gm_second=((far, width + 16, quarter), LOW),
        gw=((dp, wide, quarter), LOW),
        gw_first=((far_dp, wide, quarter), LOW),
        gw_second=((far_dp, wide, quarter), LOW),
        up_first=((far_dp * strip, hidden), LOW),
        up_second=((far_dp * strip, hidden), LOW),
        dn_first=((far_dp * strip, hidden), LOW),
        dn_second=((far_dp * strip, hidden), LOW),
        wa_first=((far_dp * strip, 3 * heads_w), LOW),
        wa_second=((far_dp * strip, 3 * heads_w), LOW),
        wsum=((mp, wide, quarter), LOW),
        **kept,
    )
    sems = dict(tab_sem=2, tile_sem=6, moment_sem=12)
    for name in (
        *("win", "ln", "wa", "wx", "wb", "wy", "wc", "wz", "ask", "give", "back"),
        *("up", "dn", "ga", "wo", "gw", "near"),
    ):
        sems[name + "_send"] = sems[name + "_recv"] = dp
    for name in ("wim", "id", "in", "ws", "gm", "wide"):
        sems[name + "_send"] = sems[name + "_recv"] = mp
    for name in ("dx", "a", "c", "e", "as", "os", "cs", "ds"):
        sems[name + "_send"] = sems[name + "_recv"] = seqs * mp
    names = [*inputs, *outputs, *buffers, *sems]
    made = pl.pallas_call(
        functools.partial(layer_kernel, cap, names),
        out_shape=[jax.ShapeDtypeStruct(shape, kind) for shape, kind in outputs.values()],
        in_specs=[spec for _, spec in inputs.values()],
        out_specs=[vmem] * len(outputs),
        scratch_shapes=[
            *[pltpu.VMEM(shape, kind) for shape, kind in buffers.values()],
            *[pltpu.SemaphoreType.DMA((number,)) for number in sems.values()],
        ],
        compiler_params=pltpu.CompilerParams(
            vmem_limit_bytes=VMEM_BYTES, collective_id=1, has_side_effects=True
        ),
        name="layer",
    )(*[value for value, _ in inputs.values()])
    return dict(zip(outputs, made))


def direction_of(weight, gradient, first, second):
    first_new = BETA_ONE * first + (1.0 - BETA_ONE) * gradient
    second_new = BETA_TWO * second + (1.0 - BETA_TWO) * gradient * gradient
    second_hat = second_new * (1.0 / (1.0 - BETA_TWO**STEP))
    inverse = lax.rsqrt(second_hat)
    root = second_hat * inverse + EPS_ADAM
    inverse = inverse * (2.0 - root * inverse)
    inverse = inverse * (2.0 - root * inverse)
    direction = first_new * (1.0 / (1.0 - BETA_ONE**STEP)) * inverse + DECAY * weight
    return first_new, second_new, direction


def update_kernel(names, *refs):
    R = types.SimpleNamespace(**dict(zip(names, refs)))
    turn = pl.program_id(0)
    norms = jnp.sqrt(R.totals[...])
    R.norms[...] = norms[0:2, 0:12]
    factors = norms[0:1, :] / (norms[1:2, :] + EPS_ADAM) * RATE

    def piece(name, here, gradient, place, rows=slice(None)):
        weight = getattr(R, name)[here]
        first_new, second_new, direction = direction_of(
            weight, gradient, getattr(R, name + "_m")[here], getattr(R, name + "_v")[here]
        )
        if isinstance(place, int):
            factor = factors[0:1, place : place + 1]
        else:
            factor = jnp.concatenate([factors[0:1, one : one + 1] for one in place], 0)
        getattr(R, name + "_m_new")[here] = first_new
        getattr(R, name + "_v_new")[here] = second_new
        getattr(R, name + "_new")[here] = weight - factor * direction

    def update(name, gradient, place, lead=(), first=0):
        def one(step, carry):
            row = pl.multiple_of(step * 8, 8)
            here = (*lead, pl.ds(pl.multiple_of(first + row, 8), 8), slice(None))
            piece(name, here, gradient[pl.ds(row, 8), :], place)
            return carry

        count = gradient.shape[0] // 8
        unroll = 5 if count % 5 == 0 else 4 if count % 4 == 0 else 1
        lax.fori_loop(0, count, one, 0, unroll=unroll)

    tile, part = R.table.shape[0], R.gtile.shape[0]
    spots = R.named.shape[1]

    def table_part(row):
        hit = (
            lax.broadcasted_iota(jnp.int32, (part, spots), 0) + (turn * tile + row)
            == R.named[0:1, :]
        )
        R.gtile[...] = dot(jnp.where(hit, 1.0, 0.0).astype(LOW), R.inc[...])
        update("table", R.gtile, 0, (), row)

    strips(tile, part, table_part)
    for group in range(3):
        update("qkv", R.red_qkv.at[group], 6 + group, (group,))
    update("up", R.red_up, 10)
    update("down", R.red_dn, 11)

    @pl.when(turn == 0)
    def _():
        update("out", R.red_out, 9)
        update("w_in", R.red_in, 1)
        piece("ln", (slice(None), slice(None)), R.red_ln[...], (2, 3, 4, 5))


def turns_of(rows, parts):
    return [
        turns
        for turns in (5, 4, 2, 1)
        if rows % (8 * turns) == 0 and all(size % (8 * turns) == 0 for size in parts)
    ][0]


def run_update(weights, moments, grads):
    names = ("table", "w_in", "ln", "qkv", "out", "up", "down")
    by_name = dict(zip(names, weights))
    rows, width = by_name["table"].shape
    strip, hidden = by_name["up"].shape
    heads_w = by_name["qkv"].shape[2]
    turns = turns_of(rows, (strip, hidden))
    tile = rows // turns
    part = max(size for size in range(8, 257, 8) if tile % size == 0)
    fixed = lambda array: pl.BlockSpec(array.shape, lambda turn: (0,) * array.ndim)
    specs = dict(
        table=pl.BlockSpec((tile, width), lambda turn: (turn, 0)),
        w_in=fixed(by_name["w_in"]),
        ln=fixed(by_name["ln"]),
        qkv=pl.BlockSpec((3, strip // turns, heads_w), lambda turn: (0, turn, 0)),
        out=fixed(by_name["out"]),
        up=pl.BlockSpec((strip // turns, hidden), lambda turn: (turn, 0)),
        down=pl.BlockSpec((hidden // turns, strip), lambda turn: (turn, 0)),
    )
    inputs = {}
    for name, weight, (first, second) in zip(names, weights, moments):
        inputs[name] = (weight, specs[name])
        inputs[name + "_m"] = (first, specs[name])
        inputs[name + "_v"] = (second, specs[name])
    for name, like in (
        ("red_up", "up"),
        ("red_dn", "down"),
        ("red_qkv", "qkv"),
        ("red_out", "out"),
        ("red_in", "w_in"),
        ("red_ln", "ln"),
    ):
        inputs[name] = (grads[name], specs[like])
    for name in ("inc", "named", "totals"):
        inputs[name] = (grads[name], fixed(grads[name]))
    outputs = {}
    for name, weight in by_name.items():
        for kind in ("_new", "_m_new", "_v_new"):
            outputs[name + kind] = (weight.shape, specs[name])
    outputs["norms"] = ((2, 12), pl.BlockSpec((2, 12), lambda turn: (0, 0)))
    results = pl.pallas_call(
        functools.partial(update_kernel, [*inputs, *outputs, "gtile"]),
        grid=(turns,),
        out_shape=[jax.ShapeDtypeStruct(shape, F32) for shape, _ in outputs.values()],
        in_specs=[spec for _, spec in inputs.values()],
        out_specs=[spec for _, spec in outputs.values()],
        scratch_shapes=[pltpu.VMEM((part, width), F32)],
        compiler_params=pltpu.CompilerParams(vmem_limit_bytes=VMEM_BYTES),
        name="update",
    )(*[value for value, _ in inputs.values()])
    return list(results)


def per_device(
    token_ids,
    levels,
    noise,
    cotangent,
    table,
    table_m,
    table_v,
    w_in,
    w_in_m,
    w_in_v,
    ln_params,
    ln_m,
    ln_v,
    w_qkv,
    qkv_m,
    qkv_v,
    w_out,
    out_m,
    out_v,
    w_up,
    up_m,
    up_v,
    w_down,
    down_m,
    down_v,
):
    dp_count = lax.axis_size("dp")
    seq_count, seq_len = token_ids.shape
    tokens = seq_count * seq_len
    model = cotangent.shape[2]
    cap = round_up(max(2, (3 * tokens + 2 * dp_count - 1) // (2 * dp_count)), 16)
    weights = (table, w_in, ln_params, w_qkv, w_out, w_up, w_down)
    moments = (
        (table_m, table_v),
        (w_in_m, w_in_v),
        (ln_m, ln_v),
        (qkv_m, qkv_v),
        (out_m, out_v),
        (up_m, up_v),
        (down_m, down_v),
    )
    grads = run_layer(
        cap,
        token_ids,
        levels,
        noise.reshape(tokens, -1),
        cotangent.reshape(tokens, model),
        weights,
        moments,
    )
    results = run_update(weights, moments, grads)
    return (grads["out"].reshape(seq_count, seq_len, model), *results)


def solution(mesh):
    return jax.shard_map(
        per_device,
        mesh=mesh,
        in_specs=(
            P(("dp", "mp"), None),
            P(("dp", "mp")),
            P(("dp", "mp"), None, None),
            P(("dp", "mp"), None, None),
            P("dp", None),
            P("dp", None),
            P("dp", None),
            P("dp", None),
            P("dp", None),
            P("dp", None),
            P(None, "dp"),
            P(None, "dp"),
            P(None, "dp"),
            P(None, "dp", "mp"),
            P(None, "dp", "mp"),
            P(None, "dp", "mp"),
            P("mp", "dp"),
            P("mp", "dp"),
            P("mp", "dp"),
            P("dp", "mp"),
            P("dp", "mp"),
            P("dp", "mp"),
            P("mp", "dp"),
            P("mp", "dp"),
            P("mp", "dp"),
        ),
        out_specs=(
            P(("dp", "mp"), None, None),
            P("dp", None),
            P("dp", None),
            P("dp", None),
            P("dp", None),
            P("dp", None),
            P("dp", None),
            P(None, "dp"),
            P(None, "dp"),
            P(None, "dp"),
            P(None, "dp", "mp"),
            P(None, "dp", "mp"),
            P(None, "dp", "mp"),
            P("mp", "dp"),
            P("mp", "dp"),
            P("mp", "dp"),
            P("dp", "mp"),
            P("dp", "mp"),
            P("dp", "mp"),
            P("mp", "dp"),
            P("mp", "dp"),
            P("mp", "dp"),
            P(),
        ),
        check_vma=False,
    )
```

```python
import functools
import types

import jax
import jax.numpy as jnp
from jax import lax
from jax.experimental import pallas as pl
from jax.experimental.pallas import tpu as pltpu
from jax.sharding import PartitionSpec as P

HD = 64
LEVELS = 64
STEP = 10


EPS_NORM = 1e-06
EPS_LAYER = 1e-05
EPS_ADAM = 1e-06
BETA_ONE = 0.9
BETA_TWO = 0.999
DECAY = 0.01
RATE = 0.5
SIGMA_TOP = 10.0

F32 = jnp.float32
LOW = jnp.bfloat16
VMEM_BYTES = 63 * 1024 * 1024


def sigma_of(levels):
    frac = levels.astype(jnp.float32) / (LEVELS - 1)
    return jnp.exp(frac * jnp.log(SIGMA_TOP))


def lamb_moments(weight, gradient, first, second):
    first_new = BETA_ONE * first + (1.0 - BETA_ONE) * gradient
    second_new = BETA_TWO * second + (1.0 - BETA_TWO) * gradient * gradient
    first_hat = first_new / (1.0 - BETA_ONE**STEP)
    second_hat = second_new / (1.0 - BETA_TWO**STEP)
    direction = first_hat / (jnp.sqrt(second_hat) + EPS_ADAM) + DECAY * weight
    return (first_new, second_new, direction)


def trust_factors(ratio):
    return (
        ratio[0],
        ratio[1],
        ratio[2:6][:, None],
        ratio[6:9][:, None, None],
        ratio[9],
        ratio[10],
        ratio[11],
    )


def round_up(value, step):
    return -(-value // step) * step


def dot(left, right):
    return jnp.dot(left, right, preferred_element_type=F32)


def dot_nt(left, right):
    return lax.dot_general(left, right, (((1,), (1,)), ((), ())), preferred_element_type=F32)


def dot_tn(left, right):
    return lax.dot_general(left, right, (((0,), (0,)), ((), ())), preferred_element_type=F32)


def strips(total, step, body, unroll=1):
    step = min(step, total)

    def one(turn, carry):
        body(pl.multiple_of(turn * step, step))
        return carry

    lax.fori_loop(0, total // step, one, 0, unroll=unroll)


class Line:
    def __init__(self, axis):
        self.axis = axis
        self.size = lax.axis_size(axis)
        self.far = self.size // 2
        self.me = lax.axis_index(axis)
        self.hi = lax.div(self.me, 2)
        self.lo = lax.rem(self.me, 2)
        self.partner = self.hi * 2 + (1 - self.lo)

    def at(self, step):
        return lax.rem(self.hi + step + self.far, self.far)

    def push(self, index, src, dst, send, recv):
        return pltpu.make_async_remote_copy(
            src_ref=src,
            dst_ref=dst,
            send_sem=send,
            recv_sem=recv,
            device_id={self.axis: index},
            device_id_type=pl.DeviceIdType.MESH,
        )

    def signal(self, sem, index):
        pl.semaphore_signal(
            sem, inc=1, device_id={self.axis: index}, device_id_type=pl.DeviceIdType.MESH
        )


def meet(pair_lines, all_lines=()):
    sem = pltpu.get_barrier_semaphore()
    count = 0
    for line in pair_lines:
        for step in range(1, line.far):
            line.signal(sem, line.at(step) * 2 + line.lo)
            count += 1
        line.signal(sem, line.partner)
        count += 1
    for line in all_lines:
        for step in range(1, line.size):
            line.signal(sem, lax.rem(line.me + step, line.size))
            count += 1
    pl.semaphore_wait(sem, count)


class Gather:
    def __init__(self, line, at, send, recv, base=0, ends=False):
        self.line, self.at, self.send, self.recv, self.base = line, at, send, recv, base
        self.ends = ends and line.far == 4

    def source(self, step):
        line = self.line
        if not self.ends:
            return line.at(-step)
        order = ((1, 2, 3), (0, 3, 2), (3, 0, 1), (2, 1, 0))
        hi = order[3][step - 1]
        for place in (2, 1, 0):
            hi = jnp.where(line.hi == place, order[place][step - 1], hi)
        return hi

    def far_sends(self, act):
        line = self.line
        for step in range(1, line.far):
            one = self.copy(line.me, step - 1, line.at(step) * 2 + line.lo)
            if self.ends and step != 2:
                pl.when(line.hi != (3 if step == 1 else 0))(functools.partial(act, one))
            else:
                act(one)

    def to_end(self, act):
        line = self.line
        dest = jnp.where(line.hi == 1, 0, 3)
        one = self.copy((3 - dest) * 2 + line.lo, 2 * line.far - 1, dest * 2 + line.lo)
        pl.when((line.hi == 1) | (line.hi == 2))(functools.partial(act, one))

    def copy(self, index, slot, dest):
        block = self.at(index)
        return self.line.push(
            dest, block, block, self.send.at[self.base + slot], self.recv.at[self.base + index]
        )

    def start_far(self):
        self.far_sends(lambda one: one.start())

    def start_near(self):
        self.copy(self.line.me, self.line.far - 1, self.line.partner).start()

    def start(self):
        self.start_far()
        self.start_near()

    def relay(self, step):
        line = self.line
        handed = self.copy(self.source(step) * 2 + line.lo, line.far - 1 + step, line.partner)
        handed.wait_recv()
        if self.ends and step == 2:
            self.to_end(lambda one: one.start())
        handed.start()

    def relays(self):
        for step in range(1, self.line.far):
            self.relay(step)

    def close(self):
        line = self.line
        for step in range(line.far):
            self.copy(line.at(-step) * 2 + (1 - line.lo), 0, line.partner).wait_recv()

    def drain(self):
        self.far_sends(lambda one: one.wait_send())
        if self.ends:
            self.to_end(lambda one: one.wait_send())
        for slot in range(self.line.far - 1, 2 * self.line.far - 1):
            self.copy(self.line.me, slot, self.line.partner).wait_send()


class Scatter:
    def __init__(self, line, part, first, second, send, recv, rows, base=0):
        self.line, self.part, self.first, self.second = line, part, first, second
        self.send, self.recv, self.rows, self.base = send, recv, rows, base

    def traded(self, hi):
        line = self.line
        return line.push(
            line.partner,
            self.part(hi * 2 + (1 - line.lo)),
            self.first(hi),
            self.send.at[self.base + hi],
            self.recv.at[self.base + hi],
        )

    def passed(self, step):
        line = self.line
        hi = line.at(step)
        return line.push(
            hi * 2 + line.lo,
            self.part(hi * 2 + line.lo),
            self.second(line.hi),
            self.send.at[self.base + line.far + step - 1],
            self.recv.at[self.base + line.far + line.hi],
        )

    def trade(self, hi):
        self.traded(hi).start()

    def trade_all(self):
        for step in range(1, self.line.far + 1):
            self.trade(self.line.at(step))

    def pass_on(self, step):
        line = self.line
        hi = line.at(step)
        self.traded(hi).wait_recv()
        mine, other = self.part(hi * 2 + line.lo), self.first(hi)
        mine[...] = (mine[...].astype(F32) + other[...].astype(F32)).astype(LOW)
        self.passed(step).start()

    def arrive(self):
        line = self.line
        self.traded(line.hi).wait_recv()
        for step in range(1, line.far):
            hi = line.at(-step)
            line.push(
                line.partner,
                self.second(hi),
                self.second(hi),
                self.send.at[self.base],
                self.recv.at[self.base + line.far + hi],
            ).wait_recv()

    def total(self, here):
        line = self.line
        value = self.part(line.me)[here, :].astype(F32) + self.first(line.hi)[here, :].astype(F32)
        for step in range(1, line.far):
            value = value + self.second(line.at(-step))[here, :].astype(F32)
        return value

    def drain(self):
        line = self.line
        for step in range(line.far):
            self.traded(line.at(step)).wait_send()
        for step in range(1, line.far):
            self.passed(step).wait_send()


def block_rows(ref, rows, first=0):
    return lambda index: ref.at[pl.ds(pl.multiple_of((index + first) * rows, rows), rows)]


def part_rows(ref, rows, first, count):
    return lambda index: ref.at[pl.ds(pl.multiple_of(index * rows + first, count), count)]


def of_index(ref):
    return lambda index: ref.at[index]


def norm_rows(values):
    center = values - jnp.mean(values, -1, keepdims=True)
    spread = jnp.mean(center * center, -1, keepdims=True)
    inverse = lax.rsqrt(spread + EPS_LAYER)
    return center * inverse, inverse


def norm_back(values, gain, grad):
    unit, inverse = norm_rows(values)
    inner = grad * gain
    shared = jnp.mean(inner, -1, keepdims=True)
    along = jnp.mean(inner * unit, -1, keepdims=True)
    return inverse * (inner - shared - unit * along), unit


def head_masks(width):
    lane = lax.broadcasted_iota(jnp.int32, (1, width), 1)
    return [
        jnp.where((lane >= head * HD) & (lane < (head + 1) * HD), 1.0, 0.0)
        for head in range(width // HD)
    ]


def spread_heads(values, masks):
    return jnp.concatenate([values * mask.astype(LOW) for mask in masks], 0)


def join_heads(values, masks, rows):
    total = values[0:rows] * masks[0]
    for head in range(1, len(masks)):
        total = total + values[head * rows : (head + 1) * rows] * masks[head]
    return total


TAIL = (
    0.2256758632450557,
    0.22566952478278277,
    0.2078438574180613,
    0.16853390514724884,
    0.14146086231844687,
    -0.005667717379728321,
    0.16915486959066833,
    -0.18294364197603524,
    0.05027260226320005,
)


def normal_tail(size, bell):
    base = 1.0 + (0.4 * 0.5**0.5) * size
    t = pl.reciprocal(base, approx=True)
    t = t * (2.0 - base * t)
    t = t * (2.0 - base * t)
    value = jnp.full_like(t, 0.5 * TAIL[-1])
    for factor in TAIL[-2::-1]:
        value = value * t + 0.5 * factor
    return value * t * bell


def far_copies(line, make, sends, recvs):
    def copy(step):
        dest = lax.rem(line.me + step, line.size)
        src, dst = make(dest, line.me)
        return line.push(dest, src, dst, sends.at[step], recvs.at[line.me])

    def wait():
        for step in range(1, line.size):
            source = lax.rem(line.me + line.size - step, line.size)
            _, dst = make(source, source)
            line.push(line.partner, dst, dst, sends.at[0], recvs.at[source]).wait_recv()

    return copy, wait


def layer_kernel(cap, names, *refs):
    R = types.SimpleNamespace(**dict(zip(names, refs)))
    dp, mp = Line("dp"), Line("mp")
    size, ways = dp.size, mp.size
    seqs, seq_len = R.ids.shape
    tokens, width = R.noise.shape
    model = R.cot.shape[1]
    heads_w = R.o.shape[1]
    hidden = R.wbf.shape[1]
    table_rows = R.table.shape[0]
    rin = R.w_in.shape[0]
    rin_up = round_up(rin, 16)
    quarter = model // ways
    strip = R.w_up.shape[0]
    spots = size * cap
    far = mp.far
    count = seqs * far
    own_strip = pl.ds(pl.multiple_of(dp.me * strip, strip), strip)
    mine = pl.ds(pl.multiple_of(dp.me * cap, cap), cap)

    some_rows = seq_len // 2

    def rows_of(piece):
        return lambda row: pl.ds(pl.multiple_of(piece * seq_len + row, some_rows), some_rows)

    def own_rows(piece):
        first = pl.multiple_of((piece * ways + mp.me) * seq_len, seq_len)
        return lambda row: pl.ds(pl.multiple_of(first + row, some_rows), some_rows)

    def by_rows(body):
        for row in range(0, seq_len, some_rows):
            body(row)

    def halves(ref, send, recv):
        return [
            Gather(mp, block_rows(ref, seq_len, piece * ways), send, recv, piece * ways)
            for piece in range(seqs)
        ]

    def sums(part, first, second, send, recv):
        return lambda piece: Scatter(
            mp,
            block_rows(part, seq_len, piece * ways),
            block_rows(first, seq_len, piece * far),
            block_rows(second, seq_len, piece * far),
            send,
            recv,
            seq_len,
            piece * ways,
        )

    def turns(body, hooks):
        def one(turn, carry):
            for place, action in hooks:
                pl.when(turn == place)(action)
            piece = lax.div(turn, far)
            hi = lax.rem(mp.hi + lax.rem(turn, far) + 1, far)
            base = pl.multiple_of((piece * ways + 2 * hi) * seq_len, 2 * seq_len)
            body(turn, piece, hi, base)
            return carry

        lax.fori_loop(0, count, one, 0)

    def hand_on(scatter, turn):
        step = lax.rem(turn, far)

        @pl.when(step != 0)
        def _():
            scatter.pass_on(step)

    def later_pieces(gathers):
        hooks = []
        for piece in range(1, seqs):
            hooks.append((piece * far - 1, gathers[piece].relays))
            hooks.append((piece * far, gathers[piece].close))
        return hooks

    def early_ends(end):
        return [((piece + 2) * far - 1, functools.partial(end, piece)) for piece in range(seqs - 1)]

    chunk = R.tab.shape[1]
    pieces = -(-table_rows // chunk)

    def fetch(piece):
        rows = min(chunk, table_rows - piece * chunk)
        return pltpu.make_async_copy(
            R.table.at[pl.ds(piece * chunk, rows)],
            R.tab.at[piece % 2, pl.ds(0, rows)],
            R.tab_sem.at[piece % 2],
        )

    for piece in range(min(2, pieces)):
        fetch(piece).start()

    names_of_moments = [
        name + kind for name in ("w_in", "ln", "qkv", "out", "up", "down") for kind in ("_m", "_v")
    ]

    def moment(name):
        return pltpu.make_async_copy(
            getattr(R, name), getattr(R, name + "_here"), R.moment_sem.at[names_of_moments.index(name)]
        )

    tile_rows = R.gtile.shape[0]
    tiles = table_rows // tile_rows

    def tile_of(tile):
        side = lax.rem(tile, 2)
        rows = pl.ds(pl.multiple_of(tile * tile_rows, tile_rows), tile_rows)
        return [
            pltpu.make_async_copy(source.at[rows], dest.at[side], R.tile_sem.at[2 * place + side])
            for place, (source, dest) in enumerate(
                ((R.table, R.tw), (R.table_m, R.tm), (R.table_v, R.tv))
            )
        ]

    eye = lax.broadcasted_iota(jnp.int32, (seq_len, seq_len), 0) == lax.broadcasted_iota(
        jnp.int32, (seq_len, seq_len), 1
    )
    id_rows = R.ids[...].astype(F32)
    ids = jnp.concatenate(
        [
            jnp.sum(jnp.where(eye, id_rows[seq : seq + 1, :], 0.0), 1, keepdims=True)
            for seq in range(seqs)
        ],
        0,
    )
    lane = lax.broadcasted_iota(jnp.int32, (tokens, 128), 1).astype(F32)
    low_end = lane * float(table_rows)
    owned = jnp.where((ids >= low_end) & (ids < low_end + float(table_rows)), 1.0, 0.0)
    before = jnp.where(
        lax.broadcasted_iota(jnp.int32, (tokens, tokens), 0)
        >= lax.broadcasted_iota(jnp.int32, (tokens, tokens), 1),
        1.0,
        0.0,
    )
    ranks = dot(before.astype(LOW), owned.astype(LOW))
    rank = jnp.sum(owned * ranks, 1, keepdims=True) - 1.0
    slot = jnp.sum(owned * lane, 1, keepdims=True) * cap + rank
    placed = jnp.where(lane == rank, 1.0, 0.0)
    upper = jnp.floor(ids * (1.0 / 256.0))
    lower = ids - upper * 256.0
    parts = jnp.concatenate([placed * upper, placed * lower, placed], 1).astype(LOW)
    asked = dot_tn(owned.astype(LOW), parts)
    asked = asked[:, :128] * 256.0 + asked[:, 128:256] + asked[:, 256:] - 1.0
    for index in range(size):
        R.ask[index] = jnp.broadcast_to(asked[index : index + 1, :], (8, 128))
    R.idx[mp.me, dp.me] = R.ask[dp.me]

    meet([mp], [dp])
    ask, ask_wait = far_copies(
        dp,
        lambda dest, source: (R.ask.at[dest], R.idx.at[mp.me, source]),
        R.ask_send,
        R.ask_recv,
    )
    for step in range(1, size):
        ask(step).start()

    mine_in = R.winf.at[mp.me]
    win = Gather(dp, block_rows(mine_in, rin), R.win_send, R.win_recv, 0, True)
    win_all = Gather(mp, of_index(R.winf), R.wim_send, R.wim_recv)
    ln = Gather(dp, of_index(R.lnf), R.ln_send, R.ln_recv)
    half_strip = strip // 2

    def in_halves(ref, *names_of):
        return [
            Gather(dp, part_rows(ref, strip, piece * half_strip, half_strip), send, recv, 0, True)
            for piece, (send, recv) in enumerate(names_of)
        ]

    wa = in_halves(R.waf, (R.wa_send, R.wa_recv), (R.wx_send, R.wx_recv))
    wb = in_halves(R.wbf, (R.wb_send, R.wb_recv), (R.wy_send, R.wy_recv))
    wc = in_halves(R.wcf, (R.wc_send, R.wc_recv), (R.wz_send, R.wz_recv))
    dxg = halves(R.dx, R.dx_send, R.dx_recv)
    ag = halves(R.a, R.a_send, R.a_recv)
    cg = halves(R.c, R.c_send, R.c_recv)
    mg = halves(R.dmid_all, R.e_send, R.e_recv)

    mine_in[pl.ds(pl.multiple_of(dp.me * rin, rin), rin), :] = (
        R.w_in[:, pl.ds(pl.multiple_of(mp.me * quarter, quarter), quarter)]
        .astype(LOW)
        .astype(R.winf.dtype)
    )
    win.start()
    shares = R.ln_params[...].astype(LOW).astype(F32)
    R.lnf[dp.me] = jnp.concatenate([shares, jnp.zeros_like(shares)], 0)
    ln.start()
    for part in range(3):
        R.waf[own_strip, part * heads_w : (part + 1) * heads_w] = R.w_qkv[part].astype(LOW)
    R.waf[own_strip, 3 * heads_w :] = R.w_out[...].T.astype(LOW)
    wa[0].start()
    wa[1].start_near()
    for name in names_of_moments:
        moment(name).start()

    for seq in range(seqs):
        level = jnp.full((seq_len, 1), R.levels[seq], jnp.int32).astype(F32) / (LEVELS - 1)
        R.sig[seq * seq_len : (seq + 1) * seq_len, :] = jnp.exp(level * jnp.log(SIGMA_TOP))

    def scale_at(here):
        sig = R.sig[here, :]
        return sig * lax.rsqrt(1.0 + sig * sig)

    for piece in range(seqs):
        here, there = rows_of(piece), own_rows(piece)

        def scale_cot(row, here=here, there=there):
            R.dx[there(row), :] = (R.cot[here(row), :].astype(F32) * scale_at(here(row))).astype(LOW)

        by_rows(scale_cot)
        dxg[piece].start()
    R.wbf[own_strip, :] = R.w_up[...].astype(LOW)
    R.wcf[own_strip, :] = R.w_down[...].T.astype(LOW)
    for gather in wb:
        gather.start_near()
    R.pick[...] = jnp.where(
        lax.broadcasted_iota(jnp.int32, (tokens, spots), 1).astype(F32) == slot, 1.0, 0.0
    ).astype(LOW)
    ln.relays()
    win.relays()

    ask_wait()
    small_eye = lax.broadcasted_iota(jnp.int32, (cap, 128), 0) == lax.broadcasted_iota(
        jnp.int32, (cap, 128), 1
    )

    def locate(index, carry):
        row = R.idx[mp.me, index][0:1, :]
        column = jnp.sum(jnp.where(small_eye, row, 0.0), 1, keepdims=True)
        local = column.astype(jnp.int32) - dp.me * table_rows
        R.loc[pl.ds(pl.multiple_of(index * cap, cap), cap), :] = jnp.broadcast_to(local, (cap, 128))
        return carry

    lax.fori_loop(0, size, locate, 0, unroll=True)
    win.close()
    win_all.start()
    found = None
    for piece in range(pieces):
        fetch(piece).wait()
        rows = min(chunk, table_rows - piece * chunk)
        if rows < chunk:
            R.tab[piece % 2, rows:, :] = jnp.zeros((chunk - rows, width), F32)
        hit = (
            lax.broadcasted_iota(jnp.int32, (spots, chunk), 1) + piece * chunk == R.loc[:, 0:1]
        )
        more = dot(jnp.where(hit, 1.0, 0.0).astype(LOW), R.tab[piece % 2].astype(LOW))
        found = more if found is None else found + more
        if piece + 2 < pieces:
            fetch(piece + 2).start()
    R.give[...] = found.astype(LOW)

    give, give_wait = far_copies(
        dp,
        lambda dest, source: (block_rows(R.give, cap)(dest), block_rows(R.got, cap)(source)),
        R.give_send,
        R.give_recv,
    )
    for step in range(1, size):
        give(step).start()
    R.got[mine, :] = R.give[mine, :]
    win_all.relays()
    wa[0].relays()
    ln.close()
    wide_ln = R.ln_params.shape[1]
    if wide_ln % 128 == 0:
        R.gains[...] = jnp.concatenate([R.lnf[index] for index in range(size)], 1)
    else:
        total = jnp.zeros((8, model), F32)
        for index in range(size):
            place = lax.broadcasted_iota(
                jnp.int32, (wide_ln, model), 1
            ) == index * wide_ln + lax.broadcasted_iota(jnp.int32, (wide_ln, model), 0)
            total = total + dot(R.lnf[index].astype(LOW), jnp.where(place, 1.0, 0.0).astype(LOW))
        R.gains[...] = total
    named = Gather(mp, of_index(R.idx), R.id_send, R.id_recv)

    give_wait()
    wa[1].start_far()
    rows = dot(R.pick[...], R.got[...])
    R.rows[...] = rows.astype(LOW)
    sig = R.sig[...]
    unit = rows * lax.rsqrt(jnp.mean(rows * rows, -1, keepdims=True) + EPS_NORM)
    R.mixed[...] = ((unit + sig * R.noise[...].astype(F32)) * lax.rsqrt(1.0 + sig * sig)).astype(LOW)
    win_all.close()
    for index in range(ways):
        R.x0[:, index * quarter : (index + 1) * quarter] = dot(
            R.mixed[...], R.winf[index].astype(LOW)
        )

    for piece in range(seqs):
        here, there = rows_of(piece), own_rows(piece)

        def first_norm(row, here=here, there=there):
            normed, _ = norm_rows(R.x0[here(row), :])
            R.a[there(row), :] = (normed * R.gains[0:1, :] + R.gains[1:2, :]).astype(LOW)

        by_rows(first_norm)
        ag[piece].start()
    for gather in dxg:
        gather.relays()
    wa[1].relays()
    for gather in wb:
        gather.start_far()
    for gather in wc:
        gather.start_near()
    named.start()
    ag[0].relays()
    for gather in (*wa, ag[0]):
        gather.close()

    att = sums(R.part, R.fold, R.fold_far, R.as_send, R.as_recv)
    dcs = sums(R.part, R.fold, R.fold_far, R.cs_send, R.cs_recv)
    das = sums(R.part, R.fold, R.fold_far, R.ds_send, R.ds_recv)
    out = sums(R.c, R.first, R.second, R.os_send, R.os_recv)
    masks = head_masks(heads_w)

    all_rows = (heads_w // HD) * seq_len
    scale = HD ** (-0.5)

    def softmax(seq, row):
        scores = R.scores[seq, row : row + 64, :]
        raised = jnp.exp((scores - jnp.max(scores, -1, keepdims=True)) * scale)
        return raised * (1.0 / jnp.sum(raised, -1, keepdims=True))

    def attend(turn, piece, hi, base):
        here = pl.ds(base, 2 * seq_len)
        R.qkv[here, :] = dot(R.a[here, :], R.waf[:, : 3 * heads_w]).astype(LOW)
        rows_at = [
            pl.ds(pl.multiple_of(base + seq * seq_len, seq_len), seq_len) for seq in range(2)
        ]
        for seq, rows in enumerate(rows_at):
            queries = spread_heads(R.qkv[rows, :heads_w], masks)
            R.scores[seq] = dot_nt(queries, R.qkv[rows, heads_w : 2 * heads_w])
        for seq, rows in enumerate(rows_at):
            for row in range(0, all_rows, 64):
                R.probs[seq, row : row + 64, :] = softmax(seq, row).astype(LOW)
            seen = dot(R.probs[seq], R.qkv[rows, 2 * heads_w : 3 * heads_w])
            R.o[rows, :] = join_heads(seen, masks, seq_len).astype(LOW)
        hand_on(att(piece), turn)
        R.part[here, :] = dot_nt(R.o[here, :], R.waf[:, 3 * heads_w :]).astype(LOW)
        att(piece).trade(hi)

    def second_norm(piece):
        scatter, here, there = att(piece), rows_of(piece), own_rows(piece)
        scatter.arrive()

        def norm(row):
            x1 = R.x0[here(row), :] + scatter.total(pl.ds(row, some_rows))
            R.out[here(row), :] = x1
            normed, _ = norm_rows(x1)
            R.c[there(row), :] = (normed * R.gains[2:3, :] + R.gains[3:4, :]).astype(LOW)

        by_rows(norm)
        cg[piece].start()

    def second_half():
        wb[0].relays()
        for gather in wc:
            gather.start_far()

    turns(attend, [*later_pieces(ag), (count - 2, second_half), *early_ends(second_norm)])
    wb[1].relays()
    second_norm(seqs - 1)
    named.relays()
    cg[0].relays()
    for gather in wb:
        gather.close()
    cg[0].close()
    for piece in range(seqs):
        att(piece).drain()

    def activate(turn, piece, hi, base):
        R.h[...] = dot(R.c[pl.ds(base, 2 * seq_len), :], R.wbf[...])

        def gelu(row):
            there = pl.ds(pl.multiple_of(base + row, 64), 64)
            step = min(256, hidden)
            for col in range(0, hidden, step):
                h = R.h[pl.ds(row, 64), col : col + step]
                bell = jnp.exp(-0.5 * h * h)
                tail = normal_tail(jnp.abs(h), bell)
                gate = jnp.where(h >= 0.0, 1.0 - tail, tail)
                slope = gate + h * (bell * 0.3989422804014327)
                R.hb[there, col : col + step] = (h * gate).astype(LOW)
                R.slope[there, col : col + step] = slope.astype(LOW)

        strips(2 * seq_len, 64, gelu)

    turns(activate, [*later_pieces(cg), (count - 1, wc[0].relays)])

    def spread(part, first, second, send, recv):
        return Scatter(
            dp,
            block_rows(part, strip),
            block_rows(first, strip),
            block_rows(second, strip),
            send,
            recv,
            strip,
        )

    up = spread(R.wbf, R.up_first, R.up_second, R.up_send, R.up_recv)
    down = spread(R.gdn, R.dn_first, R.dn_second, R.dn_send, R.dn_recv)
    first_w = spread(R.waf.at[:, : 3 * heads_w], R.wa_first, R.wa_second, R.ga_send, R.ga_recv)
    wo = spread(R.gwo, R.wo_first, R.wo_second, R.wo_send, R.wo_recv)
    due = [(scatter, step) for scatter in (down, up) for step in range(1, dp.far)]

    def pass_due(number):
        for _ in range(min(number, len(due))):
            scatter, step = due.pop(0)
            scatter.pass_on(step)

    block = 2 * strip if (2 * strip) % 128 == 0 else min(256, model)

    def grads(make, trades):
        if block == 2 * strip:

            def turn_of(turn, carry):
                hi = lax.rem(dp.hi + turn + 1, dp.far)
                make(pl.ds(pl.multiple_of(hi * block, block), block))
                for scatter in trades:
                    scatter.trade(hi)
                return carry

            lax.fori_loop(0, dp.far, turn_of, 0)
        else:
            strips(model, block, lambda col: make(pl.ds(col, block)))
            for scatter in trades:
                scatter.trade_all()

    def down_grads(cols):
        R.gdn[cols, :] = dot_tn(R.dx[:, cols], R.hb[...]).astype(LOW)

    def up_grads(cols):
        R.wbf[cols, :] = dot_tn(R.c[:, cols], R.dhb[...]).astype(LOW)

    for gather in dxg:
        gather.close()
    grads(down_grads, (down,))
    wc[1].relays()
    for gather in wc:
        gather.close()

    def feed_back(turn, piece, hi, base):
        here = pl.ds(base, 2 * seq_len)
        R.h[...] = dot(R.dx[here, :], R.wcf[...])

        def bend(row):
            there = pl.ds(pl.multiple_of(base + row, 64), 64)
            R.dhb[there, :] = (R.h[pl.ds(row, 64), :] * R.slope[there, :].astype(F32)).astype(LOW)

        strips(2 * seq_len, 64, bend)
        hand_on(dcs(piece), turn)
        R.part[here, :] = dot_nt(R.dhb[here, :], R.wbf[...]).astype(LOW)
        dcs(piece).trade(hi)

    R.norms[...] = jnp.zeros_like(R.norms)

    def second_back(piece):
        scatter, here, there = dcs(piece), rows_of(piece), own_rows(piece)
        scatter.arrive()

        def back(row):
            dc = scatter.total(pl.ds(row, some_rows))
            grad, unit = norm_back(R.out[here(row), :], R.gains[2:3, :], dc)
            grad = grad + R.cot[here(row), :].astype(F32) * scale_at(here(row))
            R.dmid[here(row), :] = grad
            R.dmid_all[there(row), :] = grad.astype(LOW)
            R.norms[2:3, :] += jnp.sum(dc * unit, 0, keepdims=True)
            R.norms[3:4, :] += jnp.sum(dc, 0, keepdims=True)

        by_rows(back)
        mg[piece].start()

    turns(feed_back, early_ends(second_back))
    for gather in (*wb, *wa):
        gather.drain()
    grads(up_grads, (up,))
    second_back(seqs - 1)
    mg[0].relays()
    mg[0].close()
    for piece in range(seqs):
        dcs(piece).drain()

    def attend_back(turn, piece, hi, base):
        here = pl.ds(base, 2 * seq_len)
        R.low[...] = dot(R.dmid_all[here, :], R.waf[:, 3 * heads_w :]).astype(LOW)
        rows_at = [
            pl.ds(pl.multiple_of(base + seq * seq_len, seq_len), seq_len) for seq in range(2)
        ]
        for seq, rows in enumerate(rows_at):
            queries = spread_heads(R.qkv[rows, :heads_w], masks)
            R.scores[seq] = dot_nt(queries, R.qkv[rows, heads_w : 2 * heads_w])
            R.upper[seq] = spread_heads(R.low[seq * seq_len : (seq + 1) * seq_len, :], masks)
            R.dprobs[seq] = dot_nt(R.upper[seq], R.qkv[rows, 2 * heads_w : 3 * heads_w])
        for seq, rows in enumerate(rows_at):
            for row in range(0, all_rows, 64):
                probs = softmax(seq, row)
                grad_probs = R.dprobs[seq, row : row + 64, :]
                inner = jnp.sum(probs * grad_probs, -1, keepdims=True)
                R.probs[seq, row : row + 64, :] = probs.astype(LOW)
                R.dscores[seq, row : row + 64, :] = (probs * (grad_probs - inner)).astype(LOW)
            keys = R.qkv[rows, heads_w : 2 * heads_w]
            queries = spread_heads(R.qkv[rows, :heads_w], masks)
            R.qkv[rows, 2 * heads_w : 3 * heads_w] = dot_tn(R.probs[seq], R.upper[seq]).astype(LOW)
            R.qkv[rows, heads_w : 2 * heads_w] = (dot_tn(R.dscores[seq], queries) * scale).astype(LOW)
            R.qkv[rows, :heads_w] = (
                join_heads(dot(R.dscores[seq], keys), masks, seq_len) * scale
            ).astype(LOW)
        hand_on(das(piece), turn)
        R.part[here, :] = dot_nt(R.qkv[here, :], R.waf[:, : 3 * heads_w]).astype(LOW)
        das(piece).trade(hi)

    def first_back(piece):
        scatter, here = das(piece), rows_of(piece)
        scatter.arrive()

        def back(row):
            da = scatter.total(pl.ds(row, some_rows))
            grad, unit = norm_back(R.x0[here(row), :], R.gains[0:1, :], da)
            R.dx0[here(row), :] = (R.dmid[here(row), :] + grad).astype(LOW)
            R.norms[0:1, :] += jnp.sum(da * unit, 0, keepdims=True)
            R.norms[1:2, :] += jnp.sum(da, 0, keepdims=True)

        by_rows(back)

    def out_grads():
        def make(cols):
            R.gwo[cols, :] = dot_tn(R.dmid_all[:, cols], R.o[...]).astype(LOW)

        grads(make, (wo,))

    turns(
        attend_back,
        [
            *later_pieces(mg),
            (count - 3, lambda: pass_due(1)),
            (count - 2, lambda: pass_due(1)),
            *early_ends(first_back),
            (count - 1, lambda: pass_due(1)),
            (count - 1, out_grads),
        ],
    )

    def attend_grads(cols):
        R.waf[cols, : 3 * heads_w] = dot_tn(R.a[:, cols], R.qkv[...]).astype(LOW)

    grads(attend_grads, (first_w,))
    pass_due(1)
    first_back(seqs - 1)

    grad_mixed = sum(
        dot_nt(R.dx0[:, index * quarter : (index + 1) * quarter], R.winf[index].astype(LOW))
        for index in range(ways)
    )
    sig = R.sig[...]
    grad_unit = grad_mixed * lax.rsqrt(1.0 + sig * sig)
    rows = R.rows[...].astype(F32)
    inverse = lax.rsqrt(jnp.mean(rows * rows, -1, keepdims=True) + EPS_NORM)
    unit = rows * inverse
    grad_rows = inverse * (grad_unit - unit * jnp.mean(grad_unit * unit, -1, keepdims=True))
    for step in range(1, size):
        give(step).wait_send()
    R.give[...] = dot_tn(R.pick[...], grad_rows.astype(LOW)).astype(LOW)
    mine_inc = block_rows(R.inc, spots)(mp.me)
    back, back_wait = far_copies(
        dp,
        lambda dest, source: (block_rows(R.give, cap)(dest), block_rows(mine_inc, cap)(source)),
        R.back_send,
        R.back_recv,
    )
    for step in range(1, size):
        back(step).start()
    mine_inc[mine, :] = R.give[mine, :]

    small_mp = Scatter(
        mp, of_index(R.gm), of_index(R.gm_first), of_index(R.gm_second), R.gm_send, R.gm_recv, width + 16
    )
    for index in range(ways):
        cols = slice(index * quarter, (index + 1) * quarter)
        R.gm[index, :width, :] = dot_tn(R.mixed[...], R.dx0[:, cols]).astype(LOW)
        R.gm[index, width:, :] = jnp.concatenate(
            [R.norms[0:4, cols], jnp.zeros((12, quarter), F32)], 0
        ).astype(LOW)
    small_mp.trade_all()
    pass_due(1)
    for step in range(1, far):
        small_mp.pass_on(step)

    for gather in cg:
        gather.drain()

    def feed_out(turn, piece, hi, base):
        here = pl.ds(base, 2 * seq_len)
        R.c[here, :] = dot_nt(R.hb[here, :], R.wcf[...]).astype(LOW)
        out(piece).trade(hi)
        hand_on(out(piece), turn)

    turns(feed_out, [])

    back_wait()
    rows_in = Gather(mp, block_rows(R.inc, spots), R.in_send, R.in_recv)
    rows_in.start()
    pass_due(len(due))
    wo.pass_on(1)
    first_w.pass_on(1)

    small = Scatter(
        dp, of_index(R.gw), of_index(R.gw_first), of_index(R.gw_second), R.gw_send, R.gw_recv, rin_up + 16
    )
    small_mp.arrive()
    summed = small_mp.total(slice(None))
    for index in range(size):
        piece = summed[index * rin : (index + 1) * rin, :]
        if rin_up > rin:
            piece = jnp.concatenate([piece, jnp.zeros((rin_up - rin, quarter), F32)], 0)
        R.gw[index, :rin_up, :] = piece.astype(LOW)
        R.gw[index, rin_up:, :] = summed[width:, :].astype(LOW)
    small.trade_all()
    rows_in.relays()
    for step in range(2, dp.far):
        wo.pass_on(step)
        first_w.pass_on(step)
    for step in range(1, dp.far):
        small.pass_on(step)

    def finish_out(piece):
        scatter, here = out(piece), rows_of(piece)
        scatter.arrive()

        def finish(row):
            R.out[here(row), :] = (
                R.out[here(row), :] + scatter.total(pl.ds(row, some_rows))
            ) * scale_at(here(row))

        by_rows(finish)

    for piece in range(seqs):
        finish_out(piece)

    named.close()
    rows_in.close()
    groups = ways * size
    some, lanes_at = min(groups, 32), min(ways * spots, 512)
    for begin in range(0, ways * spots, lanes_at):
        spot = lax.broadcasted_iota(jnp.int32, (128, lanes_at), 1).astype(F32) + float(begin)
        block_no = jnp.floor((spot + 0.5) * (1.0 / cap))
        place = lax.broadcasted_iota(jnp.int32, (128, lanes_at), 0).astype(F32)
        spread_out = jnp.where(spot - block_no * cap == place, 1.0, 0.0).astype(LOW)
        named_row = jnp.zeros((1, lanes_at), F32)
        for first in range(0, groups, some):
            wanted = jnp.concatenate(
                [
                    R.idx[index // size, index % size][0:1, :] + 1.0
                    for index in range(first, first + some)
                ],
                0,
            )
            high = jnp.floor(wanted * (1.0 / 256.0))
            rest = wanted - 256.0 * high
            laid = dot(high.astype(LOW), spread_out) * 256.0 + dot(rest.astype(LOW), spread_out) - 1.0
            own_block = block_no[0:1, :] == float(first) + lax.broadcasted_iota(
                jnp.int32, (some, lanes_at), 0
            ).astype(F32)
            named_row = named_row + jnp.sum(jnp.where(own_block, laid, 0.0), 0, keepdims=True)
        R.named[:, begin : begin + lanes_at] = jnp.broadcast_to(
            named_row.astype(jnp.int32) - dp.me * table_rows, (8, lanes_at)
        )

    once = jnp.where(mp.me == 0, 1.0, 0.0)
    lanes = lax.broadcasted_iota(jnp.int32, (1, 128), 1)
    R.sums[...] = jnp.zeros_like(R.sums)

    def put(place, squares, factor=None):
        for row, values in enumerate(squares):
            total = jnp.sum(jnp.sum(values, 0, keepdims=True), 1, keepdims=True)
            if factor is not None:
                total = total * factor
            R.sums[row : row + 1, :] += jnp.where(lanes == place, total, 0.0)

    def squares_of(weight, gradient, first, second):
        direction = direction_of(weight, gradient, first, second)[2]
        return weight * weight, direction * direction

    def folded(values):
        rows, columns = values.shape
        return jnp.sum(values.reshape(rows // 8, 8, columns), 0)

    def add_up(weight, gradient, first, second):
        squares = squares_of(weight[...], gradient[...], first[...], second[...])
        return [folded(values) for values in squares]

    for tile in range(min(2, tiles)):
        for one in tile_of(tile):
            one.start()
    zero = jnp.zeros((8, width), F32)

    def add_tile(tile, carry):
        side = lax.rem(tile, 2)
        for one in tile_of(tile):
            one.wait()
        hit = (
            lax.broadcasted_iota(jnp.int32, (tile_rows, ways * spots), 0) + tile * tile_rows
            == R.named[0:1, :]
        )
        R.gtile[...] = dot(jnp.where(hit, 1.0, 0.0).astype(LOW), R.inc[...])
        more = add_up(R.tw.at[side], R.gtile, R.tm.at[side], R.tv.at[side])

        @pl.when(tile + 2 < tiles)
        def _():
            for one in tile_of(tile + 2):
                one.start()

        return carry[0] + more[0], carry[1] + more[1]

    put(0, lax.fori_loop(0, tiles, add_tile, (zero, zero)), once)

    for name in names_of_moments:
        moment(name).wait()
    up.arrive()

    R.red_up[...] = up.total(slice(None))
    put(10, add_up(R.w_up, R.red_up, R.up_m_here, R.up_v_here))
    down.arrive()

    R.red_dn[...] = down.total(slice(None)).T
    put(11, add_up(R.w_down, R.red_dn, R.down_m_here, R.down_v_here))
    wo.arrive()
    R.red_out[...] = wo.total(slice(None)).T
    put(9, add_up(R.w_out, R.red_out, R.out_m_here, R.out_v_here))

    small.arrive()
    R.wsum[mp.me] = small.total(slice(None)).astype(LOW)
    weights_in = Gather(mp, of_index(R.wsum), R.ws_send, R.ws_recv)
    weights_in.start()
    first_w.arrive()

    value = first_w.total(slice(None))
    for part in range(3):
        R.red_qkv[part] = value[:, part * heads_w : (part + 1) * heads_w]
    weights_in.relays()
    for part in range(3):
        put(
            6 + part,
            add_up(
                R.w_qkv.at[part], R.red_qkv.at[part], R.qkv_m_here.at[part], R.qkv_v_here.at[part]
            ),
        )
    weights_in.close()
    total = jnp.concatenate([R.wsum[index].astype(F32) for index in range(ways)], 1)
    R.red_in[...] = total[:rin, :]
    put(1, add_up(R.w_in, R.red_in, R.w_in_m_here, R.w_in_v_here), once)
    if strip % 128 == 0:
        R.lnsum[...] = total[rin_up : rin_up + 8, :]
        R.red_ln[...] = R.lnsum[0:4, pl.ds(pl.multiple_of(dp.me * strip, strip), strip)]
    else:
        chosen = lax.broadcasted_iota(jnp.int32, (model, strip), 0) == dp.me * strip + (
            lax.broadcasted_iota(jnp.int32, (model, strip), 1)
        )
        R.red_ln[...] = dot(
            total[rin_up : rin_up + 8, :].astype(LOW), jnp.where(chosen, 1.0, 0.0).astype(LOW)
        )[0:4]
    squares = squares_of(R.ln_params[...], R.red_ln[...], R.ln_m_here[...], R.ln_v_here[...])
    for row in range(4):
        put(2 + row, [values[row : row + 1, :] for values in squares], once)

    R.near[dp.me] = R.sums[...]
    near, near_wait = far_copies(
        dp, lambda dest, source: (R.near.at[dp.me], R.near.at[source]), R.near_send, R.near_recv
    )
    for step in range(1, size):
        near(step).start()
    near_wait()
    R.wide[mp.me] = jnp.sum(R.near[...], 0)
    far_off, far_off_wait = far_copies(
        mp, lambda dest, source: (R.wide.at[mp.me], R.wide.at[source]), R.wide_send, R.wide_recv
    )
    for step in range(1, ways):
        far_off(step).start()
    far_off_wait()
    R.totals[...] = jnp.sum(R.wide[...], 0)

    for thing in (win, win_all, ln, *wc, *dxg, *ag, *mg, up, down, first_w, wo, small_mp, small):
        thing.drain()
    for thing in (named, rows_in, weights_in):
        thing.drain()
    for piece in range(seqs):
        out(piece).drain()
        das(piece).drain()
    for step in range(1, size):
        ask(step).wait_send()
        back(step).wait_send()
        near(step).wait_send()
    for step in range(1, ways):
        far_off(step).wait_send()


def run_layer(cap, ids, levels, noise, cot, weights, moments):
    table, w_in, ln_params, w_qkv, w_out, w_up, w_down = weights
    dp, mp = lax.axis_size("dp"), lax.axis_size("mp")
    seqs, seq_len = ids.shape
    tokens, width = noise.shape
    model = cot.shape[1]
    rin = w_in.shape[0]
    heads_w = w_qkv.shape[2]
    strip, hidden = w_up.shape
    group = tokens * mp
    spots = dp * cap
    wide = round_up(rin, 16) + 16
    far, far_dp = mp // 2, dp // 2
    quarter = model // mp
    in_kind = LOW if rin % 16 == 0 else F32
    tile_rows = max(rows for rows in range(8, 513, 8) if table.shape[0] % rows == 0)
    stacked = (heads_w // HD) * seq_len
    vmem = pl.BlockSpec(memory_space=pltpu.VMEM)
    outside = pl.BlockSpec(memory_space=pl.ANY)
    inputs = dict(
        ids=(ids, vmem),
        levels=(levels, pl.BlockSpec(memory_space=pltpu.SMEM)),
        noise=(noise, vmem),
        cot=(cot, vmem),
        table=(table, outside),
        w_in=(w_in, vmem),
        ln_params=(ln_params, vmem),
        w_qkv=(w_qkv, vmem),
        w_out=(w_out, vmem),
        w_up=(w_up, vmem),
        w_down=(w_down, vmem),
    )
    kept = {}
    for name, (first, second) in zip(("table", "w_in", "ln", "qkv", "out", "up", "down"), moments):
        inputs[name + "_m"] = (first, outside)
        inputs[name + "_v"] = (second, outside)
        if name != "table":
            kept[name + "_m_here"] = kept[name + "_v_here"] = (first.shape, F32)
    outputs = dict(
        out=((tokens, model), F32),
        red_up=((strip, hidden), F32),
        red_dn=((hidden, strip), F32),
        red_qkv=((3, strip, heads_w), F32),
        red_out=((heads_w, strip), F32),
        red_in=((rin, model), F32),
        red_ln=((4, strip), F32),
        inc=((mp * spots, width), LOW),
        named=((8, mp * spots), jnp.int32),
        totals=((8, 128), F32),
    )
    buffers = dict(
        tab=((2, round_up(table.shape[0] // 8, 128), width), F32),
        ask=((dp, 8, 128), F32),
        idx=((mp, dp, 8, 128), F32),
        loc=((spots, 128), jnp.int32),
        give=((spots, width), LOW),
        got=((spots, width), LOW),
        gtile=((tile_rows, width), F32),
        tw=((2, tile_rows, width), F32),
        tm=((2, tile_rows, width), F32),
        tv=((2, tile_rows, width), F32),
        sums=((8, 128), F32),
        near=((dp, 8, 128), F32),
        wide=((mp, 8, 128), F32),
        scores=((2, stacked, seq_len), F32),
        dprobs=((2, stacked, seq_len), F32),
        probs=((2, stacked, seq_len), LOW),
        dscores=((2, stacked, seq_len), LOW),
        upper=((2, stacked, heads_w), LOW),
        gwo=((model, heads_w), LOW),
        wo_first=((far_dp * strip, heads_w), LOW),
        wo_second=((far_dp * strip, heads_w), LOW),
        lnf=((dp, 8, ln_params.shape[1]), F32),
        gains=((8, model), F32),
        lnsum=((8, model), F32),
        sig=((tokens, 1), F32),
        pick=((tokens, spots), LOW),
        rows=((tokens, width), LOW),
        mixed=((tokens, width), LOW),
        x0=((tokens, model), F32),
        a=((group, model), LOW),
        c=((group, model), LOW),
        dx=((group, model), LOW),
        dmid=((tokens, model), F32),
        dmid_all=((group, model), LOW),
        winf=((mp, rin * dp, quarter), in_kind),
        waf=((model, 4 * heads_w), LOW),
        wbf=((model, hidden), LOW),
        wcf=((model, hidden), LOW),
        qkv=((group, 3 * heads_w), LOW),
        o=((group, heads_w), LOW),
        low=((2 * seq_len, heads_w), LOW),
        part=((group, model), LOW),
        first=((far * tokens, model), LOW),
        fold=((far * tokens, model), LOW),
        second=((far * tokens, model), LOW),
        fold_far=((far * tokens, model), LOW),
        h=((2 * seq_len, hidden), F32),
        hb=((group, hidden), LOW),
        dhb=((group, hidden), LOW),
        slope=((group, hidden), LOW),
        gdn=((model, hidden), LOW),
        dx0=((tokens, model), LOW),
        norms=((8, model), F32),
        gm=((mp, width + 16, quarter), LOW),
        gm_first=((far, width + 16, quarter), LOW),
        gm_second=((far, width + 16, quarter), LOW),
        gw=((dp, wide, quarter), LOW),
        gw_first=((far_dp, wide, quarter), LOW),
        gw_second=((far_dp, wide, quarter), LOW),
        up_first=((far_dp * strip, hidden), LOW),
        up_second=((far_dp * strip, hidden), LOW),
        dn_first=((far_dp * strip, hidden), LOW),
        dn_second=((far_dp * strip, hidden), LOW),
        wa_first=((far_dp * strip, 3 * heads_w), LOW),
        wa_second=((far_dp * strip, 3 * heads_w), LOW),
        wsum=((mp, wide, quarter), LOW),
        **kept,
    )
    sems = dict(tab_sem=2, tile_sem=6, moment_sem=12)
    for name in (
        *("win", "ln", "wa", "wx", "wb", "wy", "wc", "wz", "ask", "give", "back"),
        *("up", "dn", "ga", "wo", "gw", "near"),
    ):
        sems[name + "_send"] = sems[name + "_recv"] = dp
    for name in ("wim", "id", "in", "ws", "gm", "wide"):
        sems[name + "_send"] = sems[name + "_recv"] = mp
    for name in ("dx", "a", "c", "e", "as", "os", "cs", "ds"):
        sems[name + "_send"] = sems[name + "_recv"] = seqs * mp
    names = [*inputs, *outputs, *buffers, *sems]
    made = pl.pallas_call(
        functools.partial(layer_kernel, cap, names),
        out_shape=[jax.ShapeDtypeStruct(shape, kind) for shape, kind in outputs.values()],
        in_specs=[spec for _, spec in inputs.values()],
        out_specs=[vmem] * len(outputs),
        scratch_shapes=[
            *[pltpu.VMEM(shape, kind) for shape, kind in buffers.values()],
            *[pltpu.SemaphoreType.DMA((number,)) for number in sems.values()],
        ],
        compiler_params=pltpu.CompilerParams(
            vmem_limit_bytes=VMEM_BYTES, collective_id=1, has_side_effects=True
        ),
        name="layer",
    )(*[value for value, _ in inputs.values()])
    return dict(zip(outputs, made))


def direction_of(weight, gradient, first, second):
    first_new = BETA_ONE * first + (1.0 - BETA_ONE) * gradient
    second_new = BETA_TWO * second + (1.0 - BETA_TWO) * gradient * gradient
    second_hat = second_new * (1.0 / (1.0 - BETA_TWO**STEP))
    inverse = lax.rsqrt(second_hat)
    root = second_hat * inverse + EPS_ADAM
    inverse = inverse * (2.0 - root * inverse)
    inverse = inverse * (2.0 - root * inverse)
    direction = first_new * (1.0 / (1.0 - BETA_ONE**STEP)) * inverse + DECAY * weight
    return first_new, second_new, direction


def update_kernel(part, names, *refs):
    R = types.SimpleNamespace(**dict(zip(names, refs)))
    turn = pl.program_id(0)
    norms = jnp.sqrt(R.totals[...])
    R.norms[...] = norms[0:2, 0:12]
    factors = norms[0:1, :] / (norms[1:2, :] + EPS_ADAM) * RATE

    def piece(name, here, gradient, place, rows=slice(None)):
        weight = getattr(R, name)[here]
        first_new, second_new, direction = direction_of(
            weight, gradient, getattr(R, name + "_m")[here], getattr(R, name + "_v")[here]
        )
        if isinstance(place, int):
            factor = factors[0:1, place : place + 1]
        else:
            factor = jnp.concatenate([factors[0:1, one : one + 1] for one in place], 0)
        getattr(R, name + "_m_new")[here] = first_new
        getattr(R, name + "_v_new")[here] = second_new
        getattr(R, name + "_new")[here] = weight - factor * direction

    def update(name, gradient, place, lead=(), here=slice(None)):
        piece(name, (*lead, here, slice(None)), gradient, place)

    tile = R.table.shape[0]
    spots = R.named.shape[1]

    def table_part(row):
        hit = (
            lax.broadcasted_iota(jnp.int32, (part, spots), 0) + (turn * tile + row)
            == R.named[0:1, :]
        )
        gradient = dot(jnp.where(hit, 1.0, 0.0).astype(LOW), R.inc[...])
        update("table", gradient, 0, (), pl.ds(row, part))

    strips(tile, part, table_part)
    for group in range(3):
        update("qkv", R.red_qkv[group], 6 + group, (group,))
    update("up", R.red_up[...], 10)
    update("down", R.red_dn[...], 11)

    @pl.when(turn == 0)
    def _():
        update("out", R.red_out[...], 9)
        update("w_in", R.red_in[...], 1)
        piece("ln", (slice(None), slice(None)), R.red_ln[...], (2, 3, 4, 5))


def turns_of(rows, parts):
    return [
        turns
        for turns in (5, 4, 2, 1)
        if rows % (8 * turns) == 0 and all(size % (8 * turns) == 0 for size in parts)
    ][0]


def run_update(weights, moments, grads):
    names = ("table", "w_in", "ln", "qkv", "out", "up", "down")
    by_name = dict(zip(names, weights))
    rows, width = by_name["table"].shape
    strip, hidden = by_name["up"].shape
    heads_w = by_name["qkv"].shape[2]
    turns = turns_of(rows, (strip, hidden))
    tile = rows // turns
    part = max(size for size in range(8, 257, 8) if tile % size == 0)
    fixed = lambda array: pl.BlockSpec(array.shape, lambda turn: (0,) * array.ndim)
    specs = dict(
        table=pl.BlockSpec((tile, width), lambda turn: (turn, 0)),
        w_in=fixed(by_name["w_in"]),
        ln=fixed(by_name["ln"]),
        qkv=pl.BlockSpec((3, strip // turns, heads_w), lambda turn: (0, turn, 0)),
        out=fixed(by_name["out"]),
        up=pl.BlockSpec((strip // turns, hidden), lambda turn: (turn, 0)),
        down=pl.BlockSpec((hidden // turns, strip), lambda turn: (turn, 0)),
    )
    inputs = {}
    for name, weight, (first, second) in zip(names, weights, moments):
        inputs[name] = (weight, specs[name])
        inputs[name + "_m"] = (first, specs[name])
        inputs[name + "_v"] = (second, specs[name])
    for name, like in (
        ("red_up", "up"),
        ("red_dn", "down"),
        ("red_qkv", "qkv"),
        ("red_out", "out"),
        ("red_in", "w_in"),
        ("red_ln", "ln"),
    ):
        inputs[name] = (grads[name], specs[like])
    for name in ("inc", "named", "totals"):
        inputs[name] = (grads[name], fixed(grads[name]))
    outputs = {}
    for name, weight in by_name.items():
        for kind in ("_new", "_m_new", "_v_new"):
            outputs[name + kind] = (weight.shape, specs[name])
    outputs["norms"] = ((2, 12), pl.BlockSpec((2, 12), lambda turn: (0, 0)))
    results = pl.pallas_call(
        functools.partial(update_kernel, part, [*inputs, *outputs]),
        grid=(turns,),
        out_shape=[jax.ShapeDtypeStruct(shape, F32) for shape, _ in outputs.values()],
        in_specs=[spec for _, spec in inputs.values()],
        out_specs=[spec for _, spec in outputs.values()],
        compiler_params=pltpu.CompilerParams(vmem_limit_bytes=VMEM_BYTES),
        name="update",
    )(*[value for value, _ in inputs.values()])
    return list(results)


def per_device(
    token_ids,
    levels,
    noise,
    cotangent,
    table,
    table_m,
    table_v,
    w_in,
    w_in_m,
    w_in_v,
    ln_params,
    ln_m,
    ln_v,
    w_qkv,
    qkv_m,
    qkv_v,
    w_out,
    out_m,
    out_v,
    w_up,
    up_m,
    up_v,
    w_down,
    down_m,
    down_v,
):
    dp_count = lax.axis_size("dp")
    seq_count, seq_len = token_ids.shape
    tokens = seq_count * seq_len
    model = cotangent.shape[2]
    cap = round_up(max(2, (3 * tokens + 2 * dp_count - 1) // (2 * dp_count)), 16)
    weights = (table, w_in, ln_params, w_qkv, w_out, w_up, w_down)
    moments = (
        (table_m, table_v),
        (w_in_m, w_in_v),
        (ln_m, ln_v),
        (qkv_m, qkv_v),
        (out_m, out_v),
        (up_m, up_v),
        (down_m, down_v),
    )
    grads = run_layer(
        cap,
        token_ids,
        levels,
        noise.reshape(tokens, -1),
        cotangent.reshape(tokens, model),
        weights,
        moments,
    )
    results = run_update(weights, moments, grads)
    return (grads["out"].reshape(seq_count, seq_len, model), *results)


def solution(mesh):
    return jax.shard_map(
        per_device,
        mesh=mesh,
        in_specs=(
            P(("dp", "mp"), None),
            P(("dp", "mp")),
            P(("dp", "mp"), None, None),
            P(("dp", "mp"), None, None),
            P("dp", None),
            P("dp", None),
            P("dp", None),
            P("dp", None),
            P("dp", None),
            P("dp", None),
            P(None, "dp"),
            P(None, "dp"),
            P(None, "dp"),
            P(None, "dp", "mp"),
            P(None, "dp", "mp"),
            P(None, "dp", "mp"),
            P("mp", "dp"),
            P("mp", "dp"),
            P("mp", "dp"),
            P("dp", "mp"),
            P("dp", "mp"),
            P("dp", "mp"),
            P("mp", "dp"),
            P("mp", "dp"),
            P("mp", "dp"),
        ),
        out_specs=(
            P(("dp", "mp"), None, None),
            P("dp", None),
            P("dp", None),
            P("dp", None),
            P("dp", None),
            P("dp", None),
            P("dp", None),
            P(None, "dp"),
            P(None, "dp"),
            P(None, "dp"),
            P(None, "dp", "mp"),
            P(None, "dp", "mp"),
            P(None, "dp", "mp"),
            P("mp", "dp"),
            P("mp", "dp"),
            P("mp", "dp"),
            P("dp", "mp"),
            P("dp", "mp"),
            P("dp", "mp"),
            P("mp", "dp"),
            P("mp", "dp"),
            P("mp", "dp"),
            P(),
        ),
        check_vma=False,
    )
```

```python
import functools
import types

import jax
import jax.numpy as jnp
from jax import lax
from jax.experimental import pallas as pl
from jax.experimental.pallas import tpu as pltpu
from jax.sharding import PartitionSpec as P

HD = 64
LEVELS = 64
STEP = 10


EPS_NORM = 1e-06
EPS_LAYER = 1e-05
EPS_ADAM = 1e-06
BETA_ONE = 0.9
BETA_TWO = 0.999
DECAY = 0.01
RATE = 0.5
SIGMA_TOP = 10.0

F32 = jnp.float32
LOW = jnp.bfloat16
VMEM_BYTES = 63 * 1024 * 1024


def sigma_of(levels):
    frac = levels.astype(jnp.float32) / (LEVELS - 1)
    return jnp.exp(frac * jnp.log(SIGMA_TOP))


def lamb_moments(weight, gradient, first, second):
    first_new = BETA_ONE * first + (1.0 - BETA_ONE) * gradient
    second_new = BETA_TWO * second + (1.0 - BETA_TWO) * gradient * gradient
    first_hat = first_new / (1.0 - BETA_ONE**STEP)
    second_hat = second_new / (1.0 - BETA_TWO**STEP)
    direction = first_hat / (jnp.sqrt(second_hat) + EPS_ADAM) + DECAY * weight
    return (first_new, second_new, direction)


def trust_factors(ratio):
    return (
        ratio[0],
        ratio[1],
        ratio[2:6][:, None],
        ratio[6:9][:, None, None],
        ratio[9],
        ratio[10],
        ratio[11],
    )


def round_up(value, step):
    return -(-value // step) * step


def dot(left, right):
    return jnp.dot(left, right, preferred_element_type=F32)


def dot_nt(left, right):
    return lax.dot_general(left, right, (((1,), (1,)), ((), ())), preferred_element_type=F32)


def dot_tn(left, right):
    return lax.dot_general(left, right, (((0,), (0,)), ((), ())), preferred_element_type=F32)


def strips(total, step, body, unroll=1):
    step = min(step, total)

    def one(turn, carry):
        body(pl.multiple_of(turn * step, step))
        return carry

    lax.fori_loop(0, total // step, one, 0, unroll=unroll)


class Line:
    def __init__(self, axis):
        self.axis = axis
        self.size = lax.axis_size(axis)
        self.far = self.size // 2
        self.me = lax.axis_index(axis)
        self.hi = lax.div(self.me, 2)
        self.lo = lax.rem(self.me, 2)
        self.partner = self.hi * 2 + (1 - self.lo)

    def at(self, step):
        return lax.rem(self.hi + step + self.far, self.far)

    def push(self, index, src, dst, send, recv):
        return pltpu.make_async_remote_copy(
            src_ref=src,
            dst_ref=dst,
            send_sem=send,
            recv_sem=recv,
            device_id={self.axis: index},
            device_id_type=pl.DeviceIdType.MESH,
        )

    def signal(self, sem, index):
        pl.semaphore_signal(
            sem, inc=1, device_id={self.axis: index}, device_id_type=pl.DeviceIdType.MESH
        )


def meet(pair_lines, all_lines=()):
    sem = pltpu.get_barrier_semaphore()
    count = 0
    for line in pair_lines:
        for step in range(1, line.far):
            line.signal(sem, line.at(step) * 2 + line.lo)
            count += 1
        line.signal(sem, line.partner)
        count += 1
    for line in all_lines:
        for step in range(1, line.size):
            line.signal(sem, lax.rem(line.me + step, line.size))
            count += 1
    pl.semaphore_wait(sem, count)


class Gather:
    def __init__(self, line, at, send, recv, base=0, ends=False):
        self.line, self.at, self.send, self.recv, self.base = line, at, send, recv, base
        self.ends = ends and line.far == 4

    def source(self, step):
        line = self.line
        if not self.ends:
            return line.at(-step)
        order = ((1, 2, 3), (0, 3, 2), (3, 0, 1), (2, 1, 0))
        hi = order[3][step - 1]
        for place in (2, 1, 0):
            hi = jnp.where(line.hi == place, order[place][step - 1], hi)
        return hi

    def far_sends(self, act):
        line = self.line
        for step in range(1, line.far):
            one = self.copy(line.me, step - 1, line.at(step) * 2 + line.lo)
            if self.ends and step != 2:
                pl.when(line.hi != (3 if step == 1 else 0))(functools.partial(act, one))
            else:
                act(one)

    def to_end(self, act):
        line = self.line
        dest = jnp.where(line.hi == 1, 0, 3)
        one = self.copy((3 - dest) * 2 + line.lo, 2 * line.far - 1, dest * 2 + line.lo)
        pl.when((line.hi == 1) | (line.hi == 2))(functools.partial(act, one))

    def copy(self, index, slot, dest):
        block = self.at(index)
        return self.line.push(
            dest, block, block, self.send.at[self.base + slot], self.recv.at[self.base + index]
        )

    def start_far(self):
        self.far_sends(lambda one: one.start())

    def start_near(self):
        self.copy(self.line.me, self.line.far - 1, self.line.partner).start()

    def start(self):
        self.start_far()
        self.start_near()

    def relay(self, step):
        line = self.line
        handed = self.copy(self.source(step) * 2 + line.lo, line.far - 1 + step, line.partner)
        handed.wait_recv()
        if self.ends and step == 2:
            self.to_end(lambda one: one.start())
        handed.start()

    def relays(self):
        for step in range(1, self.line.far):
            self.relay(step)

    def close(self):
        line = self.line
        for step in range(line.far):
            self.copy(line.at(-step) * 2 + (1 - line.lo), 0, line.partner).wait_recv()

    def drain(self):
        self.far_sends(lambda one: one.wait_send())
        if self.ends:
            self.to_end(lambda one: one.wait_send())
        for slot in range(self.line.far - 1, 2 * self.line.far - 1):
            self.copy(self.line.me, slot, self.line.partner).wait_send()


class Scatter:
    def __init__(self, line, part, first, second, send, recv, base=0, extra=None):
        self.line, self.part, self.first, self.second = line, part, first, second
        self.send, self.recv, self.base = send, recv, base
        self.extra = extra if line.far == 4 else None

    def clear(self):
        line = self.line
        if self.extra is not None:

            @pl.when((line.hi == 0) | (line.hi == 3))
            def _():
                slot = self.second(3 - line.hi)
                slot[...] = jnp.zeros(slot.shape, LOW)

    def order(self, step):
        line = self.line
        if self.extra is None:
            return line.at(step)
        table = ((3, 2, 1), (2, 0, 3), (1, 3, 0), (0, 1, 2))
        hi = table[3][step - 1]
        for place in (2, 1, 0):
            hi = jnp.where(line.hi == place, table[place][step - 1], hi)
        return hi

    def traded(self, hi):
        line = self.line
        return line.push(
            line.partner,
            self.part(hi * 2 + (1 - line.lo)),
            self.first(hi),
            self.send.at[self.base + hi],
            self.recv.at[self.base + hi],
        )

    def passed(self, step):
        line = self.line
        hi = self.order(step)
        return line.push(
            hi * 2 + line.lo,
            self.part(hi * 2 + line.lo),
            self.second(line.hi),
            self.send.at[self.base + line.far + step - 1],
            self.recv.at[self.base + line.far + line.hi],
        )

    def to_next(self):
        line = self.line
        return line.push(
            jnp.where(line.hi < 2, 1, 2) * 2 + line.lo,
            self.part((3 - jnp.where(line.hi < 2, 0, 3)) * 2 + line.lo),
            self.extra,
            self.send.at[self.base + line.far],
            self.recv.at[self.base + 2 * line.far],
        )

    def turn_of(self, turn):
        line = self.line
        if self.extra is None:
            return lax.rem(line.hi + turn + 1, line.far)
        hi = line.hi
        for step in range(1, line.far):
            hi = jnp.where(turn == step - 1, self.order(step), hi)
        return hi

    def is_end(self):
        return (self.line.hi == 0) | (self.line.hi == 3)

    def trade(self, hi):
        self.traded(hi).start()

    def trade_all(self):
        for step in range(1, self.line.far + 1):
            self.trade(self.order(step) if step < self.line.far else self.line.hi)

    def pass_on(self, step):
        line = self.line
        hi = self.order(step)
        self.traded(hi).wait_recv()
        mine, other = self.part(hi * 2 + line.lo), self.first(hi)
        if self.extra is None or step == 2:
            mine[...] = (mine[...].astype(F32) + other[...].astype(F32)).astype(LOW)
            self.passed(step).start()
        elif step == 1:
            mine[...] = (mine[...].astype(F32) + other[...].astype(F32)).astype(LOW)

            @pl.when(self.is_end())
            def _():
                self.to_next().start()

            @pl.when(jnp.logical_not(self.is_end()))
            def _():
                self.passed(step).start()
        else:

            @pl.when(self.is_end())
            def _():
                mine[...] = (mine[...].astype(F32) + other[...].astype(F32)).astype(LOW)

            @pl.when(jnp.logical_not(self.is_end()))
            def _():
                line.push(
                    line.partner,
                    self.extra,
                    self.extra,
                    self.send.at[self.base],
                    self.recv.at[self.base + 2 * line.far],
                ).wait_recv()
                mine[...] = (
                    mine[...].astype(F32) + other[...].astype(F32) + self.extra[...].astype(F32)
                ).astype(LOW)

            self.passed(step).start()

    def arrive(self):
        line = self.line
        self.traded(line.hi).wait_recv()
        for step in range(1, line.far):
            hi = line.at(-step)
            one = line.push(
                line.partner,
                self.second(hi),
                self.second(hi),
                self.send.at[self.base],
                self.recv.at[self.base + line.far + hi],
            )
            if self.extra is None:
                one.wait_recv()
            else:
                pl.when(jnp.logical_not(self.is_end()) | (hi + line.hi != 3))(one.wait_recv)

    def total(self, here):
        line = self.line
        value = self.part(line.me)[here, :].astype(F32) + self.first(line.hi)[here, :].astype(F32)
        for step in range(1, line.far):
            value = value + self.second(line.at(-step))[here, :].astype(F32)
        return value

    def drain(self):
        line = self.line
        for step in range(line.far):
            self.traded(line.at(step)).wait_send()
        for step in range(1, line.far):
            if self.extra is not None and step == 1:
                pl.when(self.is_end())(lambda: self.to_next().wait_send())
                pl.when(jnp.logical_not(self.is_end()))(lambda: self.passed(1).wait_send())
            else:
                self.passed(step).wait_send()


def block_rows(ref, rows, first=0):
    return lambda index: ref.at[pl.ds(pl.multiple_of((index + first) * rows, rows), rows)]


def part_rows(ref, rows, first, count):
    return lambda index: ref.at[pl.ds(pl.multiple_of(index * rows + first, count), count)]


def of_index(ref):
    return lambda index: ref.at[index]


def norm_rows(values):
    center = values - jnp.mean(values, -1, keepdims=True)
    spread = jnp.mean(center * center, -1, keepdims=True)
    inverse = lax.rsqrt(spread + EPS_LAYER)
    return center * inverse, inverse


def norm_back(values, gain, grad):
    unit, inverse = norm_rows(values)
    inner = grad * gain
    shared = jnp.mean(inner, -1, keepdims=True)
    along = jnp.mean(inner * unit, -1, keepdims=True)
    return inverse * (inner - shared - unit * along), unit


def head_masks(width):
    lane = lax.broadcasted_iota(jnp.int32, (1, width), 1)
    return [
        jnp.where((lane >= head * HD) & (lane < (head + 1) * HD), 1.0, 0.0)
        for head in range(width // HD)
    ]


def spread_heads(values, masks):
    return jnp.concatenate([values * mask.astype(LOW) for mask in masks], 0)


def join_heads(values, masks, rows):
    total = values[0:rows] * masks[0]
    for head in range(1, len(masks)):
        total = total + values[head * rows : (head + 1) * rows] * masks[head]
    return total


TAIL = (
    0.2256758632450557,
    0.22566952478278277,
    0.2078438574180613,
    0.16853390514724884,
    0.14146086231844687,
    -0.005667717379728321,
    0.16915486959066833,
    -0.18294364197603524,
    0.05027260226320005,
)


def normal_tail(size, bell):
    base = 1.0 + (0.4 * 0.5**0.5) * size
    t = pl.reciprocal(base, approx=True)
    t = t * (2.0 - base * t)
    t = t * (2.0 - base * t)
    value = jnp.full_like(t, 0.5 * TAIL[-1])
    for factor in TAIL[-2::-1]:
        value = value * t + 0.5 * factor
    return value * t * bell


def far_copies(line, make, sends, recvs):
    def copy(step):
        dest = lax.rem(line.me + step, line.size)
        src, dst = make(dest, line.me)
        return line.push(dest, src, dst, sends.at[step], recvs.at[line.me])

    def wait():
        for step in range(1, line.size):
            source = lax.rem(line.me + line.size - step, line.size)
            _, dst = make(source, source)
            line.push(line.partner, dst, dst, sends.at[0], recvs.at[source]).wait_recv()

    return copy, wait


def layer_kernel(cap, names, *refs):
    R = types.SimpleNamespace(**dict(zip(names, refs)))
    dp, mp = Line("dp"), Line("mp")
    size, ways = dp.size, mp.size
    seqs, seq_len = R.ids.shape
    tokens, width = R.noise.shape
    model = R.cot.shape[1]
    heads_w = R.o.shape[1]
    hidden = R.wbf.shape[1]
    table_rows = R.table.shape[0]
    rin = R.w_in.shape[0]
    rin_up = round_up(rin, 16)
    quarter = model // ways
    strip = R.w_up.shape[0]
    spots = size * cap
    far = mp.far
    count = seqs * far
    own_strip = pl.ds(pl.multiple_of(dp.me * strip, strip), strip)
    mine = pl.ds(pl.multiple_of(dp.me * cap, cap), cap)

    some_rows = seq_len // 2

    def rows_of(piece):
        return lambda row: pl.ds(pl.multiple_of(piece * seq_len + row, some_rows), some_rows)

    def own_rows(piece):
        first = pl.multiple_of((piece * ways + mp.me) * seq_len, seq_len)
        return lambda row: pl.ds(pl.multiple_of(first + row, some_rows), some_rows)

    def by_rows(body):
        for row in range(0, seq_len, some_rows):
            body(row)

    def halves(ref, send, recv):
        return [
            Gather(mp, block_rows(ref, seq_len, piece * ways), send, recv, piece * ways)
            for piece in range(seqs)
        ]

    def sums(part, first, second, send, recv):
        return lambda piece: Scatter(
            mp,
            block_rows(part, seq_len, piece * ways),
            block_rows(first, seq_len, piece * far),
            block_rows(second, seq_len, piece * far),
            send,
            recv,
            piece * ways,
        )

    def turns(body, hooks):
        def one(turn, carry):
            for place, action in hooks:
                pl.when(turn == place)(action)
            piece = lax.div(turn, far)
            hi = lax.rem(mp.hi + lax.rem(turn, far) + 1, far)
            base = pl.multiple_of((piece * ways + 2 * hi) * seq_len, 2 * seq_len)
            body(turn, piece, hi, base)
            return carry

        lax.fori_loop(0, count, one, 0)

    def hand_on(scatter, turn):
        step = lax.rem(turn, far)

        @pl.when(step != 0)
        def _():
            scatter.pass_on(step)

    def later_pieces(gathers):
        hooks = []
        for piece in range(1, seqs):
            hooks.append((piece * far - 1, gathers[piece].relays))
            hooks.append((piece * far, gathers[piece].close))
        return hooks

    def early_ends(end):
        return [((piece + 2) * far - 1, functools.partial(end, piece)) for piece in range(seqs - 1)]

    chunk = R.tab.shape[1]
    pieces = -(-table_rows // chunk)

    def fetch(piece):
        rows = min(chunk, table_rows - piece * chunk)
        return pltpu.make_async_copy(
            R.table.at[pl.ds(piece * chunk, rows)],
            R.tab.at[piece % 2, pl.ds(0, rows)],
            R.tab_sem.at[piece % 2],
        )

    for piece in range(min(2, pieces)):
        fetch(piece).start()

    names_of_moments = [
        name + kind for name in ("w_in", "ln", "qkv", "out", "up", "down") for kind in ("_m", "_v")
    ]

    def moment(name):
        return pltpu.make_async_copy(
            getattr(R, name), getattr(R, name + "_here"), R.moment_sem.at[names_of_moments.index(name)]
        )

    tile_rows = R.gtile.shape[0]
    tiles = table_rows // tile_rows

    def tile_of(tile):
        side = lax.rem(tile, 2)
        rows = pl.ds(pl.multiple_of(tile * tile_rows, tile_rows), tile_rows)
        return [
            pltpu.make_async_copy(source.at[rows], dest.at[side], R.tile_sem.at[2 * place + side])
            for place, (source, dest) in enumerate(
                ((R.table, R.tw), (R.table_m, R.tm), (R.table_v, R.tv))
            )
        ]

    eye = lax.broadcasted_iota(jnp.int32, (seq_len, seq_len), 0) == lax.broadcasted_iota(
        jnp.int32, (seq_len, seq_len), 1
    )
    id_rows = R.ids[...].astype(F32)
    ids = jnp.concatenate(
        [
            jnp.sum(jnp.where(eye, id_rows[seq : seq + 1, :], 0.0), 1, keepdims=True)
            for seq in range(seqs)
        ],
        0,
    )
    lane = lax.broadcasted_iota(jnp.int32, (tokens, 128), 1).astype(F32)
    low_end = lane * float(table_rows)
    owned = jnp.where((ids >= low_end) & (ids < low_end + float(table_rows)), 1.0, 0.0)
    before = jnp.where(
        lax.broadcasted_iota(jnp.int32, (tokens, tokens), 0)
        >= lax.broadcasted_iota(jnp.int32, (tokens, tokens), 1),
        1.0,
        0.0,
    )
    ranks = dot(before.astype(LOW), owned.astype(LOW))
    rank = jnp.sum(owned * ranks, 1, keepdims=True) - 1.0
    slot = jnp.sum(owned * lane, 1, keepdims=True) * cap + rank
    placed = jnp.where(lane == rank, 1.0, 0.0)
    upper = jnp.floor(ids * (1.0 / 256.0))
    lower = ids - upper * 256.0
    parts = jnp.concatenate([placed * upper, placed * lower, placed], 1).astype(LOW)
    asked = dot_tn(owned.astype(LOW), parts)
    asked = asked[:, :128] * 256.0 + asked[:, 128:256] + asked[:, 256:] - 1.0
    for index in range(size):
        R.ask[index] = jnp.broadcast_to(asked[index : index + 1, :], (8, 128))
    R.idx[mp.me, dp.me] = R.ask[dp.me]

    def spread(part, first, second, extra, send, recv):
        blocks = [block_rows(ref, strip) for ref in (part, first, second)]
        return Scatter(dp, *blocks, send, recv, 0, extra)

    up = spread(R.wbf, R.up_first, R.up_second, R.up_extra, R.up_send, R.up_recv)
    down = spread(R.gdn, R.dn_first, R.dn_second, R.dn_extra, R.dn_send, R.dn_recv)
    first_w = spread(
        R.waf.at[:, : 3 * heads_w], R.wa_first, R.wa_second, R.wa_extra, R.ga_send, R.ga_recv
    )
    wo = spread(R.gwo, R.wo_first, R.wo_second, R.wo_extra, R.wo_send, R.wo_recv)
    small = Scatter(
        dp,
        *[of_index(ref) for ref in (R.gw, R.gw_first, R.gw_second)],
        R.gw_send,
        R.gw_recv,
        0,
        R.gw_extra,
    )
    for scatter in (up, down, first_w, wo, small):
        scatter.clear()

    meet([mp], [dp])
    ask, ask_wait = far_copies(
        dp,
        lambda dest, source: (R.ask.at[dest], R.idx.at[mp.me, source]),
        R.ask_send,
        R.ask_recv,
    )
    for step in range(1, size):
        ask(step).start()

    mine_in = R.winf.at[mp.me]
    win = Gather(dp, block_rows(mine_in, rin), R.win_send, R.win_recv, 0, True)
    win_all = Gather(mp, of_index(R.winf), R.wim_send, R.wim_recv)
    ln = Gather(dp, of_index(R.lnf), R.ln_send, R.ln_recv)
    half_strip = strip // 2

    def in_halves(ref, *names_of):
        return [
            Gather(dp, part_rows(ref, strip, piece * half_strip, half_strip), send, recv, 0, True)
            for piece, (send, recv) in enumerate(names_of)
        ]

    wa = in_halves(R.waf, (R.wa_send, R.wa_recv), (R.wx_send, R.wx_recv))
    wb = in_halves(R.wbf, (R.wb_send, R.wb_recv), (R.wy_send, R.wy_recv))
    wc = in_halves(R.wcf, (R.wc_send, R.wc_recv), (R.wz_send, R.wz_recv))
    dxg = halves(R.dx, R.dx_send, R.dx_recv)
    ag = halves(R.a, R.a_send, R.a_recv)
    cg = halves(R.c, R.c_send, R.c_recv)
    mg = halves(R.dmid_all, R.e_send, R.e_recv)

    mine_in[pl.ds(pl.multiple_of(dp.me * rin, rin), rin), :] = (
        R.w_in[:, pl.ds(pl.multiple_of(mp.me * quarter, quarter), quarter)]
        .astype(LOW)
        .astype(R.winf.dtype)
    )
    win.start()
    shares = R.ln_params[...].astype(LOW).astype(F32)
    R.lnf[dp.me] = jnp.concatenate([shares, jnp.zeros_like(shares)], 0)
    ln.start()
    for part in range(3):
        R.waf[own_strip, part * heads_w : (part + 1) * heads_w] = R.w_qkv[part].astype(LOW)
    R.waf[own_strip, 3 * heads_w :] = R.w_out[...].T.astype(LOW)
    wa[0].start()
    wa[1].start_near()
    for name in names_of_moments:
        moment(name).start()

    for seq in range(seqs):
        level = jnp.full((seq_len, 1), R.levels[seq], jnp.int32).astype(F32) / (LEVELS - 1)
        R.sig[seq * seq_len : (seq + 1) * seq_len, :] = jnp.exp(level * jnp.log(SIGMA_TOP))

    def scale_at(here):
        sig = R.sig[here, :]
        return sig * lax.rsqrt(1.0 + sig * sig)

    for piece in range(seqs):
        here, there = rows_of(piece), own_rows(piece)

        def scale_cot(row, here=here, there=there):
            R.dx[there(row), :] = (R.cot[here(row), :].astype(F32) * scale_at(here(row))).astype(LOW)

        by_rows(scale_cot)
        dxg[piece].start()
    R.wbf[own_strip, :] = R.w_up[...].astype(LOW)
    R.wcf[own_strip, :] = R.w_down[...].T.astype(LOW)
    for gather in wb:
        gather.start_near()
    R.pick[...] = jnp.where(
        lax.broadcasted_iota(jnp.int32, (tokens, spots), 1).astype(F32) == slot, 1.0, 0.0
    ).astype(LOW)
    ln.relays()
    win.relays()

    ask_wait()
    small_eye = lax.broadcasted_iota(jnp.int32, (cap, 128), 0) == lax.broadcasted_iota(
        jnp.int32, (cap, 128), 1
    )

    def locate(index, carry):
        row = R.idx[mp.me, index][0:1, :]
        column = jnp.sum(jnp.where(small_eye, row, 0.0), 1, keepdims=True)
        local = column.astype(jnp.int32) - dp.me * table_rows
        R.loc[pl.ds(pl.multiple_of(index * cap, cap), cap), :] = jnp.broadcast_to(local, (cap, 128))
        return carry

    lax.fori_loop(0, size, locate, 0, unroll=True)
    win.close()
    win_all.start()
    found = None
    for piece in range(pieces):
        fetch(piece).wait()
        rows = min(chunk, table_rows - piece * chunk)
        if rows < chunk:
            R.tab[piece % 2, rows:, :] = jnp.zeros((chunk - rows, width), F32)
        hit = (
            lax.broadcasted_iota(jnp.int32, (spots, chunk), 1) + piece * chunk == R.loc[:, 0:1]
        )
        more = dot(jnp.where(hit, 1.0, 0.0).astype(LOW), R.tab[piece % 2].astype(LOW))
        found = more if found is None else found + more
        if piece + 2 < pieces:
            fetch(piece + 2).start()
    R.give[...] = found.astype(LOW)

    give, give_wait = far_copies(
        dp,
        lambda dest, source: (block_rows(R.give, cap)(dest), block_rows(R.got, cap)(source)),
        R.give_send,
        R.give_recv,
    )
    for step in range(1, size):
        give(step).start()
    R.got[mine, :] = R.give[mine, :]
    wa[1].start_far()
    win_all.relays()
    wa[0].relays()
    ln.close()
    wide_ln = R.ln_params.shape[1]
    if wide_ln % 128 == 0:
        R.gains[...] = jnp.concatenate([R.lnf[index] for index in range(size)], 1)
    else:
        total = jnp.zeros((8, model), F32)
        for index in range(size):
            place = lax.broadcasted_iota(
                jnp.int32, (wide_ln, model), 1
            ) == index * wide_ln + lax.broadcasted_iota(jnp.int32, (wide_ln, model), 0)
            total = total + dot(R.lnf[index].astype(LOW), jnp.where(place, 1.0, 0.0).astype(LOW))
        R.gains[...] = total
    named = Gather(mp, of_index(R.idx), R.id_send, R.id_recv)

    give_wait()
    rows = dot(R.pick[...], R.got[...])
    R.rows[...] = rows.astype(LOW)
    sig = R.sig[...]
    unit = rows * lax.rsqrt(jnp.mean(rows * rows, -1, keepdims=True) + EPS_NORM)
    R.mixed[...] = ((unit + sig * R.noise[...].astype(F32)) * lax.rsqrt(1.0 + sig * sig)).astype(LOW)
    win_all.close()
    for index in range(ways):
        R.x0[:, index * quarter : (index + 1) * quarter] = dot(
            R.mixed[...], R.winf[index].astype(LOW)
        )

    for piece in range(seqs):
        here, there = rows_of(piece), own_rows(piece)

        def first_norm(row, here=here, there=there):
            normed, _ = norm_rows(R.x0[here(row), :])
            R.a[there(row), :] = (normed * R.gains[0:1, :] + R.gains[1:2, :]).astype(LOW)

        by_rows(first_norm)
        ag[piece].start()
    for gather in dxg:
        gather.relays()
    wa[1].relays()
    for gather in wb:
        gather.start_far()
    for gather in wc:
        gather.start_near()
    named.start()
    ag[0].relays()
    for gather in (*wa, ag[0]):
        gather.close()

    att = sums(R.part, R.fold, R.fold_far, R.as_send, R.as_recv)
    dcs = sums(R.part, R.fold, R.fold_far, R.cs_send, R.cs_recv)
    das = sums(R.part, R.fold, R.fold_far, R.ds_send, R.ds_recv)
    out = sums(R.c, R.first, R.second, R.os_send, R.os_recv)
    masks = head_masks(heads_w)

    all_rows = (heads_w // HD) * seq_len
    scale = HD ** (-0.5)

    def softmax(seq, row):
        scores = R.scores[seq, row : row + 64, :]
        raised = jnp.exp((scores - jnp.max(scores, -1, keepdims=True)) * scale)
        return raised * (1.0 / jnp.sum(raised, -1, keepdims=True))

    def attend(turn, piece, hi, base):
        here = pl.ds(base, 2 * seq_len)
        R.qkv[here, :] = dot(R.a[here, :], R.waf[:, : 3 * heads_w]).astype(LOW)
        rows_at = [
            pl.ds(pl.multiple_of(base + seq * seq_len, seq_len), seq_len) for seq in range(2)
        ]
        for seq, rows in enumerate(rows_at):
            queries = spread_heads(R.qkv[rows, :heads_w], masks)
            R.scores[seq] = dot_nt(queries, R.qkv[rows, heads_w : 2 * heads_w])
        for seq, rows in enumerate(rows_at):
            for row in range(0, all_rows, 64):
                R.probs[seq, row : row + 64, :] = softmax(seq, row).astype(LOW)
            seen = dot(R.probs[seq], R.qkv[rows, 2 * heads_w : 3 * heads_w])
            R.o[rows, :] = join_heads(seen, masks, seq_len).astype(LOW)
        hand_on(att(piece), turn)
        R.part[here, :] = dot_nt(R.o[here, :], R.waf[:, 3 * heads_w :]).astype(LOW)
        att(piece).trade(hi)

    def second_norm(piece):
        scatter, here, there = att(piece), rows_of(piece), own_rows(piece)
        scatter.arrive()

        def norm(row):
            x1 = R.x0[here(row), :] + scatter.total(pl.ds(row, some_rows))
            R.out[here(row), :] = x1
            normed, _ = norm_rows(x1)
            R.c[there(row), :] = (normed * R.gains[2:3, :] + R.gains[3:4, :]).astype(LOW)

        by_rows(norm)
        cg[piece].start()

    def second_half():
        wb[0].relays()
        for gather in wc:
            gather.start_far()

    turns(
        attend,
        [
            *later_pieces(ag),
            (count - 2, second_half),
            *early_ends(second_norm),
            (count - 1, wb[1].relays),
        ],
    )
    second_norm(seqs - 1)
    named.relays()
    cg[0].relays()
    for gather in wb:
        gather.close()
    cg[0].close()
    for piece in range(seqs):
        att(piece).drain()

    def activate(turn, piece, hi, base):
        R.h[...] = dot(R.c[pl.ds(base, 2 * seq_len), :], R.wbf[...])

        def gelu(row):
            there = pl.ds(pl.multiple_of(base + row, 64), 64)
            step = min(256, hidden)
            for col in range(0, hidden, step):
                h = R.h[pl.ds(row, 64), col : col + step]
                bell = jnp.exp(-0.5 * h * h)
                tail = normal_tail(jnp.abs(h), bell)
                gate = jnp.where(h >= 0.0, 1.0 - tail, tail)
                slope = gate + h * (bell * 0.3989422804014327)
                R.hb[there, col : col + step] = (h * gate).astype(LOW)
                R.slope[there, col : col + step] = slope.astype(LOW)

        strips(2 * seq_len, 64, gelu)

    turns(
        activate, [*later_pieces(cg), (count - 3, wc[0].relays), (count - 2, wc[1].relays)]
    )


    due = [(scatter, step) for scatter in (down, up) for step in range(1, dp.far)]

    def pass_due(number):
        for _ in range(min(number, len(due))):
            scatter, step = due.pop(0)
            scatter.pass_on(step)

    block = 2 * strip if (2 * strip) % 128 == 0 else min(256, model)

    def grads(make, trades):
        if block == 2 * strip:

            def turn_of(turn, carry):
                hi = up.turn_of(turn)
                make(pl.ds(pl.multiple_of(hi * block, block), block))
                for scatter in trades:
                    scatter.trade(hi)
                return carry

            lax.fori_loop(0, dp.far, turn_of, 0)
        else:
            strips(model, block, lambda col: make(pl.ds(col, block)))
            for scatter in trades:
                scatter.trade_all()

    def down_grads(cols):
        R.gdn[cols, :] = dot_tn(R.dx[:, cols], R.hb[...]).astype(LOW)

    def up_grads(cols):
        R.wbf[cols, :] = dot_tn(R.c[:, cols], R.dhb[...]).astype(LOW)

    for gather in dxg:
        gather.close()
    grads(down_grads, ())
    for gather in wc:
        gather.close()
    down.trade_all()

    def feed_back(turn, piece, hi, base):
        here = pl.ds(base, 2 * seq_len)
        R.h[...] = dot(R.dx[here, :], R.wcf[...])

        def bend(row):
            there = pl.ds(pl.multiple_of(base + row, 64), 64)
            R.dhb[there, :] = (R.h[pl.ds(row, 64), :] * R.slope[there, :].astype(F32)).astype(LOW)

        strips(2 * seq_len, 64, bend)
        hand_on(dcs(piece), turn)
        R.part[here, :] = dot_nt(R.dhb[here, :], R.wbf[...]).astype(LOW)
        dcs(piece).trade(hi)

    R.norms[...] = jnp.zeros_like(R.norms)

    def second_back(piece):
        scatter, here, there = dcs(piece), rows_of(piece), own_rows(piece)
        scatter.arrive()

        def back(row):
            dc = scatter.total(pl.ds(row, some_rows))
            grad, unit = norm_back(R.out[here(row), :], R.gains[2:3, :], dc)
            grad = grad + R.cot[here(row), :].astype(F32) * scale_at(here(row))
            R.dmid[here(row), :] = grad
            R.dmid_all[there(row), :] = grad.astype(LOW)
            R.norms[2:3, :] += jnp.sum(dc * unit, 0, keepdims=True)
            R.norms[3:4, :] += jnp.sum(dc, 0, keepdims=True)

        by_rows(back)
        mg[piece].start()

    turns(feed_back, early_ends(second_back))
    for gather in (*wb, *wa):
        gather.drain()
    grads(up_grads, ())
    second_back(seqs - 1)
    mg[0].relays()
    mg[0].close()
    for piece in range(seqs):
        dcs(piece).drain()

    def attend_back(turn, piece, hi, base):
        here = pl.ds(base, 2 * seq_len)
        R.low[...] = dot(R.dmid_all[here, :], R.waf[:, 3 * heads_w :]).astype(LOW)
        rows_at = [
            pl.ds(pl.multiple_of(base + seq * seq_len, seq_len), seq_len) for seq in range(2)
        ]
        for seq, rows in enumerate(rows_at):
            queries = spread_heads(R.qkv[rows, :heads_w], masks)
            R.scores[seq] = dot_nt(queries, R.qkv[rows, heads_w : 2 * heads_w])
            R.upper[seq] = spread_heads(R.low[seq * seq_len : (seq + 1) * seq_len, :], masks)
            R.dprobs[seq] = dot_nt(R.upper[seq], R.qkv[rows, 2 * heads_w : 3 * heads_w])
        for seq, rows in enumerate(rows_at):
            for row in range(0, all_rows, 64):
                probs = softmax(seq, row)
                grad_probs = R.dprobs[seq, row : row + 64, :]
                inner = jnp.sum(probs * grad_probs, -1, keepdims=True)
                R.probs[seq, row : row + 64, :] = probs.astype(LOW)
                R.dscores[seq, row : row + 64, :] = (probs * (grad_probs - inner)).astype(LOW)
            keys = R.qkv[rows, heads_w : 2 * heads_w]
            queries = spread_heads(R.qkv[rows, :heads_w], masks)
            R.qkv[rows, 2 * heads_w : 3 * heads_w] = dot_tn(R.probs[seq], R.upper[seq]).astype(LOW)
            R.qkv[rows, heads_w : 2 * heads_w] = (dot_tn(R.dscores[seq], queries) * scale).astype(LOW)
            R.qkv[rows, :heads_w] = (
                join_heads(dot(R.dscores[seq], keys), masks, seq_len) * scale
            ).astype(LOW)
        hand_on(das(piece), turn)
        R.part[here, :] = dot_nt(R.qkv[here, :], R.waf[:, : 3 * heads_w]).astype(LOW)
        das(piece).trade(hi)

    def first_back(piece):
        scatter, here = das(piece), rows_of(piece)
        scatter.arrive()

        def back(row):
            da = scatter.total(pl.ds(row, some_rows))
            grad, unit = norm_back(R.x0[here(row), :], R.gains[0:1, :], da)
            R.dx0[here(row), :] = (R.dmid[here(row), :] + grad).astype(LOW)
            R.norms[0:1, :] += jnp.sum(da * unit, 0, keepdims=True)
            R.norms[1:2, :] += jnp.sum(da, 0, keepdims=True)

        by_rows(back)

    def out_grads():
        def make(cols):
            R.gwo[cols, :] = dot_tn(R.dmid_all[:, cols], R.o[...]).astype(LOW)

        grads(make, (wo,))

    def queue_up():
        up.trade_all()
        pass_due(1)

    turns(
        attend_back,
        [
            *later_pieces(mg),
            (count - 3, queue_up),
            (count - 2, lambda: pass_due(1)),
            *early_ends(first_back),
            (count - 1, lambda: pass_due(max(1, dp.far - 3))),
        ],
    )

    def out_grads(cols):
        R.gwo[cols, :] = dot_tn(R.dmid_all[:, cols], R.o[...]).astype(LOW)

    def attend_grads(cols):
        R.waf[cols, : 3 * heads_w] = dot_tn(R.a[:, cols], R.qkv[...]).astype(LOW)

    grads(out_grads, (wo,))
    grads(attend_grads, (first_w,))
    first_back(seqs - 1)

    grad_mixed = sum(
        dot_nt(R.dx0[:, index * quarter : (index + 1) * quarter], R.winf[index].astype(LOW))
        for index in range(ways)
    )
    sig = R.sig[...]
    grad_unit = grad_mixed * lax.rsqrt(1.0 + sig * sig)
    rows = R.rows[...].astype(F32)
    inverse = lax.rsqrt(jnp.mean(rows * rows, -1, keepdims=True) + EPS_NORM)
    unit = rows * inverse
    grad_rows = inverse * (grad_unit - unit * jnp.mean(grad_unit * unit, -1, keepdims=True))
    for step in range(1, size):
        give(step).wait_send()
    R.give[...] = dot_tn(R.pick[...], grad_rows.astype(LOW)).astype(LOW)
    mine_inc = block_rows(R.inc, spots)(mp.me)
    back, back_wait = far_copies(
        dp,
        lambda dest, source: (block_rows(R.give, cap)(dest), block_rows(mine_inc, cap)(source)),
        R.back_send,
        R.back_recv,
    )
    for step in range(1, size):
        back(step).start()
    mine_inc[mine, :] = R.give[mine, :]

    small_mp = Scatter(
        mp, of_index(R.gm), of_index(R.gm_first), of_index(R.gm_second), R.gm_send, R.gm_recv
    )
    for index in range(ways):
        cols = slice(index * quarter, (index + 1) * quarter)
        R.gm[index, :width, :] = dot_tn(R.mixed[...], R.dx0[:, cols]).astype(LOW)
        R.gm[index, width:, :] = jnp.concatenate(
            [R.norms[0:4, cols], jnp.zeros((12, quarter), F32)], 0
        ).astype(LOW)
    small_mp.trade_all()
    pass_due(2)
    for step in range(1, far):
        small_mp.pass_on(step)

    for gather in cg:
        gather.drain()

    def feed_out(turn, piece, hi, base):
        here = pl.ds(base, 2 * seq_len)
        R.c[here, :] = dot_nt(R.hb[here, :], R.wcf[...]).astype(LOW)
        out(piece).trade(hi)
        hand_on(out(piece), turn)

    turns(feed_out, [])

    back_wait()
    rows_in = Gather(mp, block_rows(R.inc, spots), R.in_send, R.in_recv)
    rows_in.start()
    pass_due(len(due))
    for step in range(1, dp.far):
        wo.pass_on(step)

    small_mp.arrive()
    summed = small_mp.total(slice(None))
    for index in range(size):
        piece = summed[index * rin : (index + 1) * rin, :]
        if rin_up > rin:
            piece = jnp.concatenate([piece, jnp.zeros((rin_up - rin, quarter), F32)], 0)
        R.gw[index, :rin_up, :] = piece.astype(LOW)
        R.gw[index, rin_up:, :] = summed[width:, :].astype(LOW)
    small.trade_all()
    rows_in.relays()
    first_w.pass_on(1)

    def finish_out(piece):
        scatter, here = out(piece), rows_of(piece)
        scatter.arrive()

        def finish(row):
            R.out[here(row), :] = (
                R.out[here(row), :] + scatter.total(pl.ds(row, some_rows))
            ) * scale_at(here(row))

        by_rows(finish)

    for piece in range(seqs):
        finish_out(piece)

    named.close()
    rows_in.close()
    groups = ways * size
    some, lanes_at = min(groups, 32), min(ways * spots, 512)
    for begin in range(0, ways * spots, lanes_at):
        spot = lax.broadcasted_iota(jnp.int32, (128, lanes_at), 1).astype(F32) + float(begin)
        block_no = jnp.floor((spot + 0.5) * (1.0 / cap))
        place = lax.broadcasted_iota(jnp.int32, (128, lanes_at), 0).astype(F32)
        spread_out = jnp.where(spot - block_no * cap == place, 1.0, 0.0).astype(LOW)
        named_row = jnp.zeros((1, lanes_at), F32)
        for first in range(0, groups, some):
            wanted = jnp.concatenate(
                [
                    R.idx[index // size, index % size][0:1, :] + 1.0
                    for index in range(first, first + some)
                ],
                0,
            )
            high = jnp.floor(wanted * (1.0 / 256.0))
            rest = wanted - 256.0 * high
            laid = dot(high.astype(LOW), spread_out) * 256.0 + dot(rest.astype(LOW), spread_out) - 1.0
            own_block = block_no[0:1, :] == float(first) + lax.broadcasted_iota(
                jnp.int32, (some, lanes_at), 0
            ).astype(F32)
            named_row = named_row + jnp.sum(jnp.where(own_block, laid, 0.0), 0, keepdims=True)
        R.named[:, begin : begin + lanes_at] = jnp.broadcast_to(
            named_row.astype(jnp.int32) - dp.me * table_rows, (8, lanes_at)
        )

    once = jnp.where(mp.me == 0, 1.0, 0.0)
    lanes = lax.broadcasted_iota(jnp.int32, (1, 128), 1)
    R.sums[...] = jnp.zeros_like(R.sums)

    def put(place, squares, factor=None):
        for row, values in enumerate(squares):
            total = jnp.sum(jnp.sum(values, 0, keepdims=True), 1, keepdims=True)
            if factor is not None:
                total = total * factor
            R.sums[row : row + 1, :] += jnp.where(lanes == place, total, 0.0)

    def squares_of(weight, gradient, first, second):
        direction = direction_of(weight, gradient, first, second)[2]
        return weight * weight, direction * direction

    def folded(values):
        rows, columns = values.shape
        return jnp.sum(values.reshape(rows // 8, 8, columns), 0)

    def add_up(weight, gradient, first, second):
        squares = squares_of(weight[...], gradient[...], first[...], second[...])
        return [folded(values) for values in squares]

    for tile in range(min(2, tiles)):
        for one in tile_of(tile):
            one.start()
    zero = jnp.zeros((8, width), F32)

    rest = [
        functools.partial(scatter.pass_on, step)
        for scatter in (first_w, small)
        for step in range(1, dp.far)
    ][1:]
    tail_hooks = [
        (min(tiles - 1, 1 + place * (tiles - 1) // len(rest)), action)
        for place, action in enumerate(rest)
    ]

    def add_tile(tile, carry):
        side = lax.rem(tile, 2)
        for place, action in tail_hooks:
            pl.when(tile == place)(action)
        for one in tile_of(tile):
            one.wait()
        hit = (
            lax.broadcasted_iota(jnp.int32, (tile_rows, ways * spots), 0) + tile * tile_rows
            == R.named[0:1, :]
        )
        R.gtile[...] = dot(jnp.where(hit, 1.0, 0.0).astype(LOW), R.inc[...])
        more = add_up(R.tw.at[side], R.gtile, R.tm.at[side], R.tv.at[side])

        @pl.when(tile + 2 < tiles)
        def _():
            for one in tile_of(tile + 2):
                one.start()

        return carry[0] + more[0], carry[1] + more[1]

    put(0, lax.fori_loop(0, tiles, add_tile, (zero, zero)), once)

    for name in names_of_moments:
        moment(name).wait()
    up.arrive()

    R.red_up[...] = up.total(slice(None))
    put(10, add_up(R.w_up, R.red_up, R.up_m_here, R.up_v_here))
    down.arrive()

    R.red_dn[...] = down.total(slice(None)).T
    put(11, add_up(R.w_down, R.red_dn, R.down_m_here, R.down_v_here))
    wo.arrive()
    R.red_out[...] = wo.total(slice(None)).T
    put(9, add_up(R.w_out, R.red_out, R.out_m_here, R.out_v_here))

    small.arrive()
    R.wsum[mp.me] = small.total(slice(None)).astype(LOW)
    weights_in = Gather(mp, of_index(R.wsum), R.ws_send, R.ws_recv)
    weights_in.start()
    first_w.arrive()

    value = first_w.total(slice(None))
    for part in range(3):
        R.red_qkv[part] = value[:, part * heads_w : (part + 1) * heads_w]
    weights_in.relays()
    for part in range(3):
        put(
            6 + part,
            add_up(
                R.w_qkv.at[part], R.red_qkv.at[part], R.qkv_m_here.at[part], R.qkv_v_here.at[part]
            ),
        )
    weights_in.close()
    total = jnp.concatenate([R.wsum[index].astype(F32) for index in range(ways)], 1)
    R.red_in[...] = total[:rin, :]
    put(1, add_up(R.w_in, R.red_in, R.w_in_m_here, R.w_in_v_here), once)
    if strip % 128 == 0:
        R.lnsum[...] = total[rin_up : rin_up + 8, :]
        R.red_ln[...] = R.lnsum[0:4, pl.ds(pl.multiple_of(dp.me * strip, strip), strip)]
    else:
        chosen = lax.broadcasted_iota(jnp.int32, (model, strip), 0) == dp.me * strip + (
            lax.broadcasted_iota(jnp.int32, (model, strip), 1)
        )
        R.red_ln[...] = dot(
            total[rin_up : rin_up + 8, :].astype(LOW), jnp.where(chosen, 1.0, 0.0).astype(LOW)
        )[0:4]
    squares = squares_of(R.ln_params[...], R.red_ln[...], R.ln_m_here[...], R.ln_v_here[...])
    for row in range(4):
        put(2 + row, [values[row : row + 1, :] for values in squares], once)

    R.near[dp.me] = R.sums[...]
    near, near_wait = far_copies(
        dp, lambda dest, source: (R.near.at[dp.me], R.near.at[source]), R.near_send, R.near_recv
    )
    for step in range(1, size):
        near(step).start()
    near_wait()
    R.wide[mp.me] = jnp.sum(R.near[...], 0)
    far_off, far_off_wait = far_copies(
        mp, lambda dest, source: (R.wide.at[mp.me], R.wide.at[source]), R.wide_send, R.wide_recv
    )
    for step in range(1, ways):
        far_off(step).start()
    far_off_wait()
    R.totals[...] = jnp.sum(R.wide[...], 0)

    for thing in (win, win_all, ln, *wc, *dxg, *ag, *mg, up, down, first_w, wo, small_mp, small):
        thing.drain()
    for thing in (named, rows_in, weights_in):
        thing.drain()
    for piece in range(seqs):
        out(piece).drain()
        das(piece).drain()
    for step in range(1, size):
        ask(step).wait_send()
        back(step).wait_send()
        near(step).wait_send()
    for step in range(1, ways):
        far_off(step).wait_send()


def run_layer(cap, ids, levels, noise, cot, weights, moments):
    table, w_in, ln_params, w_qkv, w_out, w_up, w_down = weights
    dp, mp = lax.axis_size("dp"), lax.axis_size("mp")
    seqs, seq_len = ids.shape
    tokens, width = noise.shape
    model = cot.shape[1]
    rin = w_in.shape[0]
    heads_w = w_qkv.shape[2]
    strip, hidden = w_up.shape
    group = tokens * mp
    spots = dp * cap
    wide = round_up(rin, 16) + 16
    far, far_dp = mp // 2, dp // 2
    quarter = model // mp
    in_kind = LOW if rin % 16 == 0 else F32
    tile_rows = max(rows for rows in range(8, 513, 8) if table.shape[0] % rows == 0)
    stacked = (heads_w // HD) * seq_len
    vmem = pl.BlockSpec(memory_space=pltpu.VMEM)
    outside = pl.BlockSpec(memory_space=pl.ANY)
    inputs = dict(
        ids=(ids, vmem),
        levels=(levels, pl.BlockSpec(memory_space=pltpu.SMEM)),
        noise=(noise, vmem),
        cot=(cot, vmem),
        table=(table, outside),
        w_in=(w_in, vmem),
        ln_params=(ln_params, vmem),
        w_qkv=(w_qkv, vmem),
        w_out=(w_out, vmem),
        w_up=(w_up, vmem),
        w_down=(w_down, vmem),
    )
    kept = {}
    for name, (first, second) in zip(("table", "w_in", "ln", "qkv", "out", "up", "down"), moments):
        inputs[name + "_m"] = (first, outside)
        inputs[name + "_v"] = (second, outside)
        if name != "table":
            kept[name + "_m_here"] = kept[name + "_v_here"] = (first.shape, F32)
    outputs = dict(
        out=((tokens, model), F32),
        red_up=((strip, hidden), F32),
        red_dn=((hidden, strip), F32),
        red_qkv=((3, strip, heads_w), F32),
        red_out=((heads_w, strip), F32),
        red_in=((rin, model), F32),
        red_ln=((4, strip), F32),
        inc=((mp * spots, width), LOW),
        named=((8, mp * spots), jnp.int32),
        totals=((8, 128), F32),
    )
    buffers = dict(
        tab=((2, round_up(table.shape[0] // 8, 128), width), F32),
        ask=((dp, 8, 128), F32),
        idx=((mp, dp, 8, 128), F32),
        loc=((spots, 128), jnp.int32),
        give=((spots, width), LOW),
        got=((spots, width), LOW),
        gtile=((tile_rows, width), F32),
        tw=((2, tile_rows, width), F32),
        tm=((2, tile_rows, width), F32),
        tv=((2, tile_rows, width), F32),
        sums=((8, 128), F32),
        near=((dp, 8, 128), F32),
        wide=((mp, 8, 128), F32),
        scores=((2, stacked, seq_len), F32),
        dprobs=((2, stacked, seq_len), F32),
        probs=((2, stacked, seq_len), LOW),
        dscores=((2, stacked, seq_len), LOW),
        upper=((2, stacked, heads_w), LOW),
        gwo=((model, heads_w), LOW),
        wo_first=((far_dp * strip, heads_w), LOW),
        wo_second=((far_dp * strip, heads_w), LOW),
        lnf=((dp, 8, ln_params.shape[1]), F32),
        gains=((8, model), F32),
        lnsum=((8, model), F32),
        sig=((tokens, 1), F32),
        pick=((tokens, spots), LOW),
        rows=((tokens, width), LOW),
        mixed=((tokens, width), LOW),
        x0=((tokens, model), F32),
        a=((group, model), LOW),
        c=((group, model), LOW),
        dx=((group, model), LOW),
        dmid=((tokens, model), F32),
        dmid_all=((group, model), LOW),
        winf=((mp, rin * dp, quarter), in_kind),
        waf=((model, 4 * heads_w), LOW),
        wbf=((model, hidden), LOW),
        wcf=((model, hidden), LOW),
        qkv=((group, 3 * heads_w), LOW),
        o=((group, heads_w), LOW),
        low=((2 * seq_len, heads_w), LOW),
        part=((group, model), LOW),
        first=((far * tokens, model), LOW),
        fold=((far * tokens, model), LOW),
        second=((far * tokens, model), LOW),
        fold_far=((far * tokens, model), LOW),
        h=((2 * seq_len, hidden), F32),
        hb=((group, hidden), LOW),
        dhb=((group, hidden), LOW),
        slope=((group, hidden), LOW),
        gdn=((model, hidden), LOW),
        dx0=((tokens, model), LOW),
        norms=((8, model), F32),
        gm=((mp, width + 16, quarter), LOW),
        gm_first=((far, width + 16, quarter), LOW),
        gm_second=((far, width + 16, quarter), LOW),
        gw=((dp, wide, quarter), LOW),
        gw_first=((far_dp, wide, quarter), LOW),
        gw_second=((far_dp, wide, quarter), LOW),
        up_first=((far_dp * strip, hidden), LOW),
        up_second=((far_dp * strip, hidden), LOW),
        dn_first=((far_dp * strip, hidden), LOW),
        dn_second=((far_dp * strip, hidden), LOW),
        wa_first=((far_dp * strip, 3 * heads_w), LOW),
        wa_second=((far_dp * strip, 3 * heads_w), LOW),
        wsum=((mp, wide, quarter), LOW),
        up_extra=((strip, hidden), LOW),
        dn_extra=((strip, hidden), LOW),
        wa_extra=((strip, 3 * heads_w), LOW),
        wo_extra=((strip, heads_w), LOW),
        gw_extra=((wide, quarter), LOW),
        **kept,
    )
    sems = dict(tab_sem=2, tile_sem=6, moment_sem=12)
    for name in (
        *("win", "ln", "wa", "wx", "wb", "wy", "wc", "wz", "ask", "give", "back"),
        *("up", "dn", "ga", "wo", "gw", "near"),
    ):
        sems[name + "_send"] = sems[name + "_recv"] = dp + 1
    for name in ("wim", "id", "in", "ws", "gm", "wide"):
        sems[name + "_send"] = sems[name + "_recv"] = mp
    for name in ("dx", "a", "c", "e", "as", "os", "cs", "ds"):
        sems[name + "_send"] = sems[name + "_recv"] = seqs * mp
    names = [*inputs, *outputs, *buffers, *sems]
    made = pl.pallas_call(
        functools.partial(layer_kernel, cap, names),
        out_shape=[jax.ShapeDtypeStruct(shape, kind) for shape, kind in outputs.values()],
        in_specs=[spec for _, spec in inputs.values()],
        out_specs=[vmem] * len(outputs),
        scratch_shapes=[
            *[pltpu.VMEM(shape, kind) for shape, kind in buffers.values()],
            *[pltpu.SemaphoreType.DMA((number,)) for number in sems.values()],
        ],
        compiler_params=pltpu.CompilerParams(
            vmem_limit_bytes=VMEM_BYTES, collective_id=1, has_side_effects=True
        ),
        name="layer",
    )(*[value for value, _ in inputs.values()])
    return dict(zip(outputs, made))


def direction_of(weight, gradient, first, second):
    first_new = BETA_ONE * first + (1.0 - BETA_ONE) * gradient
    second_new = BETA_TWO * second + (1.0 - BETA_TWO) * gradient * gradient
    second_hat = second_new * (1.0 / (1.0 - BETA_TWO**STEP))
    inverse = lax.rsqrt(second_hat)
    root = second_hat * inverse + EPS_ADAM
    inverse = inverse * (2.0 - root * inverse)
    inverse = inverse * (2.0 - root * inverse)
    direction = first_new * (1.0 / (1.0 - BETA_ONE**STEP)) * inverse + DECAY * weight
    return first_new, second_new, direction


def update_kernel(part, names, *refs):
    R = types.SimpleNamespace(**dict(zip(names, refs)))
    turn = pl.program_id(0)
    R.out_rows[...] = R.made[...]
    norms = jnp.sqrt(R.totals[...])
    R.norms[...] = norms[0:2, 0:12]
    factors = norms[0:1, :] / (norms[1:2, :] + EPS_ADAM) * RATE

    def piece(name, here, gradient, place, rows=slice(None)):
        weight = getattr(R, name)[here]
        first_new, second_new, direction = direction_of(
            weight, gradient, getattr(R, name + "_m")[here], getattr(R, name + "_v")[here]
        )
        if isinstance(place, int):
            factor = factors[0:1, place : place + 1]
        else:
            factor = jnp.concatenate([factors[0:1, one : one + 1] for one in place], 0)
        getattr(R, name + "_m_new")[here] = first_new
        getattr(R, name + "_v_new")[here] = second_new
        getattr(R, name + "_new")[here] = weight - factor * direction

    def update(name, gradient, place, lead=(), here=slice(None)):
        piece(name, (*lead, here, slice(None)), gradient, place)

    tile = R.table.shape[0]
    spots = R.named.shape[1]

    def table_part(row):
        hit = (
            lax.broadcasted_iota(jnp.int32, (part, spots), 0) + (turn * tile + row)
            == R.named[0:1, :]
        )
        gradient = dot(jnp.where(hit, 1.0, 0.0).astype(LOW), R.inc[...])
        update("table", gradient, 0, (), pl.ds(row, part))

    strips(tile, part, table_part)
    for group in range(3):
        update("qkv", R.red_qkv[group], 6 + group, (group,))
    update("up", R.red_up[...], 10)
    update("down", R.red_dn[...], 11)

    @pl.when(turn == 0)
    def _():
        update("out", R.red_out[...], 9)
        update("w_in", R.red_in[...], 1)
        piece("ln", (slice(None), slice(None)), R.red_ln[...], (2, 3, 4, 5))


def turns_of(rows, parts):
    return [
        turns
        for turns in (5, 4, 2, 1)
        if rows % (8 * turns) == 0 and all(size % (8 * turns) == 0 for size in parts)
    ][0]


def run_update(weights, moments, grads):
    names = ("table", "w_in", "ln", "qkv", "out", "up", "down")
    by_name = dict(zip(names, weights))
    rows, width = by_name["table"].shape
    strip, hidden = by_name["up"].shape
    heads_w = by_name["qkv"].shape[2]
    turns = turns_of(rows, (strip, hidden))
    tile = rows // turns
    part = max(size for size in range(8, 257, 8) if tile % size == 0)
    fixed = lambda array: pl.BlockSpec(array.shape, lambda turn: (0,) * array.ndim)
    specs = dict(
        table=pl.BlockSpec((tile, width), lambda turn: (turn, 0)),
        w_in=fixed(by_name["w_in"]),
        ln=fixed(by_name["ln"]),
        qkv=pl.BlockSpec((3, strip // turns, heads_w), lambda turn: (0, turn, 0)),
        out=fixed(by_name["out"]),
        up=pl.BlockSpec((strip // turns, hidden), lambda turn: (turn, 0)),
        down=pl.BlockSpec((hidden // turns, strip), lambda turn: (turn, 0)),
    )
    inputs = {}
    for name, weight, (first, second) in zip(names, weights, moments):
        inputs[name] = (weight, specs[name])
        inputs[name + "_m"] = (first, specs[name])
        inputs[name + "_v"] = (second, specs[name])
    for name, like in (
        ("red_up", "up"),
        ("red_dn", "down"),
        ("red_qkv", "qkv"),
        ("red_out", "out"),
        ("red_in", "w_in"),
        ("red_ln", "ln"),
    ):
        inputs[name] = (grads[name], specs[like])
    for name in ("inc", "named", "totals"):
        inputs[name] = (grads[name], fixed(grads[name]))
    tokens, model = grads["out"].shape
    rows_spec = pl.BlockSpec((tokens // turns, model), lambda turn: (turn, 0))
    inputs["made"] = (grads["out"], rows_spec)
    outputs = {"out_rows": (grads["out"].shape, rows_spec)}
    for name, weight in by_name.items():
        for kind in ("_new", "_m_new", "_v_new"):
            outputs[name + kind] = (weight.shape, specs[name])
    outputs["norms"] = ((2, 12), pl.BlockSpec((2, 12), lambda turn: (0, 0)))
    results = pl.pallas_call(
        functools.partial(update_kernel, part, [*inputs, *outputs]),
        grid=(turns,),
        out_shape=[jax.ShapeDtypeStruct(shape, F32) for shape, _ in outputs.values()],
        in_specs=[spec for _, spec in inputs.values()],
        out_specs=[spec for _, spec in outputs.values()],
        compiler_params=pltpu.CompilerParams(vmem_limit_bytes=VMEM_BYTES),
        name="update",
    )(*[value for value, _ in inputs.values()])
    return list(results)


def per_device(
    token_ids,
    levels,
    noise,
    cotangent,
    table,
    table_m,
    table_v,
    w_in,
    w_in_m,
    w_in_v,
    ln_params,
    ln_m,
    ln_v,
    w_qkv,
    qkv_m,
    qkv_v,
    w_out,
    out_m,
    out_v,
    w_up,
    up_m,
    up_v,
    w_down,
    down_m,
    down_v,
):
    dp_count = lax.axis_size("dp")
    seq_count, seq_len = token_ids.shape
    tokens = seq_count * seq_len
    model = cotangent.shape[2]
    cap = round_up(max(2, (3 * tokens + 2 * dp_count - 1) // (2 * dp_count)), 16)
    weights = (table, w_in, ln_params, w_qkv, w_out, w_up, w_down)
    moments = (
        (table_m, table_v),
        (w_in_m, w_in_v),
        (ln_m, ln_v),
        (qkv_m, qkv_v),
        (out_m, out_v),
        (up_m, up_v),
        (down_m, down_v),
    )
    grads = run_layer(
        cap,
        token_ids,
        levels,
        noise.reshape(tokens, -1),
        cotangent.reshape(tokens, model),
        weights,
        moments,
    )
    out, *results = run_update(weights, moments, grads)
    return (out.reshape(seq_count, seq_len, model), *results)


def solution(mesh):
    return jax.shard_map(
        per_device,
        mesh=mesh,
        in_specs=(
            P(("dp", "mp"), None),
            P(("dp", "mp")),
            P(("dp", "mp"), None, None),
            P(("dp", "mp"), None, None),
            P("dp", None),
            P("dp", None),
            P("dp", None),
            P("dp", None),
            P("dp", None),
            P("dp", None),
            P(None, "dp"),
            P(None, "dp"),
            P(None, "dp"),
            P(None, "dp", "mp"),
            P(None, "dp", "mp"),
            P(None, "dp", "mp"),
            P("mp", "dp"),
            P("mp", "dp"),
            P("mp", "dp"),
            P("dp", "mp"),
            P("dp", "mp"),
            P("dp", "mp"),
            P("mp", "dp"),
            P("mp", "dp"),
            P("mp", "dp"),
        ),
        out_specs=(
            P(("dp", "mp"), None, None),
            P("dp", None),
            P("dp", None),
            P("dp", None),
            P("dp", None),
            P("dp", None),
            P("dp", None),
            P(None, "dp"),
            P(None, "dp"),
            P(None, "dp"),
            P(None, "dp", "mp"),
            P(None, "dp", "mp"),
            P(None, "dp", "mp"),
            P("mp", "dp"),
            P("mp", "dp"),
            P("mp", "dp"),
            P("dp", "mp"),
            P("dp", "mp"),
            P("dp", "mp"),
            P("mp", "dp"),
            P("mp", "dp"),
            P("mp", "dp"),
            P(),
        ),
        check_vma=False,
    )
```

```python
import functools
import types

import jax
import jax.numpy as jnp
from jax import lax
from jax.experimental import pallas as pl
from jax.experimental.pallas import tpu as pltpu
from jax.sharding import PartitionSpec as P

HD = 64
LEVELS = 64
STEP = 10


EPS_NORM = 1e-06
EPS_LAYER = 1e-05
EPS_ADAM = 1e-06
BETA_ONE = 0.9
BETA_TWO = 0.999
DECAY = 0.01
RATE = 0.5
SIGMA_TOP = 10.0

F32 = jnp.float32
LOW = jnp.bfloat16
VMEM_BYTES = 63 * 1024 * 1024


def sigma_of(levels):
    frac = levels.astype(jnp.float32) / (LEVELS - 1)
    return jnp.exp(frac * jnp.log(SIGMA_TOP))


def lamb_moments(weight, gradient, first, second):
    first_new = BETA_ONE * first + (1.0 - BETA_ONE) * gradient
    second_new = BETA_TWO * second + (1.0 - BETA_TWO) * gradient * gradient
    first_hat = first_new / (1.0 - BETA_ONE**STEP)
    second_hat = second_new / (1.0 - BETA_TWO**STEP)
    direction = first_hat / (jnp.sqrt(second_hat) + EPS_ADAM) + DECAY * weight
    return (first_new, second_new, direction)


def trust_factors(ratio):
    return (
        ratio[0],
        ratio[1],
        ratio[2:6][:, None],
        ratio[6:9][:, None, None],
        ratio[9],
        ratio[10],
        ratio[11],
    )


def round_up(value, step):
    return -(-value // step) * step


def dot(left, right):
    return jnp.dot(left, right, preferred_element_type=F32)


def dot_nt(left, right):
    return lax.dot_general(left, right, (((1,), (1,)), ((), ())), preferred_element_type=F32)


def dot_tn(left, right):
    return lax.dot_general(left, right, (((0,), (0,)), ((), ())), preferred_element_type=F32)


def strips(total, step, body, unroll=1):
    step = min(step, total)

    def one(turn, carry):
        body(pl.multiple_of(turn * step, step))
        return carry

    lax.fori_loop(0, total // step, one, 0, unroll=unroll)


class Line:
    def __init__(self, axis):
        self.axis = axis
        self.size = lax.axis_size(axis)
        self.far = self.size // 2
        self.me = lax.axis_index(axis)
        self.hi = lax.div(self.me, 2)
        self.lo = lax.rem(self.me, 2)
        self.partner = self.hi * 2 + (1 - self.lo)

    def at(self, step):
        return lax.rem(self.hi + step + self.far, self.far)

    def push(self, index, src, dst, send, recv):
        return pltpu.make_async_remote_copy(
            src_ref=src,
            dst_ref=dst,
            send_sem=send,
            recv_sem=recv,
            device_id={self.axis: index},
            device_id_type=pl.DeviceIdType.MESH,
        )

    def signal(self, sem, index):
        pl.semaphore_signal(
            sem, inc=1, device_id={self.axis: index}, device_id_type=pl.DeviceIdType.MESH
        )


def meet(pair_lines, all_lines=()):
    sem = pltpu.get_barrier_semaphore()
    count = 0
    for line in pair_lines:
        for step in range(1, line.far):
            line.signal(sem, line.at(step) * 2 + line.lo)
            count += 1
        line.signal(sem, line.partner)
        count += 1
    for line in all_lines:
        for step in range(1, line.size):
            line.signal(sem, lax.rem(line.me + step, line.size))
            count += 1
    pl.semaphore_wait(sem, count)


class Gather:
    def __init__(self, line, at, send, recv, base=0, ends=False):
        self.line, self.at, self.send, self.recv, self.base = line, at, send, recv, base
        self.ends = ends and line.far == 4

    def source(self, step):
        line = self.line
        if not self.ends:
            return line.at(-step)
        order = ((1, 2, 3), (0, 3, 2), (3, 0, 1), (2, 1, 0))
        hi = order[3][step - 1]
        for place in (2, 1, 0):
            hi = jnp.where(line.hi == place, order[place][step - 1], hi)
        return hi

    def far_sends(self, act):
        line = self.line
        for step in range(1, line.far):
            one = self.copy(line.me, step - 1, line.at(step) * 2 + line.lo)
            if self.ends and step != 2:
                pl.when(line.hi != (3 if step == 1 else 0))(functools.partial(act, one))
            else:
                act(one)

    def to_end(self, act):
        line = self.line
        dest = jnp.where(line.hi == 1, 0, 3)
        one = self.copy((3 - dest) * 2 + line.lo, 2 * line.far - 1, dest * 2 + line.lo)
        pl.when((line.hi == 1) | (line.hi == 2))(functools.partial(act, one))

    def copy(self, index, slot, dest):
        block = self.at(index)
        return self.line.push(
            dest, block, block, self.send.at[self.base + slot], self.recv.at[self.base + index]
        )

    def start_far(self):
        self.far_sends(lambda one: one.start())

    def start_near(self):
        self.copy(self.line.me, self.line.far - 1, self.line.partner).start()

    def start(self):
        self.start_far()
        self.start_near()

    def relay(self, step):
        line = self.line
        handed = self.copy(self.source(step) * 2 + line.lo, line.far - 1 + step, line.partner)
        handed.wait_recv()
        if self.ends and step == 2:
            self.to_end(lambda one: one.start())
        handed.start()

    def relays(self):
        for step in range(1, self.line.far):
            self.relay(step)

    def close(self):
        line = self.line
        for step in range(line.far):
            self.copy(line.at(-step) * 2 + (1 - line.lo), 0, line.partner).wait_recv()

    def drain(self):
        self.far_sends(lambda one: one.wait_send())
        if self.ends:
            self.to_end(lambda one: one.wait_send())
        for slot in range(self.line.far - 1, 2 * self.line.far - 1):
            self.copy(self.line.me, slot, self.line.partner).wait_send()


class Scatter:
    def __init__(self, line, part, first, second, send, recv, base=0, extra=None):
        self.line, self.part, self.first, self.second = line, part, first, second
        self.send, self.recv, self.base = send, recv, base
        self.extra = extra if line.far == 4 else None

    def clear(self):
        line = self.line
        if self.extra is not None:

            @pl.when((line.hi == 0) | (line.hi == 3))
            def _():
                slot = self.second(3 - line.hi)
                slot[...] = jnp.zeros(slot.shape, LOW)

    def order(self, step):
        line = self.line
        if self.extra is None:
            return line.at(step)
        table = ((3, 2, 1), (2, 0, 3), (1, 3, 0), (0, 1, 2))
        hi = table[3][step - 1]
        for place in (2, 1, 0):
            hi = jnp.where(line.hi == place, table[place][step - 1], hi)
        return hi

    def traded(self, hi):
        line = self.line
        return line.push(
            line.partner,
            self.part(hi * 2 + (1 - line.lo)),
            self.first(hi),
            self.send.at[self.base + hi],
            self.recv.at[self.base + hi],
        )

    def passed(self, step):
        line = self.line
        hi = self.order(step)
        return line.push(
            hi * 2 + line.lo,
            self.part(hi * 2 + line.lo),
            self.second(line.hi),
            self.send.at[self.base + line.far + step - 1],
            self.recv.at[self.base + line.far + line.hi],
        )

    def to_next(self):
        line = self.line
        return line.push(
            jnp.where(line.hi < 2, 1, 2) * 2 + line.lo,
            self.part((3 - jnp.where(line.hi < 2, 0, 3)) * 2 + line.lo),
            self.extra,
            self.send.at[self.base + line.far],
            self.recv.at[self.base + 2 * line.far],
        )

    def turn_of(self, turn):
        line = self.line
        if self.extra is None:
            return lax.rem(line.hi + turn + 1, line.far)
        hi = line.hi
        for step in range(1, line.far):
            hi = jnp.where(turn == step - 1, self.order(step), hi)
        return hi

    def is_end(self):
        return (self.line.hi == 0) | (self.line.hi == 3)

    def trade(self, hi):
        self.traded(hi).start()

    def trade_all(self):
        for step in range(1, self.line.far + 1):
            self.trade(self.order(step) if step < self.line.far else self.line.hi)

    def pass_on(self, step):
        line = self.line
        hi = self.order(step)
        self.traded(hi).wait_recv()
        mine, other = self.part(hi * 2 + line.lo), self.first(hi)
        if self.extra is None or step == 2:
            mine[...] = (mine[...].astype(F32) + other[...].astype(F32)).astype(LOW)
            self.passed(step).start()
        elif step == 1:
            mine[...] = (mine[...].astype(F32) + other[...].astype(F32)).astype(LOW)

            @pl.when(self.is_end())
            def _():
                self.to_next().start()

            @pl.when(jnp.logical_not(self.is_end()))
            def _():
                self.passed(step).start()
        else:

            @pl.when(self.is_end())
            def _():
                mine[...] = (mine[...].astype(F32) + other[...].astype(F32)).astype(LOW)

            @pl.when(jnp.logical_not(self.is_end()))
            def _():
                line.push(
                    line.partner,
                    self.extra,
                    self.extra,
                    self.send.at[self.base],
                    self.recv.at[self.base + 2 * line.far],
                ).wait_recv()
                mine[...] = (
                    mine[...].astype(F32) + other[...].astype(F32) + self.extra[...].astype(F32)
                ).astype(LOW)

            self.passed(step).start()

    def arrive(self):
        line = self.line
        self.traded(line.hi).wait_recv()
        for step in range(1, line.far):
            hi = line.at(-step)
            one = line.push(
                line.partner,
                self.second(hi),
                self.second(hi),
                self.send.at[self.base],
                self.recv.at[self.base + line.far + hi],
            )
            if self.extra is None:
                one.wait_recv()
            else:
                pl.when(jnp.logical_not(self.is_end()) | (hi + line.hi != 3))(one.wait_recv)

    def total(self, here):
        line = self.line
        value = self.part(line.me)[here, :].astype(F32) + self.first(line.hi)[here, :].astype(F32)
        for step in range(1, line.far):
            value = value + self.second(line.at(-step))[here, :].astype(F32)
        return value

    def drain(self):
        line = self.line
        for step in range(line.far):
            self.traded(line.at(step)).wait_send()
        for step in range(1, line.far):
            if self.extra is not None and step == 1:
                pl.when(self.is_end())(lambda: self.to_next().wait_send())
                pl.when(jnp.logical_not(self.is_end()))(lambda: self.passed(1).wait_send())
            else:
                self.passed(step).wait_send()


def block_rows(ref, rows, first=0):
    return lambda index: ref.at[pl.ds(pl.multiple_of((index + first) * rows, rows), rows)]


def part_rows(ref, rows, first, count):
    return lambda index: ref.at[pl.ds(pl.multiple_of(index * rows + first, count), count)]


def of_index(ref):
    return lambda index: ref.at[index]


def norm_rows(values):
    center = values - jnp.mean(values, -1, keepdims=True)
    spread = jnp.mean(center * center, -1, keepdims=True)
    inverse = lax.rsqrt(spread + EPS_LAYER)
    return center * inverse, inverse


def norm_back(values, gain, grad):
    unit, inverse = norm_rows(values)
    inner = grad * gain
    shared = jnp.mean(inner, -1, keepdims=True)
    along = jnp.mean(inner * unit, -1, keepdims=True)
    return inverse * (inner - shared - unit * along), unit


def head_masks(width):
    lane = lax.broadcasted_iota(jnp.int32, (1, width), 1)
    return [
        jnp.where((lane >= head * HD) & (lane < (head + 1) * HD), 1.0, 0.0)
        for head in range(width // HD)
    ]


def spread_heads(values, masks):
    return jnp.concatenate([values * mask.astype(LOW) for mask in masks], 0)


def join_heads(values, masks, rows):
    total = values[0:rows] * masks[0]
    for head in range(1, len(masks)):
        total = total + values[head * rows : (head + 1) * rows] * masks[head]
    return total


TAIL = (
    0.2256758632450557,
    0.22566952478278277,
    0.2078438574180613,
    0.16853390514724884,
    0.14146086231844687,
    -0.005667717379728321,
    0.16915486959066833,
    -0.18294364197603524,
    0.05027260226320005,
)


def normal_tail(size, bell):
    base = 1.0 + (0.4 * 0.5**0.5) * size
    t = pl.reciprocal(base, approx=True)
    t = t * (2.0 - base * t)
    t = t * (2.0 - base * t)
    value = jnp.full_like(t, 0.5 * TAIL[-1])
    for factor in TAIL[-2::-1]:
        value = value * t + 0.5 * factor
    return value * t * bell


def far_copies(line, make, sends, recvs):
    def copy(step):
        dest = lax.rem(line.me + step, line.size)
        src, dst = make(dest, line.me)
        return line.push(dest, src, dst, sends.at[step], recvs.at[line.me])

    def wait():
        for step in range(1, line.size):
            source = lax.rem(line.me + line.size - step, line.size)
            _, dst = make(source, source)
            line.push(line.partner, dst, dst, sends.at[0], recvs.at[source]).wait_recv()

    return copy, wait


def layer_kernel(cap, names, *refs):
    R = types.SimpleNamespace(**dict(zip(names, refs)))
    dp, mp = Line("dp"), Line("mp")
    size, ways = dp.size, mp.size
    seqs, seq_len = R.ids.shape
    tokens, width = R.noise.shape
    model = R.cot.shape[1]
    heads_w = R.o.shape[1]
    hidden = R.wbf.shape[1]
    table_rows = R.table.shape[0]
    rin = R.w_in.shape[0]
    rin_up = round_up(rin, 16)
    quarter = model // ways
    strip = R.w_up.shape[0]
    spots = size * cap
    far = mp.far
    count = seqs * far
    own_strip = pl.ds(pl.multiple_of(dp.me * strip, strip), strip)
    mine = pl.ds(pl.multiple_of(dp.me * cap, cap), cap)

    some_rows = seq_len // 2

    def rows_of(piece):
        return lambda row: pl.ds(pl.multiple_of(piece * seq_len + row, some_rows), some_rows)

    def own_rows(piece):
        first = pl.multiple_of((piece * ways + mp.me) * seq_len, seq_len)
        return lambda row: pl.ds(pl.multiple_of(first + row, some_rows), some_rows)

    def by_rows(body):
        for row in range(0, seq_len, some_rows):
            body(row)

    def halves(ref, send, recv):
        return [
            Gather(mp, block_rows(ref, seq_len, piece * ways), send, recv, piece * ways)
            for piece in range(seqs)
        ]

    def sums(part, first, second, send, recv):
        return lambda piece: Scatter(
            mp,
            block_rows(part, seq_len, piece * ways),
            block_rows(first, seq_len, piece * far),
            block_rows(second, seq_len, piece * far),
            send,
            recv,
            piece * ways,
        )

    many = ways * seq_len

    def turns(body, hooks=()):
        def one(piece, carry):
            def at(point):
                for place, when, action in hooks:
                    if when == point:
                        pl.when(piece == place)(action)

            base = pl.multiple_of(piece * many, many)
            body(piece, base, pl.ds(base, many), at)
            return carry

        lax.fori_loop(0, seqs, one, 0)

    def pairs(base, body):
        def one(pair, carry):
            first = pl.multiple_of(base + pair * (2 * seq_len), 2 * seq_len)
            body([pl.ds(pl.multiple_of(first + seq * seq_len, seq_len), seq_len) for seq in range(2)])
            return carry

        lax.fori_loop(0, far, one, 0)

    def chunks(total, body):
        step = min(256, total)
        lax.fori_loop(
            0,
            total // step,
            lambda turn, carry: (body(pl.ds(pl.multiple_of(turn * step, step), step)), carry)[1],
            0,
        )

    def hand_on(scatter):
        for step in range(1, far):
            scatter.pass_on(step)

    def later_pieces(gathers, point):
        hooks = []
        for piece in range(1, seqs):
            hooks.append((piece - 1, point, gathers[piece].relays))
            hooks.append((piece, "start", gathers[piece].close))
        return hooks

    chunk = R.tab.shape[1]
    pieces = -(-table_rows // chunk)

    def fetch(piece):
        rows = min(chunk, table_rows - piece * chunk)
        return pltpu.make_async_copy(
            R.table.at[pl.ds(piece * chunk, rows)],
            R.tab.at[piece % 2, pl.ds(0, rows)],
            R.tab_sem.at[piece % 2],
        )

    for piece in range(min(2, pieces)):
        fetch(piece).start()

    names_of_moments = [
        name + kind for name in ("w_in", "ln", "qkv", "out", "up", "down") for kind in ("_m", "_v")
    ]

    def moment(name):
        return pltpu.make_async_copy(
            getattr(R, name), getattr(R, name + "_here"), R.moment_sem.at[names_of_moments.index(name)]
        )

    tile_rows = R.gtile.shape[0]
    tiles = table_rows // tile_rows

    def tile_of(tile):
        side = lax.rem(tile, 2)
        rows = pl.ds(pl.multiple_of(tile * tile_rows, tile_rows), tile_rows)
        return [
            pltpu.make_async_copy(source.at[rows], dest.at[side], R.tile_sem.at[2 * place + side])
            for place, (source, dest) in enumerate(
                ((R.table, R.tw), (R.table_m, R.tm), (R.table_v, R.tv))
            )
        ]

    eye = lax.broadcasted_iota(jnp.int32, (seq_len, seq_len), 0) == lax.broadcasted_iota(
        jnp.int32, (seq_len, seq_len), 1
    )
    id_rows = R.ids[...].astype(F32)
    ids = jnp.concatenate(
        [
            jnp.sum(jnp.where(eye, id_rows[seq : seq + 1, :], 0.0), 1, keepdims=True)
            for seq in range(seqs)
        ],
        0,
    )
    lane = lax.broadcasted_iota(jnp.int32, (tokens, 128), 1).astype(F32)
    low_end = lane * float(table_rows)
    owned = jnp.where((ids >= low_end) & (ids < low_end + float(table_rows)), 1.0, 0.0)
    before = jnp.where(
        lax.broadcasted_iota(jnp.int32, (tokens, tokens), 0)
        >= lax.broadcasted_iota(jnp.int32, (tokens, tokens), 1),
        1.0,
        0.0,
    )
    ranks = dot(before.astype(LOW), owned.astype(LOW))
    rank = jnp.sum(owned * ranks, 1, keepdims=True) - 1.0
    slot = jnp.sum(owned * lane, 1, keepdims=True) * cap + rank
    placed = jnp.where(lane == rank, 1.0, 0.0)
    upper = jnp.floor(ids * (1.0 / 256.0))
    lower = ids - upper * 256.0
    parts = jnp.concatenate([placed * upper, placed * lower, placed], 1).astype(LOW)
    asked = dot_tn(owned.astype(LOW), parts)
    asked = asked[:, :128] * 256.0 + asked[:, 128:256] + asked[:, 256:] - 1.0
    wide_ln = R.ln_params.shape[1]
    shares = R.ln_params[...].astype(LOW).astype(F32)
    if wide_ln < 128:
        shares = jnp.concatenate([shares, jnp.zeros((4, 128 - wide_ln), F32)], 1)
    for index in range(size):
        R.ask[index] = jnp.concatenate(
            [asked[index : index + 1, :], shares, jnp.zeros((3, 128), F32)], 0
        )
    R.idx[mp.me, dp.me] = R.ask[dp.me]

    def spread(part, first, second, extra, send, recv):
        blocks = [block_rows(ref, strip) for ref in (part, first, second)]
        return Scatter(dp, *blocks, send, recv, 0, extra)

    up = spread(R.wbf, R.up_first, R.up_second, R.up_extra, R.up_send, R.up_recv)
    down = spread(R.gdn, R.dn_first, R.dn_second, R.dn_extra, R.dn_send, R.dn_recv)
    first_w = spread(
        R.waf.at[:, : 3 * heads_w], R.wa_first, R.wa_second, R.wa_extra, R.ga_send, R.ga_recv
    )
    wo = spread(R.gwo, R.wo_first, R.wo_second, R.wo_extra, R.wo_send, R.wo_recv)
    small = Scatter(
        dp,
        *[of_index(ref) for ref in (R.gw, R.gw_first, R.gw_second)],
        R.gw_send,
        R.gw_recv,
        0,
        R.gw_extra,
    )
    for scatter in (up, down, first_w, wo, small):
        scatter.clear()

    meet([mp], [dp])
    ask, ask_wait = far_copies(
        dp,
        lambda dest, source: (R.ask.at[dest], R.idx.at[mp.me, source]),
        R.ask_send,
        R.ask_recv,
    )
    for step in range(1, size):
        ask(step).start()

    mine_in = R.winf.at[mp.me]
    win = Gather(dp, block_rows(mine_in, rin), R.win_send, R.win_recv, 0, True)
    win_all = Gather(mp, of_index(R.winf), R.wim_send, R.wim_recv)
    wa = Gather(dp, block_rows(R.waf, strip), R.wa_send, R.wa_recv, 0, True)
    wb = Gather(dp, block_rows(R.wbf, strip), R.wb_send, R.wb_recv, 0, True)
    wc = Gather(dp, block_rows(R.wcf, strip), R.wc_send, R.wc_recv, 0, True)
    dxg = Gather(
        mp,
        lambda index: R.dx.at[:, pl.ds(pl.multiple_of(index * seq_len, seq_len), seq_len)],
        R.dx_send,
        R.dx_recv,
    )
    ag = halves(R.a, R.a_send, R.a_recv)
    cg = halves(R.c, R.c_send, R.c_recv)
    mg = halves(R.dmid_all, R.e_send, R.e_recv)

    mine_in[pl.ds(pl.multiple_of(dp.me * rin, rin), rin), :] = (
        R.w_in[:, pl.ds(pl.multiple_of(mp.me * quarter, quarter), quarter)]
        .astype(LOW)
        .astype(R.winf.dtype)
    )
    win.start()
    for part in range(3):
        R.waf[own_strip, part * heads_w : (part + 1) * heads_w] = R.w_qkv[part].astype(LOW)
    R.waf[own_strip, 3 * heads_w :] = R.w_out[...].T.astype(LOW)
    wa.start()
    for name in names_of_moments:
        moment(name).start()

    for seq in range(seqs):
        level = jnp.full((seq_len, 1), R.levels[seq], jnp.int32).astype(F32) / (LEVELS - 1)
        R.sig[seq * seq_len : (seq + 1) * seq_len, :] = jnp.exp(level * jnp.log(SIGMA_TOP))

    def scale_at(here):
        sig = R.sig[here, :]
        return sig * lax.rsqrt(1.0 + sig * sig)

    for piece in range(seqs):
        here = rows_of(piece)

        def scale_cot(row, here=here, piece=piece):
            there = pl.ds(pl.multiple_of(mp.me * seq_len + row, some_rows), some_rows)
            R.dx[piece, there, :] = (R.cot[here(row), :].astype(F32) * scale_at(here(row))).astype(LOW)

        by_rows(scale_cot)
    dxg.start()
    R.wbf[own_strip, :] = R.w_up[...].astype(LOW)
    R.wcf[own_strip, :] = R.w_down[...].T.astype(LOW)
    wb.start_near()
    R.pick[...] = jnp.where(
        lax.broadcasted_iota(jnp.int32, (tokens, spots), 1).astype(F32) == slot, 1.0, 0.0
    ).astype(LOW)
    win.relays()

    ask_wait()
    small_eye = lax.broadcasted_iota(jnp.int32, (cap, 128), 0) == lax.broadcasted_iota(
        jnp.int32, (cap, 128), 1
    )

    def locate(index, carry):
        row = R.idx[mp.me, index][0:1, :]
        column = jnp.sum(jnp.where(small_eye, row, 0.0), 1, keepdims=True)
        local = column.astype(jnp.int32) - dp.me * table_rows
        R.loc[pl.ds(pl.multiple_of(index * cap, cap), cap), :] = jnp.broadcast_to(local, (cap, 128))
        return carry

    lax.fori_loop(0, size, locate, 0, unroll=True)
    win.close()
    win_all.start()
    found = None
    for piece in range(pieces):
        fetch(piece).wait()
        rows = min(chunk, table_rows - piece * chunk)
        if rows < chunk:
            R.tab[piece % 2, rows:, :] = jnp.zeros((chunk - rows, width), F32)
        hit = (
            lax.broadcasted_iota(jnp.int32, (spots, chunk), 1) + piece * chunk == R.loc[:, 0:1]
        )
        more = dot(jnp.where(hit, 1.0, 0.0).astype(LOW), R.tab[piece % 2].astype(LOW))
        found = more if found is None else found + more
        if piece + 2 < pieces:
            fetch(piece + 2).start()
    R.give[...] = found.astype(LOW)

    give, give_wait = far_copies(
        dp,
        lambda dest, source: (block_rows(R.give, cap)(dest), block_rows(R.got, cap)(source)),
        R.give_send,
        R.give_recv,
    )
    for step in range(1, size):
        give(step).start()
    R.got[mine, :] = R.give[mine, :]
    win_all.relays()
    wa.relay(1)
    if wide_ln % 128 == 0:
        R.gains[...] = jnp.concatenate([R.idx[mp.me, index] for index in range(size)], 1)
    else:
        total = jnp.zeros((8, model), F32)
        for index in range(size):
            place = lax.broadcasted_iota(
                jnp.int32, (128, model), 1
            ) == index * wide_ln + lax.broadcasted_iota(jnp.int32, (128, model), 0)
            place = place & (lax.broadcasted_iota(jnp.int32, (128, model), 0) < wide_ln)
            total = total + dot(
                R.idx[mp.me, index].astype(LOW), jnp.where(place, 1.0, 0.0).astype(LOW)
            )
        R.gains[...] = total
    wa.relay(2)
    named = Gather(mp, of_index(R.idx), R.id_send, R.id_recv)

    give_wait()
    rows = dot(R.pick[...], R.got[...])
    R.rows[...] = rows.astype(LOW)
    sig = R.sig[...]
    unit = rows * lax.rsqrt(jnp.mean(rows * rows, -1, keepdims=True) + EPS_NORM)
    R.mixed[...] = ((unit + sig * R.noise[...].astype(F32)) * lax.rsqrt(1.0 + sig * sig)).astype(LOW)
    win_all.close()
    for index in range(ways):
        R.x0[:, index * quarter : (index + 1) * quarter] = dot(
            R.mixed[...], R.winf[index].astype(LOW)
        )

    for piece in range(seqs):
        here, there = rows_of(piece), own_rows(piece)

        def first_norm(row, here=here, there=there):
            normed, _ = norm_rows(R.x0[here(row), :])
            R.a[there(row), :] = (normed * R.gains[1:2, :] + R.gains[2:3, :]).astype(LOW)

        by_rows(first_norm)
        ag[piece].start()
    for step in range(3, dp.far):
        wa.relay(step)
    wb.start_far()
    wc.start_near()
    dxg.relays()
    named.start()
    win.drain()
    for step in range(1, size):
        ask(step).wait_send()
    ag[0].relays()
    for gather in (wa, ag[0]):
        gather.close()

    att = sums(R.part, R.fold, R.fold_far, R.as_send, R.as_recv)
    dcs = sums(R.part, R.fold, R.fold_far, R.cs_send, R.cs_recv)
    das = sums(R.part, R.fold, R.fold_far, R.ds_send, R.ds_recv)
    out = sums(R.c, R.first, R.second, R.os_send, R.os_recv)
    masks = head_masks(heads_w)

    all_rows = (heads_w // HD) * seq_len
    scale = HD ** (-0.5)

    def softmax(seq, row):
        scores = R.scores[seq, row : row + 64, :]
        raised = jnp.exp((scores - jnp.max(scores, -1, keepdims=True)) * scale)
        return raised * (1.0 / jnp.sum(raised, -1, keepdims=True))

    def attend(piece, base, here, at):
        at("start")
        for part in range(3):
            cols = slice(part * heads_w, (part + 1) * heads_w)
            R.qkv[here, cols] = dot(R.a[here, :], R.waf[:, cols]).astype(LOW)
        at("mid")

        def one(rows_at):
            for seq, rows in enumerate(rows_at):
                queries = spread_heads(R.qkv[rows, :heads_w], masks)
                R.scores[seq] = dot_nt(queries, R.qkv[rows, heads_w : 2 * heads_w])
            for seq, rows in enumerate(rows_at):
                for row in range(0, all_rows, 64):
                    R.probs[seq, row : row + 64, :] = softmax(seq, row).astype(LOW)
                seen = dot(R.probs[seq], R.qkv[rows, 2 * heads_w : 3 * heads_w])
                R.o[rows, :] = join_heads(seen, masks, seq_len).astype(LOW)

        pairs(base, one)
        at("late")

        def project(cols):
            R.part[here, cols] = dot_nt(R.o[here, :], R.waf[cols, 3 * heads_w :]).astype(LOW)

        chunks(model, project)
        att(piece).trade_all()

    def second_norm(piece):
        scatter, here, there = att(piece), rows_of(piece), own_rows(piece)
        scatter.arrive()

        def norm(row):
            x1 = R.x0[here(row), :] + scatter.total(pl.ds(row, some_rows))
            R.out[here(row), :] = x1
            normed, _ = norm_rows(x1)
            R.c[there(row), :] = (normed * R.gains[3:4, :] + R.gains[4:5, :]).astype(LOW)

        by_rows(norm)
        cg[piece].start()

    def before_late():
        wb.relay(1)
        wb.relay(2)
        wc.start_far()

    turns(
        attend,
        [
            *later_pieces(ag, "mid"),
            *[(piece + 1, "mid", functools.partial(hand_on, att(piece))) for piece in range(seqs - 1)],
            (seqs - 1, "late", before_late),
        ],
    )
    hand_on(att(seqs - 1))
    for step in range(3, dp.far):
        wb.relay(step)
    for piece in range(seqs):
        second_norm(piece)
        if piece == 0:
            for gather in (wa, *ag, dxg):
                gather.drain()
    cg[0].relays()
    wb.close()
    named.relays()
    cg[0].close()
    for piece in range(seqs):
        att(piece).drain()

    def activate(piece, base, here, at):
        at("start")

        def some(cols):
            R.h[...] = dot(R.c[here, :], R.wbf[:, cols])

            def gelu(row):
                there = pl.ds(pl.multiple_of(base + row, 64), 64)
                h = R.h[pl.ds(row, 64), :]
                bell = jnp.exp(-0.5 * h * h)
                tail = normal_tail(jnp.abs(h), bell)
                gate = jnp.where(h >= 0.0, 1.0 - tail, tail)
                slope = gate + h * (bell * 0.3989422804014327)
                R.hb[there, cols] = (h * gate).astype(LOW)
                R.slope[there, cols] = slope.astype(LOW)

            strips(many, 64, gelu, 2)

        chunks(hidden, some)
        at("end")

    def relay_wc():
        wc.relays()

    turns(activate, [*later_pieces(cg, "end"), (0, "end", relay_wc)])

    due = [(scatter, step) for scatter in (down, up) for step in range(1, dp.far)]

    def pass_due(number):
        for _ in range(min(number, len(due))):
            scatter, step = due.pop(0)
            scatter.pass_on(step)

    block = 2 * strip if (2 * strip) % 128 == 0 else min(256, model)

    def grads(make, trades):
        if block == 2 * strip:

            def turn_of(turn, carry):
                hi = up.turn_of(turn)
                make(pl.ds(pl.multiple_of(hi * block, block), block))
                for scatter in trades:
                    scatter.trade(hi)
                return carry

            lax.fori_loop(0, dp.far, turn_of, 0)
        else:
            strips(model, block, lambda col: make(pl.ds(col, block)))
            for scatter in trades:
                scatter.trade_all()

    def down_grads(cols):
        every = R.dx[:, :, cols]
        R.gdn[cols, :] = dot_tn(every.reshape(seqs * many, block), R.hb[...]).astype(LOW)

    def up_grads(cols):
        R.wbf[cols, :] = dot_tn(R.c[:, cols], R.dhb[...]).astype(LOW)

    dxg.close()
    grads(down_grads, ())
    wc.close()
    down.trade_all()
    for gather in (wb, *cg):
        gather.drain()

    def feed_back(piece, base, here, at):
        at("start")

        def some(cols):
            bent = dot(R.dx[piece], R.wcf[:, cols]) * R.slope[here, cols].astype(F32)
            R.dhb[here, cols] = bent.astype(LOW)

        chunks(hidden, some)
        at("mid")

        def project(cols):
            R.part[here, cols] = dot_nt(R.dhb[here, :], R.wbf[cols, :]).astype(LOW)

        chunks(model, project)
        dcs(piece).trade_all()

    R.norms[...] = jnp.zeros_like(R.norms)

    def second_back(piece):
        scatter, here, there = dcs(piece), rows_of(piece), own_rows(piece)
        scatter.arrive()

        def back(row):
            dc = scatter.total(pl.ds(row, some_rows))
            grad, unit = norm_back(R.out[here(row), :], R.gains[3:4, :], dc)
            grad = grad + R.cot[here(row), :].astype(F32) * scale_at(here(row))
            R.dmid[here(row), :] = grad
            R.dmid_all[there(row), :] = grad.astype(LOW)
            R.norms[2:3, :] += jnp.sum(dc * unit, 0, keepdims=True)
            R.norms[3:4, :] += jnp.sum(dc, 0, keepdims=True)

        by_rows(back)
        mg[piece].start()

    turns(
        feed_back,
        [(piece + 1, "mid", functools.partial(hand_on, dcs(piece))) for piece in range(seqs - 1)],
    )
    hand_on(dcs(seqs - 1))
    second_back(0)
    grads(up_grads, ())
    for piece in range(1, seqs):
        second_back(piece)
    pass_due(1)
    mg[0].relays()
    mg[0].close()
    for piece in range(seqs):
        dcs(piece).drain()

    def attend_back(piece, base, here, at):
        at("start")
        R.low[...] = dot(R.dmid_all[here, :], R.waf[:, 3 * heads_w :]).astype(LOW)
        at("mid")

        def one(rows_at):
            for seq, rows in enumerate(rows_at):
                queries = spread_heads(R.qkv[rows, :heads_w], masks)
                R.scores[seq] = dot_nt(queries, R.qkv[rows, heads_w : 2 * heads_w])
                upper_rows = pl.ds(pl.multiple_of(rows.start - base, seq_len), seq_len)
                R.upper[seq] = spread_heads(R.low[upper_rows, :], masks)
                R.dprobs[seq] = dot_nt(R.upper[seq], R.qkv[rows, 2 * heads_w : 3 * heads_w])
            for seq, rows in enumerate(rows_at):
                for row in range(0, all_rows, 64):
                    probs = softmax(seq, row)
                    grad_probs = R.dprobs[seq, row : row + 64, :]
                    inner = jnp.sum(probs * grad_probs, -1, keepdims=True)
                    R.probs[seq, row : row + 64, :] = probs.astype(LOW)
                    R.dscores[seq, row : row + 64, :] = (probs * (grad_probs - inner)).astype(LOW)
                keys = R.qkv[rows, heads_w : 2 * heads_w]
                queries = spread_heads(R.qkv[rows, :heads_w], masks)
                R.qkv[rows, 2 * heads_w : 3 * heads_w] = dot_tn(R.probs[seq], R.upper[seq]).astype(LOW)
                R.qkv[rows, heads_w : 2 * heads_w] = (dot_tn(R.dscores[seq], queries) * scale).astype(
                    LOW
                )
                R.qkv[rows, :heads_w] = (
                    join_heads(dot(R.dscores[seq], keys), masks, seq_len) * scale
                ).astype(LOW)

        pairs(base, one)
        at("late")

        def project(cols):
            R.part[here, cols] = dot_nt(R.qkv[here, :], R.waf[cols, : 3 * heads_w]).astype(LOW)

        chunks(model, project)
        das(piece).trade_all()

    def first_back(piece):
        scatter, here = das(piece), rows_of(piece)
        scatter.arrive()

        def back(row):
            da = scatter.total(pl.ds(row, some_rows))
            grad, unit = norm_back(R.x0[here(row), :], R.gains[1:2, :], da)
            R.dx0[here(row), :] = (R.dmid[here(row), :] + grad).astype(LOW)
            R.norms[0:1, :] += jnp.sum(da * unit, 0, keepdims=True)
            R.norms[1:2, :] += jnp.sum(da, 0, keepdims=True)

        by_rows(back)

    def out_grads():
        def make(cols):
            R.gwo[cols, :] = dot_tn(R.dmid_all[:, cols], R.o[...]).astype(LOW)

        grads(make, (wo,))

    def queue_up():
        up.trade_all()
        pass_due(1)

    def queue_up():
        up.trade_all()
        pass_due(1)

    turns(
        attend_back,
        [
            *later_pieces(mg, "mid"),
            (0, "late", queue_up),
            *[(piece + 1, "mid", functools.partial(hand_on, das(piece))) for piece in range(seqs - 1)],
            (seqs - 1, "late", lambda: pass_due(max(1, dp.far - 3))),
        ],
    )
    hand_on(das(seqs - 1))
    def out_grads(cols):
        R.gwo[cols, :] = dot_tn(R.dmid_all[:, cols], R.o[...]).astype(LOW)

    def attend_grads(cols):
        R.waf[cols, : 3 * heads_w] = dot_tn(R.a[:, cols], R.qkv[...]).astype(LOW)

    grads(out_grads, (wo,))
    first_back(0)
    grads(attend_grads, (first_w,))
    for piece in range(1, seqs):
        first_back(piece)

    grad_mixed = sum(
        dot_nt(R.dx0[:, index * quarter : (index + 1) * quarter], R.winf[index].astype(LOW))
        for index in range(ways)
    )
    sig = R.sig[...]
    grad_unit = grad_mixed * lax.rsqrt(1.0 + sig * sig)
    rows = R.rows[...].astype(F32)
    inverse = lax.rsqrt(jnp.mean(rows * rows, -1, keepdims=True) + EPS_NORM)
    unit = rows * inverse
    grad_rows = inverse * (grad_unit - unit * jnp.mean(grad_unit * unit, -1, keepdims=True))
    for step in range(1, size):
        give(step).wait_send()
    R.give[...] = dot_tn(R.pick[...], grad_rows.astype(LOW)).astype(LOW)
    mine_inc = block_rows(R.inc, spots)(mp.me)
    back, back_wait = far_copies(
        dp,
        lambda dest, source: (block_rows(R.give, cap)(dest), block_rows(mine_inc, cap)(source)),
        R.back_send,
        R.back_recv,
    )
    for step in range(1, size):
        back(step).start()
    mine_inc[mine, :] = R.give[mine, :]

    small_mp = Scatter(
        mp, of_index(R.gm), of_index(R.gm_first), of_index(R.gm_second), R.gm_send, R.gm_recv
    )
    for index in range(ways):
        cols = slice(index * quarter, (index + 1) * quarter)
        R.gm[index, :width, :] = dot_tn(R.mixed[...], R.dx0[:, cols]).astype(LOW)
        R.gm[index, width:, :] = jnp.concatenate(
            [R.norms[0:4, cols], jnp.zeros((12, quarter), F32)], 0
        ).astype(LOW)
    small_mp.trade_all()
    pass_due(2)
    for step in range(1, far):
        small_mp.pass_on(step)

    def feed_out(piece, base, here, at):
        def project(cols):
            R.c[here, cols] = dot_nt(R.hb[here, :], R.wcf[cols, :]).astype(LOW)

        chunks(model, project)
        out(piece).trade_all()

    turns(feed_out)

    back_wait()
    rows_in = Gather(mp, block_rows(R.inc, spots), R.in_send, R.in_recv)
    rows_in.start()
    pass_due(len(due))
    for step in range(1, dp.far):
        wo.pass_on(step)
    for piece in range(seqs):
        hand_on(out(piece))

    small_mp.arrive()
    summed = small_mp.total(slice(None))
    for index in range(size):
        piece = summed[index * rin : (index + 1) * rin, :]
        if rin_up > rin:
            piece = jnp.concatenate([piece, jnp.zeros((rin_up - rin, quarter), F32)], 0)
        R.gw[index, :rin_up, :] = piece.astype(LOW)
        R.gw[index, rin_up:, :] = summed[width:, :].astype(LOW)
    small.trade_all()
    rows_in.relays()
    first_w.pass_on(1)

    def finish_out(piece):
        scatter, here = out(piece), rows_of(piece)
        scatter.arrive()

        def finish(row):
            R.out[here(row), :] = (
                R.out[here(row), :] + scatter.total(pl.ds(row, some_rows))
            ) * scale_at(here(row))

        by_rows(finish)

    for piece in range(seqs):
        finish_out(piece)

    named.close()
    rows_in.close()
    groups = ways * size
    some, lanes_at = min(groups, 32), min(ways * spots, 512)
    for begin in range(0, ways * spots, lanes_at):
        spot = lax.broadcasted_iota(jnp.int32, (128, lanes_at), 1).astype(F32) + float(begin)
        block_no = jnp.floor((spot + 0.5) * (1.0 / cap))
        place = lax.broadcasted_iota(jnp.int32, (128, lanes_at), 0).astype(F32)
        spread_out = jnp.where(spot - block_no * cap == place, 1.0, 0.0).astype(LOW)
        named_row = jnp.zeros((1, lanes_at), F32)
        for first in range(0, groups, some):
            wanted = jnp.concatenate(
                [
                    R.idx[index // size, index % size][0:1, :] + 1.0
                    for index in range(first, first + some)
                ],
                0,
            )
            high = jnp.floor(wanted * (1.0 / 256.0))
            rest = wanted - 256.0 * high
            laid = dot(high.astype(LOW), spread_out) * 256.0 + dot(rest.astype(LOW), spread_out) - 1.0
            own_block = block_no[0:1, :] == float(first) + lax.broadcasted_iota(
                jnp.int32, (some, lanes_at), 0
            ).astype(F32)
            named_row = named_row + jnp.sum(jnp.where(own_block, laid, 0.0), 0, keepdims=True)
        R.named[:, begin : begin + lanes_at] = jnp.broadcast_to(
            named_row.astype(jnp.int32) - dp.me * table_rows, (8, lanes_at)
        )

    once = jnp.where(mp.me == 0, 1.0, 0.0)
    lanes = lax.broadcasted_iota(jnp.int32, (1, 128), 1)
    R.sums[...] = jnp.zeros_like(R.sums)

    def put(place, squares, factor=None):
        for row, values in enumerate(squares):
            total = jnp.sum(jnp.sum(values, 0, keepdims=True), 1, keepdims=True)
            if factor is not None:
                total = total * factor
            R.sums[row : row + 1, :] += jnp.where(lanes == place, total, 0.0)

    def squares_of(weight, gradient, first, second):
        direction = direction_of(weight, gradient, first, second)[2]
        return weight * weight, direction * direction

    def folded(values):
        rows, columns = values.shape
        return jnp.sum(values.reshape(rows // 8, 8, columns), 0)

    def add_up(weight, gradient, first, second):
        squares = squares_of(weight[...], gradient[...], first[...], second[...])
        return [folded(values) for values in squares]

    for tile in range(min(2, tiles)):
        for one in tile_of(tile):
            one.start()
    zero = jnp.zeros((8, width), F32)

    rest = [
        functools.partial(scatter.pass_on, step)
        for scatter in (first_w, small)
        for step in range(1, dp.far)
    ][1:]
    tail_hooks = [
        (min(tiles - 1, 1 + place * (tiles - 1) // len(rest)), action)
        for place, action in enumerate(rest)
    ]

    def add_tile(tile, carry):
        side = lax.rem(tile, 2)
        for place, action in tail_hooks:
            pl.when(tile == place)(action)
        for one in tile_of(tile):
            one.wait()
        hit = (
            lax.broadcasted_iota(jnp.int32, (tile_rows, ways * spots), 0) + tile * tile_rows
            == R.named[0:1, :]
        )
        R.gtile[...] = dot(jnp.where(hit, 1.0, 0.0).astype(LOW), R.inc[...])
        more = add_up(R.tw.at[side], R.gtile, R.tm.at[side], R.tv.at[side])

        @pl.when(tile + 2 < tiles)
        def _():
            for one in tile_of(tile + 2):
                one.start()

        return carry[0] + more[0], carry[1] + more[1]

    put(0, lax.fori_loop(0, tiles, add_tile, (zero, zero)), once)

    for thing in (win_all, wc, *mg, up, down, wo, small_mp, named):
        thing.drain()
    for piece in range(seqs):
        out(piece).drain()
        das(piece).drain()
    for step in range(1, size):
        back(step).wait_send()

    for name in names_of_moments:
        moment(name).wait()
    up.arrive()

    R.red_up[...] = up.total(slice(None))
    put(10, add_up(R.w_up, R.red_up, R.up_m_here, R.up_v_here))
    down.arrive()

    R.red_dn[...] = down.total(slice(None)).T
    put(11, add_up(R.w_down, R.red_dn, R.down_m_here, R.down_v_here))
    wo.arrive()
    R.red_out[...] = wo.total(slice(None)).T
    put(9, add_up(R.w_out, R.red_out, R.out_m_here, R.out_v_here))

    small.arrive()
    R.wsum[mp.me] = small.total(slice(None)).astype(LOW)
    weights_in = Gather(mp, of_index(R.wsum), R.ws_send, R.ws_recv)
    weights_in.start()
    first_w.arrive()

    value = first_w.total(slice(None))
    for part in range(3):
        R.red_qkv[part] = value[:, part * heads_w : (part + 1) * heads_w]
    weights_in.relays()
    for part in range(3):
        put(
            6 + part,
            add_up(
                R.w_qkv.at[part], R.red_qkv.at[part], R.qkv_m_here.at[part], R.qkv_v_here.at[part]
            ),
        )
    weights_in.close()
    total = jnp.concatenate([R.wsum[index].astype(F32) for index in range(ways)], 1)
    R.red_in[...] = total[:rin, :]
    put(1, add_up(R.w_in, R.red_in, R.w_in_m_here, R.w_in_v_here), once)
    if strip % 128 == 0:
        R.lnsum[...] = total[rin_up : rin_up + 8, :]
        R.red_ln[...] = R.lnsum[0:4, pl.ds(pl.multiple_of(dp.me * strip, strip), strip)]
    else:
        chosen = lax.broadcasted_iota(jnp.int32, (model, strip), 0) == dp.me * strip + (
            lax.broadcasted_iota(jnp.int32, (model, strip), 1)
        )
        R.red_ln[...] = dot(
            total[rin_up : rin_up + 8, :].astype(LOW), jnp.where(chosen, 1.0, 0.0).astype(LOW)
        )[0:4]
    squares = squares_of(R.ln_params[...], R.red_ln[...], R.ln_m_here[...], R.ln_v_here[...])
    for row in range(4):
        put(2 + row, [values[row : row + 1, :] for values in squares], once)

    R.near[dp.me] = R.sums[...]
    near, near_wait = far_copies(
        dp, lambda dest, source: (R.near.at[dp.me], R.near.at[source]), R.near_send, R.near_recv
    )
    for step in range(1, size):
        near(step).start()
    near_wait()
    R.wide[mp.me] = jnp.sum(R.near[...], 0)
    far_off, far_off_wait = far_copies(
        mp, lambda dest, source: (R.wide.at[mp.me], R.wide.at[source]), R.wide_send, R.wide_recv
    )
    for step in range(1, ways):
        far_off(step).start()
    far_off_wait()
    R.totals[...] = jnp.sum(R.wide[...], 0)

    for thing in (first_w, small, rows_in, weights_in):
        thing.drain()
    for step in range(1, size):
        near(step).wait_send()
    for step in range(1, ways):
        far_off(step).wait_send()


def run_layer(cap, ids, levels, noise, cot, weights, moments):
    table, w_in, ln_params, w_qkv, w_out, w_up, w_down = weights
    dp, mp = lax.axis_size("dp"), lax.axis_size("mp")
    seqs, seq_len = ids.shape
    tokens, width = noise.shape
    model = cot.shape[1]
    rin = w_in.shape[0]
    heads_w = w_qkv.shape[2]
    strip, hidden = w_up.shape
    group = tokens * mp
    spots = dp * cap
    wide = round_up(rin, 16) + 16
    far, far_dp = mp // 2, dp // 2
    quarter = model // mp
    in_kind = LOW if rin % 16 == 0 else F32
    tile_rows = max(rows for rows in range(8, 513, 8) if table.shape[0] % rows == 0)
    stacked = (heads_w // HD) * seq_len
    vmem = pl.BlockSpec(memory_space=pltpu.VMEM)
    outside = pl.BlockSpec(memory_space=pl.ANY)
    inputs = dict(
        ids=(ids, vmem),
        levels=(levels, pl.BlockSpec(memory_space=pltpu.SMEM)),
        noise=(noise, vmem),
        cot=(cot, vmem),
        table=(table, outside),
        w_in=(w_in, vmem),
        ln_params=(ln_params, vmem),
        w_qkv=(w_qkv, vmem),
        w_out=(w_out, vmem),
        w_up=(w_up, vmem),
        w_down=(w_down, vmem),
    )
    kept = {}
    for name, (first, second) in zip(("table", "w_in", "ln", "qkv", "out", "up", "down"), moments):
        inputs[name + "_m"] = (first, outside)
        inputs[name + "_v"] = (second, outside)
        if name != "table":
            kept[name + "_m_here"] = kept[name + "_v_here"] = (first.shape, F32)
    outputs = dict(
        out=((tokens, model), F32),
        red_up=((strip, hidden), F32),
        red_dn=((hidden, strip), F32),
        red_qkv=((3, strip, heads_w), F32),
        red_out=((heads_w, strip), F32),
        red_in=((rin, model), F32),
        red_ln=((4, strip), F32),
        inc=((mp * spots, width), LOW),
        named=((8, mp * spots), jnp.int32),
        totals=((8, 128), F32),
    )
    buffers = dict(
        tab=((2, round_up(table.shape[0] // 8, 128), width), F32),
        ask=((dp, 8, 128), F32),
        idx=((mp, dp, 8, 128), F32),
        loc=((spots, 128), jnp.int32),
        give=((spots, width), LOW),
        got=((spots, width), LOW),
        gtile=((tile_rows, width), F32),
        tw=((2, tile_rows, width), F32),
        tm=((2, tile_rows, width), F32),
        tv=((2, tile_rows, width), F32),
        sums=((8, 128), F32),
        near=((dp, 8, 128), F32),
        wide=((mp, 8, 128), F32),
        scores=((2, stacked, seq_len), F32),
        dprobs=((2, stacked, seq_len), F32),
        probs=((2, stacked, seq_len), LOW),
        dscores=((2, stacked, seq_len), LOW),
        upper=((2, stacked, heads_w), LOW),
        gwo=((model, heads_w), LOW),
        wo_first=((far_dp * strip, heads_w), LOW),
        wo_second=((far_dp * strip, heads_w), LOW),
        gains=((8, model), F32),
        lnsum=((8, model), F32),
        sig=((tokens, 1), F32),
        pick=((tokens, spots), LOW),
        rows=((tokens, width), LOW),
        mixed=((tokens, width), LOW),
        x0=((tokens, model), F32),
        a=((group, model), LOW),
        c=((group, model), LOW),
        dx=((seqs, group // seqs, model), LOW),
        dmid=((tokens, model), F32),
        dmid_all=((group, model), LOW),
        winf=((mp, rin * dp, quarter), in_kind),
        waf=((model, 4 * heads_w), LOW),
        wbf=((model, hidden), LOW),
        wcf=((model, hidden), LOW),
        qkv=((group, 3 * heads_w), LOW),
        o=((group, heads_w), LOW),
        low=((group // seqs, heads_w), LOW),
        part=((group, model), LOW),
        first=((far * tokens, model), LOW),
        fold=((far * tokens, model), LOW),
        second=((far * tokens, model), LOW),
        fold_far=((far * tokens, model), LOW),
        h=((group // seqs, min(256, hidden)), F32),
        hb=((group, hidden), LOW),
        dhb=((group, hidden), LOW),
        slope=((group, hidden), LOW),
        gdn=((model, hidden), LOW),
        dx0=((tokens, model), LOW),
        norms=((8, model), F32),
        gm=((mp, width + 16, quarter), LOW),
        gm_first=((far, width + 16, quarter), LOW),
        gm_second=((far, width + 16, quarter), LOW),
        gw=((dp, wide, quarter), LOW),
        gw_first=((far_dp, wide, quarter), LOW),
        gw_second=((far_dp, wide, quarter), LOW),
        up_first=((far_dp * strip, hidden), LOW),
        up_second=((far_dp * strip, hidden), LOW),
        dn_first=((far_dp * strip, hidden), LOW),
        dn_second=((far_dp * strip, hidden), LOW),
        wa_first=((far_dp * strip, 3 * heads_w), LOW),
        wa_second=((far_dp * strip, 3 * heads_w), LOW),
        wsum=((mp, wide, quarter), LOW),
        up_extra=((strip, hidden), LOW),
        dn_extra=((strip, hidden), LOW),
        wa_extra=((strip, 3 * heads_w), LOW),
        wo_extra=((strip, heads_w), LOW),
        gw_extra=((wide, quarter), LOW),
        **kept,
    )
    sems = dict(tab_sem=2, tile_sem=6, moment_sem=12)
    for name in (
        *("win", "wa", "wb", "wc", "ask", "give", "back"),
        *("up", "dn", "ga", "wo", "gw", "near"),
    ):
        sems[name + "_send"] = sems[name + "_recv"] = dp + 1
    for name in ("wim", "id", "in", "ws", "gm", "wide"):
        sems[name + "_send"] = sems[name + "_recv"] = mp
    for name in ("dx", "a", "c", "e", "as", "os", "cs", "ds"):
        sems[name + "_send"] = sems[name + "_recv"] = seqs * mp
    names = [*inputs, *outputs, *buffers, *sems]
    made = pl.pallas_call(
        functools.partial(layer_kernel, cap, names),
        out_shape=[jax.ShapeDtypeStruct(shape, kind) for shape, kind in outputs.values()],
        in_specs=[spec for _, spec in inputs.values()],
        out_specs=[vmem] * len(outputs),
        scratch_shapes=[
            *[pltpu.VMEM(shape, kind) for shape, kind in buffers.values()],
            *[pltpu.SemaphoreType.DMA((number,)) for number in sems.values()],
        ],
        compiler_params=pltpu.CompilerParams(
            vmem_limit_bytes=VMEM_BYTES, collective_id=1, has_side_effects=True
        ),
        name="layer",
    )(*[value for value, _ in inputs.values()])
    return dict(zip(outputs, made))


def direction_of(weight, gradient, first, second):
    first_new = BETA_ONE * first + (1.0 - BETA_ONE) * gradient
    second_new = BETA_TWO * second + (1.0 - BETA_TWO) * gradient * gradient
    second_hat = second_new * (1.0 / (1.0 - BETA_TWO**STEP))
    inverse = lax.rsqrt(second_hat)
    root = second_hat * inverse + EPS_ADAM
    inverse = inverse * (2.0 - root * inverse)
    inverse = inverse * (2.0 - root * inverse)
    direction = first_new * (1.0 / (1.0 - BETA_ONE**STEP)) * inverse + DECAY * weight
    return first_new, second_new, direction


def update_kernel(part, names, *refs):
    R = types.SimpleNamespace(**dict(zip(names, refs)))
    turn = pl.program_id(0)
    R.out_rows[...] = R.made[...]
    norms = jnp.sqrt(R.totals[...])
    R.norms[...] = norms[0:2, 0:12]
    factors = norms[0:1, :] / (norms[1:2, :] + EPS_ADAM) * RATE

    def piece(name, here, gradient, place, rows=slice(None)):
        weight = getattr(R, name)[here]
        first_new, second_new, direction = direction_of(
            weight, gradient, getattr(R, name + "_m")[here], getattr(R, name + "_v")[here]
        )
        if isinstance(place, int):
            factor = factors[0:1, place : place + 1]
        else:
            factor = jnp.concatenate([factors[0:1, one : one + 1] for one in place], 0)
        getattr(R, name + "_m_new")[here] = first_new
        getattr(R, name + "_v_new")[here] = second_new
        getattr(R, name + "_new")[here] = weight - factor * direction

    def update(name, gradient, place, lead=(), here=slice(None)):
        piece(name, (*lead, here, slice(None)), gradient, place)

    tile = R.table.shape[0]
    spots = R.named.shape[1]

    def table_part(row):
        hit = (
            lax.broadcasted_iota(jnp.int32, (part, spots), 0) + (turn * tile + row)
            == R.named[0:1, :]
        )
        gradient = dot(jnp.where(hit, 1.0, 0.0).astype(LOW), R.inc[...])
        update("table", gradient, 0, (), pl.ds(row, part))

    strips(tile, part, table_part)
    for group in range(3):
        update("qkv", R.red_qkv[group], 6 + group, (group,))
    update("up", R.red_up[...], 10)
    update("down", R.red_dn[...], 11)

    @pl.when(turn == 0)
    def _():
        update("out", R.red_out[...], 9)
        update("w_in", R.red_in[...], 1)
        piece("ln", (slice(None), slice(None)), R.red_ln[...], (2, 3, 4, 5))


def turns_of(rows, parts):
    return [
        turns
        for turns in (5, 4, 2, 1)
        if rows % (8 * turns) == 0 and all(size % (8 * turns) == 0 for size in parts)
    ][0]


def run_update(weights, moments, grads):
    names = ("table", "w_in", "ln", "qkv", "out", "up", "down")
    by_name = dict(zip(names, weights))
    rows, width = by_name["table"].shape
    strip, hidden = by_name["up"].shape
    heads_w = by_name["qkv"].shape[2]
    turns = turns_of(rows, (strip, hidden))
    tile = rows // turns
    part = max(size for size in range(8, 257, 8) if tile % size == 0)
    fixed = lambda array: pl.BlockSpec(array.shape, lambda turn: (0,) * array.ndim)
    specs = dict(
        table=pl.BlockSpec((tile, width), lambda turn: (turn, 0)),
        w_in=fixed(by_name["w_in"]),
        ln=fixed(by_name["ln"]),
        qkv=pl.BlockSpec((3, strip // turns, heads_w), lambda turn: (0, turn, 0)),
        out=fixed(by_name["out"]),
        up=pl.BlockSpec((strip // turns, hidden), lambda turn: (turn, 0)),
        down=pl.BlockSpec((hidden // turns, strip), lambda turn: (turn, 0)),
    )
    inputs = {}
    for name, weight, (first, second) in zip(names, weights, moments):
        inputs[name] = (weight, specs[name])
        inputs[name + "_m"] = (first, specs[name])
        inputs[name + "_v"] = (second, specs[name])
    for name, like in (
        ("red_up", "up"),
        ("red_dn", "down"),
        ("red_qkv", "qkv"),
        ("red_out", "out"),
        ("red_in", "w_in"),
        ("red_ln", "ln"),
    ):
        inputs[name] = (grads[name], specs[like])
    for name in ("inc", "named", "totals"):
        inputs[name] = (grads[name], fixed(grads[name]))
    tokens, model = grads["out"].shape
    rows_spec = pl.BlockSpec((tokens // turns, model), lambda turn: (turn, 0))
    inputs["made"] = (grads["out"], rows_spec)
    outputs = {"out_rows": (grads["out"].shape, rows_spec)}
    for name, weight in by_name.items():
        for kind in ("_new", "_m_new", "_v_new"):
            outputs[name + kind] = (weight.shape, specs[name])
    outputs["norms"] = ((2, 12), pl.BlockSpec((2, 12), lambda turn: (0, 0)))
    results = pl.pallas_call(
        functools.partial(update_kernel, part, [*inputs, *outputs]),
        grid=(turns,),
        out_shape=[jax.ShapeDtypeStruct(shape, F32) for shape, _ in outputs.values()],
        in_specs=[spec for _, spec in inputs.values()],
        out_specs=[spec for _, spec in outputs.values()],
        compiler_params=pltpu.CompilerParams(vmem_limit_bytes=VMEM_BYTES),
        name="update",
    )(*[value for value, _ in inputs.values()])
    return list(results)


def per_device(
    token_ids,
    levels,
    noise,
    cotangent,
    table,
    table_m,
    table_v,
    w_in,
    w_in_m,
    w_in_v,
    ln_params,
    ln_m,
    ln_v,
    w_qkv,
    qkv_m,
    qkv_v,
    w_out,
    out_m,
    out_v,
    w_up,
    up_m,
    up_v,
    w_down,
    down_m,
    down_v,
):
    dp_count = lax.axis_size("dp")
    seq_count, seq_len = token_ids.shape
    tokens = seq_count * seq_len
    model = cotangent.shape[2]
    cap = round_up(max(2, (3 * tokens + 2 * dp_count - 1) // (2 * dp_count)), 16)
    weights = (table, w_in, ln_params, w_qkv, w_out, w_up, w_down)
    moments = (
        (table_m, table_v),
        (w_in_m, w_in_v),
        (ln_m, ln_v),
        (qkv_m, qkv_v),
        (out_m, out_v),
        (up_m, up_v),
        (down_m, down_v),
    )
    grads = run_layer(
        cap,
        token_ids,
        levels,
        noise.reshape(tokens, -1),
        cotangent.reshape(tokens, model),
        weights,
        moments,
    )
    out, *results = run_update(weights, moments, grads)
    return (out.reshape(seq_count, seq_len, model), *results)


def solution(mesh):
    return jax.shard_map(
        per_device,
        mesh=mesh,
        in_specs=(
            P(("dp", "mp"), None),
            P(("dp", "mp")),
            P(("dp", "mp"), None, None),
            P(("dp", "mp"), None, None),
            P("dp", None),
            P("dp", None),
            P("dp", None),
            P("dp", None),
            P("dp", None),
            P("dp", None),
            P(None, "dp"),
            P(None, "dp"),
            P(None, "dp"),
            P(None, "dp", "mp"),
            P(None, "dp", "mp"),
            P(None, "dp", "mp"),
            P("mp", "dp"),
            P("mp", "dp"),
            P("mp", "dp"),
            P("dp", "mp"),
            P("dp", "mp"),
            P("dp", "mp"),
            P("mp", "dp"),
            P("mp", "dp"),
            P("mp", "dp"),
        ),
        out_specs=(
            P(("dp", "mp"), None, None),
            P("dp", None),
            P("dp", None),
            P("dp", None),
            P("dp", None),
            P("dp", None),
            P("dp", None),
            P(None, "dp"),
            P(None, "dp"),
            P(None, "dp"),
            P(None, "dp", "mp"),
            P(None, "dp", "mp"),
            P(None, "dp", "mp"),
            P("mp", "dp"),
            P("mp", "dp"),
            P("mp", "dp"),
            P("dp", "mp"),
            P("dp", "mp"),
            P("dp", "mp"),
            P("mp", "dp"),
            P("mp", "dp"),
            P("mp", "dp"),
            P(),
        ),
        check_vma=False,
    )
```

```python
import functools
import types

import jax
import jax.numpy as jnp
from jax import lax
from jax.experimental import pallas as pl
from jax.experimental.pallas import tpu as pltpu
from jax.sharding import PartitionSpec as P

HD = 64
LEVELS = 64
STEP = 10


EPS_NORM = 1e-06
EPS_LAYER = 1e-05
EPS_ADAM = 1e-06
BETA_ONE = 0.9
BETA_TWO = 0.999
DECAY = 0.01
RATE = 0.5
SIGMA_TOP = 10.0

F32 = jnp.float32
LOW = jnp.bfloat16
VMEM_BYTES = 63 * 1024 * 1024


def sigma_of(levels):
    frac = levels.astype(jnp.float32) / (LEVELS - 1)
    return jnp.exp(frac * jnp.log(SIGMA_TOP))


def lamb_moments(weight, gradient, first, second):
    first_new = BETA_ONE * first + (1.0 - BETA_ONE) * gradient
    second_new = BETA_TWO * second + (1.0 - BETA_TWO) * gradient * gradient
    first_hat = first_new / (1.0 - BETA_ONE**STEP)
    second_hat = second_new / (1.0 - BETA_TWO**STEP)
    direction = first_hat / (jnp.sqrt(second_hat) + EPS_ADAM) + DECAY * weight
    return (first_new, second_new, direction)


def trust_factors(ratio):
    return (
        ratio[0],
        ratio[1],
        ratio[2:6][:, None],
        ratio[6:9][:, None, None],
        ratio[9],
        ratio[10],
        ratio[11],
    )


def round_up(value, step):
    return -(-value // step) * step


def dot(left, right):
    return jnp.dot(left, right, preferred_element_type=F32)


def dot_nt(left, right):
    return lax.dot_general(left, right, (((1,), (1,)), ((), ())), preferred_element_type=F32)


def dot_tn(left, right):
    return lax.dot_general(left, right, (((0,), (0,)), ((), ())), preferred_element_type=F32)


def strips(total, step, body, unroll=1):
    step = min(step, total)

    def one(turn, carry):
        body(pl.multiple_of(turn * step, step))
        return carry

    lax.fori_loop(0, total // step, one, 0, unroll=unroll)


class Line:
    def __init__(self, axis):
        self.axis = axis
        self.size = lax.axis_size(axis)
        self.far = self.size // 2
        self.me = lax.axis_index(axis)
        self.hi = lax.div(self.me, 2)
        self.lo = lax.rem(self.me, 2)
        self.partner = self.hi * 2 + (1 - self.lo)

    def at(self, step):
        return lax.rem(self.hi + step + self.far, self.far)

    def push(self, index, src, dst, send, recv):
        return pltpu.make_async_remote_copy(
            src_ref=src,
            dst_ref=dst,
            send_sem=send,
            recv_sem=recv,
            device_id={self.axis: index},
            device_id_type=pl.DeviceIdType.MESH,
        )

    def signal(self, sem, index):
        pl.semaphore_signal(
            sem, inc=1, device_id={self.axis: index}, device_id_type=pl.DeviceIdType.MESH
        )


def meet(pair_lines, all_lines=()):
    sem = pltpu.get_barrier_semaphore()
    count = 0
    for line in pair_lines:
        for step in range(1, line.far):
            line.signal(sem, line.at(step) * 2 + line.lo)
            count += 1
        line.signal(sem, line.partner)
        count += 1
    for line in all_lines:
        for step in range(1, line.size):
            line.signal(sem, lax.rem(line.me + step, line.size))
            count += 1
    pl.semaphore_wait(sem, count)


class Gather:
    def __init__(self, line, at, send, recv, base=0, ends=False):
        self.line, self.at, self.send, self.recv, self.base = line, at, send, recv, base
        self.ends = ends and line.far == 4

    def source(self, step):
        line = self.line
        if not self.ends:
            return line.at(-step)
        order = ((1, 2, 3), (0, 3, 2), (3, 0, 1), (2, 1, 0))
        hi = order[3][step - 1]
        for place in (2, 1, 0):
            hi = jnp.where(line.hi == place, order[place][step - 1], hi)
        return hi

    def far_sends(self, act):
        line = self.line
        for step in range(1, line.far):
            one = self.copy(line.me, step - 1, line.at(step) * 2 + line.lo)
            if self.ends and step != 2:
                pl.when(line.hi != (3 if step == 1 else 0))(functools.partial(act, one))
            else:
                act(one)

    def to_end(self, act):
        line = self.line
        dest = jnp.where(line.hi == 1, 0, 3)
        one = self.copy((3 - dest) * 2 + line.lo, 2 * line.far - 1, dest * 2 + line.lo)
        pl.when((line.hi == 1) | (line.hi == 2))(functools.partial(act, one))

    def copy(self, index, slot, dest):
        block = self.at(index)
        return self.line.push(
            dest, block, block, self.send.at[self.base + slot], self.recv.at[self.base + index]
        )

    def start_far(self):
        self.far_sends(lambda one: one.start())

    def start_near(self):
        self.copy(self.line.me, self.line.far - 1, self.line.partner).start()

    def start(self):
        self.start_far()
        self.start_near()

    def relay(self, step):
        line = self.line
        handed = self.copy(self.source(step) * 2 + line.lo, line.far - 1 + step, line.partner)
        handed.wait_recv()
        if self.ends and step == 2:
            self.to_end(lambda one: one.start())
        handed.start()

    def relays(self):
        for step in range(1, self.line.far):
            self.relay(step)

    def close(self):
        line = self.line
        for step in range(line.far):
            self.copy(line.at(-step) * 2 + (1 - line.lo), 0, line.partner).wait_recv()

    def drain(self):
        self.far_sends(lambda one: one.wait_send())
        if self.ends:
            self.to_end(lambda one: one.wait_send())
        for slot in range(self.line.far - 1, 2 * self.line.far - 1):
            self.copy(self.line.me, slot, self.line.partner).wait_send()


class Scatter:
    def __init__(self, line, part, first, second, send, recv, base=0, extra=None):
        self.line, self.part, self.first, self.second = line, part, first, second
        self.send, self.recv, self.base = send, recv, base
        self.extra = extra if line.far == 4 else None

    def clear(self):
        line = self.line
        if self.extra is not None:

            @pl.when((line.hi == 0) | (line.hi == 3))
            def _():
                slot = self.second(3 - line.hi)
                slot[...] = jnp.zeros(slot.shape, LOW)

    def order(self, step):
        line = self.line
        if self.extra is None:
            return line.at(step)
        table = ((3, 2, 1), (2, 0, 3), (1, 3, 0), (0, 1, 2))
        hi = table[3][step - 1]
        for place in (2, 1, 0):
            hi = jnp.where(line.hi == place, table[place][step - 1], hi)
        return hi

    def traded(self, hi):
        line = self.line
        return line.push(
            line.partner,
            self.part(hi * 2 + (1 - line.lo)),
            self.first(hi),
            self.send.at[self.base + hi],
            self.recv.at[self.base + hi],
        )

    def passed(self, step):
        line = self.line
        hi = self.order(step)
        return line.push(
            hi * 2 + line.lo,
            self.part(hi * 2 + line.lo),
            self.second(line.hi),
            self.send.at[self.base + line.far + step - 1],
            self.recv.at[self.base + line.far + line.hi],
        )

    def to_next(self):
        line = self.line
        return line.push(
            jnp.where(line.hi < 2, 1, 2) * 2 + line.lo,
            self.part((3 - jnp.where(line.hi < 2, 0, 3)) * 2 + line.lo),
            self.extra,
            self.send.at[self.base + line.far],
            self.recv.at[self.base + 2 * line.far],
        )

    def turn_of(self, turn):
        line = self.line
        if self.extra is None:
            return lax.rem(line.hi + turn + 1, line.far)
        hi = line.hi
        for step in range(1, line.far):
            hi = jnp.where(turn == step - 1, self.order(step), hi)
        return hi

    def is_end(self):
        return (self.line.hi == 0) | (self.line.hi == 3)

    def trade(self, hi):
        self.traded(hi).start()

    def trade_all(self):
        for step in range(1, self.line.far + 1):
            self.trade(self.order(step) if step < self.line.far else self.line.hi)

    def pass_on(self, step):
        line = self.line
        hi = self.order(step)
        self.traded(hi).wait_recv()
        mine, other = self.part(hi * 2 + line.lo), self.first(hi)
        if self.extra is None or step == 2:
            mine[...] = (mine[...].astype(F32) + other[...].astype(F32)).astype(LOW)
            self.passed(step).start()
        elif step == 1:
            mine[...] = (mine[...].astype(F32) + other[...].astype(F32)).astype(LOW)

            @pl.when(self.is_end())
            def _():
                self.to_next().start()

            @pl.when(jnp.logical_not(self.is_end()))
            def _():
                self.passed(step).start()
        else:

            @pl.when(self.is_end())
            def _():
                mine[...] = (mine[...].astype(F32) + other[...].astype(F32)).astype(LOW)

            @pl.when(jnp.logical_not(self.is_end()))
            def _():
                line.push(
                    line.partner,
                    self.extra,
                    self.extra,
                    self.send.at[self.base],
                    self.recv.at[self.base + 2 * line.far],
                ).wait_recv()
                mine[...] = (
                    mine[...].astype(F32) + other[...].astype(F32) + self.extra[...].astype(F32)
                ).astype(LOW)

            self.passed(step).start()

    def arrive(self):
        line = self.line
        self.traded(line.hi).wait_recv()
        for step in range(1, line.far):
            hi = line.at(-step)
            one = line.push(
                line.partner,
                self.second(hi),
                self.second(hi),
                self.send.at[self.base],
                self.recv.at[self.base + line.far + hi],
            )
            if self.extra is None:
                one.wait_recv()
            else:
                pl.when(jnp.logical_not(self.is_end()) | (hi + line.hi != 3))(one.wait_recv)

    def total(self, here):
        line = self.line
        value = self.part(line.me)[here, :].astype(F32) + self.first(line.hi)[here, :].astype(F32)
        for step in range(1, line.far):
            value = value + self.second(line.at(-step))[here, :].astype(F32)
        return value

    def drain(self):
        line = self.line
        for step in range(line.far):
            self.traded(line.at(step)).wait_send()
        for step in range(1, line.far):
            if self.extra is not None and step == 1:
                pl.when(self.is_end())(lambda: self.to_next().wait_send())
                pl.when(jnp.logical_not(self.is_end()))(lambda: self.passed(1).wait_send())
            else:
                self.passed(step).wait_send()


def block_rows(ref, rows, first=0):
    return lambda index: ref.at[pl.ds(pl.multiple_of((index + first) * rows, rows), rows)]


def part_rows(ref, rows, first, count):
    return lambda index: ref.at[pl.ds(pl.multiple_of(index * rows + first, count), count)]


def of_index(ref):
    return lambda index: ref.at[index]


def norm_rows(values):
    center = values - jnp.mean(values, -1, keepdims=True)
    spread = jnp.mean(center * center, -1, keepdims=True)
    inverse = lax.rsqrt(spread + EPS_LAYER)
    return center * inverse, inverse


def norm_back(values, gain, grad):
    unit, inverse = norm_rows(values)
    inner = grad * gain
    shared = jnp.mean(inner, -1, keepdims=True)
    along = jnp.mean(inner * unit, -1, keepdims=True)
    return inverse * (inner - shared - unit * along), unit


def head_masks(width):
    lane = lax.broadcasted_iota(jnp.int32, (1, width), 1)
    return [
        jnp.where((lane >= head * HD) & (lane < (head + 1) * HD), 1.0, 0.0)
        for head in range(width // HD)
    ]


def spread_heads(values, masks):
    return jnp.concatenate([values * mask.astype(LOW) for mask in masks], 0)


def join_heads(values, masks, rows):
    total = values[0:rows] * masks[0]
    for head in range(1, len(masks)):
        total = total + values[head * rows : (head + 1) * rows] * masks[head]
    return total


TAIL = (
    0.2256758632450557,
    0.22566952478278277,
    0.2078438574180613,
    0.16853390514724884,
    0.14146086231844687,
    -0.005667717379728321,
    0.16915486959066833,
    -0.18294364197603524,
    0.05027260226320005,
)


def normal_tail(size, bell):
    base = 1.0 + (0.4 * 0.5**0.5) * size
    t = pl.reciprocal(base, approx=True)
    t = t * (2.0 - base * t)
    t = t * (2.0 - base * t)
    value = jnp.full_like(t, 0.5 * TAIL[-1])
    for factor in TAIL[-2::-1]:
        value = value * t + 0.5 * factor
    return value * t * bell


def far_copies(line, make, sends, recvs):
    def copy(step):
        dest = lax.rem(line.me + step, line.size)
        src, dst = make(dest, line.me)
        return line.push(dest, src, dst, sends.at[step], recvs.at[line.me])

    def wait():
        for step in range(1, line.size):
            source = lax.rem(line.me + line.size - step, line.size)
            _, dst = make(source, source)
            line.push(line.partner, dst, dst, sends.at[0], recvs.at[source]).wait_recv()

    return copy, wait


def layer_kernel(cap, names, *refs):
    R = types.SimpleNamespace(**dict(zip(names, refs)))
    dp, mp = Line("dp"), Line("mp")
    size, ways = dp.size, mp.size
    seqs, seq_len = R.ids.shape
    tokens, width = R.noise.shape
    model = R.cot.shape[1]
    heads_w = R.o.shape[1]
    hidden = R.wbf.shape[1]
    table_rows = R.table.shape[0]
    rin = R.w_in.shape[0]
    rin_up = round_up(rin, 16)
    quarter = model // ways
    strip = R.w_up.shape[0]
    spots = size * cap
    far = mp.far
    count = seqs * far
    own_strip = pl.ds(pl.multiple_of(dp.me * strip, strip), strip)
    mine = pl.ds(pl.multiple_of(dp.me * cap, cap), cap)

    some_rows = seq_len // 2

    def rows_of(piece):
        return lambda row: pl.ds(pl.multiple_of(piece * seq_len + row, some_rows), some_rows)

    def own_rows(piece):
        first = pl.multiple_of((piece * ways + mp.me) * seq_len, seq_len)
        return lambda row: pl.ds(pl.multiple_of(first + row, some_rows), some_rows)

    def by_rows(body, after=lambda half: None):
        for half in range(2):
            body(half * some_rows)
            after(half)

    class Rows:
        def __init__(self, ref, send, recv, piece):
            self.parts = [
                Gather(
                    mp,
                    lambda index, half=half: ref.at[
                        pl.ds(
                            pl.multiple_of(
                                (piece * ways + index) * seq_len + half * some_rows, some_rows
                            ),
                            some_rows,
                        )
                    ],
                    send,
                    recv,
                    (2 * piece + half) * ways,
                )
                for half in range(2)
            ]

        def start(self, half):
            self.parts[half].start()

        def relays(self):
            for part in self.parts:
                part.relays()

        def close(self):
            for part in self.parts:
                part.close()

        def drain(self):
            for part in self.parts:
                part.drain()

    def halves(ref, send, recv):
        return [Rows(ref, send, recv, piece) for piece in range(seqs)]

    chunk_cols = min(256, model)
    chunk_count = model // chunk_cols

    class Sums:
        def __init__(self, *refs):
            *self.refs, self.send, self.recv = refs

        def chunk(self, piece, chunk):
            cols = pl.ds(pl.multiple_of(chunk * chunk_cols, chunk_cols), chunk_cols)

            def blocks(ref, first):
                return lambda index: ref.at[
                    pl.ds(pl.multiple_of((index + first) * seq_len, seq_len), seq_len), cols
                ]

            firsts = (piece * ways, piece * far, piece * far)
            views = [blocks(ref, first) for ref, first in zip(self.refs, firsts)]
            return Scatter(mp, *views, self.send, self.recv, (piece * chunk_count + chunk) * ways)

        def total(self, piece, here):
            firsts = (piece * ways, piece * far, piece * far)
            views = [block_rows(ref, seq_len, first) for ref, first in zip(self.refs, firsts)]
            return Scatter(mp, *views, self.send, self.recv).total(here)

        def trade(self, piece, chunk):
            self.chunk(piece, chunk).trade_all()

        def hand_on(self, piece, chunk):
            scatter = self.chunk(piece, chunk)
            for step in range(1, far):
                scatter.pass_on(step)

        def every(self, act):
            def one(chunk, carry):
                act(chunk)
                return carry

            lax.fori_loop(0, chunk_count, one, 0)

        def hand_on_all(self, piece):
            self.every(lambda chunk: self.hand_on(piece, chunk))

        def arrive(self, piece):
            self.every(lambda chunk: self.chunk(piece, chunk).arrive())

        def drain(self, piece):
            self.every(lambda chunk: self.chunk(piece, chunk).drain())

        def products(self, piece, make):
            def one(chunk, carry):
                make(pl.ds(pl.multiple_of(chunk * chunk_cols, chunk_cols), chunk_cols))
                self.trade(piece, chunk)
                pl.when(chunk > 0)(lambda: self.hand_on(piece, chunk - 1))
                return carry

            lax.fori_loop(0, chunk_count, one, 0)

        def hand_on_last(self, piece):
            self.hand_on(piece, chunk_count - 1)

    many = ways * seq_len

    def turns(body, hooks=()):
        def one(piece, carry):
            def at(point):
                for place, when, action in hooks:
                    if when == point:
                        pl.when(piece == place)(action)

            base = pl.multiple_of(piece * many, many)
            body(piece, base, pl.ds(base, many), at)
            return carry

        lax.fori_loop(0, seqs, one, 0)

    def pairs(base, body):
        def one(pair, carry):
            first = pl.multiple_of(base + pair * (2 * seq_len), 2 * seq_len)
            body([pl.ds(pl.multiple_of(first + seq * seq_len, seq_len), seq_len) for seq in range(2)])
            return carry

        lax.fori_loop(0, far, one, 0)

    def chunks(total, body):
        step = min(256, total)
        lax.fori_loop(
            0,
            total // step,
            lambda turn, carry: (body(pl.ds(pl.multiple_of(turn * step, step), step)), carry)[1],
            0,
        )

    def later_pieces(gathers, point):
        hooks = []
        for piece in range(1, seqs):
            hooks.append((piece - 1, point, gathers[piece].relays))
            hooks.append((piece, "start", gathers[piece].close))
        return hooks

    chunk = R.tab.shape[1]
    pieces = -(-table_rows // chunk)

    def fetch(piece):
        rows = min(chunk, table_rows - piece * chunk)
        return pltpu.make_async_copy(
            R.table.at[pl.ds(piece * chunk, rows)],
            R.tab.at[piece % 2, pl.ds(0, rows)],
            R.tab_sem.at[piece % 2],
        )

    for piece in range(min(2, pieces)):
        fetch(piece).start()

    names_of_moments = [
        name + kind for name in ("w_in", "ln", "qkv", "out", "up", "down") for kind in ("_m", "_v")
    ]

    def moment(name):
        return pltpu.make_async_copy(
            getattr(R, name), getattr(R, name + "_here"), R.moment_sem.at[names_of_moments.index(name)]
        )

    tile_rows = R.tw.shape[1]
    tiles = table_rows // tile_rows

    def tile_of(tile):
        side = lax.rem(tile, 2)
        rows = pl.ds(pl.multiple_of(tile * tile_rows, tile_rows), tile_rows)
        return [
            pltpu.make_async_copy(source.at[rows], dest.at[side], R.tile_sem.at[2 * place + side])
            for place, (source, dest) in enumerate(
                ((R.table, R.tw), (R.table_m, R.tm), (R.table_v, R.tv))
            )
        ]

    eye = lax.broadcasted_iota(jnp.int32, (seq_len, seq_len), 0) == lax.broadcasted_iota(
        jnp.int32, (seq_len, seq_len), 1
    )
    id_rows = R.ids[...].astype(F32)
    ids = jnp.concatenate(
        [
            jnp.sum(jnp.where(eye, id_rows[seq : seq + 1, :], 0.0), 1, keepdims=True)
            for seq in range(seqs)
        ],
        0,
    )
    lane = lax.broadcasted_iota(jnp.int32, (tokens, 128), 1).astype(F32)
    low_end = lane * float(table_rows)
    owned = jnp.where((ids >= low_end) & (ids < low_end + float(table_rows)), 1.0, 0.0)
    before = jnp.where(
        lax.broadcasted_iota(jnp.int32, (tokens, tokens), 0)
        >= lax.broadcasted_iota(jnp.int32, (tokens, tokens), 1),
        1.0,
        0.0,
    )
    ranks = dot(before.astype(LOW), owned.astype(LOW))
    rank = jnp.sum(owned * ranks, 1, keepdims=True) - 1.0
    slot = jnp.sum(owned * lane, 1, keepdims=True) * cap + rank
    placed = jnp.where(lane == rank, 1.0, 0.0)
    upper = jnp.floor(ids * (1.0 / 256.0))
    lower = ids - upper * 256.0
    parts = jnp.concatenate([placed * upper, placed * lower, placed], 1).astype(LOW)
    asked = dot_tn(owned.astype(LOW), parts)
    asked = asked[:, :128] * 256.0 + asked[:, 128:256] + asked[:, 256:] - 1.0
    wide_ln = R.ln_params.shape[1]
    shares = R.ln_params[...].astype(LOW).astype(F32)
    if wide_ln < 128:
        shares = jnp.concatenate([shares, jnp.zeros((4, 128 - wide_ln), F32)], 1)
    for index in range(size):
        R.ask[index] = jnp.concatenate(
            [asked[index : index + 1, :], shares, jnp.zeros((3, 128), F32)], 0
        )
    R.idx[mp.me, dp.me] = R.ask[dp.me]

    def spread(part, first, second, extra, send, recv):
        blocks = [block_rows(ref, strip) for ref in (part, first, second)]
        return Scatter(dp, *blocks, send, recv, 0, extra)

    up = spread(R.wbf, R.up_first, R.up_second, R.up_extra, R.up_send, R.up_recv)
    down = spread(R.gdn, R.dn_first, R.dn_second, R.dn_extra, R.dn_send, R.dn_recv)
    first_w = spread(
        R.waf.at[:, : 3 * heads_w], R.wa_first, R.wa_second, R.wa_extra, R.ga_send, R.ga_recv
    )
    wo = spread(R.gwo, R.wo_first, R.wo_second, R.wo_extra, R.wo_send, R.wo_recv)
    small = Scatter(
        dp,
        *[of_index(ref) for ref in (R.gw, R.gw_first, R.gw_second)],
        R.gw_send,
        R.gw_recv,
        0,
        R.gw_extra,
    )
    for scatter in (up, down, first_w, wo, small):
        scatter.clear()

    meet([mp], [dp])
    ask, ask_wait = far_copies(
        dp,
        lambda dest, source: (R.ask.at[dest], R.idx.at[mp.me, source]),
        R.ask_send,
        R.ask_recv,
    )
    for step in range(1, size):
        ask(step).start()

    mine_in = R.winf.at[mp.me]
    win = Gather(dp, block_rows(mine_in, rin), R.win_send, R.win_recv, 0, True)
    win_all = Gather(mp, of_index(R.winf), R.wim_send, R.wim_recv)
    half_strip = strip // 2
    wa = [
        Gather(dp, part_rows(R.waf, strip, piece * half_strip, half_strip), send, recv, 0, True)
        for piece, (send, recv) in enumerate(((R.wa_send, R.wa_recv), (R.wx_send, R.wx_recv)))
    ]
    wb = Gather(dp, block_rows(R.wbf, strip), R.wb_send, R.wb_recv, 0, True)
    wc = Gather(dp, block_rows(R.wcf, strip), R.wc_send, R.wc_recv, 0, True)
    dxg = Gather(
        mp,
        lambda index: R.dx.at[:, pl.ds(pl.multiple_of(index * seq_len, seq_len), seq_len)],
        R.dx_send,
        R.dx_recv,
    )
    ag = halves(R.a, R.a_send, R.a_recv)
    cg = halves(R.c, R.c_send, R.c_recv)
    mg = halves(R.dmid_all, R.e_send, R.e_recv)

    mine_in[pl.ds(pl.multiple_of(dp.me * rin, rin), rin), :] = (
        R.w_in[:, pl.ds(pl.multiple_of(mp.me * quarter, quarter), quarter)]
        .astype(LOW)
        .astype(R.winf.dtype)
    )
    win.start()
    for part in range(3):
        R.waf[own_strip, part * heads_w : (part + 1) * heads_w] = R.w_qkv[part].astype(LOW)
    R.waf[own_strip, 3 * heads_w :] = R.w_out[...].T.astype(LOW)
    wa[0].start()
    wa[1].start_near()
    for name in names_of_moments:
        moment(name).start()

    for seq in range(seqs):
        level = jnp.full((seq_len, 1), R.levels[seq], jnp.int32).astype(F32) / (LEVELS - 1)
        R.sig[seq * seq_len : (seq + 1) * seq_len, :] = jnp.exp(level * jnp.log(SIGMA_TOP))

    def scale_at(here):
        sig = R.sig[here, :]
        return sig * lax.rsqrt(1.0 + sig * sig)

    for piece in range(seqs):
        here = rows_of(piece)

        def scale_cot(row, here=here, piece=piece):
            there = pl.ds(pl.multiple_of(mp.me * seq_len + row, some_rows), some_rows)
            R.dx[piece, there, :] = (R.cot[here(row), :].astype(F32) * scale_at(here(row))).astype(LOW)

        by_rows(scale_cot)
    dxg.start()
    R.wbf[own_strip, :] = R.w_up[...].astype(LOW)
    R.wcf[own_strip, :] = R.w_down[...].T.astype(LOW)
    wb.start_near()
    R.pick[...] = jnp.where(
        lax.broadcasted_iota(jnp.int32, (tokens, spots), 1).astype(F32) == slot, 1.0, 0.0
    ).astype(LOW)
    win.relays()

    ask_wait()
    small_eye = lax.broadcasted_iota(jnp.int32, (cap, 128), 0) == lax.broadcasted_iota(
        jnp.int32, (cap, 128), 1
    )

    def locate(index, carry):
        row = R.idx[mp.me, index][0:1, :]
        column = jnp.sum(jnp.where(small_eye, row, 0.0), 1, keepdims=True)
        local = column.astype(jnp.int32) - dp.me * table_rows
        R.loc[pl.ds(pl.multiple_of(index * cap, cap), cap), :] = jnp.broadcast_to(local, (cap, 128))
        return carry

    lax.fori_loop(0, size, locate, 0, unroll=True)
    win.close()
    win_all.start()
    found = None
    for piece in range(pieces):
        fetch(piece).wait()
        rows = min(chunk, table_rows - piece * chunk)
        if rows < chunk:
            R.tab[piece % 2, rows:, :] = jnp.zeros((chunk - rows, width), F32)
        hit = (
            lax.broadcasted_iota(jnp.int32, (spots, chunk), 1) + piece * chunk == R.loc[:, 0:1]
        )
        more = dot(jnp.where(hit, 1.0, 0.0).astype(LOW), R.tab[piece % 2].astype(LOW))
        found = more if found is None else found + more
        if piece + 2 < pieces:
            fetch(piece + 2).start()
    R.give[...] = found.astype(LOW)

    give, give_wait = far_copies(
        dp,
        lambda dest, source: (block_rows(R.give, cap)(dest), block_rows(R.got, cap)(source)),
        R.give_send,
        R.give_recv,
    )
    for step in range(1, size):
        give(step).start()
    R.got[mine, :] = R.give[mine, :]
    wa[1].start_far()
    win_all.relays()
    wa[0].relay(1)
    wa[0].relay(2)
    if wide_ln % 128 == 0:
        R.gains[...] = jnp.concatenate([R.idx[mp.me, index] for index in range(size)], 1)
    else:
        total = jnp.zeros((8, model), F32)
        for index in range(size):
            place = lax.broadcasted_iota(
                jnp.int32, (128, model), 1
            ) == index * wide_ln + lax.broadcasted_iota(jnp.int32, (128, model), 0)
            place = place & (lax.broadcasted_iota(jnp.int32, (128, model), 0) < wide_ln)
            total = total + dot(
                R.idx[mp.me, index].astype(LOW), jnp.where(place, 1.0, 0.0).astype(LOW)
            )
        R.gains[...] = total
    for step in range(3, dp.far):
        wa[0].relay(step)
    named = Gather(mp, of_index(R.idx), R.id_send, R.id_recv)

    give_wait()
    rows = dot(R.pick[...], R.got[...])
    R.rows[...] = rows.astype(LOW)
    sig = R.sig[...]
    unit = rows * lax.rsqrt(jnp.mean(rows * rows, -1, keepdims=True) + EPS_NORM)
    R.mixed[...] = ((unit + sig * R.noise[...].astype(F32)) * lax.rsqrt(1.0 + sig * sig)).astype(LOW)
    win_all.close()
    for index in range(ways):
        R.x0[:, index * quarter : (index + 1) * quarter] = dot(
            R.mixed[...], R.winf[index].astype(LOW)
        )

    for piece in range(seqs):
        here, there = rows_of(piece), own_rows(piece)

        def first_norm(row, here=here, there=there):
            normed, _ = norm_rows(R.x0[here(row), :])
            R.a[there(row), :] = (normed * R.gains[1:2, :] + R.gains[2:3, :]).astype(LOW)

        by_rows(first_norm, ag[piece].start)
    wa[1].relays()
    wb.start_far()
    wc.start_near()
    dxg.relays()
    named.start()
    win.drain()
    for step in range(1, size):
        ask(step).wait_send()
    ag[0].relays()
    for gather in (*wa, ag[0]):
        gather.close()

    att = Sums(R.part, R.fold, R.fold_far, R.as_send, R.as_recv)
    dcs = Sums(R.part, R.fold, R.fold_far, R.cs_send, R.cs_recv)
    das = Sums(R.part, R.fold, R.fold_far, R.ds_send, R.ds_recv)
    out = Sums(R.c, R.first, R.second, R.os_send, R.os_recv)
    masks = head_masks(heads_w)

    all_rows = (heads_w // HD) * seq_len
    scale = HD ** (-0.5)

    def softmax(seq, row):
        scores = R.scores[seq, row : row + 64, :]
        raised = jnp.exp((scores - jnp.max(scores, -1, keepdims=True)) * scale)
        return raised * (1.0 / jnp.sum(raised, -1, keepdims=True))

    def attend(piece, base, here, at):
        at("start")
        for part in range(3):
            cols = slice(part * heads_w, (part + 1) * heads_w)
            R.qkv[here, cols] = dot(R.a[here, :], R.waf[:, cols]).astype(LOW)
        at("mid")

        def one(rows_at):
            for seq, rows in enumerate(rows_at):
                queries = spread_heads(R.qkv[rows, :heads_w], masks)
                R.scores[seq] = dot_nt(queries, R.qkv[rows, heads_w : 2 * heads_w])
            for seq, rows in enumerate(rows_at):
                for row in range(0, all_rows, 64):
                    R.probs[seq, row : row + 64, :] = softmax(seq, row).astype(LOW)
                seen = dot(R.probs[seq], R.qkv[rows, 2 * heads_w : 3 * heads_w])
                R.o[rows, :] = join_heads(seen, masks, seq_len).astype(LOW)

        pairs(base, one)
        at("late")

        def project(cols):
            R.part[here, cols] = dot_nt(R.o[here, :], R.waf[cols, 3 * heads_w :]).astype(LOW)

        def one_chunk(chunk, carry):
            project(pl.ds(pl.multiple_of(chunk * chunk_cols, chunk_cols), chunk_cols))
            att.trade(piece, chunk)
            return carry

        lax.fori_loop(0, chunk_count, one_chunk, 0)

    def second_norm(piece):
        here, there = rows_of(piece), own_rows(piece)
        att.arrive(piece)

        def norm(row):
            x1 = R.x0[here(row), :] + att.total(piece, pl.ds(row, some_rows))
            R.out[here(row), :] = x1
            normed, _ = norm_rows(x1)
            R.c[there(row), :] = (normed * R.gains[3:4, :] + R.gains[4:5, :]).astype(LOW)

        by_rows(norm, cg[piece].start)

    def before_late():
        wb.relay(1)
        wb.relay(2)
        wc.start_far()

    turns(
        attend,
        [
            *later_pieces(ag, "mid"),
            *[
                (piece + 1, "mid", functools.partial(att.hand_on_all, piece))
                for piece in range(seqs - 1)
            ],
            (seqs - 1, "late", before_late),
        ],
    )
    att.hand_on_all(seqs - 1)
    for step in range(3, dp.far):
        wb.relay(step)
    for piece in range(seqs):
        second_norm(piece)
        if piece == 0:
            for gather in (*wa, *ag, dxg):
                gather.drain()
    cg[0].relays()
    wb.close()
    named.relays()
    cg[0].close()
    for piece in range(seqs):
        att.drain(piece)

    def activate(piece, base, here, at):
        at("start")

        def some(cols):
            R.h[...] = dot(R.c[here, :], R.wbf[:, cols])

            def gelu(row):
                there = pl.ds(pl.multiple_of(base + row, 64), 64)
                h = R.h[pl.ds(row, 64), :]
                bell = jnp.exp(-0.5 * h * h)
                tail = normal_tail(jnp.abs(h), bell)
                gate = jnp.where(h >= 0.0, 1.0 - tail, tail)
                slope = gate + h * (bell * 0.3989422804014327)
                R.hb[there, cols] = (h * gate).astype(LOW)
                R.slope[there, cols] = slope.astype(LOW)

            strips(many, 64, gelu, 2)

        chunks(hidden, some)
        at("end")

    def relay_wc():
        wc.relays()

    turns(activate, [*later_pieces(cg, "end"), (0, "end", relay_wc)])

    due = [(scatter, step) for scatter in (down, up) for step in range(1, dp.far)]

    def pass_due(number):
        for _ in range(min(number, len(due))):
            scatter, step = due.pop(0)
            scatter.pass_on(step)

    block = 2 * strip if (2 * strip) % 128 == 0 else min(256, model)

    def grads(make, trades):
        if block == 2 * strip:

            def turn_of(turn, carry):
                hi = up.turn_of(turn)
                make(pl.ds(pl.multiple_of(hi * block, block), block))
                for scatter in trades:
                    scatter.trade(hi)
                return carry

            lax.fori_loop(0, dp.far, turn_of, 0)
        else:
            strips(model, block, lambda col: make(pl.ds(col, block)))
            for scatter in trades:
                scatter.trade_all()

    def down_grads(cols):
        every = R.dx[:, :, cols]
        R.gdn[cols, :] = dot_tn(every.reshape(seqs * many, block), R.hb[...]).astype(LOW)

    def up_grads(cols):
        R.wbf[cols, :] = dot_tn(R.c[:, cols], R.dhb[...]).astype(LOW)

    dxg.close()
    grads(down_grads, ())
    wc.close()
    down.trade_all()
    for gather in (wb, *cg):
        gather.drain()

    def feed_back(piece, base, here, at):
        at("start")

        def some(cols):
            bent = dot(R.dx[piece], R.wcf[:, cols]) * R.slope[here, cols].astype(F32)
            R.dhb[here, cols] = bent.astype(LOW)

        chunks(hidden, some)
        at("mid")

        def project(cols):
            R.part[here, cols] = dot_nt(R.dhb[here, :], R.wbf[cols, :]).astype(LOW)

        dcs.products(piece, project)

    R.norms[...] = jnp.zeros_like(R.norms)

    def second_back(piece):
        here, there = rows_of(piece), own_rows(piece)
        dcs.arrive(piece)

        def back(row):
            dc = dcs.total(piece, pl.ds(row, some_rows))
            grad, unit = norm_back(R.out[here(row), :], R.gains[3:4, :], dc)
            grad = grad + R.cot[here(row), :].astype(F32) * scale_at(here(row))
            R.dmid[here(row), :] = grad
            R.dmid_all[there(row), :] = grad.astype(LOW)
            R.norms[2:3, :] += jnp.sum(dc * unit, 0, keepdims=True)
            R.norms[3:4, :] += jnp.sum(dc, 0, keepdims=True)

        by_rows(back, mg[piece].start)

    turns(
        feed_back,
        [
            (piece + 1, "mid", functools.partial(dcs.hand_on_last, piece))
            for piece in range(seqs - 1)
        ],
    )
    dcs.hand_on_last(seqs - 1)
    second_back(0)
    grads(up_grads, ())
    for piece in range(1, seqs):
        second_back(piece)
    pass_due(1)
    mg[0].relays()
    mg[0].close()
    for piece in range(seqs):
        dcs.drain(piece)

    def attend_back(piece, base, here, at):
        at("start")
        R.low[...] = dot(R.dmid_all[here, :], R.waf[:, 3 * heads_w :]).astype(LOW)
        at("mid")

        def one(rows_at):
            for seq, rows in enumerate(rows_at):
                queries = spread_heads(R.qkv[rows, :heads_w], masks)
                R.scores[seq] = dot_nt(queries, R.qkv[rows, heads_w : 2 * heads_w])
                upper_rows = pl.ds(pl.multiple_of(rows.start - base, seq_len), seq_len)
                R.upper[seq] = spread_heads(R.low[upper_rows, :], masks)
                R.dprobs[seq] = dot_nt(R.upper[seq], R.qkv[rows, 2 * heads_w : 3 * heads_w])
            for seq, rows in enumerate(rows_at):
                for row in range(0, all_rows, 64):
                    probs = softmax(seq, row)
                    grad_probs = R.dprobs[seq, row : row + 64, :]
                    inner = jnp.sum(probs * grad_probs, -1, keepdims=True)
                    R.probs[seq, row : row + 64, :] = probs.astype(LOW)
                    R.dscores[seq, row : row + 64, :] = (probs * (grad_probs - inner)).astype(LOW)
                keys = R.qkv[rows, heads_w : 2 * heads_w]
                queries = spread_heads(R.qkv[rows, :heads_w], masks)
                R.qkv[rows, 2 * heads_w : 3 * heads_w] = dot_tn(R.probs[seq], R.upper[seq]).astype(LOW)
                R.qkv[rows, heads_w : 2 * heads_w] = (dot_tn(R.dscores[seq], queries) * scale).astype(
                    LOW
                )
                R.qkv[rows, :heads_w] = (
                    join_heads(dot(R.dscores[seq], keys), masks, seq_len) * scale
                ).astype(LOW)

        pairs(base, one)
        at("late")

        def project(cols):
            R.part[here, cols] = dot_nt(R.qkv[here, :], R.waf[cols, : 3 * heads_w]).astype(LOW)

        das.products(piece, project)

    def first_back(piece):
        here = rows_of(piece)
        das.arrive(piece)

        def back(row):
            da = das.total(piece, pl.ds(row, some_rows))
            grad, unit = norm_back(R.x0[here(row), :], R.gains[1:2, :], da)
            R.dx0[here(row), :] = (R.dmid[here(row), :] + grad).astype(LOW)
            R.norms[0:1, :] += jnp.sum(da * unit, 0, keepdims=True)
            R.norms[1:2, :] += jnp.sum(da, 0, keepdims=True)

        by_rows(back)

    def out_grads():
        def make(cols):
            R.gwo[cols, :] = dot_tn(R.dmid_all[:, cols], R.o[...]).astype(LOW)

        grads(make, (wo,))

    def queue_up():
        up.trade_all()
        pass_due(1)

    def queue_up():
        up.trade_all()
        pass_due(1)

    turns(
        attend_back,
        [
            *later_pieces(mg, "mid"),
            (0, "late", queue_up),
            *[
                (piece + 1, "mid", functools.partial(das.hand_on_last, piece))
                for piece in range(seqs - 1)
            ],
            (seqs - 1, "late", lambda: pass_due(max(1, dp.far - 3))),
        ],
    )
    das.hand_on_last(seqs - 1)
    def out_grads(cols):
        R.gwo[cols, :] = dot_tn(R.dmid_all[:, cols], R.o[...]).astype(LOW)

    def attend_grads(cols):
        R.waf[cols, : 3 * heads_w] = dot_tn(R.a[:, cols], R.qkv[...]).astype(LOW)

    grads(out_grads, (wo,))
    first_back(0)
    grads(attend_grads, (first_w,))
    for piece in range(1, seqs):
        first_back(piece)

    grad_mixed = sum(
        dot_nt(R.dx0[:, index * quarter : (index + 1) * quarter], R.winf[index].astype(LOW))
        for index in range(ways)
    )
    sig = R.sig[...]
    grad_unit = grad_mixed * lax.rsqrt(1.0 + sig * sig)
    rows = R.rows[...].astype(F32)
    inverse = lax.rsqrt(jnp.mean(rows * rows, -1, keepdims=True) + EPS_NORM)
    unit = rows * inverse
    grad_rows = inverse * (grad_unit - unit * jnp.mean(grad_unit * unit, -1, keepdims=True))
    for step in range(1, size):
        give(step).wait_send()
    R.give[...] = dot_tn(R.pick[...], grad_rows.astype(LOW)).astype(LOW)
    mine_inc = block_rows(R.inc, spots)(mp.me)
    back, back_wait = far_copies(
        dp,
        lambda dest, source: (block_rows(R.give, cap)(dest), block_rows(mine_inc, cap)(source)),
        R.back_send,
        R.back_recv,
    )
    for step in range(1, size):
        back(step).start()
    mine_inc[mine, :] = R.give[mine, :]

    small_mp = Scatter(
        mp, of_index(R.gm), of_index(R.gm_first), of_index(R.gm_second), R.gm_send, R.gm_recv
    )
    for index in range(ways):
        cols = slice(index * quarter, (index + 1) * quarter)
        R.gm[index, :width, :] = dot_tn(R.mixed[...], R.dx0[:, cols]).astype(LOW)
        R.gm[index, width:, :] = jnp.concatenate(
            [R.norms[0:4, cols], jnp.zeros((12, quarter), F32)], 0
        ).astype(LOW)
    small_mp.trade_all()
    pass_due(2)
    for step in range(1, far):
        small_mp.pass_on(step)

    def feed_out(piece, base, here, at):
        def project(cols):
            R.c[here, cols] = dot_nt(R.hb[here, :], R.wcf[cols, :]).astype(LOW)

        out.products(piece, project)

    turns(feed_out)

    back_wait()
    rows_in = Gather(mp, block_rows(R.inc, spots), R.in_send, R.in_recv)
    rows_in.start()
    pass_due(len(due))
    for step in range(1, dp.far):
        wo.pass_on(step)
    for piece in range(seqs):
        out.hand_on_last(piece)

    small_mp.arrive()
    summed = small_mp.total(slice(None))
    for index in range(size):
        piece = summed[index * rin : (index + 1) * rin, :]
        if rin_up > rin:
            piece = jnp.concatenate([piece, jnp.zeros((rin_up - rin, quarter), F32)], 0)
        R.gw[index, :rin_up, :] = piece.astype(LOW)
        R.gw[index, rin_up:, :] = summed[width:, :].astype(LOW)
    small.trade_all()
    rows_in.relays()
    first_w.pass_on(1)

    def finish_out(piece):
        here = rows_of(piece)
        out.arrive(piece)

        def finish(row):
            R.out[here(row), :] = (
                R.out[here(row), :] + out.total(piece, pl.ds(row, some_rows))
            ) * scale_at(here(row))

        by_rows(finish)

    for piece in range(seqs):
        finish_out(piece)

    named.close()
    rows_in.close()
    groups = ways * size
    some, lanes_at = min(groups, 32), min(ways * spots, 512)
    for begin in range(0, ways * spots, lanes_at):
        spot = lax.broadcasted_iota(jnp.int32, (128, lanes_at), 1).astype(F32) + float(begin)
        block_no = jnp.floor((spot + 0.5) * (1.0 / cap))
        place = lax.broadcasted_iota(jnp.int32, (128, lanes_at), 0).astype(F32)
        spread_out = jnp.where(spot - block_no * cap == place, 1.0, 0.0).astype(LOW)
        named_row = jnp.zeros((1, lanes_at), F32)
        for first in range(0, groups, some):
            wanted = jnp.concatenate(
                [
                    R.idx[index // size, index % size][0:1, :] + 1.0
                    for index in range(first, first + some)
                ],
                0,
            )
            high = jnp.floor(wanted * (1.0 / 256.0))
            rest = wanted - 256.0 * high
            laid = dot(high.astype(LOW), spread_out) * 256.0 + dot(rest.astype(LOW), spread_out) - 1.0
            own_block = block_no[0:1, :] == float(first) + lax.broadcasted_iota(
                jnp.int32, (some, lanes_at), 0
            ).astype(F32)
            named_row = named_row + jnp.sum(jnp.where(own_block, laid, 0.0), 0, keepdims=True)
        R.named[:, begin : begin + lanes_at] = jnp.broadcast_to(
            named_row.astype(jnp.int32) - dp.me * table_rows, (8, lanes_at)
        )

    once = jnp.where(mp.me == 0, 1.0, 0.0)
    lanes = lax.broadcasted_iota(jnp.int32, (1, 128), 1)
    R.sums[...] = jnp.zeros_like(R.sums)

    def put(place, squares, factor=None):
        for row, values in enumerate(squares):
            total = jnp.sum(jnp.sum(values, 0, keepdims=True), 1, keepdims=True)
            if factor is not None:
                total = total * factor
            R.sums[row : row + 1, :] += jnp.where(lanes == place, total, 0.0)

    def squares_of(weight, gradient, first, second):
        direction = direction_of(weight, gradient, first, second)[2]
        return weight * weight, direction * direction

    def folded(values):
        rows, columns = values.shape
        return jnp.sum(values.reshape(rows // 8, 8, columns), 0)

    def add_up(weight, gradient, first, second):
        squares = squares_of(weight[...], gradient[...], first[...], second[...])
        return [folded(values) for values in squares]

    for tile in range(min(2, tiles)):
        for one in tile_of(tile):
            one.start()
    zero = jnp.zeros((8, width), F32)

    rest = [
        functools.partial(scatter.pass_on, step)
        for scatter in (first_w, small)
        for step in range(1, dp.far)
    ][1:]
    tail_hooks = [
        (min(tiles - 1, 1 + place * (tiles - 1) // len(rest)), action)
        for place, action in enumerate(rest)
    ]

    def add_tile(tile, carry):
        side = lax.rem(tile, 2)
        for place, action in tail_hooks:
            pl.when(tile == place)(action)
        for one in tile_of(tile):
            one.wait()
        hit = (
            lax.broadcasted_iota(jnp.int32, (tile_rows, ways * spots), 0) + tile * tile_rows
            == R.named[0:1, :]
        )
        gradient = dot(jnp.where(hit, 1.0, 0.0).astype(LOW), R.inc[...])
        more = add_up(R.tw.at[side], gradient, R.tm.at[side], R.tv.at[side])

        @pl.when(tile + 2 < tiles)
        def _():
            for one in tile_of(tile + 2):
                one.start()

        return carry[0] + more[0], carry[1] + more[1]

    put(0, lax.fori_loop(0, tiles, add_tile, (zero, zero)), once)

    for thing in (win_all, wc, *mg, up, down, wo, small_mp, named):
        thing.drain()
    for piece in range(seqs):
        out.drain(piece)
        das.drain(piece)
    for step in range(1, size):
        back(step).wait_send()

    for name in names_of_moments:
        moment(name).wait()
    up.arrive()

    R.red_up[...] = up.total(slice(None))
    put(10, add_up(R.w_up, R.red_up, R.up_m_here, R.up_v_here))
    down.arrive()

    R.red_dn[...] = down.total(slice(None)).T
    put(11, add_up(R.w_down, R.red_dn, R.down_m_here, R.down_v_here))
    wo.arrive()
    R.red_out[...] = wo.total(slice(None)).T
    put(9, add_up(R.w_out, R.red_out, R.out_m_here, R.out_v_here))

    small.arrive()
    R.wsum[mp.me] = small.total(slice(None)).astype(LOW)
    weights_in = Gather(mp, of_index(R.wsum), R.ws_send, R.ws_recv)
    weights_in.start()
    first_w.arrive()

    value = first_w.total(slice(None))
    for part in range(3):
        R.red_qkv[part] = value[:, part * heads_w : (part + 1) * heads_w]
    weights_in.relays()
    for part in range(3):
        put(
            6 + part,
            add_up(
                R.w_qkv.at[part], R.red_qkv.at[part], R.qkv_m_here.at[part], R.qkv_v_here.at[part]
            ),
        )
    weights_in.close()
    total = jnp.concatenate([R.wsum[index].astype(F32) for index in range(ways)], 1)
    R.red_in[...] = total[:rin, :]
    put(1, add_up(R.w_in, R.red_in, R.w_in_m_here, R.w_in_v_here), once)
    if strip % 128 == 0:
        R.lnsum[...] = total[rin_up : rin_up + 8, :]
        R.red_ln[...] = R.lnsum[0:4, pl.ds(pl.multiple_of(dp.me * strip, strip), strip)]
    else:
        chosen = lax.broadcasted_iota(jnp.int32, (model, strip), 0) == dp.me * strip + (
            lax.broadcasted_iota(jnp.int32, (model, strip), 1)
        )
        R.red_ln[...] = dot(
            total[rin_up : rin_up + 8, :].astype(LOW), jnp.where(chosen, 1.0, 0.0).astype(LOW)
        )[0:4]
    squares = squares_of(R.ln_params[...], R.red_ln[...], R.ln_m_here[...], R.ln_v_here[...])
    for row in range(4):
        put(2 + row, [values[row : row + 1, :] for values in squares], once)

    R.near[dp.me] = R.sums[...]
    near, near_wait = far_copies(
        dp, lambda dest, source: (R.near.at[dp.me], R.near.at[source]), R.near_send, R.near_recv
    )
    for step in range(1, size):
        near(step).start()
    near_wait()
    R.wide[mp.me] = jnp.sum(R.near[...], 0)
    far_off, far_off_wait = far_copies(
        mp, lambda dest, source: (R.wide.at[mp.me], R.wide.at[source]), R.wide_send, R.wide_recv
    )
    for step in range(1, ways):
        far_off(step).start()
    far_off_wait()
    R.totals[...] = jnp.sum(R.wide[...], 0)

    for thing in (first_w, small, rows_in, weights_in):
        thing.drain()
    for step in range(1, size):
        near(step).wait_send()
    for step in range(1, ways):
        far_off(step).wait_send()


def run_layer(cap, ids, levels, noise, cot, weights, moments):
    table, w_in, ln_params, w_qkv, w_out, w_up, w_down = weights
    dp, mp = lax.axis_size("dp"), lax.axis_size("mp")
    seqs, seq_len = ids.shape
    tokens, width = noise.shape
    model = cot.shape[1]
    rin = w_in.shape[0]
    heads_w = w_qkv.shape[2]
    strip, hidden = w_up.shape
    group = tokens * mp
    spots = dp * cap
    wide = round_up(rin, 16) + 16
    far, far_dp = mp // 2, dp // 2
    quarter = model // mp
    in_kind = LOW if rin % 16 == 0 else F32
    tile_rows = max(rows for rows in range(8, 513, 8) if table.shape[0] % rows == 0)
    stacked = (heads_w // HD) * seq_len
    vmem = pl.BlockSpec(memory_space=pltpu.VMEM)
    outside = pl.BlockSpec(memory_space=pl.ANY)
    inputs = dict(
        ids=(ids, vmem),
        levels=(levels, pl.BlockSpec(memory_space=pltpu.SMEM)),
        noise=(noise, vmem),
        cot=(cot, vmem),
        table=(table, outside),
        w_in=(w_in, vmem),
        ln_params=(ln_params, vmem),
        w_qkv=(w_qkv, vmem),
        w_out=(w_out, vmem),
        w_up=(w_up, vmem),
        w_down=(w_down, vmem),
    )
    kept = {}
    for name, (first, second) in zip(("table", "w_in", "ln", "qkv", "out", "up", "down"), moments):
        inputs[name + "_m"] = (first, outside)
        inputs[name + "_v"] = (second, outside)
        if name != "table":
            kept[name + "_m_here"] = kept[name + "_v_here"] = (first.shape, F32)
    outputs = dict(
        out=((tokens, model), F32),
        red_up=((strip, hidden), F32),
        red_dn=((hidden, strip), F32),
        red_qkv=((3, strip, heads_w), F32),
        red_out=((heads_w, strip), F32),
        red_in=((rin, model), F32),
        red_ln=((4, strip), F32),
        inc=((mp * spots, width), LOW),
        named=((8, mp * spots), jnp.int32),
        totals=((8, 128), F32),
    )
    buffers = dict(
        tab=((2, round_up(table.shape[0] // 8, 128), width), F32),
        ask=((dp, 8, 128), F32),
        idx=((mp, dp, 8, 128), F32),
        loc=((spots, 128), jnp.int32),
        give=((spots, width), LOW),
        got=((spots, width), LOW),
        tw=((2, tile_rows, width), F32),
        tm=((2, tile_rows, width), F32),
        tv=((2, tile_rows, width), F32),
        sums=((8, 128), F32),
        near=((dp, 8, 128), F32),
        wide=((mp, 8, 128), F32),
        scores=((2, stacked, seq_len), F32),
        dprobs=((2, stacked, seq_len), F32),
        probs=((2, stacked, seq_len), LOW),
        dscores=((2, stacked, seq_len), LOW),
        upper=((2, stacked, heads_w), LOW),
        gwo=((model, heads_w), LOW),
        wo_first=((far_dp * strip, heads_w), LOW),
        wo_second=((far_dp * strip, heads_w), LOW),
        gains=((8, model), F32),
        lnsum=((8, model), F32),
        sig=((tokens, 1), F32),
        pick=((tokens, spots), LOW),
        rows=((tokens, width), LOW),
        mixed=((tokens, width), LOW),
        x0=((tokens, model), F32),
        a=((group, model), LOW),
        c=((group, model), LOW),
        dx=((seqs, group // seqs, model), LOW),
        dmid=((tokens, model), F32),
        dmid_all=((group, model), LOW),
        winf=((mp, rin * dp, quarter), in_kind),
        waf=((model, 4 * heads_w), LOW),
        wbf=((model, hidden), LOW),
        wcf=((model, hidden), LOW),
        qkv=((group, 3 * heads_w), LOW),
        o=((group, heads_w), LOW),
        low=((group // seqs, heads_w), LOW),
        part=((group, model), LOW),
        first=((far * tokens, model), LOW),
        fold=((far * tokens, model), LOW),
        second=((far * tokens, model), LOW),
        fold_far=((far * tokens, model), LOW),
        h=((group // seqs, min(256, hidden)), F32),
        hb=((group, hidden), LOW),
        dhb=((group, hidden), LOW),
        slope=((group, hidden), LOW),
        gdn=((model, hidden), LOW),
        dx0=((tokens, model), LOW),
        norms=((8, model), F32),
        gm=((mp, width + 16, quarter), LOW),
        gm_first=((far, width + 16, quarter), LOW),
        gm_second=((far, width + 16, quarter), LOW),
        gw=((dp, wide, quarter), LOW),
        gw_first=((far_dp, wide, quarter), LOW),
        gw_second=((far_dp, wide, quarter), LOW),
        up_first=((far_dp * strip, hidden), LOW),
        up_second=((far_dp * strip, hidden), LOW),
        dn_first=((far_dp * strip, hidden), LOW),
        dn_second=((far_dp * strip, hidden), LOW),
        wa_first=((far_dp * strip, 3 * heads_w), LOW),
        wa_second=((far_dp * strip, 3 * heads_w), LOW),
        wsum=((mp, wide, quarter), LOW),
        up_extra=((strip, hidden), LOW),
        dn_extra=((strip, hidden), LOW),
        wa_extra=((strip, 3 * heads_w), LOW),
        wo_extra=((strip, heads_w), LOW),
        gw_extra=((wide, quarter), LOW),
        **kept,
    )
    sems = dict(tab_sem=2, tile_sem=6, moment_sem=12)
    for name in (
        *("win", "wa", "wx", "wb", "wc", "ask", "give", "back"),
        *("up", "dn", "ga", "wo", "gw", "near"),
    ):
        sems[name + "_send"] = sems[name + "_recv"] = dp + 1
    for name in ("wim", "id", "in", "ws", "gm", "wide"):
        sems[name + "_send"] = sems[name + "_recv"] = mp
    for name in ("dx", "a", "c", "e"):
        sems[name + "_send"] = sems[name + "_recv"] = 2 * seqs * mp
    for name in ("as", "os", "cs", "ds"):
        sems[name + "_send"] = sems[name + "_recv"] = seqs * mp * (model // min(256, model))
    names = [*inputs, *outputs, *buffers, *sems]
    made = pl.pallas_call(
        functools.partial(layer_kernel, cap, names),
        out_shape=[jax.ShapeDtypeStruct(shape, kind) for shape, kind in outputs.values()],
        in_specs=[spec for _, spec in inputs.values()],
        out_specs=[vmem] * len(outputs),
        scratch_shapes=[
            *[pltpu.VMEM(shape, kind) for shape, kind in buffers.values()],
            *[pltpu.SemaphoreType.DMA((number,)) for number in sems.values()],
        ],
        compiler_params=pltpu.CompilerParams(
            vmem_limit_bytes=VMEM_BYTES, collective_id=1, has_side_effects=True
        ),
        name="layer",
    )(*[value for value, _ in inputs.values()])
    return dict(zip(outputs, made))


def direction_of(weight, gradient, first, second):
    first_new = BETA_ONE * first + (1.0 - BETA_ONE) * gradient
    second_new = BETA_TWO * second + (1.0 - BETA_TWO) * gradient * gradient
    second_hat = second_new * (1.0 / (1.0 - BETA_TWO**STEP))
    inverse = lax.rsqrt(second_hat)
    root = second_hat * inverse + EPS_ADAM
    inverse = inverse * (2.0 - root * inverse)
    inverse = inverse * (2.0 - root * inverse)
    direction = first_new * (1.0 / (1.0 - BETA_ONE**STEP)) * inverse + DECAY * weight
    return first_new, second_new, direction


def update_kernel(part, names, *refs):
    R = types.SimpleNamespace(**dict(zip(names, refs)))
    turn = pl.program_id(0)
    R.out_rows[...] = R.made[...]
    norms = jnp.sqrt(R.totals[...])
    R.norms[...] = norms[0:2, 0:12]
    factors = norms[0:1, :] / (norms[1:2, :] + EPS_ADAM) * RATE

    def piece(name, here, gradient, place, rows=slice(None)):
        weight = getattr(R, name)[here]
        first_new, second_new, direction = direction_of(
            weight, gradient, getattr(R, name + "_m")[here], getattr(R, name + "_v")[here]
        )
        if isinstance(place, int):
            factor = factors[0:1, place : place + 1]
        else:
            factor = jnp.concatenate([factors[0:1, one : one + 1] for one in place], 0)
        getattr(R, name + "_m_new")[here] = first_new
        getattr(R, name + "_v_new")[here] = second_new
        getattr(R, name + "_new")[here] = weight - factor * direction

    def update(name, gradient, place, lead=(), here=slice(None)):
        piece(name, (*lead, here, slice(None)), gradient, place)

    tile = R.table.shape[0]
    spots = R.named.shape[1]

    def table_part(row):
        hit = (
            lax.broadcasted_iota(jnp.int32, (part, spots), 0) + (turn * tile + row)
            == R.named[0:1, :]
        )
        gradient = dot(jnp.where(hit, 1.0, 0.0).astype(LOW), R.inc[...])
        update("table", gradient, 0, (), pl.ds(row, part))

    strips(tile, part, table_part)
    for group in range(3):
        update("qkv", R.red_qkv[group], 6 + group, (group,))
    update("up", R.red_up[...], 10)
    update("down", R.red_dn[...], 11)

    @pl.when(turn == 0)
    def _():
        update("out", R.red_out[...], 9)
        update("w_in", R.red_in[...], 1)
        piece("ln", (slice(None), slice(None)), R.red_ln[...], (2, 3, 4, 5))


def turns_of(rows, parts):
    return [
        turns
        for turns in (5, 4, 2, 1)
        if rows % (8 * turns) == 0 and all(size % (8 * turns) == 0 for size in parts)
    ][0]


def run_update(weights, moments, grads):
    names = ("table", "w_in", "ln", "qkv", "out", "up", "down")
    by_name = dict(zip(names, weights))
    rows, width = by_name["table"].shape
    strip, hidden = by_name["up"].shape
    heads_w = by_name["qkv"].shape[2]
    turns = turns_of(rows, (strip, hidden))
    tile = rows // turns
    part = max(size for size in range(8, 257, 8) if tile % size == 0)
    fixed = lambda array: pl.BlockSpec(array.shape, lambda turn: (0,) * array.ndim)
    specs = dict(
        table=pl.BlockSpec((tile, width), lambda turn: (turn, 0)),
        w_in=fixed(by_name["w_in"]),
        ln=fixed(by_name["ln"]),
        qkv=pl.BlockSpec((3, strip // turns, heads_w), lambda turn: (0, turn, 0)),
        out=fixed(by_name["out"]),
        up=pl.BlockSpec((strip // turns, hidden), lambda turn: (turn, 0)),
        down=pl.BlockSpec((hidden // turns, strip), lambda turn: (turn, 0)),
    )
    inputs = {}
    for name, weight, (first, second) in zip(names, weights, moments):
        inputs[name] = (weight, specs[name])
        inputs[name + "_m"] = (first, specs[name])
        inputs[name + "_v"] = (second, specs[name])
    for name, like in (
        ("red_up", "up"),
        ("red_dn", "down"),
        ("red_qkv", "qkv"),
        ("red_out", "out"),
        ("red_in", "w_in"),
        ("red_ln", "ln"),
    ):
        inputs[name] = (grads[name], specs[like])
    for name in ("inc", "named", "totals"):
        inputs[name] = (grads[name], fixed(grads[name]))
    tokens, model = grads["out"].shape
    rows_spec = pl.BlockSpec((tokens // turns, model), lambda turn: (turn, 0))
    inputs["made"] = (grads["out"], rows_spec)
    outputs = {"out_rows": (grads["out"].shape, rows_spec)}
    for name, weight in by_name.items():
        for kind in ("_new", "_m_new", "_v_new"):
            outputs[name + kind] = (weight.shape, specs[name])
    outputs["norms"] = ((2, 12), pl.BlockSpec((2, 12), lambda turn: (0, 0)))
    results = pl.pallas_call(
        functools.partial(update_kernel, part, [*inputs, *outputs]),
        grid=(turns,),
        out_shape=[jax.ShapeDtypeStruct(shape, F32) for shape, _ in outputs.values()],
        in_specs=[spec for _, spec in inputs.values()],
        out_specs=[spec for _, spec in outputs.values()],
        compiler_params=pltpu.CompilerParams(vmem_limit_bytes=VMEM_BYTES),
        name="update",
    )(*[value for value, _ in inputs.values()])
    return list(results)


def per_device(
    token_ids,
    levels,
    noise,
    cotangent,
    table,
    table_m,
    table_v,
    w_in,
    w_in_m,
    w_in_v,
    ln_params,
    ln_m,
    ln_v,
    w_qkv,
    qkv_m,
    qkv_v,
    w_out,
    out_m,
    out_v,
    w_up,
    up_m,
    up_v,
    w_down,
    down_m,
    down_v,
):
    dp_count = lax.axis_size("dp")
    seq_count, seq_len = token_ids.shape
    tokens = seq_count * seq_len
    model = cotangent.shape[2]
    cap = round_up(max(2, (3 * tokens + 2 * dp_count - 1) // (2 * dp_count)), 16)
    weights = (table, w_in, ln_params, w_qkv, w_out, w_up, w_down)
    moments = (
        (table_m, table_v),
        (w_in_m, w_in_v),
        (ln_m, ln_v),
        (qkv_m, qkv_v),
        (out_m, out_v),
        (up_m, up_v),
        (down_m, down_v),
    )
    grads = run_layer(
        cap,
        token_ids,
        levels,
        noise.reshape(tokens, -1),
        cotangent.reshape(tokens, model),
        weights,
        moments,
    )
    out, *results = run_update(weights, moments, grads)
    return (out.reshape(seq_count, seq_len, model), *results)


def solution(mesh):
    return jax.shard_map(
        per_device,
        mesh=mesh,
        in_specs=(
            P(("dp", "mp"), None),
            P(("dp", "mp")),
            P(("dp", "mp"), None, None),
            P(("dp", "mp"), None, None),
            P("dp", None),
            P("dp", None),
            P("dp", None),
            P("dp", None),
            P("dp", None),
            P("dp", None),
            P(None, "dp"),
            P(None, "dp"),
            P(None, "dp"),
            P(None, "dp", "mp"),
            P(None, "dp", "mp"),
            P(None, "dp", "mp"),
            P("mp", "dp"),
            P("mp", "dp"),
            P("mp", "dp"),
            P("dp", "mp"),
            P("dp", "mp"),
            P("dp", "mp"),
            P("mp", "dp"),
            P("mp", "dp"),
            P("mp", "dp"),
        ),
        out_specs=(
            P(("dp", "mp"), None, None),
            P("dp", None),
            P("dp", None),
            P("dp", None),
            P("dp", None),
            P("dp", None),
            P("dp", None),
            P(None, "dp"),
            P(None, "dp"),
            P(None, "dp"),
            P(None, "dp", "mp"),
            P(None, "dp", "mp"),
            P(None, "dp", "mp"),
            P("mp", "dp"),
            P("mp", "dp"),
            P("mp", "dp"),
            P("dp", "mp"),
            P("dp", "mp"),
            P("dp", "mp"),
            P("mp", "dp"),
            P("mp", "dp"),
            P("mp", "dp"),
            P(),
        ),
        check_vma=False,
    )
```

```python
import functools
import types

import jax
import jax.numpy as jnp
from jax import lax
from jax.experimental import pallas as pl
from jax.experimental.pallas import tpu as pltpu
from jax.sharding import PartitionSpec as P

HD = 64
LEVELS = 64
STEP = 10


EPS_NORM = 1e-06
EPS_LAYER = 1e-05
EPS_ADAM = 1e-06
BETA_ONE = 0.9
BETA_TWO = 0.999
DECAY = 0.01
RATE = 0.5
SIGMA_TOP = 10.0

F32 = jnp.float32
LOW = jnp.bfloat16
VMEM_BYTES = 63 * 1024 * 1024


def sigma_of(levels):
    frac = levels.astype(jnp.float32) / (LEVELS - 1)
    return jnp.exp(frac * jnp.log(SIGMA_TOP))


def lamb_moments(weight, gradient, first, second):
    first_new = BETA_ONE * first + (1.0 - BETA_ONE) * gradient
    second_new = BETA_TWO * second + (1.0 - BETA_TWO) * gradient * gradient
    first_hat = first_new / (1.0 - BETA_ONE**STEP)
    second_hat = second_new / (1.0 - BETA_TWO**STEP)
    direction = first_hat / (jnp.sqrt(second_hat) + EPS_ADAM) + DECAY * weight
    return (first_new, second_new, direction)


def trust_factors(ratio):
    return (
        ratio[0],
        ratio[1],
        ratio[2:6][:, None],
        ratio[6:9][:, None, None],
        ratio[9],
        ratio[10],
        ratio[11],
    )


def round_up(value, step):
    return -(-value // step) * step


def dot(left, right):
    return jnp.dot(left, right, preferred_element_type=F32)


def dot_nt(left, right):
    return lax.dot_general(left, right, (((1,), (1,)), ((), ())), preferred_element_type=F32)


def dot_tn(left, right):
    return lax.dot_general(left, right, (((0,), (0,)), ((), ())), preferred_element_type=F32)


def strips(total, step, body, unroll=1):
    step = min(step, total)

    def one(turn, carry):
        body(pl.multiple_of(turn * step, step))
        return carry

    lax.fori_loop(0, total // step, one, 0, unroll=unroll)


class Line:
    def __init__(self, axis):
        self.axis = axis
        self.size = lax.axis_size(axis)
        self.far = self.size // 2
        self.me = lax.axis_index(axis)
        self.hi = lax.div(self.me, 2)
        self.lo = lax.rem(self.me, 2)
        self.partner = self.hi * 2 + (1 - self.lo)

    def at(self, step):
        return lax.rem(self.hi + step + self.far, self.far)

    def push(self, index, src, dst, send, recv):
        return pltpu.make_async_remote_copy(
            src_ref=src,
            dst_ref=dst,
            send_sem=send,
            recv_sem=recv,
            device_id={self.axis: index},
            device_id_type=pl.DeviceIdType.MESH,
        )

    def signal(self, sem, index):
        pl.semaphore_signal(
            sem, inc=1, device_id={self.axis: index}, device_id_type=pl.DeviceIdType.MESH
        )


def meet(pair_lines, all_lines=()):
    sem = pltpu.get_barrier_semaphore()
    count = 0
    for line in pair_lines:
        for step in range(1, line.far):
            line.signal(sem, line.at(step) * 2 + line.lo)
            count += 1
        line.signal(sem, line.partner)
        count += 1
    for line in all_lines:
        for step in range(1, line.size):
            line.signal(sem, lax.rem(line.me + step, line.size))
            count += 1
    pl.semaphore_wait(sem, count)


class Gather:
    def __init__(self, line, at, send, recv, base=0, ends=False):
        self.line, self.at, self.send, self.recv, self.base = line, at, send, recv, base
        self.ends = ends and line.far == 4

    def source(self, step):
        line = self.line
        if not self.ends:
            return line.at(-step)
        order = ((1, 2, 3), (0, 3, 2), (3, 0, 1), (2, 1, 0))
        hi = order[3][step - 1]
        for place in (2, 1, 0):
            hi = jnp.where(line.hi == place, order[place][step - 1], hi)
        return hi

    def far_sends(self, act):
        line = self.line
        for step in range(1, line.far):
            one = self.copy(line.me, step - 1, line.at(step) * 2 + line.lo)
            if self.ends and step != 2:
                pl.when(line.hi != (3 if step == 1 else 0))(functools.partial(act, one))
            else:
                act(one)

    def to_end(self, act):
        line = self.line
        dest = jnp.where(line.hi == 1, 0, 3)
        one = self.copy((3 - dest) * 2 + line.lo, 2 * line.far - 1, dest * 2 + line.lo)
        pl.when((line.hi == 1) | (line.hi == 2))(functools.partial(act, one))

    def copy(self, index, slot, dest):
        block = self.at(index)
        return self.line.push(
            dest, block, block, self.send.at[self.base + slot], self.recv.at[self.base + index]
        )

    def start_far(self):
        self.far_sends(lambda one: one.start())

    def start_near(self):
        self.copy(self.line.me, self.line.far - 1, self.line.partner).start()

    def start(self):
        self.start_far()
        self.start_near()

    def relay(self, step):
        line = self.line
        handed = self.copy(self.source(step) * 2 + line.lo, line.far - 1 + step, line.partner)
        handed.wait_recv()
        if self.ends and step == 2:
            self.to_end(lambda one: one.start())
        handed.start()

    def relays(self):
        for step in range(1, self.line.far):
            self.relay(step)

    def close(self):
        line = self.line
        for step in range(line.far):
            self.copy(line.at(-step) * 2 + (1 - line.lo), 0, line.partner).wait_recv()

    def drain(self):
        self.far_sends(lambda one: one.wait_send())
        if self.ends:
            self.to_end(lambda one: one.wait_send())
        for slot in range(self.line.far - 1, 2 * self.line.far - 1):
            self.copy(self.line.me, slot, self.line.partner).wait_send()


class Scatter:
    def __init__(self, line, part, first, second, send, recv, base=0, extra=None):
        self.line, self.part, self.first, self.second = line, part, first, second
        self.send, self.recv, self.base = send, recv, base
        self.extra = extra if line.far == 4 else None

    def clear(self):
        line = self.line
        if self.extra is not None:

            @pl.when((line.hi == 0) | (line.hi == 3))
            def _():
                slot = self.second(3 - line.hi)
                slot[...] = jnp.zeros(slot.shape, LOW)

    def order(self, step):
        line = self.line
        if self.extra is None:
            return line.at(step)
        table = ((3, 2, 1), (2, 0, 3), (1, 3, 0), (0, 1, 2))
        hi = table[3][step - 1]
        for place in (2, 1, 0):
            hi = jnp.where(line.hi == place, table[place][step - 1], hi)
        return hi

    def traded(self, hi):
        line = self.line
        return line.push(
            line.partner,
            self.part(hi * 2 + (1 - line.lo)),
            self.first(hi),
            self.send.at[self.base + hi],
            self.recv.at[self.base + hi],
        )

    def passed(self, step):
        line = self.line
        hi = self.order(step)
        return line.push(
            hi * 2 + line.lo,
            self.part(hi * 2 + line.lo),
            self.second(line.hi),
            self.send.at[self.base + line.far + step - 1],
            self.recv.at[self.base + line.far + line.hi],
        )

    def to_next(self):
        line = self.line
        return line.push(
            jnp.where(line.hi < 2, 1, 2) * 2 + line.lo,
            self.part((3 - jnp.where(line.hi < 2, 0, 3)) * 2 + line.lo),
            self.extra,
            self.send.at[self.base + line.far],
            self.recv.at[self.base + 2 * line.far],
        )

    def turn_of(self, turn):
        line = self.line
        if self.extra is None:
            return lax.rem(line.hi + turn + 1, line.far)
        hi = line.hi
        for step in range(1, line.far):
            hi = jnp.where(turn == step - 1, self.order(step), hi)
        return hi

    def is_end(self):
        return (self.line.hi == 0) | (self.line.hi == 3)

    def trade(self, hi):
        self.traded(hi).start()

    def trade_all(self):
        for step in range(1, self.line.far + 1):
            self.trade(self.order(step) if step < self.line.far else self.line.hi)

    def pass_on(self, step):
        line = self.line
        hi = self.order(step)
        self.traded(hi).wait_recv()
        mine, other = self.part(hi * 2 + line.lo), self.first(hi)
        if self.extra is None or step == 2:
            mine[...] = (mine[...].astype(F32) + other[...].astype(F32)).astype(LOW)
            self.passed(step).start()
        elif step == 1:
            mine[...] = (mine[...].astype(F32) + other[...].astype(F32)).astype(LOW)

            @pl.when(self.is_end())
            def _():
                self.to_next().start()

            @pl.when(jnp.logical_not(self.is_end()))
            def _():
                self.passed(step).start()
        else:

            @pl.when(self.is_end())
            def _():
                mine[...] = (mine[...].astype(F32) + other[...].astype(F32)).astype(LOW)

            @pl.when(jnp.logical_not(self.is_end()))
            def _():
                line.push(
                    line.partner,
                    self.extra,
                    self.extra,
                    self.send.at[self.base],
                    self.recv.at[self.base + 2 * line.far],
                ).wait_recv()
                mine[...] = (
                    mine[...].astype(F32) + other[...].astype(F32) + self.extra[...].astype(F32)
                ).astype(LOW)

            self.passed(step).start()

    def arrive(self):
        line = self.line
        self.traded(line.hi).wait_recv()
        for step in range(1, line.far):
            hi = line.at(-step)
            one = line.push(
                line.partner,
                self.second(hi),
                self.second(hi),
                self.send.at[self.base],
                self.recv.at[self.base + line.far + hi],
            )
            if self.extra is None:
                one.wait_recv()
            else:
                pl.when(jnp.logical_not(self.is_end()) | (hi + line.hi != 3))(one.wait_recv)

    def total(self, here):
        line = self.line
        value = self.part(line.me)[here, :].astype(F32) + self.first(line.hi)[here, :].astype(F32)
        for step in range(1, line.far):
            value = value + self.second(line.at(-step))[here, :].astype(F32)
        return value

    def drain(self):
        line = self.line
        for step in range(line.far):
            self.traded(line.at(step)).wait_send()
        for step in range(1, line.far):
            if self.extra is not None and step == 1:
                pl.when(self.is_end())(lambda: self.to_next().wait_send())
                pl.when(jnp.logical_not(self.is_end()))(lambda: self.passed(1).wait_send())
            else:
                self.passed(step).wait_send()


def block_rows(ref, rows, first=0):
    return lambda index: ref.at[pl.ds(pl.multiple_of((index + first) * rows, rows), rows)]


def part_rows(ref, rows, first, count):
    return lambda index: ref.at[pl.ds(pl.multiple_of(index * rows + first, count), count)]


def of_index(ref):
    return lambda index: ref.at[index]


def norm_rows(values):
    center = values - jnp.mean(values, -1, keepdims=True)
    spread = jnp.mean(center * center, -1, keepdims=True)
    inverse = lax.rsqrt(spread + EPS_LAYER)
    return center * inverse, inverse


def norm_back(values, gain, grad):
    unit, inverse = norm_rows(values)
    inner = grad * gain
    shared = jnp.mean(inner, -1, keepdims=True)
    along = jnp.mean(inner * unit, -1, keepdims=True)
    return inverse * (inner - shared - unit * along), unit


def head_masks(width):
    lane = lax.broadcasted_iota(jnp.int32, (1, width), 1)
    return [
        jnp.where((lane >= head * HD) & (lane < (head + 1) * HD), 1.0, 0.0)
        for head in range(width // HD)
    ]


def spread_heads(values, masks):
    return jnp.concatenate([values * mask.astype(LOW) for mask in masks], 0)


def join_heads(values, masks, rows):
    total = values[0:rows] * masks[0]
    for head in range(1, len(masks)):
        total = total + values[head * rows : (head + 1) * rows] * masks[head]
    return total


TAIL = (
    0.2256758632450557,
    0.22566952478278277,
    0.2078438574180613,
    0.16853390514724884,
    0.14146086231844687,
    -0.005667717379728321,
    0.16915486959066833,
    -0.18294364197603524,
    0.05027260226320005,
)


def normal_tail(size, bell):
    base = 1.0 + (0.4 * 0.5**0.5) * size
    t = pl.reciprocal(base, approx=True)
    t = t * (2.0 - base * t)
    t = t * (2.0 - base * t)
    value = jnp.full_like(t, 0.5 * TAIL[-1])
    for factor in TAIL[-2::-1]:
        value = value * t + 0.5 * factor
    return value * t * bell


def far_copies(line, make, sends, recvs):
    def copy(step):
        dest = lax.rem(line.me + step, line.size)
        src, dst = make(dest, line.me)
        return line.push(dest, src, dst, sends.at[step], recvs.at[line.me])

    def wait():
        for step in range(1, line.size):
            source = lax.rem(line.me + line.size - step, line.size)
            _, dst = make(source, source)
            line.push(line.partner, dst, dst, sends.at[0], recvs.at[source]).wait_recv()

    return copy, wait


def layer_kernel(cap, names, *refs):
    R = types.SimpleNamespace(**dict(zip(names, refs)))
    dp, mp = Line("dp"), Line("mp")
    size, ways = dp.size, mp.size
    seqs, seq_len = R.ids.shape
    tokens, width = R.noise.shape
    model = R.cot.shape[1]
    heads_w = R.o.shape[1]
    hidden = R.wbf.shape[1]
    table_rows = R.table.shape[0]
    rin = R.w_in.shape[0]
    rin_up = round_up(rin, 16)
    quarter = model // ways
    strip = R.w_up.shape[0]
    spots = size * cap
    far = mp.far
    count = seqs * far
    own_strip = pl.ds(pl.multiple_of(dp.me * strip, strip), strip)
    mine = pl.ds(pl.multiple_of(dp.me * cap, cap), cap)

    some_rows = seq_len // 2

    def rows_of(piece):
        return lambda row: pl.ds(pl.multiple_of(piece * seq_len + row, some_rows), some_rows)

    def own_rows(piece):
        first = pl.multiple_of((piece * ways + mp.me) * seq_len, seq_len)
        return lambda row: pl.ds(pl.multiple_of(first + row, some_rows), some_rows)

    def by_rows(body, after=lambda half: None):
        for half in range(2):
            body(half * some_rows)
            after(half)

    class Rows:
        def __init__(self, ref, send, recv, piece):
            self.parts = [
                Gather(
                    mp,
                    lambda index, half=half: ref.at[
                        pl.ds(
                            pl.multiple_of(
                                (piece * ways + index) * seq_len + half * some_rows, some_rows
                            ),
                            some_rows,
                        )
                    ],
                    send,
                    recv,
                    (2 * piece + half) * ways,
                )
                for half in range(2)
            ]

        def start(self, half):
            self.parts[half].start()

        def relays(self):
            for part in self.parts:
                part.relays()

        def close(self):
            for part in self.parts:
                part.close()

        def drain(self):
            for part in self.parts:
                part.drain()

    def halves(ref, send, recv):
        return [Rows(ref, send, recv, piece) for piece in range(seqs)]

    chunk_cols = min(256, model)
    chunk_count = model // chunk_cols

    class Sums:
        def __init__(self, *refs):
            *self.refs, self.send, self.recv = refs

        def chunk(self, piece, chunk):
            cols = pl.ds(pl.multiple_of(chunk * chunk_cols, chunk_cols), chunk_cols)

            def blocks(ref, first):
                return lambda index: ref.at[
                    pl.ds(pl.multiple_of((index + first) * seq_len, seq_len), seq_len), cols
                ]

            firsts = (piece * ways, piece * far, piece * far)
            views = [blocks(ref, first) for ref, first in zip(self.refs, firsts)]
            return Scatter(mp, *views, self.send, self.recv, (piece * chunk_count + chunk) * ways)

        def total(self, piece, here):
            firsts = (piece * ways, piece * far, piece * far)
            views = [block_rows(ref, seq_len, first) for ref, first in zip(self.refs, firsts)]
            return Scatter(mp, *views, self.send, self.recv).total(here)

        def trade(self, piece, chunk):
            self.chunk(piece, chunk).trade_all()

        def hand_on(self, piece, chunk):
            scatter = self.chunk(piece, chunk)
            for step in range(1, far):
                scatter.pass_on(step)

        def every(self, act):
            def one(chunk, carry):
                act(chunk)
                return carry

            lax.fori_loop(0, chunk_count, one, 0)

        def hand_on_all(self, piece):
            self.every(lambda chunk: self.hand_on(piece, chunk))

        def arrive(self, piece):
            self.every(lambda chunk: self.chunk(piece, chunk).arrive())

        def drain(self, piece):
            self.every(lambda chunk: self.chunk(piece, chunk).drain())

        def products(self, piece, make):
            def one(chunk, carry):
                make(pl.ds(pl.multiple_of(chunk * chunk_cols, chunk_cols), chunk_cols))
                self.trade(piece, chunk)
                pl.when(chunk > 0)(lambda: self.hand_on(piece, chunk - 1))
                return carry

            lax.fori_loop(0, chunk_count, one, 0)

        def hand_on_last(self, piece):
            self.hand_on(piece, chunk_count - 1)

    many = ways * seq_len

    def turns(body, hooks=()):
        def one(piece, carry):
            def at(point):
                for place, when, action in hooks:
                    if when == point:
                        pl.when(piece == place)(action)

            base = pl.multiple_of(piece * many, many)
            body(piece, base, pl.ds(base, many), at)
            return carry

        lax.fori_loop(0, seqs, one, 0)

    def pairs(base, body):
        def one(pair, carry):
            first = pl.multiple_of(base + pair * (2 * seq_len), 2 * seq_len)
            body([pl.ds(pl.multiple_of(first + seq * seq_len, seq_len), seq_len) for seq in range(2)])
            return carry

        lax.fori_loop(0, far, one, 0)

    def chunks(total, body):
        step = min(256, total)
        lax.fori_loop(
            0,
            total // step,
            lambda turn, carry: (body(pl.ds(pl.multiple_of(turn * step, step), step)), carry)[1],
            0,
        )

    def later_pieces(gathers, point):
        hooks = []
        for piece in range(1, seqs):
            hooks.append((piece - 1, point, gathers[piece].relays))
            hooks.append((piece, "start", gathers[piece].close))
        return hooks

    chunk = R.tab.shape[1]
    pieces = -(-table_rows // chunk)

    def fetch(piece):
        rows = min(chunk, table_rows - piece * chunk)
        return pltpu.make_async_copy(
            R.table.at[pl.ds(piece * chunk, rows)],
            R.tab.at[piece % 2, pl.ds(0, rows)],
            R.tab_sem.at[piece % 2],
        )

    for piece in range(min(2, pieces)):
        fetch(piece).start()

    names_of_moments = [
        name + kind for name in ("w_in", "ln", "qkv", "out", "up", "down") for kind in ("_m", "_v")
    ]

    def moment(name):
        return pltpu.make_async_copy(
            getattr(R, name), getattr(R, name + "_here"), R.moment_sem.at[names_of_moments.index(name)]
        )

    tile_rows = R.tw.shape[1]
    tiles = table_rows // tile_rows

    def tile_of(tile):
        side = lax.rem(tile, 2)
        rows = pl.ds(pl.multiple_of(tile * tile_rows, tile_rows), tile_rows)
        return [
            pltpu.make_async_copy(source.at[rows], dest.at[side], R.tile_sem.at[2 * place + side])
            for place, (source, dest) in enumerate(
                ((R.table, R.tw), (R.table_m, R.tm), (R.table_v, R.tv))
            )
        ]

    eye = lax.broadcasted_iota(jnp.int32, (seq_len, seq_len), 0) == lax.broadcasted_iota(
        jnp.int32, (seq_len, seq_len), 1
    )
    id_rows = R.ids[...].astype(F32)
    ids = jnp.concatenate(
        [
            jnp.sum(jnp.where(eye, id_rows[seq : seq + 1, :], 0.0), 1, keepdims=True)
            for seq in range(seqs)
        ],
        0,
    )
    lane = lax.broadcasted_iota(jnp.int32, (tokens, 128), 1).astype(F32)
    low_end = lane * float(table_rows)
    owned = jnp.where((ids >= low_end) & (ids < low_end + float(table_rows)), 1.0, 0.0)
    before = jnp.where(
        lax.broadcasted_iota(jnp.int32, (tokens, tokens), 0)
        >= lax.broadcasted_iota(jnp.int32, (tokens, tokens), 1),
        1.0,
        0.0,
    )
    ranks = dot(before.astype(LOW), owned.astype(LOW))
    rank = jnp.sum(owned * ranks, 1, keepdims=True) - 1.0
    slot = jnp.sum(owned * lane, 1, keepdims=True) * cap + rank
    placed = jnp.where(lane == rank, 1.0, 0.0)
    upper = jnp.floor(ids * (1.0 / 256.0))
    lower = ids - upper * 256.0
    parts = jnp.concatenate([placed * upper, placed * lower, placed], 1).astype(LOW)
    asked = dot_tn(owned.astype(LOW), parts)
    asked = asked[:, :128] * 256.0 + asked[:, 128:256] + asked[:, 256:] - 1.0
    wide_ln = R.ln_params.shape[1]
    shares = R.ln_params[...].astype(LOW).astype(F32)
    if wide_ln < 128:
        shares = jnp.concatenate([shares, jnp.zeros((4, 128 - wide_ln), F32)], 1)
    for index in range(size):
        R.ask[index] = jnp.concatenate(
            [asked[index : index + 1, :], shares, jnp.zeros((3, 128), F32)], 0
        )
    R.idx[mp.me, dp.me] = R.ask[dp.me]

    def spread(part, first, second, extra, send, recv):
        blocks = [block_rows(ref, strip) for ref in (part, first, second)]
        return Scatter(dp, *blocks, send, recv, 0, extra)

    up = spread(R.wbf, R.up_first, R.up_second, R.up_extra, R.up_send, R.up_recv)
    down = spread(R.gdn, R.dn_first, R.dn_second, R.dn_extra, R.dn_send, R.dn_recv)
    first_w = spread(
        R.waf.at[:, : 3 * heads_w], R.wa_first, R.wa_second, R.wa_extra, R.ga_send, R.ga_recv
    )
    wo = spread(R.gwo, R.wo_first, R.wo_second, R.wo_extra, R.wo_send, R.wo_recv)
    small = Scatter(
        dp,
        *[of_index(ref) for ref in (R.gw, R.gw_first, R.gw_second)],
        R.gw_send,
        R.gw_recv,
        0,
        R.gw_extra,
    )
    for scatter in (up, down, first_w, wo, small):
        scatter.clear()

    meet([mp], [dp])
    ask, ask_wait = far_copies(
        dp,
        lambda dest, source: (R.ask.at[dest], R.idx.at[mp.me, source]),
        R.ask_send,
        R.ask_recv,
    )
    for step in range(1, size):
        ask(step).start()

    mine_in = R.winf.at[mp.me]
    win = Gather(dp, block_rows(mine_in, rin), R.win_send, R.win_recv, 0, True)
    win_all = Gather(mp, of_index(R.winf), R.wim_send, R.wim_recv)
    half_strip = strip // 2
    wa = [
        Gather(dp, part_rows(R.waf, strip, piece * half_strip, half_strip), send, recv, 0, True)
        for piece, (send, recv) in enumerate(((R.wa_send, R.wa_recv), (R.wx_send, R.wx_recv)))
    ]
    wb = Gather(dp, block_rows(R.wbf, strip), R.wb_send, R.wb_recv, 0, True)
    wc = Gather(dp, block_rows(R.wcf, strip), R.wc_send, R.wc_recv, 0, True)
    dxg = Gather(
        mp,
        lambda index: R.dx.at[:, pl.ds(pl.multiple_of(index * seq_len, seq_len), seq_len)],
        R.dx_send,
        R.dx_recv,
    )
    ag = halves(R.a, R.a_send, R.a_recv)
    cg = halves(R.c, R.c_send, R.c_recv)
    mg = halves(R.dmid_all, R.e_send, R.e_recv)

    mine_in[pl.ds(pl.multiple_of(dp.me * rin, rin), rin), :] = (
        R.w_in[:, pl.ds(pl.multiple_of(mp.me * quarter, quarter), quarter)]
        .astype(LOW)
        .astype(R.winf.dtype)
    )
    win.start()
    for part in range(3):
        R.waf[own_strip, part * heads_w : (part + 1) * heads_w] = R.w_qkv[part].astype(LOW)
    R.waf[own_strip, 3 * heads_w :] = R.w_out[...].T.astype(LOW)
    wa[0].start()
    wa[1].start_near()
    for name in names_of_moments:
        moment(name).start()

    for seq in range(seqs):
        level = jnp.full((seq_len, 1), R.levels[seq], jnp.int32).astype(F32) / (LEVELS - 1)
        R.sig[seq * seq_len : (seq + 1) * seq_len, :] = jnp.exp(level * jnp.log(SIGMA_TOP))

    def scale_at(here):
        sig = R.sig[here, :]
        return sig * lax.rsqrt(1.0 + sig * sig)

    for piece in range(seqs):
        here = rows_of(piece)

        def scale_cot(row, here=here, piece=piece):
            there = pl.ds(pl.multiple_of(mp.me * seq_len + row, some_rows), some_rows)
            R.dx[piece, there, :] = (R.cot[here(row), :].astype(F32) * scale_at(here(row))).astype(LOW)

        by_rows(scale_cot)
    dxg.start()
    R.wbf[own_strip, :] = R.w_up[...].astype(LOW)
    R.wcf[own_strip, :] = R.w_down[...].T.astype(LOW)
    wb.start_near()
    R.pick[...] = jnp.where(
        lax.broadcasted_iota(jnp.int32, (tokens, spots), 1).astype(F32) == slot, 1.0, 0.0
    ).astype(LOW)
    win.relays()

    ask_wait()
    small_eye = lax.broadcasted_iota(jnp.int32, (cap, 128), 0) == lax.broadcasted_iota(
        jnp.int32, (cap, 128), 1
    )

    def locate(index, carry):
        row = R.idx[mp.me, index][0:1, :]
        column = jnp.sum(jnp.where(small_eye, row, 0.0), 1, keepdims=True)
        local = column.astype(jnp.int32) - dp.me * table_rows
        R.loc[pl.ds(pl.multiple_of(index * cap, cap), cap), :] = jnp.broadcast_to(local, (cap, 128))
        return carry

    lax.fori_loop(0, size, locate, 0, unroll=True)
    win.close()
    win_all.start()
    found = None
    for piece in range(pieces):
        fetch(piece).wait()
        rows = min(chunk, table_rows - piece * chunk)
        if rows < chunk:
            R.tab[piece % 2, rows:, :] = jnp.zeros((chunk - rows, width), F32)
        hit = (
            lax.broadcasted_iota(jnp.int32, (spots, chunk), 1) + piece * chunk == R.loc[:, 0:1]
        )
        more = dot(jnp.where(hit, 1.0, 0.0).astype(LOW), R.tab[piece % 2].astype(LOW))
        found = more if found is None else found + more
        if piece + 2 < pieces:
            fetch(piece + 2).start()
    R.give[...] = found.astype(LOW)

    give, give_wait = far_copies(
        dp,
        lambda dest, source: (block_rows(R.give, cap)(dest), block_rows(R.got, cap)(source)),
        R.give_send,
        R.give_recv,
    )
    for step in range(1, size):
        give(step).start()
    R.got[mine, :] = R.give[mine, :]
    wa[1].start_far()
    win_all.relays()
    wa[0].relay(1)
    wa[0].relay(2)
    if wide_ln % 128 == 0:
        R.gains[...] = jnp.concatenate([R.idx[mp.me, index] for index in range(size)], 1)
    else:
        total = jnp.zeros((8, model), F32)
        for index in range(size):
            place = lax.broadcasted_iota(
                jnp.int32, (128, model), 1
            ) == index * wide_ln + lax.broadcasted_iota(jnp.int32, (128, model), 0)
            place = place & (lax.broadcasted_iota(jnp.int32, (128, model), 0) < wide_ln)
            total = total + dot(
                R.idx[mp.me, index].astype(LOW), jnp.where(place, 1.0, 0.0).astype(LOW)
            )
        R.gains[...] = total
    for step in range(3, dp.far):
        wa[0].relay(step)
    named = Gather(mp, of_index(R.idx), R.id_send, R.id_recv)

    give_wait()
    rows = dot(R.pick[...], R.got[...])
    R.rows[...] = rows.astype(LOW)
    sig = R.sig[...]
    unit = rows * lax.rsqrt(jnp.mean(rows * rows, -1, keepdims=True) + EPS_NORM)
    R.mixed[...] = ((unit + sig * R.noise[...].astype(F32)) * lax.rsqrt(1.0 + sig * sig)).astype(LOW)
    win_all.close()
    for index in range(ways):
        R.x0[:, index * quarter : (index + 1) * quarter] = dot(
            R.mixed[...], R.winf[index].astype(LOW)
        )

    for piece in range(seqs):
        here, there = rows_of(piece), own_rows(piece)

        def first_norm(row, here=here, there=there):
            normed, _ = norm_rows(R.x0[here(row), :])
            R.a[there(row), :] = (normed * R.gains[1:2, :] + R.gains[2:3, :]).astype(LOW)

        by_rows(first_norm, ag[piece].start)
    wa[1].relay(1)
    wb.start_far()
    for step in range(2, dp.far):
        wa[1].relay(step)
    dxg.relays()
    ag[0].relays()
    for gather in (*wa, ag[0]):
        gather.close()

    att = Sums(R.part, R.fold, R.fold_far, R.as_send, R.as_recv)
    dcs = Sums(R.part, R.fold, R.fold_far, R.cs_send, R.cs_recv)
    das = Sums(R.part, R.fold, R.fold_far, R.ds_send, R.ds_recv)
    out = Sums(R.c, R.first, R.second, R.os_send, R.os_recv)
    masks = head_masks(heads_w)

    all_rows = (heads_w // HD) * seq_len
    scale = HD ** (-0.5)

    def softmax(seq, row):
        scores = R.scores[seq, row : row + 64, :]
        raised = jnp.exp((scores - jnp.max(scores, -1, keepdims=True)) * scale)
        return raised * (1.0 / jnp.sum(raised, -1, keepdims=True))

    def attend(piece, base, here, at):
        at("start")
        for part in range(3):
            cols = slice(part * heads_w, (part + 1) * heads_w)
            R.qkv[here, cols] = dot(R.a[here, :], R.waf[:, cols]).astype(LOW)
        at("mid")

        def one(rows_at):
            for seq, rows in enumerate(rows_at):
                queries = spread_heads(R.qkv[rows, :heads_w], masks)
                R.scores[seq] = dot_nt(queries, R.qkv[rows, heads_w : 2 * heads_w])
            for seq, rows in enumerate(rows_at):
                for row in range(0, all_rows, 64):
                    R.probs[seq, row : row + 64, :] = softmax(seq, row).astype(LOW)
                seen = dot(R.probs[seq], R.qkv[rows, 2 * heads_w : 3 * heads_w])
                R.o[rows, :] = join_heads(seen, masks, seq_len).astype(LOW)

        pairs(base, one)
        at("late")

        def project(cols):
            R.part[here, cols] = dot_nt(R.o[here, :], R.waf[cols, 3 * heads_w :]).astype(LOW)

        def one_chunk(chunk, carry):
            project(pl.ds(pl.multiple_of(chunk * chunk_cols, chunk_cols), chunk_cols))
            att.trade(piece, chunk)
            return carry

        lax.fori_loop(0, chunk_count, one_chunk, 0)

    def second_norm(piece):
        here, there = rows_of(piece), own_rows(piece)
        att.arrive(piece)

        def norm(row):
            x1 = R.x0[here(row), :] + att.total(piece, pl.ds(row, some_rows))
            R.out[here(row), :] = x1
            normed, _ = norm_rows(x1)
            R.c[there(row), :] = (normed * R.gains[3:4, :] + R.gains[4:5, :]).astype(LOW)

        by_rows(norm, cg[piece].start)

    def first_wb():
        wb.relay(1)
        wc.start_near()
        wc.start_far()

    def last_wb():
        for step in range(3, dp.far):
            wb.relay(step)
        named.start()

    turns(
        attend,
        [
            *later_pieces(ag, "mid"),
            *[
                (piece + 1, "mid", functools.partial(att.hand_on_all, piece))
                for piece in range(seqs - 1)
            ],
            (0, "mid", first_wb),
            (0, "late", lambda: wb.relay(2)),
            (1, "mid", last_wb),
        ],
    )
    att.hand_on_all(seqs - 1)
    wc.relay(1)
    for piece in range(seqs):
        second_norm(piece)
        if piece == 0:
            for gather in (*wa, *ag, dxg, win):
                gather.drain()
            for step in range(1, size):
                ask(step).wait_send()
    cg[0].relays()
    wc.relay(2)
    wb.close()
    named.relays()
    cg[0].close()
    for piece in range(seqs):
        att.drain(piece)

    def activate(piece, base, here, at):
        at("start")

        def some(cols):
            R.h[...] = dot(R.c[here, :], R.wbf[:, cols])

            def gelu(row):
                there = pl.ds(pl.multiple_of(base + row, 64), 64)
                h = R.h[pl.ds(row, 64), :]
                bell = jnp.exp(-0.5 * h * h)
                tail = normal_tail(jnp.abs(h), bell)
                gate = jnp.where(h >= 0.0, 1.0 - tail, tail)
                slope = gate + h * (bell * 0.3989422804014327)
                R.hb[there, cols] = (h * gate).astype(LOW)
                R.slope[there, cols] = slope.astype(LOW)

            strips(many, 64, gelu, 2)

        chunks(hidden, some)
        at("end")

    def last_wc():
        for step in range(3, dp.far):
            wc.relay(step)

    turns(activate, [*later_pieces(cg, "end"), (0, "end", last_wc)])

    due = [(scatter, step) for scatter in (down, up) for step in range(1, dp.far)]

    def pass_due(number):
        for _ in range(min(number, len(due))):
            scatter, step = due.pop(0)
            scatter.pass_on(step)

    block = 2 * strip if (2 * strip) % 128 == 0 else min(256, model)

    def grads(make, trades):
        if block == 2 * strip:

            def turn_of(turn, carry):
                hi = up.turn_of(turn)
                make(pl.ds(pl.multiple_of(hi * block, block), block))
                for scatter in trades:
                    scatter.trade(hi)
                return carry

            lax.fori_loop(0, dp.far, turn_of, 0)
        else:
            strips(model, block, lambda col: make(pl.ds(col, block)))
            for scatter in trades:
                scatter.trade_all()

    def down_grads(cols):
        every = R.dx[:, :, cols]
        R.gdn[cols, :] = dot_tn(every.reshape(seqs * many, block), R.hb[...]).astype(LOW)

    def up_grads(cols):
        R.wbf[cols, :] = dot_tn(R.c[:, cols], R.dhb[...]).astype(LOW)

    dxg.close()
    grads(down_grads, (down,))
    wc.close()
    for gather in (wb, *cg):
        gather.drain()

    def feed_back(piece, base, here, at):
        at("start")

        def some(cols):
            bent = dot(R.dx[piece], R.wcf[:, cols]) * R.slope[here, cols].astype(F32)
            R.dhb[here, cols] = bent.astype(LOW)

        chunks(hidden, some)
        at("mid")

        def project(cols):
            R.part[here, cols] = dot_nt(R.dhb[here, :], R.wbf[cols, :]).astype(LOW)

        dcs.products(piece, project)

    R.norms[...] = jnp.zeros_like(R.norms)

    def second_back(piece):
        here, there = rows_of(piece), own_rows(piece)
        dcs.arrive(piece)

        def back(row):
            dc = dcs.total(piece, pl.ds(row, some_rows))
            grad, unit = norm_back(R.out[here(row), :], R.gains[3:4, :], dc)
            grad = grad + R.cot[here(row), :].astype(F32) * scale_at(here(row))
            R.dmid[here(row), :] = grad
            R.dmid_all[there(row), :] = grad.astype(LOW)
            R.norms[2:3, :] += jnp.sum(dc * unit, 0, keepdims=True)
            R.norms[3:4, :] += jnp.sum(dc, 0, keepdims=True)

        by_rows(back, mg[piece].start)

    turns(
        feed_back,
        [
            *[
                (piece + 1, "mid", functools.partial(dcs.hand_on_last, piece))
                for piece in range(seqs - 1)
            ],
            (1, "mid", lambda: pass_due(1)),
        ],
    )
    dcs.hand_on_last(seqs - 1)
    second_back(0)
    pass_due(1)
    grads(up_grads, (up,))
    for piece in range(1, seqs):
        second_back(piece)
    pass_due(max(1, dp.far - 3))
    mg[0].relays()
    mg[0].close()
    for piece in range(seqs):
        dcs.drain(piece)

    def attend_back(piece, base, here, at):
        at("start")
        R.low[...] = dot(R.dmid_all[here, :], R.waf[:, 3 * heads_w :]).astype(LOW)
        at("mid")

        def one(rows_at):
            for seq, rows in enumerate(rows_at):
                queries = spread_heads(R.qkv[rows, :heads_w], masks)
                R.scores[seq] = dot_nt(queries, R.qkv[rows, heads_w : 2 * heads_w])
                upper_rows = pl.ds(pl.multiple_of(rows.start - base, seq_len), seq_len)
                R.upper[seq] = spread_heads(R.low[upper_rows, :], masks)
                R.dprobs[seq] = dot_nt(R.upper[seq], R.qkv[rows, 2 * heads_w : 3 * heads_w])
            for seq, rows in enumerate(rows_at):
                for row in range(0, all_rows, 64):
                    probs = softmax(seq, row)
                    grad_probs = R.dprobs[seq, row : row + 64, :]
                    inner = jnp.sum(probs * grad_probs, -1, keepdims=True)
                    R.probs[seq, row : row + 64, :] = probs.astype(LOW)
                    R.dscores[seq, row : row + 64, :] = (probs * (grad_probs - inner)).astype(LOW)
                keys = R.qkv[rows, heads_w : 2 * heads_w]
                queries = spread_heads(R.qkv[rows, :heads_w], masks)
                R.qkv[rows, 2 * heads_w : 3 * heads_w] = dot_tn(R.probs[seq], R.upper[seq]).astype(LOW)
                R.qkv[rows, heads_w : 2 * heads_w] = (dot_tn(R.dscores[seq], queries) * scale).astype(
                    LOW
                )
                R.qkv[rows, :heads_w] = (
                    join_heads(dot(R.dscores[seq], keys), masks, seq_len) * scale
                ).astype(LOW)

        pairs(base, one)
        at("late")

        def project(cols):
            R.part[here, cols] = dot_nt(R.qkv[here, :], R.waf[cols, : 3 * heads_w]).astype(LOW)

        das.products(piece, project)

    def first_back(piece):
        here = rows_of(piece)
        das.arrive(piece)

        def back(row):
            da = das.total(piece, pl.ds(row, some_rows))
            grad, unit = norm_back(R.x0[here(row), :], R.gains[1:2, :], da)
            R.dx0[here(row), :] = (R.dmid[here(row), :] + grad).astype(LOW)
            R.norms[0:1, :] += jnp.sum(da * unit, 0, keepdims=True)
            R.norms[1:2, :] += jnp.sum(da, 0, keepdims=True)

        by_rows(back)

    def out_grads():
        def make(cols):
            R.gwo[cols, :] = dot_tn(R.dmid_all[:, cols], R.o[...]).astype(LOW)

        grads(make, (wo,))

    turns(
        attend_back,
        [
            *later_pieces(mg, "mid"),
            (0, "late", lambda: pass_due(1)),
            *[
                (piece + 1, "mid", functools.partial(das.hand_on_last, piece))
                for piece in range(seqs - 1)
            ],
            (seqs - 1, "late", lambda: pass_due(1)),
        ],
    )
    das.hand_on_last(seqs - 1)
    def out_grads(cols):
        R.gwo[cols, :] = dot_tn(R.dmid_all[:, cols], R.o[...]).astype(LOW)

    def attend_grads(cols):
        R.waf[cols, : 3 * heads_w] = dot_tn(R.a[:, cols], R.qkv[...]).astype(LOW)

    grads(out_grads, (wo,))
    first_back(0)
    grads(attend_grads, (first_w,))
    for piece in range(1, seqs):
        first_back(piece)

    grad_mixed = sum(
        dot_nt(R.dx0[:, index * quarter : (index + 1) * quarter], R.winf[index].astype(LOW))
        for index in range(ways)
    )
    sig = R.sig[...]
    grad_unit = grad_mixed * lax.rsqrt(1.0 + sig * sig)
    rows = R.rows[...].astype(F32)
    inverse = lax.rsqrt(jnp.mean(rows * rows, -1, keepdims=True) + EPS_NORM)
    unit = rows * inverse
    grad_rows = inverse * (grad_unit - unit * jnp.mean(grad_unit * unit, -1, keepdims=True))
    for step in range(1, size):
        give(step).wait_send()
    R.give[...] = dot_tn(R.pick[...], grad_rows.astype(LOW)).astype(LOW)
    mine_inc = block_rows(R.inc, spots)(mp.me)
    back, back_wait = far_copies(
        dp,
        lambda dest, source: (block_rows(R.give, cap)(dest), block_rows(mine_inc, cap)(source)),
        R.back_send,
        R.back_recv,
    )
    for step in range(1, size):
        back(step).start()
    mine_inc[mine, :] = R.give[mine, :]

    small_mp = Scatter(
        mp, of_index(R.gm), of_index(R.gm_first), of_index(R.gm_second), R.gm_send, R.gm_recv
    )
    for index in range(ways):
        cols = slice(index * quarter, (index + 1) * quarter)
        R.gm[index, :width, :] = dot_tn(R.mixed[...], R.dx0[:, cols]).astype(LOW)
        R.gm[index, width:, :] = jnp.concatenate(
            [R.norms[0:4, cols], jnp.zeros((12, quarter), F32)], 0
        ).astype(LOW)
    small_mp.trade_all()
    pass_due(len(due))
    for step in range(1, far):
        small_mp.pass_on(step)

    for step in range(1, dp.far):
        wo.pass_on(step)

    def feed_out(piece, base, here, at):
        def project(cols):
            R.c[here, cols] = dot_nt(R.hb[here, :], R.wcf[cols, :]).astype(LOW)

        out.products(piece, project)

    turns(feed_out)
    first_w.pass_on(1)
    back_wait()
    rows_in = Gather(mp, block_rows(R.inc, spots), R.in_send, R.in_recv)
    rows_in.start()
    for piece in range(seqs):
        out.hand_on_last(piece)

    small_mp.arrive()
    summed = small_mp.total(slice(None))
    for index in range(size):
        piece = summed[index * rin : (index + 1) * rin, :]
        if rin_up > rin:
            piece = jnp.concatenate([piece, jnp.zeros((rin_up - rin, quarter), F32)], 0)
        R.gw[index, :rin_up, :] = piece.astype(LOW)
        R.gw[index, rin_up:, :] = summed[width:, :].astype(LOW)
    small.trade_all()
    rows_in.relays()
    first_w.pass_on(2)

    def finish_out(piece):
        here = rows_of(piece)
        out.arrive(piece)

        def finish(row):
            R.out[here(row), :] = (
                R.out[here(row), :] + out.total(piece, pl.ds(row, some_rows))
            ) * scale_at(here(row))

        by_rows(finish)

    for piece in range(seqs):
        finish_out(piece)

    named.close()
    rows_in.close()
    groups = ways * size
    some, lanes_at = min(groups, 32), min(ways * spots, 512)
    for begin in range(0, ways * spots, lanes_at):
        spot = lax.broadcasted_iota(jnp.int32, (128, lanes_at), 1).astype(F32) + float(begin)
        block_no = jnp.floor((spot + 0.5) * (1.0 / cap))
        place = lax.broadcasted_iota(jnp.int32, (128, lanes_at), 0).astype(F32)
        spread_out = jnp.where(spot - block_no * cap == place, 1.0, 0.0).astype(LOW)
        named_row = jnp.zeros((1, lanes_at), F32)
        for first in range(0, groups, some):
            wanted = jnp.concatenate(
                [
                    R.idx[index // size, index % size][0:1, :] + 1.0
                    for index in range(first, first + some)
                ],
                0,
            )
            high = jnp.floor(wanted * (1.0 / 256.0))
            rest = wanted - 256.0 * high
            laid = dot(high.astype(LOW), spread_out) * 256.0 + dot(rest.astype(LOW), spread_out) - 1.0
            own_block = block_no[0:1, :] == float(first) + lax.broadcasted_iota(
                jnp.int32, (some, lanes_at), 0
            ).astype(F32)
            named_row = named_row + jnp.sum(jnp.where(own_block, laid, 0.0), 0, keepdims=True)
        R.named[:, begin : begin + lanes_at] = jnp.broadcast_to(
            named_row.astype(jnp.int32) - dp.me * table_rows, (8, lanes_at)
        )

    once = jnp.where(mp.me == 0, 1.0, 0.0)
    lanes = lax.broadcasted_iota(jnp.int32, (1, 128), 1)
    R.sums[...] = jnp.zeros_like(R.sums)

    def put(place, squares, factor=None):
        for row, values in enumerate(squares):
            total = jnp.sum(jnp.sum(values, 0, keepdims=True), 1, keepdims=True)
            if factor is not None:
                total = total * factor
            R.sums[row : row + 1, :] += jnp.where(lanes == place, total, 0.0)

    def squares_of(weight, gradient, first, second):
        direction = direction_of(weight, gradient, first, second)[2]
        return weight * weight, direction * direction

    def folded(values):
        rows, columns = values.shape
        return jnp.sum(values.reshape(rows // 8, 8, columns), 0)

    def add_up(weight, gradient, first, second):
        squares = squares_of(weight[...], gradient[...], first[...], second[...])
        return [folded(values) for values in squares]

    for tile in range(min(2, tiles)):
        for one in tile_of(tile):
            one.start()
    zero = jnp.zeros((8, width), F32)

    rest = [
        functools.partial(scatter.pass_on, step)
        for scatter in (first_w, small)
        for step in range(1, dp.far)
    ][2:]
    tail_hooks = [
        (min(tiles - 1, 1 + place * (tiles - 1) // len(rest)), action)
        for place, action in enumerate(rest)
    ]

    def add_tile(tile, carry):
        side = lax.rem(tile, 2)
        for place, action in tail_hooks:
            pl.when(tile == place)(action)
        for one in tile_of(tile):
            one.wait()
        hit = (
            lax.broadcasted_iota(jnp.int32, (tile_rows, ways * spots), 0) + tile * tile_rows
            == R.named[0:1, :]
        )
        gradient = dot(jnp.where(hit, 1.0, 0.0).astype(LOW), R.inc[...])
        more = add_up(R.tw.at[side], gradient, R.tm.at[side], R.tv.at[side])

        @pl.when(tile + 2 < tiles)
        def _():
            for one in tile_of(tile + 2):
                one.start()

        return carry[0] + more[0], carry[1] + more[1]

    put(0, lax.fori_loop(0, tiles, add_tile, (zero, zero)), once)

    for thing in (win_all, wc, *mg, up, down, wo, small_mp, named):
        thing.drain()
    for piece in range(seqs):
        out.drain(piece)
        das.drain(piece)
    for step in range(1, size):
        back(step).wait_send()

    for name in names_of_moments:
        moment(name).wait()
    up.arrive()

    R.red_up[...] = up.total(slice(None))
    put(10, add_up(R.w_up, R.red_up, R.up_m_here, R.up_v_here))
    down.arrive()

    R.red_dn[...] = down.total(slice(None)).T
    put(11, add_up(R.w_down, R.red_dn, R.down_m_here, R.down_v_here))
    wo.arrive()
    R.red_out[...] = wo.total(slice(None)).T
    put(9, add_up(R.w_out, R.red_out, R.out_m_here, R.out_v_here))

    small.arrive()
    R.wsum[mp.me] = small.total(slice(None)).astype(LOW)
    weights_in = Gather(mp, of_index(R.wsum), R.ws_send, R.ws_recv)
    weights_in.start()
    first_w.arrive()

    value = first_w.total(slice(None))
    for part in range(3):
        R.red_qkv[part] = value[:, part * heads_w : (part + 1) * heads_w]
    weights_in.relays()
    for part in range(3):
        put(
            6 + part,
            add_up(
                R.w_qkv.at[part], R.red_qkv.at[part], R.qkv_m_here.at[part], R.qkv_v_here.at[part]
            ),
        )
    weights_in.close()
    total = jnp.concatenate([R.wsum[index].astype(F32) for index in range(ways)], 1)
    R.red_in[...] = total[:rin, :]
    put(1, add_up(R.w_in, R.red_in, R.w_in_m_here, R.w_in_v_here), once)
    if strip % 128 == 0:
        R.lnsum[...] = total[rin_up : rin_up + 8, :]
        R.red_ln[...] = R.lnsum[0:4, pl.ds(pl.multiple_of(dp.me * strip, strip), strip)]
    else:
        chosen = lax.broadcasted_iota(jnp.int32, (model, strip), 0) == dp.me * strip + (
            lax.broadcasted_iota(jnp.int32, (model, strip), 1)
        )
        R.red_ln[...] = dot(
            total[rin_up : rin_up + 8, :].astype(LOW), jnp.where(chosen, 1.0, 0.0).astype(LOW)
        )[0:4]
    squares = squares_of(R.ln_params[...], R.red_ln[...], R.ln_m_here[...], R.ln_v_here[...])
    for row in range(4):
        put(2 + row, [values[row : row + 1, :] for values in squares], once)

    R.near[dp.me] = R.sums[...]
    near, near_wait = far_copies(
        dp, lambda dest, source: (R.near.at[dp.me], R.near.at[source]), R.near_send, R.near_recv
    )
    for step in range(1, size):
        near(step).start()
    near_wait()
    R.wide[mp.me] = jnp.sum(R.near[...], 0)
    far_off, far_off_wait = far_copies(
        mp, lambda dest, source: (R.wide.at[mp.me], R.wide.at[source]), R.wide_send, R.wide_recv
    )
    for step in range(1, ways):
        far_off(step).start()
    far_off_wait()
    R.totals[...] = jnp.sum(R.wide[...], 0)

    for thing in (first_w, small, rows_in, weights_in):
        thing.drain()
    for step in range(1, size):
        near(step).wait_send()
    for step in range(1, ways):
        far_off(step).wait_send()


def run_layer(cap, ids, levels, noise, cot, weights, moments):
    table, w_in, ln_params, w_qkv, w_out, w_up, w_down = weights
    dp, mp = lax.axis_size("dp"), lax.axis_size("mp")
    seqs, seq_len = ids.shape
    tokens, width = noise.shape
    model = cot.shape[1]
    rin = w_in.shape[0]
    heads_w = w_qkv.shape[2]
    strip, hidden = w_up.shape
    group = tokens * mp
    spots = dp * cap
    wide = round_up(rin, 16) + 16
    far, far_dp = mp // 2, dp // 2
    quarter = model // mp
    in_kind = LOW if rin % 16 == 0 else F32
    tile_rows = max(rows for rows in range(8, 513, 8) if table.shape[0] % rows == 0)
    stacked = (heads_w // HD) * seq_len
    vmem = pl.BlockSpec(memory_space=pltpu.VMEM)
    outside = pl.BlockSpec(memory_space=pl.ANY)
    inputs = dict(
        ids=(ids, vmem),
        levels=(levels, pl.BlockSpec(memory_space=pltpu.SMEM)),
        noise=(noise, vmem),
        cot=(cot, vmem),
        table=(table, outside),
        w_in=(w_in, vmem),
        ln_params=(ln_params, vmem),
        w_qkv=(w_qkv, vmem),
        w_out=(w_out, vmem),
        w_up=(w_up, vmem),
        w_down=(w_down, vmem),
    )
    kept = {}
    for name, (first, second) in zip(("table", "w_in", "ln", "qkv", "out", "up", "down"), moments):
        inputs[name + "_m"] = (first, outside)
        inputs[name + "_v"] = (second, outside)
        if name != "table":
            kept[name + "_m_here"] = kept[name + "_v_here"] = (first.shape, F32)
    outputs = dict(
        out=((tokens, model), F32),
        red_up=((strip, hidden), F32),
        red_dn=((hidden, strip), F32),
        red_qkv=((3, strip, heads_w), F32),
        red_out=((heads_w, strip), F32),
        red_in=((rin, model), F32),
        red_ln=((4, strip), F32),
        inc=((mp * spots, width), LOW),
        named=((8, mp * spots), jnp.int32),
        totals=((8, 128), F32),
    )
    buffers = dict(
        tab=((2, round_up(table.shape[0] // 8, 128), width), F32),
        ask=((dp, 8, 128), F32),
        idx=((mp, dp, 8, 128), F32),
        loc=((spots, 128), jnp.int32),
        give=((spots, width), LOW),
        got=((spots, width), LOW),
        tw=((2, tile_rows, width), F32),
        tm=((2, tile_rows, width), F32),
        tv=((2, tile_rows, width), F32),
        sums=((8, 128), F32),
        near=((dp, 8, 128), F32),
        wide=((mp, 8, 128), F32),
        scores=((2, stacked, seq_len), F32),
        dprobs=((2, stacked, seq_len), F32),
        probs=((2, stacked, seq_len), LOW),
        dscores=((2, stacked, seq_len), LOW),
        upper=((2, stacked, heads_w), LOW),
        gwo=((model, heads_w), LOW),
        wo_first=((far_dp * strip, heads_w), LOW),
        wo_second=((far_dp * strip, heads_w), LOW),
        gains=((8, model), F32),
        lnsum=((8, model), F32),
        sig=((tokens, 1), F32),
        pick=((tokens, spots), LOW),
        rows=((tokens, width), LOW),
        mixed=((tokens, width), LOW),
        x0=((tokens, model), F32),
        a=((group, model), LOW),
        c=((group, model), LOW),
        dx=((seqs, group // seqs, model), LOW),
        dmid=((tokens, model), F32),
        dmid_all=((group, model), LOW),
        winf=((mp, rin * dp, quarter), in_kind),
        waf=((model, 4 * heads_w), LOW),
        wbf=((model, hidden), LOW),
        wcf=((model, hidden), LOW),
        qkv=((group, 3 * heads_w), LOW),
        o=((group, heads_w), LOW),
        low=((group // seqs, heads_w), LOW),
        part=((group, model), LOW),
        first=((far * tokens, model), LOW),
        fold=((far * tokens, model), LOW),
        second=((far * tokens, model), LOW),
        fold_far=((far * tokens, model), LOW),
        h=((group // seqs, min(256, hidden)), F32),
        hb=((group, hidden), LOW),
        dhb=((group, hidden), LOW),
        slope=((group, hidden), LOW),
        gdn=((model, hidden), LOW),
        dx0=((tokens, model), LOW),
        norms=((8, model), F32),
        gm=((mp, width + 16, quarter), LOW),
        gm_first=((far, width + 16, quarter), LOW),
        gm_second=((far, width + 16, quarter), LOW),
        gw=((dp, wide, quarter), LOW),
        gw_first=((far_dp, wide, quarter), LOW),
        gw_second=((far_dp, wide, quarter), LOW),
        up_first=((far_dp * strip, hidden), LOW),
        up_second=((far_dp * strip, hidden), LOW),
        dn_first=((far_dp * strip, hidden), LOW),
        dn_second=((far_dp * strip, hidden), LOW),
        wa_first=((far_dp * strip, 3 * heads_w), LOW),
        wa_second=((far_dp * strip, 3 * heads_w), LOW),
        wsum=((mp, wide, quarter), LOW),
        up_extra=((strip, hidden), LOW),
        dn_extra=((strip, hidden), LOW),
        wa_extra=((strip, 3 * heads_w), LOW),
        wo_extra=((strip, heads_w), LOW),
        gw_extra=((wide, quarter), LOW),
        **kept,
    )
    sems = dict(tab_sem=2, tile_sem=6, moment_sem=12)
    for name in (
        *("win", "wa", "wx", "wb", "wc", "ask", "give", "back"),
        *("up", "dn", "ga", "wo", "gw", "near"),
    ):
        sems[name + "_send"] = sems[name + "_recv"] = dp + 1
    for name in ("wim", "id", "in", "ws", "gm", "wide"):
        sems[name + "_send"] = sems[name + "_recv"] = mp
    for name in ("dx", "a", "c", "e"):
        sems[name + "_send"] = sems[name + "_recv"] = 2 * seqs * mp
    for name in ("as", "os", "cs", "ds"):
        sems[name + "_send"] = sems[name + "_recv"] = seqs * mp * (model // min(256, model))
    names = [*inputs, *outputs, *buffers, *sems]
    made = pl.pallas_call(
        functools.partial(layer_kernel, cap, names),
        out_shape=[jax.ShapeDtypeStruct(shape, kind) for shape, kind in outputs.values()],
        in_specs=[spec for _, spec in inputs.values()],
        out_specs=[vmem] * len(outputs),
        scratch_shapes=[
            *[pltpu.VMEM(shape, kind) for shape, kind in buffers.values()],
            *[pltpu.SemaphoreType.DMA((number,)) for number in sems.values()],
        ],
        compiler_params=pltpu.CompilerParams(
            vmem_limit_bytes=VMEM_BYTES, collective_id=1, has_side_effects=True
        ),
        name="layer",
    )(*[value for value, _ in inputs.values()])
    return dict(zip(outputs, made))


def direction_of(weight, gradient, first, second):
    first_new = BETA_ONE * first + (1.0 - BETA_ONE) * gradient
    second_new = BETA_TWO * second + (1.0 - BETA_TWO) * gradient * gradient
    second_hat = second_new * (1.0 / (1.0 - BETA_TWO**STEP))
    inverse = lax.rsqrt(second_hat)
    root = second_hat * inverse + EPS_ADAM
    inverse = inverse * (2.0 - root * inverse)
    inverse = inverse * (2.0 - root * inverse)
    direction = first_new * (1.0 / (1.0 - BETA_ONE**STEP)) * inverse + DECAY * weight
    return first_new, second_new, direction


def update_kernel(part, names, *refs):
    R = types.SimpleNamespace(**dict(zip(names, refs)))
    turn = pl.program_id(0)
    R.out_rows[...] = R.made[...]
    norms = jnp.sqrt(R.totals[...])
    R.norms[...] = norms[0:2, 0:12]
    factors = norms[0:1, :] / (norms[1:2, :] + EPS_ADAM) * RATE

    def piece(name, here, gradient, place, rows=slice(None)):
        weight = getattr(R, name)[here]
        first_new, second_new, direction = direction_of(
            weight, gradient, getattr(R, name + "_m")[here], getattr(R, name + "_v")[here]
        )
        if isinstance(place, int):
            factor = factors[0:1, place : place + 1]
        else:
            factor = jnp.concatenate([factors[0:1, one : one + 1] for one in place], 0)
        getattr(R, name + "_m_new")[here] = first_new
        getattr(R, name + "_v_new")[here] = second_new
        getattr(R, name + "_new")[here] = weight - factor * direction

    def update(name, gradient, place, lead=(), here=slice(None)):
        piece(name, (*lead, here, slice(None)), gradient, place)

    tile = R.table.shape[0]
    spots = R.named.shape[1]

    def table_part(row):
        hit = (
            lax.broadcasted_iota(jnp.int32, (part, spots), 0) + (turn * tile + row)
            == R.named[0:1, :]
        )
        gradient = dot(jnp.where(hit, 1.0, 0.0).astype(LOW), R.inc[...])
        update("table", gradient, 0, (), pl.ds(row, part))

    strips(tile, part, table_part)
    for group in range(3):
        update("qkv", R.red_qkv[group], 6 + group, (group,))
    update("up", R.red_up[...], 10)
    update("down", R.red_dn[...], 11)

    @pl.when(turn == 0)
    def _():
        update("out", R.red_out[...], 9)
        update("w_in", R.red_in[...], 1)
        piece("ln", (slice(None), slice(None)), R.red_ln[...], (2, 3, 4, 5))


def turns_of(rows, parts):
    return [
        turns
        for turns in (5, 4, 2, 1)
        if rows % (8 * turns) == 0 and all(size % (8 * turns) == 0 for size in parts)
    ][0]


def run_update(weights, moments, grads):
    names = ("table", "w_in", "ln", "qkv", "out", "up", "down")
    by_name = dict(zip(names, weights))
    rows, width = by_name["table"].shape
    strip, hidden = by_name["up"].shape
    heads_w = by_name["qkv"].shape[2]
    turns = turns_of(rows, (strip, hidden))
    tile = rows // turns
    part = max(size for size in range(8, 257, 8) if tile % size == 0)
    fixed = lambda array: pl.BlockSpec(array.shape, lambda turn: (0,) * array.ndim)
    specs = dict(
        table=pl.BlockSpec((tile, width), lambda turn: (turn, 0)),
        w_in=fixed(by_name["w_in"]),
        ln=fixed(by_name["ln"]),
        qkv=pl.BlockSpec((3, strip // turns, heads_w), lambda turn: (0, turn, 0)),
        out=fixed(by_name["out"]),
        up=pl.BlockSpec((strip // turns, hidden), lambda turn: (turn, 0)),
        down=pl.BlockSpec((hidden // turns, strip), lambda turn: (turn, 0)),
    )
    inputs = {}
    for name, weight, (first, second) in zip(names, weights, moments):
        inputs[name] = (weight, specs[name])
        inputs[name + "_m"] = (first, specs[name])
        inputs[name + "_v"] = (second, specs[name])
    for name, like in (
        ("red_up", "up"),
        ("red_dn", "down"),
        ("red_qkv", "qkv"),
        ("red_out", "out"),
        ("red_in", "w_in"),
        ("red_ln", "ln"),
    ):
        inputs[name] = (grads[name], specs[like])
    for name in ("inc", "named", "totals"):
        inputs[name] = (grads[name], fixed(grads[name]))
    tokens, model = grads["out"].shape
    rows_spec = pl.BlockSpec((tokens // turns, model), lambda turn: (turn, 0))
    inputs["made"] = (grads["out"], rows_spec)
    outputs = {"out_rows": (grads["out"].shape, rows_spec)}
    for name, weight in by_name.items():
        for kind in ("_new", "_m_new", "_v_new"):
            outputs[name + kind] = (weight.shape, specs[name])
    outputs["norms"] = ((2, 12), pl.BlockSpec((2, 12), lambda turn: (0, 0)))
    results = pl.pallas_call(
        functools.partial(update_kernel, part, [*inputs, *outputs]),
        grid=(turns,),
        out_shape=[jax.ShapeDtypeStruct(shape, F32) for shape, _ in outputs.values()],
        in_specs=[spec for _, spec in inputs.values()],
        out_specs=[spec for _, spec in outputs.values()],
        compiler_params=pltpu.CompilerParams(vmem_limit_bytes=VMEM_BYTES),
        name="update",
    )(*[value for value, _ in inputs.values()])
    return list(results)


def per_device(
    token_ids,
    levels,
    noise,
    cotangent,
    table,
    table_m,
    table_v,
    w_in,
    w_in_m,
    w_in_v,
    ln_params,
    ln_m,
    ln_v,
    w_qkv,
    qkv_m,
    qkv_v,
    w_out,
    out_m,
    out_v,
    w_up,
    up_m,
    up_v,
    w_down,
    down_m,
    down_v,
):
    dp_count = lax.axis_size("dp")
    seq_count, seq_len = token_ids.shape
    tokens = seq_count * seq_len
    model = cotangent.shape[2]
    cap = round_up(max(2, (3 * tokens + 2 * dp_count - 1) // (2 * dp_count)), 16)
    weights = (table, w_in, ln_params, w_qkv, w_out, w_up, w_down)
    moments = (
        (table_m, table_v),
        (w_in_m, w_in_v),
        (ln_m, ln_v),
        (qkv_m, qkv_v),
        (out_m, out_v),
        (up_m, up_v),
        (down_m, down_v),
    )
    grads = run_layer(
        cap,
        token_ids,
        levels,
        noise.reshape(tokens, -1),
        cotangent.reshape(tokens, model),
        weights,
        moments,
    )
    out, *results = run_update(weights, moments, grads)
    return (out.reshape(seq_count, seq_len, model), *results)


def solution(mesh):
    return jax.shard_map(
        per_device,
        mesh=mesh,
        in_specs=(
            P(("dp", "mp"), None),
            P(("dp", "mp")),
            P(("dp", "mp"), None, None),
            P(("dp", "mp"), None, None),
            P("dp", None),
            P("dp", None),
            P("dp", None),
            P("dp", None),
            P("dp", None),
            P("dp", None),
            P(None, "dp"),
            P(None, "dp"),
            P(None, "dp"),
            P(None, "dp", "mp"),
            P(None, "dp", "mp"),
            P(None, "dp", "mp"),
            P("mp", "dp"),
            P("mp", "dp"),
            P("mp", "dp"),
            P("dp", "mp"),
            P("dp", "mp"),
            P("dp", "mp"),
            P("mp", "dp"),
            P("mp", "dp"),
            P("mp", "dp"),
        ),
        out_specs=(
            P(("dp", "mp"), None, None),
            P("dp", None),
            P("dp", None),
            P("dp", None),
            P("dp", None),
            P("dp", None),
            P("dp", None),
            P(None, "dp"),
            P(None, "dp"),
            P(None, "dp"),
            P(None, "dp", "mp"),
            P(None, "dp", "mp"),
            P(None, "dp", "mp"),
            P("mp", "dp"),
            P("mp", "dp"),
            P("mp", "dp"),
            P("dp", "mp"),
            P("dp", "mp"),
            P("dp", "mp"),
            P("mp", "dp"),
            P("mp", "dp"),
            P("mp", "dp"),
            P(),
        ),
        check_vma=False,
    )
```

```python
import functools
import types

import jax
import jax.numpy as jnp
from jax import lax
from jax.experimental import pallas as pl
from jax.experimental.pallas import tpu as pltpu
from jax.sharding import PartitionSpec as P

HD = 64
LEVELS = 64
STEP = 10


EPS_NORM = 1e-06
EPS_LAYER = 1e-05
EPS_ADAM = 1e-06
BETA_ONE = 0.9
BETA_TWO = 0.999
DECAY = 0.01
RATE = 0.5
SIGMA_TOP = 10.0

F32 = jnp.float32
LOW = jnp.bfloat16
VMEM_BYTES = 63 * 1024 * 1024


def sigma_of(levels):
    frac = levels.astype(jnp.float32) / (LEVELS - 1)
    return jnp.exp(frac * jnp.log(SIGMA_TOP))


def lamb_moments(weight, gradient, first, second):
    first_new = BETA_ONE * first + (1.0 - BETA_ONE) * gradient
    second_new = BETA_TWO * second + (1.0 - BETA_TWO) * gradient * gradient
    first_hat = first_new / (1.0 - BETA_ONE**STEP)
    second_hat = second_new / (1.0 - BETA_TWO**STEP)
    direction = first_hat / (jnp.sqrt(second_hat) + EPS_ADAM) + DECAY * weight
    return (first_new, second_new, direction)


def trust_factors(ratio):
    return (
        ratio[0],
        ratio[1],
        ratio[2:6][:, None],
        ratio[6:9][:, None, None],
        ratio[9],
        ratio[10],
        ratio[11],
    )


def round_up(value, step):
    return -(-value // step) * step


def dot(left, right):
    return jnp.dot(left, right, preferred_element_type=F32)


def dot_nt(left, right):
    return lax.dot_general(left, right, (((1,), (1,)), ((), ())), preferred_element_type=F32)


def dot_tn(left, right):
    return lax.dot_general(left, right, (((0,), (0,)), ((), ())), preferred_element_type=F32)


def strips(total, step, body, unroll=1):
    step = min(step, total)

    def one(turn, carry):
        body(pl.multiple_of(turn * step, step))
        return carry

    lax.fori_loop(0, total // step, one, 0, unroll=unroll)


class Line:
    def __init__(self, axis):
        self.axis = axis
        self.size = lax.axis_size(axis)
        self.far = self.size // 2
        self.me = lax.axis_index(axis)
        self.hi = lax.div(self.me, 2)
        self.lo = lax.rem(self.me, 2)
        self.partner = self.hi * 2 + (1 - self.lo)

    def at(self, step):
        return lax.rem(self.hi + step + self.far, self.far)

    def push(self, index, src, dst, send, recv):
        return pltpu.make_async_remote_copy(
            src_ref=src,
            dst_ref=dst,
            send_sem=send,
            recv_sem=recv,
            device_id={self.axis: index},
            device_id_type=pl.DeviceIdType.MESH,
        )

    def signal(self, sem, index):
        pl.semaphore_signal(
            sem, inc=1, device_id={self.axis: index}, device_id_type=pl.DeviceIdType.MESH
        )


def meet(pair_lines, all_lines=()):
    sem = pltpu.get_barrier_semaphore()
    count = 0
    for line in pair_lines:
        for step in range(1, line.far):
            line.signal(sem, line.at(step) * 2 + line.lo)
            count += 1
        line.signal(sem, line.partner)
        count += 1
    for line in all_lines:
        for step in range(1, line.size):
            line.signal(sem, lax.rem(line.me + step, line.size))
            count += 1
    pl.semaphore_wait(sem, count)


class Gather:
    def __init__(self, line, at, send, recv, base=0, ends=False):
        self.line, self.at, self.send, self.recv, self.base = line, at, send, recv, base
        self.ends = ends and line.far == 4

    def source(self, step):
        line = self.line
        if not self.ends:
            return line.at(-step)
        order = ((1, 2, 3), (0, 3, 2), (3, 0, 1), (2, 1, 0))
        hi = order[3][step - 1]
        for place in (2, 1, 0):
            hi = jnp.where(line.hi == place, order[place][step - 1], hi)
        return hi

    def far_sends(self, act):
        line = self.line
        for step in range(1, line.far):
            one = self.copy(line.me, step - 1, line.at(step) * 2 + line.lo)
            if self.ends and step != 2:
                pl.when(line.hi != (3 if step == 1 else 0))(functools.partial(act, one))
            else:
                act(one)

    def to_end(self, act):
        line = self.line
        dest = jnp.where(line.hi == 1, 0, 3)
        one = self.copy((3 - dest) * 2 + line.lo, 2 * line.far - 1, dest * 2 + line.lo)
        pl.when((line.hi == 1) | (line.hi == 2))(functools.partial(act, one))

    def copy(self, index, slot, dest):
        block = self.at(index)
        return self.line.push(
            dest, block, block, self.send.at[self.base + slot], self.recv.at[self.base + index]
        )

    def start_far(self):
        self.far_sends(lambda one: one.start())

    def start_near(self):
        self.copy(self.line.me, self.line.far - 1, self.line.partner).start()

    def start(self):
        self.start_far()
        self.start_near()

    def relay(self, step):
        line = self.line
        handed = self.copy(self.source(step) * 2 + line.lo, line.far - 1 + step, line.partner)
        handed.wait_recv()
        if self.ends and step == 2:
            self.to_end(lambda one: one.start())
        handed.start()

    def relays(self):
        for step in range(1, self.line.far):
            self.relay(step)

    def close(self):
        line = self.line
        for step in range(line.far):
            self.copy(line.at(-step) * 2 + (1 - line.lo), 0, line.partner).wait_recv()

    def drain(self):
        self.far_sends(lambda one: one.wait_send())
        if self.ends:
            self.to_end(lambda one: one.wait_send())
        for slot in range(self.line.far - 1, 2 * self.line.far - 1):
            self.copy(self.line.me, slot, self.line.partner).wait_send()


class SideGather(Gather):
    def other(self, act):
        line = self.line
        for step in range(1, line.far):
            one = self.copy(line.partner, line.far - 1 + step, line.at(step) * 2 + line.lo)
            if self.ends and step != 2:
                pl.when(line.hi != (3 if step == 1 else 0))(functools.partial(act, one))
            else:
                act(one)

    def to_ends(self, parity, slot, act):
        line = self.line
        dest = jnp.where(line.hi == 1, 0, 3)
        one = self.copy((3 - dest) * 2 + parity, slot, dest * 2 + line.lo)
        pl.when((line.hi == 1) | (line.hi == 2))(functools.partial(act, one))

    def start_other(self):
        self.copy(self.line.partner, 0, self.line.partner).wait_recv()
        self.other(lambda one: one.start())

    def taken(self, step):
        line = self.line
        for parity, slot in ((line.lo, 2 * line.far - 1), (1 - line.lo, 2 * line.far)):
            self.copy(self.source(step) * 2 + parity, 0, line.partner).wait_recv()
            if self.ends and step == 2:
                self.to_ends(parity, slot, lambda one: one.start())

    def forward(self):
        if self.line.far > 2:
            self.taken(2)

    def close(self):
        for step in range(1, self.line.far):
            if step != 2:
                self.taken(step)

    def drain(self):
        line = self.line
        self.far_sends(lambda one: one.wait_send())
        self.copy(line.me, line.far - 1, line.partner).wait_send()
        self.other(lambda one: one.wait_send())
        if self.ends:
            for parity, slot in ((line.lo, 2 * line.far - 1), (1 - line.lo, 2 * line.far)):
                self.to_ends(parity, slot, lambda one: one.wait_send())


class SideScatter:
    def __init__(self, line, part, second, first, send, recv):
        self.line, self.part, self.second, self.first = line, part, second, first
        self.send, self.recv = send, recv

    def far_copy(self, step, parity):
        line = self.line
        hi = line.at(step)
        return line.push(
            hi * 2 + line.lo,
            self.part(hi * 2 + parity),
            self.second(parity * line.far + line.hi),
            self.send.at[2 * (step - 1) + parity],
            self.recv.at[parity * line.far + line.hi],
        )

    def near_copy(self):
        line = self.line
        return line.push(
            line.partner,
            self.part(line.partner),
            self.first,
            self.send.at[2 * line.far - 2],
            self.recv.at[2 * line.far],
        )

    def start(self):
        for step in range(1, self.line.far):
            for parity in range(2):
                self.far_copy(step, parity).start()

    def sum_of(self, parity):
        line = self.line
        value = self.part(line.hi * 2 + parity)[...].astype(F32)
        for step in range(1, line.far):
            index = parity * line.far + line.at(-step)
            block = self.second(index)
            line.push(
                line.partner, block, block, self.send.at[0], self.recv.at[index]
            ).wait_recv()
            value = value + block[...].astype(F32)
        return value

    def trade(self):
        given = self.part(self.line.partner)
        given[...] = self.sum_of(1 - self.line.lo).astype(LOW)
        self.near_copy().start()

    def arrive(self):
        pass

    def total(self):
        value = self.sum_of(self.line.lo)
        self.near_copy().wait_recv()
        return value + self.first[...].astype(F32)

    def drain(self):
        for step in range(1, self.line.far):
            for parity in range(2):
                self.far_copy(step, parity).wait_send()
        self.near_copy().wait_send()


class Scatter:
    def __init__(self, line, part, first, second, send, recv, base=0, extra=None):
        self.line, self.part, self.first, self.second = line, part, first, second
        self.send, self.recv, self.base = send, recv, base
        self.extra = extra if line.far == 4 else None

    def clear(self):
        line = self.line
        if self.extra is not None:

            @pl.when((line.hi == 0) | (line.hi == 3))
            def _():
                slot = self.second(3 - line.hi)
                slot[...] = jnp.zeros(slot.shape, LOW)

    def order(self, step):
        line = self.line
        if self.extra is None:
            return line.at(step)
        table = ((3, 2, 1), (2, 0, 3), (1, 3, 0), (0, 1, 2))
        hi = table[3][step - 1]
        for place in (2, 1, 0):
            hi = jnp.where(line.hi == place, table[place][step - 1], hi)
        return hi

    def traded(self, hi):
        line = self.line
        return line.push(
            line.partner,
            self.part(hi * 2 + (1 - line.lo)),
            self.first(hi),
            self.send.at[self.base + hi],
            self.recv.at[self.base + hi],
        )

    def passed(self, step):
        line = self.line
        hi = self.order(step)
        return line.push(
            hi * 2 + line.lo,
            self.part(hi * 2 + line.lo),
            self.second(line.hi),
            self.send.at[self.base + line.far + step - 1],
            self.recv.at[self.base + line.far + line.hi],
        )

    def to_next(self):
        line = self.line
        return line.push(
            jnp.where(line.hi < 2, 1, 2) * 2 + line.lo,
            self.part((3 - jnp.where(line.hi < 2, 0, 3)) * 2 + line.lo),
            self.extra,
            self.send.at[self.base + line.far],
            self.recv.at[self.base + 2 * line.far],
        )

    def turn_of(self, turn):
        line = self.line
        if self.extra is None:
            return lax.rem(line.hi + turn + 1, line.far)
        hi = line.hi
        for step in range(1, line.far):
            hi = jnp.where(turn == step - 1, self.order(step), hi)
        return hi

    def is_end(self):
        return (self.line.hi == 0) | (self.line.hi == 3)

    def trade(self, hi):
        self.traded(hi).start()

    def trade_all(self):
        for step in range(1, self.line.far + 1):
            self.trade(self.order(step) if step < self.line.far else self.line.hi)

    def pass_on(self, step):
        line = self.line
        hi = self.order(step)
        self.traded(hi).wait_recv()
        mine, other = self.part(hi * 2 + line.lo), self.first(hi)
        if self.extra is None or step == 2:
            mine[...] = (mine[...].astype(F32) + other[...].astype(F32)).astype(LOW)
            self.passed(step).start()
        elif step == 1:
            mine[...] = (mine[...].astype(F32) + other[...].astype(F32)).astype(LOW)

            @pl.when(self.is_end())
            def _():
                self.to_next().start()

            @pl.when(jnp.logical_not(self.is_end()))
            def _():
                self.passed(step).start()
        else:

            @pl.when(self.is_end())
            def _():
                mine[...] = (mine[...].astype(F32) + other[...].astype(F32)).astype(LOW)

            @pl.when(jnp.logical_not(self.is_end()))
            def _():
                line.push(
                    line.partner,
                    self.extra,
                    self.extra,
                    self.send.at[self.base],
                    self.recv.at[self.base + 2 * line.far],
                ).wait_recv()
                mine[...] = (
                    mine[...].astype(F32) + other[...].astype(F32) + self.extra[...].astype(F32)
                ).astype(LOW)

            self.passed(step).start()

    def arrive(self):
        line = self.line
        self.traded(line.hi).wait_recv()
        for step in range(1, line.far):
            hi = line.at(-step)
            one = line.push(
                line.partner,
                self.second(hi),
                self.second(hi),
                self.send.at[self.base],
                self.recv.at[self.base + line.far + hi],
            )
            if self.extra is None:
                one.wait_recv()
            else:
                pl.when(jnp.logical_not(self.is_end()) | (hi + line.hi != 3))(one.wait_recv)

    def total(self, here):
        line = self.line
        value = self.part(line.me)[here, :].astype(F32) + self.first(line.hi)[here, :].astype(F32)
        for step in range(1, line.far):
            value = value + self.second(line.at(-step))[here, :].astype(F32)
        return value

    def drain(self):
        line = self.line
        for step in range(line.far):
            self.traded(line.at(step)).wait_send()
        for step in range(1, line.far):
            if self.extra is not None and step == 1:
                pl.when(self.is_end())(lambda: self.to_next().wait_send())
                pl.when(jnp.logical_not(self.is_end()))(lambda: self.passed(1).wait_send())
            else:
                self.passed(step).wait_send()


def block_rows(ref, rows, first=0):
    return lambda index: ref.at[pl.ds(pl.multiple_of((index + first) * rows, rows), rows)]


def part_rows(ref, rows, first, count):
    return lambda index: ref.at[pl.ds(pl.multiple_of(index * rows + first, count), count)]


def of_index(ref):
    return lambda index: ref.at[index]


def norm_rows(values):
    center = values - jnp.mean(values, -1, keepdims=True)
    spread = jnp.mean(center * center, -1, keepdims=True)
    inverse = lax.rsqrt(spread + EPS_LAYER)
    return center * inverse, inverse


def norm_back(values, gain, grad):
    unit, inverse = norm_rows(values)
    inner = grad * gain
    shared = jnp.mean(inner, -1, keepdims=True)
    along = jnp.mean(inner * unit, -1, keepdims=True)
    return inverse * (inner - shared - unit * along), unit


def head_masks(width):
    lane = lax.broadcasted_iota(jnp.int32, (1, width), 1)
    return [
        jnp.where((lane >= head * HD) & (lane < (head + 1) * HD), 1.0, 0.0)
        for head in range(width // HD)
    ]


def spread_heads(values, masks):
    return jnp.concatenate([values * mask.astype(LOW) for mask in masks], 0)


def join_heads(values, masks, rows):
    total = values[0:rows] * masks[0]
    for head in range(1, len(masks)):
        total = total + values[head * rows : (head + 1) * rows] * masks[head]
    return total


TAIL = (
    0.2256758632450557,
    0.22566952478278277,
    0.2078438574180613,
    0.16853390514724884,
    0.14146086231844687,
    -0.005667717379728321,
    0.16915486959066833,
    -0.18294364197603524,
    0.05027260226320005,
)


def normal_tail(size, bell):
    base = 1.0 + (0.4 * 0.5**0.5) * size
    t = pl.reciprocal(base, approx=True)
    t = t * (2.0 - base * t)
    t = t * (2.0 - base * t)
    value = jnp.full_like(t, 0.5 * TAIL[-1])
    for factor in TAIL[-2::-1]:
        value = value * t + 0.5 * factor
    return value * t * bell


def far_copies(line, make, sends, recvs):
    def copy(step):
        dest = lax.rem(line.me + step, line.size)
        src, dst = make(dest, line.me)
        return line.push(dest, src, dst, sends.at[step], recvs.at[line.me])

    def wait():
        for step in range(1, line.size):
            source = lax.rem(line.me + line.size - step, line.size)
            _, dst = make(source, source)
            line.push(line.partner, dst, dst, sends.at[0], recvs.at[source]).wait_recv()

    return copy, wait


def layer_kernel(cap, names, *refs):
    R = types.SimpleNamespace(**dict(zip(names, refs)))
    dp, mp = Line("dp"), Line("mp")
    size, ways = dp.size, mp.size
    seqs, seq_len = R.ids.shape
    tokens, width = R.noise.shape
    model = R.cot.shape[1]
    heads_w = R.o.shape[1]
    hidden = R.wbf.shape[1]
    table_rows = R.table.shape[0]
    rin = R.w_in.shape[0]
    rin_up = round_up(rin, 16)
    quarter = model // ways
    strip = R.w_up.shape[0]
    spots = size * cap
    far = mp.far
    count = seqs * far
    half_strip = strip // 2
    own_strip = pl.ds(pl.multiple_of(dp.me * strip, strip), strip)
    mine = pl.ds(pl.multiple_of(dp.me * cap, cap), cap)

    some_rows = seq_len // 2

    def rows_of(piece):
        return lambda row: pl.ds(pl.multiple_of(piece * seq_len + row, some_rows), some_rows)

    def own_rows(piece):
        first = pl.multiple_of((piece * ways + mp.me) * seq_len, seq_len)
        return lambda row: pl.ds(pl.multiple_of(first + row, some_rows), some_rows)

    def by_rows(body, after=lambda half: None):
        for half in range(2):
            body(half * some_rows)
            after(half)

    class Rows:
        def __init__(self, ref, send, recv, piece):
            self.parts = [
                Gather(
                    mp,
                    lambda index, half=half: ref.at[
                        pl.ds(
                            pl.multiple_of(
                                (piece * ways + index) * seq_len + half * some_rows, some_rows
                            ),
                            some_rows,
                        )
                    ],
                    send,
                    recv,
                    (2 * piece + half) * ways,
                )
                for half in range(2)
            ]

        def start(self, half):
            self.parts[half].start()

        def relays(self):
            for part in self.parts:
                part.relays()

        def close(self):
            for part in self.parts:
                part.close()

        def drain(self):
            for part in self.parts:
                part.drain()

    def halves(ref, send, recv):
        return [Rows(ref, send, recv, piece) for piece in range(seqs)]

    chunk_cols = min(256, model)
    chunk_count = model // chunk_cols

    class Sums:
        def __init__(self, *refs):
            *self.refs, self.send, self.recv = refs

        def chunk(self, piece, chunk):
            cols = pl.ds(pl.multiple_of(chunk * chunk_cols, chunk_cols), chunk_cols)

            def blocks(ref, first):
                return lambda index: ref.at[
                    pl.ds(pl.multiple_of((index + first) * seq_len, seq_len), seq_len), cols
                ]

            firsts = (piece * ways, piece * far, piece * far)
            views = [blocks(ref, first) for ref, first in zip(self.refs, firsts)]
            return Scatter(mp, *views, self.send, self.recv, (piece * chunk_count + chunk) * ways)

        def total(self, piece, here):
            firsts = (piece * ways, piece * far, piece * far)
            views = [block_rows(ref, seq_len, first) for ref, first in zip(self.refs, firsts)]
            return Scatter(mp, *views, self.send, self.recv).total(here)

        def trade(self, piece, chunk):
            self.chunk(piece, chunk).trade_all()

        def hand_on(self, piece, chunk):
            scatter = self.chunk(piece, chunk)
            for step in range(1, far):
                scatter.pass_on(step)

        def every(self, act):
            def one(chunk, carry):
                act(chunk)
                return carry

            lax.fori_loop(0, chunk_count, one, 0)

        def hand_on_all(self, piece):
            self.every(lambda chunk: self.hand_on(piece, chunk))

        def arrive(self, piece):
            self.every(lambda chunk: self.chunk(piece, chunk).arrive())

        def drain(self, piece):
            self.every(lambda chunk: self.chunk(piece, chunk).drain())

        def products(self, piece, make):
            def one(chunk, carry):
                make(pl.ds(pl.multiple_of(chunk * chunk_cols, chunk_cols), chunk_cols))
                self.trade(piece, chunk)
                pl.when(chunk > 0)(lambda: self.hand_on(piece, chunk - 1))
                return carry

            lax.fori_loop(0, chunk_count, one, 0)

        def hand_on_last(self, piece):
            self.hand_on(piece, chunk_count - 1)

    many = ways * seq_len

    def turns(body, hooks=()):
        def one(piece, carry):
            def at(point):
                for place, when, action in hooks:
                    if when == point:
                        pl.when(piece == place)(action)

            base = pl.multiple_of(piece * many, many)
            body(piece, base, pl.ds(base, many), at)
            return carry

        lax.fori_loop(0, seqs, one, 0)

    def pairs(base, body):
        def one(pair, carry):
            first = pl.multiple_of(base + pair * (2 * seq_len), 2 * seq_len)
            body([pl.ds(pl.multiple_of(first + seq * seq_len, seq_len), seq_len) for seq in range(2)])
            return carry

        lax.fori_loop(0, far, one, 0)

    def chunks(total, body):
        step = min(256, total)
        lax.fori_loop(
            0,
            total // step,
            lambda turn, carry: (body(pl.ds(pl.multiple_of(turn * step, step), step)), carry)[1],
            0,
        )

    def later_pieces(gathers, point):
        hooks = []
        for piece in range(1, seqs):
            hooks.append((piece - 1, point, gathers[piece].relays))
            hooks.append((piece, "start", gathers[piece].close))
        return hooks

    chunk = R.tab.shape[1]
    pieces = -(-table_rows // chunk)

    def fetch(piece):
        rows = min(chunk, table_rows - piece * chunk)
        return pltpu.make_async_copy(
            R.table.at[pl.ds(piece * chunk, rows)],
            R.tab.at[piece % 2, pl.ds(0, rows)],
            R.tab_sem.at[piece % 2],
        )

    for piece in range(min(2, pieces)):
        fetch(piece).start()

    names_of_moments = [
        name + kind for name in ("w_in", "ln", "qkv", "out", "up", "down") for kind in ("_m", "_v")
    ]

    def moment(name):
        return pltpu.make_async_copy(
            getattr(R, name), getattr(R, name + "_here"), R.moment_sem.at[names_of_moments.index(name)]
        )

    tile_rows = R.tw.shape[1]
    tiles = table_rows // tile_rows

    shares_of = -(-tiles // ways)

    def share_tile(turn):
        return lax.min(turn * ways + mp.me, tiles - 1)

    def tile_of(turn):
        side = lax.rem(turn, 2)
        rows = pl.ds(pl.multiple_of(share_tile(turn) * tile_rows, tile_rows), tile_rows)
        return [
            pltpu.make_async_copy(source.at[rows], dest.at[side], R.tile_sem.at[2 * place + side])
            for place, (source, dest) in enumerate(
                ((R.table, R.tw), (R.table_m, R.tm), (R.table_v, R.tv))
            )
        ]

    eye = lax.broadcasted_iota(jnp.int32, (seq_len, seq_len), 0) == lax.broadcasted_iota(
        jnp.int32, (seq_len, seq_len), 1
    )
    id_rows = R.ids[...].astype(F32)
    ids = jnp.concatenate(
        [
            jnp.sum(jnp.where(eye, id_rows[seq : seq + 1, :], 0.0), 1, keepdims=True)
            for seq in range(seqs)
        ],
        0,
    )
    lane = lax.broadcasted_iota(jnp.int32, (tokens, 128), 1).astype(F32)
    low_end = lane * float(table_rows)
    owned = jnp.where((ids >= low_end) & (ids < low_end + float(table_rows)), 1.0, 0.0)
    before = jnp.where(
        lax.broadcasted_iota(jnp.int32, (tokens, tokens), 0)
        >= lax.broadcasted_iota(jnp.int32, (tokens, tokens), 1),
        1.0,
        0.0,
    )
    ranks = dot(before.astype(LOW), owned.astype(LOW))
    rank = jnp.sum(owned * ranks, 1, keepdims=True) - 1.0
    slot = jnp.sum(owned * lane, 1, keepdims=True) * cap + rank
    placed = jnp.where(lane == rank, 1.0, 0.0)
    upper = jnp.floor(ids * (1.0 / 256.0))
    lower = ids - upper * 256.0
    parts = jnp.concatenate([placed * upper, placed * lower, placed], 1).astype(LOW)
    asked = dot_tn(owned.astype(LOW), parts)
    asked = asked[:, :128] * 256.0 + asked[:, 128:256] + asked[:, 256:] - 1.0
    wide_ln = R.ln_params.shape[1]
    shares = R.ln_params[...].astype(LOW).astype(F32)
    if wide_ln < 128:
        shares = jnp.concatenate([shares, jnp.zeros((4, 128 - wide_ln), F32)], 1)
    for index in range(size):
        R.ask[index] = jnp.concatenate(
            [asked[index : index + 1, :], shares, jnp.zeros((3, 128), F32)], 0
        )
    R.idx[mp.me, dp.me] = R.ask[dp.me]

    def spread(part, first, second, extra, send, recv):
        blocks = [block_rows(ref, strip) for ref in (part, first, second)]
        return Scatter(dp, *blocks, send, recv, 0, extra)

    up = spread(R.wbf, R.up_first, R.up_second, R.up_extra, R.up_send, R.up_recv)
    down = spread(R.gdn, R.dn_first, R.dn_second, R.dn_extra, R.dn_send, R.dn_recv)
    first_w = spread(
        R.waf.at[:, : 3 * heads_w], R.wa_first, R.wa_second, R.wa_extra, R.ga_send, R.ga_recv
    )
    wo = SideScatter(
        dp,
        *[block_rows(ref, strip) for ref in (R.gwo, R.wo_second)],
        R.wo_first,
        R.wo_send,
        R.wo_recv,
    )
    small = Scatter(
        dp,
        *[of_index(ref) for ref in (R.gw, R.gw_first, R.gw_second)],
        R.gw_send,
        R.gw_recv,
        0,
        R.gw_extra,
    )
    for scatter in (up, down, first_w, small):
        scatter.clear()

    meet([mp], [dp])
    ask, ask_wait = far_copies(
        dp,
        lambda dest, source: (R.ask.at[dest], R.idx.at[mp.me, source]),
        R.ask_send,
        R.ask_recv,
    )
    for step in range(1, size):
        ask(step).start()

    mine_in = R.winf.at[mp.me]
    win = Gather(dp, block_rows(mine_in, rin), R.win_send, R.win_recv, 0, True)
    win_all = Gather(mp, of_index(R.winf), R.wim_send, R.wim_recv)
    wa = [
        Gather(dp, part_rows(R.waf, strip, piece * half_strip, half_strip), send, recv, 0, True)
        for piece, (send, recv) in enumerate(((R.wa_send, R.wa_recv), (R.wx_send, R.wx_recv)))
    ]
    wb = Gather(dp, block_rows(R.wbf, strip), R.wb_send, R.wb_recv, 0, True)
    wc = Gather(dp, part_rows(R.wcf, strip, 0, half_strip), R.wc_send, R.wc_recv, 0, True)
    wd = SideGather(dp, part_rows(R.wcf, strip, half_strip, half_strip), R.wd_send, R.wd_recv, 0, True)
    dxg = Gather(
        mp,
        lambda index: R.dx.at[:, pl.ds(pl.multiple_of(index * seq_len, seq_len), seq_len)],
        R.dx_send,
        R.dx_recv,
    )
    ag = halves(R.a, R.a_send, R.a_recv)
    cg = halves(R.c, R.c_send, R.c_recv)
    mg = halves(R.dmid_all, R.e_send, R.e_recv)

    mine_in[pl.ds(pl.multiple_of(dp.me * rin, rin), rin), :] = (
        R.w_in[:, pl.ds(pl.multiple_of(mp.me * quarter, quarter), quarter)]
        .astype(LOW)
        .astype(R.winf.dtype)
    )
    win.start()
    for part in range(3):
        R.waf[own_strip, part * heads_w : (part + 1) * heads_w] = R.w_qkv[part].astype(LOW)
    R.waf[own_strip, 3 * heads_w :] = R.w_out[...].T.astype(LOW)
    wa[0].start()
    wa[1].start_near()
    for name in names_of_moments:
        moment(name).start()

    for seq in range(seqs):
        level = jnp.full((seq_len, 1), R.levels[seq], jnp.int32).astype(F32) / (LEVELS - 1)
        R.sig[seq * seq_len : (seq + 1) * seq_len, :] = jnp.exp(level * jnp.log(SIGMA_TOP))

    def scale_at(here):
        sig = R.sig[here, :]
        return sig * lax.rsqrt(1.0 + sig * sig)

    for piece in range(seqs):
        here = rows_of(piece)

        def scale_cot(row, here=here, piece=piece):
            there = pl.ds(pl.multiple_of(mp.me * seq_len + row, some_rows), some_rows)
            R.dx[piece, there, :] = (R.cot[here(row), :].astype(F32) * scale_at(here(row))).astype(LOW)

        by_rows(scale_cot)
    dxg.start()
    R.wbf[own_strip, :] = R.w_up[...].astype(LOW)
    R.wcf[own_strip, :] = R.w_down[...].T.astype(LOW)
    wb.start_near()
    R.pick[...] = jnp.where(
        lax.broadcasted_iota(jnp.int32, (tokens, spots), 1).astype(F32) == slot, 1.0, 0.0
    ).astype(LOW)
    win.relays()

    ask_wait()
    small_eye = lax.broadcasted_iota(jnp.int32, (cap, 128), 0) == lax.broadcasted_iota(
        jnp.int32, (cap, 128), 1
    )

    def locate(index, carry):
        row = R.idx[mp.me, index][0:1, :]
        column = jnp.sum(jnp.where(small_eye, row, 0.0), 1, keepdims=True)
        local = column.astype(jnp.int32) - dp.me * table_rows
        R.loc[pl.ds(pl.multiple_of(index * cap, cap), cap), :] = jnp.broadcast_to(local, (cap, 128))
        return carry

    lax.fori_loop(0, size, locate, 0, unroll=True)
    win.close()
    win_all.start()
    found = None
    for piece in range(pieces):
        fetch(piece).wait()
        rows = min(chunk, table_rows - piece * chunk)
        if rows < chunk:
            R.tab[piece % 2, rows:, :] = jnp.zeros((chunk - rows, width), F32)
        hit = (
            lax.broadcasted_iota(jnp.int32, (spots, chunk), 1) + piece * chunk == R.loc[:, 0:1]
        )
        more = dot(jnp.where(hit, 1.0, 0.0).astype(LOW), R.tab[piece % 2].astype(LOW))
        found = more if found is None else found + more
        if piece + 2 < pieces:
            fetch(piece + 2).start()
    R.give[...] = found.astype(LOW)

    give, give_wait = far_copies(
        dp,
        lambda dest, source: (block_rows(R.give, cap)(dest), block_rows(R.got, cap)(source)),
        R.give_send,
        R.give_recv,
    )
    for step in range(1, size):
        give(step).start()
    R.got[mine, :] = R.give[mine, :]
    wa[1].start_far()
    win_all.relays()
    wa[0].relay(1)
    wa[0].relay(2)
    if wide_ln % 128 == 0:
        R.gains[...] = jnp.concatenate([R.idx[mp.me, index] for index in range(size)], 1)
    else:
        total = jnp.zeros((8, model), F32)
        for index in range(size):
            place = lax.broadcasted_iota(
                jnp.int32, (128, model), 1
            ) == index * wide_ln + lax.broadcasted_iota(jnp.int32, (128, model), 0)
            place = place & (lax.broadcasted_iota(jnp.int32, (128, model), 0) < wide_ln)
            total = total + dot(
                R.idx[mp.me, index].astype(LOW), jnp.where(place, 1.0, 0.0).astype(LOW)
            )
        R.gains[...] = total
    for step in range(3, dp.far):
        wa[0].relay(step)
    named = Gather(mp, of_index(R.idx), R.id_send, R.id_recv)

    give_wait()
    rows = dot(R.pick[...], R.got[...])
    R.rows[...] = rows.astype(LOW)
    sig = R.sig[...]
    unit = rows * lax.rsqrt(jnp.mean(rows * rows, -1, keepdims=True) + EPS_NORM)
    R.mixed[...] = ((unit + sig * R.noise[...].astype(F32)) * lax.rsqrt(1.0 + sig * sig)).astype(LOW)
    win_all.close()
    for index in range(ways):
        R.x0[:, index * quarter : (index + 1) * quarter] = dot(
            R.mixed[...], R.winf[index].astype(LOW)
        )

    for piece in range(seqs):
        here, there = rows_of(piece), own_rows(piece)

        def first_norm(row, here=here, there=there):
            normed, _ = norm_rows(R.x0[here(row), :])
            R.a[there(row), :] = (normed * R.gains[1:2, :] + R.gains[2:3, :]).astype(LOW)

        by_rows(first_norm, ag[piece].start)
    wa[1].relay(1)
    wb.start_far()
    for step in range(2, dp.far):
        wa[1].relay(step)
    dxg.relays()
    ag[0].relays()
    for gather in (*wa, ag[0]):
        gather.close()

    att = Sums(R.part, R.fold, R.fold_far, R.as_send, R.as_recv)
    dcs = Sums(R.part, R.fold, R.fold_far, R.cs_send, R.cs_recv)
    das = Sums(R.part, R.fold, R.fold_far, R.ds_send, R.ds_recv)
    out = Sums(R.c, R.first, R.second, R.os_send, R.os_recv)
    masks = head_masks(heads_w)

    all_rows = (heads_w // HD) * seq_len
    scale = HD ** (-0.5)

    def softmax(seq, row):
        scores = R.scores[seq, row : row + 64, :]
        raised = jnp.exp((scores - jnp.max(scores, -1, keepdims=True)) * scale)
        return raised * (1.0 / jnp.sum(raised, -1, keepdims=True))

    def attend(piece, base, here, at):
        at("start")
        for part in range(3):
            cols = slice(part * heads_w, (part + 1) * heads_w)
            R.qkv[here, cols] = dot(R.a[here, :], R.waf[:, cols]).astype(LOW)
        at("mid")

        def one(rows_at):
            for seq, rows in enumerate(rows_at):
                queries = spread_heads(R.qkv[rows, :heads_w], masks)
                R.scores[seq] = dot_nt(queries, R.qkv[rows, heads_w : 2 * heads_w])
            for seq, rows in enumerate(rows_at):
                for row in range(0, all_rows, 64):
                    R.probs[seq, row : row + 64, :] = softmax(seq, row).astype(LOW)
                seen = dot(R.probs[seq], R.qkv[rows, 2 * heads_w : 3 * heads_w])
                R.o[rows, :] = join_heads(seen, masks, seq_len).astype(LOW)

        pairs(base, one)
        at("late")

        def project(cols):
            R.part[here, cols] = dot_nt(R.o[here, :], R.waf[cols, 3 * heads_w :]).astype(LOW)

        def one_chunk(chunk, carry):
            project(pl.ds(pl.multiple_of(chunk * chunk_cols, chunk_cols), chunk_cols))
            att.trade(piece, chunk)
            return carry

        lax.fori_loop(0, chunk_count, one_chunk, 0)

    def second_norm(piece):
        here, there = rows_of(piece), own_rows(piece)
        att.arrive(piece)

        def norm(row):
            x1 = R.x0[here(row), :] + att.total(piece, pl.ds(row, some_rows))
            R.out[here(row), :] = x1
            normed, _ = norm_rows(x1)
            R.c[there(row), :] = (normed * R.gains[3:4, :] + R.gains[4:5, :]).astype(LOW)

        by_rows(norm, cg[piece].start)

    def first_wb():
        wb.relay(1)
        wd.start_near()
        wc.start_near()
        wc.start_far()

    def middle_wb():
        wb.relay(2)
        wd.start_far()

    def last_wb():
        wd.start_other()
        for step in range(3, dp.far):
            wb.relay(step)
        named.start()

    turns(
        attend,
        [
            *later_pieces(ag, "mid"),
            *[
                (piece + 1, "mid", functools.partial(att.hand_on_all, piece))
                for piece in range(seqs - 1)
            ],
            (0, "mid", first_wb),
            (0, "late", middle_wb),
            (1, "mid", last_wb),
        ],
    )
    att.hand_on_all(seqs - 1)
    wc.relay(1)
    for piece in range(seqs):
        second_norm(piece)
        if piece == 0:
            for gather in (*wa, *ag, dxg, win):
                gather.drain()
            for step in range(1, size):
                ask(step).wait_send()
    cg[0].relays()
    wc.relay(2)
    wb.close()
    named.relays()
    cg[0].close()
    for piece in range(seqs):
        att.drain(piece)

    def activate(piece, base, here, at):
        at("start")

        def some(cols):
            R.h[...] = dot(R.c[here, :], R.wbf[:, cols])

            def gelu(row):
                there = pl.ds(pl.multiple_of(base + row, 64), 64)
                h = R.h[pl.ds(row, 64), :]
                bell = jnp.exp(-0.5 * h * h)
                tail = normal_tail(jnp.abs(h), bell)
                gate = jnp.where(h >= 0.0, 1.0 - tail, tail)
                slope = gate + h * (bell * 0.3989422804014327)
                R.hb[there, cols] = (h * gate).astype(LOW)
                R.slope[there, cols] = slope.astype(LOW)

            strips(many, 64, gelu, 2)

        chunks(hidden, some)
        at("end")

    def last_wc():
        for step in range(3, dp.far):
            wc.relay(step)

    turns(activate, [*later_pieces(cg, "end"), (0, "end", last_wc), (seqs - 1, "end", wd.forward)])

    due = [(scatter, step) for scatter in (down, up) for step in range(1, dp.far)]

    def pass_due(number):
        for _ in range(min(number, len(due))):
            scatter, step = due.pop(0)
            scatter.pass_on(step)

    block = 2 * strip if (2 * strip) % 128 == 0 else min(256, model)

    def grads(make, trades):
        if block == 2 * strip:

            def turn_of(turn, carry):
                hi = up.turn_of(turn)
                make(pl.ds(pl.multiple_of(hi * block, block), block))
                for scatter in trades:
                    scatter.trade(hi)
                return carry

            lax.fori_loop(0, dp.far, turn_of, 0)
        else:
            strips(model, block, lambda col: make(pl.ds(col, block)))
            for scatter in trades:
                scatter.trade_all()

    def down_grads(cols):
        every = R.dx[:, :, cols]
        R.gdn[cols, :] = dot_tn(every.reshape(seqs * many, block), R.hb[...]).astype(LOW)

    def up_grads(cols):
        R.wbf[cols, :] = dot_tn(R.c[:, cols], R.dhb[...]).astype(LOW)

    dxg.close()
    grads(down_grads, (down,))
    named.close()
    groups = ways * size
    some, lanes_at = min(groups, 32), min(ways * spots, 512)
    for begin in range(0, ways * spots, lanes_at):
        spot = lax.broadcasted_iota(jnp.int32, (128, lanes_at), 1).astype(F32) + float(begin)
        block_no = jnp.floor((spot + 0.5) * (1.0 / cap))
        place = lax.broadcasted_iota(jnp.int32, (128, lanes_at), 0).astype(F32)
        spread_out = jnp.where(spot - block_no * cap == place, 1.0, 0.0).astype(LOW)
        named_row = jnp.zeros((1, lanes_at), F32)
        for first in range(0, groups, some):
            wanted = jnp.concatenate(
                [
                    R.idx[index // size, index % size][0:1, :] + 1.0
                    for index in range(first, first + some)
                ],
                0,
            )
            high = jnp.floor(wanted * (1.0 / 256.0))
            rest = wanted - 256.0 * high
            laid = dot(high.astype(LOW), spread_out) * 256.0 + dot(rest.astype(LOW), spread_out) - 1.0
            own_block = block_no[0:1, :] == float(first) + lax.broadcasted_iota(
                jnp.int32, (some, lanes_at), 0
            ).astype(F32)
            named_row = named_row + jnp.sum(jnp.where(own_block, laid, 0.0), 0, keepdims=True)
        R.named[:, begin : begin + lanes_at] = jnp.broadcast_to(
            named_row.astype(jnp.int32) - dp.me * table_rows, (8, lanes_at)
        )
    named.drain()
    wc.close()
    wd.close()
    for gather in (wb, *cg):
        gather.drain()

    def feed_back(piece, base, here, at):
        at("start")

        def some(cols):
            bent = dot(R.dx[piece], R.wcf[:, cols]) * R.slope[here, cols].astype(F32)
            R.dhb[here, cols] = bent.astype(LOW)

        chunks(hidden, some)
        at("mid")

        def project(cols):
            R.part[here, cols] = dot_nt(R.dhb[here, :], R.wbf[cols, :]).astype(LOW)

        dcs.products(piece, project)

    R.norms[...] = jnp.zeros_like(R.norms)

    def second_back(piece):
        here, there = rows_of(piece), own_rows(piece)
        dcs.arrive(piece)

        def back(row):
            dc = dcs.total(piece, pl.ds(row, some_rows))
            grad, unit = norm_back(R.out[here(row), :], R.gains[3:4, :], dc)
            grad = grad + R.cot[here(row), :].astype(F32) * scale_at(here(row))
            R.dmid[here(row), :] = grad
            R.dmid_all[there(row), :] = grad.astype(LOW)
            R.norms[2:3, :] += jnp.sum(dc * unit, 0, keepdims=True)
            R.norms[3:4, :] += jnp.sum(dc, 0, keepdims=True)

        by_rows(back, mg[piece].start)

    turns(
        feed_back,
        [
            *[
                (piece + 1, "mid", functools.partial(dcs.hand_on_last, piece))
                for piece in range(seqs - 1)
            ],
            (1, "mid", lambda: pass_due(1)),
        ],
    )
    dcs.hand_on_last(seqs - 1)
    second_back(0)
    pass_due(1)
    grads(up_grads, (up,))
    for piece in range(1, seqs):
        second_back(piece)
    pass_due(max(1, dp.far - 3))
    mg[0].relays()
    mg[0].close()
    for piece in range(seqs):
        dcs.drain(piece)

    def attend_back(piece, base, here, at):
        at("start")
        R.low[...] = dot(R.dmid_all[here, :], R.waf[:, 3 * heads_w :]).astype(LOW)
        at("mid")

        def one(rows_at):
            for seq, rows in enumerate(rows_at):
                queries = spread_heads(R.qkv[rows, :heads_w], masks)
                R.scores[seq] = dot_nt(queries, R.qkv[rows, heads_w : 2 * heads_w])
                upper_rows = pl.ds(pl.multiple_of(rows.start - base, seq_len), seq_len)
                R.upper[seq] = spread_heads(R.low[upper_rows, :], masks)
                R.dprobs[seq] = dot_nt(R.upper[seq], R.qkv[rows, 2 * heads_w : 3 * heads_w])
            for seq, rows in enumerate(rows_at):
                for row in range(0, all_rows, 64):
                    probs = softmax(seq, row)
                    grad_probs = R.dprobs[seq, row : row + 64, :]
                    inner = jnp.sum(probs * grad_probs, -1, keepdims=True)
                    R.probs[seq, row : row + 64, :] = probs.astype(LOW)
                    R.dscores[seq, row : row + 64, :] = (probs * (grad_probs - inner)).astype(LOW)
                keys = R.qkv[rows, heads_w : 2 * heads_w]
                queries = spread_heads(R.qkv[rows, :heads_w], masks)
                R.qkv[rows, 2 * heads_w : 3 * heads_w] = dot_tn(R.probs[seq], R.upper[seq]).astype(LOW)
                R.qkv[rows, heads_w : 2 * heads_w] = (dot_tn(R.dscores[seq], queries) * scale).astype(
                    LOW
                )
                R.qkv[rows, :heads_w] = (
                    join_heads(dot(R.dscores[seq], keys), masks, seq_len) * scale
                ).astype(LOW)

        pairs(base, one)
        at("late")

        def project(cols):
            R.part[here, cols] = dot_nt(R.qkv[here, :], R.waf[cols, : 3 * heads_w]).astype(LOW)

        das.products(piece, project)

    def first_back(piece):
        here = rows_of(piece)
        das.arrive(piece)

        def back(row):
            da = das.total(piece, pl.ds(row, some_rows))
            grad, unit = norm_back(R.x0[here(row), :], R.gains[1:2, :], da)
            R.dx0[here(row), :] = (R.dmid[here(row), :] + grad).astype(LOW)
            R.norms[0:1, :] += jnp.sum(da * unit, 0, keepdims=True)
            R.norms[1:2, :] += jnp.sum(da, 0, keepdims=True)

        by_rows(back)

    def out_grads():
        def make(cols):
            R.gwo[cols, :] = dot_tn(R.dmid_all[:, cols], R.o[...]).astype(LOW)

        grads(make, (wo,))

    turns(
        attend_back,
        [
            *later_pieces(mg, "mid"),
            (0, "late", lambda: pass_due(1)),
            *[
                (piece + 1, "mid", functools.partial(das.hand_on_last, piece))
                for piece in range(seqs - 1)
            ],
            (seqs - 1, "late", lambda: pass_due(1)),
        ],
    )
    das.hand_on_last(seqs - 1)
    def out_grads(cols):
        R.gwo[cols, :] = dot_tn(R.dmid_all[:, cols], R.o[...]).astype(LOW)

    def attend_grads(cols):
        R.waf[cols, : 3 * heads_w] = dot_tn(R.a[:, cols], R.qkv[...]).astype(LOW)

    grads(out_grads, ())
    wo.start()
    first_back(0)
    grads(attend_grads, (first_w,))
    for piece in range(1, seqs):
        first_back(piece)

    grad_mixed = sum(
        dot_nt(R.dx0[:, index * quarter : (index + 1) * quarter], R.winf[index].astype(LOW))
        for index in range(ways)
    )
    sig = R.sig[...]
    grad_unit = grad_mixed * lax.rsqrt(1.0 + sig * sig)
    rows = R.rows[...].astype(F32)
    inverse = lax.rsqrt(jnp.mean(rows * rows, -1, keepdims=True) + EPS_NORM)
    unit = rows * inverse
    grad_rows = inverse * (grad_unit - unit * jnp.mean(grad_unit * unit, -1, keepdims=True))
    for step in range(1, size):
        give(step).wait_send()
    R.give[...] = dot_tn(R.pick[...], grad_rows.astype(LOW)).astype(LOW)
    mine_inc = block_rows(R.inc, spots)(mp.me)
    back, back_wait = far_copies(
        dp,
        lambda dest, source: (block_rows(R.give, cap)(dest), block_rows(mine_inc, cap)(source)),
        R.back_send,
        R.back_recv,
    )
    for step in range(1, size):
        back(step).start()
    mine_inc[mine, :] = R.give[mine, :]

    small_mp = Scatter(
        mp, of_index(R.gm), of_index(R.gm_first), of_index(R.gm_second), R.gm_send, R.gm_recv
    )
    for index in range(ways):
        cols = slice(index * quarter, (index + 1) * quarter)
        R.gm[index, :width, :] = dot_tn(R.mixed[...], R.dx0[:, cols]).astype(LOW)
        R.gm[index, width:, :] = jnp.concatenate(
            [R.norms[0:4, cols], jnp.zeros((12, quarter), F32)], 0
        ).astype(LOW)
    small_mp.trade_all()
    pass_due(len(due))
    for step in range(1, far):
        small_mp.pass_on(step)

    def feed_out(piece, base, here, at):
        def project(cols):
            R.c[here, cols] = dot_nt(R.hb[here, :], R.wcf[cols, :]).astype(LOW)

        out.products(piece, project)

    turns(feed_out)
    wo.trade()
    first_w.pass_on(1)
    for turn in range(min(2, shares_of)):
        for one in tile_of(turn):
            one.start()
    back_wait()
    rows_in = Gather(mp, block_rows(R.inc, spots), R.in_send, R.in_recv)
    rows_in.start()
    for piece in range(seqs):
        out.hand_on_last(piece)

    small_mp.arrive()
    summed = small_mp.total(slice(None))
    for index in range(size):
        piece = summed[index * rin : (index + 1) * rin, :]
        if rin_up > rin:
            piece = jnp.concatenate([piece, jnp.zeros((rin_up - rin, quarter), F32)], 0)
        R.gw[index, :rin_up, :] = piece.astype(LOW)
        R.gw[index, rin_up:, :] = summed[width:, :].astype(LOW)
    small.trade_all()
    rows_in.relays()
    first_w.pass_on(2)

    def finish_out(piece):
        here = rows_of(piece)
        out.arrive(piece)

        def finish(row):
            R.out[here(row), :] = (
                R.out[here(row), :] + out.total(piece, pl.ds(row, some_rows))
            ) * scale_at(here(row))

        by_rows(finish)

    for piece in range(seqs):
        finish_out(piece)

    rows_in.close()

    once = jnp.where(mp.me == 0, 1.0, 0.0)
    lanes = lax.broadcasted_iota(jnp.int32, (1, 128), 1)
    R.sums[...] = jnp.zeros_like(R.sums)

    def put(place, squares, factor=None):
        for row, values in enumerate(squares):
            total = jnp.sum(jnp.sum(values, 0, keepdims=True), 1, keepdims=True)
            if factor is not None:
                total = total * factor
            R.sums[row : row + 1, :] += jnp.where(lanes == place, total, 0.0)

    def squares_of(weight, gradient, first, second):
        direction = direction_of(weight, gradient, first, second)[2]
        return weight * weight, direction * direction

    def folded(values):
        rows, columns = values.shape
        return jnp.sum(values.reshape(rows // 8, 8, columns), 0)

    def add_up(weight, gradient, first, second):
        squares = squares_of(weight[...], gradient[...], first[...], second[...])
        return [folded(values) for values in squares]

    zero = jnp.zeros((8, width), F32)

    rest = [
        functools.partial(scatter.pass_on, step)
        for scatter in (first_w, small)
        for step in range(1, dp.far)
    ][2:]
    tail_hooks = [
        (min(shares_of - 1, place * shares_of // len(rest)), action)
        for place, action in enumerate(rest)
    ]

    def add_tile(turn, carry):
        side = lax.rem(turn, 2)
        for place, action in tail_hooks:
            pl.when(turn == place)(action)
        for one in tile_of(turn):
            one.wait()
        hit = (
            lax.broadcasted_iota(jnp.int32, (tile_rows, ways * spots), 0)
            + share_tile(turn) * tile_rows
            == R.named[0:1, :]
        )
        gradient = dot(jnp.where(hit, 1.0, 0.0).astype(LOW), R.inc[...])
        more = add_up(R.tw.at[side], gradient, R.tm.at[side], R.tv.at[side])
        counts = jnp.where(turn * ways + mp.me < tiles, 1.0, 0.0)

        @pl.when(turn + 2 < shares_of)
        def _():
            for one in tile_of(turn + 2):
                one.start()

        return carry[0] + counts * more[0], carry[1] + counts * more[1]

    put(0, lax.fori_loop(0, shares_of, add_tile, (zero, zero)))

    for thing in (win_all, wc, wd, *mg, up, down, small_mp):
        thing.drain()
    for piece in range(seqs):
        out.drain(piece)
        das.drain(piece)
    for step in range(1, size):
        back(step).wait_send()

    for name in names_of_moments:
        moment(name).wait()
    up.arrive()

    R.red_up[...] = up.total(slice(None))
    put(10, add_up(R.w_up, R.red_up, R.up_m_here, R.up_v_here))
    down.arrive()

    R.red_dn[...] = down.total(slice(None)).T
    put(11, add_up(R.w_down, R.red_dn, R.down_m_here, R.down_v_here))
    wo.arrive()
    R.red_out[...] = wo.total().T
    put(9, add_up(R.w_out, R.red_out, R.out_m_here, R.out_v_here))

    small.arrive()
    R.wsum[mp.me] = small.total(slice(None)).astype(LOW)
    weights_in = Gather(mp, of_index(R.wsum), R.ws_send, R.ws_recv)
    weights_in.start()
    first_w.arrive()

    value = first_w.total(slice(None))
    for part in range(3):
        R.red_qkv[part] = value[:, part * heads_w : (part + 1) * heads_w]
    weights_in.relays()
    for part in range(3):
        put(
            6 + part,
            add_up(
                R.w_qkv.at[part], R.red_qkv.at[part], R.qkv_m_here.at[part], R.qkv_v_here.at[part]
            ),
        )
    weights_in.close()
    total = jnp.concatenate([R.wsum[index].astype(F32) for index in range(ways)], 1)
    R.red_in[...] = total[:rin, :]
    put(1, add_up(R.w_in, R.red_in, R.w_in_m_here, R.w_in_v_here), once)
    if strip % 128 == 0:
        R.lnsum[...] = total[rin_up : rin_up + 8, :]
        R.red_ln[...] = R.lnsum[0:4, pl.ds(pl.multiple_of(dp.me * strip, strip), strip)]
    else:
        chosen = lax.broadcasted_iota(jnp.int32, (model, strip), 0) == dp.me * strip + (
            lax.broadcasted_iota(jnp.int32, (model, strip), 1)
        )
        R.red_ln[...] = dot(
            total[rin_up : rin_up + 8, :].astype(LOW), jnp.where(chosen, 1.0, 0.0).astype(LOW)
        )[0:4]
    squares = squares_of(R.ln_params[...], R.red_ln[...], R.ln_m_here[...], R.ln_v_here[...])
    for row in range(4):
        put(2 + row, [values[row : row + 1, :] for values in squares], once)

    R.near[dp.me] = R.sums[...]
    near, near_wait = far_copies(
        dp, lambda dest, source: (R.near.at[dp.me], R.near.at[source]), R.near_send, R.near_recv
    )
    for step in range(1, size):
        near(step).start()
    near_wait()
    R.wide[mp.me] = jnp.sum(R.near[...], 0)
    far_off, far_off_wait = far_copies(
        mp, lambda dest, source: (R.wide.at[mp.me], R.wide.at[source]), R.wide_send, R.wide_recv
    )
    for step in range(1, ways):
        far_off(step).start()
    far_off_wait()
    R.totals[...] = jnp.sum(R.wide[...], 0)

    for thing in (wo, first_w, small, rows_in, weights_in):
        thing.drain()
    for step in range(1, size):
        near(step).wait_send()
    for step in range(1, ways):
        far_off(step).wait_send()


def run_layer(cap, ids, levels, noise, cot, weights, moments):
    table, w_in, ln_params, w_qkv, w_out, w_up, w_down = weights
    dp, mp = lax.axis_size("dp"), lax.axis_size("mp")
    seqs, seq_len = ids.shape
    tokens, width = noise.shape
    model = cot.shape[1]
    rin = w_in.shape[0]
    heads_w = w_qkv.shape[2]
    strip, hidden = w_up.shape
    group = tokens * mp
    spots = dp * cap
    wide = round_up(rin, 16) + 16
    far, far_dp = mp // 2, dp // 2
    quarter = model // mp
    in_kind = LOW if rin % 16 == 0 else F32
    tile_rows = max(rows for rows in range(8, 257, 8) if table.shape[0] % rows == 0)
    stacked = (heads_w // HD) * seq_len
    vmem = pl.BlockSpec(memory_space=pltpu.VMEM)
    outside = pl.BlockSpec(memory_space=pl.ANY)
    inputs = dict(
        ids=(ids, vmem),
        levels=(levels, pl.BlockSpec(memory_space=pltpu.SMEM)),
        noise=(noise, vmem),
        cot=(cot, vmem),
        table=(table, outside),
        w_in=(w_in, vmem),
        ln_params=(ln_params, vmem),
        w_qkv=(w_qkv, vmem),
        w_out=(w_out, vmem),
        w_up=(w_up, vmem),
        w_down=(w_down, vmem),
    )
    kept = {}
    for name, (first, second) in zip(("table", "w_in", "ln", "qkv", "out", "up", "down"), moments):
        inputs[name + "_m"] = (first, outside)
        inputs[name + "_v"] = (second, outside)
        if name != "table":
            kept[name + "_m_here"] = kept[name + "_v_here"] = (first.shape, F32)
    outputs = dict(
        out=((tokens, model), F32),
        red_up=((strip, hidden), F32),
        red_dn=((hidden, strip), F32),
        red_qkv=((3, strip, heads_w), F32),
        red_out=((heads_w, strip), F32),
        red_in=((rin, model), F32),
        red_ln=((4, strip), F32),
        inc=((mp * spots, width), LOW),
        named=((8, mp * spots), jnp.int32),
        totals=((8, 128), F32),
    )
    buffers = dict(
        tab=((2, round_up(table.shape[0] // 8, 128), width), F32),
        ask=((dp, 8, 128), F32),
        idx=((mp, dp, 8, 128), F32),
        loc=((spots, 128), jnp.int32),
        give=((spots, width), LOW),
        got=((spots, width), LOW),
        tw=((2, tile_rows, width), F32),
        tm=((2, tile_rows, width), F32),
        tv=((2, tile_rows, width), F32),
        sums=((8, 128), F32),
        near=((dp, 8, 128), F32),
        wide=((mp, 8, 128), F32),
        scores=((2, stacked, seq_len), F32),
        dprobs=((2, stacked, seq_len), F32),
        probs=((2, stacked, seq_len), LOW),
        dscores=((2, stacked, seq_len), LOW),
        upper=((2, stacked, heads_w), LOW),
        gwo=((model, heads_w), LOW),
        wo_first=((strip, heads_w), LOW),
        wo_second=((dp * strip, heads_w), LOW),
        gains=((8, model), F32),
        lnsum=((8, model), F32),
        sig=((tokens, 1), F32),
        pick=((tokens, spots), LOW),
        rows=((tokens, width), LOW),
        mixed=((tokens, width), LOW),
        x0=((tokens, model), F32),
        a=((group, model), LOW),
        c=((group, model), LOW),
        dx=((seqs, group // seqs, model), LOW),
        dmid=((tokens, model), F32),
        dmid_all=((group, model), LOW),
        winf=((mp, rin * dp, quarter), in_kind),
        waf=((model, 4 * heads_w), LOW),
        wbf=((model, hidden), LOW),
        wcf=((model, hidden), LOW),
        qkv=((group, 3 * heads_w), LOW),
        o=((group, heads_w), LOW),
        low=((group // seqs, heads_w), LOW),
        part=((group, model), LOW),
        first=((far * tokens, model), LOW),
        fold=((far * tokens, model), LOW),
        second=((far * tokens, model), LOW),
        fold_far=((far * tokens, model), LOW),
        h=((group // seqs, min(256, hidden)), F32),
        hb=((group, hidden), LOW),
        dhb=((group, hidden), LOW),
        slope=((group, hidden), LOW),
        gdn=((model, hidden), LOW),
        dx0=((tokens, model), LOW),
        norms=((8, model), F32),
        gm=((mp, width + 16, quarter), LOW),
        gm_first=((far, width + 16, quarter), LOW),
        gm_second=((far, width + 16, quarter), LOW),
        gw=((dp, wide, quarter), LOW),
        gw_first=((far_dp, wide, quarter), LOW),
        gw_second=((far_dp, wide, quarter), LOW),
        up_first=((far_dp * strip, hidden), LOW),
        up_second=((far_dp * strip, hidden), LOW),
        dn_first=((far_dp * strip, hidden), LOW),
        dn_second=((far_dp * strip, hidden), LOW),
        wa_first=((far_dp * strip, 3 * heads_w), LOW),
        wa_second=((far_dp * strip, 3 * heads_w), LOW),
        wsum=((mp, wide, quarter), LOW),
        up_extra=((strip, hidden), LOW),
        dn_extra=((strip, hidden), LOW),
        wa_extra=((strip, 3 * heads_w), LOW),
        gw_extra=((wide, quarter), LOW),
        **kept,
    )
    sems = dict(tab_sem=2, tile_sem=6, moment_sem=12)
    for name in (
        *("win", "wa", "wx", "wb", "wc", "wd", "ask", "give", "back"),
        *("up", "dn", "ga", "wo", "gw", "near"),
    ):
        sems[name + "_send"] = sems[name + "_recv"] = dp + 1
    for name in ("wim", "id", "in", "ws", "gm", "wide"):
        sems[name + "_send"] = sems[name + "_recv"] = mp
    for name in ("dx", "a", "c", "e"):
        sems[name + "_send"] = sems[name + "_recv"] = 2 * seqs * mp
    for name in ("as", "os", "cs", "ds"):
        sems[name + "_send"] = sems[name + "_recv"] = seqs * mp * (model // min(256, model))
    names = [*inputs, *outputs, *buffers, *sems]
    made = pl.pallas_call(
        functools.partial(layer_kernel, cap, names),
        out_shape=[jax.ShapeDtypeStruct(shape, kind) for shape, kind in outputs.values()],
        in_specs=[spec for _, spec in inputs.values()],
        out_specs=[vmem] * len(outputs),
        scratch_shapes=[
            *[pltpu.VMEM(shape, kind) for shape, kind in buffers.values()],
            *[pltpu.SemaphoreType.DMA((number,)) for number in sems.values()],
        ],
        compiler_params=pltpu.CompilerParams(
            vmem_limit_bytes=VMEM_BYTES, collective_id=1, has_side_effects=True
        ),
        name="layer",
    )(*[value for value, _ in inputs.values()])
    return dict(zip(outputs, made))


def direction_of(weight, gradient, first, second):
    first_new = BETA_ONE * first + (1.0 - BETA_ONE) * gradient
    second_new = BETA_TWO * second + (1.0 - BETA_TWO) * gradient * gradient
    second_hat = second_new * (1.0 / (1.0 - BETA_TWO**STEP))
    inverse = lax.rsqrt(second_hat)
    root = second_hat * inverse + EPS_ADAM
    inverse = inverse * (2.0 - root * inverse)
    inverse = inverse * (2.0 - root * inverse)
    direction = first_new * (1.0 / (1.0 - BETA_ONE**STEP)) * inverse + DECAY * weight
    return first_new, second_new, direction


def update_kernel(part, names, *refs):
    R = types.SimpleNamespace(**dict(zip(names, refs)))
    turn = pl.program_id(0)
    R.out_rows[...] = R.made[...]
    norms = jnp.sqrt(R.totals[...])
    R.norms[...] = norms[0:2, 0:12]
    factors = norms[0:1, :] / (norms[1:2, :] + EPS_ADAM) * RATE

    def piece(name, here, gradient, place, rows=slice(None)):
        weight = getattr(R, name)[here]
        first_new, second_new, direction = direction_of(
            weight, gradient, getattr(R, name + "_m")[here], getattr(R, name + "_v")[here]
        )
        if isinstance(place, int):
            factor = factors[0:1, place : place + 1]
        else:
            factor = jnp.concatenate([factors[0:1, one : one + 1] for one in place], 0)
        getattr(R, name + "_m_new")[here] = first_new
        getattr(R, name + "_v_new")[here] = second_new
        getattr(R, name + "_new")[here] = weight - factor * direction

    def update(name, gradient, place, lead=(), here=slice(None)):
        piece(name, (*lead, here, slice(None)), gradient, place)

    tile = R.table.shape[0]
    spots = R.named.shape[1]

    def table_part(row):
        hit = (
            lax.broadcasted_iota(jnp.int32, (part, spots), 0) + (turn * tile + row)
            == R.named[0:1, :]
        )
        gradient = dot(jnp.where(hit, 1.0, 0.0).astype(LOW), R.inc[...])
        update("table", gradient, 0, (), pl.ds(row, part))

    strips(tile, part, table_part)
    for group in range(3):
        update("qkv", R.red_qkv[group], 6 + group, (group,))
    update("up", R.red_up[...], 10)
    update("down", R.red_dn[...], 11)

    @pl.when(turn == 0)
    def _():
        update("out", R.red_out[...], 9)
        update("w_in", R.red_in[...], 1)
        piece("ln", (slice(None), slice(None)), R.red_ln[...], (2, 3, 4, 5))


def turns_of(rows, parts):
    return [
        turns
        for turns in (5, 4, 2, 1)
        if rows % (8 * turns) == 0 and all(size % (8 * turns) == 0 for size in parts)
    ][0]


def run_update(weights, moments, grads):
    names = ("table", "w_in", "ln", "qkv", "out", "up", "down")
    by_name = dict(zip(names, weights))
    rows, width = by_name["table"].shape
    strip, hidden = by_name["up"].shape
    heads_w = by_name["qkv"].shape[2]
    turns = turns_of(rows, (strip, hidden))
    tile = rows // turns
    part = max(size for size in range(8, 257, 8) if tile % size == 0)
    fixed = lambda array: pl.BlockSpec(array.shape, lambda turn: (0,) * array.ndim)
    specs = dict(
        table=pl.BlockSpec((tile, width), lambda turn: (turn, 0)),
        w_in=fixed(by_name["w_in"]),
        ln=fixed(by_name["ln"]),
        qkv=pl.BlockSpec((3, strip // turns, heads_w), lambda turn: (0, turn, 0)),
        out=fixed(by_name["out"]),
        up=pl.BlockSpec((strip // turns, hidden), lambda turn: (turn, 0)),
        down=pl.BlockSpec((hidden // turns, strip), lambda turn: (turn, 0)),
    )
    inputs = {}
    for name, weight, (first, second) in zip(names, weights, moments):
        inputs[name] = (weight, specs[name])
        inputs[name + "_m"] = (first, specs[name])
        inputs[name + "_v"] = (second, specs[name])
    for name, like in (
        ("red_up", "up"),
        ("red_dn", "down"),
        ("red_qkv", "qkv"),
        ("red_out", "out"),
        ("red_in", "w_in"),
        ("red_ln", "ln"),
    ):
        inputs[name] = (grads[name], specs[like])
    for name in ("inc", "named", "totals"):
        inputs[name] = (grads[name], fixed(grads[name]))
    tokens, model = grads["out"].shape
    rows_spec = pl.BlockSpec((tokens // turns, model), lambda turn: (turn, 0))
    inputs["made"] = (grads["out"], rows_spec)
    outputs = {"out_rows": (grads["out"].shape, rows_spec)}
    for name, weight in by_name.items():
        for kind in ("_new", "_m_new", "_v_new"):
            outputs[name + kind] = (weight.shape, specs[name])
    outputs["norms"] = ((2, 12), pl.BlockSpec((2, 12), lambda turn: (0, 0)))
    results = pl.pallas_call(
        functools.partial(update_kernel, part, [*inputs, *outputs]),
        grid=(turns,),
        out_shape=[jax.ShapeDtypeStruct(shape, F32) for shape, _ in outputs.values()],
        in_specs=[spec for _, spec in inputs.values()],
        out_specs=[spec for _, spec in outputs.values()],
        compiler_params=pltpu.CompilerParams(vmem_limit_bytes=VMEM_BYTES),
        name="update",
    )(*[value for value, _ in inputs.values()])
    return list(results)


def per_device(
    token_ids,
    levels,
    noise,
    cotangent,
    table,
    table_m,
    table_v,
    w_in,
    w_in_m,
    w_in_v,
    ln_params,
    ln_m,
    ln_v,
    w_qkv,
    qkv_m,
    qkv_v,
    w_out,
    out_m,
    out_v,
    w_up,
    up_m,
    up_v,
    w_down,
    down_m,
    down_v,
):
    dp_count = lax.axis_size("dp")
    seq_count, seq_len = token_ids.shape
    tokens = seq_count * seq_len
    model = cotangent.shape[2]
    cap = round_up(max(2, (3 * tokens + 2 * dp_count - 1) // (2 * dp_count)), 16)
    weights = (table, w_in, ln_params, w_qkv, w_out, w_up, w_down)
    moments = (
        (table_m, table_v),
        (w_in_m, w_in_v),
        (ln_m, ln_v),
        (qkv_m, qkv_v),
        (out_m, out_v),
        (up_m, up_v),
        (down_m, down_v),
    )
    grads = run_layer(
        cap,
        token_ids,
        levels,
        noise.reshape(tokens, -1),
        cotangent.reshape(tokens, model),
        weights,
        moments,
    )
    out, *results = run_update(weights, moments, grads)
    return (out.reshape(seq_count, seq_len, model), *results)


def solution(mesh):
    return jax.shard_map(
        per_device,
        mesh=mesh,
        in_specs=(
            P(("dp", "mp"), None),
            P(("dp", "mp")),
            P(("dp", "mp"), None, None),
            P(("dp", "mp"), None, None),
            P("dp", None),
            P("dp", None),
            P("dp", None),
            P("dp", None),
            P("dp", None),
            P("dp", None),
            P(None, "dp"),
            P(None, "dp"),
            P(None, "dp"),
            P(None, "dp", "mp"),
            P(None, "dp", "mp"),
            P(None, "dp", "mp"),
            P("mp", "dp"),
            P("mp", "dp"),
            P("mp", "dp"),
            P("dp", "mp"),
            P("dp", "mp"),
            P("dp", "mp"),
            P("mp", "dp"),
            P("mp", "dp"),
            P("mp", "dp"),
        ),
        out_specs=(
            P(("dp", "mp"), None, None),
            P("dp", None),
            P("dp", None),
            P("dp", None),
            P("dp", None),
            P("dp", None),
            P("dp", None),
            P(None, "dp"),
            P(None, "dp"),
            P(None, "dp"),
            P(None, "dp", "mp"),
            P(None, "dp", "mp"),
            P(None, "dp", "mp"),
            P("mp", "dp"),
            P("mp", "dp"),
            P("mp", "dp"),
            P("dp", "mp"),
            P("dp", "mp"),
            P("dp", "mp"),
            P("mp", "dp"),
            P("mp", "dp"),
            P("mp", "dp"),
            P(),
        ),
        check_vma=False,
    )
```

```python
import functools
import types

import jax
import jax.numpy as jnp
from jax import lax
from jax.experimental import pallas as pl
from jax.experimental.pallas import tpu as pltpu
from jax.sharding import PartitionSpec as P

HD = 64
LEVELS = 64
STEP = 10


EPS_NORM = 1e-06
EPS_LAYER = 1e-05
EPS_ADAM = 1e-06
BETA_ONE = 0.9
BETA_TWO = 0.999
DECAY = 0.01
RATE = 0.5
SIGMA_TOP = 10.0

F32 = jnp.float32
LOW = jnp.bfloat16
VMEM_BYTES = 63 * 1024 * 1024


def sigma_of(levels):
    frac = levels.astype(jnp.float32) / (LEVELS - 1)
    return jnp.exp(frac * jnp.log(SIGMA_TOP))


def lamb_moments(weight, gradient, first, second):
    first_new = BETA_ONE * first + (1.0 - BETA_ONE) * gradient
    second_new = BETA_TWO * second + (1.0 - BETA_TWO) * gradient * gradient
    first_hat = first_new / (1.0 - BETA_ONE**STEP)
    second_hat = second_new / (1.0 - BETA_TWO**STEP)
    direction = first_hat / (jnp.sqrt(second_hat) + EPS_ADAM) + DECAY * weight
    return (first_new, second_new, direction)


def trust_factors(ratio):
    return (
        ratio[0],
        ratio[1],
        ratio[2:6][:, None],
        ratio[6:9][:, None, None],
        ratio[9],
        ratio[10],
        ratio[11],
    )


def round_up(value, step):
    return -(-value // step) * step


def dot(left, right):
    return jnp.dot(left, right, preferred_element_type=F32)


def dot_nt(left, right):
    return lax.dot_general(left, right, (((1,), (1,)), ((), ())), preferred_element_type=F32)


def dot_tn(left, right):
    return lax.dot_general(left, right, (((0,), (0,)), ((), ())), preferred_element_type=F32)


def strips(total, step, body, unroll=1):
    step = min(step, total)

    def one(turn, carry):
        body(pl.multiple_of(turn * step, step))
        return carry

    lax.fori_loop(0, total // step, one, 0, unroll=unroll)


class Line:
    def __init__(self, axis):
        self.axis = axis
        self.size = lax.axis_size(axis)
        self.far = self.size // 2
        self.me = lax.axis_index(axis)
        self.hi = lax.div(self.me, 2)
        self.lo = lax.rem(self.me, 2)
        self.partner = self.hi * 2 + (1 - self.lo)

    def at(self, step):
        return lax.rem(self.hi + step + self.far, self.far)

    def push(self, index, src, dst, send, recv):
        return pltpu.make_async_remote_copy(
            src_ref=src,
            dst_ref=dst,
            send_sem=send,
            recv_sem=recv,
            device_id={self.axis: index},
            device_id_type=pl.DeviceIdType.MESH,
        )

    def signal(self, sem, index):
        pl.semaphore_signal(
            sem, inc=1, device_id={self.axis: index}, device_id_type=pl.DeviceIdType.MESH
        )


def meet(pair_lines, all_lines=()):
    sem = pltpu.get_barrier_semaphore()
    count = 0
    for line in pair_lines:
        for step in range(1, line.far):
            line.signal(sem, line.at(step) * 2 + line.lo)
            count += 1
        line.signal(sem, line.partner)
        count += 1
    for line in all_lines:
        for step in range(1, line.size):
            line.signal(sem, lax.rem(line.me + step, line.size))
            count += 1
    pl.semaphore_wait(sem, count)


class Gather:
    def __init__(self, line, at, send, recv, base=0, ends=False):
        self.line, self.at, self.send, self.recv, self.base = line, at, send, recv, base
        self.ends = ends and line.far == 4

    def source(self, step):
        line = self.line
        if not self.ends:
            return line.at(-step)
        order = ((1, 2, 3), (0, 3, 2), (3, 0, 1), (2, 1, 0))
        hi = order[3][step - 1]
        for place in (2, 1, 0):
            hi = jnp.where(line.hi == place, order[place][step - 1], hi)
        return hi

    def far_sends(self, act):
        line = self.line
        for step in range(1, line.far):
            one = self.copy(line.me, step - 1, line.at(step) * 2 + line.lo)
            if self.ends and step != 2:
                pl.when(line.hi != (3 if step == 1 else 0))(functools.partial(act, one))
            else:
                act(one)

    def to_end(self, act):
        line = self.line
        dest = jnp.where(line.hi == 1, 0, 3)
        one = self.copy((3 - dest) * 2 + line.lo, 2 * line.far - 1, dest * 2 + line.lo)
        pl.when((line.hi == 1) | (line.hi == 2))(functools.partial(act, one))

    def copy(self, index, slot, dest):
        block = self.at(index)
        return self.line.push(
            dest, block, block, self.send.at[self.base + slot], self.recv.at[self.base + index]
        )

    def start_far(self):
        self.far_sends(lambda one: one.start())

    def start_near(self):
        self.copy(self.line.me, self.line.far - 1, self.line.partner).start()

    def start(self):
        self.start_far()
        self.start_near()

    def relay(self, step):
        line = self.line
        handed = self.copy(self.source(step) * 2 + line.lo, line.far - 1 + step, line.partner)
        handed.wait_recv()
        if self.ends and step == 2:
            self.to_end(lambda one: one.start())
        handed.start()

    def relays(self):
        for step in range(1, self.line.far):
            self.relay(step)

    def close(self):
        line = self.line
        for step in range(line.far):
            self.copy(line.at(-step) * 2 + (1 - line.lo), 0, line.partner).wait_recv()

    def drain(self):
        self.far_sends(lambda one: one.wait_send())
        if self.ends:
            self.to_end(lambda one: one.wait_send())
        for slot in range(self.line.far - 1, 2 * self.line.far - 1):
            self.copy(self.line.me, slot, self.line.partner).wait_send()


class SideGather(Gather):
    def other(self, act):
        line = self.line
        for step in range(1, line.far):
            one = self.copy(line.partner, line.far - 1 + step, line.at(step) * 2 + line.lo)
            if self.ends and step != 2:
                pl.when(line.hi != (3 if step == 1 else 0))(functools.partial(act, one))
            else:
                act(one)

    def to_ends(self, parity, slot, act):
        line = self.line
        dest = jnp.where(line.hi == 1, 0, 3)
        one = self.copy((3 - dest) * 2 + parity, slot, dest * 2 + line.lo)
        pl.when((line.hi == 1) | (line.hi == 2))(functools.partial(act, one))

    def start_other(self):
        self.copy(self.line.partner, 0, self.line.partner).wait_recv()
        self.other(lambda one: one.start())

    def taken(self, step):
        line = self.line
        for parity, slot in ((line.lo, 2 * line.far - 1), (1 - line.lo, 2 * line.far)):
            self.copy(self.source(step) * 2 + parity, 0, line.partner).wait_recv()
            if self.ends and step == 2:
                self.to_ends(parity, slot, lambda one: one.start())

    def forward(self):
        if self.line.far > 2:
            self.taken(2)

    def close(self):
        for step in range(1, self.line.far):
            if step != 2:
                self.taken(step)

    def drain(self):
        line = self.line
        self.far_sends(lambda one: one.wait_send())
        self.copy(line.me, line.far - 1, line.partner).wait_send()
        self.other(lambda one: one.wait_send())
        if self.ends:
            for parity, slot in ((line.lo, 2 * line.far - 1), (1 - line.lo, 2 * line.far)):
                self.to_ends(parity, slot, lambda one: one.wait_send())


class SideScatter:
    def __init__(self, line, part, second, first, send, recv):
        self.line, self.part, self.second, self.first = line, part, second, first
        self.send, self.recv = send, recv

    def far_copy(self, step, parity):
        line = self.line
        hi = line.at(step)
        return line.push(
            hi * 2 + line.lo,
            self.part(hi * 2 + parity),
            self.second(parity * line.far + line.hi),
            self.send.at[2 * (step - 1) + parity],
            self.recv.at[parity * line.far + line.hi],
        )

    def near_copy(self):
        line = self.line
        return line.push(
            line.partner,
            self.part(line.partner),
            self.first,
            self.send.at[2 * line.far - 2],
            self.recv.at[2 * line.far],
        )

    def start(self):
        for step in range(1, self.line.far):
            for parity in range(2):
                self.far_copy(step, parity).start()

    def sum_of(self, parity):
        line = self.line
        value = self.part(line.hi * 2 + parity)[...].astype(F32)
        for step in range(1, line.far):
            index = parity * line.far + line.at(-step)
            block = self.second(index)
            line.push(
                line.partner, block, block, self.send.at[0], self.recv.at[index]
            ).wait_recv()
            value = value + block[...].astype(F32)
        return value

    def trade(self):
        given = self.part(self.line.partner)
        given[...] = self.sum_of(1 - self.line.lo).astype(LOW)
        self.near_copy().start()

    def arrive(self):
        pass

    def total(self):
        value = self.sum_of(self.line.lo)
        self.near_copy().wait_recv()
        return value + self.first[...].astype(F32)

    def drain(self):
        for step in range(1, self.line.far):
            for parity in range(2):
                self.far_copy(step, parity).wait_send()
        self.near_copy().wait_send()


class Scatter:
    def __init__(self, line, part, first, second, send, recv, base=0, extra=None):
        self.line, self.part, self.first, self.second = line, part, first, second
        self.send, self.recv, self.base = send, recv, base
        self.extra = extra if line.far == 4 else None

    def clear(self):
        line = self.line
        if self.extra is not None:

            @pl.when((line.hi == 0) | (line.hi == 3))
            def _():
                slot = self.second(3 - line.hi)
                slot[...] = jnp.zeros(slot.shape, LOW)

    def order(self, step):
        line = self.line
        if self.extra is None:
            return line.at(step)
        table = ((3, 2, 1), (2, 0, 3), (1, 3, 0), (0, 1, 2))
        hi = table[3][step - 1]
        for place in (2, 1, 0):
            hi = jnp.where(line.hi == place, table[place][step - 1], hi)
        return hi

    def traded(self, hi):
        line = self.line
        return line.push(
            line.partner,
            self.part(hi * 2 + (1 - line.lo)),
            self.first(hi),
            self.send.at[self.base + hi],
            self.recv.at[self.base + hi],
        )

    def passed(self, step):
        line = self.line
        hi = self.order(step)
        return line.push(
            hi * 2 + line.lo,
            self.part(hi * 2 + line.lo),
            self.second(line.hi),
            self.send.at[self.base + line.far + step - 1],
            self.recv.at[self.base + line.far + line.hi],
        )

    def to_next(self):
        line = self.line
        return line.push(
            jnp.where(line.hi < 2, 1, 2) * 2 + line.lo,
            self.part((3 - jnp.where(line.hi < 2, 0, 3)) * 2 + line.lo),
            self.extra,
            self.send.at[self.base + line.far],
            self.recv.at[self.base + 2 * line.far],
        )

    def turn_of(self, turn):
        line = self.line
        if self.extra is None:
            return lax.rem(line.hi + turn + 1, line.far)
        hi = line.hi
        for step in range(1, line.far):
            hi = jnp.where(turn == step - 1, self.order(step), hi)
        return hi

    def is_end(self):
        return (self.line.hi == 0) | (self.line.hi == 3)

    def trade(self, hi):
        self.traded(hi).start()

    def trade_all(self):
        for step in range(1, self.line.far + 1):
            self.trade(self.order(step) if step < self.line.far else self.line.hi)

    def pass_on(self, step):
        line = self.line
        hi = self.order(step)
        self.traded(hi).wait_recv()
        mine, other = self.part(hi * 2 + line.lo), self.first(hi)
        if self.extra is None or step == 2:
            mine[...] = (mine[...].astype(F32) + other[...].astype(F32)).astype(LOW)
            self.passed(step).start()
        elif step == 1:
            mine[...] = (mine[...].astype(F32) + other[...].astype(F32)).astype(LOW)

            @pl.when(self.is_end())
            def _():
                self.to_next().start()

            @pl.when(jnp.logical_not(self.is_end()))
            def _():
                self.passed(step).start()
        else:

            @pl.when(self.is_end())
            def _():
                mine[...] = (mine[...].astype(F32) + other[...].astype(F32)).astype(LOW)

            @pl.when(jnp.logical_not(self.is_end()))
            def _():
                line.push(
                    line.partner,
                    self.extra,
                    self.extra,
                    self.send.at[self.base],
                    self.recv.at[self.base + 2 * line.far],
                ).wait_recv()
                mine[...] = (
                    mine[...].astype(F32) + other[...].astype(F32) + self.extra[...].astype(F32)
                ).astype(LOW)

            self.passed(step).start()

    def arrive(self):
        line = self.line
        self.traded(line.hi).wait_recv()
        for step in range(1, line.far):
            hi = line.at(-step)
            one = line.push(
                line.partner,
                self.second(hi),
                self.second(hi),
                self.send.at[self.base],
                self.recv.at[self.base + line.far + hi],
            )
            if self.extra is None:
                one.wait_recv()
            else:
                pl.when(jnp.logical_not(self.is_end()) | (hi + line.hi != 3))(one.wait_recv)

    def total(self, here):
        line = self.line
        value = self.part(line.me)[here, :].astype(F32) + self.first(line.hi)[here, :].astype(F32)
        for step in range(1, line.far):
            value = value + self.second(line.at(-step))[here, :].astype(F32)
        return value

    def drain(self):
        line = self.line
        for step in range(line.far):
            self.traded(line.at(step)).wait_send()
        for step in range(1, line.far):
            if self.extra is not None and step == 1:
                pl.when(self.is_end())(lambda: self.to_next().wait_send())
                pl.when(jnp.logical_not(self.is_end()))(lambda: self.passed(1).wait_send())
            else:
                self.passed(step).wait_send()


def block_rows(ref, rows, first=0):
    return lambda index: ref.at[pl.ds(pl.multiple_of((index + first) * rows, rows), rows)]


def part_rows(ref, rows, first, count):
    return lambda index: ref.at[pl.ds(pl.multiple_of(index * rows + first, count), count)]


def of_index(ref):
    return lambda index: ref.at[index]


def norm_rows(values):
    center = values - jnp.mean(values, -1, keepdims=True)
    spread = jnp.mean(center * center, -1, keepdims=True)
    inverse = lax.rsqrt(spread + EPS_LAYER)
    return center * inverse, inverse


def norm_back(values, gain, grad):
    unit, inverse = norm_rows(values)
    inner = grad * gain
    shared = jnp.mean(inner, -1, keepdims=True)
    along = jnp.mean(inner * unit, -1, keepdims=True)
    return inverse * (inner - shared - unit * along), unit


def head_masks(width):
    lane = lax.broadcasted_iota(jnp.int32, (1, width), 1)
    return [
        jnp.where((lane >= head * HD) & (lane < (head + 1) * HD), 1.0, 0.0)
        for head in range(width // HD)
    ]


def spread_heads(values, masks):
    return jnp.concatenate([values * mask.astype(LOW) for mask in masks], 0)


def join_heads(values, masks, rows):
    total = values[0:rows] * masks[0]
    for head in range(1, len(masks)):
        total = total + values[head * rows : (head + 1) * rows] * masks[head]
    return total


TAIL = (
    0.2256758632450557,
    0.22566952478278277,
    0.2078438574180613,
    0.16853390514724884,
    0.14146086231844687,
    -0.005667717379728321,
    0.16915486959066833,
    -0.18294364197603524,
    0.05027260226320005,
)


def normal_tail(size, bell):
    base = 1.0 + (0.4 * 0.5**0.5) * size
    t = pl.reciprocal(base, approx=True)
    t = t * (2.0 - base * t)
    t = t * (2.0 - base * t)
    value = jnp.full_like(t, 0.5 * TAIL[-1])
    for factor in TAIL[-2::-1]:
        value = value * t + 0.5 * factor
    return value * t * bell


def far_copies(line, make, sends, recvs):
    def copy(step):
        dest = lax.rem(line.me + step, line.size)
        src, dst = make(dest, line.me)
        return line.push(dest, src, dst, sends.at[step], recvs.at[line.me])

    def wait():
        for step in range(1, line.size):
            source = lax.rem(line.me + line.size - step, line.size)
            _, dst = make(source, source)
            line.push(line.partner, dst, dst, sends.at[0], recvs.at[source]).wait_recv()

    return copy, wait


def layer_kernel(cap, names, *refs):
    R = types.SimpleNamespace(**dict(zip(names, refs)))
    dp, mp = Line("dp"), Line("mp")
    size, ways = dp.size, mp.size
    seqs, seq_len = R.ids.shape
    tokens, width = R.noise.shape
    model = R.cot.shape[1]
    heads_w = R.o.shape[1]
    hidden = R.wbf.shape[1]
    table_rows = R.table.shape[0]
    rin = R.w_in.shape[0]
    rin_up = round_up(rin, 16)
    quarter = model // ways
    strip = R.w_up.shape[0]
    spots = size * cap
    far = mp.far
    count = seqs * far
    half_strip = strip // 2
    own_strip = pl.ds(pl.multiple_of(dp.me * strip, strip), strip)
    mine = pl.ds(pl.multiple_of(dp.me * cap, cap), cap)

    some_rows = seq_len // 2

    def rows_of(piece):
        return lambda row: pl.ds(pl.multiple_of(piece * seq_len + row, some_rows), some_rows)

    def own_rows(piece):
        first = pl.multiple_of((piece * ways + mp.me) * seq_len, seq_len)
        return lambda row: pl.ds(pl.multiple_of(first + row, some_rows), some_rows)

    def by_rows(body, after=lambda half: None):
        for half in range(2):
            body(half * some_rows)
            after(half)

    class Rows:
        def __init__(self, ref, send, recv, piece):
            self.parts = [
                Gather(
                    mp,
                    lambda index, half=half: ref.at[
                        pl.ds(
                            pl.multiple_of(
                                (piece * ways + index) * seq_len + half * some_rows, some_rows
                            ),
                            some_rows,
                        )
                    ],
                    send,
                    recv,
                    (2 * piece + half) * ways,
                )
                for half in range(2)
            ]

        def start(self, half):
            self.parts[half].start()

        def relays(self):
            for part in self.parts:
                part.relays()

        def close(self):
            for part in self.parts:
                part.close()

        def drain(self):
            for part in self.parts:
                part.drain()

    def halves(ref, send, recv):
        return [Rows(ref, send, recv, piece) for piece in range(seqs)]

    chunk_cols = min(256, 262144 // (seqs * ways * seq_len))
    chunk_count = model // chunk_cols

    class Sums:
        def __init__(self, *refs):
            *self.refs, self.send, self.recv = refs

        def chunk(self, piece, chunk):
            cols = pl.ds(pl.multiple_of(chunk * chunk_cols, chunk_cols), chunk_cols)

            def blocks(ref, first):
                return lambda index: ref.at[
                    pl.ds(pl.multiple_of((index + first) * seq_len, seq_len), seq_len), cols
                ]

            firsts = (piece * ways, piece * far, piece * far)
            views = [blocks(ref, first) for ref, first in zip(self.refs, firsts)]
            return Scatter(mp, *views, self.send, self.recv, (piece * chunk_count + chunk) * ways)

        def total(self, piece, here):
            firsts = (piece * ways, piece * far, piece * far)
            views = [block_rows(ref, seq_len, first) for ref, first in zip(self.refs, firsts)]
            return Scatter(mp, *views, self.send, self.recv).total(here)

        def trade(self, chunk):
            for piece in range(seqs):
                self.chunk(piece, chunk).trade_all()

        def hand_on(self, chunk):
            for piece in range(seqs):
                scatter = self.chunk(piece, chunk)
                for step in range(1, far):
                    scatter.pass_on(step)

        def every(self, act):
            def one(chunk, carry):
                act(chunk)
                return carry

            lax.fori_loop(0, chunk_count, one, 0)

        def hand_on_all(self):
            self.every(self.hand_on)

        def arrive(self, piece):
            self.every(lambda chunk: self.chunk(piece, chunk).arrive())

        def drain(self, piece):
            self.every(lambda chunk: self.chunk(piece, chunk).drain())

        def products(self, make):
            def one(chunk, carry):
                make(pl.ds(pl.multiple_of(chunk * chunk_cols, chunk_cols), chunk_cols))
                self.trade(chunk)
                pl.when(chunk > 0)(lambda: self.hand_on(chunk - 1))
                return carry

            lax.fori_loop(0, chunk_count, one, 0)

        def hand_on_last(self):
            self.hand_on(chunk_count - 1)

    group = seqs * ways * seq_len
    col_step = min(256, 262144 // group)

    def pairs(body, hooks):
        def one(pair, carry):
            for place, action in hooks:
                pl.when(pair == place)(action)
            first = pl.multiple_of(pair * (2 * seq_len), 2 * seq_len)
            body([pl.ds(pl.multiple_of(first + seq * seq_len, seq_len), seq_len) for seq in range(2)])
            return carry

        lax.fori_loop(0, group // (2 * seq_len), one, 0)

    def chunks(total, body, hooks=()):
        step = min(col_step, total)

        def one(turn, carry):
            for place, action in hooks:
                pl.when(turn == place)(action)
            body(pl.ds(pl.multiple_of(turn * step, step), step))
            return carry

        lax.fori_loop(0, total // step, one, 0)

    chunk = R.tab.shape[1]
    pieces = -(-table_rows // chunk)

    def fetch(piece):
        rows = min(chunk, table_rows - piece * chunk)
        return pltpu.make_async_copy(
            R.table.at[pl.ds(piece * chunk, rows)],
            R.tab.at[piece % 2, pl.ds(0, rows)],
            R.tab_sem.at[piece % 2],
        )

    for piece in range(min(2, pieces)):
        fetch(piece).start()

    names_of_moments = [
        name + kind for name in ("w_in", "ln", "qkv", "out", "up", "down") for kind in ("_m", "_v")
    ]

    def moment(name):
        return pltpu.make_async_copy(
            getattr(R, name), getattr(R, name + "_here"), R.moment_sem.at[names_of_moments.index(name)]
        )

    tile_rows = R.tw.shape[1]
    tiles = table_rows // tile_rows

    shares_of = -(-tiles // ways)

    def share_tile(turn):
        return lax.min(turn * ways + mp.me, tiles - 1)

    def tile_of(turn):
        side = lax.rem(turn, 2)
        rows = pl.ds(pl.multiple_of(share_tile(turn) * tile_rows, tile_rows), tile_rows)
        return [
            pltpu.make_async_copy(source.at[rows], dest.at[side], R.tile_sem.at[2 * place + side])
            for place, (source, dest) in enumerate(
                ((R.table, R.tw), (R.table_m, R.tm), (R.table_v, R.tv))
            )
        ]

    eye = lax.broadcasted_iota(jnp.int32, (seq_len, seq_len), 0) == lax.broadcasted_iota(
        jnp.int32, (seq_len, seq_len), 1
    )
    id_rows = R.ids[...].astype(F32)
    ids = jnp.concatenate(
        [
            jnp.sum(jnp.where(eye, id_rows[seq : seq + 1, :], 0.0), 1, keepdims=True)
            for seq in range(seqs)
        ],
        0,
    )
    lane = lax.broadcasted_iota(jnp.int32, (tokens, 128), 1).astype(F32)
    low_end = lane * float(table_rows)
    owned = jnp.where((ids >= low_end) & (ids < low_end + float(table_rows)), 1.0, 0.0)
    before = jnp.where(
        lax.broadcasted_iota(jnp.int32, (tokens, tokens), 0)
        >= lax.broadcasted_iota(jnp.int32, (tokens, tokens), 1),
        1.0,
        0.0,
    )
    ranks = dot(before.astype(LOW), owned.astype(LOW))
    rank = jnp.sum(owned * ranks, 1, keepdims=True) - 1.0
    slot = jnp.sum(owned * lane, 1, keepdims=True) * cap + rank
    placed = jnp.where(lane == rank, 1.0, 0.0)
    upper = jnp.floor(ids * (1.0 / 256.0))
    lower = ids - upper * 256.0
    parts = jnp.concatenate([placed * upper, placed * lower, placed], 1).astype(LOW)
    asked = dot_tn(owned.astype(LOW), parts)
    asked = asked[:, :128] * 256.0 + asked[:, 128:256] + asked[:, 256:] - 1.0
    wide_ln = R.ln_params.shape[1]
    shares = R.ln_params[...].astype(LOW).astype(F32)
    if wide_ln < 128:
        shares = jnp.concatenate([shares, jnp.zeros((4, 128 - wide_ln), F32)], 1)
    for index in range(size):
        R.ask[index] = jnp.concatenate(
            [asked[index : index + 1, :], shares, jnp.zeros((3, 128), F32)], 0
        )
    R.idx[mp.me, dp.me] = R.ask[dp.me]

    def spread(part, first, second, extra, send, recv):
        blocks = [block_rows(ref, strip) for ref in (part, first, second)]
        return Scatter(dp, *blocks, send, recv, 0, extra)

    up = spread(R.wbf, R.up_first, R.up_second, R.up_extra, R.up_send, R.up_recv)
    down = spread(R.gdn, R.dn_first, R.dn_second, R.dn_extra, R.dn_send, R.dn_recv)
    first_w = spread(
        R.waf.at[:, : 3 * heads_w], R.wa_first, R.wa_second, R.wa_extra, R.ga_send, R.ga_recv
    )
    wo = SideScatter(
        dp,
        *[block_rows(ref, strip) for ref in (R.gwo, R.wo_second)],
        R.wo_first,
        R.wo_send,
        R.wo_recv,
    )
    small = Scatter(
        dp,
        *[of_index(ref) for ref in (R.gw, R.gw_first, R.gw_second)],
        R.gw_send,
        R.gw_recv,
        0,
        R.gw_extra,
    )
    for scatter in (up, down, first_w, small):
        scatter.clear()

    meet([mp], [dp])
    ask, ask_wait = far_copies(
        dp,
        lambda dest, source: (R.ask.at[dest], R.idx.at[mp.me, source]),
        R.ask_send,
        R.ask_recv,
    )
    for step in range(1, size):
        ask(step).start()

    mine_in = R.winf.at[mp.me]
    win = Gather(dp, block_rows(mine_in, rin), R.win_send, R.win_recv, 0, True)
    win_all = Gather(mp, of_index(R.winf), R.wim_send, R.wim_recv)
    wa = [
        Gather(dp, part_rows(R.waf, strip, piece * half_strip, half_strip), send, recv, 0, True)
        for piece, (send, recv) in enumerate(((R.wa_send, R.wa_recv), (R.wx_send, R.wx_recv)))
    ]
    wb = Gather(dp, block_rows(R.wbf, strip), R.wb_send, R.wb_recv, 0, True)
    wc = Gather(dp, part_rows(R.wcf, strip, 0, half_strip), R.wc_send, R.wc_recv, 0, True)
    wd = SideGather(dp, part_rows(R.wcf, strip, half_strip, half_strip), R.wd_send, R.wd_recv, 0, True)
    dxg = Gather(
        mp,
        lambda index: R.dx.at[:, pl.ds(pl.multiple_of(index * seq_len, seq_len), seq_len)],
        R.dx_send,
        R.dx_recv,
    )
    ag = halves(R.a, R.a_send, R.a_recv)
    cg = halves(R.c, R.c_send, R.c_recv)
    mg = halves(R.dmid_all, R.e_send, R.e_recv)

    mine_in[pl.ds(pl.multiple_of(dp.me * rin, rin), rin), :] = (
        R.w_in[:, pl.ds(pl.multiple_of(mp.me * quarter, quarter), quarter)]
        .astype(LOW)
        .astype(R.winf.dtype)
    )
    win.start()
    for part in range(3):
        R.waf[own_strip, part * heads_w : (part + 1) * heads_w] = R.w_qkv[part].astype(LOW)
    R.waf[own_strip, 3 * heads_w :] = R.w_out[...].T.astype(LOW)
    wa[0].start()
    wa[1].start_near()
    for name in names_of_moments:
        moment(name).start()

    for seq in range(seqs):
        level = jnp.full((seq_len, 1), R.levels[seq], jnp.int32).astype(F32) / (LEVELS - 1)
        R.sig[seq * seq_len : (seq + 1) * seq_len, :] = jnp.exp(level * jnp.log(SIGMA_TOP))

    def scale_at(here):
        sig = R.sig[here, :]
        return sig * lax.rsqrt(1.0 + sig * sig)

    for piece in range(seqs):
        here = rows_of(piece)

        def scale_cot(row, here=here, piece=piece):
            there = pl.ds(pl.multiple_of(mp.me * seq_len + row, some_rows), some_rows)
            R.dx[piece, there, :] = (R.cot[here(row), :].astype(F32) * scale_at(here(row))).astype(LOW)

        by_rows(scale_cot)
    dxg.start()
    R.wbf[own_strip, :] = R.w_up[...].astype(LOW)
    R.wcf[own_strip, :] = R.w_down[...].T.astype(LOW)
    wb.start_near()
    R.pick[...] = jnp.where(
        lax.broadcasted_iota(jnp.int32, (tokens, spots), 1).astype(F32) == slot, 1.0, 0.0
    ).astype(LOW)
    win.relays()

    ask_wait()
    small_eye = lax.broadcasted_iota(jnp.int32, (cap, 128), 0) == lax.broadcasted_iota(
        jnp.int32, (cap, 128), 1
    )

    def locate(index, carry):
        row = R.idx[mp.me, index][0:1, :]
        column = jnp.sum(jnp.where(small_eye, row, 0.0), 1, keepdims=True)
        local = column.astype(jnp.int32) - dp.me * table_rows
        R.loc[pl.ds(pl.multiple_of(index * cap, cap), cap), :] = jnp.broadcast_to(local, (cap, 128))
        return carry

    lax.fori_loop(0, size, locate, 0, unroll=True)
    win.close()
    win_all.start()
    found = None
    for piece in range(pieces):
        fetch(piece).wait()
        rows = min(chunk, table_rows - piece * chunk)
        if rows < chunk:
            R.tab[piece % 2, rows:, :] = jnp.zeros((chunk - rows, width), F32)
        hit = (
            lax.broadcasted_iota(jnp.int32, (spots, chunk), 1) + piece * chunk == R.loc[:, 0:1]
        )
        more = dot(jnp.where(hit, 1.0, 0.0).astype(LOW), R.tab[piece % 2].astype(LOW))
        found = more if found is None else found + more
        if piece + 2 < pieces:
            fetch(piece + 2).start()
    R.give[...] = found.astype(LOW)

    give, give_wait = far_copies(
        dp,
        lambda dest, source: (block_rows(R.give, cap)(dest), block_rows(R.got, cap)(source)),
        R.give_send,
        R.give_recv,
    )
    for step in range(1, size):
        give(step).start()
    R.got[mine, :] = R.give[mine, :]
    wa[1].start_far()
    win_all.relays()
    wa[0].relay(1)
    wa[0].relay(2)
    if wide_ln % 128 == 0:
        R.gains[...] = jnp.concatenate([R.idx[mp.me, index] for index in range(size)], 1)
    else:
        total = jnp.zeros((8, model), F32)
        for index in range(size):
            place = lax.broadcasted_iota(
                jnp.int32, (128, model), 1
            ) == index * wide_ln + lax.broadcasted_iota(jnp.int32, (128, model), 0)
            place = place & (lax.broadcasted_iota(jnp.int32, (128, model), 0) < wide_ln)
            total = total + dot(
                R.idx[mp.me, index].astype(LOW), jnp.where(place, 1.0, 0.0).astype(LOW)
            )
        R.gains[...] = total
    for step in range(3, dp.far):
        wa[0].relay(step)
    named = Gather(mp, of_index(R.idx), R.id_send, R.id_recv)

    give_wait()
    rows = dot(R.pick[...], R.got[...])
    R.rows[...] = rows.astype(LOW)
    sig = R.sig[...]
    unit = rows * lax.rsqrt(jnp.mean(rows * rows, -1, keepdims=True) + EPS_NORM)
    R.mixed[...] = ((unit + sig * R.noise[...].astype(F32)) * lax.rsqrt(1.0 + sig * sig)).astype(LOW)
    win_all.close()
    for index in range(ways):
        R.x0[:, index * quarter : (index + 1) * quarter] = dot(
            R.mixed[...], R.winf[index].astype(LOW)
        )

    for piece in range(seqs):
        here, there = rows_of(piece), own_rows(piece)

        def first_norm(row, here=here, there=there):
            normed, _ = norm_rows(R.x0[here(row), :])
            R.a[there(row), :] = (normed * R.gains[1:2, :] + R.gains[2:3, :]).astype(LOW)

        by_rows(first_norm, ag[piece].start)
    wa[1].relay(1)
    wb.start_far()
    for step in range(2, dp.far):
        wa[1].relay(step)
    dxg.relays()
    for gather in ag:
        gather.relays()
    for gather in (*wa, *ag):
        gather.close()

    att = Sums(R.part, R.fold, R.fold_far, R.as_send, R.as_recv)
    dcs = Sums(R.part, R.fold, R.fold_far, R.cs_send, R.cs_recv)
    das = Sums(R.part, R.fold, R.fold_far, R.ds_send, R.ds_recv)
    out = Sums(R.c, R.first, R.second, R.os_send, R.os_recv)
    masks = head_masks(heads_w)

    all_rows = (heads_w // HD) * seq_len
    scale = HD ** (-0.5)

    def softmax(seq, row):
        scores = R.scores[seq, row : row + 64, :]
        raised = jnp.exp((scores - jnp.max(scores, -1, keepdims=True)) * scale)
        return raised * (1.0 / jnp.sum(raised, -1, keepdims=True))

    def attend(rows_at):
        for seq, rows in enumerate(rows_at):
            queries = spread_heads(R.qkv[rows, :heads_w], masks)
            R.scores[seq] = dot_nt(queries, R.qkv[rows, heads_w : 2 * heads_w])
        for seq, rows in enumerate(rows_at):
            for row in range(0, all_rows, 64):
                R.probs[seq, row : row + 64, :] = softmax(seq, row).astype(LOW)
            seen = dot(R.probs[seq], R.qkv[rows, 2 * heads_w : 3 * heads_w])
            R.o[rows, :] = join_heads(seen, masks, seq_len).astype(LOW)

    def second_norm(piece):
        here, there = rows_of(piece), own_rows(piece)
        att.arrive(piece)

        def norm(row):
            x1 = R.x0[here(row), :] + att.total(piece, pl.ds(row, some_rows))
            R.out[here(row), :] = x1
            normed, _ = norm_rows(x1)
            R.c[there(row), :] = (normed * R.gains[3:4, :] + R.gains[4:5, :]).astype(LOW)

        by_rows(norm, cg[piece].start)

    def middle_wb():
        wb.relay(2)
        wd.start_far()

    def last_wb():
        wd.start_other()
        for step in range(3, dp.far):
            wb.relay(step)
        named.start()

    for part in range(3):
        cols = slice(part * heads_w, (part + 1) * heads_w)
        R.qkv[:, cols] = dot(R.a[...], R.waf[:, cols]).astype(LOW)
    wb.relay(1)
    wd.start_near()
    wc.start_near()
    wc.start_far()
    turns = group // (2 * seq_len)
    pairs(attend, [(min(1, turns - 1), middle_wb), (turns - 1, last_wb)])

    def project(chunk, carry):
        cols = pl.ds(pl.multiple_of(chunk * chunk_cols, chunk_cols), chunk_cols)
        R.part[:, cols] = dot_nt(R.o[...], R.waf[cols, 3 * heads_w :]).astype(LOW)
        att.trade(chunk)
        return carry

    lax.fori_loop(0, chunk_count, project, 0)
    att.hand_on_all()
    wc.relay(1)
    for gather in (*wa, *ag, dxg, win):
        gather.drain()
    for step in range(1, size):
        ask(step).wait_send()
    for piece in range(seqs):
        second_norm(piece)
    for piece in range(seqs):
        cg[piece].relays()
    wc.relay(2)
    wb.close()
    named.relays()
    for piece in range(seqs):
        cg[piece].close()
        att.drain(piece)

    def activate(cols):
        R.h[...] = dot(R.c[...], R.wbf[:, cols])

        def gelu(row):
            here = pl.ds(row, 64)
            h = R.h[here, :]
            bell = jnp.exp(-0.5 * h * h)
            tail = normal_tail(jnp.abs(h), bell)
            gate = jnp.where(h >= 0.0, 1.0 - tail, tail)
            slope = gate + h * (bell * 0.3989422804014327)
            R.hb[here, cols] = (h * gate).astype(LOW)
            R.slope[here, cols] = slope.astype(LOW)

        strips(group, 64, gelu, 2)

    def last_wc():
        for step in range(3, dp.far):
            wc.relay(step)

    parts_of = hidden // min(col_step, hidden)
    chunks(hidden, activate, [(min(1, parts_of - 1), last_wc), (parts_of - 1, wd.forward)])

    due = [(scatter, step) for scatter in (down, up) for step in range(1, dp.far)]

    def pass_due(number):
        for _ in range(min(number, len(due))):
            scatter, step = due.pop(0)
            scatter.pass_on(step)

    block = 2 * strip if (2 * strip) % 128 == 0 else min(256, model)

    def grads(make, trades):
        if block == 2 * strip:

            def turn_of(turn, carry):
                hi = up.turn_of(turn)
                make(pl.ds(pl.multiple_of(hi * block, block), block))
                for scatter in trades:
                    scatter.trade(hi)
                return carry

            lax.fori_loop(0, dp.far, turn_of, 0)
        else:
            strips(model, block, lambda col: make(pl.ds(col, block)))
            for scatter in trades:
                scatter.trade_all()

    def down_grads(cols):
        every = R.dx[:, :, cols]
        R.gdn[cols, :] = dot_tn(every.reshape(group, block), R.hb[...]).astype(LOW)

    def up_grads(cols):
        R.wbf[cols, :] = dot_tn(R.c[:, cols], R.dhb[...]).astype(LOW)

    dxg.close()
    grads(down_grads, (down,))
    named.close()
    groups = ways * size
    some, lanes_at = min(groups, 32), min(ways * spots, 512)
    for begin in range(0, ways * spots, lanes_at):
        spot = lax.broadcasted_iota(jnp.int32, (128, lanes_at), 1).astype(F32) + float(begin)
        block_no = jnp.floor((spot + 0.5) * (1.0 / cap))
        place = lax.broadcasted_iota(jnp.int32, (128, lanes_at), 0).astype(F32)
        spread_out = jnp.where(spot - block_no * cap == place, 1.0, 0.0).astype(LOW)
        named_row = jnp.zeros((1, lanes_at), F32)
        for first in range(0, groups, some):
            wanted = jnp.concatenate(
                [
                    R.idx[index // size, index % size][0:1, :] + 1.0
                    for index in range(first, first + some)
                ],
                0,
            )
            high = jnp.floor(wanted * (1.0 / 256.0))
            rest = wanted - 256.0 * high
            laid = dot(high.astype(LOW), spread_out) * 256.0 + dot(rest.astype(LOW), spread_out) - 1.0
            own_block = block_no[0:1, :] == float(first) + lax.broadcasted_iota(
                jnp.int32, (some, lanes_at), 0
            ).astype(F32)
            named_row = named_row + jnp.sum(jnp.where(own_block, laid, 0.0), 0, keepdims=True)
        R.named[:, begin : begin + lanes_at] = jnp.broadcast_to(
            named_row.astype(jnp.int32) - dp.me * table_rows, (8, lanes_at)
        )
    named.drain()
    wc.close()
    wd.close()
    for gather in (wb, *cg):
        gather.drain()

    def bend(cols):
        every = R.dx[...].reshape(group, model)
        bent = dot(every, R.wcf[:, cols]) * R.slope[:, cols].astype(F32)
        R.dhb[:, cols] = bent.astype(LOW)

    def feed_back(cols):
        R.part[:, cols] = dot_nt(R.dhb[...], R.wbf[cols, :]).astype(LOW)

    def feed_out(cols):
        R.c[:, cols] = dot_nt(R.hb[...], R.wcf[cols, :]).astype(LOW)

    R.norms[...] = jnp.zeros_like(R.norms)

    def second_back(piece):
        here, there = rows_of(piece), own_rows(piece)
        dcs.arrive(piece)

        def back(row):
            dc = dcs.total(piece, pl.ds(row, some_rows))
            grad, unit = norm_back(R.out[here(row), :], R.gains[3:4, :], dc)
            grad = grad + R.cot[here(row), :].astype(F32) * scale_at(here(row))
            R.dmid[here(row), :] = grad
            R.dmid_all[there(row), :] = grad.astype(LOW)
            R.norms[2:3, :] += jnp.sum(dc * unit, 0, keepdims=True)
            R.norms[3:4, :] += jnp.sum(dc, 0, keepdims=True)

        by_rows(back, mg[piece].start)

    chunks(hidden, bend)
    pass_due(1)
    dcs.products(feed_back)
    dcs.hand_on_last()
    pass_due(1)
    grads(up_grads, (up,))
    for piece in range(seqs):
        second_back(piece)
    pass_due(max(1, dp.far - 3))
    out.products(feed_out)
    for piece in range(seqs):
        mg[piece].relays()
    out.hand_on_last()
    for piece in range(seqs):
        mg[piece].close()
        dcs.drain(piece)

    def attend_back(rows_at):
        for seq, rows in enumerate(rows_at):
            queries = spread_heads(R.qkv[rows, :heads_w], masks)
            R.scores[seq] = dot_nt(queries, R.qkv[rows, heads_w : 2 * heads_w])
            R.upper[seq] = spread_heads(R.low[rows, :], masks)
            R.dprobs[seq] = dot_nt(R.upper[seq], R.qkv[rows, 2 * heads_w : 3 * heads_w])
        for seq, rows in enumerate(rows_at):
            for row in range(0, all_rows, 64):
                probs = softmax(seq, row)
                grad_probs = R.dprobs[seq, row : row + 64, :]
                inner = jnp.sum(probs * grad_probs, -1, keepdims=True)
                R.probs[seq, row : row + 64, :] = probs.astype(LOW)
                R.dscores[seq, row : row + 64, :] = (probs * (grad_probs - inner)).astype(LOW)
            keys = R.qkv[rows, heads_w : 2 * heads_w]
            queries = spread_heads(R.qkv[rows, :heads_w], masks)
            R.qkv[rows, 2 * heads_w : 3 * heads_w] = dot_tn(R.probs[seq], R.upper[seq]).astype(LOW)
            R.qkv[rows, heads_w : 2 * heads_w] = (dot_tn(R.dscores[seq], queries) * scale).astype(LOW)
            R.qkv[rows, :heads_w] = (
                join_heads(dot(R.dscores[seq], keys), masks, seq_len) * scale
            ).astype(LOW)

    def back_project(cols):
        R.part[:, cols] = dot_nt(R.qkv[...], R.waf[cols, : 3 * heads_w]).astype(LOW)

    def first_back(piece):
        here = rows_of(piece)
        das.arrive(piece)

        def back(row):
            da = das.total(piece, pl.ds(row, some_rows))
            grad, unit = norm_back(R.x0[here(row), :], R.gains[1:2, :], da)
            R.dx0[here(row), :] = (R.dmid[here(row), :] + grad).astype(LOW)
            R.norms[0:1, :] += jnp.sum(da * unit, 0, keepdims=True)
            R.norms[1:2, :] += jnp.sum(da, 0, keepdims=True)

        by_rows(back)

    def out_grads():
        def make(cols):
            R.gwo[cols, :] = dot_tn(R.dmid_all[:, cols], R.o[...]).astype(LOW)

        grads(make, (wo,))

    R.low[...] = dot(R.dmid_all[...], R.waf[:, 3 * heads_w :]).astype(LOW)
    pass_due(1)
    pairs(attend_back, [(turns // 2, lambda: pass_due(1)), (turns - 1, lambda: pass_due(1))])
    das.products(back_project)
    das.hand_on_last()
    def out_grads(cols):
        R.gwo[cols, :] = dot_tn(R.dmid_all[:, cols], R.o[...]).astype(LOW)

    def attend_grads(cols):
        R.waf[cols, : 3 * heads_w] = dot_tn(R.a[:, cols], R.qkv[...]).astype(LOW)

    grads(out_grads, ())
    wo.start()
    grads(attend_grads, (first_w,))
    for piece in range(seqs):
        first_back(piece)

    grad_mixed = sum(
        dot_nt(R.dx0[:, index * quarter : (index + 1) * quarter], R.winf[index].astype(LOW))
        for index in range(ways)
    )
    sig = R.sig[...]
    grad_unit = grad_mixed * lax.rsqrt(1.0 + sig * sig)
    rows = R.rows[...].astype(F32)
    inverse = lax.rsqrt(jnp.mean(rows * rows, -1, keepdims=True) + EPS_NORM)
    unit = rows * inverse
    grad_rows = inverse * (grad_unit - unit * jnp.mean(grad_unit * unit, -1, keepdims=True))
    for step in range(1, size):
        give(step).wait_send()
    R.give[...] = dot_tn(R.pick[...], grad_rows.astype(LOW)).astype(LOW)
    mine_inc = block_rows(R.inc, spots)(mp.me)
    back, back_wait = far_copies(
        dp,
        lambda dest, source: (block_rows(R.give, cap)(dest), block_rows(mine_inc, cap)(source)),
        R.back_send,
        R.back_recv,
    )
    for step in range(1, size):
        back(step).start()
    mine_inc[mine, :] = R.give[mine, :]

    small_mp = Scatter(
        mp, of_index(R.gm), of_index(R.gm_first), of_index(R.gm_second), R.gm_send, R.gm_recv
    )
    for index in range(ways):
        cols = slice(index * quarter, (index + 1) * quarter)
        R.gm[index, :width, :] = dot_tn(R.mixed[...], R.dx0[:, cols]).astype(LOW)
        R.gm[index, width:, :] = jnp.concatenate(
            [R.norms[0:4, cols], jnp.zeros((12, quarter), F32)], 0
        ).astype(LOW)
    small_mp.trade_all()
    pass_due(len(due))
    for step in range(1, far):
        small_mp.pass_on(step)

    wo.trade()
    first_w.pass_on(1)
    for turn in range(min(2, shares_of)):
        for one in tile_of(turn):
            one.start()
    back_wait()
    rows_in = Gather(mp, block_rows(R.inc, spots), R.in_send, R.in_recv)
    rows_in.start()

    small_mp.arrive()
    summed = small_mp.total(slice(None))
    for index in range(size):
        piece = summed[index * rin : (index + 1) * rin, :]
        if rin_up > rin:
            piece = jnp.concatenate([piece, jnp.zeros((rin_up - rin, quarter), F32)], 0)
        R.gw[index, :rin_up, :] = piece.astype(LOW)
        R.gw[index, rin_up:, :] = summed[width:, :].astype(LOW)
    small.trade_all()
    rows_in.relays()
    first_w.pass_on(2)

    def finish_out(piece):
        here = rows_of(piece)
        out.arrive(piece)

        def finish(row):
            R.out[here(row), :] = (
                R.out[here(row), :] + out.total(piece, pl.ds(row, some_rows))
            ) * scale_at(here(row))

        by_rows(finish)

    for piece in range(seqs):
        finish_out(piece)

    rows_in.close()

    once = jnp.where(mp.me == 0, 1.0, 0.0)
    lanes = lax.broadcasted_iota(jnp.int32, (1, 128), 1)
    R.sums[...] = jnp.zeros_like(R.sums)

    def put(place, squares, factor=None):
        for row, values in enumerate(squares):
            total = jnp.sum(jnp.sum(values, 0, keepdims=True), 1, keepdims=True)
            if factor is not None:
                total = total * factor
            R.sums[row : row + 1, :] += jnp.where(lanes == place, total, 0.0)

    def squares_of(weight, gradient, first, second):
        direction = direction_of(weight, gradient, first, second)[2]
        return weight * weight, direction * direction

    def folded(values):
        rows, columns = values.shape
        return jnp.sum(values.reshape(rows // 8, 8, columns), 0)

    def add_up(weight, gradient, first, second):
        squares = squares_of(weight[...], gradient[...], first[...], second[...])
        return [folded(values) for values in squares]

    zero = jnp.zeros((8, width), F32)

    rest = [
        functools.partial(scatter.pass_on, step)
        for scatter in (first_w, small)
        for step in range(1, dp.far)
    ][2:]
    tail_hooks = [
        (min(shares_of - 1, place * shares_of // len(rest)), action)
        for place, action in enumerate(rest)
    ]

    def add_tile(turn, carry):
        side = lax.rem(turn, 2)
        for place, action in tail_hooks:
            pl.when(turn == place)(action)
        for one in tile_of(turn):
            one.wait()
        hit = (
            lax.broadcasted_iota(jnp.int32, (tile_rows, ways * spots), 0)
            + share_tile(turn) * tile_rows
            == R.named[0:1, :]
        )
        gradient = dot(jnp.where(hit, 1.0, 0.0).astype(LOW), R.inc[...])
        more = add_up(R.tw.at[side], gradient, R.tm.at[side], R.tv.at[side])
        counts = jnp.where(turn * ways + mp.me < tiles, 1.0, 0.0)

        @pl.when(turn + 2 < shares_of)
        def _():
            for one in tile_of(turn + 2):
                one.start()

        return carry[0] + counts * more[0], carry[1] + counts * more[1]

    put(0, lax.fori_loop(0, shares_of, add_tile, (zero, zero)))

    for thing in (win_all, wc, wd, *mg, up, down, small_mp):
        thing.drain()
    for piece in range(seqs):
        out.drain(piece)
        das.drain(piece)
    for step in range(1, size):
        back(step).wait_send()

    for name in names_of_moments:
        moment(name).wait()
    up.arrive()

    R.red_up[...] = up.total(slice(None))
    put(10, add_up(R.w_up, R.red_up, R.up_m_here, R.up_v_here))
    down.arrive()

    R.red_dn[...] = down.total(slice(None)).T
    put(11, add_up(R.w_down, R.red_dn, R.down_m_here, R.down_v_here))
    wo.arrive()
    R.red_out[...] = wo.total().T
    put(9, add_up(R.w_out, R.red_out, R.out_m_here, R.out_v_here))

    small.arrive()
    R.wsum[mp.me] = small.total(slice(None)).astype(LOW)
    weights_in = Gather(mp, of_index(R.wsum), R.ws_send, R.ws_recv)
    weights_in.start()
    first_w.arrive()

    value = first_w.total(slice(None))
    for part in range(3):
        R.red_qkv[part] = value[:, part * heads_w : (part + 1) * heads_w]
    weights_in.relays()
    for part in range(3):
        put(
            6 + part,
            add_up(
                R.w_qkv.at[part], R.red_qkv.at[part], R.qkv_m_here.at[part], R.qkv_v_here.at[part]
            ),
        )
    weights_in.close()
    total = jnp.concatenate([R.wsum[index].astype(F32) for index in range(ways)], 1)
    R.red_in[...] = total[:rin, :]
    put(1, add_up(R.w_in, R.red_in, R.w_in_m_here, R.w_in_v_here), once)
    if strip % 128 == 0:
        R.lnsum[...] = total[rin_up : rin_up + 8, :]
        R.red_ln[...] = R.lnsum[0:4, pl.ds(pl.multiple_of(dp.me * strip, strip), strip)]
    else:
        chosen = lax.broadcasted_iota(jnp.int32, (model, strip), 0) == dp.me * strip + (
            lax.broadcasted_iota(jnp.int32, (model, strip), 1)
        )
        R.red_ln[...] = dot(
            total[rin_up : rin_up + 8, :].astype(LOW), jnp.where(chosen, 1.0, 0.0).astype(LOW)
        )[0:4]
    squares = squares_of(R.ln_params[...], R.red_ln[...], R.ln_m_here[...], R.ln_v_here[...])
    for row in range(4):
        put(2 + row, [values[row : row + 1, :] for values in squares], once)

    R.near[dp.me] = R.sums[...]
    near, near_wait = far_copies(
        dp, lambda dest, source: (R.near.at[dp.me], R.near.at[source]), R.near_send, R.near_recv
    )
    for step in range(1, size):
        near(step).start()
    near_wait()
    R.wide[mp.me] = jnp.sum(R.near[...], 0)
    far_off, far_off_wait = far_copies(
        mp, lambda dest, source: (R.wide.at[mp.me], R.wide.at[source]), R.wide_send, R.wide_recv
    )
    for step in range(1, ways):
        far_off(step).start()
    far_off_wait()
    R.totals[...] = jnp.sum(R.wide[...], 0)

    for thing in (wo, first_w, small, rows_in, weights_in):
        thing.drain()
    for step in range(1, size):
        near(step).wait_send()
    for step in range(1, ways):
        far_off(step).wait_send()


def run_layer(cap, ids, levels, noise, cot, weights, moments):
    table, w_in, ln_params, w_qkv, w_out, w_up, w_down = weights
    dp, mp = lax.axis_size("dp"), lax.axis_size("mp")
    seqs, seq_len = ids.shape
    tokens, width = noise.shape
    model = cot.shape[1]
    rin = w_in.shape[0]
    heads_w = w_qkv.shape[2]
    strip, hidden = w_up.shape
    group = tokens * mp
    spots = dp * cap
    wide = round_up(rin, 16) + 16
    far, far_dp = mp // 2, dp // 2
    quarter = model // mp
    in_kind = LOW if rin % 16 == 0 else F32
    tile_rows = max(rows for rows in range(8, 257, 8) if table.shape[0] % rows == 0)
    stacked = (heads_w // HD) * seq_len
    vmem = pl.BlockSpec(memory_space=pltpu.VMEM)
    outside = pl.BlockSpec(memory_space=pl.ANY)
    inputs = dict(
        ids=(ids, vmem),
        levels=(levels, pl.BlockSpec(memory_space=pltpu.SMEM)),
        noise=(noise, vmem),
        cot=(cot, vmem),
        table=(table, outside),
        w_in=(w_in, vmem),
        ln_params=(ln_params, vmem),
        w_qkv=(w_qkv, vmem),
        w_out=(w_out, vmem),
        w_up=(w_up, vmem),
        w_down=(w_down, vmem),
    )
    kept = {}
    for name, (first, second) in zip(("table", "w_in", "ln", "qkv", "out", "up", "down"), moments):
        inputs[name + "_m"] = (first, outside)
        inputs[name + "_v"] = (second, outside)
        if name != "table":
            kept[name + "_m_here"] = kept[name + "_v_here"] = (first.shape, F32)
    outputs = dict(
        out=((tokens, model), F32),
        red_up=((strip, hidden), F32),
        red_dn=((hidden, strip), F32),
        red_qkv=((3, strip, heads_w), F32),
        red_out=((heads_w, strip), F32),
        red_in=((rin, model), F32),
        red_ln=((4, strip), F32),
        inc=((mp * spots, width), LOW),
        named=((8, mp * spots), jnp.int32),
        totals=((8, 128), F32),
    )
    buffers = dict(
        tab=((2, round_up(table.shape[0] // 8, 128), width), F32),
        ask=((dp, 8, 128), F32),
        idx=((mp, dp, 8, 128), F32),
        loc=((spots, 128), jnp.int32),
        give=((spots, width), LOW),
        got=((spots, width), LOW),
        tw=((2, tile_rows, width), F32),
        tm=((2, tile_rows, width), F32),
        tv=((2, tile_rows, width), F32),
        sums=((8, 128), F32),
        near=((dp, 8, 128), F32),
        wide=((mp, 8, 128), F32),
        scores=((2, stacked, seq_len), F32),
        dprobs=((2, stacked, seq_len), F32),
        probs=((2, stacked, seq_len), LOW),
        dscores=((2, stacked, seq_len), LOW),
        upper=((2, stacked, heads_w), LOW),
        gwo=((model, heads_w), LOW),
        wo_first=((strip, heads_w), LOW),
        wo_second=((dp * strip, heads_w), LOW),
        gains=((8, model), F32),
        lnsum=((8, model), F32),
        sig=((tokens, 1), F32),
        pick=((tokens, spots), LOW),
        rows=((tokens, width), LOW),
        mixed=((tokens, width), LOW),
        x0=((tokens, model), F32),
        a=((group, model), LOW),
        c=((group, model), LOW),
        dx=((seqs, group // seqs, model), LOW),
        dmid=((tokens, model), F32),
        dmid_all=((group, model), LOW),
        winf=((mp, rin * dp, quarter), in_kind),
        waf=((model, 4 * heads_w), LOW),
        wbf=((model, hidden), LOW),
        wcf=((model, hidden), LOW),
        qkv=((group, 3 * heads_w), LOW),
        o=((group, heads_w), LOW),
        low=((group, heads_w), LOW),
        part=((group, model), LOW),
        first=((far * tokens, model), LOW),
        fold=((far * tokens, model), LOW),
        second=((far * tokens, model), LOW),
        fold_far=((far * tokens, model), LOW),
        h=((group, min(256, 262144 // group, hidden)), F32),
        hb=((group, hidden), LOW),
        dhb=((group, hidden), LOW),
        slope=((group, hidden), LOW),
        gdn=((model, hidden), LOW),
        dx0=((tokens, model), LOW),
        norms=((8, model), F32),
        gm=((mp, width + 16, quarter), LOW),
        gm_first=((far, width + 16, quarter), LOW),
        gm_second=((far, width + 16, quarter), LOW),
        gw=((dp, wide, quarter), LOW),
        gw_first=((far_dp, wide, quarter), LOW),
        gw_second=((far_dp, wide, quarter), LOW),
        up_first=((far_dp * strip, hidden), LOW),
        up_second=((far_dp * strip, hidden), LOW),
        dn_first=((far_dp * strip, hidden), LOW),
        dn_second=((far_dp * strip, hidden), LOW),
        wa_first=((far_dp * strip, 3 * heads_w), LOW),
        wa_second=((far_dp * strip, 3 * heads_w), LOW),
        wsum=((mp, wide, quarter), LOW),
        up_extra=((strip, hidden), LOW),
        dn_extra=((strip, hidden), LOW),
        wa_extra=((strip, 3 * heads_w), LOW),
        gw_extra=((wide, quarter), LOW),
        **kept,
    )
    sems = dict(tab_sem=2, tile_sem=6, moment_sem=12)
    for name in (
        *("win", "wa", "wx", "wb", "wc", "wd", "ask", "give", "back"),
        *("up", "dn", "ga", "wo", "gw", "near"),
    ):
        sems[name + "_send"] = sems[name + "_recv"] = dp + 1
    for name in ("wim", "id", "in", "ws", "gm", "wide"):
        sems[name + "_send"] = sems[name + "_recv"] = mp
    for name in ("dx", "a", "c", "e"):
        sems[name + "_send"] = sems[name + "_recv"] = 2 * seqs * mp
    for name in ("as", "os", "cs", "ds"):
        sems[name + "_send"] = sems[name + "_recv"] = seqs * mp * (model // min(256, 262144 // group))
    names = [*inputs, *outputs, *buffers, *sems]
    made = pl.pallas_call(
        functools.partial(layer_kernel, cap, names),
        out_shape=[jax.ShapeDtypeStruct(shape, kind) for shape, kind in outputs.values()],
        in_specs=[spec for _, spec in inputs.values()],
        out_specs=[vmem] * len(outputs),
        scratch_shapes=[
            *[pltpu.VMEM(shape, kind) for shape, kind in buffers.values()],
            *[pltpu.SemaphoreType.DMA((number,)) for number in sems.values()],
        ],
        compiler_params=pltpu.CompilerParams(
            vmem_limit_bytes=VMEM_BYTES, collective_id=1, has_side_effects=True
        ),
        name="layer",
    )(*[value for value, _ in inputs.values()])
    return dict(zip(outputs, made))


def direction_of(weight, gradient, first, second):
    first_new = BETA_ONE * first + (1.0 - BETA_ONE) * gradient
    second_new = BETA_TWO * second + (1.0 - BETA_TWO) * gradient * gradient
    second_hat = second_new * (1.0 / (1.0 - BETA_TWO**STEP))
    inverse = lax.rsqrt(second_hat)
    root = second_hat * inverse + EPS_ADAM
    inverse = inverse * (2.0 - root * inverse)
    inverse = inverse * (2.0 - root * inverse)
    direction = first_new * (1.0 / (1.0 - BETA_ONE**STEP)) * inverse + DECAY * weight
    return first_new, second_new, direction


def update_kernel(part, names, *refs):
    R = types.SimpleNamespace(**dict(zip(names, refs)))
    turn = pl.program_id(0)
    R.out_rows[...] = R.made[...]
    norms = jnp.sqrt(R.totals[...])
    R.norms[...] = norms[0:2, 0:12]
    factors = norms[0:1, :] / (norms[1:2, :] + EPS_ADAM) * RATE

    def piece(name, here, gradient, place, rows=slice(None)):
        weight = getattr(R, name)[here]
        first_new, second_new, direction = direction_of(
            weight, gradient, getattr(R, name + "_m")[here], getattr(R, name + "_v")[here]
        )
        if isinstance(place, int):
            factor = factors[0:1, place : place + 1]
        else:
            factor = jnp.concatenate([factors[0:1, one : one + 1] for one in place], 0)
        getattr(R, name + "_m_new")[here] = first_new
        getattr(R, name + "_v_new")[here] = second_new
        getattr(R, name + "_new")[here] = weight - factor * direction

    def update(name, gradient, place, lead=(), here=slice(None)):
        piece(name, (*lead, here, slice(None)), gradient, place)

    tile = R.table.shape[0]
    spots = R.named.shape[1]

    def table_part(row):
        hit = (
            lax.broadcasted_iota(jnp.int32, (part, spots), 0) + (turn * tile + row)
            == R.named[0:1, :]
        )
        gradient = dot(jnp.where(hit, 1.0, 0.0).astype(LOW), R.inc[...])
        update("table", gradient, 0, (), pl.ds(row, part))

    strips(tile, part, table_part)
    for group in range(3):
        update("qkv", R.red_qkv[group], 6 + group, (group,))
    update("up", R.red_up[...], 10)
    update("down", R.red_dn[...], 11)

    @pl.when(turn == 0)
    def _():
        update("out", R.red_out[...], 9)
        update("w_in", R.red_in[...], 1)
        piece("ln", (slice(None), slice(None)), R.red_ln[...], (2, 3, 4, 5))


def turns_of(rows, parts):
    return [
        turns
        for turns in (5, 4, 2, 1)
        if rows % (8 * turns) == 0 and all(size % (8 * turns) == 0 for size in parts)
    ][0]


def run_update(weights, moments, grads):
    names = ("table", "w_in", "ln", "qkv", "out", "up", "down")
    by_name = dict(zip(names, weights))
    rows, width = by_name["table"].shape
    strip, hidden = by_name["up"].shape
    heads_w = by_name["qkv"].shape[2]
    turns = turns_of(rows, (strip, hidden))
    tile = rows // turns
    part = max(size for size in range(8, 257, 8) if tile % size == 0)
    fixed = lambda array: pl.BlockSpec(array.shape, lambda turn: (0,) * array.ndim)
    specs = dict(
        table=pl.BlockSpec((tile, width), lambda turn: (turn, 0)),
        w_in=fixed(by_name["w_in"]),
        ln=fixed(by_name["ln"]),
        qkv=pl.BlockSpec((3, strip // turns, heads_w), lambda turn: (0, turn, 0)),
        out=fixed(by_name["out"]),
        up=pl.BlockSpec((strip // turns, hidden), lambda turn: (turn, 0)),
        down=pl.BlockSpec((hidden // turns, strip), lambda turn: (turn, 0)),
    )
    inputs = {}
    for name, weight, (first, second) in zip(names, weights, moments):
        inputs[name] = (weight, specs[name])
        inputs[name + "_m"] = (first, specs[name])
        inputs[name + "_v"] = (second, specs[name])
    for name, like in (
        ("red_up", "up"),
        ("red_dn", "down"),
        ("red_qkv", "qkv"),
        ("red_out", "out"),
        ("red_in", "w_in"),
        ("red_ln", "ln"),
    ):
        inputs[name] = (grads[name], specs[like])
    for name in ("inc", "named", "totals"):
        inputs[name] = (grads[name], fixed(grads[name]))
    tokens, model = grads["out"].shape
    rows_spec = pl.BlockSpec((tokens // turns, model), lambda turn: (turn, 0))
    inputs["made"] = (grads["out"], rows_spec)
    outputs = {"out_rows": (grads["out"].shape, rows_spec)}
    for name, weight in by_name.items():
        for kind in ("_new", "_m_new", "_v_new"):
            outputs[name + kind] = (weight.shape, specs[name])
    outputs["norms"] = ((2, 12), pl.BlockSpec((2, 12), lambda turn: (0, 0)))
    results = pl.pallas_call(
        functools.partial(update_kernel, part, [*inputs, *outputs]),
        grid=(turns,),
        out_shape=[jax.ShapeDtypeStruct(shape, F32) for shape, _ in outputs.values()],
        in_specs=[spec for _, spec in inputs.values()],
        out_specs=[spec for _, spec in outputs.values()],
        compiler_params=pltpu.CompilerParams(vmem_limit_bytes=VMEM_BYTES),
        name="update",
    )(*[value for value, _ in inputs.values()])
    return list(results)


def per_device(
    token_ids,
    levels,
    noise,
    cotangent,
    table,
    table_m,
    table_v,
    w_in,
    w_in_m,
    w_in_v,
    ln_params,
    ln_m,
    ln_v,
    w_qkv,
    qkv_m,
    qkv_v,
    w_out,
    out_m,
    out_v,
    w_up,
    up_m,
    up_v,
    w_down,
    down_m,
    down_v,
):
    dp_count = lax.axis_size("dp")
    seq_count, seq_len = token_ids.shape
    tokens = seq_count * seq_len
    model = cotangent.shape[2]
    cap = round_up(max(2, (3 * tokens + 2 * dp_count - 1) // (2 * dp_count)), 16)
    weights = (table, w_in, ln_params, w_qkv, w_out, w_up, w_down)
    moments = (
        (table_m, table_v),
        (w_in_m, w_in_v),
        (ln_m, ln_v),
        (qkv_m, qkv_v),
        (out_m, out_v),
        (up_m, up_v),
        (down_m, down_v),
    )
    grads = run_layer(
        cap,
        token_ids,
        levels,
        noise.reshape(tokens, -1),
        cotangent.reshape(tokens, model),
        weights,
        moments,
    )
    out, *results = run_update(weights, moments, grads)
    return (out.reshape(seq_count, seq_len, model), *results)


def solution(mesh):
    return jax.shard_map(
        per_device,
        mesh=mesh,
        in_specs=(
            P(("dp", "mp"), None),
            P(("dp", "mp")),
            P(("dp", "mp"), None, None),
            P(("dp", "mp"), None, None),
            P("dp", None),
            P("dp", None),
            P("dp", None),
            P("dp", None),
            P("dp", None),
            P("dp", None),
            P(None, "dp"),
            P(None, "dp"),
            P(None, "dp"),
            P(None, "dp", "mp"),
            P(None, "dp", "mp"),
            P(None, "dp", "mp"),
            P("mp", "dp"),
            P("mp", "dp"),
            P("mp", "dp"),
            P("dp", "mp"),
            P("dp", "mp"),
            P("dp", "mp"),
            P("mp", "dp"),
            P("mp", "dp"),
            P("mp", "dp"),
        ),
        out_specs=(
            P(("dp", "mp"), None, None),
            P("dp", None),
            P("dp", None),
            P("dp", None),
            P("dp", None),
            P("dp", None),
            P("dp", None),
            P(None, "dp"),
            P(None, "dp"),
            P(None, "dp"),
            P(None, "dp", "mp"),
            P(None, "dp", "mp"),
            P(None, "dp", "mp"),
            P("mp", "dp"),
            P("mp", "dp"),
            P("mp", "dp"),
            P("dp", "mp"),
            P("dp", "mp"),
            P("dp", "mp"),
            P("mp", "dp"),
            P("mp", "dp"),
            P("mp", "dp"),
            P(),
        ),
        check_vma=False,
    )
```

```python
import functools
import types

import jax
import jax.numpy as jnp
from jax import lax
from jax.experimental import pallas as pl
from jax.experimental.pallas import tpu as pltpu
from jax.sharding import PartitionSpec as P

HD = 64
LEVELS = 64
STEP = 10


EPS_NORM = 1e-06
EPS_LAYER = 1e-05
EPS_ADAM = 1e-06
BETA_ONE = 0.9
BETA_TWO = 0.999
DECAY = 0.01
RATE = 0.5
SIGMA_TOP = 10.0

F32 = jnp.float32
LOW = jnp.bfloat16
VMEM_BYTES = 63 * 1024 * 1024


def sigma_of(levels):
    frac = levels.astype(jnp.float32) / (LEVELS - 1)
    return jnp.exp(frac * jnp.log(SIGMA_TOP))


def lamb_moments(weight, gradient, first, second):
    first_new = BETA_ONE * first + (1.0 - BETA_ONE) * gradient
    second_new = BETA_TWO * second + (1.0 - BETA_TWO) * gradient * gradient
    first_hat = first_new / (1.0 - BETA_ONE**STEP)
    second_hat = second_new / (1.0 - BETA_TWO**STEP)
    direction = first_hat / (jnp.sqrt(second_hat) + EPS_ADAM) + DECAY * weight
    return (first_new, second_new, direction)


def trust_factors(ratio):
    return (
        ratio[0],
        ratio[1],
        ratio[2:6][:, None],
        ratio[6:9][:, None, None],
        ratio[9],
        ratio[10],
        ratio[11],
    )


def round_up(value, step):
    return -(-value // step) * step


def dot(left, right):
    return jnp.dot(left, right, preferred_element_type=F32)


def dot_nt(left, right):
    return lax.dot_general(left, right, (((1,), (1,)), ((), ())), preferred_element_type=F32)


def dot_tn(left, right):
    return lax.dot_general(left, right, (((0,), (0,)), ((), ())), preferred_element_type=F32)


def strips(total, step, body, unroll=1):
    step = min(step, total)

    def one(turn, carry):
        body(pl.multiple_of(turn * step, step))
        return carry

    lax.fori_loop(0, total // step, one, 0, unroll=unroll)


class Line:
    def __init__(self, axis):
        self.axis = axis
        self.size = lax.axis_size(axis)
        self.far = self.size // 2
        self.me = lax.axis_index(axis)
        self.hi = lax.div(self.me, 2)
        self.lo = lax.rem(self.me, 2)
        self.partner = self.hi * 2 + (1 - self.lo)

    def at(self, step):
        return lax.rem(self.hi + step + self.far, self.far)

    def push(self, index, src, dst, send, recv):
        return pltpu.make_async_remote_copy(
            src_ref=src,
            dst_ref=dst,
            send_sem=send,
            recv_sem=recv,
            device_id={self.axis: index},
            device_id_type=pl.DeviceIdType.MESH,
        )

    def signal(self, sem, index):
        pl.semaphore_signal(
            sem, inc=1, device_id={self.axis: index}, device_id_type=pl.DeviceIdType.MESH
        )


def meet(pair_lines, all_lines=()):
    sem = pltpu.get_barrier_semaphore()
    count = 0
    for line in pair_lines:
        for step in range(1, line.far):
            line.signal(sem, line.at(step) * 2 + line.lo)
            count += 1
        line.signal(sem, line.partner)
        count += 1
    for line in all_lines:
        for step in range(1, line.size):
            line.signal(sem, lax.rem(line.me + step, line.size))
            count += 1
    pl.semaphore_wait(sem, count)


class Gather:
    def __init__(self, line, at, send, recv, base=0, ends=False):
        self.line, self.at, self.send, self.recv, self.base = line, at, send, recv, base
        self.ends = ends and line.far == 4

    def source(self, step):
        line = self.line
        if not self.ends:
            return line.at(-step)
        order = ((1, 2, 3), (0, 3, 2), (3, 0, 1), (2, 1, 0))
        hi = order[3][step - 1]
        for place in (2, 1, 0):
            hi = jnp.where(line.hi == place, order[place][step - 1], hi)
        return hi

    def far_sends(self, act):
        line = self.line
        for step in range(1, line.far):
            one = self.copy(line.me, step - 1, line.at(step) * 2 + line.lo)
            if self.ends and step != 2:
                pl.when(line.hi != (3 if step == 1 else 0))(functools.partial(act, one))
            else:
                act(one)

    def to_end(self, act):
        line = self.line
        dest = jnp.where(line.hi == 1, 0, 3)
        one = self.copy((3 - dest) * 2 + line.lo, 2 * line.far - 1, dest * 2 + line.lo)
        pl.when((line.hi == 1) | (line.hi == 2))(functools.partial(act, one))

    def copy(self, index, slot, dest):
        block = self.at(index)
        return self.line.push(
            dest, block, block, self.send.at[self.base + slot], self.recv.at[self.base + index]
        )

    def start_far(self):
        self.far_sends(lambda one: one.start())

    def start_near(self):
        self.copy(self.line.me, self.line.far - 1, self.line.partner).start()

    def start(self):
        self.start_far()
        self.start_near()

    def relay(self, step):
        line = self.line
        handed = self.copy(self.source(step) * 2 + line.lo, line.far - 1 + step, line.partner)
        handed.wait_recv()
        if self.ends and step == 2:
            self.to_end(lambda one: one.start())
        handed.start()

    def relays(self):
        for step in range(1, self.line.far):
            self.relay(step)

    def close(self):
        line = self.line
        for step in range(line.far):
            self.copy(line.at(-step) * 2 + (1 - line.lo), 0, line.partner).wait_recv()

    def drain(self):
        self.far_sends(lambda one: one.wait_send())
        if self.ends:
            self.to_end(lambda one: one.wait_send())
        for slot in range(self.line.far - 1, 2 * self.line.far - 1):
            self.copy(self.line.me, slot, self.line.partner).wait_send()


class SideGather(Gather):
    def other(self, act):
        line = self.line
        for step in range(1, line.far):
            one = self.copy(line.partner, line.far - 1 + step, line.at(step) * 2 + line.lo)
            if self.ends and step != 2:
                pl.when(line.hi != (3 if step == 1 else 0))(functools.partial(act, one))
            else:
                act(one)

    def to_ends(self, parity, slot, act):
        line = self.line
        dest = jnp.where(line.hi == 1, 0, 3)
        one = self.copy((3 - dest) * 2 + parity, slot, dest * 2 + line.lo)
        pl.when((line.hi == 1) | (line.hi == 2))(functools.partial(act, one))

    def start_other(self):
        self.copy(self.line.partner, 0, self.line.partner).wait_recv()
        self.other(lambda one: one.start())

    def taken(self, step):
        line = self.line
        for parity, slot in ((line.lo, 2 * line.far - 1), (1 - line.lo, 2 * line.far)):
            self.copy(self.source(step) * 2 + parity, 0, line.partner).wait_recv()
            if self.ends and step == 2:
                self.to_ends(parity, slot, lambda one: one.start())

    def forward(self):
        if self.line.far > 2:
            self.taken(2)

    def close(self):
        for step in range(1, self.line.far):
            if step != 2:
                self.taken(step)

    def drain(self):
        line = self.line
        self.far_sends(lambda one: one.wait_send())
        self.copy(line.me, line.far - 1, line.partner).wait_send()
        self.other(lambda one: one.wait_send())
        if self.ends:
            for parity, slot in ((line.lo, 2 * line.far - 1), (1 - line.lo, 2 * line.far)):
                self.to_ends(parity, slot, lambda one: one.wait_send())


class SideScatter:
    def __init__(self, line, part, second, first, send, recv):
        self.line, self.part, self.second, self.first = line, part, second, first
        self.send, self.recv = send, recv

    def far_copy(self, step, parity):
        line = self.line
        hi = line.at(step)
        return line.push(
            hi * 2 + line.lo,
            self.part(hi * 2 + parity),
            self.second(parity * line.far + line.hi),
            self.send.at[2 * (step - 1) + parity],
            self.recv.at[parity * line.far + line.hi],
        )

    def near_copy(self):
        line = self.line
        return line.push(
            line.partner,
            self.part(line.partner),
            self.first,
            self.send.at[2 * line.far - 2],
            self.recv.at[2 * line.far],
        )

    def start(self):
        for step in range(1, self.line.far):
            for parity in range(2):
                self.far_copy(step, parity).start()

    def sum_of(self, parity):
        line = self.line
        value = self.part(line.hi * 2 + parity)[...].astype(F32)
        for step in range(1, line.far):
            index = parity * line.far + line.at(-step)
            block = self.second(index)
            line.push(
                line.partner, block, block, self.send.at[0], self.recv.at[index]
            ).wait_recv()
            value = value + block[...].astype(F32)
        return value

    def trade(self):
        given = self.part(self.line.partner)
        given[...] = self.sum_of(1 - self.line.lo).astype(LOW)
        self.near_copy().start()

    def arrive(self):
        pass

    def total(self):
        value = self.sum_of(self.line.lo)
        self.near_copy().wait_recv()
        return value + self.first[...].astype(F32)

    def drain(self):
        for step in range(1, self.line.far):
            for parity in range(2):
                self.far_copy(step, parity).wait_send()
        self.near_copy().wait_send()


class Scatter:
    def __init__(self, line, part, first, second, send, recv, base=0, extra=None):
        self.line, self.part, self.first, self.second = line, part, first, second
        self.send, self.recv, self.base = send, recv, base
        self.extra = extra if line.far == 4 else None

    def clear(self):
        line = self.line
        if self.extra is not None:

            @pl.when((line.hi == 0) | (line.hi == 3))
            def _():
                slot = self.second(3 - line.hi)
                slot[...] = jnp.zeros(slot.shape, LOW)

    def order(self, step):
        line = self.line
        if self.extra is None:
            return line.at(step)
        table = ((3, 2, 1), (2, 0, 3), (1, 3, 0), (0, 1, 2))
        hi = table[3][step - 1]
        for place in (2, 1, 0):
            hi = jnp.where(line.hi == place, table[place][step - 1], hi)
        return hi

    def traded(self, hi):
        line = self.line
        return line.push(
            line.partner,
            self.part(hi * 2 + (1 - line.lo)),
            self.first(hi),
            self.send.at[self.base + hi],
            self.recv.at[self.base + hi],
        )

    def passed(self, step):
        line = self.line
        hi = self.order(step)
        return line.push(
            hi * 2 + line.lo,
            self.part(hi * 2 + line.lo),
            self.second(line.hi),
            self.send.at[self.base + line.far + step - 1],
            self.recv.at[self.base + line.far + line.hi],
        )

    def to_next(self):
        line = self.line
        return line.push(
            jnp.where(line.hi < 2, 1, 2) * 2 + line.lo,
            self.part((3 - jnp.where(line.hi < 2, 0, 3)) * 2 + line.lo),
            self.extra,
            self.send.at[self.base + line.far],
            self.recv.at[self.base + 2 * line.far],
        )

    def turn_of(self, turn):
        line = self.line
        if self.extra is None:
            return lax.rem(line.hi + turn + 1, line.far)
        hi = line.hi
        for step in range(1, line.far):
            hi = jnp.where(turn == step - 1, self.order(step), hi)
        return hi

    def is_end(self):
        return (self.line.hi == 0) | (self.line.hi == 3)

    def trade(self, hi):
        self.traded(hi).start()

    def trade_all(self):
        for step in range(1, self.line.far + 1):
            self.trade(self.order(step) if step < self.line.far else self.line.hi)

    def pass_on(self, step):
        line = self.line
        hi = self.order(step)
        self.traded(hi).wait_recv()
        mine, other = self.part(hi * 2 + line.lo), self.first(hi)
        if self.extra is None or step == 2:
            mine[...] = (mine[...].astype(F32) + other[...].astype(F32)).astype(LOW)
            self.passed(step).start()
        elif step == 1:
            mine[...] = (mine[...].astype(F32) + other[...].astype(F32)).astype(LOW)

            @pl.when(self.is_end())
            def _():
                self.to_next().start()

            @pl.when(jnp.logical_not(self.is_end()))
            def _():
                self.passed(step).start()
        else:

            @pl.when(self.is_end())
            def _():
                mine[...] = (mine[...].astype(F32) + other[...].astype(F32)).astype(LOW)

            @pl.when(jnp.logical_not(self.is_end()))
            def _():
                line.push(
                    line.partner,
                    self.extra,
                    self.extra,
                    self.send.at[self.base],
                    self.recv.at[self.base + 2 * line.far],
                ).wait_recv()
                mine[...] = (
                    mine[...].astype(F32) + other[...].astype(F32) + self.extra[...].astype(F32)
                ).astype(LOW)

            self.passed(step).start()

    def arrive(self):
        line = self.line
        self.traded(line.hi).wait_recv()
        for step in range(1, line.far):
            hi = line.at(-step)
            one = line.push(
                line.partner,
                self.second(hi),
                self.second(hi),
                self.send.at[self.base],
                self.recv.at[self.base + line.far + hi],
            )
            if self.extra is None:
                one.wait_recv()
            else:
                pl.when(jnp.logical_not(self.is_end()) | (hi + line.hi != 3))(one.wait_recv)

    def total(self, here):
        line = self.line
        value = self.part(line.me)[here, :].astype(F32) + self.first(line.hi)[here, :].astype(F32)
        for step in range(1, line.far):
            value = value + self.second(line.at(-step))[here, :].astype(F32)
        return value

    def drain(self):
        line = self.line
        for step in range(line.far):
            self.traded(line.at(step)).wait_send()
        for step in range(1, line.far):
            if self.extra is not None and step == 1:
                pl.when(self.is_end())(lambda: self.to_next().wait_send())
                pl.when(jnp.logical_not(self.is_end()))(lambda: self.passed(1).wait_send())
            else:
                self.passed(step).wait_send()


def block_rows(ref, rows, first=0):
    return lambda index: ref.at[pl.ds(pl.multiple_of((index + first) * rows, rows), rows)]


def part_rows(ref, rows, first, count):
    return lambda index: ref.at[pl.ds(pl.multiple_of(index * rows + first, count), count)]


def of_index(ref):
    return lambda index: ref.at[index]


def norm_rows(values):
    center = values - jnp.mean(values, -1, keepdims=True)
    spread = jnp.mean(center * center, -1, keepdims=True)
    inverse = lax.rsqrt(spread + EPS_LAYER)
    return center * inverse, inverse


def norm_back(values, gain, grad):
    unit, inverse = norm_rows(values)
    inner = grad * gain
    shared = jnp.mean(inner, -1, keepdims=True)
    along = jnp.mean(inner * unit, -1, keepdims=True)
    return inverse * (inner - shared - unit * along), unit


def head_masks(width):
    lane = lax.broadcasted_iota(jnp.int32, (1, width), 1)
    return [
        jnp.where((lane >= head * HD) & (lane < (head + 1) * HD), 1.0, 0.0)
        for head in range(width // HD)
    ]


def spread_heads(values, masks):
    return jnp.concatenate([values * mask.astype(LOW) for mask in masks], 0)


def join_heads(values, masks, rows):
    total = values[0:rows] * masks[0]
    for head in range(1, len(masks)):
        total = total + values[head * rows : (head + 1) * rows] * masks[head]
    return total


TAIL = (
    0.2256758632450557,
    0.22566952478278277,
    0.2078438574180613,
    0.16853390514724884,
    0.14146086231844687,
    -0.005667717379728321,
    0.16915486959066833,
    -0.18294364197603524,
    0.05027260226320005,
)


def normal_tail(size, bell):
    base = 1.0 + (0.4 * 0.5**0.5) * size
    t = pl.reciprocal(base, approx=True)
    t = t * (2.0 - base * t)
    t = t * (2.0 - base * t)
    value = jnp.full_like(t, 0.5 * TAIL[-1])
    for factor in TAIL[-2::-1]:
        value = value * t + 0.5 * factor
    return value * t * bell


def far_copies(line, make, sends, recvs):
    def copy(step):
        dest = lax.rem(line.me + step, line.size)
        src, dst = make(dest, line.me)
        return line.push(dest, src, dst, sends.at[step], recvs.at[line.me])

    def wait():
        for step in range(1, line.size):
            source = lax.rem(line.me + line.size - step, line.size)
            _, dst = make(source, source)
            line.push(line.partner, dst, dst, sends.at[0], recvs.at[source]).wait_recv()

    return copy, wait


def layer_kernel(cap, names, *refs):
    R = types.SimpleNamespace(**dict(zip(names, refs)))
    dp, mp = Line("dp"), Line("mp")
    size, ways = dp.size, mp.size
    seqs, seq_len = R.ids.shape
    tokens, width = R.noise.shape
    model = R.cot.shape[1]
    heads_w = R.o.shape[1]
    hidden = R.wbf.shape[1]
    table_rows = R.table.shape[0]
    rin = R.w_in.shape[0]
    rin_up = round_up(rin, 16)
    quarter = model // ways
    strip = R.w_up.shape[0]
    spots = size * cap
    far = mp.far
    count = seqs * far
    half_strip = strip // 2
    own_strip = pl.ds(pl.multiple_of(dp.me * strip, strip), strip)
    mine = pl.ds(pl.multiple_of(dp.me * cap, cap), cap)

    some_rows = seq_len // 2

    def rows_of(piece):
        return lambda row: pl.ds(pl.multiple_of(piece * seq_len + row, some_rows), some_rows)

    def own_rows(piece):
        first = pl.multiple_of((piece * ways + mp.me) * seq_len, seq_len)
        return lambda row: pl.ds(pl.multiple_of(first + row, some_rows), some_rows)

    def by_rows(body, after=lambda half: None):
        for half in range(2):
            body(half * some_rows)
            after(half)

    class Rows:
        def __init__(self, ref, send, recv, piece):
            self.parts = [
                Gather(
                    mp,
                    lambda index, half=half: ref.at[
                        pl.ds(
                            pl.multiple_of(
                                (piece * ways + index) * seq_len + half * some_rows, some_rows
                            ),
                            some_rows,
                        )
                    ],
                    send,
                    recv,
                    (2 * piece + half) * ways,
                )
                for half in range(2)
            ]

        def start(self, half):
            self.parts[half].start()

        def relays(self):
            for part in self.parts:
                part.relays()

        def close(self):
            for part in self.parts:
                part.close()

        def drain(self):
            for part in self.parts:
                part.drain()

    def halves(ref, send, recv):
        return [Rows(ref, send, recv, piece) for piece in range(seqs)]

    chunk_cols = min(256, model)
    chunk_count = model // chunk_cols

    class Sums:
        def __init__(self, *refs):
            *self.refs, self.send, self.recv = refs

        def chunk(self, piece, chunk):
            cols = pl.ds(pl.multiple_of(chunk * chunk_cols, chunk_cols), chunk_cols)

            def blocks(ref, first):
                return lambda index: ref.at[
                    pl.ds(pl.multiple_of((index + first) * seq_len, seq_len), seq_len), cols
                ]

            firsts = (piece * ways, piece * far, piece * far)
            views = [blocks(ref, first) for ref, first in zip(self.refs, firsts)]
            return Scatter(mp, *views, self.send, self.recv, (piece * chunk_count + chunk) * ways)

        def total(self, piece, here):
            firsts = (piece * ways, piece * far, piece * far)
            views = [block_rows(ref, seq_len, first) for ref, first in zip(self.refs, firsts)]
            return Scatter(mp, *views, self.send, self.recv).total(here)

        def trade(self, piece, chunk):
            self.chunk(piece, chunk).trade_all()

        def hand_on(self, piece, chunk):
            scatter = self.chunk(piece, chunk)
            for step in range(1, far):
                scatter.pass_on(step)

        def every(self, act):
            def one(chunk, carry):
                act(chunk)
                return carry

            lax.fori_loop(0, chunk_count, one, 0)

        def hand_on_all(self, piece):
            self.every(lambda chunk: self.hand_on(piece, chunk))

        def arrive(self, piece):
            self.every(lambda chunk: self.chunk(piece, chunk).arrive())

        def drain(self, piece):
            self.every(lambda chunk: self.chunk(piece, chunk).drain())

        def products(self, piece, make):
            def one(chunk, carry):
                make(pl.ds(pl.multiple_of(chunk * chunk_cols, chunk_cols), chunk_cols))
                self.trade(piece, chunk)
                pl.when(chunk > 0)(lambda: self.hand_on(piece, chunk - 1))
                return carry

            lax.fori_loop(0, chunk_count, one, 0)

        def hand_on_last(self, piece):
            self.hand_on(piece, chunk_count - 1)

    many = ways * seq_len

    def turns(body, hooks=()):
        def one(piece, carry):
            def at(point):
                for place, when, action in hooks:
                    if when == point:
                        pl.when(piece == place)(action)

            base = pl.multiple_of(piece * many, many)
            body(piece, base, pl.ds(base, many), at)
            return carry

        lax.fori_loop(0, seqs, one, 0)

    def pairs(base, body):
        def one(pair, carry):
            first = pl.multiple_of(base + pair * (2 * seq_len), 2 * seq_len)
            body([pl.ds(pl.multiple_of(first + seq * seq_len, seq_len), seq_len) for seq in range(2)])
            return carry

        lax.fori_loop(0, far, one, 0)

    def chunks(total, body):
        step = min(256, total)
        lax.fori_loop(
            0,
            total // step,
            lambda turn, carry: (body(pl.ds(pl.multiple_of(turn * step, step), step)), carry)[1],
            0,
        )

    def later_pieces(gathers, point):
        hooks = []
        for piece in range(1, seqs):
            hooks.append((piece - 1, point, gathers[piece].relays))
            hooks.append((piece, "start", gathers[piece].close))
        return hooks

    chunk = R.tab.shape[1]
    pieces = -(-table_rows // chunk)

    def fetch(piece):
        rows = min(chunk, table_rows - piece * chunk)
        return pltpu.make_async_copy(
            R.table.at[pl.ds(piece * chunk, rows)],
            R.tab.at[piece % 2, pl.ds(0, rows)],
            R.tab_sem.at[piece % 2],
        )

    for piece in range(min(2, pieces)):
        fetch(piece).start()

    names_of_moments = [
        name + kind for name in ("w_in", "ln", "qkv", "out", "up", "down") for kind in ("_m", "_v")
    ]

    def moment(name):
        return pltpu.make_async_copy(
            getattr(R, name), getattr(R, name + "_here"), R.moment_sem.at[names_of_moments.index(name)]
        )

    tile_rows = R.tw.shape[1]
    tiles = table_rows // tile_rows

    shares_of = -(-tiles // ways)

    def share_tile(turn):
        return lax.min(turn * ways + mp.me, tiles - 1)

    def tile_of(turn):
        side = lax.rem(turn, 2)
        rows = pl.ds(pl.multiple_of(share_tile(turn) * tile_rows, tile_rows), tile_rows)
        return [
            pltpu.make_async_copy(source.at[rows], dest.at[side], R.tile_sem.at[2 * place + side])
            for place, (source, dest) in enumerate(
                ((R.table, R.tw), (R.table_m, R.tm), (R.table_v, R.tv))
            )
        ]

    eye = lax.broadcasted_iota(jnp.int32, (seq_len, seq_len), 0) == lax.broadcasted_iota(
        jnp.int32, (seq_len, seq_len), 1
    )
    id_rows = R.ids[...].astype(F32)
    ids = jnp.concatenate(
        [
            jnp.sum(jnp.where(eye, id_rows[seq : seq + 1, :], 0.0), 1, keepdims=True)
            for seq in range(seqs)
        ],
        0,
    )
    lane = lax.broadcasted_iota(jnp.int32, (tokens, 128), 1).astype(F32)
    low_end = lane * float(table_rows)
    owned = jnp.where((ids >= low_end) & (ids < low_end + float(table_rows)), 1.0, 0.0)
    before = jnp.where(
        lax.broadcasted_iota(jnp.int32, (tokens, tokens), 0)
        >= lax.broadcasted_iota(jnp.int32, (tokens, tokens), 1),
        1.0,
        0.0,
    )
    ranks = dot(before.astype(LOW), owned.astype(LOW))
    rank = jnp.sum(owned * ranks, 1, keepdims=True) - 1.0
    slot = jnp.sum(owned * lane, 1, keepdims=True) * cap + rank
    placed = jnp.where(lane == rank, 1.0, 0.0)
    upper = jnp.floor(ids * (1.0 / 256.0))
    lower = ids - upper * 256.0
    parts = jnp.concatenate([placed * upper, placed * lower, placed], 1).astype(LOW)
    asked = dot_tn(owned.astype(LOW), parts)
    asked = asked[:, :128] * 256.0 + asked[:, 128:256] + asked[:, 256:] - 1.0
    wide_ln = R.ln_params.shape[1]
    shares = R.ln_params[...].astype(LOW).astype(F32)
    if wide_ln < 128:
        shares = jnp.concatenate([shares, jnp.zeros((4, 128 - wide_ln), F32)], 1)
    for index in range(size):
        R.ask[index] = jnp.concatenate(
            [asked[index : index + 1, :], shares, jnp.zeros((3, 128), F32)], 0
        )
    R.idx[mp.me, dp.me] = R.ask[dp.me]

    def spread(part, first, second, extra, send, recv):
        blocks = [block_rows(ref, strip) for ref in (part, first, second)]
        return Scatter(dp, *blocks, send, recv, 0, extra)

    up = spread(R.wbf, R.up_first, R.up_second, R.up_extra, R.up_send, R.up_recv)
    down = spread(R.gdn, R.dn_first, R.dn_second, R.dn_extra, R.dn_send, R.dn_recv)
    first_w = spread(
        R.waf.at[:, : 3 * heads_w], R.wa_first, R.wa_second, R.wa_extra, R.ga_send, R.ga_recv
    )
    wo = SideScatter(
        dp,
        *[block_rows(ref, strip) for ref in (R.gwo, R.wo_second)],
        R.wo_first,
        R.wo_send,
        R.wo_recv,
    )
    small = Scatter(
        dp,
        *[of_index(ref) for ref in (R.gw, R.gw_first, R.gw_second)],
        R.gw_send,
        R.gw_recv,
        0,
        R.gw_extra,
    )
    for scatter in (up, down, first_w, small):
        scatter.clear()

    meet([mp], [dp])
    ask, ask_wait = far_copies(
        dp,
        lambda dest, source: (R.ask.at[dest], R.idx.at[mp.me, source]),
        R.ask_send,
        R.ask_recv,
    )
    for step in range(1, size):
        ask(step).start()

    mine_in = R.winf.at[mp.me]
    win = Gather(dp, block_rows(mine_in, rin), R.win_send, R.win_recv, 0, True)
    win_all = Gather(mp, of_index(R.winf), R.wim_send, R.wim_recv)
    wa = [
        Gather(dp, part_rows(R.waf, strip, piece * half_strip, half_strip), send, recv, 0, True)
        for piece, (send, recv) in enumerate(((R.wa_send, R.wa_recv), (R.wx_send, R.wx_recv)))
    ]
    wb = Gather(dp, block_rows(R.wbf, strip), R.wb_send, R.wb_recv, 0, True)
    wc = Gather(dp, part_rows(R.wcf, strip, 0, half_strip), R.wc_send, R.wc_recv, 0, True)
    wd = SideGather(dp, part_rows(R.wcf, strip, half_strip, half_strip), R.wd_send, R.wd_recv, 0, True)
    dxg = Gather(
        mp,
        lambda index: R.dx.at[:, pl.ds(pl.multiple_of(index * seq_len, seq_len), seq_len)],
        R.dx_send,
        R.dx_recv,
    )
    ag = halves(R.a, R.a_send, R.a_recv)
    cg = halves(R.c, R.c_send, R.c_recv)
    mg = halves(R.dmid_all, R.e_send, R.e_recv)

    mine_in[pl.ds(pl.multiple_of(dp.me * rin, rin), rin), :] = (
        R.w_in[:, pl.ds(pl.multiple_of(mp.me * quarter, quarter), quarter)]
        .astype(LOW)
        .astype(R.winf.dtype)
    )
    win.start()
    for part in range(3):
        R.waf[own_strip, part * heads_w : (part + 1) * heads_w] = R.w_qkv[part].astype(LOW)
    R.waf[own_strip, 3 * heads_w :] = R.w_out[...].T.astype(LOW)
    wa[0].start()
    wa[1].start_near()
    for name in names_of_moments:
        moment(name).start()

    win.relays()

    ask_wait()
    small_eye = lax.broadcasted_iota(jnp.int32, (cap, 128), 0) == lax.broadcasted_iota(
        jnp.int32, (cap, 128), 1
    )

    def locate(index, carry):
        row = R.idx[mp.me, index][0:1, :]
        column = jnp.sum(jnp.where(small_eye, row, 0.0), 1, keepdims=True)
        local = column.astype(jnp.int32) - dp.me * table_rows
        R.loc[pl.ds(pl.multiple_of(index * cap, cap), cap), :] = jnp.broadcast_to(local, (cap, 128))
        return carry

    lax.fori_loop(0, size, locate, 0, unroll=True)
    found = None
    for piece in range(pieces):
        fetch(piece).wait()
        rows = min(chunk, table_rows - piece * chunk)
        if rows < chunk:
            R.tab[piece % 2, rows:, :] = jnp.zeros((chunk - rows, width), F32)
        hit = (
            lax.broadcasted_iota(jnp.int32, (spots, chunk), 1) + piece * chunk == R.loc[:, 0:1]
        )
        more = dot(jnp.where(hit, 1.0, 0.0).astype(LOW), R.tab[piece % 2].astype(LOW))
        found = more if found is None else found + more
        if piece + 2 < pieces:
            fetch(piece + 2).start()
    R.give[...] = found.astype(LOW)

    give, give_wait = far_copies(
        dp,
        lambda dest, source: (block_rows(R.give, cap)(dest), block_rows(R.got, cap)(source)),
        R.give_send,
        R.give_recv,
    )
    for step in range(1, size):
        give(step).start()
    R.got[mine, :] = R.give[mine, :]
    wa[1].start_far()
    win.close()
    win_all.start()
    wa[0].relay(1)
    for seq in range(seqs):
        level = jnp.full((seq_len, 1), R.levels[seq], jnp.int32).astype(F32) / (LEVELS - 1)
        R.sig[seq * seq_len : (seq + 1) * seq_len, :] = jnp.exp(level * jnp.log(SIGMA_TOP))

    def scale_at(here):
        sig = R.sig[here, :]
        return sig * lax.rsqrt(1.0 + sig * sig)

    for piece in range(seqs):
        here = rows_of(piece)

        def scale_cot(row, here=here, piece=piece):
            there = pl.ds(pl.multiple_of(mp.me * seq_len + row, some_rows), some_rows)
            R.dx[piece, there, :] = (R.cot[here(row), :].astype(F32) * scale_at(here(row))).astype(LOW)

        by_rows(scale_cot)
    dxg.start()
    R.wbf[own_strip, :] = R.w_up[...].astype(LOW)
    R.wcf[own_strip, :] = R.w_down[...].T.astype(LOW)
    wb.start_near()
    R.pick[...] = jnp.where(
        lax.broadcasted_iota(jnp.int32, (tokens, spots), 1).astype(F32) == slot, 1.0, 0.0
    ).astype(LOW)
    win_all.relays()
    wa[0].relay(2)
    if wide_ln % 128 == 0:
        R.gains[...] = jnp.concatenate([R.idx[mp.me, index] for index in range(size)], 1)
    else:
        total = jnp.zeros((8, model), F32)
        for index in range(size):
            place = lax.broadcasted_iota(
                jnp.int32, (128, model), 1
            ) == index * wide_ln + lax.broadcasted_iota(jnp.int32, (128, model), 0)
            place = place & (lax.broadcasted_iota(jnp.int32, (128, model), 0) < wide_ln)
            total = total + dot(
                R.idx[mp.me, index].astype(LOW), jnp.where(place, 1.0, 0.0).astype(LOW)
            )
        R.gains[...] = total
    for step in range(3, dp.far):
        wa[0].relay(step)
    named = Gather(mp, of_index(R.idx), R.id_send, R.id_recv)

    give_wait()
    rows = dot(R.pick[...], R.got[...])
    R.rows[...] = rows.astype(LOW)
    sig = R.sig[...]
    unit = rows * lax.rsqrt(jnp.mean(rows * rows, -1, keepdims=True) + EPS_NORM)
    R.mixed[...] = ((unit + sig * R.noise[...].astype(F32)) * lax.rsqrt(1.0 + sig * sig)).astype(LOW)
    win_all.close()
    for index in range(ways):
        R.x0[:, index * quarter : (index + 1) * quarter] = dot(
            R.mixed[...], R.winf[index].astype(LOW)
        )

    for piece in range(seqs):
        here, there = rows_of(piece), own_rows(piece)

        def first_norm(row, here=here, there=there):
            normed, _ = norm_rows(R.x0[here(row), :])
            R.a[there(row), :] = (normed * R.gains[1:2, :] + R.gains[2:3, :]).astype(LOW)

        by_rows(first_norm, ag[piece].start)
    wa[1].relay(1)
    wb.start_far()
    for step in range(2, dp.far):
        wa[1].relay(step)
    dxg.relays()
    ag[0].relays()
    for gather in (*wa, ag[0]):
        gather.close()

    att = Sums(R.part, R.fold, R.fold_far, R.as_send, R.as_recv)
    dcs = Sums(R.part, R.fold, R.fold_far, R.cs_send, R.cs_recv)
    das = Sums(R.part, R.fold, R.fold_far, R.ds_send, R.ds_recv)
    out = Sums(R.c, R.first, R.second, R.os_send, R.os_recv)
    masks = head_masks(heads_w)

    all_rows = (heads_w // HD) * seq_len
    scale = HD ** (-0.5)

    def softmax(seq, row):
        scores = R.scores[seq, row : row + 64, :]
        raised = jnp.exp((scores - jnp.max(scores, -1, keepdims=True)) * scale)
        return raised * (1.0 / jnp.sum(raised, -1, keepdims=True))

    def attend(piece, base, here, at):
        at("start")
        for part in range(3):
            cols = slice(part * heads_w, (part + 1) * heads_w)
            R.qkv[here, cols] = dot(R.a[here, :], R.waf[:, cols]).astype(LOW)
        at("mid")

        def one(rows_at):
            for seq, rows in enumerate(rows_at):
                queries = spread_heads(R.qkv[rows, :heads_w], masks)
                R.scores[seq] = dot_nt(queries, R.qkv[rows, heads_w : 2 * heads_w])
            for seq, rows in enumerate(rows_at):
                for row in range(0, all_rows, 64):
                    R.probs[seq, row : row + 64, :] = softmax(seq, row).astype(LOW)
                seen = dot(R.probs[seq], R.qkv[rows, 2 * heads_w : 3 * heads_w])
                R.o[rows, :] = join_heads(seen, masks, seq_len).astype(LOW)

        pairs(base, one)
        at("late")

        def project(cols):
            R.part[here, cols] = dot_nt(R.o[here, :], R.waf[cols, 3 * heads_w :]).astype(LOW)

        def one_chunk(chunk, carry):
            project(pl.ds(pl.multiple_of(chunk * chunk_cols, chunk_cols), chunk_cols))
            att.trade(piece, chunk)
            return carry

        lax.fori_loop(0, chunk_count, one_chunk, 0)

    def second_norm(piece):
        here, there = rows_of(piece), own_rows(piece)
        att.arrive(piece)

        def norm(row):
            x1 = R.x0[here(row), :] + att.total(piece, pl.ds(row, some_rows))
            R.out[here(row), :] = x1
            normed, _ = norm_rows(x1)
            R.c[there(row), :] = (normed * R.gains[3:4, :] + R.gains[4:5, :]).astype(LOW)

        by_rows(norm, cg[piece].start)

    def first_wb():
        wb.relay(1)
        wd.start_near()
        wc.start_near()
        wc.start_far()

    def middle_wb():
        wb.relay(2)
        wd.start_far()

    def last_wb():
        wd.start_other()
        for step in range(3, dp.far):
            wb.relay(step)
        named.start()

    turns(
        attend,
        [
            *later_pieces(ag, "mid"),
            *[
                (piece + 1, "mid", functools.partial(att.hand_on_all, piece))
                for piece in range(seqs - 1)
            ],
            (0, "mid", first_wb),
            (0, "late", middle_wb),
            (1, "mid", last_wb),
            *[
                (piece + 1, "late", functools.partial(second_norm, piece))
                for piece in range(seqs - 1)
            ],
        ],
    )
    att.hand_on_all(seqs - 1)
    wc.relay(1)
    for gather in (*wa, *ag, dxg, win):
        gather.drain()
    for step in range(1, size):
        ask(step).wait_send()
    second_norm(seqs - 1)
    cg[0].relays()
    wc.relay(2)
    wb.close()
    named.relays()
    cg[0].close()
    for piece in range(seqs):
        att.drain(piece)

    def activate(piece, base, here, at):
        at("start")

        def some(cols):
            R.h[...] = dot(R.c[here, :], R.wbf[:, cols])

            def gelu(row):
                there = pl.ds(pl.multiple_of(base + row, 64), 64)
                h = R.h[pl.ds(row, 64), :]
                bell = jnp.exp(-0.5 * h * h)
                tail = normal_tail(jnp.abs(h), bell)
                gate = jnp.where(h >= 0.0, 1.0 - tail, tail)
                slope = gate + h * (bell * 0.3989422804014327)
                R.hb[there, cols] = (h * gate).astype(LOW)
                R.slope[there, cols] = slope.astype(LOW)

            strips(many, 64, gelu, 2)

        chunks(hidden, some)
        at("end")

    def last_wc():
        for step in range(3, dp.far):
            wc.relay(step)

    turns(activate, [*later_pieces(cg, "end"), (0, "end", last_wc), (seqs - 1, "start", wd.forward)])

    due = [(scatter, step) for scatter in (down, up) for step in range(1, dp.far)]

    def pass_due(number):
        for _ in range(min(number, len(due))):
            scatter, step = due.pop(0)
            scatter.pass_on(step)

    block = 2 * strip if (2 * strip) % 128 == 0 else min(256, model)

    def grads(make, trades):
        if block == 2 * strip:

            def turn_of(turn, carry):
                hi = up.turn_of(turn)
                make(pl.ds(pl.multiple_of(hi * block, block), block))
                for scatter in trades:
                    scatter.trade(hi)
                return carry

            lax.fori_loop(0, dp.far, turn_of, 0)
        else:
            strips(model, block, lambda col: make(pl.ds(col, block)))
            for scatter in trades:
                scatter.trade_all()

    def down_grads(cols):
        every = R.dx[:, :, cols]
        R.gdn[cols, :] = dot_tn(every.reshape(seqs * many, block), R.hb[...]).astype(LOW)

    def up_grads(cols):
        R.wbf[cols, :] = dot_tn(R.c[:, cols], R.dhb[...]).astype(LOW)

    dxg.close()
    grads(down_grads, (down,))
    named.close()
    groups = ways * size
    some, lanes_at = min(groups, 32), min(ways * spots, 512)
    for begin in range(0, ways * spots, lanes_at):
        spot = lax.broadcasted_iota(jnp.int32, (128, lanes_at), 1).astype(F32) + float(begin)
        block_no = jnp.floor((spot + 0.5) * (1.0 / cap))
        place = lax.broadcasted_iota(jnp.int32, (128, lanes_at), 0).astype(F32)
        spread_out = jnp.where(spot - block_no * cap == place, 1.0, 0.0).astype(LOW)
        named_row = jnp.zeros((1, lanes_at), F32)
        for first in range(0, groups, some):
            wanted = jnp.concatenate(
                [
                    R.idx[index // size, index % size][0:1, :] + 1.0
                    for index in range(first, first + some)
                ],
                0,
            )
            high = jnp.floor(wanted * (1.0 / 256.0))
            rest = wanted - 256.0 * high
            laid = dot(high.astype(LOW), spread_out) * 256.0 + dot(rest.astype(LOW), spread_out) - 1.0
            own_block = block_no[0:1, :] == float(first) + lax.broadcasted_iota(
                jnp.int32, (some, lanes_at), 0
            ).astype(F32)
            named_row = named_row + jnp.sum(jnp.where(own_block, laid, 0.0), 0, keepdims=True)
        R.named[:, begin : begin + lanes_at] = jnp.broadcast_to(
            named_row.astype(jnp.int32) - dp.me * table_rows, (8, lanes_at)
        )
    named.drain()
    wc.close()
    wd.close()
    for gather in (wb, *cg):
        gather.drain()

    def feed_back(piece, base, here, at):
        at("start")

        def some(cols):
            bent = dot(R.dx[piece], R.wcf[:, cols]) * R.slope[here, cols].astype(F32)
            R.dhb[here, cols] = bent.astype(LOW)

        chunks(hidden, some)
        at("mid")

        def project(cols):
            R.part[here, cols] = dot_nt(R.dhb[here, :], R.wbf[cols, :]).astype(LOW)

        dcs.products(piece, project)

    R.norms[...] = jnp.zeros_like(R.norms)

    def second_back(piece):
        here, there = rows_of(piece), own_rows(piece)
        dcs.arrive(piece)

        def back(row):
            dc = dcs.total(piece, pl.ds(row, some_rows))
            grad, unit = norm_back(R.out[here(row), :], R.gains[3:4, :], dc)
            grad = grad + R.cot[here(row), :].astype(F32) * scale_at(here(row))
            R.dmid[here(row), :] = grad
            R.dmid_all[there(row), :] = grad.astype(LOW)
            R.norms[2:3, :] += jnp.sum(dc * unit, 0, keepdims=True)
            R.norms[3:4, :] += jnp.sum(dc, 0, keepdims=True)

        by_rows(back, mg[piece].start)

    turns(
        feed_back,
        [
            *[
                (piece + 1, "mid", functools.partial(dcs.hand_on_last, piece))
                for piece in range(seqs - 1)
            ],
            (1, "mid", lambda: pass_due(1)),
        ],
    )
    dcs.hand_on_last(seqs - 1)
    second_back(0)
    pass_due(1)
    grads(up_grads, (up,))
    for piece in range(1, seqs):
        second_back(piece)
    pass_due(max(1, dp.far - 3))
    mg[0].relays()
    mg[0].close()
    for piece in range(seqs):
        dcs.drain(piece)

    def attend_back(piece, base, here, at):
        at("start")
        R.low[...] = dot(R.dmid_all[here, :], R.waf[:, 3 * heads_w :]).astype(LOW)
        at("mid")

        def one(rows_at):
            for seq, rows in enumerate(rows_at):
                queries = spread_heads(R.qkv[rows, :heads_w], masks)
                R.scores[seq] = dot_nt(queries, R.qkv[rows, heads_w : 2 * heads_w])
                upper_rows = pl.ds(pl.multiple_of(rows.start - base, seq_len), seq_len)
                R.upper[seq] = spread_heads(R.low[upper_rows, :], masks)
                R.dprobs[seq] = dot_nt(R.upper[seq], R.qkv[rows, 2 * heads_w : 3 * heads_w])
            for seq, rows in enumerate(rows_at):
                for row in range(0, all_rows, 64):
                    probs = softmax(seq, row)
                    grad_probs = R.dprobs[seq, row : row + 64, :]
                    inner = jnp.sum(probs * grad_probs, -1, keepdims=True)
                    R.probs[seq, row : row + 64, :] = probs.astype(LOW)
                    R.dscores[seq, row : row + 64, :] = (probs * (grad_probs - inner)).astype(LOW)
                keys = R.qkv[rows, heads_w : 2 * heads_w]
                queries = spread_heads(R.qkv[rows, :heads_w], masks)
                R.qkv[rows, 2 * heads_w : 3 * heads_w] = dot_tn(R.probs[seq], R.upper[seq]).astype(LOW)
                R.qkv[rows, heads_w : 2 * heads_w] = (dot_tn(R.dscores[seq], queries) * scale).astype(
                    LOW
                )
                R.qkv[rows, :heads_w] = (
                    join_heads(dot(R.dscores[seq], keys), masks, seq_len) * scale
                ).astype(LOW)

        pairs(base, one)
        at("late")

        def project(cols):
            R.part[here, cols] = dot_nt(R.qkv[here, :], R.waf[cols, : 3 * heads_w]).astype(LOW)

        das.products(piece, project)

    def first_back(piece):
        here = rows_of(piece)
        das.arrive(piece)

        def back(row):
            da = das.total(piece, pl.ds(row, some_rows))
            grad, unit = norm_back(R.x0[here(row), :], R.gains[1:2, :], da)
            R.dx0[here(row), :] = (R.dmid[here(row), :] + grad).astype(LOW)
            R.norms[0:1, :] += jnp.sum(da * unit, 0, keepdims=True)
            R.norms[1:2, :] += jnp.sum(da, 0, keepdims=True)

        by_rows(back)

    def out_grads():
        def make(cols):
            R.gwo[cols, :] = dot_tn(R.dmid_all[:, cols], R.o[...]).astype(LOW)

        grads(make, (wo,))

    turns(
        attend_back,
        [
            *later_pieces(mg, "mid"),
            (0, "late", lambda: pass_due(1)),
            *[
                (piece + 1, "mid", functools.partial(das.hand_on_last, piece))
                for piece in range(seqs - 1)
            ],
            (seqs - 1, "late", lambda: pass_due(1)),
        ],
    )
    das.hand_on_last(seqs - 1)
    def out_grads(cols):
        R.gwo[cols, :] = dot_tn(R.dmid_all[:, cols], R.o[...]).astype(LOW)

    def attend_grads(cols):
        R.waf[cols, : 3 * heads_w] = dot_tn(R.a[:, cols], R.qkv[...]).astype(LOW)

    grads(out_grads, ())
    wo.start()
    first_back(0)
    grads(attend_grads, (first_w,))
    for piece in range(1, seqs):
        first_back(piece)

    grad_mixed = sum(
        dot_nt(R.dx0[:, index * quarter : (index + 1) * quarter], R.winf[index].astype(LOW))
        for index in range(ways)
    )
    sig = R.sig[...]
    grad_unit = grad_mixed * lax.rsqrt(1.0 + sig * sig)
    rows = R.rows[...].astype(F32)
    inverse = lax.rsqrt(jnp.mean(rows * rows, -1, keepdims=True) + EPS_NORM)
    unit = rows * inverse
    grad_rows = inverse * (grad_unit - unit * jnp.mean(grad_unit * unit, -1, keepdims=True))
    for step in range(1, size):
        give(step).wait_send()
    R.give[...] = dot_tn(R.pick[...], grad_rows.astype(LOW)).astype(LOW)
    mine_inc = block_rows(R.inc, spots)(mp.me)
    back, back_wait = far_copies(
        dp,
        lambda dest, source: (block_rows(R.give, cap)(dest), block_rows(mine_inc, cap)(source)),
        R.back_send,
        R.back_recv,
    )
    for step in range(1, size):
        back(step).start()
    mine_inc[mine, :] = R.give[mine, :]

    small_mp = Scatter(
        mp, of_index(R.gm), of_index(R.gm_first), of_index(R.gm_second), R.gm_send, R.gm_recv
    )
    for index in range(ways):
        cols = slice(index * quarter, (index + 1) * quarter)
        R.gm[index, :width, :] = dot_tn(R.mixed[...], R.dx0[:, cols]).astype(LOW)
        R.gm[index, width:, :] = jnp.concatenate(
            [R.norms[0:4, cols], jnp.zeros((12, quarter), F32)], 0
        ).astype(LOW)
    small_mp.trade_all()
    pass_due(len(due))
    for step in range(1, far):
        small_mp.pass_on(step)

    first_w.pass_on(1)

    def feed_out(piece, base, here, at):
        def project(cols):
            R.c[here, cols] = dot_nt(R.hb[here, :], R.wcf[cols, :]).astype(LOW)

        out.products(piece, project)

    turns(feed_out)
    wo.trade()
    first_w.pass_on(2)
    for turn in range(min(2, shares_of)):
        for one in tile_of(turn):
            one.start()
    back_wait()
    rows_in = Gather(mp, block_rows(R.inc, spots), R.in_send, R.in_recv)
    rows_in.start()
    for piece in range(seqs):
        out.hand_on_last(piece)

    small_mp.arrive()
    summed = small_mp.total(slice(None))
    for index in range(size):
        piece = summed[index * rin : (index + 1) * rin, :]
        if rin_up > rin:
            piece = jnp.concatenate([piece, jnp.zeros((rin_up - rin, quarter), F32)], 0)
        R.gw[index, :rin_up, :] = piece.astype(LOW)
        R.gw[index, rin_up:, :] = summed[width:, :].astype(LOW)
    small.trade_all()
    rows_in.relays()
    for step in range(3, dp.far):
        first_w.pass_on(step)

    def finish_out(piece):
        here = rows_of(piece)
        out.arrive(piece)

        def finish(row):
            R.out[here(row), :] = (
                R.out[here(row), :] + out.total(piece, pl.ds(row, some_rows))
            ) * scale_at(here(row))

        by_rows(finish)

    for piece in range(seqs):
        finish_out(piece)

    rows_in.close()

    once = jnp.where(mp.me == 0, 1.0, 0.0)
    lanes = lax.broadcasted_iota(jnp.int32, (1, 128), 1)
    R.sums[...] = jnp.zeros_like(R.sums)

    def put(place, squares, factor=None):
        for row, values in enumerate(squares):
            total = jnp.sum(jnp.sum(values, 0, keepdims=True), 1, keepdims=True)
            if factor is not None:
                total = total * factor
            R.sums[row : row + 1, :] += jnp.where(lanes == place, total, 0.0)

    def squares_of(weight, gradient, first, second):
        direction = direction_of(weight, gradient, first, second)[2]
        return weight * weight, direction * direction

    def folded(values):
        rows, columns = values.shape
        return jnp.sum(values.reshape(rows // 8, 8, columns), 0)

    def add_up(weight, gradient, first, second):
        squares = squares_of(weight[...], gradient[...], first[...], second[...])
        return [folded(values) for values in squares]

    zero = jnp.zeros((8, width), F32)

    rest = [
        functools.partial(scatter.pass_on, step)
        for scatter in (small,)
        for step in range(1, dp.far)
    ]
    tail_hooks = [
        (min(shares_of - 1, place * shares_of // len(rest)), action)
        for place, action in enumerate(rest)
    ]

    def add_tile(turn, carry):
        side = lax.rem(turn, 2)
        for place, action in tail_hooks:
            pl.when(turn == place)(action)
        for one in tile_of(turn):
            one.wait()
        hit = (
            lax.broadcasted_iota(jnp.int32, (tile_rows, ways * spots), 0)
            + share_tile(turn) * tile_rows
            == R.named[0:1, :]
        )
        gradient = dot(jnp.where(hit, 1.0, 0.0).astype(LOW), R.inc[...])
        more = add_up(R.tw.at[side], gradient, R.tm.at[side], R.tv.at[side])
        counts = jnp.where(turn * ways + mp.me < tiles, 1.0, 0.0)

        @pl.when(turn + 2 < shares_of)
        def _():
            for one in tile_of(turn + 2):
                one.start()

        return carry[0] + counts * more[0], carry[1] + counts * more[1]

    put(0, lax.fori_loop(0, shares_of, add_tile, (zero, zero)))

    for thing in (win_all, wc, wd, *mg, up, down, small_mp):
        thing.drain()
    for piece in range(seqs):
        out.drain(piece)
        das.drain(piece)
    for step in range(1, size):
        back(step).wait_send()

    for name in names_of_moments:
        moment(name).wait()
    up.arrive()

    R.red_up[...] = up.total(slice(None))
    put(10, add_up(R.w_up, R.red_up, R.up_m_here, R.up_v_here))
    down.arrive()

    R.red_dn[...] = down.total(slice(None)).T
    put(11, add_up(R.w_down, R.red_dn, R.down_m_here, R.down_v_here))
    wo.arrive()
    R.red_out[...] = wo.total().T
    put(9, add_up(R.w_out, R.red_out, R.out_m_here, R.out_v_here))

    small.arrive()
    R.wsum[mp.me] = small.total(slice(None)).astype(LOW)
    weights_in = Gather(mp, of_index(R.wsum), R.ws_send, R.ws_recv)
    weights_in.start()
    first_w.arrive()

    value = first_w.total(slice(None))
    for part in range(3):
        R.red_qkv[part] = value[:, part * heads_w : (part + 1) * heads_w]
    weights_in.relays()
    for part in range(3):
        put(
            6 + part,
            add_up(
                R.w_qkv.at[part], R.red_qkv.at[part], R.qkv_m_here.at[part], R.qkv_v_here.at[part]
            ),
        )
    weights_in.close()
    total = jnp.concatenate([R.wsum[index].astype(F32) for index in range(ways)], 1)
    R.red_in[...] = total[:rin, :]
    put(1, add_up(R.w_in, R.red_in, R.w_in_m_here, R.w_in_v_here), once)
    if strip % 128 == 0:
        R.lnsum[...] = total[rin_up : rin_up + 8, :]
        R.red_ln[...] = R.lnsum[0:4, pl.ds(pl.multiple_of(dp.me * strip, strip), strip)]
    else:
        chosen = lax.broadcasted_iota(jnp.int32, (model, strip), 0) == dp.me * strip + (
            lax.broadcasted_iota(jnp.int32, (model, strip), 1)
        )
        R.red_ln[...] = dot(
            total[rin_up : rin_up + 8, :].astype(LOW), jnp.where(chosen, 1.0, 0.0).astype(LOW)
        )[0:4]
    squares = squares_of(R.ln_params[...], R.red_ln[...], R.ln_m_here[...], R.ln_v_here[...])
    for row in range(4):
        put(2 + row, [values[row : row + 1, :] for values in squares], once)

    R.near[dp.me] = R.sums[...]
    near, near_wait = far_copies(
        dp, lambda dest, source: (R.near.at[dp.me], R.near.at[source]), R.near_send, R.near_recv
    )
    for step in range(1, size):
        near(step).start()
    near_wait()
    R.wide[mp.me] = jnp.sum(R.near[...], 0)
    far_off, far_off_wait = far_copies(
        mp, lambda dest, source: (R.wide.at[mp.me], R.wide.at[source]), R.wide_send, R.wide_recv
    )
    for step in range(1, ways):
        far_off(step).start()
    far_off_wait()
    R.totals[...] = jnp.sum(R.wide[...], 0)

    for thing in (wo, first_w, small, rows_in, weights_in):
        thing.drain()
    for step in range(1, size):
        near(step).wait_send()
    for step in range(1, ways):
        far_off(step).wait_send()


def run_layer(cap, ids, levels, noise, cot, weights, moments):
    table, w_in, ln_params, w_qkv, w_out, w_up, w_down = weights
    dp, mp = lax.axis_size("dp"), lax.axis_size("mp")
    seqs, seq_len = ids.shape
    tokens, width = noise.shape
    model = cot.shape[1]
    rin = w_in.shape[0]
    heads_w = w_qkv.shape[2]
    strip, hidden = w_up.shape
    group = tokens * mp
    spots = dp * cap
    wide = round_up(rin, 16) + 16
    far, far_dp = mp // 2, dp // 2
    quarter = model // mp
    in_kind = LOW if rin % 16 == 0 else F32
    tile_rows = max(rows for rows in range(8, 257, 8) if table.shape[0] % rows == 0)
    stacked = (heads_w // HD) * seq_len
    vmem = pl.BlockSpec(memory_space=pltpu.VMEM)
    outside = pl.BlockSpec(memory_space=pl.ANY)
    inputs = dict(
        ids=(ids, vmem),
        levels=(levels, pl.BlockSpec(memory_space=pltpu.SMEM)),
        noise=(noise, vmem),
        cot=(cot, vmem),
        table=(table, outside),
        w_in=(w_in, vmem),
        ln_params=(ln_params, vmem),
        w_qkv=(w_qkv, vmem),
        w_out=(w_out, vmem),
        w_up=(w_up, vmem),
        w_down=(w_down, vmem),
    )
    kept = {}
    for name, (first, second) in zip(("table", "w_in", "ln", "qkv", "out", "up", "down"), moments):
        inputs[name + "_m"] = (first, outside)
        inputs[name + "_v"] = (second, outside)
        if name != "table":
            kept[name + "_m_here"] = kept[name + "_v_here"] = (first.shape, F32)
    outputs = dict(
        out=((tokens, model), F32),
        red_up=((strip, hidden), F32),
        red_dn=((hidden, strip), F32),
        red_qkv=((3, strip, heads_w), F32),
        red_out=((heads_w, strip), F32),
        red_in=((rin, model), F32),
        red_ln=((4, strip), F32),
        inc=((mp * spots, width), LOW),
        named=((8, mp * spots), jnp.int32),
        totals=((8, 128), F32),
    )
    buffers = dict(
        tab=((2, round_up(table.shape[0] // 8, 128), width), F32),
        ask=((dp, 8, 128), F32),
        idx=((mp, dp, 8, 128), F32),
        loc=((spots, 128), jnp.int32),
        give=((spots, width), LOW),
        got=((spots, width), LOW),
        tw=((2, tile_rows, width), F32),
        tm=((2, tile_rows, width), F32),
        tv=((2, tile_rows, width), F32),
        sums=((8, 128), F32),
        near=((dp, 8, 128), F32),
        wide=((mp, 8, 128), F32),
        scores=((2, stacked, seq_len), F32),
        dprobs=((2, stacked, seq_len), F32),
        probs=((2, stacked, seq_len), LOW),
        dscores=((2, stacked, seq_len), LOW),
        upper=((2, stacked, heads_w), LOW),
        gwo=((model, heads_w), LOW),
        wo_first=((strip, heads_w), LOW),
        wo_second=((dp * strip, heads_w), LOW),
        gains=((8, model), F32),
        lnsum=((8, model), F32),
        sig=((tokens, 1), F32),
        pick=((tokens, spots), LOW),
        rows=((tokens, width), LOW),
        mixed=((tokens, width), LOW),
        x0=((tokens, model), F32),
        a=((group, model), LOW),
        c=((group, model), LOW),
        dx=((seqs, group // seqs, model), LOW),
        dmid=((tokens, model), F32),
        dmid_all=((group, model), LOW),
        winf=((mp, rin * dp, quarter), in_kind),
        waf=((model, 4 * heads_w), LOW),
        wbf=((model, hidden), LOW),
        wcf=((model, hidden), LOW),
        qkv=((group, 3 * heads_w), LOW),
        o=((group, heads_w), LOW),
        low=((group // seqs, heads_w), LOW),
        part=((group, model), LOW),
        first=((far * tokens, model), LOW),
        fold=((far * tokens, model), LOW),
        second=((far * tokens, model), LOW),
        fold_far=((far * tokens, model), LOW),
        h=((group // seqs, min(256, hidden)), F32),
        hb=((group, hidden), LOW),
        dhb=((group, hidden), LOW),
        slope=((group, hidden), LOW),
        gdn=((model, hidden), LOW),
        dx0=((tokens, model), LOW),
        norms=((8, model), F32),
        gm=((mp, width + 16, quarter), LOW),
        gm_first=((far, width + 16, quarter), LOW),
        gm_second=((far, width + 16, quarter), LOW),
        gw=((dp, wide, quarter), LOW),
        gw_first=((far_dp, wide, quarter), LOW),
        gw_second=((far_dp, wide, quarter), LOW),
        up_first=((far_dp * strip, hidden), LOW),
        up_second=((far_dp * strip, hidden), LOW),
        dn_first=((far_dp * strip, hidden), LOW),
        dn_second=((far_dp * strip, hidden), LOW),
        wa_first=((far_dp * strip, 3 * heads_w), LOW),
        wa_second=((far_dp * strip, 3 * heads_w), LOW),
        wsum=((mp, wide, quarter), LOW),
        up_extra=((strip, hidden), LOW),
        dn_extra=((strip, hidden), LOW),
        wa_extra=((strip, 3 * heads_w), LOW),
        gw_extra=((wide, quarter), LOW),
        **kept,
    )
    sems = dict(tab_sem=2, tile_sem=6, moment_sem=12)
    for name in (
        *("win", "wa", "wx", "wb", "wc", "wd", "ask", "give", "back"),
        *("up", "dn", "ga", "wo", "gw", "near"),
    ):
        sems[name + "_send"] = sems[name + "_recv"] = dp + 1
    for name in ("wim", "id", "in", "ws", "gm", "wide"):
        sems[name + "_send"] = sems[name + "_recv"] = mp
    for name in ("dx", "a", "c", "e"):
        sems[name + "_send"] = sems[name + "_recv"] = 2 * seqs * mp
    for name in ("as", "os", "cs", "ds"):
        sems[name + "_send"] = sems[name + "_recv"] = seqs * mp * (model // min(256, model))
    names = [*inputs, *outputs, *buffers, *sems]
    made = pl.pallas_call(
        functools.partial(layer_kernel, cap, names),
        out_shape=[jax.ShapeDtypeStruct(shape, kind) for shape, kind in outputs.values()],
        in_specs=[spec for _, spec in inputs.values()],
        out_specs=[vmem] * len(outputs),
        scratch_shapes=[
            *[pltpu.VMEM(shape, kind) for shape, kind in buffers.values()],
            *[pltpu.SemaphoreType.DMA((number,)) for number in sems.values()],
        ],
        compiler_params=pltpu.CompilerParams(
            vmem_limit_bytes=VMEM_BYTES, collective_id=1, has_side_effects=True
        ),
        name="layer",
    )(*[value for value, _ in inputs.values()])
    return dict(zip(outputs, made))


def direction_of(weight, gradient, first, second):
    first_new = BETA_ONE * first + (1.0 - BETA_ONE) * gradient
    second_new = BETA_TWO * second + (1.0 - BETA_TWO) * gradient * gradient
    second_hat = second_new * (1.0 / (1.0 - BETA_TWO**STEP))
    inverse = lax.rsqrt(second_hat)
    root = second_hat * inverse + EPS_ADAM
    inverse = inverse * (2.0 - root * inverse)
    inverse = inverse * (2.0 - root * inverse)
    direction = first_new * (1.0 / (1.0 - BETA_ONE**STEP)) * inverse + DECAY * weight
    return first_new, second_new, direction


def update_kernel(part, names, *refs):
    R = types.SimpleNamespace(**dict(zip(names, refs)))
    turn = pl.program_id(0)
    R.out_rows[...] = R.made[...]
    norms = jnp.sqrt(R.totals[...])
    R.norms[...] = norms[0:2, 0:12]
    factors = norms[0:1, :] / (norms[1:2, :] + EPS_ADAM) * RATE

    def piece(name, here, gradient, place, rows=slice(None)):
        weight = getattr(R, name)[here]
        first_new, second_new, direction = direction_of(
            weight, gradient, getattr(R, name + "_m")[here], getattr(R, name + "_v")[here]
        )
        if isinstance(place, int):
            factor = factors[0:1, place : place + 1]
        else:
            factor = jnp.concatenate([factors[0:1, one : one + 1] for one in place], 0)
        getattr(R, name + "_m_new")[here] = first_new
        getattr(R, name + "_v_new")[here] = second_new
        getattr(R, name + "_new")[here] = weight - factor * direction

    def update(name, gradient, place, lead=(), here=slice(None)):
        piece(name, (*lead, here, slice(None)), gradient, place)

    tile = R.table.shape[0]
    spots = R.named.shape[1]

    def table_part(row):
        hit = (
            lax.broadcasted_iota(jnp.int32, (part, spots), 0) + (turn * tile + row)
            == R.named[0:1, :]
        )
        gradient = dot(jnp.where(hit, 1.0, 0.0).astype(LOW), R.inc[...])
        update("table", gradient, 0, (), pl.ds(row, part))

    strips(tile, part, table_part)
    for group in range(3):
        update("qkv", R.red_qkv[group], 6 + group, (group,))
    update("up", R.red_up[...], 10)
    update("down", R.red_dn[...], 11)

    @pl.when(turn == 0)
    def _():
        update("out", R.red_out[...], 9)
        update("w_in", R.red_in[...], 1)
        piece("ln", (slice(None), slice(None)), R.red_ln[...], (2, 3, 4, 5))


def turns_of(rows, parts):
    return [
        turns
        for turns in (5, 4, 2, 1)
        if rows % (8 * turns) == 0 and all(size % (8 * turns) == 0 for size in parts)
    ][0]


def run_update(weights, moments, grads):
    names = ("table", "w_in", "ln", "qkv", "out", "up", "down")
    by_name = dict(zip(names, weights))
    rows, width = by_name["table"].shape
    strip, hidden = by_name["up"].shape
    heads_w = by_name["qkv"].shape[2]
    turns = turns_of(rows, (strip, hidden))
    tile = rows // turns
    part = max(size for size in range(8, 257, 8) if tile % size == 0)
    fixed = lambda array: pl.BlockSpec(array.shape, lambda turn: (0,) * array.ndim)
    specs = dict(
        table=pl.BlockSpec((tile, width), lambda turn: (turn, 0)),
        w_in=fixed(by_name["w_in"]),
        ln=fixed(by_name["ln"]),
        qkv=pl.BlockSpec((3, strip // turns, heads_w), lambda turn: (0, turn, 0)),
        out=fixed(by_name["out"]),
        up=pl.BlockSpec((strip // turns, hidden), lambda turn: (turn, 0)),
        down=pl.BlockSpec((hidden // turns, strip), lambda turn: (turn, 0)),
    )
    inputs = {}
    for name, weight, (first, second) in zip(names, weights, moments):
        inputs[name] = (weight, specs[name])
        inputs[name + "_m"] = (first, specs[name])
        inputs[name + "_v"] = (second, specs[name])
    for name, like in (
        ("red_up", "up"),
        ("red_dn", "down"),
        ("red_qkv", "qkv"),
        ("red_out", "out"),
        ("red_in", "w_in"),
        ("red_ln", "ln"),
    ):
        inputs[name] = (grads[name], specs[like])
    for name in ("inc", "named", "totals"):
        inputs[name] = (grads[name], fixed(grads[name]))
    tokens, model = grads["out"].shape
    rows_spec = pl.BlockSpec((tokens // turns, model), lambda turn: (turn, 0))
    inputs["made"] = (grads["out"], rows_spec)
    outputs = {"out_rows": (grads["out"].shape, rows_spec)}
    for name, weight in by_name.items():
        for kind in ("_new", "_m_new", "_v_new"):
            outputs[name + kind] = (weight.shape, specs[name])
    outputs["norms"] = ((2, 12), pl.BlockSpec((2, 12), lambda turn: (0, 0)))
    results = pl.pallas_call(
        functools.partial(update_kernel, part, [*inputs, *outputs]),
        grid=(turns,),
        out_shape=[jax.ShapeDtypeStruct(shape, F32) for shape, _ in outputs.values()],
        in_specs=[spec for _, spec in inputs.values()],
        out_specs=[spec for _, spec in outputs.values()],
        compiler_params=pltpu.CompilerParams(vmem_limit_bytes=VMEM_BYTES),
        name="update",
    )(*[value for value, _ in inputs.values()])
    return list(results)


def per_device(
    token_ids,
    levels,
    noise,
    cotangent,
    table,
    table_m,
    table_v,
    w_in,
    w_in_m,
    w_in_v,
    ln_params,
    ln_m,
    ln_v,
    w_qkv,
    qkv_m,
    qkv_v,
    w_out,
    out_m,
    out_v,
    w_up,
    up_m,
    up_v,
    w_down,
    down_m,
    down_v,
):
    dp_count = lax.axis_size("dp")
    seq_count, seq_len = token_ids.shape
    tokens = seq_count * seq_len
    model = cotangent.shape[2]
    cap = round_up(max(2, (3 * tokens + 2 * dp_count - 1) // (2 * dp_count)), 16)
    weights = (table, w_in, ln_params, w_qkv, w_out, w_up, w_down)
    moments = (
        (table_m, table_v),
        (w_in_m, w_in_v),
        (ln_m, ln_v),
        (qkv_m, qkv_v),
        (out_m, out_v),
        (up_m, up_v),
        (down_m, down_v),
    )
    grads = run_layer(
        cap,
        token_ids,
        levels,
        noise.reshape(tokens, -1),
        cotangent.reshape(tokens, model),
        weights,
        moments,
    )
    out, *results = run_update(weights, moments, grads)
    return (out.reshape(seq_count, seq_len, model), *results)


def solution(mesh):
    return jax.shard_map(
        per_device,
        mesh=mesh,
        in_specs=(
            P(("dp", "mp"), None),
            P(("dp", "mp")),
            P(("dp", "mp"), None, None),
            P(("dp", "mp"), None, None),
            P("dp", None),
            P("dp", None),
            P("dp", None),
            P("dp", None),
            P("dp", None),
            P("dp", None),
            P(None, "dp"),
            P(None, "dp"),
            P(None, "dp"),
            P(None, "dp", "mp"),
            P(None, "dp", "mp"),
            P(None, "dp", "mp"),
            P("mp", "dp"),
            P("mp", "dp"),
            P("mp", "dp"),
            P("dp", "mp"),
            P("dp", "mp"),
            P("dp", "mp"),
            P("mp", "dp"),
            P("mp", "dp"),
            P("mp", "dp"),
        ),
        out_specs=(
            P(("dp", "mp"), None, None),
            P("dp", None),
            P("dp", None),
            P("dp", None),
            P("dp", None),
            P("dp", None),
            P("dp", None),
            P(None, "dp"),
            P(None, "dp"),
            P(None, "dp"),
            P(None, "dp", "mp"),
            P(None, "dp", "mp"),
            P(None, "dp", "mp"),
            P("mp", "dp"),
            P("mp", "dp"),
            P("mp", "dp"),
            P("dp", "mp"),
            P("dp", "mp"),
            P("dp", "mp"),
            P("mp", "dp"),
            P("mp", "dp"),
            P("mp", "dp"),
            P(),
        ),
        check_vma=False,
    )
```

```python
import functools
import types

import jax
import jax.numpy as jnp
from jax import lax
from jax.experimental import pallas as pl
from jax.experimental.pallas import tpu as pltpu
from jax.sharding import PartitionSpec as P

HD = 64
LEVELS = 64
STEP = 10


EPS_NORM = 1e-06
EPS_LAYER = 1e-05
EPS_ADAM = 1e-06
BETA_ONE = 0.9
BETA_TWO = 0.999
DECAY = 0.01
RATE = 0.5
SIGMA_TOP = 10.0

F32 = jnp.float32
LOW = jnp.bfloat16
VMEM_BYTES = 63 * 1024 * 1024


def sigma_of(levels):
    frac = levels.astype(jnp.float32) / (LEVELS - 1)
    return jnp.exp(frac * jnp.log(SIGMA_TOP))


def lamb_moments(weight, gradient, first, second):
    first_new = BETA_ONE * first + (1.0 - BETA_ONE) * gradient
    second_new = BETA_TWO * second + (1.0 - BETA_TWO) * gradient * gradient
    first_hat = first_new / (1.0 - BETA_ONE**STEP)
    second_hat = second_new / (1.0 - BETA_TWO**STEP)
    direction = first_hat / (jnp.sqrt(second_hat) + EPS_ADAM) + DECAY * weight
    return (first_new, second_new, direction)


def trust_factors(ratio):
    return (
        ratio[0],
        ratio[1],
        ratio[2:6][:, None],
        ratio[6:9][:, None, None],
        ratio[9],
        ratio[10],
        ratio[11],
    )


def round_up(value, step):
    return -(-value // step) * step


def dot(left, right):
    return jnp.dot(left, right, preferred_element_type=F32)


def dot_nt(left, right):
    return lax.dot_general(left, right, (((1,), (1,)), ((), ())), preferred_element_type=F32)


def dot_tn(left, right):
    return lax.dot_general(left, right, (((0,), (0,)), ((), ())), preferred_element_type=F32)


def strips(total, step, body, unroll=1):
    step = min(step, total)

    def one(turn, carry):
        body(pl.multiple_of(turn * step, step))
        return carry

    lax.fori_loop(0, total // step, one, 0, unroll=unroll)


class Line:
    def __init__(self, axis):
        self.axis = axis
        self.size = lax.axis_size(axis)
        self.far = self.size // 2
        self.me = lax.axis_index(axis)
        self.hi = lax.div(self.me, 2)
        self.lo = lax.rem(self.me, 2)
        self.partner = self.hi * 2 + (1 - self.lo)

    def at(self, step):
        return lax.rem(self.hi + step + self.far, self.far)

    def push(self, index, src, dst, send, recv):
        return pltpu.make_async_remote_copy(
            src_ref=src,
            dst_ref=dst,
            send_sem=send,
            recv_sem=recv,
            device_id={self.axis: index},
            device_id_type=pl.DeviceIdType.MESH,
        )

    def signal(self, sem, index):
        pl.semaphore_signal(
            sem, inc=1, device_id={self.axis: index}, device_id_type=pl.DeviceIdType.MESH
        )


def meet(pair_lines, all_lines=()):
    sem = pltpu.get_barrier_semaphore()
    count = 0
    for line in pair_lines:
        for step in range(1, line.far):
            line.signal(sem, line.at(step) * 2 + line.lo)
            count += 1
        line.signal(sem, line.partner)
        count += 1
    for line in all_lines:
        for step in range(1, line.size):
            line.signal(sem, lax.rem(line.me + step, line.size))
            count += 1
    pl.semaphore_wait(sem, count)


class Gather:
    def __init__(self, line, at, send, recv, base=0, ends=False):
        self.line, self.at, self.send, self.recv, self.base = line, at, send, recv, base
        self.ends = ends and line.far == 4

    def source(self, step):
        line = self.line
        if not self.ends:
            return line.at(-step)
        order = ((1, 2, 3), (0, 3, 2), (3, 0, 1), (2, 1, 0))
        hi = order[3][step - 1]
        for place in (2, 1, 0):
            hi = jnp.where(line.hi == place, order[place][step - 1], hi)
        return hi

    def far_sends(self, act):
        line = self.line
        for step in range(1, line.far):
            one = self.copy(line.me, step - 1, line.at(step) * 2 + line.lo)
            if self.ends and step != 2:
                pl.when(line.hi != (3 if step == 1 else 0))(functools.partial(act, one))
            else:
                act(one)

    def to_end(self, act):
        line = self.line
        dest = jnp.where(line.hi == 1, 0, 3)
        one = self.copy((3 - dest) * 2 + line.lo, 2 * line.far - 1, dest * 2 + line.lo)
        pl.when((line.hi == 1) | (line.hi == 2))(functools.partial(act, one))

    def copy(self, index, slot, dest):
        block = self.at(index)
        return self.line.push(
            dest, block, block, self.send.at[self.base + slot], self.recv.at[self.base + index]
        )

    def start_far(self):
        self.far_sends(lambda one: one.start())

    def start_near(self):
        self.copy(self.line.me, self.line.far - 1, self.line.partner).start()

    def start(self):
        self.start_far()
        self.start_near()

    def relay(self, step):
        line = self.line
        handed = self.copy(self.source(step) * 2 + line.lo, line.far - 1 + step, line.partner)
        handed.wait_recv()
        if self.ends and step == 2:
            self.to_end(lambda one: one.start())
        handed.start()

    def relays(self):
        for step in range(1, self.line.far):
            self.relay(step)

    def close(self):
        line = self.line
        for step in range(line.far):
            self.copy(line.at(-step) * 2 + (1 - line.lo), 0, line.partner).wait_recv()

    def drain(self):
        self.far_sends(lambda one: one.wait_send())
        if self.ends:
            self.to_end(lambda one: one.wait_send())
        for slot in range(self.line.far - 1, 2 * self.line.far - 1):
            self.copy(self.line.me, slot, self.line.partner).wait_send()


class SideGather(Gather):
    def other(self, act):
        line = self.line
        for step in range(1, line.far):
            one = self.copy(line.partner, line.far - 1 + step, line.at(step) * 2 + line.lo)
            if self.ends and step != 2:
                pl.when(line.hi != (3 if step == 1 else 0))(functools.partial(act, one))
            else:
                act(one)

    def to_ends(self, parity, slot, act):
        line = self.line
        dest = jnp.where(line.hi == 1, 0, 3)
        one = self.copy((3 - dest) * 2 + parity, slot, dest * 2 + line.lo)
        pl.when((line.hi == 1) | (line.hi == 2))(functools.partial(act, one))

    def start_other(self):
        self.copy(self.line.partner, 0, self.line.partner).wait_recv()
        self.other(lambda one: one.start())

    def taken(self, step):
        line = self.line
        for parity, slot in ((line.lo, 2 * line.far - 1), (1 - line.lo, 2 * line.far)):
            self.copy(self.source(step) * 2 + parity, 0, line.partner).wait_recv()
            if self.ends and step == 2:
                self.to_ends(parity, slot, lambda one: one.start())

    def forward(self):
        if self.line.far > 2:
            self.taken(2)

    def close(self):
        for step in range(1, self.line.far):
            if step != 2:
                self.taken(step)

    def drain(self):
        line = self.line
        self.far_sends(lambda one: one.wait_send())
        self.copy(line.me, line.far - 1, line.partner).wait_send()
        self.other(lambda one: one.wait_send())
        if self.ends:
            for parity, slot in ((line.lo, 2 * line.far - 1), (1 - line.lo, 2 * line.far)):
                self.to_ends(parity, slot, lambda one: one.wait_send())


class SideScatter:
    def __init__(self, line, part, second, first, send, recv):
        self.line, self.part, self.second, self.first = line, part, second, first
        self.send, self.recv = send, recv

    def far_copy(self, step, parity):
        line = self.line
        hi = line.at(step)
        return line.push(
            hi * 2 + line.lo,
            self.part(hi * 2 + parity),
            self.second(parity * line.far + line.hi),
            self.send.at[2 * (step - 1) + parity],
            self.recv.at[parity * line.far + line.hi],
        )

    def near_copy(self):
        line = self.line
        return line.push(
            line.partner,
            self.part(line.partner),
            self.first,
            self.send.at[2 * line.far - 2],
            self.recv.at[2 * line.far],
        )

    def start(self):
        for step in range(1, self.line.far):
            for parity in range(2):
                self.far_copy(step, parity).start()

    def sum_of(self, parity):
        line = self.line
        value = self.part(line.hi * 2 + parity)[...].astype(F32)
        for step in range(1, line.far):
            index = parity * line.far + line.at(-step)
            block = self.second(index)
            line.push(
                line.partner, block, block, self.send.at[0], self.recv.at[index]
            ).wait_recv()
            value = value + block[...].astype(F32)
        return value

    def trade(self):
        given = self.part(self.line.partner)
        given[...] = self.sum_of(1 - self.line.lo).astype(LOW)
        self.near_copy().start()

    def arrive(self):
        pass

    def total(self):
        value = self.sum_of(self.line.lo)
        self.near_copy().wait_recv()
        return value + self.first[...].astype(F32)

    def drain(self):
        for step in range(1, self.line.far):
            for parity in range(2):
                self.far_copy(step, parity).wait_send()
        self.near_copy().wait_send()


class Scatter:
    def __init__(self, line, part, first, second, send, recv, base=0, extra=None):
        self.line, self.part, self.first, self.second = line, part, first, second
        self.send, self.recv, self.base = send, recv, base
        self.extra = extra if line.far == 4 else None

    def clear(self):
        line = self.line
        if self.extra is not None:

            @pl.when((line.hi == 0) | (line.hi == 3))
            def _():
                slot = self.second(3 - line.hi)
                slot[...] = jnp.zeros(slot.shape, LOW)

    def order(self, step):
        line = self.line
        if self.extra is None:
            return line.at(step)
        table = ((3, 2, 1), (2, 0, 3), (1, 3, 0), (0, 1, 2))
        hi = table[3][step - 1]
        for place in (2, 1, 0):
            hi = jnp.where(line.hi == place, table[place][step - 1], hi)
        return hi

    def traded(self, hi):
        line = self.line
        return line.push(
            line.partner,
            self.part(hi * 2 + (1 - line.lo)),
            self.first(hi),
            self.send.at[self.base + hi],
            self.recv.at[self.base + hi],
        )

    def passed(self, step):
        line = self.line
        hi = self.order(step)
        return line.push(
            hi * 2 + line.lo,
            self.part(hi * 2 + line.lo),
            self.second(line.hi),
            self.send.at[self.base + line.far + step - 1],
            self.recv.at[self.base + line.far + line.hi],
        )

    def to_next(self):
        line = self.line
        return line.push(
            jnp.where(line.hi < 2, 1, 2) * 2 + line.lo,
            self.part((3 - jnp.where(line.hi < 2, 0, 3)) * 2 + line.lo),
            self.extra,
            self.send.at[self.base + line.far],
            self.recv.at[self.base + 2 * line.far],
        )

    def turn_of(self, turn):
        line = self.line
        if self.extra is None:
            return lax.rem(line.hi + turn + 1, line.far)
        hi = line.hi
        for step in range(1, line.far):
            hi = jnp.where(turn == step - 1, self.order(step), hi)
        return hi

    def is_end(self):
        return (self.line.hi == 0) | (self.line.hi == 3)

    def trade(self, hi):
        self.traded(hi).start()

    def trade_all(self):
        for step in range(1, self.line.far + 1):
            self.trade(self.order(step) if step < self.line.far else self.line.hi)

    def pass_on(self, step):
        line = self.line
        hi = self.order(step)
        self.traded(hi).wait_recv()
        mine, other = self.part(hi * 2 + line.lo), self.first(hi)
        if self.extra is None or step == 2:
            mine[...] = (mine[...].astype(F32) + other[...].astype(F32)).astype(LOW)
            self.passed(step).start()
        elif step == 1:
            mine[...] = (mine[...].astype(F32) + other[...].astype(F32)).astype(LOW)

            @pl.when(self.is_end())
            def _():
                self.to_next().start()

            @pl.when(jnp.logical_not(self.is_end()))
            def _():
                self.passed(step).start()
        else:

            @pl.when(self.is_end())
            def _():
                mine[...] = (mine[...].astype(F32) + other[...].astype(F32)).astype(LOW)

            @pl.when(jnp.logical_not(self.is_end()))
            def _():
                line.push(
                    line.partner,
                    self.extra,
                    self.extra,
                    self.send.at[self.base],
                    self.recv.at[self.base + 2 * line.far],
                ).wait_recv()
                mine[...] = (
                    mine[...].astype(F32) + other[...].astype(F32) + self.extra[...].astype(F32)
                ).astype(LOW)

            self.passed(step).start()

    def arrive(self):
        line = self.line
        self.traded(line.hi).wait_recv()
        for step in range(1, line.far):
            hi = line.at(-step)
            one = line.push(
                line.partner,
                self.second(hi),
                self.second(hi),
                self.send.at[self.base],
                self.recv.at[self.base + line.far + hi],
            )
            if self.extra is None:
                one.wait_recv()
            else:
                pl.when(jnp.logical_not(self.is_end()) | (hi + line.hi != 3))(one.wait_recv)

    def total(self, here):
        line = self.line
        value = self.part(line.me)[here, :].astype(F32) + self.first(line.hi)[here, :].astype(F32)
        for step in range(1, line.far):
            value = value + self.second(line.at(-step))[here, :].astype(F32)
        return value

    def drain(self):
        line = self.line
        for step in range(line.far):
            self.traded(line.at(step)).wait_send()
        for step in range(1, line.far):
            if self.extra is not None and step == 1:
                pl.when(self.is_end())(lambda: self.to_next().wait_send())
                pl.when(jnp.logical_not(self.is_end()))(lambda: self.passed(1).wait_send())
            else:
                self.passed(step).wait_send()


def block_rows(ref, rows, first=0):
    return lambda index: ref.at[pl.ds(pl.multiple_of((index + first) * rows, rows), rows)]


def part_rows(ref, rows, first, count):
    return lambda index: ref.at[pl.ds(pl.multiple_of(index * rows + first, count), count)]


def of_index(ref):
    return lambda index: ref.at[index]


def norm_rows(values):
    center = values - jnp.mean(values, -1, keepdims=True)
    spread = jnp.mean(center * center, -1, keepdims=True)
    inverse = lax.rsqrt(spread + EPS_LAYER)
    return center * inverse, inverse


def norm_back(values, gain, grad):
    unit, inverse = norm_rows(values)
    inner = grad * gain
    shared = jnp.mean(inner, -1, keepdims=True)
    along = jnp.mean(inner * unit, -1, keepdims=True)
    return inverse * (inner - shared - unit * along), unit


def head_masks(width):
    lane = lax.broadcasted_iota(jnp.int32, (1, width), 1)
    return [
        jnp.where((lane >= head * HD) & (lane < (head + 1) * HD), 1.0, 0.0)
        for head in range(width // HD)
    ]


def spread_heads(values, masks):
    return jnp.concatenate([values * mask.astype(LOW) for mask in masks], 0)


def join_heads(values, masks, rows):
    total = values[0:rows] * masks[0]
    for head in range(1, len(masks)):
        total = total + values[head * rows : (head + 1) * rows] * masks[head]
    return total


TAIL = (
    0.2256758632450557,
    0.22566952478278277,
    0.2078438574180613,
    0.16853390514724884,
    0.14146086231844687,
    -0.005667717379728321,
    0.16915486959066833,
    -0.18294364197603524,
    0.05027260226320005,
)


def normal_tail(size, bell):
    base = 1.0 + (0.4 * 0.5**0.5) * size
    t = pl.reciprocal(base, approx=True)
    t = t * (2.0 - base * t)
    t = t * (2.0 - base * t)
    value = jnp.full_like(t, 0.5 * TAIL[-1])
    for factor in TAIL[-2::-1]:
        value = value * t + 0.5 * factor
    return value * t * bell


def far_copies(line, make, sends, recvs):
    def copy(step):
        dest = lax.rem(line.me + step, line.size)
        src, dst = make(dest, line.me)
        return line.push(dest, src, dst, sends.at[step], recvs.at[line.me])

    def wait():
        for step in range(1, line.size):
            source = lax.rem(line.me + line.size - step, line.size)
            _, dst = make(source, source)
            line.push(line.partner, dst, dst, sends.at[0], recvs.at[source]).wait_recv()

    return copy, wait


def layer_kernel(cap, names, *refs):
    R = types.SimpleNamespace(**dict(zip(names, refs)))
    dp, mp = Line("dp"), Line("mp")
    size, ways = dp.size, mp.size
    seqs, seq_len = R.ids.shape
    tokens, width = R.noise.shape
    model = R.cot.shape[1]
    heads_w = R.o.shape[1]
    hidden = R.wbf.shape[1]
    table_rows = R.table.shape[0]
    rin = R.w_in.shape[0]
    rin_up = round_up(rin, 16)
    quarter = model // ways
    strip = R.w_up.shape[0]
    spots = size * cap
    far = mp.far
    count = seqs * far
    half_strip = strip // 2
    own_strip = pl.ds(pl.multiple_of(dp.me * strip, strip), strip)
    mine = pl.ds(pl.multiple_of(dp.me * cap, cap), cap)

    some_rows = seq_len // 2

    def rows_of(piece):
        return lambda row: pl.ds(pl.multiple_of(piece * seq_len + row, some_rows), some_rows)

    def own_rows(piece):
        first = pl.multiple_of((piece * ways + mp.me) * seq_len, seq_len)
        return lambda row: pl.ds(pl.multiple_of(first + row, some_rows), some_rows)

    def by_rows(body, after=lambda half: None):
        for half in range(2):
            body(half * some_rows)
            after(half)

    class Rows:
        def __init__(self, ref, send, recv, piece):
            self.parts = [
                Gather(
                    mp,
                    lambda index, half=half: ref.at[
                        pl.ds(
                            pl.multiple_of(
                                (piece * ways + index) * seq_len + half * some_rows, some_rows
                            ),
                            some_rows,
                        )
                    ],
                    send,
                    recv,
                    (2 * piece + half) * ways,
                )
                for half in range(2)
            ]

        def start(self, half):
            self.parts[half].start()

        def relays(self):
            for part in self.parts:
                part.relays()

        def close(self):
            for part in self.parts:
                part.close()

        def drain(self):
            for part in self.parts:
                part.drain()

    def halves(ref, send, recv):
        return [Rows(ref, send, recv, piece) for piece in range(seqs)]

    chunk_cols = min(256, model)
    chunk_count = model // chunk_cols

    class Sums:
        def __init__(self, *refs):
            *self.refs, self.send, self.recv = refs

        def chunk(self, piece, chunk):
            cols = pl.ds(pl.multiple_of(chunk * chunk_cols, chunk_cols), chunk_cols)

            def blocks(ref, first):
                return lambda index: ref.at[
                    pl.ds(pl.multiple_of((index + first) * seq_len, seq_len), seq_len), cols
                ]

            firsts = (piece * ways, piece * far, piece * far)
            views = [blocks(ref, first) for ref, first in zip(self.refs, firsts)]
            return Scatter(mp, *views, self.send, self.recv, (piece * chunk_count + chunk) * ways)

        def total(self, piece, here):
            firsts = (piece * ways, piece * far, piece * far)
            views = [block_rows(ref, seq_len, first) for ref, first in zip(self.refs, firsts)]
            return Scatter(mp, *views, self.send, self.recv).total(here)

        def trade(self, piece, chunk):
            self.chunk(piece, chunk).trade_all()

        def hand_on(self, piece, chunk):
            scatter = self.chunk(piece, chunk)
            for step in range(1, far):
                scatter.pass_on(step)

        def every(self, act):
            def one(chunk, carry):
                act(chunk)
                return carry

            lax.fori_loop(0, chunk_count, one, 0)

        def hand_on_all(self, piece):
            self.every(lambda chunk: self.hand_on(piece, chunk))

        def arrive(self, piece):
            self.every(lambda chunk: self.chunk(piece, chunk).arrive())

        def drain(self, piece):
            self.every(lambda chunk: self.chunk(piece, chunk).drain())

        def products(self, piece, make):
            def one(chunk, carry):
                make(pl.ds(pl.multiple_of(chunk * chunk_cols, chunk_cols), chunk_cols))
                self.trade(piece, chunk)
                pl.when(chunk > 0)(lambda: self.hand_on(piece, chunk - 1))
                return carry

            lax.fori_loop(0, chunk_count, one, 0)

        def hand_on_last(self, piece):
            self.hand_on(piece, chunk_count - 1)

    many = ways * seq_len

    def turns(body, hooks=()):
        def one(piece, carry):
            def at(point):
                for place, when, action in hooks:
                    if when == point:
                        pl.when(piece == place)(action)

            base = pl.multiple_of(piece * many, many)
            body(piece, base, pl.ds(base, many), at)
            return carry

        lax.fori_loop(0, seqs, one, 0)

    def pairs(base, body):
        def one(pair, carry):
            first = pl.multiple_of(base + pair * (2 * seq_len), 2 * seq_len)
            body([pl.ds(pl.multiple_of(first + seq * seq_len, seq_len), seq_len) for seq in range(2)])
            return carry

        lax.fori_loop(0, far, one, 0)

    def chunks(total, body):
        step = min(256, total)
        lax.fori_loop(
            0,
            total // step,
            lambda turn, carry: (body(pl.ds(pl.multiple_of(turn * step, step), step)), carry)[1],
            0,
        )

    def later_pieces(gathers, point):
        hooks = []
        for piece in range(1, seqs):
            hooks.append((piece - 1, point, gathers[piece].relays))
            hooks.append((piece, "start", gathers[piece].close))
        return hooks

    chunk = R.tab.shape[1]
    pieces = -(-table_rows // chunk)

    def fetch(piece):
        rows = min(chunk, table_rows - piece * chunk)
        return pltpu.make_async_copy(
            R.table.at[pl.ds(piece * chunk, rows)],
            R.tab.at[piece % 2, pl.ds(0, rows)],
            R.tab_sem.at[piece % 2],
        )

    for piece in range(min(2, pieces)):
        fetch(piece).start()

    names_of_moments = [
        name + kind for name in ("w_in", "ln", "qkv", "out", "up", "down") for kind in ("_m", "_v")
    ]

    def store(name):
        place = ("out", "red_up", "red_dn", "red_qkv", "inc").index(name)
        return pltpu.make_async_copy(
            getattr(R, name), getattr(R, name + "_hbm"), R.store_sem.at[place]
        )

    def moment(name):
        return pltpu.make_async_copy(
            getattr(R, name), getattr(R, name + "_here"), R.moment_sem.at[names_of_moments.index(name)]
        )

    tile_rows = R.tw.shape[1]
    tiles = table_rows // tile_rows

    shares_of = -(-tiles // ways)

    def share_tile(turn):
        return lax.min(turn * ways + mp.me, tiles - 1)

    def tile_of(turn):
        side = lax.rem(turn, 2)
        rows = pl.ds(pl.multiple_of(share_tile(turn) * tile_rows, tile_rows), tile_rows)
        return [
            pltpu.make_async_copy(source.at[rows], dest.at[side], R.tile_sem.at[2 * place + side])
            for place, (source, dest) in enumerate(
                ((R.table, R.tw), (R.table_m, R.tm), (R.table_v, R.tv))
            )
        ]

    eye = lax.broadcasted_iota(jnp.int32, (seq_len, seq_len), 0) == lax.broadcasted_iota(
        jnp.int32, (seq_len, seq_len), 1
    )
    id_rows = R.ids[...].astype(F32)
    ids = jnp.concatenate(
        [
            jnp.sum(jnp.where(eye, id_rows[seq : seq + 1, :], 0.0), 1, keepdims=True)
            for seq in range(seqs)
        ],
        0,
    )
    lane = lax.broadcasted_iota(jnp.int32, (tokens, 128), 1).astype(F32)
    low_end = lane * float(table_rows)
    owned = jnp.where((ids >= low_end) & (ids < low_end + float(table_rows)), 1.0, 0.0)
    before = jnp.where(
        lax.broadcasted_iota(jnp.int32, (tokens, tokens), 0)
        >= lax.broadcasted_iota(jnp.int32, (tokens, tokens), 1),
        1.0,
        0.0,
    )
    ranks = dot(before.astype(LOW), owned.astype(LOW))
    rank = jnp.sum(owned * ranks, 1, keepdims=True) - 1.0
    slot = jnp.sum(owned * lane, 1, keepdims=True) * cap + rank
    placed = jnp.where(lane == rank, 1.0, 0.0)
    upper = jnp.floor(ids * (1.0 / 256.0))
    lower = ids - upper * 256.0
    parts = jnp.concatenate([placed * upper, placed * lower, placed], 1).astype(LOW)
    asked = dot_tn(owned.astype(LOW), parts)
    asked = asked[:, :128] * 256.0 + asked[:, 128:256] + asked[:, 256:] - 1.0
    wide_ln = R.ln_params.shape[1]
    shares = R.ln_params[...].astype(LOW).astype(F32)
    if wide_ln < 128:
        shares = jnp.concatenate([shares, jnp.zeros((4, 128 - wide_ln), F32)], 1)
    for index in range(size):
        R.ask[index] = jnp.concatenate(
            [asked[index : index + 1, :], shares, jnp.zeros((3, 128), F32)], 0
        )
    R.idx[mp.me, dp.me] = R.ask[dp.me]

    def spread(part, first, second, extra, send, recv):
        blocks = [block_rows(ref, strip) for ref in (part, first, second)]
        return Scatter(dp, *blocks, send, recv, 0, extra)

    up = spread(R.wbf, R.up_first, R.up_second, R.up_extra, R.up_send, R.up_recv)
    down = spread(R.gdn, R.dn_first, R.dn_second, R.dn_extra, R.dn_send, R.dn_recv)
    first_w = spread(
        R.waf.at[:, : 3 * heads_w], R.wa_first, R.wa_second, R.wa_extra, R.ga_send, R.ga_recv
    )
    wo = SideScatter(
        dp,
        *[block_rows(ref, strip) for ref in (R.gwo, R.wo_second)],
        R.wo_first,
        R.wo_send,
        R.wo_recv,
    )
    for scatter in (up, down, first_w):
        scatter.clear()

    meet([mp], [dp])
    ask, ask_wait = far_copies(
        dp,
        lambda dest, source: (R.ask.at[dest], R.idx.at[mp.me, source]),
        R.ask_send,
        R.ask_recv,
    )
    for step in range(1, size):
        ask(step).start()

    mine_in = R.winf.at[mp.me]
    win = Gather(dp, block_rows(mine_in, rin), R.win_send, R.win_recv, 0, True)
    win_all = Gather(mp, of_index(R.winf), R.wim_send, R.wim_recv)
    wa = [
        Gather(dp, part_rows(R.waf, strip, piece * half_strip, half_strip), send, recv, 0, True)
        for piece, (send, recv) in enumerate(((R.wa_send, R.wa_recv), (R.wx_send, R.wx_recv)))
    ]
    wb = Gather(dp, block_rows(R.wbf, strip), R.wb_send, R.wb_recv, 0, True)
    wc = Gather(dp, part_rows(R.wcf, strip, 0, half_strip), R.wc_send, R.wc_recv, 0, True)
    wd = SideGather(dp, part_rows(R.wcf, strip, half_strip, half_strip), R.wd_send, R.wd_recv, 0, True)
    dxg = Gather(
        mp,
        lambda index: R.dx.at[:, pl.ds(pl.multiple_of(index * seq_len, seq_len), seq_len)],
        R.dx_send,
        R.dx_recv,
    )
    ag = halves(R.a, R.a_send, R.a_recv)
    cg = halves(R.c, R.c_send, R.c_recv)
    mg = halves(R.dmid_all, R.e_send, R.e_recv)

    mine_in[pl.ds(pl.multiple_of(dp.me * rin, rin), rin), :] = (
        R.w_in[:, pl.ds(pl.multiple_of(mp.me * quarter, quarter), quarter)]
        .astype(LOW)
        .astype(R.winf.dtype)
    )
    win.start()
    for part in range(3):
        R.waf[own_strip, part * heads_w : (part + 1) * heads_w] = R.w_qkv[part].astype(LOW)
    R.waf[own_strip, 3 * heads_w :] = R.w_out[...].T.astype(LOW)
    wa[0].start()
    wa[1].start_near()

    ask_wait()
    small_eye = lax.broadcasted_iota(jnp.int32, (cap, 128), 0) == lax.broadcasted_iota(
        jnp.int32, (cap, 128), 1
    )

    def locate(index, carry):
        row = R.idx[mp.me, index][0:1, :]
        column = jnp.sum(jnp.where(small_eye, row, 0.0), 1, keepdims=True)
        local = column.astype(jnp.int32) - dp.me * table_rows
        R.loc[pl.ds(pl.multiple_of(index * cap, cap), cap), :] = jnp.broadcast_to(local, (cap, 128))
        return carry

    lax.fori_loop(0, size, locate, 0, unroll=True)
    win.relays()
    found = None
    for piece in range(pieces):
        fetch(piece).wait()
        rows = min(chunk, table_rows - piece * chunk)
        if rows < chunk:
            R.tab[piece % 2, rows:, :] = jnp.zeros((chunk - rows, width), F32)
        hit = (
            lax.broadcasted_iota(jnp.int32, (spots, chunk), 1) + piece * chunk == R.loc[:, 0:1]
        )
        more = dot(jnp.where(hit, 1.0, 0.0).astype(LOW), R.tab[piece % 2].astype(LOW))
        found = more if found is None else found + more
        if piece + 2 < pieces:
            fetch(piece + 2).start()
    R.give[...] = found.astype(LOW)

    give, give_wait = far_copies(
        dp,
        lambda dest, source: (block_rows(R.give, cap)(dest), block_rows(R.got, cap)(source)),
        R.give_send,
        R.give_recv,
    )
    for step in range(1, size):
        give(step).start()
    R.got[mine, :] = R.give[mine, :]
    wa[1].start_far()
    named = Gather(mp, of_index(R.idx), R.id_send, R.id_recv)
    named.start()
    for name in names_of_moments:
        moment(name).start()
    win.close()
    win_all.start()
    wa[0].relay(1)
    for seq in range(seqs):
        level = jnp.full((seq_len, 1), R.levels[seq], jnp.int32).astype(F32) / (LEVELS - 1)
        R.sig[seq * seq_len : (seq + 1) * seq_len, :] = jnp.exp(level * jnp.log(SIGMA_TOP))

    def scale_at(here):
        sig = R.sig[here, :]
        return sig * lax.rsqrt(1.0 + sig * sig)

    for piece in range(seqs):
        here = rows_of(piece)

        def scale_cot(row, here=here, piece=piece):
            there = pl.ds(pl.multiple_of(mp.me * seq_len + row, some_rows), some_rows)
            R.dx[piece, there, :] = (R.cot[here(row), :].astype(F32) * scale_at(here(row))).astype(LOW)

        by_rows(scale_cot)
    dxg.start()
    R.wbf[own_strip, :] = R.w_up[...].astype(LOW)
    R.wcf[own_strip, :] = R.w_down[...].T.astype(LOW)
    wb.start_near()
    R.pick[...] = jnp.where(
        lax.broadcasted_iota(jnp.int32, (tokens, spots), 1).astype(F32) == slot, 1.0, 0.0
    ).astype(LOW)
    win_all.relays()
    named.relays()
    wa[0].relay(2)
    if wide_ln % 128 == 0:
        R.gains[...] = jnp.concatenate([R.idx[mp.me, index] for index in range(size)], 1)
    else:
        total = jnp.zeros((8, model), F32)
        for index in range(size):
            place = lax.broadcasted_iota(
                jnp.int32, (128, model), 1
            ) == index * wide_ln + lax.broadcasted_iota(jnp.int32, (128, model), 0)
            place = place & (lax.broadcasted_iota(jnp.int32, (128, model), 0) < wide_ln)
            total = total + dot(
                R.idx[mp.me, index].astype(LOW), jnp.where(place, 1.0, 0.0).astype(LOW)
            )
        R.gains[...] = total
    for step in range(3, dp.far):
        wa[0].relay(step)

    give_wait()
    rows = dot(R.pick[...], R.got[...])
    R.rows[...] = rows.astype(LOW)
    sig = R.sig[...]
    unit = rows * lax.rsqrt(jnp.mean(rows * rows, -1, keepdims=True) + EPS_NORM)
    R.mixed[...] = ((unit + sig * R.noise[...].astype(F32)) * lax.rsqrt(1.0 + sig * sig)).astype(LOW)
    win_all.close()
    for index in range(ways):
        R.x0[:, index * quarter : (index + 1) * quarter] = dot(
            R.mixed[...], R.winf[index].astype(LOW)
        )

    for piece in range(seqs):
        here, there = rows_of(piece), own_rows(piece)

        def first_norm(row, here=here, there=there):
            normed, _ = norm_rows(R.x0[here(row), :])
            R.a[there(row), :] = (normed * R.gains[1:2, :] + R.gains[2:3, :]).astype(LOW)

        by_rows(first_norm, ag[piece].start)
    wa[1].relay(1)
    wb.start_far()
    for step in range(2, dp.far):
        wa[1].relay(step)
    dxg.relays()
    ag[0].relays()
    named.close()
    groups = ways * size
    some, lanes_at = min(groups, 32), min(ways * spots, 512)
    for begin in range(0, ways * spots, lanes_at):
        spot = lax.broadcasted_iota(jnp.int32, (128, lanes_at), 1).astype(F32) + float(begin)
        block_no = jnp.floor((spot + 0.5) * (1.0 / cap))
        place = lax.broadcasted_iota(jnp.int32, (128, lanes_at), 0).astype(F32)
        spread_out = jnp.where(spot - block_no * cap == place, 1.0, 0.0).astype(LOW)
        named_row = jnp.zeros((1, lanes_at), F32)
        for first in range(0, groups, some):
            wanted = jnp.concatenate(
                [
                    R.idx[index // size, index % size][0:1, :] + 1.0
                    for index in range(first, first + some)
                ],
                0,
            )
            high = jnp.floor(wanted * (1.0 / 256.0))
            rest = wanted - 256.0 * high
            laid = dot(high.astype(LOW), spread_out) * 256.0 + dot(rest.astype(LOW), spread_out) - 1.0
            own_block = block_no[0:1, :] == float(first) + lax.broadcasted_iota(
                jnp.int32, (some, lanes_at), 0
            ).astype(F32)
            named_row = named_row + jnp.sum(jnp.where(own_block, laid, 0.0), 0, keepdims=True)
        R.named[:, begin : begin + lanes_at] = jnp.broadcast_to(
            named_row.astype(jnp.int32) - dp.me * table_rows, (8, lanes_at)
        )
    named.drain()
    for gather in (*wa, ag[0]):
        gather.close()

    att = Sums(R.part, R.fold, R.fold_far, R.as_send, R.as_recv)
    dcs = Sums(R.part, R.fold, R.fold_far, R.cs_send, R.cs_recv)
    das = Sums(R.part, R.fold, R.fold_far, R.ds_send, R.ds_recv)
    out = Sums(R.c, R.first, R.second, R.os_send, R.os_recv)
    masks = head_masks(heads_w)

    all_rows = (heads_w // HD) * seq_len
    scale = HD ** (-0.5)

    def softmax(seq, row):
        scores = R.scores[seq, row : row + 64, :]
        raised = jnp.exp((scores - jnp.max(scores, -1, keepdims=True)) * scale)
        return raised * (1.0 / jnp.sum(raised, -1, keepdims=True))

    def attend(piece, base, here, at):
        at("start")
        for part in range(3):
            cols = slice(part * heads_w, (part + 1) * heads_w)
            R.qkv[here, cols] = dot(R.a[here, :], R.waf[:, cols]).astype(LOW)
        at("mid")

        def one(rows_at):
            for seq, rows in enumerate(rows_at):
                queries = spread_heads(R.qkv[rows, :heads_w], masks)
                R.scores[seq] = dot_nt(queries, R.qkv[rows, heads_w : 2 * heads_w])
            for seq, rows in enumerate(rows_at):
                for row in range(0, all_rows, 64):
                    R.probs[seq, row : row + 64, :] = softmax(seq, row).astype(LOW)
                seen = dot(R.probs[seq], R.qkv[rows, 2 * heads_w : 3 * heads_w])
                R.o[rows, :] = join_heads(seen, masks, seq_len).astype(LOW)

        pairs(base, one)
        at("late")

        def project(cols):
            R.part[here, cols] = dot_nt(R.o[here, :], R.waf[cols, 3 * heads_w :]).astype(LOW)

        def one_chunk(chunk, carry):
            project(pl.ds(pl.multiple_of(chunk * chunk_cols, chunk_cols), chunk_cols))
            att.trade(piece, chunk)
            return carry

        lax.fori_loop(0, chunk_count, one_chunk, 0)

    def second_norm(piece):
        here, there = rows_of(piece), own_rows(piece)
        att.arrive(piece)

        def norm(row):
            x1 = R.x0[here(row), :] + att.total(piece, pl.ds(row, some_rows))
            R.out[here(row), :] = x1
            normed, _ = norm_rows(x1)
            R.c[there(row), :] = (normed * R.gains[3:4, :] + R.gains[4:5, :]).astype(LOW)

        by_rows(norm, cg[piece].start)

    def first_wb():
        wb.relay(1)
        wd.start_near()
        wc.start_near()
        wc.start_far()

    def middle_wb():
        wb.relay(2)
        wd.start_far()

    def last_wb():
        wd.start_other()
        for step in range(3, dp.far):
            wb.relay(step)

    turns(
        attend,
        [
            *later_pieces(ag, "mid"),
            *[
                (piece + 1, "mid", functools.partial(att.hand_on_all, piece))
                for piece in range(seqs - 1)
            ],
            (0, "mid", first_wb),
            (0, "late", middle_wb),
            (1, "mid", last_wb),
            *[
                (piece + 1, "late", functools.partial(second_norm, piece))
                for piece in range(seqs - 1)
            ],
        ],
    )
    att.hand_on_all(seqs - 1)
    wc.relay(1)
    for gather in (*wa, *ag, dxg, win):
        gather.drain()
    for step in range(1, size):
        ask(step).wait_send()
    second_norm(seqs - 1)
    cg[0].relays()
    wc.relay(2)
    wb.close()
    cg[0].close()
    for piece in range(seqs):
        att.drain(piece)

    def activate(piece, base, here, at):
        at("start")

        def some(cols):
            R.h[...] = dot(R.c[here, :], R.wbf[:, cols])

            def gelu(row):
                there = pl.ds(pl.multiple_of(base + row, 64), 64)
                h = R.h[pl.ds(row, 64), :]
                bell = jnp.exp(-0.5 * h * h)
                tail = normal_tail(jnp.abs(h), bell)
                gate = jnp.where(h >= 0.0, 1.0 - tail, tail)
                slope = gate + h * (bell * 0.3989422804014327)
                R.hb[there, cols] = (h * gate).astype(LOW)
                R.slope[there, cols] = slope.astype(LOW)

            strips(many, 64, gelu, 2)

        chunks(hidden, some)
        at("end")

    def last_wc():
        for step in range(3, dp.far):
            wc.relay(step)

    turns(activate, [*later_pieces(cg, "end"), (0, "end", last_wc), (seqs - 1, "start", wd.forward)])

    due = [(scatter, step) for scatter in (down, up) for step in range(1, dp.far)]

    def pass_due(number):
        for _ in range(min(number, len(due))):
            scatter, step = due.pop(0)
            scatter.pass_on(step)

    block = 2 * strip if (2 * strip) % 128 == 0 else min(256, model)

    def grads(make, trades):
        if block == 2 * strip:

            def turn_of(turn, carry):
                hi = up.turn_of(turn)
                make(pl.ds(pl.multiple_of(hi * block, block), block))
                for scatter in trades:
                    scatter.trade(hi)
                return carry

            lax.fori_loop(0, dp.far, turn_of, 0)
        else:
            strips(model, block, lambda col: make(pl.ds(col, block)))
            for scatter in trades:
                scatter.trade_all()

    def down_grads(cols):
        every = R.dx[:, :, cols]
        R.gdn[cols, :] = dot_tn(every.reshape(seqs * many, block), R.hb[...]).astype(LOW)

    def up_grads(cols):
        R.wbf[cols, :] = dot_tn(R.c[:, cols], R.dhb[...]).astype(LOW)

    dxg.close()
    grads(down_grads, (down,))
    wc.close()
    wd.close()
    for gather in (wb, *cg):
        gather.drain()

    def feed_back(piece, base, here, at):
        at("start")

        def some(cols):
            bent = dot(R.dx[piece], R.wcf[:, cols]) * R.slope[here, cols].astype(F32)
            R.dhb[here, cols] = bent.astype(LOW)

        chunks(hidden, some)
        at("mid")

        def project(cols):
            R.part[here, cols] = dot_nt(R.dhb[here, :], R.wbf[cols, :]).astype(LOW)

        dcs.products(piece, project)

    R.norms[...] = jnp.zeros_like(R.norms)

    def second_back(piece):
        here, there = rows_of(piece), own_rows(piece)
        dcs.arrive(piece)

        def back(row):
            dc = dcs.total(piece, pl.ds(row, some_rows))
            grad, unit = norm_back(R.out[here(row), :], R.gains[3:4, :], dc)
            grad = grad + R.cot[here(row), :].astype(F32) * scale_at(here(row))
            R.dmid[here(row), :] = grad
            R.dmid_all[there(row), :] = grad.astype(LOW)
            R.norms[2:3, :] += jnp.sum(dc * unit, 0, keepdims=True)
            R.norms[3:4, :] += jnp.sum(dc, 0, keepdims=True)

        by_rows(back, mg[piece].start)

    turns(
        feed_back,
        [
            *[
                (piece + 1, "mid", functools.partial(dcs.hand_on_last, piece))
                for piece in range(seqs - 1)
            ],
            (1, "mid", lambda: pass_due(1)),
        ],
    )
    dcs.hand_on_last(seqs - 1)
    second_back(0)
    pass_due(1)
    grads(up_grads, (up,))
    for piece in range(1, seqs):
        second_back(piece)
    pass_due(max(1, dp.far - 3))
    mg[0].relays()
    mg[0].close()
    for piece in range(seqs):
        dcs.drain(piece)

    def attend_back(piece, base, here, at):
        at("start")
        R.low[...] = dot(R.dmid_all[here, :], R.waf[:, 3 * heads_w :]).astype(LOW)
        at("mid")

        def one(rows_at):
            for seq, rows in enumerate(rows_at):
                queries = spread_heads(R.qkv[rows, :heads_w], masks)
                R.scores[seq] = dot_nt(queries, R.qkv[rows, heads_w : 2 * heads_w])
                upper_rows = pl.ds(pl.multiple_of(rows.start - base, seq_len), seq_len)
                R.upper[seq] = spread_heads(R.low[upper_rows, :], masks)
                R.dprobs[seq] = dot_nt(R.upper[seq], R.qkv[rows, 2 * heads_w : 3 * heads_w])
            for seq, rows in enumerate(rows_at):
                for row in range(0, all_rows, 64):
                    probs = softmax(seq, row)
                    grad_probs = R.dprobs[seq, row : row + 64, :]
                    inner = jnp.sum(probs * grad_probs, -1, keepdims=True)
                    R.probs[seq, row : row + 64, :] = probs.astype(LOW)
                    R.dscores[seq, row : row + 64, :] = (probs * (grad_probs - inner)).astype(LOW)
                keys = R.qkv[rows, heads_w : 2 * heads_w]
                queries = spread_heads(R.qkv[rows, :heads_w], masks)
                R.qkv[rows, 2 * heads_w : 3 * heads_w] = dot_tn(R.probs[seq], R.upper[seq]).astype(LOW)
                R.qkv[rows, heads_w : 2 * heads_w] = (dot_tn(R.dscores[seq], queries) * scale).astype(
                    LOW
                )
                R.qkv[rows, :heads_w] = (
                    join_heads(dot(R.dscores[seq], keys), masks, seq_len) * scale
                ).astype(LOW)

        pairs(base, one)
        at("late")

        def project(cols):
            R.part[here, cols] = dot_nt(R.qkv[here, :], R.waf[cols, : 3 * heads_w]).astype(LOW)

        das.products(piece, project)

    def first_back(piece):
        here = rows_of(piece)
        das.arrive(piece)

        def back(row):
            da = das.total(piece, pl.ds(row, some_rows))
            grad, unit = norm_back(R.x0[here(row), :], R.gains[1:2, :], da)
            R.dx0[here(row), :] = (R.dmid[here(row), :] + grad).astype(LOW)
            R.norms[0:1, :] += jnp.sum(da * unit, 0, keepdims=True)
            R.norms[1:2, :] += jnp.sum(da, 0, keepdims=True)

        by_rows(back)

    def out_grads():
        def make(cols):
            R.gwo[cols, :] = dot_tn(R.dmid_all[:, cols], R.o[...]).astype(LOW)

        grads(make, (wo,))

    turns(
        attend_back,
        [
            *later_pieces(mg, "mid"),
            (0, "late", lambda: pass_due(1)),
            *[
                (piece + 1, "mid", functools.partial(das.hand_on_last, piece))
                for piece in range(seqs - 1)
            ],
            (seqs - 1, "late", lambda: pass_due(1)),
        ],
    )
    das.hand_on_last(seqs - 1)
    def out_grads(cols):
        R.gwo[cols, :] = dot_tn(R.dmid_all[:, cols], R.o[...]).astype(LOW)

    def attend_grads(cols):
        R.waf[cols, : 3 * heads_w] = dot_tn(R.a[:, cols], R.qkv[...]).astype(LOW)

    first_back(0)
    pass_due(len(due))
    grads(attend_grads, (first_w,))
    grads(out_grads, ())
    wo.start()
    for piece in range(1, seqs):
        first_back(piece)

    grad_mixed = sum(
        dot_nt(R.dx0[:, index * quarter : (index + 1) * quarter], R.winf[index].astype(LOW))
        for index in range(ways)
    )
    sig = R.sig[...]
    grad_unit = grad_mixed * lax.rsqrt(1.0 + sig * sig)
    rows = R.rows[...].astype(F32)
    inverse = lax.rsqrt(jnp.mean(rows * rows, -1, keepdims=True) + EPS_NORM)
    unit = rows * inverse
    grad_rows = inverse * (grad_unit - unit * jnp.mean(grad_unit * unit, -1, keepdims=True))
    for step in range(1, size):
        give(step).wait_send()
    R.give[...] = dot_tn(R.pick[...], grad_rows.astype(LOW)).astype(LOW)
    mine_inc = block_rows(R.inc, spots)(mp.me)
    back, back_wait = far_copies(
        dp,
        lambda dest, source: (block_rows(R.give, cap)(dest), block_rows(mine_inc, cap)(source)),
        R.back_send,
        R.back_recv,
    )
    for step in range(1, size):
        back(step).start()
    mine_inc[mine, :] = R.give[mine, :]

    small_mp = Scatter(
        mp, of_index(R.gm), of_index(R.gm_first), of_index(R.gm_second), R.gm_send, R.gm_recv
    )
    for index in range(ways):
        cols = slice(index * quarter, (index + 1) * quarter)
        R.gm[index, :width, :] = dot_tn(R.mixed[...], R.dx0[:, cols]).astype(LOW)
        R.gm[index, width:, :] = jnp.concatenate(
            [R.norms[0:4, cols], jnp.zeros((12, quarter), F32)], 0
        ).astype(LOW)
    small_mp.trade_all()
    for step in range(1, far):
        small_mp.pass_on(step)

    first_w.pass_on(1)

    def feed_out(piece, base, here, at):
        def project(cols):
            R.c[here, cols] = dot_nt(R.hb[here, :], R.wcf[cols, :]).astype(LOW)

        out.products(piece, project)

    turns(feed_out)
    wo.trade()
    first_w.pass_on(2)
    for turn in range(min(2, shares_of)):
        for one in tile_of(turn):
            one.start()
    back_wait()
    rows_in = Gather(mp, block_rows(R.inc, spots), R.in_send, R.in_recv)
    rows_in.start()
    for piece in range(seqs):
        out.hand_on_last(piece)

    small_mp.arrive()
    summed = small_mp.total(slice(None))
    for index in range(size):
        piece = summed[index * rin : (index + 1) * rin, :]
        if rin_up > rin:
            piece = jnp.concatenate([piece, jnp.zeros((rin_up - rin, quarter), F32)], 0)
        R.gw[index, :rin_up, :] = piece.astype(LOW)
        R.gw[index, rin_up:, :] = summed[width:, :].astype(LOW)
    R.gw_in[dp.me] = R.gw[dp.me]
    small, small_wait = far_copies(
        dp, lambda dest, source: (R.gw.at[dest], R.gw_in.at[source]), R.gw_send, R.gw_recv
    )
    for step in range(1, size):
        small(step).start()
    rows_in.relays()
    for step in range(3, dp.far):
        first_w.pass_on(step)

    def finish_out(piece):
        here = rows_of(piece)
        out.arrive(piece)

        def finish(row):
            R.out[here(row), :] = (
                R.out[here(row), :] + out.total(piece, pl.ds(row, some_rows))
            ) * scale_at(here(row))

        by_rows(finish)

    for piece in range(seqs):
        finish_out(piece)
    store("out").start()

    rows_in.close()
    store("inc").start()

    once = jnp.where(mp.me == 0, 1.0, 0.0)
    lanes = lax.broadcasted_iota(jnp.int32, (1, 128), 1)
    R.sums[...] = jnp.zeros_like(R.sums)

    def put(place, squares, factor=None):
        for row, values in enumerate(squares):
            total = jnp.sum(jnp.sum(values, 0, keepdims=True), 1, keepdims=True)
            if factor is not None:
                total = total * factor
            R.sums[row : row + 1, :] += jnp.where(lanes == place, total, 0.0)

    def squares_of(weight, gradient, first, second):
        direction = direction_of(weight, gradient, first, second)[2]
        return weight * weight, direction * direction

    def folded(values):
        rows, columns = values.shape
        return jnp.sum(values.reshape(rows // 8, 8, columns), 0)

    def add_up(weight, gradient, first, second):
        squares = squares_of(weight[...], gradient[...], first[...], second[...])
        return [folded(values) for values in squares]

    zero = jnp.zeros((8, width), F32)

    def add_tile(turn, carry):
        side = lax.rem(turn, 2)
        for one in tile_of(turn):
            one.wait()
        hit = (
            lax.broadcasted_iota(jnp.int32, (tile_rows, ways * spots), 0)
            + share_tile(turn) * tile_rows
            == R.named[0:1, :]
        )
        gradient = dot(jnp.where(hit, 1.0, 0.0).astype(LOW), R.inc[...])
        more = add_up(R.tw.at[side], gradient, R.tm.at[side], R.tv.at[side])
        counts = jnp.where(turn * ways + mp.me < tiles, 1.0, 0.0)

        @pl.when(turn + 2 < shares_of)
        def _():
            for one in tile_of(turn + 2):
                one.start()

        return carry[0] + counts * more[0], carry[1] + counts * more[1]

    put(0, lax.fori_loop(0, shares_of, add_tile, (zero, zero)))

    for thing in (win_all, wc, wd, *mg, up, down, small_mp):
        thing.drain()
    for piece in range(seqs):
        out.drain(piece)
        das.drain(piece)
    for step in range(1, size):
        back(step).wait_send()

    for name in names_of_moments:
        moment(name).wait()
    up.arrive()

    R.red_up[...] = up.total(slice(None))
    store("red_up").start()
    put(10, add_up(R.w_up, R.red_up, R.up_m_here, R.up_v_here))
    down.arrive()

    R.red_dn[...] = down.total(slice(None)).T
    store("red_dn").start()
    put(11, add_up(R.w_down, R.red_dn, R.down_m_here, R.down_v_here))
    wo.arrive()
    R.red_out[...] = wo.total().T
    put(9, add_up(R.w_out, R.red_out, R.out_m_here, R.out_v_here))

    small_wait()
    R.wsum[mp.me] = jnp.sum(R.gw_in[...].astype(F32), 0).astype(LOW)
    weights_in = Gather(mp, of_index(R.wsum), R.ws_send, R.ws_recv)
    weights_in.start()
    first_w.arrive()

    value = first_w.total(slice(None))
    for part in range(3):
        R.red_qkv[part] = value[:, part * heads_w : (part + 1) * heads_w]
    store("red_qkv").start()
    weights_in.relays()
    for part in range(3):
        put(
            6 + part,
            add_up(
                R.w_qkv.at[part], R.red_qkv.at[part], R.qkv_m_here.at[part], R.qkv_v_here.at[part]
            ),
        )
    weights_in.close()
    total = jnp.concatenate([R.wsum[index].astype(F32) for index in range(ways)], 1)
    R.red_in[...] = total[:rin, :]
    put(1, add_up(R.w_in, R.red_in, R.w_in_m_here, R.w_in_v_here), once)
    if strip % 128 == 0:
        R.lnsum[...] = total[rin_up : rin_up + 8, :]
        R.red_ln[...] = R.lnsum[0:4, pl.ds(pl.multiple_of(dp.me * strip, strip), strip)]
    else:
        chosen = lax.broadcasted_iota(jnp.int32, (model, strip), 0) == dp.me * strip + (
            lax.broadcasted_iota(jnp.int32, (model, strip), 1)
        )
        R.red_ln[...] = dot(
            total[rin_up : rin_up + 8, :].astype(LOW), jnp.where(chosen, 1.0, 0.0).astype(LOW)
        )[0:4]
    squares = squares_of(R.ln_params[...], R.red_ln[...], R.ln_m_here[...], R.ln_v_here[...])
    for row in range(4):
        put(2 + row, [values[row : row + 1, :] for values in squares], once)

    R.near[dp.me] = R.sums[...]
    near, near_wait = far_copies(
        dp, lambda dest, source: (R.near.at[dp.me], R.near.at[source]), R.near_send, R.near_recv
    )
    for step in range(1, size):
        near(step).start()
    near_wait()
    R.wide[mp.me] = jnp.sum(R.near[...], 0)
    far_off, far_off_wait = far_copies(
        mp, lambda dest, source: (R.wide.at[mp.me], R.wide.at[source]), R.wide_send, R.wide_recv
    )
    for step in range(1, ways):
        far_off(step).start()
    far_off_wait()
    R.totals[...] = jnp.sum(R.wide[...], 0)

    for thing in (wo, first_w, rows_in, weights_in):
        thing.drain()
    for step in range(1, size):
        near(step).wait_send()
        small(step).wait_send()
    for step in range(1, ways):
        far_off(step).wait_send()
    for name in ("out", "red_up", "red_dn", "red_qkv", "inc"):
        store(name).wait()


def run_layer(cap, ids, levels, noise, cot, weights, moments):
    table, w_in, ln_params, w_qkv, w_out, w_up, w_down = weights
    dp, mp = lax.axis_size("dp"), lax.axis_size("mp")
    seqs, seq_len = ids.shape
    tokens, width = noise.shape
    model = cot.shape[1]
    rin = w_in.shape[0]
    heads_w = w_qkv.shape[2]
    strip, hidden = w_up.shape
    group = tokens * mp
    spots = dp * cap
    wide = round_up(rin, 16) + 16
    far, far_dp = mp // 2, dp // 2
    quarter = model // mp
    in_kind = LOW if rin % 16 == 0 else F32
    tile_rows = max(rows for rows in range(8, 257, 8) if table.shape[0] % rows == 0)
    stacked = (heads_w // HD) * seq_len
    vmem = pl.BlockSpec(memory_space=pltpu.VMEM)
    outside = pl.BlockSpec(memory_space=pl.ANY)
    inputs = dict(
        ids=(ids, vmem),
        levels=(levels, pl.BlockSpec(memory_space=pltpu.SMEM)),
        noise=(noise, vmem),
        cot=(cot, vmem),
        table=(table, outside),
        w_in=(w_in, vmem),
        ln_params=(ln_params, vmem),
        w_qkv=(w_qkv, vmem),
        w_out=(w_out, vmem),
        w_up=(w_up, vmem),
        w_down=(w_down, vmem),
    )
    kept = {}
    for name, (first, second) in zip(("table", "w_in", "ln", "qkv", "out", "up", "down"), moments):
        inputs[name + "_m"] = (first, outside)
        inputs[name + "_v"] = (second, outside)
        if name != "table":
            kept[name + "_m_here"] = kept[name + "_v_here"] = (first.shape, F32)
    own_stores = dict(
        out=((tokens, model), F32),
        red_up=((strip, hidden), F32),
        red_dn=((hidden, strip), F32),
        red_qkv=((3, strip, heads_w), F32),
        inc=((mp * spots, width), LOW),
    )
    outputs = dict(
        **{name + "_hbm": shape for name, shape in own_stores.items()},
        red_out=((heads_w, strip), F32),
        red_in=((rin, model), F32),
        red_ln=((4, strip), F32),
        named=((8, mp * spots), jnp.int32),
        totals=((8, 128), F32),
    )
    buffers = dict(
        tab=((2, round_up(table.shape[0] // 8, 128), width), F32),
        ask=((dp, 8, 128), F32),
        idx=((mp, dp, 8, 128), F32),
        loc=((spots, 128), jnp.int32),
        give=((spots, width), LOW),
        got=((spots, width), LOW),
        tw=((2, tile_rows, width), F32),
        tm=((2, tile_rows, width), F32),
        tv=((2, tile_rows, width), F32),
        sums=((8, 128), F32),
        near=((dp, 8, 128), F32),
        wide=((mp, 8, 128), F32),
        scores=((2, stacked, seq_len), F32),
        dprobs=((2, stacked, seq_len), F32),
        probs=((2, stacked, seq_len), LOW),
        dscores=((2, stacked, seq_len), LOW),
        upper=((2, stacked, heads_w), LOW),
        gwo=((model, heads_w), LOW),
        wo_first=((strip, heads_w), LOW),
        wo_second=((dp * strip, heads_w), LOW),
        gains=((8, model), F32),
        lnsum=((8, model), F32),
        sig=((tokens, 1), F32),
        pick=((tokens, spots), LOW),
        rows=((tokens, width), LOW),
        mixed=((tokens, width), LOW),
        x0=((tokens, model), F32),
        a=((group, model), LOW),
        c=((group, model), LOW),
        dx=((seqs, group // seqs, model), LOW),
        dmid=((tokens, model), F32),
        dmid_all=((group, model), LOW),
        winf=((mp, rin * dp, quarter), in_kind),
        waf=((model, 4 * heads_w), LOW),
        wbf=((model, hidden), LOW),
        wcf=((model, hidden), LOW),
        qkv=((group, 3 * heads_w), LOW),
        o=((group, heads_w), LOW),
        low=((group // seqs, heads_w), LOW),
        part=((group, model), LOW),
        first=((far * tokens, model), LOW),
        fold=((far * tokens, model), LOW),
        second=((far * tokens, model), LOW),
        fold_far=((far * tokens, model), LOW),
        h=((group // seqs, min(256, hidden)), F32),
        hb=((group, hidden), LOW),
        dhb=((group, hidden), LOW),
        slope=((group, hidden), LOW),
        gdn=((model, hidden), LOW),
        dx0=((tokens, model), LOW),
        norms=((8, model), F32),
        gm=((mp, width + 16, quarter), LOW),
        gm_first=((far, width + 16, quarter), LOW),
        gm_second=((far, width + 16, quarter), LOW),
        gw=((dp, wide, quarter), LOW),
        gw_in=((dp, wide, quarter), LOW),
        up_first=((far_dp * strip, hidden), LOW),
        up_second=((far_dp * strip, hidden), LOW),
        dn_first=((far_dp * strip, hidden), LOW),
        dn_second=((far_dp * strip, hidden), LOW),
        wa_first=((far_dp * strip, 3 * heads_w), LOW),
        wa_second=((far_dp * strip, 3 * heads_w), LOW),
        wsum=((mp, wide, quarter), LOW),
        up_extra=((strip, hidden), LOW),
        dn_extra=((strip, hidden), LOW),
        wa_extra=((strip, 3 * heads_w), LOW),
        **kept,
        **own_stores,
    )
    sems = dict(store_sem=5, tab_sem=2, tile_sem=6, moment_sem=12)
    for name in (
        *("win", "wa", "wx", "wb", "wc", "wd", "ask", "give", "back"),
        *("up", "dn", "ga", "wo", "gw", "near"),
    ):
        sems[name + "_send"] = sems[name + "_recv"] = dp + 1
    for name in ("wim", "id", "in", "ws", "gm", "wide"):
        sems[name + "_send"] = sems[name + "_recv"] = mp
    for name in ("dx", "a", "c", "e"):
        sems[name + "_send"] = sems[name + "_recv"] = 2 * seqs * mp
    for name in ("as", "os", "cs", "ds"):
        sems[name + "_send"] = sems[name + "_recv"] = seqs * mp * (model // min(256, model))
    names = [*inputs, *outputs, *buffers, *sems]
    made = pl.pallas_call(
        functools.partial(layer_kernel, cap, names),
        out_shape=[jax.ShapeDtypeStruct(shape, kind) for shape, kind in outputs.values()],
        in_specs=[spec for _, spec in inputs.values()],
        out_specs=[outside if name.endswith("_hbm") else vmem for name in outputs],
        scratch_shapes=[
            *[pltpu.VMEM(shape, kind) for shape, kind in buffers.values()],
            *[pltpu.SemaphoreType.DMA((number,)) for number in sems.values()],
        ],
        compiler_params=pltpu.CompilerParams(
            vmem_limit_bytes=VMEM_BYTES, collective_id=1, has_side_effects=True
        ),
        name="layer",
    )(*[value for value, _ in inputs.values()])
    return {name.removesuffix("_hbm"): value for name, value in zip(outputs, made)}


def direction_of(weight, gradient, first, second):
    first_new = BETA_ONE * first + (1.0 - BETA_ONE) * gradient
    second_new = BETA_TWO * second + (1.0 - BETA_TWO) * gradient * gradient
    second_hat = second_new * (1.0 / (1.0 - BETA_TWO**STEP))
    inverse = lax.rsqrt(second_hat)
    root = second_hat * inverse + EPS_ADAM
    inverse = inverse * (2.0 - root * inverse)
    inverse = inverse * (2.0 - root * inverse)
    direction = first_new * (1.0 / (1.0 - BETA_ONE**STEP)) * inverse + DECAY * weight
    return first_new, second_new, direction


def update_kernel(part, names, *refs):
    R = types.SimpleNamespace(**dict(zip(names, refs)))
    turn = pl.program_id(0)
    R.out_rows[...] = R.made[...]
    norms = jnp.sqrt(R.totals[...])
    R.norms[...] = norms[0:2, 0:12]
    factors = norms[0:1, :] / (norms[1:2, :] + EPS_ADAM) * RATE

    def piece(name, here, gradient, place, rows=slice(None)):
        weight = getattr(R, name)[here]
        first_new, second_new, direction = direction_of(
            weight, gradient, getattr(R, name + "_m")[here], getattr(R, name + "_v")[here]
        )
        if isinstance(place, int):
            factor = factors[0:1, place : place + 1]
        else:
            factor = jnp.concatenate([factors[0:1, one : one + 1] for one in place], 0)
        getattr(R, name + "_m_new")[here] = first_new
        getattr(R, name + "_v_new")[here] = second_new
        getattr(R, name + "_new")[here] = weight - factor * direction

    def update(name, gradient, place, lead=(), here=slice(None)):
        piece(name, (*lead, here, slice(None)), gradient, place)

    tile = R.table.shape[0]
    spots = R.named.shape[1]

    def table_part(row):
        hit = (
            lax.broadcasted_iota(jnp.int32, (part, spots), 0) + (turn * tile + row)
            == R.named[0:1, :]
        )
        gradient = dot(jnp.where(hit, 1.0, 0.0).astype(LOW), R.inc[...])
        update("table", gradient, 0, (), pl.ds(row, part))

    strips(tile, part, table_part)
    for group in range(3):
        update("qkv", R.red_qkv[group], 6 + group, (group,))
    update("up", R.red_up[...], 10)
    update("down", R.red_dn[...], 11)

    @pl.when(turn == 0)
    def _():
        update("out", R.red_out[...], 9)
        update("w_in", R.red_in[...], 1)
        piece("ln", (slice(None), slice(None)), R.red_ln[...], (2, 3, 4, 5))


def turns_of(rows, parts):
    return [
        turns
        for turns in (5, 4, 2, 1)
        if rows % (8 * turns) == 0 and all(size % (8 * turns) == 0 for size in parts)
    ][0]


def run_update(weights, moments, grads):
    names = ("table", "w_in", "ln", "qkv", "out", "up", "down")
    by_name = dict(zip(names, weights))
    rows, width = by_name["table"].shape
    strip, hidden = by_name["up"].shape
    heads_w = by_name["qkv"].shape[2]
    turns = turns_of(rows, (strip, hidden))
    tile = rows // turns
    part = max(size for size in range(8, 257, 8) if tile % size == 0)
    fixed = lambda array: pl.BlockSpec(array.shape, lambda turn: (0,) * array.ndim)
    specs = dict(
        table=pl.BlockSpec((tile, width), lambda turn: (turn, 0)),
        w_in=fixed(by_name["w_in"]),
        ln=fixed(by_name["ln"]),
        qkv=pl.BlockSpec((3, strip // turns, heads_w), lambda turn: (0, turn, 0)),
        out=fixed(by_name["out"]),
        up=pl.BlockSpec((strip // turns, hidden), lambda turn: (turn, 0)),
        down=pl.BlockSpec((hidden // turns, strip), lambda turn: (turn, 0)),
    )
    inputs = {}
    for name, weight, (first, second) in zip(names, weights, moments):
        inputs[name] = (weight, specs[name])
        inputs[name + "_m"] = (first, specs[name])
        inputs[name + "_v"] = (second, specs[name])
    for name, like in (
        ("red_up", "up"),
        ("red_dn", "down"),
        ("red_qkv", "qkv"),
        ("red_out", "out"),
        ("red_in", "w_in"),
        ("red_ln", "ln"),
    ):
        inputs[name] = (grads[name], specs[like])
    for name in ("inc", "named", "totals"):
        inputs[name] = (grads[name], fixed(grads[name]))
    tokens, model = grads["out"].shape
    rows_spec = pl.BlockSpec((tokens // turns, model), lambda turn: (turn, 0))
    inputs["made"] = (grads["out"], rows_spec)
    outputs = {"out_rows": (grads["out"].shape, rows_spec)}
    for name, weight in by_name.items():
        for kind in ("_new", "_m_new", "_v_new"):
            outputs[name + kind] = (weight.shape, specs[name])
    outputs["norms"] = ((2, 12), pl.BlockSpec((2, 12), lambda turn: (0, 0)))
    results = pl.pallas_call(
        functools.partial(update_kernel, part, [*inputs, *outputs]),
        grid=(turns,),
        out_shape=[jax.ShapeDtypeStruct(shape, F32) for shape, _ in outputs.values()],
        in_specs=[spec for _, spec in inputs.values()],
        out_specs=[spec for _, spec in outputs.values()],
        compiler_params=pltpu.CompilerParams(vmem_limit_bytes=VMEM_BYTES),
        name="update",
    )(*[value for value, _ in inputs.values()])
    return list(results)


def per_device(
    token_ids,
    levels,
    noise,
    cotangent,
    table,
    table_m,
    table_v,
    w_in,
    w_in_m,
    w_in_v,
    ln_params,
    ln_m,
    ln_v,
    w_qkv,
    qkv_m,
    qkv_v,
    w_out,
    out_m,
    out_v,
    w_up,
    up_m,
    up_v,
    w_down,
    down_m,
    down_v,
):
    dp_count = lax.axis_size("dp")
    seq_count, seq_len = token_ids.shape
    tokens = seq_count * seq_len
    model = cotangent.shape[2]
    cap = round_up(max(2, (3 * tokens + 2 * dp_count - 1) // (2 * dp_count)), 16)
    weights = (table, w_in, ln_params, w_qkv, w_out, w_up, w_down)
    moments = (
        (table_m, table_v),
        (w_in_m, w_in_v),
        (ln_m, ln_v),
        (qkv_m, qkv_v),
        (out_m, out_v),
        (up_m, up_v),
        (down_m, down_v),
    )
    grads = run_layer(
        cap,
        token_ids,
        levels,
        noise.reshape(tokens, -1),
        cotangent.reshape(tokens, model),
        weights,
        moments,
    )
    out, *results = run_update(weights, moments, grads)
    return (out.reshape(seq_count, seq_len, model), *results)


def solution(mesh):
    return jax.shard_map(
        per_device,
        mesh=mesh,
        in_specs=(
            P(("dp", "mp"), None),
            P(("dp", "mp")),
            P(("dp", "mp"), None, None),
            P(("dp", "mp"), None, None),
            P("dp", None),
            P("dp", None),
            P("dp", None),
            P("dp", None),
            P("dp", None),
            P("dp", None),
            P(None, "dp"),
            P(None, "dp"),
            P(None, "dp"),
            P(None, "dp", "mp"),
            P(None, "dp", "mp"),
            P(None, "dp", "mp"),
            P("mp", "dp"),
            P("mp", "dp"),
            P("mp", "dp"),
            P("dp", "mp"),
            P("dp", "mp"),
            P("dp", "mp"),
            P("mp", "dp"),
            P("mp", "dp"),
            P("mp", "dp"),
        ),
        out_specs=(
            P(("dp", "mp"), None, None),
            P("dp", None),
            P("dp", None),
            P("dp", None),
            P("dp", None),
            P("dp", None),
            P("dp", None),
            P(None, "dp"),
            P(None, "dp"),
            P(None, "dp"),
            P(None, "dp", "mp"),
            P(None, "dp", "mp"),
            P(None, "dp", "mp"),
            P("mp", "dp"),
            P("mp", "dp"),
            P("mp", "dp"),
            P("dp", "mp"),
            P("dp", "mp"),
            P("dp", "mp"),
            P("mp", "dp"),
            P("mp", "dp"),
            P("mp", "dp"),
            P(),
        ),
        check_vma=False,
    )
```

```python
import functools
import types

import jax
import jax.numpy as jnp
from jax import lax
from jax.experimental import pallas as pl
from jax.experimental.pallas import tpu as pltpu
from jax.sharding import PartitionSpec as P

HD = 64
LEVELS = 64
STEP = 10


EPS_NORM = 1e-06
EPS_LAYER = 1e-05
EPS_ADAM = 1e-06
BETA_ONE = 0.9
BETA_TWO = 0.999
DECAY = 0.01
RATE = 0.5
SIGMA_TOP = 10.0

F32 = jnp.float32
LOW = jnp.bfloat16
VMEM_BYTES = 63 * 1024 * 1024


def sigma_of(levels):
    frac = levels.astype(jnp.float32) / (LEVELS - 1)
    return jnp.exp(frac * jnp.log(SIGMA_TOP))


def lamb_moments(weight, gradient, first, second):
    first_new = BETA_ONE * first + (1.0 - BETA_ONE) * gradient
    second_new = BETA_TWO * second + (1.0 - BETA_TWO) * gradient * gradient
    first_hat = first_new / (1.0 - BETA_ONE**STEP)
    second_hat = second_new / (1.0 - BETA_TWO**STEP)
    direction = first_hat / (jnp.sqrt(second_hat) + EPS_ADAM) + DECAY * weight
    return (first_new, second_new, direction)


def trust_factors(ratio):
    return (
        ratio[0],
        ratio[1],
        ratio[2:6][:, None],
        ratio[6:9][:, None, None],
        ratio[9],
        ratio[10],
        ratio[11],
    )


def round_up(value, step):
    return -(-value // step) * step


def dot(left, right):
    return jnp.dot(left, right, preferred_element_type=F32)


def dot_nt(left, right):
    return lax.dot_general(left, right, (((1,), (1,)), ((), ())), preferred_element_type=F32)


def dot_tn(left, right):
    return lax.dot_general(left, right, (((0,), (0,)), ((), ())), preferred_element_type=F32)


def strips(total, step, body, unroll=1):
    step = min(step, total)

    def one(turn, carry):
        body(pl.multiple_of(turn * step, step))
        return carry

    lax.fori_loop(0, total // step, one, 0, unroll=unroll)


class Line:
    def __init__(self, axis):
        self.axis = axis
        self.size = lax.axis_size(axis)
        self.far = self.size // 2
        self.me = lax.axis_index(axis)
        self.hi = lax.div(self.me, 2)
        self.lo = lax.rem(self.me, 2)
        self.partner = self.hi * 2 + (1 - self.lo)

    def at(self, step):
        return lax.rem(self.hi + step + self.far, self.far)

    def push(self, index, src, dst, send, recv):
        return pltpu.make_async_remote_copy(
            src_ref=src,
            dst_ref=dst,
            send_sem=send,
            recv_sem=recv,
            device_id={self.axis: index},
            device_id_type=pl.DeviceIdType.MESH,
        )

    def signal(self, sem, index):
        pl.semaphore_signal(
            sem, inc=1, device_id={self.axis: index}, device_id_type=pl.DeviceIdType.MESH
        )


def meet(pair_lines, all_lines=()):
    sem = pltpu.get_barrier_semaphore()
    count = 0
    for line in pair_lines:
        for step in range(1, line.far):
            line.signal(sem, line.at(step) * 2 + line.lo)
            count += 1
        line.signal(sem, line.partner)
        count += 1
    for line in all_lines:
        for step in range(1, line.size):
            line.signal(sem, lax.rem(line.me + step, line.size))
            count += 1
    pl.semaphore_wait(sem, count)


class Gather:
    def __init__(self, line, at, send, recv, base=0, ends=False):
        self.line, self.at, self.send, self.recv, self.base = line, at, send, recv, base
        self.ends = ends and line.far == 4

    def source(self, step):
        line = self.line
        if not self.ends:
            return line.at(-step)
        order = ((1, 2, 3), (0, 3, 2), (3, 0, 1), (2, 1, 0))
        hi = order[3][step - 1]
        for place in (2, 1, 0):
            hi = jnp.where(line.hi == place, order[place][step - 1], hi)
        return hi

    def far_sends(self, act):
        line = self.line
        for step in range(1, line.far):
            one = self.copy(line.me, step - 1, line.at(step) * 2 + line.lo)
            if self.ends and step != 2:
                pl.when(line.hi != (3 if step == 1 else 0))(functools.partial(act, one))
            else:
                act(one)

    def to_end(self, act):
        line = self.line
        dest = jnp.where(line.hi == 1, 0, 3)
        one = self.copy((3 - dest) * 2 + line.lo, 2 * line.far - 1, dest * 2 + line.lo)
        pl.when((line.hi == 1) | (line.hi == 2))(functools.partial(act, one))

    def copy(self, index, slot, dest):
        block = self.at(index)
        return self.line.push(
            dest, block, block, self.send.at[self.base + slot], self.recv.at[self.base + index]
        )

    def start_far(self):
        self.far_sends(lambda one: one.start())

    def start_near(self):
        self.copy(self.line.me, self.line.far - 1, self.line.partner).start()

    def start(self):
        self.start_far()
        self.start_near()

    def relay(self, step):
        line = self.line
        handed = self.copy(self.source(step) * 2 + line.lo, line.far - 1 + step, line.partner)
        handed.wait_recv()
        if self.ends and step == 2:
            self.to_end(lambda one: one.start())
        handed.start()

    def relays(self):
        for step in range(1, self.line.far):
            self.relay(step)

    def close(self):
        line = self.line
        for step in range(line.far):
            self.copy(line.at(-step) * 2 + (1 - line.lo), 0, line.partner).wait_recv()

    def drain(self):
        self.far_sends(lambda one: one.wait_send())
        if self.ends:
            self.to_end(lambda one: one.wait_send())
        for slot in range(self.line.far - 1, 2 * self.line.far - 1):
            self.copy(self.line.me, slot, self.line.partner).wait_send()


class SideGather(Gather):
    def other(self, act):
        line = self.line
        for step in range(1, line.far):
            one = self.copy(line.partner, line.far - 1 + step, line.at(step) * 2 + line.lo)
            if self.ends and step != 2:
                pl.when(line.hi != (3 if step == 1 else 0))(functools.partial(act, one))
            else:
                act(one)

    def to_ends(self, parity, slot, act):
        line = self.line
        dest = jnp.where(line.hi == 1, 0, 3)
        one = self.copy((3 - dest) * 2 + parity, slot, dest * 2 + line.lo)
        pl.when((line.hi == 1) | (line.hi == 2))(functools.partial(act, one))

    def start_other(self):
        self.copy(self.line.partner, 0, self.line.partner).wait_recv()
        self.other(lambda one: one.start())

    def taken(self, step):
        line = self.line
        for parity, slot in ((line.lo, 2 * line.far - 1), (1 - line.lo, 2 * line.far)):
            self.copy(self.source(step) * 2 + parity, 0, line.partner).wait_recv()
            if self.ends and step == 2:
                self.to_ends(parity, slot, lambda one: one.start())

    def forward(self):
        if self.line.far > 2:
            self.taken(2)

    def close(self):
        for step in range(1, self.line.far):
            if step != 2:
                self.taken(step)

    def drain(self):
        line = self.line
        self.far_sends(lambda one: one.wait_send())
        self.copy(line.me, line.far - 1, line.partner).wait_send()
        self.other(lambda one: one.wait_send())
        if self.ends:
            for parity, slot in ((line.lo, 2 * line.far - 1), (1 - line.lo, 2 * line.far)):
                self.to_ends(parity, slot, lambda one: one.wait_send())


class SideScatter:
    def __init__(self, line, part, second, first, send, recv):
        self.line, self.part, self.second, self.first = line, part, second, first
        self.send, self.recv = send, recv

    def far_copy(self, step, parity):
        line = self.line
        hi = line.at(step)
        return line.push(
            hi * 2 + line.lo,
            self.part(hi * 2 + parity),
            self.second(parity * line.far + line.hi),
            self.send.at[2 * (step - 1) + parity],
            self.recv.at[parity * line.far + line.hi],
        )

    def near_copy(self):
        line = self.line
        return line.push(
            line.partner,
            self.part(line.partner),
            self.first,
            self.send.at[2 * line.far - 2],
            self.recv.at[2 * line.far],
        )

    def start(self):
        for step in range(1, self.line.far):
            for parity in range(2):
                self.far_copy(step, parity).start()

    def sum_of(self, parity):
        line = self.line
        value = self.part(line.hi * 2 + parity)[...].astype(F32)
        for step in range(1, line.far):
            index = parity * line.far + line.at(-step)
            block = self.second(index)
            line.push(
                line.partner, block, block, self.send.at[0], self.recv.at[index]
            ).wait_recv()
            value = value + block[...].astype(F32)
        return value

    def trade(self):
        given = self.part(self.line.partner)
        given[...] = self.sum_of(1 - self.line.lo).astype(LOW)
        self.near_copy().start()

    def arrive(self):
        pass

    def total(self):
        value = self.sum_of(self.line.lo)
        self.near_copy().wait_recv()
        return value + self.first[...].astype(F32)

    def drain(self):
        for step in range(1, self.line.far):
            for parity in range(2):
                self.far_copy(step, parity).wait_send()
        self.near_copy().wait_send()


class Scatter:
    def __init__(self, line, part, first, second, send, recv, base=0, extra=None):
        self.line, self.part, self.first, self.second = line, part, first, second
        self.send, self.recv, self.base = send, recv, base
        self.extra = extra if line.far == 4 else None

    def clear(self):
        line = self.line
        if self.extra is not None:

            @pl.when((line.hi == 0) | (line.hi == 3))
            def _():
                slot = self.second(3 - line.hi)
                slot[...] = jnp.zeros(slot.shape, LOW)

    def order(self, step):
        line = self.line
        if self.extra is None:
            return line.at(step)
        table = ((3, 2, 1), (2, 0, 3), (1, 3, 0), (0, 1, 2))
        hi = table[3][step - 1]
        for place in (2, 1, 0):
            hi = jnp.where(line.hi == place, table[place][step - 1], hi)
        return hi

    def traded(self, hi):
        line = self.line
        return line.push(
            line.partner,
            self.part(hi * 2 + (1 - line.lo)),
            self.first(hi),
            self.send.at[self.base + hi],
            self.recv.at[self.base + hi],
        )

    def passed(self, step):
        line = self.line
        hi = self.order(step)
        return line.push(
            hi * 2 + line.lo,
            self.part(hi * 2 + line.lo),
            self.second(line.hi),
            self.send.at[self.base + line.far + step - 1],
            self.recv.at[self.base + line.far + line.hi],
        )

    def to_next(self):
        line = self.line
        return line.push(
            jnp.where(line.hi < 2, 1, 2) * 2 + line.lo,
            self.part((3 - jnp.where(line.hi < 2, 0, 3)) * 2 + line.lo),
            self.extra,
            self.send.at[self.base + line.far],
            self.recv.at[self.base + 2 * line.far],
        )

    def turn_of(self, turn):
        line = self.line
        if self.extra is None:
            return lax.rem(line.hi + turn + 1, line.far)
        hi = line.hi
        for step in range(1, line.far):
            hi = jnp.where(turn == step - 1, self.order(step), hi)
        return hi

    def is_end(self):
        return (self.line.hi == 0) | (self.line.hi == 3)

    def trade(self, hi):
        self.traded(hi).start()

    def trade_all(self):
        for step in range(1, self.line.far + 1):
            self.trade(self.order(step) if step < self.line.far else self.line.hi)

    def pass_on(self, step):
        line = self.line
        hi = self.order(step)
        self.traded(hi).wait_recv()
        mine, other = self.part(hi * 2 + line.lo), self.first(hi)
        if self.extra is None or step == 2:
            mine[...] = (mine[...].astype(F32) + other[...].astype(F32)).astype(LOW)
            self.passed(step).start()
        elif step == 1:
            mine[...] = (mine[...].astype(F32) + other[...].astype(F32)).astype(LOW)

            @pl.when(self.is_end())
            def _():
                self.to_next().start()

            @pl.when(jnp.logical_not(self.is_end()))
            def _():
                self.passed(step).start()
        else:

            @pl.when(self.is_end())
            def _():
                mine[...] = (mine[...].astype(F32) + other[...].astype(F32)).astype(LOW)

            @pl.when(jnp.logical_not(self.is_end()))
            def _():
                line.push(
                    line.partner,
                    self.extra,
                    self.extra,
                    self.send.at[self.base],
                    self.recv.at[self.base + 2 * line.far],
                ).wait_recv()
                mine[...] = (
                    mine[...].astype(F32) + other[...].astype(F32) + self.extra[...].astype(F32)
                ).astype(LOW)

            self.passed(step).start()

    def arrive(self):
        line = self.line
        self.traded(line.hi).wait_recv()
        for step in range(1, line.far):
            hi = line.at(-step)
            one = line.push(
                line.partner,
                self.second(hi),
                self.second(hi),
                self.send.at[self.base],
                self.recv.at[self.base + line.far + hi],
            )
            if self.extra is None:
                one.wait_recv()
            else:
                pl.when(jnp.logical_not(self.is_end()) | (hi + line.hi != 3))(one.wait_recv)

    def total(self, here):
        line = self.line
        value = self.part(line.me)[here, :].astype(F32) + self.first(line.hi)[here, :].astype(F32)
        for step in range(1, line.far):
            value = value + self.second(line.at(-step))[here, :].astype(F32)
        return value

    def drain(self):
        line = self.line
        for step in range(line.far):
            self.traded(line.at(step)).wait_send()
        for step in range(1, line.far):
            if self.extra is not None and step == 1:
                pl.when(self.is_end())(lambda: self.to_next().wait_send())
                pl.when(jnp.logical_not(self.is_end()))(lambda: self.passed(1).wait_send())
            else:
                self.passed(step).wait_send()


def block_rows(ref, rows, first=0):
    return lambda index: ref.at[pl.ds(pl.multiple_of((index + first) * rows, rows), rows)]


def part_rows(ref, rows, first, count):
    return lambda index: ref.at[pl.ds(pl.multiple_of(index * rows + first, count), count)]


def of_index(ref):
    return lambda index: ref.at[index]


def norm_rows(values):
    center = values - jnp.mean(values, -1, keepdims=True)
    spread = jnp.mean(center * center, -1, keepdims=True)
    inverse = lax.rsqrt(spread + EPS_LAYER)
    return center * inverse, inverse


def norm_back(values, gain, grad):
    unit, inverse = norm_rows(values)
    inner = grad * gain
    shared = jnp.mean(inner, -1, keepdims=True)
    along = jnp.mean(inner * unit, -1, keepdims=True)
    return inverse * (inner - shared - unit * along), unit


def head_masks(width):
    lane = lax.broadcasted_iota(jnp.int32, (1, width), 1)
    return [
        jnp.where((lane >= head * HD) & (lane < (head + 1) * HD), 1.0, 0.0)
        for head in range(width // HD)
    ]


def spread_heads(values, masks):
    return jnp.concatenate([values * mask.astype(LOW) for mask in masks], 0)


def join_heads(values, masks, rows):
    total = values[0:rows] * masks[0]
    for head in range(1, len(masks)):
        total = total + values[head * rows : (head + 1) * rows] * masks[head]
    return total


TAIL = (
    0.2256758632450557,
    0.22566952478278277,
    0.2078438574180613,
    0.16853390514724884,
    0.14146086231844687,
    -0.005667717379728321,
    0.16915486959066833,
    -0.18294364197603524,
    0.05027260226320005,
)


def normal_tail(size, bell):
    base = 1.0 + (0.4 * 0.5**0.5) * size
    t = pl.reciprocal(base, approx=True)
    t = t * (2.0 - base * t)
    t = t * (2.0 - base * t)
    value = jnp.full_like(t, 0.5 * TAIL[-1])
    for factor in TAIL[-2::-1]:
        value = value * t + 0.5 * factor
    return value * t * bell


def far_copies(line, make, sends, recvs):
    def copy(step):
        dest = lax.rem(line.me + step, line.size)
        src, dst = make(dest, line.me)
        return line.push(dest, src, dst, sends.at[step], recvs.at[line.me])

    def wait():
        for step in range(1, line.size):
            source = lax.rem(line.me + line.size - step, line.size)
            _, dst = make(source, source)
            line.push(line.partner, dst, dst, sends.at[0], recvs.at[source]).wait_recv()

    return copy, wait


def layer_kernel(cap, names, *refs):
    R = types.SimpleNamespace(**dict(zip(names, refs)))
    dp, mp = Line("dp"), Line("mp")
    size, ways = dp.size, mp.size
    seqs, seq_len = R.ids.shape
    tokens, width = R.noise.shape
    model = R.cot.shape[1]
    heads_w = R.o.shape[1]
    hidden = R.wbf.shape[1]
    table_rows = R.table.shape[0]
    rin = R.w_in.shape[0]
    rin_up = round_up(rin, 16)
    quarter = model // ways
    strip = R.w_up.shape[0]
    spots = size * cap
    far = mp.far
    count = seqs * far
    half_strip = strip // 2
    own_strip = pl.ds(pl.multiple_of(dp.me * strip, strip), strip)
    mine = pl.ds(pl.multiple_of(dp.me * cap, cap), cap)

    some_rows = seq_len // 2

    def rows_of(piece):
        return lambda row: pl.ds(pl.multiple_of(piece * seq_len + row, some_rows), some_rows)

    def own_rows(piece):
        first = pl.multiple_of((piece * ways + mp.me) * seq_len, seq_len)
        return lambda row: pl.ds(pl.multiple_of(first + row, some_rows), some_rows)

    def by_rows(body, after=lambda half: None):
        for half in range(2):
            body(half * some_rows)
            after(half)

    class Rows:
        def __init__(self, ref, send, recv, piece):
            self.parts = [
                Gather(
                    mp,
                    lambda index, half=half: ref.at[
                        pl.ds(
                            pl.multiple_of(
                                (piece * ways + index) * seq_len + half * some_rows, some_rows
                            ),
                            some_rows,
                        )
                    ],
                    send,
                    recv,
                    (2 * piece + half) * ways,
                )
                for half in range(2)
            ]

        def start(self, half):
            self.parts[half].start()

        def relays(self):
            for part in self.parts:
                part.relays()

        def close(self):
            for part in self.parts:
                part.close()

        def drain(self):
            for part in self.parts:
                part.drain()

    def halves(ref, send, recv):
        return [Rows(ref, send, recv, piece) for piece in range(seqs)]

    chunk_cols = min(256, model)
    chunk_count = model // chunk_cols

    class Sums:
        def __init__(self, *refs):
            *self.refs, self.send, self.recv = refs

        def chunk(self, piece, chunk):
            cols = pl.ds(pl.multiple_of(chunk * chunk_cols, chunk_cols), chunk_cols)

            def blocks(ref, first):
                return lambda index: ref.at[
                    pl.ds(pl.multiple_of((index + first) * seq_len, seq_len), seq_len), cols
                ]

            firsts = (piece * ways, piece * far, piece * far)
            views = [blocks(ref, first) for ref, first in zip(self.refs, firsts)]
            return Scatter(mp, *views, self.send, self.recv, (piece * chunk_count + chunk) * ways)

        def total(self, piece, here):
            firsts = (piece * ways, piece * far, piece * far)
            views = [block_rows(ref, seq_len, first) for ref, first in zip(self.refs, firsts)]
            return Scatter(mp, *views, self.send, self.recv).total(here)

        def trade(self, piece, chunk):
            self.chunk(piece, chunk).trade_all()

        def hand_on(self, piece, chunk):
            scatter = self.chunk(piece, chunk)
            for step in range(1, far):
                scatter.pass_on(step)

        def every(self, act):
            def one(chunk, carry):
                act(chunk)
                return carry

            lax.fori_loop(0, chunk_count, one, 0)

        def hand_on_all(self, piece):
            self.every(lambda chunk: self.hand_on(piece, chunk))

        def arrive(self, piece):
            self.every(lambda chunk: self.chunk(piece, chunk).arrive())

        def drain(self, piece):
            self.every(lambda chunk: self.chunk(piece, chunk).drain())

        def products(self, piece, make):
            def one(chunk, carry):
                make(pl.ds(pl.multiple_of(chunk * chunk_cols, chunk_cols), chunk_cols))
                self.trade(piece, chunk)
                pl.when(chunk > 0)(lambda: self.hand_on(piece, chunk - 1))
                return carry

            lax.fori_loop(0, chunk_count, one, 0)

        def hand_on_last(self, piece):
            self.hand_on(piece, chunk_count - 1)

    many = ways * seq_len

    def turns(body, hooks=()):
        def one(piece, carry):
            def at(point):
                for place, when, action in hooks:
                    if when == point:
                        pl.when(piece == place)(action)

            base = pl.multiple_of(piece * many, many)
            body(piece, base, pl.ds(base, many), at)
            return carry

        lax.fori_loop(0, seqs, one, 0)

    def pairs(base, body):
        def one(pair, carry):
            first = pl.multiple_of(base + pair * (2 * seq_len), 2 * seq_len)
            body([pl.ds(pl.multiple_of(first + seq * seq_len, seq_len), seq_len) for seq in range(2)])
            return carry

        lax.fori_loop(0, far, one, 0)

    def chunks(total, body, before=lambda turn: None):
        step = min(256, total)

        def one(turn, carry):
            before(turn)
            body(pl.ds(pl.multiple_of(turn * step, step), step))
            return carry

        lax.fori_loop(0, total // step, one, 0)

    def later_pieces(gathers, point):
        hooks = []
        for piece in range(1, seqs):
            hooks.append((piece - 1, point, gathers[piece].relays))
            hooks.append((piece, "start", gathers[piece].close))
        return hooks

    chunk = R.tab.shape[1]
    pieces = -(-table_rows // chunk)

    def fetch(piece):
        rows = min(chunk, table_rows - piece * chunk)
        return pltpu.make_async_copy(
            R.table.at[pl.ds(piece * chunk, rows)],
            R.tab.at[piece % 2, pl.ds(0, rows)],
            R.tab_sem.at[piece % 2],
        )

    for piece in range(min(2, pieces)):
        fetch(piece).start()

    names_of_moments = [
        name + kind for name in ("w_in", "ln", "qkv", "out", "up", "down") for kind in ("_m", "_v")
    ]

    def store(name):
        place = ("out", "red_up", "red_dn", "red_qkv", "inc").index(name)
        return pltpu.make_async_copy(
            getattr(R, name), getattr(R, name + "_hbm"), R.store_sem.at[place]
        )

    def moment(name):
        return pltpu.make_async_copy(
            getattr(R, name), getattr(R, name + "_here"), R.moment_sem.at[names_of_moments.index(name)]
        )

    tile_rows = R.tw.shape[1]
    tiles = table_rows // tile_rows

    shares_of = -(-tiles // ways)

    def share_tile(turn):
        return lax.min(turn * ways + mp.me, tiles - 1)

    def tile_of(turn):
        side = lax.rem(turn, 2)
        rows = pl.ds(pl.multiple_of(share_tile(turn) * tile_rows, tile_rows), tile_rows)
        return [
            pltpu.make_async_copy(source.at[rows], dest.at[side], R.tile_sem.at[2 * place + side])
            for place, (source, dest) in enumerate(
                ((R.table, R.tw), (R.table_m, R.tm), (R.table_v, R.tv))
            )
        ]

    eye = lax.broadcasted_iota(jnp.int32, (seq_len, seq_len), 0) == lax.broadcasted_iota(
        jnp.int32, (seq_len, seq_len), 1
    )
    id_rows = R.ids[...].astype(F32)
    ids = jnp.concatenate(
        [
            jnp.sum(jnp.where(eye, id_rows[seq : seq + 1, :], 0.0), 1, keepdims=True)
            for seq in range(seqs)
        ],
        0,
    )
    lane = lax.broadcasted_iota(jnp.int32, (tokens, 128), 1).astype(F32)
    low_end = lane * float(table_rows)
    owned = jnp.where((ids >= low_end) & (ids < low_end + float(table_rows)), 1.0, 0.0)
    before = jnp.where(
        lax.broadcasted_iota(jnp.int32, (tokens, tokens), 0)
        >= lax.broadcasted_iota(jnp.int32, (tokens, tokens), 1),
        1.0,
        0.0,
    )
    ranks = dot(before.astype(LOW), owned.astype(LOW))
    rank = jnp.sum(owned * ranks, 1, keepdims=True) - 1.0
    slot = jnp.sum(owned * lane, 1, keepdims=True) * cap + rank
    placed = jnp.where(lane == rank, 1.0, 0.0)
    upper = jnp.floor(ids * (1.0 / 256.0))
    lower = ids - upper * 256.0
    parts = jnp.concatenate([placed * upper, placed * lower, placed], 1).astype(LOW)
    asked = dot_tn(owned.astype(LOW), parts)
    asked = asked[:, :128] * 256.0 + asked[:, 128:256] + asked[:, 256:] - 1.0
    wide_ln = R.ln_params.shape[1]
    shares = R.ln_params[...].astype(LOW).astype(F32)
    if wide_ln < 128:
        shares = jnp.concatenate([shares, jnp.zeros((4, 128 - wide_ln), F32)], 1)
    for index in range(size):
        R.ask[index] = jnp.concatenate(
            [asked[index : index + 1, :], shares, jnp.zeros((3, 128), F32)], 0
        )
    R.idx[mp.me, dp.me] = R.ask[dp.me]

    def spread(part, first, second, extra, send, recv):
        blocks = [block_rows(ref, strip) for ref in (part, first, second)]
        return Scatter(dp, *blocks, send, recv, 0, extra)

    up = spread(R.wbf, R.up_first, R.up_second, R.up_extra, R.up_send, R.up_recv)
    down = spread(R.gdn, R.dn_first, R.dn_second, R.dn_extra, R.dn_send, R.dn_recv)
    first_w = spread(
        R.waf.at[:, : 3 * heads_w], R.wa_first, R.wa_second, R.wa_extra, R.ga_send, R.ga_recv
    )
    wo = SideScatter(
        dp,
        *[block_rows(ref, strip) for ref in (R.gwo, R.wo_second)],
        R.wo_first,
        R.wo_send,
        R.wo_recv,
    )
    for scatter in (up, down, first_w):
        scatter.clear()

    meet([mp], [dp])
    ask, ask_wait = far_copies(
        dp,
        lambda dest, source: (R.ask.at[dest], R.idx.at[mp.me, source]),
        R.ask_send,
        R.ask_recv,
    )
    for step in range(1, size):
        ask(step).start()

    mine_in = R.winf.at[mp.me]
    win = Gather(dp, block_rows(mine_in, rin), R.win_send, R.win_recv, 0, True)
    win_all = Gather(mp, of_index(R.winf), R.wim_send, R.wim_recv)
    wa = [
        Gather(dp, part_rows(R.waf, strip, piece * half_strip, half_strip), send, recv, 0, True)
        for piece, (send, recv) in enumerate(((R.wa_send, R.wa_recv), (R.wx_send, R.wx_recv)))
    ]
    wb = Gather(dp, block_rows(R.wbf, strip), R.wb_send, R.wb_recv, 0, True)
    wc = Gather(dp, part_rows(R.wcf, strip, 0, half_strip), R.wc_send, R.wc_recv, 0, True)
    wd = SideGather(dp, part_rows(R.wcf, strip, half_strip, half_strip), R.wd_send, R.wd_recv, 0, True)
    dxg = Gather(
        mp,
        lambda index: R.dx.at[:, pl.ds(pl.multiple_of(index * seq_len, seq_len), seq_len)],
        R.dx_send,
        R.dx_recv,
    )
    ag = halves(R.a, R.a_send, R.a_recv)
    cg = halves(R.c, R.c_send, R.c_recv)
    mg = halves(R.dmid_all, R.e_send, R.e_recv)

    mine_in[pl.ds(pl.multiple_of(dp.me * rin, rin), rin), :] = (
        R.w_in[:, pl.ds(pl.multiple_of(mp.me * quarter, quarter), quarter)]
        .astype(LOW)
        .astype(R.winf.dtype)
    )
    win.start()
    for part in range(3):
        R.waf[own_strip, part * heads_w : (part + 1) * heads_w] = R.w_qkv[part].astype(LOW)
    R.waf[own_strip, 3 * heads_w :] = R.w_out[...].T.astype(LOW)
    wa[0].start()
    wa[1].start_near()

    ask_wait()
    small_eye = lax.broadcasted_iota(jnp.int32, (cap, 128), 0) == lax.broadcasted_iota(
        jnp.int32, (cap, 128), 1
    )

    def locate(index, carry):
        row = R.idx[mp.me, index][0:1, :]
        column = jnp.sum(jnp.where(small_eye, row, 0.0), 1, keepdims=True)
        local = column.astype(jnp.int32) - dp.me * table_rows
        R.loc[pl.ds(pl.multiple_of(index * cap, cap), cap), :] = jnp.broadcast_to(local, (cap, 128))
        return carry

    lax.fori_loop(0, size, locate, 0, unroll=True)
    win.relays()
    found = None
    for piece in range(pieces):
        fetch(piece).wait()
        rows = min(chunk, table_rows - piece * chunk)
        if rows < chunk:
            R.tab[piece % 2, rows:, :] = jnp.zeros((chunk - rows, width), F32)
        hit = (
            lax.broadcasted_iota(jnp.int32, (spots, chunk), 1) + piece * chunk == R.loc[:, 0:1]
        )
        more = dot(jnp.where(hit, 1.0, 0.0).astype(LOW), R.tab[piece % 2].astype(LOW))
        found = more if found is None else found + more
        if piece + 2 < pieces:
            fetch(piece + 2).start()
    R.give[...] = found.astype(LOW)

    give, give_wait = far_copies(
        dp,
        lambda dest, source: (block_rows(R.give, cap)(dest), block_rows(R.got, cap)(source)),
        R.give_send,
        R.give_recv,
    )
    for step in range(1, size):
        give(step).start()
    R.got[mine, :] = R.give[mine, :]
    wa[1].start_far()
    named = Gather(mp, of_index(R.idx), R.id_send, R.id_recv)
    named.start()
    for name in names_of_moments:
        moment(name).start()
    win.close()
    win_all.start()
    wa[0].relay(1)
    for seq in range(seqs):
        level = jnp.full((seq_len, 1), R.levels[seq], jnp.int32).astype(F32) / (LEVELS - 1)
        R.sig[seq * seq_len : (seq + 1) * seq_len, :] = jnp.exp(level * jnp.log(SIGMA_TOP))

    def scale_at(here):
        sig = R.sig[here, :]
        return sig * lax.rsqrt(1.0 + sig * sig)

    for piece in range(seqs):
        here = rows_of(piece)

        def scale_cot(row, here=here, piece=piece):
            there = pl.ds(pl.multiple_of(mp.me * seq_len + row, some_rows), some_rows)
            R.dx[piece, there, :] = (R.cot[here(row), :].astype(F32) * scale_at(here(row))).astype(LOW)

        by_rows(scale_cot)
    dxg.start()
    R.wbf[own_strip, :] = R.w_up[...].astype(LOW)
    R.wcf[own_strip, :] = R.w_down[...].T.astype(LOW)
    wb.start_near()
    R.pick[...] = jnp.where(
        lax.broadcasted_iota(jnp.int32, (tokens, spots), 1).astype(F32) == slot, 1.0, 0.0
    ).astype(LOW)
    win_all.relays()
    named.relays()
    wa[0].relay(2)
    if wide_ln % 128 == 0:
        R.gains[...] = jnp.concatenate([R.idx[mp.me, index] for index in range(size)], 1)
    else:
        total = jnp.zeros((8, model), F32)
        for index in range(size):
            place = lax.broadcasted_iota(
                jnp.int32, (128, model), 1
            ) == index * wide_ln + lax.broadcasted_iota(jnp.int32, (128, model), 0)
            place = place & (lax.broadcasted_iota(jnp.int32, (128, model), 0) < wide_ln)
            total = total + dot(
                R.idx[mp.me, index].astype(LOW), jnp.where(place, 1.0, 0.0).astype(LOW)
            )
        R.gains[...] = total
    for step in range(3, dp.far):
        wa[0].relay(step)

    give_wait()
    rows = dot(R.pick[...], R.got[...])
    R.rows[...] = rows.astype(LOW)
    sig = R.sig[...]
    unit = rows * lax.rsqrt(jnp.mean(rows * rows, -1, keepdims=True) + EPS_NORM)
    R.mixed[...] = ((unit + sig * R.noise[...].astype(F32)) * lax.rsqrt(1.0 + sig * sig)).astype(LOW)
    win_all.close()
    for index in range(ways):
        R.x0[:, index * quarter : (index + 1) * quarter] = dot(
            R.mixed[...], R.winf[index].astype(LOW)
        )

    for piece in range(seqs):
        here, there = rows_of(piece), own_rows(piece)

        def first_norm(row, here=here, there=there):
            normed, _ = norm_rows(R.x0[here(row), :])
            R.a[there(row), :] = (normed * R.gains[1:2, :] + R.gains[2:3, :]).astype(LOW)

        by_rows(first_norm, ag[piece].start)
    wb.start_far()
    wa[1].relay(1)
    for step in range(2, dp.far):
        wa[1].relay(step)
    dxg.relays()
    ag[0].relays()
    wd.start_near()
    wc.start_near()
    wc.start_far()
    for gather in (*wa, ag[0]):
        gather.close()

    att = Sums(R.part, R.fold, R.fold_far, R.as_send, R.as_recv)
    dcs = Sums(R.part, R.fold, R.fold_far, R.cs_send, R.cs_recv)
    das = Sums(R.part, R.fold, R.fold_far, R.ds_send, R.ds_recv)
    out = Sums(R.c, R.first, R.second, R.os_send, R.os_recv)
    masks = head_masks(heads_w)

    all_rows = (heads_w // HD) * seq_len
    scale = HD ** (-0.5)

    def softmax(seq, row):
        scores = R.scores[seq, row : row + 64, :]
        raised = jnp.exp((scores - jnp.max(scores, -1, keepdims=True)) * scale)
        return raised * (1.0 / jnp.sum(raised, -1, keepdims=True))

    def attend(piece, base, here, at):
        at("start")
        for part in range(3):
            cols = slice(part * heads_w, (part + 1) * heads_w)
            R.qkv[here, cols] = dot(R.a[here, :], R.waf[:, cols]).astype(LOW)
        at("mid")

        def one(rows_at):
            for seq, rows in enumerate(rows_at):
                queries = spread_heads(R.qkv[rows, :heads_w], masks)
                R.scores[seq] = dot_nt(queries, R.qkv[rows, heads_w : 2 * heads_w])
            for seq, rows in enumerate(rows_at):
                for row in range(0, all_rows, 64):
                    R.probs[seq, row : row + 64, :] = softmax(seq, row).astype(LOW)
                seen = dot(R.probs[seq], R.qkv[rows, 2 * heads_w : 3 * heads_w])
                R.o[rows, :] = join_heads(seen, masks, seq_len).astype(LOW)

        pairs(base, one)
        at("late")

        def project(cols):
            R.part[here, cols] = dot_nt(R.o[here, :], R.waf[cols, 3 * heads_w :]).astype(LOW)

        def one_chunk(chunk, carry):
            project(pl.ds(pl.multiple_of(chunk * chunk_cols, chunk_cols), chunk_cols))
            att.trade(piece, chunk)
            return carry

        lax.fori_loop(0, chunk_count, one_chunk, 0)

    def second_norm(piece):
        here, there = rows_of(piece), own_rows(piece)
        att.arrive(piece)

        def norm(row):
            x1 = R.x0[here(row), :] + att.total(piece, pl.ds(row, some_rows))
            R.out[here(row), :] = x1
            normed, _ = norm_rows(x1)
            R.c[there(row), :] = (normed * R.gains[3:4, :] + R.gains[4:5, :]).astype(LOW)

        by_rows(norm, cg[piece].start)

    def first_wb():
        wb.relay(1)
        wd.start_far()

    def middle_wb():
        wb.relay(2)
        wd.start_other()

    def last_wb():
        for step in range(3, dp.far):
            wb.relay(step)

    turns(
        attend,
        [
            *later_pieces(ag, "mid"),
            *[
                (piece + 1, "mid", functools.partial(att.hand_on_all, piece))
                for piece in range(seqs - 1)
            ],
            (0, "mid", first_wb),
            (0, "late", middle_wb),
            (1, "mid", last_wb),
            *[
                (piece + 1, "late", functools.partial(second_norm, piece))
                for piece in range(seqs - 1)
            ],
        ],
    )
    att.hand_on_all(seqs - 1)
    cg[0].relays()
    wc.relay(1)
    wb.close()
    cg[0].close()

    def activate(piece, base, here, at):
        at("start")

        def some(cols):
            R.h[...] = dot(R.c[here, :], R.wbf[:, cols])

            def gelu(row):
                there = pl.ds(pl.multiple_of(base + row, 64), 64)
                h = R.h[pl.ds(row, 64), :]
                bell = jnp.exp(-0.5 * h * h)
                tail = normal_tail(jnp.abs(h), bell)
                gate = jnp.where(h >= 0.0, 1.0 - tail, tail)
                slope = gate + h * (bell * 0.3989422804014327)
                R.hb[there, cols] = (h * gate).astype(LOW)
                R.slope[there, cols] = slope.astype(LOW)

            strips(many, 64, gelu, 2)

        def before(turn):
            for place in range(seqs - 1):
                pl.when((piece == place) & (turn == 1))(functools.partial(second_norm, place + 1))

        chunks(hidden, some, before)
        at("end")

    def last_wc():
        wc.relay(2)
        for step in range(3, dp.far):
            wc.relay(step)

    turns(activate, [*later_pieces(cg, "end"), (0, "end", last_wc), (seqs - 1, "start", wd.forward)])
    for piece in range(seqs):
        att.drain(piece)

    due = [(scatter, step) for scatter in (down, up) for step in range(1, dp.far)]

    def pass_due(number):
        for _ in range(min(number, len(due))):
            scatter, step = due.pop(0)
            scatter.pass_on(step)

    block = 2 * strip if (2 * strip) % 128 == 0 else min(256, model)

    def grads(make, trades):
        if block == 2 * strip:

            def turn_of(turn, carry):
                hi = up.turn_of(turn)
                make(pl.ds(pl.multiple_of(hi * block, block), block))
                for scatter in trades:
                    scatter.trade(hi)
                return carry

            lax.fori_loop(0, dp.far, turn_of, 0)
        else:
            strips(model, block, lambda col: make(pl.ds(col, block)))
            for scatter in trades:
                scatter.trade_all()

    def down_grads(cols):
        every = R.dx[:, :, cols]
        R.gdn[cols, :] = dot_tn(every.reshape(seqs * many, block), R.hb[...]).astype(LOW)

    def up_grads(cols):
        R.wbf[cols, :] = dot_tn(R.c[:, cols], R.dhb[...]).astype(LOW)

    dxg.close()
    grads(down_grads, (down,))
    named.close()
    groups = ways * size
    some, lanes_at = min(groups, 32), min(ways * spots, 512)
    for begin in range(0, ways * spots, lanes_at):
        spot = lax.broadcasted_iota(jnp.int32, (128, lanes_at), 1).astype(F32) + float(begin)
        block_no = jnp.floor((spot + 0.5) * (1.0 / cap))
        place = lax.broadcasted_iota(jnp.int32, (128, lanes_at), 0).astype(F32)
        spread_out = jnp.where(spot - block_no * cap == place, 1.0, 0.0).astype(LOW)
        named_row = jnp.zeros((1, lanes_at), F32)
        for first in range(0, groups, some):
            wanted = jnp.concatenate(
                [
                    R.idx[index // size, index % size][0:1, :] + 1.0
                    for index in range(first, first + some)
                ],
                0,
            )
            high = jnp.floor(wanted * (1.0 / 256.0))
            rest = wanted - 256.0 * high
            laid = dot(high.astype(LOW), spread_out) * 256.0 + dot(rest.astype(LOW), spread_out) - 1.0
            own_block = block_no[0:1, :] == float(first) + lax.broadcasted_iota(
                jnp.int32, (some, lanes_at), 0
            ).astype(F32)
            named_row = named_row + jnp.sum(jnp.where(own_block, laid, 0.0), 0, keepdims=True)
        R.named[:, begin : begin + lanes_at] = jnp.broadcast_to(
            named_row.astype(jnp.int32) - dp.me * table_rows, (8, lanes_at)
        )
    wc.close()
    wd.close()
    for gather in (wb, *cg):
        gather.drain()

    def feed_back(piece, base, here, at):
        at("start")

        def some(cols):
            bent = dot(R.dx[piece], R.wcf[:, cols]) * R.slope[here, cols].astype(F32)
            R.dhb[here, cols] = bent.astype(LOW)

        chunks(hidden, some)
        at("mid")

        def project(cols):
            R.part[here, cols] = dot_nt(R.dhb[here, :], R.wbf[cols, :]).astype(LOW)

        dcs.products(piece, project)

    R.norms[...] = jnp.zeros_like(R.norms)

    def second_back(piece):
        here, there = rows_of(piece), own_rows(piece)
        dcs.arrive(piece)

        def back(row):
            dc = dcs.total(piece, pl.ds(row, some_rows))
            grad, unit = norm_back(R.out[here(row), :], R.gains[3:4, :], dc)
            grad = grad + R.cot[here(row), :].astype(F32) * scale_at(here(row))
            R.dmid[here(row), :] = grad
            R.dmid_all[there(row), :] = grad.astype(LOW)
            R.norms[2:3, :] += jnp.sum(dc * unit, 0, keepdims=True)
            R.norms[3:4, :] += jnp.sum(dc, 0, keepdims=True)

        by_rows(back, mg[piece].start)

    turns(
        feed_back,
        [
            *[
                (piece + 1, "mid", functools.partial(dcs.hand_on_last, piece))
                for piece in range(seqs - 1)
            ],
            (1, "mid", lambda: pass_due(1)),
        ],
    )
    dcs.hand_on_last(seqs - 1)
    second_back(0)
    pass_due(1)
    grads(up_grads, (up,))
    for piece in range(1, seqs):
        second_back(piece)
    pass_due(max(1, dp.far - 3))
    mg[0].relays()
    mg[0].close()
    for piece in range(seqs):
        dcs.drain(piece)

    def attend_back(piece, base, here, at):
        at("start")
        R.low[...] = dot(R.dmid_all[here, :], R.waf[:, 3 * heads_w :]).astype(LOW)
        at("mid")

        def one(rows_at):
            for seq, rows in enumerate(rows_at):
                queries = spread_heads(R.qkv[rows, :heads_w], masks)
                R.scores[seq] = dot_nt(queries, R.qkv[rows, heads_w : 2 * heads_w])
                upper_rows = pl.ds(pl.multiple_of(rows.start - base, seq_len), seq_len)
                R.upper[seq] = spread_heads(R.low[upper_rows, :], masks)
                R.dprobs[seq] = dot_nt(R.upper[seq], R.qkv[rows, 2 * heads_w : 3 * heads_w])
            for seq, rows in enumerate(rows_at):
                for row in range(0, all_rows, 64):
                    probs = softmax(seq, row)
                    grad_probs = R.dprobs[seq, row : row + 64, :]
                    inner = jnp.sum(probs * grad_probs, -1, keepdims=True)
                    R.probs[seq, row : row + 64, :] = probs.astype(LOW)
                    R.dscores[seq, row : row + 64, :] = (probs * (grad_probs - inner)).astype(LOW)
                keys = R.qkv[rows, heads_w : 2 * heads_w]
                queries = spread_heads(R.qkv[rows, :heads_w], masks)
                R.qkv[rows, 2 * heads_w : 3 * heads_w] = dot_tn(R.probs[seq], R.upper[seq]).astype(LOW)
                R.qkv[rows, heads_w : 2 * heads_w] = (dot_tn(R.dscores[seq], queries) * scale).astype(
                    LOW
                )
                R.qkv[rows, :heads_w] = (
                    join_heads(dot(R.dscores[seq], keys), masks, seq_len) * scale
                ).astype(LOW)

        pairs(base, one)
        at("late")

        def project(cols):
            R.part[here, cols] = dot_nt(R.qkv[here, :], R.waf[cols, : 3 * heads_w]).astype(LOW)

        das.products(piece, project)

    def first_back(piece):
        here = rows_of(piece)
        das.arrive(piece)

        def back(row):
            da = das.total(piece, pl.ds(row, some_rows))
            grad, unit = norm_back(R.x0[here(row), :], R.gains[1:2, :], da)
            R.dx0[here(row), :] = (R.dmid[here(row), :] + grad).astype(LOW)
            R.norms[0:1, :] += jnp.sum(da * unit, 0, keepdims=True)
            R.norms[1:2, :] += jnp.sum(da, 0, keepdims=True)

        by_rows(back)

    def out_grads():
        def make(cols):
            R.gwo[cols, :] = dot_tn(R.dmid_all[:, cols], R.o[...]).astype(LOW)

        grads(make, (wo,))

    turns(
        attend_back,
        [
            *later_pieces(mg, "mid"),
            (0, "late", lambda: pass_due(1)),
            *[
                (piece + 1, "mid", functools.partial(das.hand_on_last, piece))
                for piece in range(seqs - 1)
            ],
            (seqs - 1, "late", lambda: pass_due(1)),
        ],
    )
    das.hand_on_last(seqs - 1)
    def out_grads(cols):
        R.gwo[cols, :] = dot_tn(R.dmid_all[:, cols], R.o[...]).astype(LOW)

    def attend_grads(cols):
        R.waf[cols, : 3 * heads_w] = dot_tn(R.a[:, cols], R.qkv[...]).astype(LOW)

    first_back(0)
    pass_due(len(due))
    for gather in (*wa, *ag, dxg, win):
        gather.drain()
    for step in range(1, size):
        ask(step).wait_send()
    grads(attend_grads, (first_w,))
    grads(out_grads, ())
    wo.start()
    for piece in range(1, seqs):
        first_back(piece)

    grad_mixed = sum(
        dot_nt(R.dx0[:, index * quarter : (index + 1) * quarter], R.winf[index].astype(LOW))
        for index in range(ways)
    )
    sig = R.sig[...]
    grad_unit = grad_mixed * lax.rsqrt(1.0 + sig * sig)
    rows = R.rows[...].astype(F32)
    inverse = lax.rsqrt(jnp.mean(rows * rows, -1, keepdims=True) + EPS_NORM)
    unit = rows * inverse
    grad_rows = inverse * (grad_unit - unit * jnp.mean(grad_unit * unit, -1, keepdims=True))
    for step in range(1, size):
        give(step).wait_send()
    R.give[...] = dot_tn(R.pick[...], grad_rows.astype(LOW)).astype(LOW)
    mine_inc = block_rows(R.inc, spots)(mp.me)
    back, back_wait = far_copies(
        dp,
        lambda dest, source: (block_rows(R.give, cap)(dest), block_rows(mine_inc, cap)(source)),
        R.back_send,
        R.back_recv,
    )
    for step in range(1, size):
        back(step).start()
    mine_inc[mine, :] = R.give[mine, :]

    small_mp = Scatter(
        mp, of_index(R.gm), of_index(R.gm_first), of_index(R.gm_second), R.gm_send, R.gm_recv
    )
    for index in range(ways):
        cols = slice(index * quarter, (index + 1) * quarter)
        R.gm[index, :width, :] = dot_tn(R.mixed[...], R.dx0[:, cols]).astype(LOW)
        R.gm[index, width:, :] = jnp.concatenate(
            [R.norms[0:4, cols], jnp.zeros((12, quarter), F32)], 0
        ).astype(LOW)
    small_mp.trade_all()
    for step in range(1, far):
        small_mp.pass_on(step)

    first_w.pass_on(1)

    def feed_out(piece, base, here, at):
        def project(cols):
            R.c[here, cols] = dot_nt(R.hb[here, :], R.wcf[cols, :]).astype(LOW)

        out.products(piece, project)

    turns(feed_out)
    wo.trade()
    first_w.pass_on(2)
    for turn in range(min(2, shares_of)):
        for one in tile_of(turn):
            one.start()
    back_wait()
    rows_in = Gather(mp, block_rows(R.inc, spots), R.in_send, R.in_recv)
    rows_in.start()
    for piece in range(seqs):
        out.hand_on_last(piece)

    small_mp.arrive()
    summed = small_mp.total(slice(None))
    for index in range(size):
        piece = summed[index * rin : (index + 1) * rin, :]
        if rin_up > rin:
            piece = jnp.concatenate([piece, jnp.zeros((rin_up - rin, quarter), F32)], 0)
        R.gw[index, :rin_up, :] = piece.astype(LOW)
        R.gw[index, rin_up:, :] = summed[width:, :].astype(LOW)
    R.gw_in[dp.me] = R.gw[dp.me]
    small, small_wait = far_copies(
        dp, lambda dest, source: (R.gw.at[dest], R.gw_in.at[source]), R.gw_send, R.gw_recv
    )
    for step in range(1, size):
        small(step).start()
    rows_in.relays()
    for step in range(3, dp.far):
        first_w.pass_on(step)

    def finish_out(piece):
        here = rows_of(piece)
        out.arrive(piece)

        def finish(row):
            R.out[here(row), :] = (
                R.out[here(row), :] + out.total(piece, pl.ds(row, some_rows))
            ) * scale_at(here(row))

        by_rows(finish)

    for piece in range(seqs):
        finish_out(piece)
    store("out").start()

    rows_in.close()
    store("inc").start()

    once = jnp.where(mp.me == 0, 1.0, 0.0)
    lanes = lax.broadcasted_iota(jnp.int32, (1, 128), 1)
    R.sums[...] = jnp.zeros_like(R.sums)

    def put(place, squares, factor=None):
        for row, values in enumerate(squares):
            total = jnp.sum(jnp.sum(values, 0, keepdims=True), 1, keepdims=True)
            if factor is not None:
                total = total * factor
            R.sums[row : row + 1, :] += jnp.where(lanes == place, total, 0.0)

    def squares_of(weight, gradient, first, second):
        direction = direction_of(weight, gradient, first, second)[2]
        return weight * weight, direction * direction

    def folded(values):
        rows, columns = values.shape
        return jnp.sum(values.reshape(rows // 8, 8, columns), 0)

    def add_up(weight, gradient, first, second):
        squares = squares_of(weight[...], gradient[...], first[...], second[...])
        return [folded(values) for values in squares]

    zero = jnp.zeros((8, width), F32)

    def add_tile(turn, carry):
        side = lax.rem(turn, 2)
        for one in tile_of(turn):
            one.wait()
        hit = (
            lax.broadcasted_iota(jnp.int32, (tile_rows, ways * spots), 0)
            + share_tile(turn) * tile_rows
            == R.named[0:1, :]
        )
        gradient = dot(jnp.where(hit, 1.0, 0.0).astype(LOW), R.inc[...])
        more = add_up(R.tw.at[side], gradient, R.tm.at[side], R.tv.at[side])
        counts = jnp.where(turn * ways + mp.me < tiles, 1.0, 0.0)

        @pl.when(turn + 2 < shares_of)
        def _():
            for one in tile_of(turn + 2):
                one.start()

        return carry[0] + counts * more[0], carry[1] + counts * more[1]

    put(0, lax.fori_loop(0, shares_of, add_tile, (zero, zero)))

    for thing in (win_all, wc, wd, *mg, up, down, small_mp, named):
        thing.drain()
    for piece in range(seqs):
        out.drain(piece)
        das.drain(piece)
    for step in range(1, size):
        back(step).wait_send()

    for name in names_of_moments:
        moment(name).wait()
    up.arrive()

    R.red_up[...] = up.total(slice(None))
    store("red_up").start()
    put(10, add_up(R.w_up, R.red_up, R.up_m_here, R.up_v_here))
    down.arrive()

    R.red_dn[...] = down.total(slice(None)).T
    store("red_dn").start()
    put(11, add_up(R.w_down, R.red_dn, R.down_m_here, R.down_v_here))
    wo.arrive()
    R.red_out[...] = wo.total().T
    put(9, add_up(R.w_out, R.red_out, R.out_m_here, R.out_v_here))

    small_wait()
    R.wsum[mp.me] = jnp.sum(R.gw_in[...].astype(F32), 0).astype(LOW)
    weights_in = Gather(mp, of_index(R.wsum), R.ws_send, R.ws_recv)
    weights_in.start()
    first_w.arrive()

    value = first_w.total(slice(None))
    for part in range(3):
        R.red_qkv[part] = value[:, part * heads_w : (part + 1) * heads_w]
    store("red_qkv").start()
    weights_in.relays()
    for part in range(3):
        put(
            6 + part,
            add_up(
                R.w_qkv.at[part], R.red_qkv.at[part], R.qkv_m_here.at[part], R.qkv_v_here.at[part]
            ),
        )
    weights_in.close()
    total = jnp.concatenate([R.wsum[index].astype(F32) for index in range(ways)], 1)
    R.red_in[...] = total[:rin, :]
    put(1, add_up(R.w_in, R.red_in, R.w_in_m_here, R.w_in_v_here), once)
    if strip % 128 == 0:
        R.lnsum[...] = total[rin_up : rin_up + 8, :]
        R.red_ln[...] = R.lnsum[0:4, pl.ds(pl.multiple_of(dp.me * strip, strip), strip)]
    else:
        chosen = lax.broadcasted_iota(jnp.int32, (model, strip), 0) == dp.me * strip + (
            lax.broadcasted_iota(jnp.int32, (model, strip), 1)
        )
        R.red_ln[...] = dot(
            total[rin_up : rin_up + 8, :].astype(LOW), jnp.where(chosen, 1.0, 0.0).astype(LOW)
        )[0:4]
    squares = squares_of(R.ln_params[...], R.red_ln[...], R.ln_m_here[...], R.ln_v_here[...])
    for row in range(4):
        put(2 + row, [values[row : row + 1, :] for values in squares], once)

    R.near[dp.me] = R.sums[...]
    near, near_wait = far_copies(
        dp, lambda dest, source: (R.near.at[dp.me], R.near.at[source]), R.near_send, R.near_recv
    )
    for step in range(1, size):
        near(step).start()
    near_wait()
    R.wide[mp.me] = jnp.sum(R.near[...], 0)
    far_off, far_off_wait = far_copies(
        mp, lambda dest, source: (R.wide.at[mp.me], R.wide.at[source]), R.wide_send, R.wide_recv
    )
    for step in range(1, ways):
        far_off(step).start()
    far_off_wait()
    R.totals[...] = jnp.sum(R.wide[...], 0)

    for thing in (wo, first_w, rows_in, weights_in):
        thing.drain()
    for step in range(1, size):
        near(step).wait_send()
        small(step).wait_send()
    for step in range(1, ways):
        far_off(step).wait_send()
    for name in ("out", "red_up", "red_dn", "red_qkv", "inc"):
        store(name).wait()


def run_layer(cap, ids, levels, noise, cot, weights, moments):
    table, w_in, ln_params, w_qkv, w_out, w_up, w_down = weights
    dp, mp = lax.axis_size("dp"), lax.axis_size("mp")
    seqs, seq_len = ids.shape
    tokens, width = noise.shape
    model = cot.shape[1]
    rin = w_in.shape[0]
    heads_w = w_qkv.shape[2]
    strip, hidden = w_up.shape
    group = tokens * mp
    spots = dp * cap
    wide = round_up(rin, 16) + 16
    far, far_dp = mp // 2, dp // 2
    quarter = model // mp
    in_kind = LOW if rin % 16 == 0 else F32
    tile_rows = max(rows for rows in range(8, 257, 8) if table.shape[0] % rows == 0)
    stacked = (heads_w // HD) * seq_len
    vmem = pl.BlockSpec(memory_space=pltpu.VMEM)
    outside = pl.BlockSpec(memory_space=pl.ANY)
    inputs = dict(
        ids=(ids, vmem),
        levels=(levels, pl.BlockSpec(memory_space=pltpu.SMEM)),
        noise=(noise, vmem),
        cot=(cot, vmem),
        table=(table, outside),
        w_in=(w_in, vmem),
        ln_params=(ln_params, vmem),
        w_qkv=(w_qkv, vmem),
        w_out=(w_out, vmem),
        w_up=(w_up, vmem),
        w_down=(w_down, vmem),
    )
    kept = {}
    for name, (first, second) in zip(("table", "w_in", "ln", "qkv", "out", "up", "down"), moments):
        inputs[name + "_m"] = (first, outside)
        inputs[name + "_v"] = (second, outside)
        if name != "table":
            kept[name + "_m_here"] = kept[name + "_v_here"] = (first.shape, F32)
    own_stores = dict(
        out=((tokens, model), F32),
        red_up=((strip, hidden), F32),
        red_dn=((hidden, strip), F32),
        red_qkv=((3, strip, heads_w), F32),
        inc=((mp * spots, width), LOW),
    )
    outputs = dict(
        **{name + "_hbm": shape for name, shape in own_stores.items()},
        red_out=((heads_w, strip), F32),
        red_in=((rin, model), F32),
        red_ln=((4, strip), F32),
        named=((8, mp * spots), jnp.int32),
        totals=((8, 128), F32),
    )
    buffers = dict(
        tab=((2, round_up(table.shape[0] // 8, 128), width), F32),
        ask=((dp, 8, 128), F32),
        idx=((mp, dp, 8, 128), F32),
        loc=((spots, 128), jnp.int32),
        give=((spots, width), LOW),
        got=((spots, width), LOW),
        tw=((2, tile_rows, width), F32),
        tm=((2, tile_rows, width), F32),
        tv=((2, tile_rows, width), F32),
        sums=((8, 128), F32),
        near=((dp, 8, 128), F32),
        wide=((mp, 8, 128), F32),
        scores=((2, stacked, seq_len), F32),
        dprobs=((2, stacked, seq_len), F32),
        probs=((2, stacked, seq_len), LOW),
        dscores=((2, stacked, seq_len), LOW),
        upper=((2, stacked, heads_w), LOW),
        gwo=((model, heads_w), LOW),
        wo_first=((strip, heads_w), LOW),
        wo_second=((dp * strip, heads_w), LOW),
        gains=((8, model), F32),
        lnsum=((8, model), F32),
        sig=((tokens, 1), F32),
        pick=((tokens, spots), LOW),
        rows=((tokens, width), LOW),
        mixed=((tokens, width), LOW),
        x0=((tokens, model), F32),
        a=((group, model), LOW),
        c=((group, model), LOW),
        dx=((seqs, group // seqs, model), LOW),
        dmid=((tokens, model), F32),
        dmid_all=((group, model), LOW),
        winf=((mp, rin * dp, quarter), in_kind),
        waf=((model, 4 * heads_w), LOW),
        wbf=((model, hidden), LOW),
        wcf=((model, hidden), LOW),
        qkv=((group, 3 * heads_w), LOW),
        o=((group, heads_w), LOW),
        low=((group // seqs, heads_w), LOW),
        part=((group, model), LOW),
        first=((far * tokens, model), LOW),
        fold=((far * tokens, model), LOW),
        second=((far * tokens, model), LOW),
        fold_far=((far * tokens, model), LOW),
        h=((group // seqs, min(256, hidden)), F32),
        hb=((group, hidden), LOW),
        dhb=((group, hidden), LOW),
        slope=((group, hidden), LOW),
        gdn=((model, hidden), LOW),
        dx0=((tokens, model), LOW),
        norms=((8, model), F32),
        gm=((mp, width + 16, quarter), LOW),
        gm_first=((far, width + 16, quarter), LOW),
        gm_second=((far, width + 16, quarter), LOW),
        gw=((dp, wide, quarter), LOW),
        gw_in=((dp, wide, quarter), LOW),
        up_first=((far_dp * strip, hidden), LOW),
        up_second=((far_dp * strip, hidden), LOW),
        dn_first=((far_dp * strip, hidden), LOW),
        dn_second=((far_dp * strip, hidden), LOW),
        wa_first=((far_dp * strip, 3 * heads_w), LOW),
        wa_second=((far_dp * strip, 3 * heads_w), LOW),
        wsum=((mp, wide, quarter), LOW),
        up_extra=((strip, hidden), LOW),
        dn_extra=((strip, hidden), LOW),
        wa_extra=((strip, 3 * heads_w), LOW),
        **kept,
        **own_stores,
    )
    sems = dict(store_sem=5, tab_sem=2, tile_sem=6, moment_sem=12)
    for name in (
        *("win", "wa", "wx", "wb", "wc", "wd", "ask", "give", "back"),
        *("up", "dn", "ga", "wo", "gw", "near"),
    ):
        sems[name + "_send"] = sems[name + "_recv"] = dp + 1
    for name in ("wim", "id", "in", "ws", "gm", "wide"):
        sems[name + "_send"] = sems[name + "_recv"] = mp
    for name in ("dx", "a", "c", "e"):
        sems[name + "_send"] = sems[name + "_recv"] = 2 * seqs * mp
    for name in ("as", "os", "cs", "ds"):
        sems[name + "_send"] = sems[name + "_recv"] = seqs * mp * (model // min(256, model))
    names = [*inputs, *outputs, *buffers, *sems]
    made = pl.pallas_call(
        functools.partial(layer_kernel, cap, names),
        out_shape=[jax.ShapeDtypeStruct(shape, kind) for shape, kind in outputs.values()],
        in_specs=[spec for _, spec in inputs.values()],
        out_specs=[outside if name.endswith("_hbm") else vmem for name in outputs],
        scratch_shapes=[
            *[pltpu.VMEM(shape, kind) for shape, kind in buffers.values()],
            *[pltpu.SemaphoreType.DMA((number,)) for number in sems.values()],
        ],
        compiler_params=pltpu.CompilerParams(
            vmem_limit_bytes=VMEM_BYTES, collective_id=1, has_side_effects=True
        ),
        name="layer",
    )(*[value for value, _ in inputs.values()])
    return {name.removesuffix("_hbm"): value for name, value in zip(outputs, made)}


def direction_of(weight, gradient, first, second):
    first_new = BETA_ONE * first + (1.0 - BETA_ONE) * gradient
    second_new = BETA_TWO * second + (1.0 - BETA_TWO) * gradient * gradient
    second_hat = second_new * (1.0 / (1.0 - BETA_TWO**STEP))
    inverse = lax.rsqrt(second_hat)
    root = second_hat * inverse + EPS_ADAM
    inverse = inverse * (2.0 - root * inverse)
    inverse = inverse * (2.0 - root * inverse)
    direction = first_new * (1.0 / (1.0 - BETA_ONE**STEP)) * inverse + DECAY * weight
    return first_new, second_new, direction


def update_kernel(part, names, *refs):
    R = types.SimpleNamespace(**dict(zip(names, refs)))
    turn = pl.program_id(0)
    R.out_rows[...] = R.made[...]
    norms = jnp.sqrt(R.totals[...])
    R.norms[...] = norms[0:2, 0:12]
    factors = norms[0:1, :] / (norms[1:2, :] + EPS_ADAM) * RATE

    def piece(name, here, gradient, place, rows=slice(None)):
        weight = getattr(R, name)[here]
        first_new, second_new, direction = direction_of(
            weight, gradient, getattr(R, name + "_m")[here], getattr(R, name + "_v")[here]
        )
        if isinstance(place, int):
            factor = factors[0:1, place : place + 1]
        else:
            factor = jnp.concatenate([factors[0:1, one : one + 1] for one in place], 0)
        getattr(R, name + "_m_new")[here] = first_new
        getattr(R, name + "_v_new")[here] = second_new
        getattr(R, name + "_new")[here] = weight - factor * direction

    def update(name, gradient, place, lead=(), here=slice(None)):
        piece(name, (*lead, here, slice(None)), gradient, place)

    tile = R.table.shape[0]
    spots = R.named.shape[1]

    def table_part(row):
        hit = (
            lax.broadcasted_iota(jnp.int32, (part, spots), 0) + (turn * tile + row)
            == R.named[0:1, :]
        )
        gradient = dot(jnp.where(hit, 1.0, 0.0).astype(LOW), R.inc[...])
        update("table", gradient, 0, (), pl.ds(row, part))

    strips(tile, part, table_part)
    for group in range(3):
        update("qkv", R.red_qkv[group], 6 + group, (group,))
    update("up", R.red_up[...], 10)
    update("down", R.red_dn[...], 11)

    @pl.when(turn == 0)
    def _():
        update("out", R.red_out[...], 9)
        update("w_in", R.red_in[...], 1)
        piece("ln", (slice(None), slice(None)), R.red_ln[...], (2, 3, 4, 5))


def turns_of(rows, parts):
    return [
        turns
        for turns in (5, 4, 2, 1)
        if rows % (8 * turns) == 0 and all(size % (8 * turns) == 0 for size in parts)
    ][0]


def run_update(weights, moments, grads):
    names = ("table", "w_in", "ln", "qkv", "out", "up", "down")
    by_name = dict(zip(names, weights))
    rows, width = by_name["table"].shape
    strip, hidden = by_name["up"].shape
    heads_w = by_name["qkv"].shape[2]
    turns = turns_of(rows, (strip, hidden))
    tile = rows // turns
    part = max(size for size in range(8, 257, 8) if tile % size == 0)
    fixed = lambda array: pl.BlockSpec(array.shape, lambda turn: (0,) * array.ndim)
    specs = dict(
        table=pl.BlockSpec((tile, width), lambda turn: (turn, 0)),
        w_in=fixed(by_name["w_in"]),
        ln=fixed(by_name["ln"]),
        qkv=pl.BlockSpec((3, strip // turns, heads_w), lambda turn: (0, turn, 0)),
        out=fixed(by_name["out"]),
        up=pl.BlockSpec((strip // turns, hidden), lambda turn: (turn, 0)),
        down=pl.BlockSpec((hidden // turns, strip), lambda turn: (turn, 0)),
    )
    inputs = {}
    for name, weight, (first, second) in zip(names, weights, moments):
        inputs[name] = (weight, specs[name])
        inputs[name + "_m"] = (first, specs[name])
        inputs[name + "_v"] = (second, specs[name])
    for name, like in (
        ("red_up", "up"),
        ("red_dn", "down"),
        ("red_qkv", "qkv"),
        ("red_out", "out"),
        ("red_in", "w_in"),
        ("red_ln", "ln"),
    ):
        inputs[name] = (grads[name], specs[like])
    for name in ("inc", "named", "totals"):
        inputs[name] = (grads[name], fixed(grads[name]))
    tokens, model = grads["out"].shape
    rows_spec = pl.BlockSpec((tokens // turns, model), lambda turn: (turn, 0))
    inputs["made"] = (grads["out"], rows_spec)
    outputs = {"out_rows": (grads["out"].shape, rows_spec)}
    for name, weight in by_name.items():
        for kind in ("_new", "_m_new", "_v_new"):
            outputs[name + kind] = (weight.shape, specs[name])
    outputs["norms"] = ((2, 12), pl.BlockSpec((2, 12), lambda turn: (0, 0)))
    results = pl.pallas_call(
        functools.partial(update_kernel, part, [*inputs, *outputs]),
        grid=(turns,),
        out_shape=[jax.ShapeDtypeStruct(shape, F32) for shape, _ in outputs.values()],
        in_specs=[spec for _, spec in inputs.values()],
        out_specs=[spec for _, spec in outputs.values()],
        compiler_params=pltpu.CompilerParams(vmem_limit_bytes=VMEM_BYTES),
        name="update",
    )(*[value for value, _ in inputs.values()])
    return list(results)


def per_device(
    token_ids,
    levels,
    noise,
    cotangent,
    table,
    table_m,
    table_v,
    w_in,
    w_in_m,
    w_in_v,
    ln_params,
    ln_m,
    ln_v,
    w_qkv,
    qkv_m,
    qkv_v,
    w_out,
    out_m,
    out_v,
    w_up,
    up_m,
    up_v,
    w_down,
    down_m,
    down_v,
):
    dp_count = lax.axis_size("dp")
    seq_count, seq_len = token_ids.shape
    tokens = seq_count * seq_len
    model = cotangent.shape[2]
    cap = round_up(max(2, (3 * tokens + 2 * dp_count - 1) // (2 * dp_count)), 16)
    weights = (table, w_in, ln_params, w_qkv, w_out, w_up, w_down)
    moments = (
        (table_m, table_v),
        (w_in_m, w_in_v),
        (ln_m, ln_v),
        (qkv_m, qkv_v),
        (out_m, out_v),
        (up_m, up_v),
        (down_m, down_v),
    )
    grads = run_layer(
        cap,
        token_ids,
        levels,
        noise.reshape(tokens, -1),
        cotangent.reshape(tokens, model),
        weights,
        moments,
    )
    out, *results = run_update(weights, moments, grads)
    return (out.reshape(seq_count, seq_len, model), *results)


def solution(mesh):
    return jax.shard_map(
        per_device,
        mesh=mesh,
        in_specs=(
            P(("dp", "mp"), None),
            P(("dp", "mp")),
            P(("dp", "mp"), None, None),
            P(("dp", "mp"), None, None),
            P("dp", None),
            P("dp", None),
            P("dp", None),
            P("dp", None),
            P("dp", None),
            P("dp", None),
            P(None, "dp"),
            P(None, "dp"),
            P(None, "dp"),
            P(None, "dp", "mp"),
            P(None, "dp", "mp"),
            P(None, "dp", "mp"),
            P("mp", "dp"),
            P("mp", "dp"),
            P("mp", "dp"),
            P("dp", "mp"),
            P("dp", "mp"),
            P("dp", "mp"),
            P("mp", "dp"),
            P("mp", "dp"),
            P("mp", "dp"),
        ),
        out_specs=(
            P(("dp", "mp"), None, None),
            P("dp", None),
            P("dp", None),
            P("dp", None),
            P("dp", None),
            P("dp", None),
            P("dp", None),
            P(None, "dp"),
            P(None, "dp"),
            P(None, "dp"),
            P(None, "dp", "mp"),
            P(None, "dp", "mp"),
            P(None, "dp", "mp"),
            P("mp", "dp"),
            P("mp", "dp"),
            P("mp", "dp"),
            P("dp", "mp"),
            P("dp", "mp"),
            P("dp", "mp"),
            P("mp", "dp"),
            P("mp", "dp"),
            P("mp", "dp"),
            P(),
        ),
        check_vma=False,
    )
```

```python
import functools
import types

import jax
import jax.numpy as jnp
from jax import lax
from jax.experimental import pallas as pl
from jax.experimental.pallas import tpu as pltpu
from jax.sharding import PartitionSpec as P

HD = 64
LEVELS = 64
STEP = 10


EPS_NORM = 1e-06
EPS_LAYER = 1e-05
EPS_ADAM = 1e-06
BETA_ONE = 0.9
BETA_TWO = 0.999
DECAY = 0.01
RATE = 0.5
SIGMA_TOP = 10.0

F32 = jnp.float32
LOW = jnp.bfloat16
VMEM_BYTES = 63 * 1024 * 1024


def sigma_of(levels):
    frac = levels.astype(jnp.float32) / (LEVELS - 1)
    return jnp.exp(frac * jnp.log(SIGMA_TOP))


def lamb_moments(weight, gradient, first, second):
    first_new = BETA_ONE * first + (1.0 - BETA_ONE) * gradient
    second_new = BETA_TWO * second + (1.0 - BETA_TWO) * gradient * gradient
    first_hat = first_new / (1.0 - BETA_ONE**STEP)
    second_hat = second_new / (1.0 - BETA_TWO**STEP)
    direction = first_hat / (jnp.sqrt(second_hat) + EPS_ADAM) + DECAY * weight
    return (first_new, second_new, direction)


def trust_factors(ratio):
    return (
        ratio[0],
        ratio[1],
        ratio[2:6][:, None],
        ratio[6:9][:, None, None],
        ratio[9],
        ratio[10],
        ratio[11],
    )


def round_up(value, step):
    return -(-value // step) * step


def dot(left, right):
    return jnp.dot(left, right, preferred_element_type=F32)


def dot_nt(left, right):
    return lax.dot_general(left, right, (((1,), (1,)), ((), ())), preferred_element_type=F32)


def dot_tn(left, right):
    return lax.dot_general(left, right, (((0,), (0,)), ((), ())), preferred_element_type=F32)


def strips(total, step, body, unroll=1):
    step = min(step, total)

    def one(turn, carry):
        body(pl.multiple_of(turn * step, step))
        return carry

    lax.fori_loop(0, total // step, one, 0, unroll=unroll)


class Line:
    def __init__(self, axis):
        self.axis = axis
        self.size = lax.axis_size(axis)
        self.far = self.size // 2
        self.me = lax.axis_index(axis)
        self.hi = lax.div(self.me, 2)
        self.lo = lax.rem(self.me, 2)
        self.partner = self.hi * 2 + (1 - self.lo)

    def at(self, step):
        return lax.rem(self.hi + step + self.far, self.far)

    def push(self, index, src, dst, send, recv):
        return pltpu.make_async_remote_copy(
            src_ref=src,
            dst_ref=dst,
            send_sem=send,
            recv_sem=recv,
            device_id={self.axis: index},
            device_id_type=pl.DeviceIdType.MESH,
        )

    def signal(self, sem, index):
        pl.semaphore_signal(
            sem, inc=1, device_id={self.axis: index}, device_id_type=pl.DeviceIdType.MESH
        )


def meet(pair_lines, all_lines=()):
    sem = pltpu.get_barrier_semaphore()
    count = 0
    for line in pair_lines:
        for step in range(1, line.far):
            line.signal(sem, line.at(step) * 2 + line.lo)
            count += 1
        line.signal(sem, line.partner)
        count += 1
    for line in all_lines:
        for step in range(1, line.size):
            line.signal(sem, lax.rem(line.me + step, line.size))
            count += 1
    pl.semaphore_wait(sem, count)


class Gather:
    def __init__(self, line, at, send, recv, base=0, ends=False):
        self.line, self.at, self.send, self.recv, self.base = line, at, send, recv, base
        self.ends = ends and line.far == 4

    def source(self, step):
        line = self.line
        if not self.ends:
            return line.at(-step)
        order = ((1, 2, 3), (0, 3, 2), (3, 0, 1), (2, 1, 0))
        hi = order[3][step - 1]
        for place in (2, 1, 0):
            hi = jnp.where(line.hi == place, order[place][step - 1], hi)
        return hi

    def far_sends(self, act):
        line = self.line
        for step in range(1, line.far):
            one = self.copy(line.me, step - 1, line.at(step) * 2 + line.lo)
            if self.ends and step != 2:
                pl.when(line.hi != (3 if step == 1 else 0))(functools.partial(act, one))
            else:
                act(one)

    def to_end(self, act):
        line = self.line
        dest = jnp.where(line.hi == 1, 0, 3)
        one = self.copy((3 - dest) * 2 + line.lo, 2 * line.far - 1, dest * 2 + line.lo)
        pl.when((line.hi == 1) | (line.hi == 2))(functools.partial(act, one))

    def copy(self, index, slot, dest):
        block = self.at(index)
        return self.line.push(
            dest, block, block, self.send.at[self.base + slot], self.recv.at[self.base + index]
        )

    def start_far(self):
        self.far_sends(lambda one: one.start())

    def start_near(self):
        self.copy(self.line.me, self.line.far - 1, self.line.partner).start()

    def start(self):
        self.start_far()
        self.start_near()

    def relay(self, step):
        line = self.line
        handed = self.copy(self.source(step) * 2 + line.lo, line.far - 1 + step, line.partner)
        handed.wait_recv()
        if self.ends and step == 2:
            self.to_end(lambda one: one.start())
        handed.start()

    def relays(self):
        for step in range(1, self.line.far):
            self.relay(step)

    def close(self):
        line = self.line
        for step in range(line.far):
            self.copy(line.at(-step) * 2 + (1 - line.lo), 0, line.partner).wait_recv()

    def drain(self):
        self.far_sends(lambda one: one.wait_send())
        if self.ends:
            self.to_end(lambda one: one.wait_send())
        for slot in range(self.line.far - 1, 2 * self.line.far - 1):
            self.copy(self.line.me, slot, self.line.partner).wait_send()


class SideGather(Gather):
    def other(self, act):
        line = self.line
        for step in range(1, line.far):
            one = self.copy(line.partner, line.far - 1 + step, line.at(step) * 2 + line.lo)
            if self.ends and step != 2:
                pl.when(line.hi != (3 if step == 1 else 0))(functools.partial(act, one))
            else:
                act(one)

    def to_ends(self, parity, slot, act):
        line = self.line
        dest = jnp.where(line.hi == 1, 0, 3)
        one = self.copy((3 - dest) * 2 + parity, slot, dest * 2 + line.lo)
        pl.when((line.hi == 1) | (line.hi == 2))(functools.partial(act, one))

    def start_other(self):
        self.copy(self.line.partner, 0, self.line.partner).wait_recv()
        self.other(lambda one: one.start())

    def taken(self, step):
        line = self.line
        for parity, slot in ((line.lo, 2 * line.far - 1), (1 - line.lo, 2 * line.far)):
            self.copy(self.source(step) * 2 + parity, 0, line.partner).wait_recv()
            if self.ends and step == 2:
                self.to_ends(parity, slot, lambda one: one.start())

    def forward(self):
        if self.line.far > 2:
            self.taken(2)

    def close(self):
        for step in range(1, self.line.far):
            if step != 2:
                self.taken(step)

    def drain(self):
        line = self.line
        self.far_sends(lambda one: one.wait_send())
        self.copy(line.me, line.far - 1, line.partner).wait_send()
        self.other(lambda one: one.wait_send())
        if self.ends:
            for parity, slot in ((line.lo, 2 * line.far - 1), (1 - line.lo, 2 * line.far)):
                self.to_ends(parity, slot, lambda one: one.wait_send())


class SideScatter:
    def __init__(self, line, part, second, first, send, recv):
        self.line, self.part, self.second, self.first = line, part, second, first
        self.send, self.recv = send, recv

    def far_copy(self, step, parity):
        line = self.line
        hi = line.at(step)
        return line.push(
            hi * 2 + line.lo,
            self.part(hi * 2 + parity),
            self.second(parity * line.far + line.hi),
            self.send.at[2 * (step - 1) + parity],
            self.recv.at[parity * line.far + line.hi],
        )

    def near_copy(self):
        line = self.line
        return line.push(
            line.partner,
            self.part(line.partner),
            self.first,
            self.send.at[2 * line.far - 2],
            self.recv.at[2 * line.far],
        )

    def start(self):
        for step in range(1, self.line.far):
            for parity in range(2):
                self.far_copy(step, parity).start()

    def sum_of(self, parity):
        line = self.line
        value = self.part(line.hi * 2 + parity)[...].astype(F32)
        for step in range(1, line.far):
            index = parity * line.far + line.at(-step)
            block = self.second(index)
            line.push(
                line.partner, block, block, self.send.at[0], self.recv.at[index]
            ).wait_recv()
            value = value + block[...].astype(F32)
        return value

    def trade(self):
        given = self.part(self.line.partner)
        given[...] = self.sum_of(1 - self.line.lo).astype(LOW)
        self.near_copy().start()

    def arrive(self):
        pass

    def total(self):
        value = self.sum_of(self.line.lo)
        self.near_copy().wait_recv()
        return value + self.first[...].astype(F32)

    def drain(self):
        for step in range(1, self.line.far):
            for parity in range(2):
                self.far_copy(step, parity).wait_send()
        self.near_copy().wait_send()


class Scatter:
    def __init__(self, line, part, first, second, send, recv, base=0, extra=None):
        self.line, self.part, self.first, self.second = line, part, first, second
        self.send, self.recv, self.base = send, recv, base
        self.extra = extra if line.far == 4 else None

    def clear(self):
        line = self.line
        if self.extra is not None:

            @pl.when((line.hi == 0) | (line.hi == 3))
            def _():
                slot = self.second(3 - line.hi)
                slot[...] = jnp.zeros(slot.shape, LOW)

    def order(self, step):
        line = self.line
        if self.extra is None:
            return line.at(step)
        table = ((3, 2, 1), (2, 0, 3), (1, 3, 0), (0, 1, 2))
        hi = table[3][step - 1]
        for place in (2, 1, 0):
            hi = jnp.where(line.hi == place, table[place][step - 1], hi)
        return hi

    def traded(self, hi):
        line = self.line
        return line.push(
            line.partner,
            self.part(hi * 2 + (1 - line.lo)),
            self.first(hi),
            self.send.at[self.base + hi],
            self.recv.at[self.base + hi],
        )

    def passed(self, step):
        line = self.line
        hi = self.order(step)
        return line.push(
            hi * 2 + line.lo,
            self.part(hi * 2 + line.lo),
            self.second(line.hi),
            self.send.at[self.base + line.far + step - 1],
            self.recv.at[self.base + line.far + line.hi],
        )

    def to_next(self):
        line = self.line
        return line.push(
            jnp.where(line.hi < 2, 1, 2) * 2 + line.lo,
            self.part((3 - jnp.where(line.hi < 2, 0, 3)) * 2 + line.lo),
            self.extra,
            self.send.at[self.base + line.far],
            self.recv.at[self.base + 2 * line.far],
        )

    def turn_of(self, turn):
        line = self.line
        if self.extra is None:
            return lax.rem(line.hi + turn + 1, line.far)
        hi = line.hi
        for step in range(1, line.far):
            hi = jnp.where(turn == step - 1, self.order(step), hi)
        return hi

    def is_end(self):
        return (self.line.hi == 0) | (self.line.hi == 3)

    def trade(self, hi):
        self.traded(hi).start()

    def trade_all(self):
        for step in range(1, self.line.far + 1):
            self.trade(self.order(step) if step < self.line.far else self.line.hi)

    def pass_on(self, step):
        line = self.line
        hi = self.order(step)
        self.traded(hi).wait_recv()
        mine, other = self.part(hi * 2 + line.lo), self.first(hi)
        if self.extra is None or step == 2:
            mine[...] = (mine[...].astype(F32) + other[...].astype(F32)).astype(LOW)
            self.passed(step).start()
        elif step == 1:
            mine[...] = (mine[...].astype(F32) + other[...].astype(F32)).astype(LOW)

            @pl.when(self.is_end())
            def _():
                self.to_next().start()

            @pl.when(jnp.logical_not(self.is_end()))
            def _():
                self.passed(step).start()
        else:

            @pl.when(self.is_end())
            def _():
                mine[...] = (mine[...].astype(F32) + other[...].astype(F32)).astype(LOW)

            @pl.when(jnp.logical_not(self.is_end()))
            def _():
                line.push(
                    line.partner,
                    self.extra,
                    self.extra,
                    self.send.at[self.base],
                    self.recv.at[self.base + 2 * line.far],
                ).wait_recv()
                mine[...] = (
                    mine[...].astype(F32) + other[...].astype(F32) + self.extra[...].astype(F32)
                ).astype(LOW)

            self.passed(step).start()

    def arrive(self):
        line = self.line
        self.traded(line.hi).wait_recv()
        for step in range(1, line.far):
            hi = line.at(-step)
            one = line.push(
                line.partner,
                self.second(hi),
                self.second(hi),
                self.send.at[self.base],
                self.recv.at[self.base + line.far + hi],
            )
            if self.extra is None:
                one.wait_recv()
            else:
                pl.when(jnp.logical_not(self.is_end()) | (hi + line.hi != 3))(one.wait_recv)

    def total(self, here):
        line = self.line
        value = self.part(line.me)[here, :].astype(F32) + self.first(line.hi)[here, :].astype(F32)
        for step in range(1, line.far):
            value = value + self.second(line.at(-step))[here, :].astype(F32)
        return value

    def drain(self):
        line = self.line
        for step in range(line.far):
            self.traded(line.at(step)).wait_send()
        for step in range(1, line.far):
            if self.extra is not None and step == 1:
                pl.when(self.is_end())(lambda: self.to_next().wait_send())
                pl.when(jnp.logical_not(self.is_end()))(lambda: self.passed(1).wait_send())
            else:
                self.passed(step).wait_send()


def block_rows(ref, rows, first=0):
    return lambda index: ref.at[pl.ds(pl.multiple_of((index + first) * rows, rows), rows)]


def part_rows(ref, rows, first, count):
    return lambda index: ref.at[pl.ds(pl.multiple_of(index * rows + first, count), count)]


def of_index(ref):
    return lambda index: ref.at[index]


def norm_rows(values):
    center = values - jnp.mean(values, -1, keepdims=True)
    spread = jnp.mean(center * center, -1, keepdims=True)
    inverse = lax.rsqrt(spread + EPS_LAYER)
    return center * inverse, inverse


def norm_back(values, gain, grad):
    unit, inverse = norm_rows(values)
    inner = grad * gain
    shared = jnp.mean(inner, -1, keepdims=True)
    along = jnp.mean(inner * unit, -1, keepdims=True)
    return inverse * (inner - shared - unit * along), unit


def head_masks(width):
    lane = lax.broadcasted_iota(jnp.int32, (1, width), 1)
    return [
        jnp.where((lane >= head * HD) & (lane < (head + 1) * HD), 1.0, 0.0)
        for head in range(width // HD)
    ]


def spread_heads(values, masks):
    return jnp.concatenate([values * mask.astype(LOW) for mask in masks], 0)


def join_heads(values, masks, rows):
    total = values[0:rows] * masks[0]
    for head in range(1, len(masks)):
        total = total + values[head * rows : (head + 1) * rows] * masks[head]
    return total


TAIL = (
    0.2256758632450557,
    0.22566952478278277,
    0.2078438574180613,
    0.16853390514724884,
    0.14146086231844687,
    -0.005667717379728321,
    0.16915486959066833,
    -0.18294364197603524,
    0.05027260226320005,
)


def normal_tail(size, bell):
    base = 1.0 + (0.4 * 0.5**0.5) * size
    t = pl.reciprocal(base, approx=True)
    t = t * (2.0 - base * t)
    t = t * (2.0 - base * t)
    value = jnp.full_like(t, 0.5 * TAIL[-1])
    for factor in TAIL[-2::-1]:
        value = value * t + 0.5 * factor
    return value * t * bell


def far_copies(line, make, sends, recvs):
    def copy(step):
        dest = lax.rem(line.me + step, line.size)
        src, dst = make(dest, line.me)
        return line.push(dest, src, dst, sends.at[step], recvs.at[line.me])

    def wait():
        for step in range(1, line.size):
            source = lax.rem(line.me + line.size - step, line.size)
            _, dst = make(source, source)
            line.push(line.partner, dst, dst, sends.at[0], recvs.at[source]).wait_recv()

    return copy, wait


def layer_kernel(cap, names, *refs):
    R = types.SimpleNamespace(**dict(zip(names, refs)))
    dp, mp = Line("dp"), Line("mp")
    size, ways = dp.size, mp.size
    seqs, seq_len = R.ids.shape
    tokens, width = R.noise.shape
    model = R.cot.shape[1]
    heads_w = R.o.shape[1]
    hidden = R.wbf.shape[1]
    table_rows = R.table.shape[0]
    rin = R.w_in.shape[0]
    rin_up = round_up(rin, 16)
    quarter = model // ways
    strip = R.w_up.shape[0]
    spots = size * cap
    far = mp.far
    count = seqs * far
    half_strip = strip // 2
    own_strip = pl.ds(pl.multiple_of(dp.me * strip, strip), strip)
    mine = pl.ds(pl.multiple_of(dp.me * cap, cap), cap)

    some_rows = seq_len // 2

    def rows_of(piece):
        return lambda row: pl.ds(pl.multiple_of(piece * seq_len + row, some_rows), some_rows)

    def own_rows(piece):
        first = pl.multiple_of((piece * ways + mp.me) * seq_len, seq_len)
        return lambda row: pl.ds(pl.multiple_of(first + row, some_rows), some_rows)

    def by_rows(body, after=lambda half: None):
        for half in range(2):
            body(half * some_rows)
            after(half)

    class Rows:
        def __init__(self, ref, send, recv, piece):
            self.parts = [
                Gather(
                    mp,
                    lambda index, half=half: ref.at[
                        pl.ds(
                            pl.multiple_of(
                                (piece * ways + index) * seq_len + half * some_rows, some_rows
                            ),
                            some_rows,
                        )
                    ],
                    send,
                    recv,
                    (2 * piece + half) * ways,
                )
                for half in range(2)
            ]

        def start(self, half):
            self.parts[half].start()

        def relays(self):
            for part in self.parts:
                part.relays()

        def close(self):
            for part in self.parts:
                part.close()

        def drain(self):
            for part in self.parts:
                part.drain()

    def halves(ref, send, recv):
        return [Rows(ref, send, recv, piece) for piece in range(seqs)]

    chunk_cols = min(256, model)
    chunk_count = model // chunk_cols

    class Sums:
        def __init__(self, *refs):
            *self.refs, self.send, self.recv = refs

        def chunk(self, piece, chunk):
            cols = pl.ds(pl.multiple_of(chunk * chunk_cols, chunk_cols), chunk_cols)

            def blocks(ref, first):
                return lambda index: ref.at[
                    pl.ds(pl.multiple_of((index + first) * seq_len, seq_len), seq_len), cols
                ]

            firsts = (piece * ways, piece * far, piece * far)
            views = [blocks(ref, first) for ref, first in zip(self.refs, firsts)]
            return Scatter(mp, *views, self.send, self.recv, (piece * chunk_count + chunk) * ways)

        def total(self, piece, here):
            firsts = (piece * ways, piece * far, piece * far)
            views = [block_rows(ref, seq_len, first) for ref, first in zip(self.refs, firsts)]
            return Scatter(mp, *views, self.send, self.recv).total(here)

        def trade(self, piece, chunk):
            self.chunk(piece, chunk).trade_all()

        def hand_on(self, piece, chunk):
            scatter = self.chunk(piece, chunk)
            for step in range(1, far):
                scatter.pass_on(step)

        def every(self, act):
            def one(chunk, carry):
                act(chunk)
                return carry

            lax.fori_loop(0, chunk_count, one, 0)

        def hand_on_all(self, piece):
            self.every(lambda chunk: self.hand_on(piece, chunk))

        def arrive(self, piece):
            self.every(lambda chunk: self.chunk(piece, chunk).arrive())

        def drain(self, piece):
            self.every(lambda chunk: self.chunk(piece, chunk).drain())

        def products(self, piece, make):
            def one(chunk, carry):
                make(pl.ds(pl.multiple_of(chunk * chunk_cols, chunk_cols), chunk_cols))
                self.trade(piece, chunk)
                pl.when(chunk > 0)(lambda: self.hand_on(piece, chunk - 1))
                return carry

            lax.fori_loop(0, chunk_count, one, 0)

        def hand_on_last(self, piece):
            self.hand_on(piece, chunk_count - 1)

    many = ways * seq_len

    def turns(body, hooks=()):
        def one(piece, carry):
            def at(point):
                for place, when, action in hooks:
                    if when == point:
                        pl.when(piece == place)(action)

            base = pl.multiple_of(piece * many, many)
            body(piece, base, pl.ds(base, many), at)
            return carry

        lax.fori_loop(0, seqs, one, 0)

    def pairs(base, body):
        def one(pair, carry):
            first = pl.multiple_of(base + pair * (2 * seq_len), 2 * seq_len)
            body([pl.ds(pl.multiple_of(first + seq * seq_len, seq_len), seq_len) for seq in range(2)])
            return carry

        lax.fori_loop(0, far, one, 0)

    def chunks(total, body):
        step = min(256, total)
        lax.fori_loop(
            0,
            total // step,
            lambda turn, carry: (body(pl.ds(pl.multiple_of(turn * step, step), step)), carry)[1],
            0,
        )

    def later_pieces(gathers, point):
        hooks = []
        for piece in range(1, seqs):
            hooks.append((piece - 1, point, gathers[piece].relays))
            hooks.append((piece, "start", gathers[piece].close))
        return hooks

    chunk = R.tab.shape[1]
    pieces = -(-table_rows // chunk)

    def fetch(piece):
        rows = min(chunk, table_rows - piece * chunk)
        return pltpu.make_async_copy(
            R.table.at[pl.ds(piece * chunk, rows)],
            R.tab.at[piece % 2, pl.ds(0, rows)],
            R.tab_sem.at[piece % 2],
        )

    for piece in range(min(2, pieces)):
        fetch(piece).start()

    names_of_moments = [
        name + kind for name in ("w_in", "ln", "qkv", "out", "up", "down") for kind in ("_m", "_v")
    ]

    def store(name):
        place = ("out", "red_up", "red_dn", "red_qkv", "inc").index(name)
        return pltpu.make_async_copy(
            getattr(R, name), getattr(R, name + "_hbm"), R.store_sem.at[place]
        )

    def moment(name):
        return pltpu.make_async_copy(
            getattr(R, name), getattr(R, name + "_here"), R.moment_sem.at[names_of_moments.index(name)]
        )

    tile_rows = R.tw.shape[1]
    tiles = table_rows // tile_rows

    shares_of = -(-tiles // ways)

    def share_tile(turn):
        return lax.min(turn * ways + mp.me, tiles - 1)

    def tile_of(turn):
        side = lax.rem(turn, 2)
        rows = pl.ds(pl.multiple_of(share_tile(turn) * tile_rows, tile_rows), tile_rows)
        return [
            pltpu.make_async_copy(source.at[rows], dest.at[side], R.tile_sem.at[2 * place + side])
            for place, (source, dest) in enumerate(
                ((R.table, R.tw), (R.table_m, R.tm), (R.table_v, R.tv))
            )
        ]

    eye = lax.broadcasted_iota(jnp.int32, (seq_len, seq_len), 0) == lax.broadcasted_iota(
        jnp.int32, (seq_len, seq_len), 1
    )
    id_rows = R.ids[...].astype(F32)
    ids = jnp.concatenate(
        [
            jnp.sum(jnp.where(eye, id_rows[seq : seq + 1, :], 0.0), 1, keepdims=True)
            for seq in range(seqs)
        ],
        0,
    )
    lane = lax.broadcasted_iota(jnp.int32, (tokens, 128), 1).astype(F32)
    low_end = lane * float(table_rows)
    owned = jnp.where((ids >= low_end) & (ids < low_end + float(table_rows)), 1.0, 0.0)
    before = jnp.where(
        lax.broadcasted_iota(jnp.int32, (tokens, tokens), 0)
        >= lax.broadcasted_iota(jnp.int32, (tokens, tokens), 1),
        1.0,
        0.0,
    )
    ranks = dot(before.astype(LOW), owned.astype(LOW))
    rank = jnp.sum(owned * ranks, 1, keepdims=True) - 1.0
    slot = jnp.sum(owned * lane, 1, keepdims=True) * cap + rank
    placed = jnp.where(lane == rank, 1.0, 0.0)
    upper = jnp.floor(ids * (1.0 / 256.0))
    lower = ids - upper * 256.0
    parts = jnp.concatenate([placed * upper, placed * lower, placed], 1).astype(LOW)
    asked = dot_tn(owned.astype(LOW), parts)
    asked = asked[:, :128] * 256.0 + asked[:, 128:256] + asked[:, 256:] - 1.0
    wide_ln = R.ln_params.shape[1]
    shares = R.ln_params[...].astype(LOW).astype(F32)
    if wide_ln < 128:
        shares = jnp.concatenate([shares, jnp.zeros((4, 128 - wide_ln), F32)], 1)
    for index in range(size):
        R.ask[index] = jnp.concatenate(
            [asked[index : index + 1, :], shares, jnp.zeros((3, 128), F32)], 0
        )
    R.idx[mp.me, dp.me] = R.ask[dp.me]

    def spread(part, first, second, extra, send, recv):
        blocks = [block_rows(ref, strip) for ref in (part, first, second)]
        return Scatter(dp, *blocks, send, recv, 0, extra)

    up = spread(R.wbf, R.up_first, R.up_second, R.up_extra, R.up_send, R.up_recv)
    down = spread(R.gdn, R.dn_first, R.dn_second, R.dn_extra, R.dn_send, R.dn_recv)
    first_w = spread(
        R.waf.at[:, : 3 * heads_w], R.wa_first, R.wa_second, R.wa_extra, R.ga_send, R.ga_recv
    )
    wo = SideScatter(
        dp,
        *[block_rows(ref, strip) for ref in (R.gwo, R.wo_second)],
        R.wo_first,
        R.wo_send,
        R.wo_recv,
    )
    for scatter in (up, down, first_w):
        scatter.clear()

    meet([mp], [dp])
    ask, ask_wait = far_copies(
        dp,
        lambda dest, source: (R.ask.at[dest], R.idx.at[mp.me, source]),
        R.ask_send,
        R.ask_recv,
    )
    for step in range(1, size):
        ask(step).start()

    mine_in = R.winf.at[mp.me]
    win = Gather(dp, block_rows(mine_in, rin), R.win_send, R.win_recv, 0, True)
    win_all = Gather(mp, of_index(R.winf), R.wim_send, R.wim_recv)
    wa = [
        Gather(dp, part_rows(R.waf, strip, piece * half_strip, half_strip), send, recv, 0, True)
        for piece, (send, recv) in enumerate(((R.wa_send, R.wa_recv), (R.wx_send, R.wx_recv)))
    ]
    wb = Gather(dp, block_rows(R.wbf, strip), R.wb_send, R.wb_recv, 0, True)
    wc = Gather(dp, part_rows(R.wcf, strip, 0, half_strip), R.wc_send, R.wc_recv, 0, True)
    wd = SideGather(dp, part_rows(R.wcf, strip, half_strip, half_strip), R.wd_send, R.wd_recv, 0, True)
    dxg = Gather(
        mp,
        lambda index: R.dx.at[:, pl.ds(pl.multiple_of(index * seq_len, seq_len), seq_len)],
        R.dx_send,
        R.dx_recv,
    )
    ag = halves(R.a, R.a_send, R.a_recv)
    cg = halves(R.c, R.c_send, R.c_recv)
    mg = halves(R.dmid_all, R.e_send, R.e_recv)

    mine_in[pl.ds(pl.multiple_of(dp.me * rin, rin), rin), :] = (
        R.w_in[:, pl.ds(pl.multiple_of(mp.me * quarter, quarter), quarter)]
        .astype(LOW)
        .astype(R.winf.dtype)
    )
    win.start()
    for part in range(3):
        R.waf[own_strip, part * heads_w : (part + 1) * heads_w] = R.w_qkv[part].astype(LOW)
    R.waf[own_strip, 3 * heads_w :] = R.w_out[...].T.astype(LOW)
    wa[0].start()
    wa[1].start_near()

    ask_wait()
    small_eye = lax.broadcasted_iota(jnp.int32, (cap, 128), 0) == lax.broadcasted_iota(
        jnp.int32, (cap, 128), 1
    )

    def locate(index, carry):
        row = R.idx[mp.me, index][0:1, :]
        column = jnp.sum(jnp.where(small_eye, row, 0.0), 1, keepdims=True)
        local = column.astype(jnp.int32) - dp.me * table_rows
        R.loc[pl.ds(pl.multiple_of(index * cap, cap), cap), :] = jnp.broadcast_to(local, (cap, 128))
        return carry

    lax.fori_loop(0, size, locate, 0, unroll=True)
    win.relays()
    found = None
    for piece in range(pieces):
        fetch(piece).wait()
        rows = min(chunk, table_rows - piece * chunk)
        if rows < chunk:
            R.tab[piece % 2, rows:, :] = jnp.zeros((chunk - rows, width), F32)
        hit = (
            lax.broadcasted_iota(jnp.int32, (spots, chunk), 1) + piece * chunk == R.loc[:, 0:1]
        )
        more = dot(jnp.where(hit, 1.0, 0.0).astype(LOW), R.tab[piece % 2].astype(LOW))
        found = more if found is None else found + more
        if piece + 2 < pieces:
            fetch(piece + 2).start()
    R.give[...] = found.astype(LOW)

    give, give_wait = far_copies(
        dp,
        lambda dest, source: (block_rows(R.give, cap)(dest), block_rows(R.got, cap)(source)),
        R.give_send,
        R.give_recv,
    )
    for step in range(1, size):
        give(step).start()
    R.got[mine, :] = R.give[mine, :]
    wa[1].start_far()
    named = Gather(mp, of_index(R.idx), R.id_send, R.id_recv)
    named.start()
    for name in names_of_moments:
        moment(name).start()
    win.close()
    win_all.start()
    wa[0].relay(1)
    for seq in range(seqs):
        level = jnp.full((seq_len, 1), R.levels[seq], jnp.int32).astype(F32) / (LEVELS - 1)
        R.sig[seq * seq_len : (seq + 1) * seq_len, :] = jnp.exp(level * jnp.log(SIGMA_TOP))

    def scale_at(here):
        sig = R.sig[here, :]
        return sig * lax.rsqrt(1.0 + sig * sig)

    for piece in range(seqs):
        here = rows_of(piece)

        def scale_cot(row, here=here, piece=piece):
            there = pl.ds(pl.multiple_of(mp.me * seq_len + row, some_rows), some_rows)
            R.dx[piece, there, :] = (R.cot[here(row), :].astype(F32) * scale_at(here(row))).astype(LOW)

        by_rows(scale_cot)
    dxg.start()
    R.wbf[own_strip, :] = R.w_up[...].astype(LOW)
    R.wcf[own_strip, :] = R.w_down[...].T.astype(LOW)
    wb.start_near()
    R.pick[...] = jnp.where(
        lax.broadcasted_iota(jnp.int32, (tokens, spots), 1).astype(F32) == slot, 1.0, 0.0
    ).astype(LOW)
    win_all.relays()
    named.relays()
    wa[0].relay(2)
    if wide_ln % 128 == 0:
        R.gains[...] = jnp.concatenate([R.idx[mp.me, index] for index in range(size)], 1)
    else:
        total = jnp.zeros((8, model), F32)
        for index in range(size):
            place = lax.broadcasted_iota(
                jnp.int32, (128, model), 1
            ) == index * wide_ln + lax.broadcasted_iota(jnp.int32, (128, model), 0)
            place = place & (lax.broadcasted_iota(jnp.int32, (128, model), 0) < wide_ln)
            total = total + dot(
                R.idx[mp.me, index].astype(LOW), jnp.where(place, 1.0, 0.0).astype(LOW)
            )
        R.gains[...] = total
    for step in range(3, dp.far):
        wa[0].relay(step)

    give_wait()
    rows = dot(R.pick[...], R.got[...])
    R.rows[...] = rows.astype(LOW)
    sig = R.sig[...]
    unit = rows * lax.rsqrt(jnp.mean(rows * rows, -1, keepdims=True) + EPS_NORM)
    R.mixed[...] = ((unit + sig * R.noise[...].astype(F32)) * lax.rsqrt(1.0 + sig * sig)).astype(LOW)
    win_all.close()
    for index in range(ways):
        R.x0[:, index * quarter : (index + 1) * quarter] = dot(
            R.mixed[...], R.winf[index].astype(LOW)
        )

    for piece in range(seqs):
        here, there = rows_of(piece), own_rows(piece)

        def first_norm(row, here=here, there=there):
            normed, _ = norm_rows(R.x0[here(row), :])
            R.a[there(row), :] = (normed * R.gains[1:2, :] + R.gains[2:3, :]).astype(LOW)

        by_rows(first_norm, ag[piece].start)
    wa[1].relays()
    wb.start_far()
    dxg.relays()
    ag[0].relays()
    for gather in (*wa, ag[0]):
        gather.close()

    att = Sums(R.part, R.fold, R.fold_far, R.as_send, R.as_recv)
    dcs = Sums(R.part, R.fold, R.fold_far, R.cs_send, R.cs_recv)
    das = Sums(R.part, R.fold, R.fold_far, R.ds_send, R.ds_recv)
    out = Sums(R.c, R.first, R.second, R.os_send, R.os_recv)
    masks = head_masks(heads_w)

    all_rows = (heads_w // HD) * seq_len
    scale = HD ** (-0.5)

    def softmax(seq, row):
        scores = R.scores[seq, row : row + 64, :]
        raised = jnp.exp((scores - jnp.max(scores, -1, keepdims=True)) * scale)
        return raised * (1.0 / jnp.sum(raised, -1, keepdims=True))

    def attend(piece, base, here, at):
        at("start")
        for part in range(3):
            cols = slice(part * heads_w, (part + 1) * heads_w)
            R.qkv[here, cols] = dot(R.a[here, :], R.waf[:, cols]).astype(LOW)
        at("mid")

        def one(rows_at):
            for seq, rows in enumerate(rows_at):
                queries = spread_heads(R.qkv[rows, :heads_w], masks)
                R.scores[seq] = dot_nt(queries, R.qkv[rows, heads_w : 2 * heads_w])
            for seq, rows in enumerate(rows_at):
                for row in range(0, all_rows, 64):
                    R.probs[seq, row : row + 64, :] = softmax(seq, row).astype(LOW)
                seen = dot(R.probs[seq], R.qkv[rows, 2 * heads_w : 3 * heads_w])
                R.o[rows, :] = join_heads(seen, masks, seq_len).astype(LOW)

        pairs(base, one)
        at("late")

        def project(cols):
            R.part[here, cols] = dot_nt(R.o[here, :], R.waf[cols, 3 * heads_w :]).astype(LOW)

        def one_chunk(chunk, carry):
            project(pl.ds(pl.multiple_of(chunk * chunk_cols, chunk_cols), chunk_cols))
            att.trade(piece, chunk)
            return carry

        lax.fori_loop(0, chunk_count, one_chunk, 0)

    def second_norm(piece):
        here, there = rows_of(piece), own_rows(piece)
        att.arrive(piece)

        def norm(row):
            x1 = R.x0[here(row), :] + att.total(piece, pl.ds(row, some_rows))
            R.out[here(row), :] = x1
            normed, _ = norm_rows(x1)
            R.c[there(row), :] = (normed * R.gains[3:4, :] + R.gains[4:5, :]).astype(LOW)

        by_rows(norm, cg[piece].start)

    def first_wb():
        wb.relay(1)
        wd.start_near()
        wc.start_near()
        wc.start_far()

    def middle_wb():
        wb.relay(2)
        wd.start_far()

    def last_wb():
        wd.start_other()
        for step in range(3, dp.far):
            wb.relay(step)

    turns(
        attend,
        [
            *later_pieces(ag, "mid"),
            *[
                (piece + 1, "mid", functools.partial(att.hand_on_all, piece))
                for piece in range(seqs - 1)
            ],
            (0, "mid", first_wb),
            (0, "late", middle_wb),
            (1, "mid", last_wb),
            *[
                (piece + 1, "late", functools.partial(second_norm, piece))
                for piece in range(seqs - 1)
            ],
        ],
    )
    att.hand_on_all(seqs - 1)
    wc.relay(1)
    for gather in (*wa, *ag, dxg, win):
        gather.drain()
    for step in range(1, size):
        ask(step).wait_send()
    second_norm(seqs - 1)
    cg[0].relays()
    wc.relay(2)
    wb.close()
    cg[0].close()
    for piece in range(seqs):
        att.drain(piece)

    def activate(piece, base, here, at):
        at("start")

        def some(cols):
            R.h[...] = dot(R.c[here, :], R.wbf[:, cols])

            def gelu(row):
                there = pl.ds(pl.multiple_of(base + row, 64), 64)
                h = R.h[pl.ds(row, 64), :]
                bell = jnp.exp(-0.5 * h * h)
                tail = normal_tail(jnp.abs(h), bell)
                gate = jnp.where(h >= 0.0, 1.0 - tail, tail)
                slope = gate + h * (bell * 0.3989422804014327)
                R.hb[there, cols] = (h * gate).astype(LOW)
                R.slope[there, cols] = slope.astype(LOW)

            strips(many, 64, gelu, 2)

        chunks(hidden, some)
        at("end")

    def last_wc():
        for step in range(3, dp.far):
            wc.relay(step)

    turns(activate, [*later_pieces(cg, "end"), (0, "end", last_wc), (seqs - 1, "start", wd.forward)])

    due = [(scatter, step) for scatter in (down, up) for step in range(1, dp.far)]

    def pass_due(number):
        for _ in range(min(number, len(due))):
            scatter, step = due.pop(0)
            scatter.pass_on(step)

    block = 2 * strip if (2 * strip) % 128 == 0 else min(256, model)

    def grads(make, trades):
        if block == 2 * strip:

            def turn_of(turn, carry):
                hi = up.turn_of(turn)
                make(pl.ds(pl.multiple_of(hi * block, block), block))
                for scatter in trades:
                    scatter.trade(hi)
                return carry

            lax.fori_loop(0, dp.far, turn_of, 0)
        else:
            strips(model, block, lambda col: make(pl.ds(col, block)))
            for scatter in trades:
                scatter.trade_all()

    def down_grads(cols):
        every = R.dx[:, :, cols]
        R.gdn[cols, :] = dot_tn(every.reshape(seqs * many, block), R.hb[...]).astype(LOW)

    def up_grads(cols):
        R.wbf[cols, :] = dot_tn(R.c[:, cols], R.dhb[...]).astype(LOW)

    dxg.close()
    grads(down_grads, (down,))
    named.close()
    groups = ways * size
    some, lanes_at = min(groups, 32), min(ways * spots, 512)
    for begin in range(0, ways * spots, lanes_at):
        spot = lax.broadcasted_iota(jnp.int32, (128, lanes_at), 1).astype(F32) + float(begin)
        block_no = jnp.floor((spot + 0.5) * (1.0 / cap))
        place = lax.broadcasted_iota(jnp.int32, (128, lanes_at), 0).astype(F32)
        spread_out = jnp.where(spot - block_no * cap == place, 1.0, 0.0).astype(LOW)
        named_row = jnp.zeros((1, lanes_at), F32)
        for first in range(0, groups, some):
            wanted = jnp.concatenate(
                [
                    R.idx[index // size, index % size][0:1, :] + 1.0
                    for index in range(first, first + some)
                ],
                0,
            )
            high = jnp.floor(wanted * (1.0 / 256.0))
            rest = wanted - 256.0 * high
            laid = dot(high.astype(LOW), spread_out) * 256.0 + dot(rest.astype(LOW), spread_out) - 1.0
            own_block = block_no[0:1, :] == float(first) + lax.broadcasted_iota(
                jnp.int32, (some, lanes_at), 0
            ).astype(F32)
            named_row = named_row + jnp.sum(jnp.where(own_block, laid, 0.0), 0, keepdims=True)
        R.named[:, begin : begin + lanes_at] = jnp.broadcast_to(
            named_row.astype(jnp.int32) - dp.me * table_rows, (8, lanes_at)
        )
    wc.close()
    wd.close()
    for gather in (wb, *cg):
        gather.drain()

    def feed_back(piece, base, here, at):
        at("start")

        def some(cols):
            bent = dot(R.dx[piece], R.wcf[:, cols]) * R.slope[here, cols].astype(F32)
            R.dhb[here, cols] = bent.astype(LOW)

        chunks(hidden, some)
        at("mid")

        def project(cols):
            R.part[here, cols] = dot_nt(R.dhb[here, :], R.wbf[cols, :]).astype(LOW)

        dcs.products(piece, project)

    R.norms[...] = jnp.zeros_like(R.norms)

    def second_back(piece):
        here, there = rows_of(piece), own_rows(piece)
        dcs.arrive(piece)

        def back(row):
            dc = dcs.total(piece, pl.ds(row, some_rows))
            grad, unit = norm_back(R.out[here(row), :], R.gains[3:4, :], dc)
            grad = grad + R.cot[here(row), :].astype(F32) * scale_at(here(row))
            R.dmid[here(row), :] = grad
            R.dmid_all[there(row), :] = grad.astype(LOW)
            R.norms[2:3, :] += jnp.sum(dc * unit, 0, keepdims=True)
            R.norms[3:4, :] += jnp.sum(dc, 0, keepdims=True)

        by_rows(back, mg[piece].start)

    turns(
        feed_back,
        [
            *[
                (piece + 1, "mid", functools.partial(dcs.hand_on_last, piece))
                for piece in range(seqs - 1)
            ],
            (1, "mid", lambda: pass_due(1)),
        ],
    )
    dcs.hand_on_last(seqs - 1)
    second_back(0)
    pass_due(1)
    grads(up_grads, (up,))
    for piece in range(1, seqs):
        second_back(piece)
    pass_due(max(1, dp.far - 3))
    mg[0].relays()
    mg[0].close()
    for piece in range(seqs):
        dcs.drain(piece)

    def attend_back(piece, base, here, at):
        at("start")
        R.low[...] = dot(R.dmid_all[here, :], R.waf[:, 3 * heads_w :]).astype(LOW)
        at("mid")

        def one(rows_at):
            for seq, rows in enumerate(rows_at):
                queries = spread_heads(R.qkv[rows, :heads_w], masks)
                R.scores[seq] = dot_nt(queries, R.qkv[rows, heads_w : 2 * heads_w])
                upper_rows = pl.ds(pl.multiple_of(rows.start - base, seq_len), seq_len)
                R.upper[seq] = spread_heads(R.low[upper_rows, :], masks)
                R.dprobs[seq] = dot_nt(R.upper[seq], R.qkv[rows, 2 * heads_w : 3 * heads_w])
            for seq, rows in enumerate(rows_at):
                for row in range(0, all_rows, 64):
                    probs = softmax(seq, row)
                    grad_probs = R.dprobs[seq, row : row + 64, :]
                    inner = jnp.sum(probs * grad_probs, -1, keepdims=True)
                    R.probs[seq, row : row + 64, :] = probs.astype(LOW)
                    R.dscores[seq, row : row + 64, :] = (probs * (grad_probs - inner)).astype(LOW)
                keys = R.qkv[rows, heads_w : 2 * heads_w]
                queries = spread_heads(R.qkv[rows, :heads_w], masks)
                R.qkv[rows, 2 * heads_w : 3 * heads_w] = dot_tn(R.probs[seq], R.upper[seq]).astype(LOW)
                R.qkv[rows, heads_w : 2 * heads_w] = (dot_tn(R.dscores[seq], queries) * scale).astype(
                    LOW
                )
                R.qkv[rows, :heads_w] = (
                    join_heads(dot(R.dscores[seq], keys), masks, seq_len) * scale
                ).astype(LOW)

        pairs(base, one)
        at("late")

        def project(cols):
            R.part[here, cols] = dot_nt(R.qkv[here, :], R.waf[cols, : 3 * heads_w]).astype(LOW)

        das.products(piece, project)

    def first_back(piece):
        here = rows_of(piece)
        das.arrive(piece)

        def back(row):
            da = das.total(piece, pl.ds(row, some_rows))
            grad, unit = norm_back(R.x0[here(row), :], R.gains[1:2, :], da)
            R.dx0[here(row), :] = (R.dmid[here(row), :] + grad).astype(LOW)
            R.norms[0:1, :] += jnp.sum(da * unit, 0, keepdims=True)
            R.norms[1:2, :] += jnp.sum(da, 0, keepdims=True)

        by_rows(back)

    def out_grads():
        def make(cols):
            R.gwo[cols, :] = dot_tn(R.dmid_all[:, cols], R.o[...]).astype(LOW)

        grads(make, (wo,))

    turns(
        attend_back,
        [
            *later_pieces(mg, "mid"),
            (0, "late", lambda: pass_due(1)),
            *[
                (piece + 1, "mid", functools.partial(das.hand_on_last, piece))
                for piece in range(seqs - 1)
            ],
            (seqs - 1, "late", lambda: pass_due(1)),
        ],
    )
    das.hand_on_last(seqs - 1)
    def out_grads(cols):
        R.gwo[cols, :] = dot_tn(R.dmid_all[:, cols], R.o[...]).astype(LOW)

    def attend_grads(cols):
        R.waf[cols, : 3 * heads_w] = dot_tn(R.a[:, cols], R.qkv[...]).astype(LOW)

    first_back(0)
    pass_due(len(due))
    grads(attend_grads, (first_w,))
    grads(out_grads, ())
    wo.start()
    for piece in range(1, seqs):
        first_back(piece)

    grad_mixed = sum(
        dot_nt(R.dx0[:, index * quarter : (index + 1) * quarter], R.winf[index].astype(LOW))
        for index in range(ways)
    )
    sig = R.sig[...]
    grad_unit = grad_mixed * lax.rsqrt(1.0 + sig * sig)
    rows = R.rows[...].astype(F32)
    inverse = lax.rsqrt(jnp.mean(rows * rows, -1, keepdims=True) + EPS_NORM)
    unit = rows * inverse
    grad_rows = inverse * (grad_unit - unit * jnp.mean(grad_unit * unit, -1, keepdims=True))
    for step in range(1, size):
        give(step).wait_send()
    R.give[...] = dot_tn(R.pick[...], grad_rows.astype(LOW)).astype(LOW)
    mine_inc = block_rows(R.inc, spots)(mp.me)
    back, back_wait = far_copies(
        dp,
        lambda dest, source: (block_rows(R.give, cap)(dest), block_rows(mine_inc, cap)(source)),
        R.back_send,
        R.back_recv,
    )
    for step in range(1, size):
        back(step).start()
    mine_inc[mine, :] = R.give[mine, :]

    small_mp = Scatter(
        mp, of_index(R.gm), of_index(R.gm_first), of_index(R.gm_second), R.gm_send, R.gm_recv
    )
    for index in range(ways):
        cols = slice(index * quarter, (index + 1) * quarter)
        R.gm[index, :width, :] = dot_tn(R.mixed[...], R.dx0[:, cols]).astype(LOW)
        R.gm[index, width:, :] = jnp.concatenate(
            [R.norms[0:4, cols], jnp.zeros((12, quarter), F32)], 0
        ).astype(LOW)
    small_mp.trade_all()
    for step in range(1, far):
        small_mp.pass_on(step)

    first_w.pass_on(1)

    def feed_out(piece, base, here, at):
        def project(cols):
            R.c[here, cols] = dot_nt(R.hb[here, :], R.wcf[cols, :]).astype(LOW)

        out.products(piece, project)

    turns(feed_out)
    wo.trade()
    first_w.pass_on(2)
    for turn in range(min(2, shares_of)):
        for one in tile_of(turn):
            one.start()
    back_wait()
    rows_in = Gather(mp, block_rows(R.inc, spots), R.in_send, R.in_recv)
    rows_in.start()
    for piece in range(seqs):
        out.hand_on_last(piece)

    small_mp.arrive()
    summed = small_mp.total(slice(None))
    for index in range(size):
        piece = summed[index * rin : (index + 1) * rin, :]
        if rin_up > rin:
            piece = jnp.concatenate([piece, jnp.zeros((rin_up - rin, quarter), F32)], 0)
        R.gw[index, :rin_up, :] = piece.astype(LOW)
        R.gw[index, rin_up:, :] = summed[width:, :].astype(LOW)
    R.gw_in[dp.me] = R.gw[dp.me]
    small, small_wait = far_copies(
        dp, lambda dest, source: (R.gw.at[dest], R.gw_in.at[source]), R.gw_send, R.gw_recv
    )
    for step in range(1, size):
        small(step).start()
    rows_in.relays()
    for step in range(3, dp.far):
        first_w.pass_on(step)

    def finish_out(piece):
        here = rows_of(piece)
        out.arrive(piece)

        def finish(row):
            R.out[here(row), :] = (
                R.out[here(row), :] + out.total(piece, pl.ds(row, some_rows))
            ) * scale_at(here(row))

        by_rows(finish)

    for piece in range(seqs):
        finish_out(piece)
    store("out").start()

    rows_in.close()
    store("inc").start()

    once = jnp.where(mp.me == 0, 1.0, 0.0)
    lanes = lax.broadcasted_iota(jnp.int32, (1, 128), 1)
    R.sums[...] = jnp.zeros_like(R.sums)

    def put(place, squares, factor=None):
        for row, values in enumerate(squares):
            total = jnp.sum(jnp.sum(values, 0, keepdims=True), 1, keepdims=True)
            if factor is not None:
                total = total * factor
            R.sums[row : row + 1, :] += jnp.where(lanes == place, total, 0.0)

    def squares_of(weight, gradient, first, second):
        direction = direction_of(weight, gradient, first, second)[2]
        return weight * weight, direction * direction

    def folded(values):
        rows, columns = values.shape
        return jnp.sum(values.reshape(rows // 8, 8, columns), 0)

    def add_up(weight, gradient, first, second):
        squares = squares_of(weight[...], gradient[...], first[...], second[...])
        return [folded(values) for values in squares]

    zero = jnp.zeros((8, width), F32)

    def add_tile(turn, carry):
        side = lax.rem(turn, 2)
        for one in tile_of(turn):
            one.wait()
        hit = (
            lax.broadcasted_iota(jnp.int32, (tile_rows, ways * spots), 0)
            + share_tile(turn) * tile_rows
            == R.named[0:1, :]
        )
        gradient = dot(jnp.where(hit, 1.0, 0.0).astype(LOW), R.inc[...])
        more = add_up(R.tw.at[side], gradient, R.tm.at[side], R.tv.at[side])
        counts = jnp.where(turn * ways + mp.me < tiles, 1.0, 0.0)

        @pl.when(turn + 2 < shares_of)
        def _():
            for one in tile_of(turn + 2):
                one.start()

        return carry[0] + counts * more[0], carry[1] + counts * more[1]

    put(0, lax.fori_loop(0, shares_of, add_tile, (zero, zero)))

    for thing in (win_all, wc, wd, *mg, up, down, small_mp, named):
        thing.drain()
    for piece in range(seqs):
        out.drain(piece)
        das.drain(piece)
    for step in range(1, size):
        back(step).wait_send()

    for name in names_of_moments:
        moment(name).wait()
    up.arrive()

    R.red_up[...] = up.total(slice(None))
    store("red_up").start()
    put(10, add_up(R.w_up, R.red_up, R.up_m_here, R.up_v_here))
    down.arrive()

    R.red_dn[...] = down.total(slice(None)).T
    store("red_dn").start()
    put(11, add_up(R.w_down, R.red_dn, R.down_m_here, R.down_v_here))
    wo.arrive()
    R.red_out[...] = wo.total().T
    put(9, add_up(R.w_out, R.red_out, R.out_m_here, R.out_v_here))

    small_wait()
    R.wsum[mp.me] = jnp.sum(R.gw_in[...].astype(F32), 0).astype(LOW)
    weights_in = Gather(mp, of_index(R.wsum), R.ws_send, R.ws_recv)
    weights_in.start()
    first_w.arrive()

    value = first_w.total(slice(None))
    for part in range(3):
        R.red_qkv[part] = value[:, part * heads_w : (part + 1) * heads_w]
    store("red_qkv").start()
    weights_in.relays()
    for part in range(3):
        put(
            6 + part,
            add_up(
                R.w_qkv.at[part], R.red_qkv.at[part], R.qkv_m_here.at[part], R.qkv_v_here.at[part]
            ),
        )
    weights_in.close()
    total = jnp.concatenate([R.wsum[index].astype(F32) for index in range(ways)], 1)
    R.red_in[...] = total[:rin, :]
    put(1, add_up(R.w_in, R.red_in, R.w_in_m_here, R.w_in_v_here), once)
    if strip % 128 == 0:
        R.lnsum[...] = total[rin_up : rin_up + 8, :]
        R.red_ln[...] = R.lnsum[0:4, pl.ds(pl.multiple_of(dp.me * strip, strip), strip)]
    else:
        chosen = lax.broadcasted_iota(jnp.int32, (model, strip), 0) == dp.me * strip + (
            lax.broadcasted_iota(jnp.int32, (model, strip), 1)
        )
        R.red_ln[...] = dot(
            total[rin_up : rin_up + 8, :].astype(LOW), jnp.where(chosen, 1.0, 0.0).astype(LOW)
        )[0:4]
    squares = squares_of(R.ln_params[...], R.red_ln[...], R.ln_m_here[...], R.ln_v_here[...])
    for row in range(4):
        put(2 + row, [values[row : row + 1, :] for values in squares], once)

    R.near[dp.me] = R.sums[...]
    near, near_wait = far_copies(
        dp, lambda dest, source: (R.near.at[dp.me], R.near.at[source]), R.near_send, R.near_recv
    )
    for step in range(1, size):
        near(step).start()
    near_wait()
    R.wide[mp.me] = jnp.sum(R.near[...], 0)
    far_off, far_off_wait = far_copies(
        mp, lambda dest, source: (R.wide.at[mp.me], R.wide.at[source]), R.wide_send, R.wide_recv
    )
    for step in range(1, ways):
        far_off(step).start()
    far_off_wait()
    R.totals[...] = jnp.sum(R.wide[...], 0)

    for thing in (wo, first_w, rows_in, weights_in):
        thing.drain()
    for step in range(1, size):
        near(step).wait_send()
        small(step).wait_send()
    for step in range(1, ways):
        far_off(step).wait_send()
    for name in ("out", "red_up", "red_dn", "red_qkv", "inc"):
        store(name).wait()


def run_layer(cap, ids, levels, noise, cot, weights, moments):
    table, w_in, ln_params, w_qkv, w_out, w_up, w_down = weights
    dp, mp = lax.axis_size("dp"), lax.axis_size("mp")
    seqs, seq_len = ids.shape
    tokens, width = noise.shape
    model = cot.shape[1]
    rin = w_in.shape[0]
    heads_w = w_qkv.shape[2]
    strip, hidden = w_up.shape
    group = tokens * mp
    spots = dp * cap
    wide = round_up(rin, 16) + 16
    far, far_dp = mp // 2, dp // 2
    quarter = model // mp
    in_kind = LOW if rin % 16 == 0 else F32
    tile_rows = max(rows for rows in range(8, 257, 8) if table.shape[0] % rows == 0)
    stacked = (heads_w // HD) * seq_len
    vmem = pl.BlockSpec(memory_space=pltpu.VMEM)
    outside = pl.BlockSpec(memory_space=pl.ANY)
    inputs = dict(
        ids=(ids, vmem),
        levels=(levels, pl.BlockSpec(memory_space=pltpu.SMEM)),
        noise=(noise, vmem),
        cot=(cot, vmem),
        table=(table, outside),
        w_in=(w_in, vmem),
        ln_params=(ln_params, vmem),
        w_qkv=(w_qkv, vmem),
        w_out=(w_out, vmem),
        w_up=(w_up, vmem),
        w_down=(w_down, vmem),
    )
    kept = {}
    for name, (first, second) in zip(("table", "w_in", "ln", "qkv", "out", "up", "down"), moments):
        inputs[name + "_m"] = (first, outside)
        inputs[name + "_v"] = (second, outside)
        if name != "table":
            kept[name + "_m_here"] = kept[name + "_v_here"] = (first.shape, F32)
    own_stores = dict(
        out=((tokens, model), F32),
        red_up=((strip, hidden), F32),
        red_dn=((hidden, strip), F32),
        red_qkv=((3, strip, heads_w), F32),
        inc=((mp * spots, width), LOW),
    )
    outputs = dict(
        **{name + "_hbm": shape for name, shape in own_stores.items()},
        red_out=((heads_w, strip), F32),
        red_in=((rin, model), F32),
        red_ln=((4, strip), F32),
        named=((8, mp * spots), jnp.int32),
        totals=((8, 128), F32),
    )
    buffers = dict(
        tab=((2, round_up(table.shape[0] // 8, 128), width), F32),
        ask=((dp, 8, 128), F32),
        idx=((mp, dp, 8, 128), F32),
        loc=((spots, 128), jnp.int32),
        give=((spots, width), LOW),
        got=((spots, width), LOW),
        tw=((2, tile_rows, width), F32),
        tm=((2, tile_rows, width), F32),
        tv=((2, tile_rows, width), F32),
        sums=((8, 128), F32),
        near=((dp, 8, 128), F32),
        wide=((mp, 8, 128), F32),
        scores=((2, stacked, seq_len), F32),
        dprobs=((2, stacked, seq_len), F32),
        probs=((2, stacked, seq_len), LOW),
        dscores=((2, stacked, seq_len), LOW),
        upper=((2, stacked, heads_w), LOW),
        gwo=((model, heads_w), LOW),
        wo_first=((strip, heads_w), LOW),
        wo_second=((dp * strip, heads_w), LOW),
        gains=((8, model), F32),
        lnsum=((8, model), F32),
        sig=((tokens, 1), F32),
        pick=((tokens, spots), LOW),
        rows=((tokens, width), LOW),
        mixed=((tokens, width), LOW),
        x0=((tokens, model), F32),
        a=((group, model), LOW),
        c=((group, model), LOW),
        dx=((seqs, group // seqs, model), LOW),
        dmid=((tokens, model), F32),
        dmid_all=((group, model), LOW),
        winf=((mp, rin * dp, quarter), in_kind),
        waf=((model, 4 * heads_w), LOW),
        wbf=((model, hidden), LOW),
        wcf=((model, hidden), LOW),
        qkv=((group, 3 * heads_w), LOW),
        o=((group, heads_w), LOW),
        low=((group // seqs, heads_w), LOW),
        part=((group, model), LOW),
        first=((far * tokens, model), LOW),
        fold=((far * tokens, model), LOW),
        second=((far * tokens, model), LOW),
        fold_far=((far * tokens, model), LOW),
        h=((group // seqs, min(256, hidden)), F32),
        hb=((group, hidden), LOW),
        dhb=((group, hidden), LOW),
        slope=((group, hidden), LOW),
        gdn=((model, hidden), LOW),
        dx0=((tokens, model), LOW),
        norms=((8, model), F32),
        gm=((mp, width + 16, quarter), LOW),
        gm_first=((far, width + 16, quarter), LOW),
        gm_second=((far, width + 16, quarter), LOW),
        gw=((dp, wide, quarter), LOW),
        gw_in=((dp, wide, quarter), LOW),
        up_first=((far_dp * strip, hidden), LOW),
        up_second=((far_dp * strip, hidden), LOW),
        dn_first=((far_dp * strip, hidden), LOW),
        dn_second=((far_dp * strip, hidden), LOW),
        wa_first=((far_dp * strip, 3 * heads_w), LOW),
        wa_second=((far_dp * strip, 3 * heads_w), LOW),
        wsum=((mp, wide, quarter), LOW),
        up_extra=((strip, hidden), LOW),
        dn_extra=((strip, hidden), LOW),
        wa_extra=((strip, 3 * heads_w), LOW),
        **kept,
        **own_stores,
    )
    sems = dict(store_sem=5, tab_sem=2, tile_sem=6, moment_sem=12)
    for name in (
        *("win", "wa", "wx", "wb", "wc", "wd", "ask", "give", "back"),
        *("up", "dn", "ga", "wo", "gw", "near"),
    ):
        sems[name + "_send"] = sems[name + "_recv"] = dp + 1
    for name in ("wim", "id", "in", "ws", "gm", "wide"):
        sems[name + "_send"] = sems[name + "_recv"] = mp
    for name in ("dx", "a", "c", "e"):
        sems[name + "_send"] = sems[name + "_recv"] = 2 * seqs * mp
    for name in ("as", "os", "cs", "ds"):
        sems[name + "_send"] = sems[name + "_recv"] = seqs * mp * (model // min(256, model))
    names = [*inputs, *outputs, *buffers, *sems]
    made = pl.pallas_call(
        functools.partial(layer_kernel, cap, names),
        out_shape=[jax.ShapeDtypeStruct(shape, kind) for shape, kind in outputs.values()],
        in_specs=[spec for _, spec in inputs.values()],
        out_specs=[outside if name.endswith("_hbm") else vmem for name in outputs],
        scratch_shapes=[
            *[pltpu.VMEM(shape, kind) for shape, kind in buffers.values()],
            *[pltpu.SemaphoreType.DMA((number,)) for number in sems.values()],
        ],
        compiler_params=pltpu.CompilerParams(
            vmem_limit_bytes=VMEM_BYTES, collective_id=1, has_side_effects=True
        ),
        name="layer",
    )(*[value for value, _ in inputs.values()])
    return {name.removesuffix("_hbm"): value for name, value in zip(outputs, made)}


def direction_of(weight, gradient, first, second):
    first_new = BETA_ONE * first + (1.0 - BETA_ONE) * gradient
    second_new = BETA_TWO * second + (1.0 - BETA_TWO) * gradient * gradient
    second_hat = second_new * (1.0 / (1.0 - BETA_TWO**STEP))
    inverse = lax.rsqrt(second_hat)
    root = second_hat * inverse + EPS_ADAM
    inverse = inverse * (2.0 - root * inverse)
    inverse = inverse * (2.0 - root * inverse)
    direction = first_new * (1.0 / (1.0 - BETA_ONE**STEP)) * inverse + DECAY * weight
    return first_new, second_new, direction


def update_kernel(part, names, *refs):
    R = types.SimpleNamespace(**dict(zip(names, refs)))
    turn = pl.program_id(0)
    R.out_rows[...] = R.made[...]
    norms = jnp.sqrt(R.totals[...])
    R.norms[...] = norms[0:2, 0:12]
    factors = norms[0:1, :] / (norms[1:2, :] + EPS_ADAM) * RATE

    def piece(name, here, gradient, place, rows=slice(None)):
        weight = getattr(R, name)[here]
        first_new, second_new, direction = direction_of(
            weight, gradient, getattr(R, name + "_m")[here], getattr(R, name + "_v")[here]
        )
        if isinstance(place, int):
            factor = factors[0:1, place : place + 1]
        else:
            factor = jnp.concatenate([factors[0:1, one : one + 1] for one in place], 0)
        getattr(R, name + "_m_new")[here] = first_new
        getattr(R, name + "_v_new")[here] = second_new
        getattr(R, name + "_new")[here] = weight - factor * direction

    def update(name, gradient, place, lead=(), here=slice(None)):
        piece(name, (*lead, here, slice(None)), gradient, place)

    tile = R.table.shape[0]
    spots = R.named.shape[1]

    def table_part(row):
        hit = (
            lax.broadcasted_iota(jnp.int32, (part, spots), 0) + (turn * tile + row)
            == R.named[0:1, :]
        )
        gradient = dot(jnp.where(hit, 1.0, 0.0).astype(LOW), R.inc[...])
        update("table", gradient, 0, (), pl.ds(row, part))

    strips(tile, part, table_part)
    for group in range(3):
        update("qkv", R.red_qkv[group], 6 + group, (group,))
    update("up", R.red_up[...], 10)
    update("down", R.red_dn[...], 11)

    @pl.when(turn == 0)
    def _():
        update("out", R.red_out[...], 9)
        update("w_in", R.red_in[...], 1)
        piece("ln", (slice(None), slice(None)), R.red_ln[...], (2, 3, 4, 5))


def turns_of(rows, parts):
    return [
        turns
        for turns in (5, 4, 2, 1)
        if rows % (8 * turns) == 0 and all(size % (8 * turns) == 0 for size in parts)
    ][0]


def run_update(weights, moments, grads):
    names = ("table", "w_in", "ln", "qkv", "out", "up", "down")
    by_name = dict(zip(names, weights))
    rows, width = by_name["table"].shape
    strip, hidden = by_name["up"].shape
    heads_w = by_name["qkv"].shape[2]
    turns = turns_of(rows, (strip, hidden))
    tile = rows // turns
    part = max(size for size in range(8, 257, 8) if tile % size == 0)
    fixed = lambda array: pl.BlockSpec(array.shape, lambda turn: (0,) * array.ndim)
    specs = dict(
        table=pl.BlockSpec((tile, width), lambda turn: (turn, 0)),
        w_in=fixed(by_name["w_in"]),
        ln=fixed(by_name["ln"]),
        qkv=pl.BlockSpec((3, strip // turns, heads_w), lambda turn: (0, turn, 0)),
        out=fixed(by_name["out"]),
        up=pl.BlockSpec((strip // turns, hidden), lambda turn: (turn, 0)),
        down=pl.BlockSpec((hidden // turns, strip), lambda turn: (turn, 0)),
    )
    inputs = {}
    for name, weight, (first, second) in zip(names, weights, moments):
        inputs[name] = (weight, specs[name])
        inputs[name + "_m"] = (first, specs[name])
        inputs[name + "_v"] = (second, specs[name])
    for name, like in (
        ("red_up", "up"),
        ("red_dn", "down"),
        ("red_qkv", "qkv"),
        ("red_out", "out"),
        ("red_in", "w_in"),
        ("red_ln", "ln"),
    ):
        inputs[name] = (grads[name], specs[like])
    for name in ("inc", "named", "totals"):
        inputs[name] = (grads[name], fixed(grads[name]))
    tokens, model = grads["out"].shape
    rows_spec = pl.BlockSpec((tokens // turns, model), lambda turn: (turn, 0))
    inputs["made"] = (grads["out"], rows_spec)
    outputs = {"out_rows": (grads["out"].shape, rows_spec)}
    for name, weight in by_name.items():
        for kind in ("_new", "_m_new", "_v_new"):
            outputs[name + kind] = (weight.shape, specs[name])
    outputs["norms"] = ((2, 12), pl.BlockSpec((2, 12), lambda turn: (0, 0)))
    results = pl.pallas_call(
        functools.partial(update_kernel, part, [*inputs, *outputs]),
        grid=(turns,),
        out_shape=[jax.ShapeDtypeStruct(shape, F32) for shape, _ in outputs.values()],
        in_specs=[spec for _, spec in inputs.values()],
        out_specs=[spec for _, spec in outputs.values()],
        compiler_params=pltpu.CompilerParams(vmem_limit_bytes=VMEM_BYTES),
        name="update",
    )(*[value for value, _ in inputs.values()])
    return list(results)


def per_device(
    token_ids,
    levels,
    noise,
    cotangent,
    table,
    table_m,
    table_v,
    w_in,
    w_in_m,
    w_in_v,
    ln_params,
    ln_m,
    ln_v,
    w_qkv,
    qkv_m,
    qkv_v,
    w_out,
    out_m,
    out_v,
    w_up,
    up_m,
    up_v,
    w_down,
    down_m,
    down_v,
):
    dp_count = lax.axis_size("dp")
    seq_count, seq_len = token_ids.shape
    tokens = seq_count * seq_len
    model = cotangent.shape[2]
    cap = round_up(max(2, (3 * tokens + 2 * dp_count - 1) // (2 * dp_count)), 16)
    weights = (table, w_in, ln_params, w_qkv, w_out, w_up, w_down)
    moments = (
        (table_m, table_v),
        (w_in_m, w_in_v),
        (ln_m, ln_v),
        (qkv_m, qkv_v),
        (out_m, out_v),
        (up_m, up_v),
        (down_m, down_v),
    )
    grads = run_layer(
        cap,
        token_ids,
        levels,
        noise.reshape(tokens, -1),
        cotangent.reshape(tokens, model),
        weights,
        moments,
    )
    out, *results = run_update(weights, moments, grads)
    return (out.reshape(seq_count, seq_len, model), *results)


def solution(mesh):
    return jax.shard_map(
        per_device,
        mesh=mesh,
        in_specs=(
            P(("dp", "mp"), None),
            P(("dp", "mp")),
            P(("dp", "mp"), None, None),
            P(("dp", "mp"), None, None),
            P("dp", None),
            P("dp", None),
            P("dp", None),
            P("dp", None),
            P("dp", None),
            P("dp", None),
            P(None, "dp"),
            P(None, "dp"),
            P(None, "dp"),
            P(None, "dp", "mp"),
            P(None, "dp", "mp"),
            P(None, "dp", "mp"),
            P("mp", "dp"),
            P("mp", "dp"),
            P("mp", "dp"),
            P("dp", "mp"),
            P("dp", "mp"),
            P("dp", "mp"),
            P("mp", "dp"),
            P("mp", "dp"),
            P("mp", "dp"),
        ),
        out_specs=(
            P(("dp", "mp"), None, None),
            P("dp", None),
            P("dp", None),
            P("dp", None),
            P("dp", None),
            P("dp", None),
            P("dp", None),
            P(None, "dp"),
            P(None, "dp"),
            P(None, "dp"),
            P(None, "dp", "mp"),
            P(None, "dp", "mp"),
            P(None, "dp", "mp"),
            P("mp", "dp"),
            P("mp", "dp"),
            P("mp", "dp"),
            P("dp", "mp"),
            P("dp", "mp"),
            P("dp", "mp"),
            P("mp", "dp"),
            P("mp", "dp"),
            P("mp", "dp"),
            P(),
        ),
        check_vma=False,
    )
```
